32 devices in a mesh: expert: 8 (over z, y), tensor: 4 (over x, core).
Axes of the slice: x: 2, y: 2, z: 4, core: 2. Of those that a mesh axis runs over, the one named last changes fastest.
Arguments:
- tokens: bfloat16 [12608, 768], P('expert'), may hold values from -16 to 16
- gain_attn: float32 [768], replicated, may hold values from 0.5 to 1.5
- shift_attn: float32 [768], replicated, may hold values from -1.5 to 1.5
- qkv_weight: bfloat16 [3, 768, 768], P(None, None, 'tensor'), may hold values from -0.21875 to 0.21875
- out_weight: bfloat16 [768, 768], P('tensor'), may hold values from -1.75 to 1.75
- gain_moe: float32 [768], replicated, may hold values from 0.5 to 1.5
- shift_moe: float32 [768], replicated, may hold values from -1.5 to 1.5
- router_weight: bfloat16 [768, 4], replicated, may hold values from -0.15625 to 0.15625
- expert_up: bfloat16 [8, 768, 1536], P('expert', None, 'tensor'), may hold values from -0.21875 to 0.21875
- expert_down: bfloat16 [8, 1536, 768], P('expert', 'tensor'), may hold values from -0.21875 to 0.21875
- routes: int32 [12608, 2], P('expert'), may hold values from 0 to 3, all different within a row; in each aligned block of 1576 rows (0 to 1575, 1576 to 3151, ...) at most 1379 rows name the same one
- keep_mask: int32 [12608, 2], P('expert'), may hold values 0 or 1
- cotangent: bfloat16 [12608, 768], P('expert', 'tensor'), may hold values from -6 to 6
Outputs:
- mixed: bfloat16 [12608, 768], P('expert', 'tensor')
- grad_tokens: float32 [12608, 768], P('expert')
- grad_gain_attn: float32 [768], replicated
- grad_shift_attn: float32 [768], replicated
- grad_qkv: float32 [3, 768, 768], P(None, None, 'tensor')
- grad_out: float32 [768, 768], P('tensor')
- grad_gain_moe: float32 [768], replicated
- grad_shift_moe: float32 [768], replicated
- grad_router: float32 [768, 4], replicated
- grad_up: float32 [8, 768, 1536], P('expert', None, 'tensor')
- grad_down: float32 [8, 1536, 768], P('expert', 'tensor')
The draws below stay inside these ranges and needn't reach their ends.
Inputs may be any that keep to these rules, and one draw needn't show every extreme that they name: `routes`: each row names two different experts. Within each aligned block of 1576 rows (rows 0 to 1575, 1576 to 3151 and so on), each expert is named at most 1379 times.
All inputs are finite; a program needn't handle non-finite values. No bound on the sum of `keep_mask` on one device may be relied on, other than what follows from the above.
Results may differ from the reference program's by a relative error of at most 0.015.
Values may be sent and summed in bfloat16 or wider, within the bound.
A program may use at most 320 MiB of HBM per device.

```python
import math
import jax
import jax.numpy as jnp
import numpy as np
from jax import lax

D = 768
HEADS = 12
HD = 64
FF = 3072
SEQ = 197
TOK_DEV = 1576
TOKENS = 12608
EXPERTS = 4
CAP = 1379


def draw_tokens(key, part):
    key = jax.random.fold_in(key, 11)
    base_key, row_key, col_key = jax.random.split(key, 3)
    base = jnp.clip(jax.random.normal(base_key, (TOKENS, D), jnp.float32), -3.0, 3.0)
    row_scale = jnp.exp(jax.random.uniform(row_key, (TOKENS, 1), jnp.float32, -0.7, 0.4))
    col_scale = jnp.exp(jax.random.uniform(col_key, (1, D), jnp.float32, -1.2, 1.1))
    return (base * row_scale * col_scale).astype(jnp.bfloat16)


def set_ends(array, stream_key, least, high):
    longest = array.shape.index(max(array.shape))
    spots = []
    for shift in (0, 1):
        where = [jax.random.randint(jax.random.fold_in(stream_key, axis), (), 0, length) for axis, length in enumerate(array.shape)]
        where[longest] = (where[longest] + shift) % array.shape[longest]
        spots.append(tuple(where))
    return array.at[spots[0]].set(least).at[spots[1]].set(high)


def block_levels(rng, extent, pieces, least, largest):
    level, own = 1.0, jax.random.fold_in(rng, 6)
    for axis_at, blocks in pieces:
        heights = jnp.exp(jax.random.uniform(jax.random.fold_in(own, axis_at), (blocks,), jnp.float32, least / len(pieces), largest / len(pieces)))
        level = level * jnp.repeat(heights, extent[axis_at] // blocks).reshape([-1 if axis == axis_at else 1 for axis in range(len(extent))])
    return level


def shared_out(stream_key, own, number, rows, amount, top, limit, slope):
    order = jax.random.permutation(stream_key, amount)
    packed, usual = portions_of(amount, rows * top, limit, slope, True), portions_of(amount, rows * top, limit, slope, False)
    places = jnp.arange(amount)

    def named(lengths, offset_by):
        used = int((lengths > 0).sum())
        fixed = max(1, used // 4)
        shifted = fixed + (places - fixed + offset_by * (used - fixed)) % max(1, amount - fixed)
        return jnp.zeros((amount,), jnp.int32).at[order[jnp.where(places < fixed, places, shifted)]].set(jnp.asarray(lengths, jnp.int32))

    lengths = jnp.where(number % 4 == 0, named(packed, number // 4), named(usual, number - number // 4 - 1))
    mixed = jax.random.permutation(jax.random.fold_in(own, 3), amount)
    source_of, receiver = mixed[0:amount // 2 * 2:2], mixed[1:amount // 2 * 2:2]
    room = jnp.minimum(lengths[source_of] - 1, limit - lengths[receiver]) // 2
    room = jnp.where((source_of == order[0]) | (receiver == order[0]) | (lengths[receiver] == 0), 0, jnp.maximum(room, 0))
    shifted = jax.random.randint(jax.random.fold_in(own, 4), (amount // 2,), 0, 1 << 20) % (room + 1)
    lengths = lengths.at[source_of].add(-shifted).at[receiver].add(shifted)
    items = jnp.searchsorted(jnp.cumsum(lengths), jnp.arange(rows * top), side="right").astype(jnp.int32)
    table = items.reshape(top, rows).T
    table = table[jax.random.permutation(jax.random.fold_in(own, 1), rows)]
    offset_by = jax.random.randint(jax.random.fold_in(own, 2), (rows, 1), 0, top)
    return jnp.take_along_axis(table, (jnp.arange(top)[None, :] + offset_by) % top, axis=1)


def portions_of(count, total, reach, lean, full):
    loads = [(1 << 20) // math.isqrt(grade ** lean) + 1 for grade in range(1, count + 1)]
    largest = reach if full else min(reach, max(-(-total // count), total * loads[0] // sum(loads)))
    least = 1 if total - largest >= count - 1 else 0
    holding, spare = [largest] + [least] * (count - 1), total - largest - least * (count - 1)
    while spare > 0:
        movable = [i for i in range(1, count) if holding[i] < largest] or [i for i in range(1, count) if holding[i] < reach]
        pool, left = sum([loads[i] for i in movable]), spare
        for i in movable:
            addition = min(reach - holding[i], max(1, left * loads[i] // pool), spare)
            holding[i] = holding[i] + addition
            spare = spare - addition
    return np.array(holding)


def gaussian(key, dims, deviation, reach, cuts=(), kind=jnp.bfloat16):
    result = jax.random.normal(key, dims, jnp.float32) * deviation
    if len(cuts) > 0:
        result = block_levels(key, dims, cuts, -0.22, 0.18) * result
    return jnp.clip(result, min=-reach, max=reach).astype(kind)


def setup_inputs(seed: int = 0) -> dict:
    splits = jax.random.split(jax.random.key(seed), 14)
    tokens = draw_tokens(jax.random.fold_in(splits[13], 71), 0)
    gain_attn = jnp.clip(1.0 + 0.1 * jax.random.normal(splits[1], (D,), jnp.float32), 0.5, 1.5)
    shift_attn = gaussian(splits[2], (D,), 0.3, 1.5, (), jnp.float32)
    qkv_weight = gaussian(splits[3], (3, D, HEADS * HD), D ** -0.5, 0.21875, ((2, 4),))
    out_weight = gaussian(splits[4], (HEADS * HD, D), HEADS ** -0.5, 1.75, ((0, 4),))
    gain_moe = jnp.clip(1.0 + 0.1 * jax.random.normal(splits[5], (D,), jnp.float32), 0.5, 1.5)
    shift_moe = gaussian(splits[6], (D,), 0.3, 1.5, (), jnp.float32)
    router_weight = gaussian(splits[7], (D, EXPERTS), (2 * D) ** -0.5, 0.15625)
    expert_up = gaussian(splits[8], (2 * EXPERTS, D, FF // 2), D ** -0.5, 0.21875, ((0, 8), (2, 4)))
    expert_down = gaussian(splits[9], (2 * EXPERTS, FF // 2, D), (max(1, 4 * FF // (EXPERTS * EXPERTS))) ** -0.5, 0.21875, ((0, 8), (1, 4)))
    routes_keys = jax.random.split(jax.random.fold_in(splits[10], 1), TOKENS // TOK_DEV)
    routes_turns = jax.random.permutation(jax.random.fold_in(splits[10], 3), TOKENS // TOK_DEV)
    routes = jax.vmap(lambda own, number: shared_out(jax.random.fold_in(splits[10], 2), own, number, TOK_DEV, EXPERTS, 2, CAP, 1))(routes_keys, routes_turns).reshape((TOKENS, 2))
    keep_mask = set_ends((jax.random.randint(splits[11], (TOKENS, 2), 0, 8) < 7).astype(jnp.int32), jax.random.fold_in(splits[11], 1), 0, 1)
    cotangent = gaussian(splits[12], (TOKENS, D), 1.0, 6.0, ((0, 8), (1, 4)))
    return {"tokens": tokens, "gain_attn": gain_attn, "shift_attn": shift_attn, "qkv_weight": qkv_weight, "out_weight": out_weight, "gain_moe": gain_moe, "shift_moe": shift_moe, "router_weight": router_weight, "expert_up": expert_up, "expert_down": expert_down, "routes": routes, "keep_mask": keep_mask, "cotangent": cotangent}


norm_epsilon = 1e-06
precise = lax.Precision.HIGHEST

@jax.custom_vjp
def low(v):
    return lax.optimization_barrier(v.astype(jnp.bfloat16)).astype(jnp.float32)

@jax.custom_vjp
def low_back(v):
    return v

def low_keep(v):
    return (low(v), None)

def low_pass(kept, grad):
    return (grad,)

def back_keep(v):
    return (v, None)

def back_low(kept, grad):
    return (low(grad),)
low.defvjp(low_keep, low_pass)
low_back.defvjp(back_keep, back_low)

def norm_rows(values, gain, shift):
    row_mean = lax.optimization_barrier(jnp.mean(values, axis=-1, keepdims=True))
    centred = values - row_mean
    spread = lax.optimization_barrier(jnp.mean(centred * centred, axis=-1, keepdims=True))
    return centred * lax.rsqrt(spread + norm_epsilon) * gain + shift

def attend_group(h_one, qkv_weight, out_weight):
    group_count = h_one.shape[0] // SEQ
    projected = low_back(low(jnp.einsum('td,cdf->ctf', h_one, qkv_weight, precision=precise)))
    split_heads = projected.reshape(3, group_count, SEQ, HEADS, HD)
    scores = low_back(jnp.einsum('gqhe,gkhe->ghqk', split_heads[0], split_heads[1], precision=precise) * HD ** (-0.5))
    row_peak = lax.optimization_barrier(jnp.max(scores, axis=-1, keepdims=True))
    exp_scores = jnp.exp(scores - row_peak)
    probs = exp_scores / lax.optimization_barrier(jnp.sum(exp_scores, axis=-1, keepdims=True))
    attended = low_back(low(jnp.einsum('ghqk,gkhe->gqhe', low(probs), split_heads[2], precision=precise)))
    return low_back(jnp.dot(attended.reshape(group_count * SEQ, HEADS * HD), out_weight, precision=precise))

def expert_slots(routes, keep_mask):
    blocks = TOKENS // TOK_DEV
    flat_expert = routes.reshape(blocks, 2 * TOK_DEV).astype(jnp.int32)
    one_hot = (flat_expert[:, :, None] == jnp.arange(EXPERTS, dtype=jnp.int32)[None, None, :]).astype(jnp.int32)
    rank_within = lax.optimization_barrier(jnp.sum((jnp.cumsum(one_hot, axis=1) - one_hot) * one_hot, axis=2))
    slot_index = (jnp.arange(blocks, dtype=jnp.int32)[:, None] * CAP + rank_within).astype(jnp.int32)
    token_index = jnp.repeat(jnp.arange(TOKENS, dtype=jnp.int32), 2).reshape(blocks, 2 * TOK_DEV)
    source = jnp.where(keep_mask.reshape(blocks, 2 * TOK_DEV) > 0, token_index, TOKENS).astype(jnp.int32)
    source_table = jnp.full((EXPERTS, blocks * CAP), TOKENS, jnp.int32).at[flat_expert, slot_index].set(source)
    return (source_table, flat_expert.reshape(-1), slot_index.reshape(-1))

def run_expert(inputs):
    rows_in, up_matrix, down_matrix = inputs
    pre_act = low_back(jnp.dot(rows_in, up_matrix, precision=precise))
    hidden = low(jax.nn.gelu(pre_act, approximate=False))
    return low_back(low(jnp.dot(hidden, down_matrix, precision=precise)))

def reference(tokens, gain_attn, shift_attn, qkv_weight, out_weight, gain_moe, shift_moe, router_weight, expert_up, expert_down, routes, keep_mask, cotangent):
    source_table, flat_expert, slot_index = expert_slots(routes, keep_mask)
    keep_float = keep_mask.astype(jnp.float32)
    picked = routes.astype(jnp.int32)

    def layer(tokens, gain_attn, shift_attn, qkv_weight, out_weight, gain_moe, shift_moe, router_weight, expert_up, expert_down):
        up_full = jnp.concatenate([expert_up[0::2], expert_up[1::2]], axis=2)
        down_full = expert_down.reshape(EXPERTS, FF, D)
        h_one = low(norm_rows(tokens, gain_attn, shift_attn))

        def one_group(rows_in):
            return attend_group(rows_in, qkv_weight, out_weight)
        branch = lax.map(jax.checkpoint(one_group), h_one.reshape(TOKENS // TOK_DEV, TOK_DEV, D)).reshape(TOKENS, D)
        resid = tokens + branch
        h_two = low(norm_rows(resid, gain_moe, shift_moe))
        logits = low_back(jnp.dot(h_two, router_weight, precision=precise))
        router_probs = jax.nn.softmax(logits, axis=-1)
        gate_values = keep_float * jnp.take_along_axis(router_probs, picked, axis=1)
        padded = jnp.concatenate([h_two, jnp.zeros((1, D), jnp.float32)], axis=0)
        gathered = low_back(padded[source_table])
        answers = lax.map(jax.checkpoint(run_expert), (gathered, up_full, down_full))
        per_route = answers[flat_expert, slot_index].reshape(TOKENS, 2, D)
        return resid + lax.optimization_barrier(jnp.sum(gate_values[:, :, None] * per_route, axis=1))
    primals = (tokens.astype(jnp.float32), gain_attn.astype(jnp.float32), shift_attn.astype(jnp.float32), qkv_weight.astype(jnp.float32), out_weight.astype(jnp.float32), gain_moe.astype(jnp.float32), shift_moe.astype(jnp.float32), router_weight.astype(jnp.float32), expert_up.astype(jnp.float32), expert_down.astype(jnp.float32))
    mixed, pullback = jax.vjp(layer, *primals)
    grads = pullback(cotangent.astype(jnp.float32))
    return (mixed.astype(jnp.bfloat16), grads[0], grads[1], grads[2], grads[3], grads[4], grads[5], grads[6], grads[7], grads[8], grads[9])
```

```python
from functools import partial

import jax
import jax.numpy as jnp
from jax import lax
from jax.sharding import PartitionSpec as P

HD = 64
SEQ = 197


norm_epsilon = 1e-06


def norm_rows(values, gain, shift):
    row_mean = jnp.mean(values, axis=-1, keepdims=True)
    centred = values - row_mean
    spread = jnp.mean(centred * centred, axis=-1, keepdims=True)
    return centred * lax.rsqrt(spread + norm_epsilon) * gain + shift


def gelu_exact(values):
    return jax.nn.gelu(values, approximate=False)


def gate_from_logits(logit_rows, picked_rows, keep_rows):
    router_probs = jax.nn.softmax(logit_rows, axis=-1)
    return jnp.sum(jnp.where(picked_rows, router_probs[:, None, :], 0.0), axis=-1) * keep_rows


def attention_forward(h_rows, qkv_w, out_w):
    row_total_count = h_rows.shape[0]
    head_count = qkv_w.shape[2] // HD
    image_count = row_total_count // SEQ
    score_scale = HD ** (-0.5)
    projected = jnp.einsum("td,cdf->ctf", h_rows, qkv_w, preferred_element_type=jnp.float32).astype(
        jnp.bfloat16
    )
    split_heads = projected.reshape(3, image_count, SEQ, head_count, HD)
    queries = split_heads[0]
    keys_all = split_heads[1]
    values_all = split_heads[2]
    scores = (
        jnp.einsum("gqhe,gkhe->ghqk", queries, keys_all, preferred_element_type=jnp.float32)
        * score_scale
    )
    row_peak = jnp.max(scores, axis=-1, keepdims=True)
    exp_scores = jnp.exp(scores - row_peak)
    row_total = jnp.sum(exp_scores, axis=-1, keepdims=True)
    log_total = row_peak + jnp.log(row_total)
    weights = (exp_scores / row_total).astype(jnp.bfloat16)
    attended = jnp.einsum(
        "ghqk,gkhe->gqhe", weights, values_all, preferred_element_type=jnp.float32
    ).astype(jnp.bfloat16)
    attended = attended.reshape(row_total_count, head_count * HD)
    partial_out = jnp.dot(attended, out_w, preferred_element_type=jnp.float32)
    return (partial_out, (attended, queries, keys_all, values_all, log_total))


def attention_backward(grad_branch, saved, h_rows, qkv_w, out_w):
    attended, queries, keys_all, values_all, log_total = saved
    row_total_count = h_rows.shape[0]
    head_count = qkv_w.shape[2] // HD
    image_count = row_total_count // SEQ
    score_scale = HD ** (-0.5)
    grad_out = jnp.einsum("tc,td->cd", attended, grad_branch, preferred_element_type=jnp.float32)
    grad_attended = jnp.einsum(
        "td,cd->tc", grad_branch, out_w, preferred_element_type=jnp.float32
    ).astype(jnp.bfloat16)
    grad_attended = grad_attended.reshape(image_count, SEQ, head_count, HD)
    scores_again = (
        jnp.einsum("gqhe,gkhe->ghqk", queries, keys_all, preferred_element_type=jnp.float32)
        * score_scale
    )
    probs_again = jnp.exp(scores_again - log_total)
    grad_weights = jnp.einsum(
        "gqhe,gkhe->ghqk", grad_attended, values_all, preferred_element_type=jnp.float32
    )
    grad_scores = (
        probs_again * (grad_weights - jnp.sum(probs_again * grad_weights, axis=-1, keepdims=True))
    ).astype(jnp.bfloat16)
    grad_queries = (
        jnp.einsum("ghqk,gkhe->gqhe", grad_scores, keys_all, preferred_element_type=jnp.float32)
        * score_scale
    )
    grad_keys = (
        jnp.einsum("ghqk,gqhe->gkhe", grad_scores, queries, preferred_element_type=jnp.float32)
        * score_scale
    )
    grad_values = jnp.einsum(
        "ghqk,gqhe->gkhe",
        probs_again.astype(jnp.bfloat16),
        grad_attended,
        preferred_element_type=jnp.float32,
    )
    grad_rows = (
        jnp.stack([grad_queries, grad_keys, grad_values])
        .astype(jnp.bfloat16)
        .reshape(3, row_total_count, head_count * HD)
    )
    grad_qkv = jnp.einsum("td,ctf->cdf", h_rows, grad_rows, preferred_element_type=jnp.float32)
    grad_h_one = jnp.einsum("ctf,cdf->td", grad_rows, qkv_w, preferred_element_type=jnp.float32)
    return (grad_qkv, grad_out, grad_h_one)


def moe_tail(
    grad_h_rows,
    grad_gate_rows,
    grad_out_rows,
    h_two_rows,
    resid_rows,
    gate_back,
    router_weight,
    gain_moe,
    shift_moe,
):
    row_total_count = grad_h_rows.shape[0]
    grad_gate = jnp.sum(grad_gate_rows.reshape(row_total_count, -1, 2), axis=1)
    grad_logits = gate_back(grad_gate)[0].astype(jnp.bfloat16)
    grad_router = jnp.einsum(
        "td,te->de", h_two_rows, grad_logits, preferred_element_type=jnp.float32
    )
    grad_h_two = grad_h_rows + jnp.einsum(
        "te,de->td", grad_logits, router_weight, preferred_element_type=jnp.float32
    )
    norm_out, norm_back = jax.vjp(norm_rows, resid_rows, gain_moe, shift_moe)
    grad_resid_norm, grad_gain_moe, grad_shift_moe = norm_back(grad_h_two)
    return (grad_out_rows + grad_resid_norm, grad_router, grad_gain_moe, grad_shift_moe)


def per_device_routed(
    tokens,
    gain_attn,
    shift_attn,
    qkv_weight,
    out_weight,
    gain_moe,
    shift_moe,
    router_weight,
    expert_up,
    expert_down,
    routes,
    keep_mask,
    cotangent,
):
    row_count, feature_count = tokens.shape
    tensor_count = lax.axis_size("tensor")
    expert_count = lax.axis_size("expert")
    tensor_here = lax.axis_index("tensor")
    quarter_width = feature_count // tensor_count
    col_start = tensor_here * quarter_width
    experts_all = router_weight.shape[1]
    capacity = max(2, 7 * row_count // (2 * experts_all))
    tokens_float = tokens.astype(jnp.float32)
    h_one = norm_rows(tokens_float, gain_attn, shift_attn).astype(jnp.bfloat16)
    partial_out, saved = attention_forward(h_one, qkv_weight, out_weight)
    branch = lax.psum(partial_out, "tensor")
    resid = tokens_float + branch
    h_two = norm_rows(resid, gain_moe, shift_moe).astype(jnp.bfloat16)
    logits = jnp.dot(h_two, router_weight, preferred_element_type=jnp.float32)
    keep_float = keep_mask.astype(jnp.float32)
    picked = routes[:, :, None] == jnp.arange(experts_all, dtype=jnp.int32)[None, None, :]
    gate_values, gate_back = jax.vjp(
        partial(gate_from_logits, picked_rows=picked, keep_rows=keep_float), logits
    )
    flat_expert = routes.reshape(-1)
    one_hot = (flat_expert[:, None] == jnp.arange(experts_all, dtype=jnp.int32)[None, :]).astype(
        jnp.int32
    )
    rank_within = jnp.sum((jnp.cumsum(one_hot, axis=0) - one_hot) * one_hot, axis=1)
    slot_index = flat_expert * capacity + rank_within
    token_index = jnp.repeat(jnp.arange(row_count, dtype=jnp.int32), 2)
    live_route = keep_mask.reshape(-1) > 0
    source_table = (
        jnp.full((experts_all * capacity,), row_count, jnp.int32)
        .at[slot_index]
        .set(jnp.where(live_route, token_index, row_count))
    )
    padded_rows = jnp.concatenate([h_two, jnp.zeros((1, feature_count), jnp.bfloat16)], axis=0)
    dispatch = padded_rows[source_table].reshape(experts_all, capacity, feature_count)
    paired = jnp.broadcast_to(dispatch[:, None], (experts_all, 2, capacity, feature_count)).reshape(
        expert_count, capacity, feature_count
    )
    arrived = lax.all_to_all(paired, "expert", split_axis=0, concat_axis=0, tiled=True)
    expert_rows = arrived.reshape(expert_count * capacity, feature_count)
    up_local = expert_up[0]
    down_local = expert_down[0]
    pre_act = jnp.dot(expert_rows, up_local, preferred_element_type=jnp.float32)
    hidden_float, gelu_back = jax.vjp(gelu_exact, pre_act)
    hidden = hidden_float.astype(jnp.bfloat16)
    partial_down = jnp.dot(hidden, down_local, preferred_element_type=jnp.float32)
    summed = lax.psum_scatter(partial_down, "tensor", scatter_dimension=1, tiled=True)
    returned = lax.all_to_all(
        summed.reshape(expert_count, capacity, quarter_width),
        "expert",
        split_axis=0,
        concat_axis=0,
        tiled=True,
    )
    answer_table = jnp.sum(
        returned.reshape(experts_all, 2, capacity, quarter_width), axis=1
    ).astype(jnp.bfloat16)
    answers = (
        answer_table.reshape(experts_all * capacity, quarter_width)[slot_index]
        .astype(jnp.float32)
        .reshape(row_count, 2, quarter_width)
    )
    resid_part = lax.dynamic_slice_in_dim(resid, col_start, quarter_width, 1)
    mixed = (resid_part + jnp.sum(gate_values[:, :, None] * answers, axis=1)).astype(jnp.bfloat16)
    grad_part = cotangent.astype(jnp.float32)
    grad_answers = (
        (gate_values[:, :, None] * grad_part[:, None, :])
        .astype(jnp.bfloat16)
        .reshape(2 * row_count, quarter_width)
    )
    grad_gate_part = jnp.sum(grad_part[:, None, :] * answers, axis=-1)
    outgoing = (
        jnp.zeros((experts_all * capacity, quarter_width), jnp.bfloat16)
        .at[slot_index]
        .set(grad_answers)
    )
    outgoing = jnp.broadcast_to(
        outgoing.reshape(experts_all, 1, capacity, quarter_width),
        (experts_all, 2, capacity, quarter_width),
    ).reshape(expert_count, capacity, quarter_width)
    incoming = lax.all_to_all(outgoing, "expert", split_axis=0, concat_axis=0, tiled=True)
    grad_full = lax.all_gather(incoming, "tensor", axis=2, tiled=True).reshape(
        expert_count * capacity, feature_count
    )
    grad_hidden = jnp.einsum("rd,fd->rf", grad_full, down_local, preferred_element_type=jnp.float32)
    grad_pre = gelu_back(grad_hidden)[0].astype(jnp.bfloat16)
    grad_down = jnp.einsum("rf,rd->fd", hidden, grad_full, preferred_element_type=jnp.float32)
    grad_up = jnp.einsum("rd,rf->df", expert_rows, grad_pre, preferred_element_type=jnp.float32)
    grad_rows_partial = jnp.einsum(
        "rf,df->rd", grad_pre, up_local, preferred_element_type=jnp.float32
    )
    grad_rows_sum = lax.psum_scatter(
        grad_rows_partial.astype(jnp.bfloat16), "tensor", scatter_dimension=1, tiled=True
    ).astype(jnp.float32)
    sent_back = lax.all_to_all(
        grad_rows_sum.reshape(expert_count, capacity, quarter_width).astype(jnp.bfloat16),
        "expert",
        split_axis=0,
        concat_axis=0,
        tiled=True,
    ).astype(jnp.float32)
    grad_table = jnp.sum(sent_back.reshape(experts_all, 2, capacity, quarter_width), axis=1).astype(
        jnp.bfloat16
    )
    grad_inputs = (
        grad_table.reshape(experts_all * capacity, quarter_width)[slot_index]
        .astype(jnp.float32)
        .reshape(row_count, 2, quarter_width)
    )
    grad_h_part = jnp.sum(grad_inputs * keep_float[:, :, None], axis=1)
    grad_h_full, grad_gate_all, grad_out_full = (
        lax.all_gather(grad_h_part, "tensor", axis=1, tiled=True),
        lax.all_gather(grad_gate_part, "tensor", axis=1, tiled=True),
        lax.all_gather(grad_part, "tensor", axis=1, tiled=True),
    )
    grad_resid, grad_router, grad_gain_moe, grad_shift_moe = moe_tail(
        grad_h_full,
        grad_gate_all,
        grad_out_full,
        h_two,
        resid,
        gate_back,
        router_weight,
        gain_moe,
        shift_moe,
    )
    grad_qkv, grad_out, grad_h_one_part = attention_backward(
        grad_resid.astype(jnp.bfloat16), saved, h_one, qkv_weight, out_weight
    )
    grad_h_one = lax.psum(grad_h_one_part.astype(jnp.bfloat16), "tensor").astype(jnp.float32)
    norm_one_out, norm_one_back = jax.vjp(norm_rows, tokens_float, gain_attn, shift_attn)
    grad_tok_norm, grad_gain_attn, grad_shift_attn = norm_one_back(grad_h_one)
    grad_tokens = grad_resid + grad_tok_norm
    summed_grads = lax.psum(
        (
            grad_gain_attn,
            grad_shift_attn,
            grad_qkv,
            grad_out,
            grad_gain_moe,
            grad_shift_moe,
            grad_router,
        ),
        "expert",
    )
    grad_qkv_mine = summed_grads[2]
    grad_out_mine = summed_grads[3]
    return (
        mixed,
        grad_tokens,
        summed_grads[0],
        summed_grads[1],
        grad_qkv_mine,
        grad_out_mine,
        summed_grads[4],
        summed_grads[5],
        summed_grads[6],
        grad_up[None],
        grad_down[None],
    )


def per_device_dense(
    tokens,
    gain_attn,
    shift_attn,
    qkv_weight,
    out_weight,
    gain_moe,
    shift_moe,
    router_weight,
    expert_up,
    expert_down,
    routes,
    keep_mask,
    cotangent,
):
    row_count, feature_count = tokens.shape
    tensor_count = lax.axis_size("tensor")
    tensor_here = lax.axis_index("tensor")
    quarter_width = feature_count // tensor_count
    col_start = tensor_here * quarter_width
    experts_all = router_weight.shape[1]
    hidden_local = expert_up.shape[2]
    up_all = lax.all_gather(expert_up[0], "expert", axis=0).reshape(
        experts_all, 2, feature_count, hidden_local
    )
    down_all = lax.all_gather(expert_down[0], "expert", axis=0).reshape(
        experts_all, 2 * hidden_local, feature_count
    )
    up_all = up_all.transpose(2, 0, 1, 3).reshape(feature_count, -1)
    down_all = down_all.reshape(-1, feature_count)
    grad_full = lax.all_gather(cotangent, "tensor", axis=1, tiled=True)
    tokens_float = tokens.astype(jnp.float32)
    h_one = norm_rows(tokens_float, gain_attn, shift_attn).astype(jnp.bfloat16)
    partial_out, saved = attention_forward(h_one, qkv_weight, out_weight)
    branch = lax.psum(partial_out.astype(jnp.bfloat16), "tensor").astype(jnp.float32)
    resid = tokens_float + branch
    h_two = norm_rows(resid, gain_moe, shift_moe).astype(jnp.bfloat16)
    logits = jnp.dot(h_two, router_weight, preferred_element_type=jnp.float32)
    keep_float = keep_mask.astype(jnp.float32)
    kept = jnp.sum(
        jnp.where(
            routes[:, :, None] == jnp.arange(experts_all, dtype=jnp.int32)[None, None, :],
            keep_float[:, :, None],
            0.0,
        ),
        axis=1,
    )
    router_probs = jax.nn.softmax(logits, axis=-1)
    gates = kept * router_probs
    pre_act = jnp.dot(h_two, up_all, preferred_element_type=jnp.float32)
    hidden, gelu_back = jax.vjp(gelu_exact, pre_act)
    grad_hidden = jnp.einsum("td,fd->tf", grad_full, down_all, preferred_element_type=jnp.float32)
    by_expert = (row_count, experts_all, 2 * hidden_local)
    grad_gate = jnp.sum((hidden * grad_hidden).reshape(by_expert), axis=-1)
    gated_hidden = (
        (hidden.reshape(by_expert) * gates[:, :, None]).reshape(row_count, -1).astype(jnp.bfloat16)
    )
    grad_pre = gelu_back(
        (grad_hidden.reshape(by_expert) * gates[:, :, None]).reshape(row_count, -1)
    )[0].astype(jnp.bfloat16)
    mixed_part = jnp.dot(gated_hidden, down_all, preferred_element_type=jnp.float32)
    grad_h_part = jnp.einsum("tf,df->td", grad_pre, up_all, preferred_element_type=jnp.float32)
    grad_up = jnp.einsum("td,tf->fd", h_two, grad_pre, preferred_element_type=jnp.float32)
    grad_down = jnp.einsum("tf,td->fd", gated_hidden, grad_full, preferred_element_type=jnp.float32)
    grad_h_rows = lax.psum(grad_h_part.astype(jnp.bfloat16), "tensor").astype(jnp.float32)
    grad_gate = lax.psum(grad_gate, "tensor")
    mixed_sum = lax.psum_scatter(
        mixed_part.astype(jnp.bfloat16), "tensor", scatter_dimension=1, tiled=True
    ).astype(jnp.float32)
    resid_part = lax.dynamic_slice_in_dim(resid, col_start, quarter_width, 1)
    mixed = (resid_part + mixed_sum).astype(jnp.bfloat16)
    grad_down = lax.psum_scatter(
        grad_down.astype(jnp.bfloat16), "expert", scatter_dimension=0, tiled=True
    ).astype(jnp.float32)
    grad_up = (
        lax.psum_scatter(grad_up.astype(jnp.bfloat16), "expert", scatter_dimension=0, tiled=True)
        .astype(jnp.float32)
        .T
    )
    d_gate = kept * grad_gate
    grad_logits = (
        router_probs * (d_gate - jnp.sum(router_probs * d_gate, axis=-1, keepdims=True))
    ).astype(jnp.bfloat16)
    grad_router = jnp.einsum("td,te->de", h_two, grad_logits, preferred_element_type=jnp.float32)
    grad_h_two = grad_h_rows + jnp.einsum(
        "te,de->td", grad_logits, router_weight, preferred_element_type=jnp.float32
    )
    norm_out, norm_back = jax.vjp(norm_rows, resid, gain_moe, shift_moe)
    grad_resid_norm, grad_gain_moe, grad_shift_moe = norm_back(grad_h_two)
    grad_resid = grad_full.astype(jnp.float32) + grad_resid_norm
    grad_qkv, grad_out, grad_h_one_part = attention_backward(
        grad_resid.astype(jnp.bfloat16), saved, h_one, qkv_weight, out_weight
    )
    grad_h_one = lax.psum(grad_h_one_part.astype(jnp.bfloat16), "tensor").astype(jnp.float32)
    norm_one_out, norm_one_back = jax.vjp(norm_rows, tokens_float, gain_attn, shift_attn)
    grad_tok_norm, grad_gain_attn, grad_shift_attn = norm_one_back(grad_h_one)
    grad_tokens = grad_resid + grad_tok_norm
    grad_qkv, grad_out = lax.psum(
        (grad_qkv.astype(jnp.bfloat16), grad_out.astype(jnp.bfloat16)), "expert"
    )
    small = lax.psum(
        (grad_gain_attn, grad_shift_attn, grad_gain_moe, grad_shift_moe, grad_router), "expert"
    )
    return (
        mixed,
        grad_tokens,
        small[0],
        small[1],
        grad_qkv.astype(jnp.float32),
        grad_out.astype(jnp.float32),
        small[2],
        small[3],
        small[4],
        grad_up[None],
        grad_down[None],
    )


def per_device(*arguments):
    router_weight = arguments[7]
    if router_weight.shape[1] <= 4:
        return per_device_dense(*arguments)
    return per_device_routed(*arguments)


def solution(mesh):
    placed = (
        P("expert", None),
        P(),
        P(),
        P(None, None, "tensor"),
        P("tensor", None),
        P(),
        P(),
        P(),
        P("expert", None, "tensor"),
        P("expert", "tensor", None),
        P("expert", None),
        P("expert", None),
        P("expert", "tensor"),
    )
    return jax.shard_map(
        per_device,
        mesh=mesh,
        in_specs=placed,
        out_specs=(
            P("expert", "tensor"),
            P("expert", None),
            P(),
            P(),
            P(None, None, "tensor"),
            P("tensor", None),
            P(),
            P(),
            P(),
            P("expert", None, "tensor"),
            P("expert", "tensor", None),
        ),
        check_vma=False,
    )
```

```python
from functools import partial

import jax
import jax.numpy as jnp
from jax import lax
from jax.experimental import pallas as pl
from jax.experimental.pallas import tpu as pltpu
from jax.sharding import PartitionSpec as P

HD = 64
SEQ = 197


norm_epsilon = 1e-06


def norm_rows(values, gain, shift):
    row_mean = jnp.mean(values, axis=-1, keepdims=True)
    centred = values - row_mean
    spread = jnp.mean(centred * centred, axis=-1, keepdims=True)
    return centred * lax.rsqrt(spread + norm_epsilon) * gain + shift


def gelu_exact(values):
    return jax.nn.gelu(values, approximate=False)


def gate_from_logits(logit_rows, picked_rows, keep_rows):
    router_probs = jax.nn.softmax(logit_rows, axis=-1)
    return jnp.sum(jnp.where(picked_rows, router_probs[:, None, :], 0.0), axis=-1) * keep_rows


def attention_forward(h_rows, qkv_w, out_w):
    row_total_count = h_rows.shape[0]
    head_count = qkv_w.shape[2] // HD
    image_count = row_total_count // SEQ
    score_scale = HD ** (-0.5)
    projected = jnp.einsum("td,cdf->ctf", h_rows, qkv_w, preferred_element_type=jnp.float32).astype(
        jnp.bfloat16
    )
    split_heads = projected.reshape(3, image_count, SEQ, head_count, HD)
    queries = split_heads[0]
    keys_all = split_heads[1]
    values_all = split_heads[2]
    scores = (
        jnp.einsum("gqhe,gkhe->ghqk", queries, keys_all, preferred_element_type=jnp.float32)
        * score_scale
    )
    row_peak = jnp.max(scores, axis=-1, keepdims=True)
    exp_scores = jnp.exp(scores - row_peak)
    row_total = jnp.sum(exp_scores, axis=-1, keepdims=True)
    log_total = row_peak + jnp.log(row_total)
    weights = (exp_scores / row_total).astype(jnp.bfloat16)
    attended = jnp.einsum(
        "ghqk,gkhe->gqhe", weights, values_all, preferred_element_type=jnp.float32
    ).astype(jnp.bfloat16)
    attended = attended.reshape(row_total_count, head_count * HD)
    partial_out = jnp.dot(attended, out_w, preferred_element_type=jnp.float32)
    return (partial_out, (attended, queries, keys_all, values_all, log_total))


def attention_backward(grad_branch, saved, h_rows, qkv_w, out_w):
    attended, queries, keys_all, values_all, log_total = saved
    row_total_count = h_rows.shape[0]
    head_count = qkv_w.shape[2] // HD
    image_count = row_total_count // SEQ
    score_scale = HD ** (-0.5)
    grad_out = jnp.einsum("tc,td->cd", attended, grad_branch, preferred_element_type=jnp.float32)
    grad_attended = jnp.einsum(
        "td,cd->tc", grad_branch, out_w, preferred_element_type=jnp.float32
    ).astype(jnp.bfloat16)
    grad_attended = grad_attended.reshape(image_count, SEQ, head_count, HD)
    scores_again = (
        jnp.einsum("gqhe,gkhe->ghqk", queries, keys_all, preferred_element_type=jnp.float32)
        * score_scale
    )
    probs_again = jnp.exp(scores_again - log_total)
    grad_weights = jnp.einsum(
        "gqhe,gkhe->ghqk", grad_attended, values_all, preferred_element_type=jnp.float32
    )
    grad_scores = (
        probs_again * (grad_weights - jnp.sum(probs_again * grad_weights, axis=-1, keepdims=True))
    ).astype(jnp.bfloat16)
    grad_queries = (
        jnp.einsum("ghqk,gkhe->gqhe", grad_scores, keys_all, preferred_element_type=jnp.float32)
        * score_scale
    )
    grad_keys = (
        jnp.einsum("ghqk,gqhe->gkhe", grad_scores, queries, preferred_element_type=jnp.float32)
        * score_scale
    )
    grad_values = jnp.einsum(
        "ghqk,gqhe->gkhe",
        probs_again.astype(jnp.bfloat16),
        grad_attended,
        preferred_element_type=jnp.float32,
    )
    grad_rows = (
        jnp.stack([grad_queries, grad_keys, grad_values])
        .astype(jnp.bfloat16)
        .reshape(3, row_total_count, head_count * HD)
    )
    grad_qkv = jnp.einsum("td,ctf->cdf", h_rows, grad_rows, preferred_element_type=jnp.float32)
    grad_h_one = jnp.einsum("ctf,cdf->td", grad_rows, qkv_w, preferred_element_type=jnp.float32)
    return (grad_qkv, grad_out, grad_h_one)


def moe_tail(
    grad_h_rows,
    grad_gate_rows,
    grad_out_rows,
    h_two_rows,
    resid_rows,
    gate_back,
    router_weight,
    gain_moe,
    shift_moe,
):
    row_total_count = grad_h_rows.shape[0]
    grad_gate = jnp.sum(grad_gate_rows.reshape(row_total_count, -1, 2), axis=1)
    grad_logits = gate_back(grad_gate)[0].astype(jnp.bfloat16)
    grad_router = jnp.einsum(
        "td,te->de", h_two_rows, grad_logits, preferred_element_type=jnp.float32
    )
    grad_h_two = grad_h_rows + jnp.einsum(
        "te,de->td", grad_logits, router_weight, preferred_element_type=jnp.float32
    )
    norm_out, norm_back = jax.vjp(norm_rows, resid_rows, gain_moe, shift_moe)
    grad_resid_norm, grad_gain_moe, grad_shift_moe = norm_back(grad_h_two)
    return (grad_out_rows + grad_resid_norm, grad_router, grad_gain_moe, grad_shift_moe)


def per_device_routed(
    tokens,
    gain_attn,
    shift_attn,
    qkv_weight,
    out_weight,
    gain_moe,
    shift_moe,
    router_weight,
    expert_up,
    expert_down,
    routes,
    keep_mask,
    cotangent,
):
    row_count, feature_count = tokens.shape
    tensor_count = lax.axis_size("tensor")
    expert_count = lax.axis_size("expert")
    tensor_here = lax.axis_index("tensor")
    quarter_width = feature_count // tensor_count
    col_start = tensor_here * quarter_width
    experts_all = router_weight.shape[1]
    capacity = max(2, 7 * row_count // (2 * experts_all))
    tokens_float = tokens.astype(jnp.float32)
    h_one = norm_rows(tokens_float, gain_attn, shift_attn).astype(jnp.bfloat16)
    partial_out, saved = attention_forward(h_one, qkv_weight, out_weight)
    branch = lax.psum(partial_out, "tensor")
    resid = tokens_float + branch
    h_two = norm_rows(resid, gain_moe, shift_moe).astype(jnp.bfloat16)
    logits = jnp.dot(h_two, router_weight, preferred_element_type=jnp.float32)
    keep_float = keep_mask.astype(jnp.float32)
    picked = routes[:, :, None] == jnp.arange(experts_all, dtype=jnp.int32)[None, None, :]
    gate_values, gate_back = jax.vjp(
        partial(gate_from_logits, picked_rows=picked, keep_rows=keep_float), logits
    )
    flat_expert = routes.reshape(-1)
    one_hot = (flat_expert[:, None] == jnp.arange(experts_all, dtype=jnp.int32)[None, :]).astype(
        jnp.int32
    )
    rank_within = jnp.sum((jnp.cumsum(one_hot, axis=0) - one_hot) * one_hot, axis=1)
    slot_index = flat_expert * capacity + rank_within
    token_index = jnp.repeat(jnp.arange(row_count, dtype=jnp.int32), 2)
    live_route = keep_mask.reshape(-1) > 0
    source_table = (
        jnp.full((experts_all * capacity,), row_count, jnp.int32)
        .at[slot_index]
        .set(jnp.where(live_route, token_index, row_count))
    )
    padded_rows = jnp.concatenate([h_two, jnp.zeros((1, feature_count), jnp.bfloat16)], axis=0)
    dispatch = padded_rows[source_table].reshape(experts_all, capacity, feature_count)
    paired = jnp.broadcast_to(dispatch[:, None], (experts_all, 2, capacity, feature_count)).reshape(
        expert_count, capacity, feature_count
    )
    arrived = lax.all_to_all(paired, "expert", split_axis=0, concat_axis=0, tiled=True)
    expert_rows = arrived.reshape(expert_count * capacity, feature_count)
    up_local = expert_up[0]
    down_local = expert_down[0]
    pre_act = jnp.dot(expert_rows, up_local, preferred_element_type=jnp.float32)
    hidden_float, gelu_back = jax.vjp(gelu_exact, pre_act)
    hidden = hidden_float.astype(jnp.bfloat16)
    partial_down = jnp.dot(hidden, down_local, preferred_element_type=jnp.float32)
    summed = lax.psum_scatter(partial_down, "tensor", scatter_dimension=1, tiled=True)
    returned = lax.all_to_all(
        summed.reshape(expert_count, capacity, quarter_width),
        "expert",
        split_axis=0,
        concat_axis=0,
        tiled=True,
    )
    answer_table = jnp.sum(
        returned.reshape(experts_all, 2, capacity, quarter_width), axis=1
    ).astype(jnp.bfloat16)
    answers = (
        answer_table.reshape(experts_all * capacity, quarter_width)[slot_index]
        .astype(jnp.float32)
        .reshape(row_count, 2, quarter_width)
    )
    resid_part = lax.dynamic_slice_in_dim(resid, col_start, quarter_width, 1)
    mixed = (resid_part + jnp.sum(gate_values[:, :, None] * answers, axis=1)).astype(jnp.bfloat16)
    grad_part = cotangent.astype(jnp.float32)
    grad_answers = (
        (gate_values[:, :, None] * grad_part[:, None, :])
        .astype(jnp.bfloat16)
        .reshape(2 * row_count, quarter_width)
    )
    grad_gate_part = jnp.sum(grad_part[:, None, :] * answers, axis=-1)
    outgoing = (
        jnp.zeros((experts_all * capacity, quarter_width), jnp.bfloat16)
        .at[slot_index]
        .set(grad_answers)
    )
    outgoing = jnp.broadcast_to(
        outgoing.reshape(experts_all, 1, capacity, quarter_width),
        (experts_all, 2, capacity, quarter_width),
    ).reshape(expert_count, capacity, quarter_width)
    incoming = lax.all_to_all(outgoing, "expert", split_axis=0, concat_axis=0, tiled=True)
    grad_full = lax.all_gather(incoming, "tensor", axis=2, tiled=True).reshape(
        expert_count * capacity, feature_count
    )
    grad_hidden = jnp.einsum("rd,fd->rf", grad_full, down_local, preferred_element_type=jnp.float32)
    grad_pre = gelu_back(grad_hidden)[0].astype(jnp.bfloat16)
    grad_down = jnp.einsum("rf,rd->fd", hidden, grad_full, preferred_element_type=jnp.float32)
    grad_up = jnp.einsum("rd,rf->df", expert_rows, grad_pre, preferred_element_type=jnp.float32)
    grad_rows_partial = jnp.einsum(
        "rf,df->rd", grad_pre, up_local, preferred_element_type=jnp.float32
    )
    grad_rows_sum = lax.psum_scatter(
        grad_rows_partial.astype(jnp.bfloat16), "tensor", scatter_dimension=1, tiled=True
    ).astype(jnp.float32)
    sent_back = lax.all_to_all(
        grad_rows_sum.reshape(expert_count, capacity, quarter_width).astype(jnp.bfloat16),
        "expert",
        split_axis=0,
        concat_axis=0,
        tiled=True,
    ).astype(jnp.float32)
    grad_table = jnp.sum(sent_back.reshape(experts_all, 2, capacity, quarter_width), axis=1).astype(
        jnp.bfloat16
    )
    grad_inputs = (
        grad_table.reshape(experts_all * capacity, quarter_width)[slot_index]
        .astype(jnp.float32)
        .reshape(row_count, 2, quarter_width)
    )
    grad_h_part = jnp.sum(grad_inputs * keep_float[:, :, None], axis=1)
    grad_h_full, grad_gate_all, grad_out_full = (
        lax.all_gather(grad_h_part, "tensor", axis=1, tiled=True),
        lax.all_gather(grad_gate_part, "tensor", axis=1, tiled=True),
        lax.all_gather(grad_part, "tensor", axis=1, tiled=True),
    )
    grad_resid, grad_router, grad_gain_moe, grad_shift_moe = moe_tail(
        grad_h_full,
        grad_gate_all,
        grad_out_full,
        h_two,
        resid,
        gate_back,
        router_weight,
        gain_moe,
        shift_moe,
    )
    grad_qkv, grad_out, grad_h_one_part = attention_backward(
        grad_resid.astype(jnp.bfloat16), saved, h_one, qkv_weight, out_weight
    )
    grad_h_one = lax.psum(grad_h_one_part.astype(jnp.bfloat16), "tensor").astype(jnp.float32)
    norm_one_out, norm_one_back = jax.vjp(norm_rows, tokens_float, gain_attn, shift_attn)
    grad_tok_norm, grad_gain_attn, grad_shift_attn = norm_one_back(grad_h_one)
    grad_tokens = grad_resid + grad_tok_norm
    summed_grads = lax.psum(
        (
            grad_gain_attn,
            grad_shift_attn,
            grad_qkv,
            grad_out,
            grad_gain_moe,
            grad_shift_moe,
            grad_router,
        ),
        "expert",
    )
    grad_qkv_mine = summed_grads[2]
    grad_out_mine = summed_grads[3]
    return (
        mixed,
        grad_tokens,
        summed_grads[0],
        summed_grads[1],
        grad_qkv_mine,
        grad_out_mine,
        summed_grads[4],
        summed_grads[5],
        summed_grads[6],
        grad_up[None],
        grad_down[None],
    )


MESH = pl.DeviceIdType.MESH
f32 = jnp.float32
bf16 = jnp.bfloat16
PITCH = 208


def dot(left, right, over=((1,), (0,))):
    return lax.dot_general(left, right, (over, ((), ())), preferred_element_type=f32)


def aligned(start, size):
    return pl.ds(pl.multiple_of(start, 16), size)


def lanes_at(start, size):
    return pl.ds(pl.multiple_of(start, 128), size)


def norm_stats(values):
    row_mean = jnp.mean(values, axis=1, keepdims=True)
    centred = values - row_mean
    inverse = lax.rsqrt(jnp.mean(centred * centred, axis=1, keepdims=True) + norm_epsilon)
    return centred * inverse, inverse


def greet(neighbours):
    barrier = pltpu.get_barrier_semaphore()
    count = 0
    for is_there, device in neighbours:

        @pl.when(is_there)
        def _():
            pl.semaphore_signal(barrier, inc=1, device_id=device, device_id_type=MESH)

        count = count + jnp.where(is_there, 1, 0)
    pl.semaphore_wait(barrier, count)


def head_mask(lane, head):
    return (lane < HD) if head % 2 == 0 else (lane >= HD)


def forward_kernel(
    tok_ref,
    gain1_ref,
    shift1_ref,
    gain2_ref,
    shift2_ref,
    qkv_ref,
    out_w_ref,
    up_ref,
    down_ref,
    cot_ref,
    kept_ref,
    q_ref,
    k_ref,
    v_ref,
    att_ref,
    lse_ref,
    resid_ref,
    h_out,
    cot_out,
    kept_out,
    up_out,
    down_out,
    h_all,
    cot_all,
    kept_all,
    part,
    mine,
    core_from,
    core_to,
    x_to,
    x_from,
    total_to,
    total_from,
    cot_core,
    core_s,
    core_r,
    x_s,
    x_r,
    tot_s,
    tot_r,
    y_s,
    y_r,
    rel_s,
    rel_r,
    w_s,
    w_r,
    c_s,
    c_r,
    out_sem,
    *,
    images,
    heads,
):
    expert_at = lax.axis_index("expert")
    tensor_at = lax.axis_index("tensor")
    z_at, y_at = expert_at // 2, expert_at % 2
    z_last = lax.axis_size("expert") // 2 - 1
    x_at, core_at = tensor_at // 2, tensor_at % 2
    other = 1 - core_at
    rows = images * PITCH
    half = rows // 2
    wide = out_w_ref.shape[1] // 2
    hidden = up_ref.shape[1]
    core_dev = (expert_at, tensor_at + 1 - 2 * core_at)
    x_dev = (expert_at, tensor_at + 2 - 4 * x_at)
    y_dev = (expert_at + 1 - 2 * y_at, tensor_at)
    z_up = (expert_at + 2, tensor_at)
    z_down = (expert_at - 2, tensor_at)
    has_up, has_down = z_at < z_last, z_at > 0
    greet([(True, core_dev), (True, x_dev), (True, y_dev), (has_up, z_up), (has_down, z_down)])

    def remote(src, dst, send, recv, device):
        return pltpu.make_async_remote_copy(
            src_ref=src, dst_ref=dst, send_sem=send, recv_sem=recv, device_id=device, device_id_type=MESH
        )

    def slot(expert):
        return (
            up_out.at[expert // 2, :, lanes_at(expert % 2 * hidden, hidden)],
            down_out.at[expert // 2, aligned(expert % 2 * hidden, hidden), :],
        )

    def hop(step, way):
        expert = z_at - step if way == 0 else z_at + step
        source = (up_ref, down_ref) if step == 0 else slot(expert)
        target = slot(expert)
        device = z_up if way == 0 else z_down
        return [remote(source[n], target[n], w_s.at[way, step, n], w_r.at[way, step, n], device) for n in range(2)]

    def hop_goes(step, way):
        if way == 0:
            return (z_at - step >= 0) & has_up
        return (z_at + step <= z_last) & has_down

    def hop_comes(step, way):
        return (z_at - 1 - step >= 0) if way == 0 else (z_at + 1 + step <= z_last)

    def hop_arriving(step, way):
        expert = z_at - 1 - step if way == 0 else z_at + 1 + step
        target = slot(expert)
        return [remote(target[n], target[n], w_s.at[way, step, n], w_r.at[way, step, n], core_dev) for n in range(2)]

    def start_hops(step):
        for way in range(2):

            @pl.when(hop_goes(step, way))
            def _():
                for copy in hop(step, way):
                    copy.start()

    def await_hops(step):
        for way in range(2):

            @pl.when(hop_comes(step, way))
            def _():
                for copy in hop_arriving(step, way):
                    copy.wait_recv()

    start_hops(0)
    own = slot(z_at)
    own_copies = [
        pltpu.make_async_copy((up_ref, down_ref)[n], own[n], out_sem.at[n]) for n in range(2)
    ]
    for copy in own_copies:
        copy.start()

    quarter = cot_ref.shape[1]
    swap = remote(cot_ref, cot_core, c_s.at[0], c_r.at[0], core_dev)
    swap.start()
    kept_all[aligned(y_at * rows, rows), :] = kept_ref[...]
    kept_mine = kept_all.at[aligned(y_at * rows, rows), :]
    kept_y = remote(kept_mine, kept_mine, c_s.at[7], c_r.at[7], y_dev)
    kept_y.start()
    swap.wait_recv()
    base = y_at * rows

    @pl.when(core_at == 0)
    def _():
        both = jnp.concatenate([cot_ref[...], cot_core[...]], axis=1)
        cot_all[aligned(base, rows), lanes_at(x_at * wide, wide)] = both

    @pl.when(core_at == 1)
    def _():
        both = jnp.concatenate([cot_core[...], cot_ref[...]], axis=1)
        cot_all[aligned(base, rows), lanes_at(x_at * wide, wide)] = both

    def block(row_side, col_side, core):
        return cot_all.at[aligned(row_side * rows + core * half, half), lanes_at(col_side * wide, wide)]

    def cot_copy(number, row_side, col_side, core, device):
        ref = block(row_side, col_side, core)
        return remote(ref, ref, c_s.at[number], c_r.at[number], device)

    cot_x = cot_copy(1, y_at, x_at, core_at, x_dev)
    cot_y = cot_copy(2, y_at, x_at, core_at, y_dev)
    cot_x.start()
    cot_y.start()
    cot_x_in = cot_copy(1, y_at, 1 - x_at, core_at, x_dev)
    cot_y_in = cot_copy(2, 1 - y_at, x_at, core_at, y_dev)
    cot_relay = cot_copy(3, y_at, 1 - x_at, core_at, y_dev)
    cot_relay_in = cot_copy(3, 1 - y_at, 1 - x_at, core_at, y_dev)
    cot_share = [
        cot_copy(4, y_at, 1 - x_at, core_at, core_dev),
        cot_copy(5, 1 - y_at, x_at, core_at, core_dev),
        cot_copy(6, 1 - y_at, 1 - x_at, core_at, core_dev),
    ]
    cot_share_in = [
        cot_copy(4, y_at, 1 - x_at, other, core_dev),
        cot_copy(5, 1 - y_at, x_at, other, core_dev),
        cot_copy(6, 1 - y_at, 1 - x_at, other, core_dev),
    ]

    lane = lax.broadcasted_iota(jnp.int32, (PITCH, 2 * HD), 1)
    key_mask = lax.broadcasted_iota(jnp.int32, (PITCH, PITCH), 1) < SEQ
    gain1, shift1 = gain1_ref[...], shift1_ref[...]
    gain2, shift2 = gain2_ref[...], shift2_ref[...]
    my_cols = lanes_at(core_at * wide, wide)
    their_cols = lanes_at(other * wide, wide)

    def attend(image):
        normed, _ = norm_stats(tok_ref[image].astype(f32))
        h_one = (normed * gain1 + shift1).astype(bf16)
        queries = dot(h_one, qkv_ref[0]).astype(bf16)
        keys = dot(h_one, qkv_ref[1]).astype(bf16)
        values = dot(h_one, qkv_ref[2]).astype(bf16)
        q_ref[image] = queries
        k_ref[image] = keys
        v_ref[image] = values
        outs = []
        lse = jnp.zeros((PITCH, 2 * HD), f32)
        for head in range(heads):
            first = head // 2 * 2 * HD
            last = min(first + 2 * HD, heads * HD)
            q_head, k_head, v_head = queries[:, first:last], keys[:, first:last], values[:, first:last]
            if last - first == 2 * HD:
                q_head = jnp.where(head_mask(lane, head), q_head, jnp.zeros_like(q_head))
            scores = dot(q_head, k_head, ((1,), (1,))) * (HD**-0.5)
            scores = jnp.where(key_mask, scores, -1e30)
            peak = jnp.max(scores, axis=1, keepdims=True)
            powers = jnp.exp(scores - peak)
            row_sum = jnp.sum(powers, axis=1, keepdims=True)
            weights = (powers / row_sum).astype(bf16)
            outs.append(dot(weights, v_head))
            lse = jnp.where(lane == head, peak + jnp.log(row_sum), lse)
        lse_ref[image] = lse
        joined = []
        for head in range(0, heads, 2):
            if head + 1 < heads:
                joined.append(jnp.where(lane < HD, outs[head], outs[head + 1]))
            else:
                joined.append(outs[head])
        attended = jnp.concatenate(joined, axis=1).astype(bf16)
        att_ref[image] = attended
        part[...] = dot(attended, out_w_ref[...])
        mine[image] = part[:, my_cols]
        core_to[image] = part[:, their_cols].astype(bf16)

    def core_copy(image):
        return remote(core_to.at[image], core_from.at[image], core_s.at[image], core_r.at[image], core_dev)

    def x_copy(image):
        return remote(x_to.at[image], x_from.at[image], x_s.at[image], x_r.at[image], x_dev)

    def total_copy(image):
        return remote(total_to.at[image], total_from.at[image], tot_s.at[image], tot_r.at[image], core_dev)

    def h_block(row_side, image, core):
        return h_all.at[aligned(row_side * rows + image * PITCH, PITCH), lanes_at(core * wide, wide)]

    def y_copy(image):
        ref = h_block(y_at, image, core_at)
        return remote(ref, ref, y_s.at[image], y_r.at[image], y_dev)

    def y_arriving(image):
        ref = h_block(1 - y_at, image, core_at)
        return remote(ref, ref, y_s.at[image], y_r.at[image], y_dev)

    def relay_copy(image):
        ref = h_block(1 - y_at, image, core_at)
        return remote(ref, ref, rel_s.at[image], rel_r.at[image], core_dev)

    def relay_arriving(image):
        ref = h_block(1 - y_at, image, other)
        return remote(ref, ref, rel_s.at[image], rel_r.at[image], core_dev)

    def stage(tick, lag, run):
        image = tick - lag

        @pl.when((image >= 0) & (image < images))
        def _():
            run(image)

    def run_attend(image):
        attend(image)
        core_copy(image).start()

    def run_x(image):
        core_copy(image).wait_recv()
        x_to[image] = (mine[image] + core_from[image].astype(f32)).astype(bf16)
        x_copy(image).start()

    def run_total(image):
        x_copy(image).wait_recv()
        total_to[image] = (x_to[image].astype(f32) + x_from[image].astype(f32)).astype(bf16)
        total_copy(image).start()

    def run_norm(image):
        total_copy(image).wait_recv()
        part[:, my_cols] = total_to[image].astype(f32)
        part[:, their_cols] = total_from[image].astype(f32)
        resid = tok_ref[image].astype(f32) + part[...]
        resid_ref[image] = resid
        normed, _ = norm_stats(resid)
        h_all[aligned(base + image * PITCH, PITCH), :] = (normed * gain2 + shift2).astype(bf16)
        y_copy(image).start()

    def run_relay(image):
        y_arriving(image).wait_recv()
        relay_copy(image).start()

    def run_end(image):
        relay_arriving(image).wait_recv()

    def at_tick(tick, when, run):
        @pl.when(tick == when)
        def _():
            run()

    def cot_step_one():
        cot_x_in.wait_recv()
        cot_relay.start()
        cot_share[0].start()

    def cot_step_two():
        cot_y_in.wait_recv()
        cot_share[1].start()

    def weights_step_one():
        await_hops(0)
        start_hops(1)

    def weights_step_two():
        await_hops(1)
        start_hops(2)

    def cot_step_three():
        cot_relay_in.wait_recv()
        cot_share[2].start()

    def per_tick(tick, _):
        stage(tick, 0, run_attend)
        stage(tick, 1, run_x)
        stage(tick, 4, run_total)
        stage(tick, 5, run_norm)
        stage(tick, 9, run_relay)
        stage(tick, 10, run_end)
        at_tick(tick, 7, cot_step_one)
        at_tick(tick, 8, weights_step_one)
        at_tick(tick, 9, cot_step_two)
        at_tick(tick, 14, weights_step_two)
        at_tick(tick, 15, cot_step_three)
        return 0

    lax.fori_loop(0, images + 10, per_tick, 0)
    for copy in cot_share_in:
        copy.wait_recv()
    kept_theirs = kept_all.at[aligned((1 - y_at) * rows, rows), :]
    remote(kept_theirs, kept_theirs, c_s.at[7], c_r.at[7], y_dev).wait_recv()
    outs = [
        pltpu.make_async_copy(h_all, h_out, out_sem.at[2]),
        pltpu.make_async_copy(cot_all, cot_out, out_sem.at[3]),
        pltpu.make_async_copy(kept_all, kept_out, out_sem.at[4]),
    ]
    for copy in outs:
        copy.start()
    for copy in (swap, kept_y, cot_x, cot_y, cot_relay, *cot_share):
        copy.wait_send()

    def drain(image, _):
        core_copy(image).wait_send()
        x_copy(image).wait_send()
        total_copy(image).wait_send()
        y_copy(image).wait_send()
        relay_copy(image).wait_send()
        return 0

    lax.fori_loop(0, images, drain, 0)
    await_hops(2)
    for step in range(3):
        for way in range(2):

            @pl.when(hop_goes(step, way))
            def _():
                for copy in hop(step, way):
                    copy.wait_send()

    for copy in (*own_copies, *outs):
        copy.wait()


def run_forward(tok, gain1, shift1, gain2, shift2, qkv_w, out_w, up, down, cot, kept):
    images = tok.shape[0]
    rows = images * PITCH
    features = tok.shape[2]
    share = out_w.shape[0]
    heads = share // HD
    hidden = up.shape[1]
    wide = features // 2
    vmem = pl.BlockSpec(memory_space=pltpu.VMEM)
    anywhere = pl.BlockSpec(memory_space=pl.ANY)
    shape = jax.ShapeDtypeStruct
    block = (images, PITCH, wide)
    dma = pltpu.SemaphoreType.DMA
    return pl.pallas_call(
        partial(forward_kernel, images=images, heads=heads),
        out_shape=[
            shape((images, PITCH, share), bf16),
            shape((images, PITCH, share), bf16),
            shape((images, PITCH, share), bf16),
            shape((images, PITCH, share), bf16),
            shape((images, PITCH, 128), f32),
            shape((images, PITCH, features), f32),
            shape((2 * rows, features), bf16),
            shape((2 * rows, features), bf16),
            shape((2 * rows, 128), bf16),
            shape((2, features, 2 * hidden), bf16),
            shape((2, 2 * hidden, features), bf16),
        ],
        in_specs=[vmem] * 7 + [anywhere] * 2 + [vmem] * 2,
        out_specs=[vmem] * 6 + [anywhere] * 5,
        scratch_shapes=[
            pltpu.VMEM((2 * rows, features), bf16),
            pltpu.VMEM((2 * rows, features), bf16),
            pltpu.VMEM((2 * rows, 128), bf16),
            pltpu.VMEM((PITCH, features), f32),
            pltpu.VMEM(block, f32),
            pltpu.VMEM(block, bf16),
            pltpu.VMEM(block, bf16),
            pltpu.VMEM(block, bf16),
            pltpu.VMEM(block, bf16),
            pltpu.VMEM(block, bf16),
            pltpu.VMEM(block, bf16),
            pltpu.VMEM((rows, share), bf16),
        ]
        + [dma((images,))] * 10
        + [dma((2, 3, 2))] * 2
        + [dma((8,))] * 2
        + [dma((5,))],
        compiler_params=pltpu.CompilerParams(
            collective_id=1, has_side_effects=True, vmem_limit_bytes=60 << 20
        ),
    )(tok, gain1, shift1, gain2, shift2, qkv_w, out_w, up, down, cot, kept)


def expert_kernel(
    h_ref,
    cot_ref,
    up_ref,
    down_ref,
    kept_ref,
    router_ref,
    mixed_ref,
    grad_h_ref,
    grad_up_ref,
    grad_down_ref,
    grad_router_ref,
    up_sum,
    down_sum,
    *,
    experts,
    block,
):
    pairs = up_ref.shape[0]
    hidden = up_ref.shape[2] // 2
    lane = lax.broadcasted_iota(jnp.int32, (block, 128), 1)
    up_sum[...] = jnp.zeros_like(up_sum)
    down_sum[...] = jnp.zeros_like(down_sum)
    grad_router_ref[...] = jnp.zeros_like(grad_router_ref)

    def per_block(number, _):
        at = pl.ds(pl.multiple_of(number * block, block), block)
        h_rows, cot_rows = h_ref[at, :], cot_ref[at, :]
        h_turned, cot_turned = h_rows.T, cot_rows.T
        logits = jnp.where(lane < experts, dot(h_rows, router_ref[...]), -1e30)
        powers = jnp.exp(logits - jnp.max(logits, axis=1, keepdims=True))
        probs = powers / jnp.sum(powers, axis=1, keepdims=True)
        kept = kept_ref[at, :].astype(f32)
        gates = kept * probs
        grad_gate = jnp.zeros((block, 128), f32)
        mixed = grad_h = 0.0
        for pair in range(pairs):
            pre_act = dot(h_rows, up_ref[pair])
            back = dot(cot_rows, down_ref[pair], ((1,), (1,)))
            normal_cdf = 0.5 + 0.5 * lax.erf(pre_act * 0.7071067811865476)
            gelu = pre_act * normal_cdf
            slope = normal_cdf + pre_act * (0.3989422804014327 * jnp.exp(-0.5 * pre_act * pre_act))
            product = gelu * back
            spread = []
            for side in range(2):
                expert = 2 * pair + side
                part = jnp.sum(product[:, side * hidden : (side + 1) * hidden], axis=1, keepdims=True)
                grad_gate = jnp.where(lane == expert, part, grad_gate)
                spread.append(jnp.broadcast_to(gates[:, expert : expert + 1], (block, hidden)))
            gate = jnp.concatenate(spread, axis=1)
            hidden_rows = (gelu * gate).astype(bf16)
            grad_pre = (slope * back * gate).astype(bf16)
            mixed += dot(hidden_rows, down_ref[pair])
            grad_h += dot(grad_pre, up_ref[pair], ((1,), (1,)))
            up_sum[pair] += dot(h_turned, grad_pre)
            down_sum[pair] += dot(cot_turned, hidden_rows)
        grad_gate = kept * grad_gate
        grad_logits = (
            probs * (grad_gate - jnp.sum(probs * grad_gate, axis=1, keepdims=True))
        ).astype(bf16)
        mixed_ref[at, :] = mixed.astype(bf16)
        grad_h_ref[at, :] = (grad_h + dot(grad_logits, router_ref[...], ((1,), (1,)))).astype(bf16)
        grad_router_ref[...] += dot(h_turned, grad_logits)
        return 0

    lax.fori_loop(0, h_ref.shape[0] // block, per_block, 0)
    grad_up_ref[...] = up_sum[...].astype(bf16)
    grad_down_ref[...] = down_sum[...].astype(bf16)


def run_experts(h_rows, cot_rows, up, down, kept, router, experts):
    rows, features = h_rows.shape
    pairs, _, width = up.shape
    vmem = pl.BlockSpec(memory_space=pltpu.VMEM)
    shape = jax.ShapeDtypeStruct
    return pl.pallas_call(
        partial(expert_kernel, experts=experts, block=256),
        out_shape=[
            shape((rows, features), bf16),
            shape((rows, features), bf16),
            shape((pairs, features, width), bf16),
            shape((pairs, features, width), bf16),
            shape((features, 128), f32),
        ],
        in_specs=[vmem] * 6,
        out_specs=[vmem] * 5,
        scratch_shapes=[pltpu.VMEM((pairs, features, width), f32)] * 2,
        compiler_params=pltpu.CompilerParams(vmem_limit_bytes=60 << 20),
    )(h_rows, cot_rows, up, down, kept, router)


def per_image(rows_in):
    images = rows_in.shape[0] // SEQ
    blocks = rows_in.reshape(images, SEQ, rows_in.shape[1])
    return jnp.pad(blocks, ((0, 0), (0, PITCH - SEQ), (0, 0)))


def unpad(blocks):
    images = blocks.shape[0]
    return blocks[:, :SEQ].reshape(images * SEQ, blocks.shape[2])


def per_device_dense(
    tokens,
    gain_attn,
    shift_attn,
    qkv_weight,
    out_weight,
    gain_moe,
    shift_moe,
    router_weight,
    expert_up,
    expert_down,
    routes,
    keep_mask,
    cotangent,
):
    row_count, feature_count = tokens.shape
    images = row_count // SEQ
    rows = images * PITCH
    tensor_count = lax.axis_size("tensor")
    expert_count = lax.axis_size("expert")
    tensor_here = lax.axis_index("tensor")
    expert_here = lax.axis_index("expert")
    quarter_width = feature_count // tensor_count
    experts_all = router_weight.shape[1]
    hidden = expert_up.shape[2]
    chosen = routes[:, :, None] == jnp.arange(128, dtype=jnp.int32)[None, None, :]
    kept = jnp.sum(jnp.where(chosen, keep_mask[:, :, None], 0), axis=1).astype(bf16)
    router_wide = jnp.pad(router_weight, ((0, 0), (0, 128 - experts_all)))
    tok = per_image(tokens)
    queries, keys, values, attended, lse, resid, h_all, cot_all, kept_all, up_all, down_all = run_forward(
        tok,
        gain_attn[None],
        shift_attn[None],
        gain_moe[None],
        shift_moe[None],
        qkv_weight,
        out_weight,
        expert_up[0],
        expert_down[0],
        per_image(cotangent).reshape(rows, quarter_width),
        per_image(kept).reshape(rows, 128),
    )
    mixed_part, grad_h_part, grad_up, grad_down, grad_router = run_experts(
        h_all, cot_all, up_all, down_all, kept_all, router_wide, experts_all
    )
    y_groups = [[2 * z, 2 * z + 1] for z in range(expert_count // 2)]
    z_groups = [[2 * z + y for z in range(expert_count // 2)] for y in range(2)]
    grad_h_rows = lax.psum(
        lax.psum_scatter(grad_h_part, "expert", scatter_dimension=0, axis_index_groups=y_groups, tiled=True),
        "tensor",
    ).astype(f32)
    mixed_sum = lax.psum_scatter(
        lax.psum_scatter(mixed_part, "expert", scatter_dimension=0, axis_index_groups=y_groups, tiled=True),
        "tensor",
        scatter_dimension=1,
        tiled=True,
    ).astype(f32)

    def to_owner(grads):
        apart = grads.reshape(2, feature_count, 2, hidden).transpose(0, 2, 1, 3)
        apart = apart.reshape(experts_all * feature_count, hidden)
        return lax.psum_scatter(
            apart, "expert", scatter_dimension=0, axis_index_groups=z_groups, tiled=True
        ).astype(f32)

    grad_up = to_owner(grad_up)
    grad_down = to_owner(grad_down).T
    resid = resid.reshape(rows, feature_count)
    resid_part = lax.dynamic_slice_in_dim(resid, tensor_here * quarter_width, quarter_width, 1)
    mixed = (resid_part + mixed_sum).astype(bf16)
    norm_out, norm_back = jax.vjp(norm_rows, resid, gain_moe, shift_moe)
    grad_resid_norm, grad_gain_moe, grad_shift_moe = norm_back(grad_h_rows)
    cot_mine = lax.dynamic_slice_in_dim(cot_all, expert_here % 2 * rows, rows, 0)
    grad_resid = unpad((cot_mine.astype(f32) + grad_resid_norm).reshape(images, PITCH, feature_count))
    head_count = qkv_weight.shape[2] // HD
    tokens_float = tokens.astype(f32)
    h_one = norm_rows(tokens_float, gain_attn, shift_attn).astype(bf16)
    by_head = (images, SEQ, head_count, HD)
    log_total = lse[:, :SEQ, :head_count].transpose(0, 2, 1)[..., None]
    saved = (
        unpad(attended),
        unpad(queries).reshape(by_head),
        unpad(keys).reshape(by_head),
        unpad(values).reshape(by_head),
        log_total,
    )
    grad_qkv, grad_out, grad_h_one_part = attention_backward(
        grad_resid.astype(bf16), saved, h_one, qkv_weight, out_weight
    )
    grad_h_one = lax.psum(grad_h_one_part.astype(bf16), "tensor").astype(f32)
    norm_one_out, norm_one_back = jax.vjp(norm_rows, tokens_float, gain_attn, shift_attn)
    grad_tok_norm, grad_gain_attn, grad_shift_attn = norm_one_back(grad_h_one)
    grad_tokens = grad_resid + grad_tok_norm
    grad_qkv, grad_out = lax.psum((grad_qkv.astype(bf16), grad_out.astype(bf16)), "expert")
    small = lax.psum((grad_gain_attn, grad_shift_attn, grad_gain_moe, grad_shift_moe), "expert")
    grad_router = lax.psum(grad_router[:, :experts_all], ("expert", "tensor"))
    return (
        unpad(mixed.reshape(images, PITCH, quarter_width)),
        grad_tokens,
        small[0],
        small[1],
        grad_qkv.astype(f32),
        grad_out.astype(f32),
        small[2],
        small[3],
        grad_router,
        grad_up[None],
        grad_down[None],
    )


def per_device(*arguments):
    router_weight = arguments[7]
    if router_weight.shape[1] <= 4:
        return per_device_dense(*arguments)
    return per_device_routed(*arguments)


def solution(mesh):
    placed = (
        P("expert", None),
        P(),
        P(),
        P(None, None, "tensor"),
        P("tensor", None),
        P(),
        P(),
        P(),
        P("expert", None, "tensor"),
        P("expert", "tensor", None),
        P("expert", None),
        P("expert", None),
        P("expert", "tensor"),
    )
    return jax.shard_map(
        per_device,
        mesh=mesh,
        in_specs=placed,
        out_specs=(
            P("expert", "tensor"),
            P("expert", None),
            P(),
            P(),
            P(None, None, "tensor"),
            P("tensor", None),
            P(),
            P(),
            P(),
            P("expert", None, "tensor"),
            P("expert", "tensor", None),
        ),
        check_vma=False,
    )
```

```python
from functools import partial

import jax
import jax.numpy as jnp
from jax import lax
from jax.experimental import pallas as pl
from jax.experimental.pallas import tpu as pltpu
from jax.sharding import PartitionSpec as P

HD = 64
SEQ = 197


norm_epsilon = 1e-06


def norm_rows(values, gain, shift):
    row_mean = jnp.mean(values, axis=-1, keepdims=True)
    centred = values - row_mean
    spread = jnp.mean(centred * centred, axis=-1, keepdims=True)
    return centred * lax.rsqrt(spread + norm_epsilon) * gain + shift


def gelu_exact(values):
    return jax.nn.gelu(values, approximate=False)


def gate_from_logits(logit_rows, picked_rows, keep_rows):
    router_probs = jax.nn.softmax(logit_rows, axis=-1)
    return jnp.sum(jnp.where(picked_rows, router_probs[:, None, :], 0.0), axis=-1) * keep_rows


def attention_forward(h_rows, qkv_w, out_w):
    row_total_count = h_rows.shape[0]
    head_count = qkv_w.shape[2] // HD
    image_count = row_total_count // SEQ
    score_scale = HD ** (-0.5)
    projected = jnp.einsum("td,cdf->ctf", h_rows, qkv_w, preferred_element_type=jnp.float32).astype(
        jnp.bfloat16
    )
    split_heads = projected.reshape(3, image_count, SEQ, head_count, HD)
    queries = split_heads[0]
    keys_all = split_heads[1]
    values_all = split_heads[2]
    scores = (
        jnp.einsum("gqhe,gkhe->ghqk", queries, keys_all, preferred_element_type=jnp.float32)
        * score_scale
    )
    row_peak = jnp.max(scores, axis=-1, keepdims=True)
    exp_scores = jnp.exp(scores - row_peak)
    row_total = jnp.sum(exp_scores, axis=-1, keepdims=True)
    log_total = row_peak + jnp.log(row_total)
    weights = (exp_scores / row_total).astype(jnp.bfloat16)
    attended = jnp.einsum(
        "ghqk,gkhe->gqhe", weights, values_all, preferred_element_type=jnp.float32
    ).astype(jnp.bfloat16)
    attended = attended.reshape(row_total_count, head_count * HD)
    partial_out = jnp.dot(attended, out_w, preferred_element_type=jnp.float32)
    return (partial_out, (attended, queries, keys_all, values_all, log_total))


def attention_backward(grad_branch, saved, h_rows, qkv_w, out_w):
    attended, queries, keys_all, values_all, log_total = saved
    row_total_count = h_rows.shape[0]
    head_count = qkv_w.shape[2] // HD
    image_count = row_total_count // SEQ
    score_scale = HD ** (-0.5)
    grad_out = jnp.einsum("tc,td->cd", attended, grad_branch, preferred_element_type=jnp.float32)
    grad_attended = jnp.einsum(
        "td,cd->tc", grad_branch, out_w, preferred_element_type=jnp.float32
    ).astype(jnp.bfloat16)
    grad_attended = grad_attended.reshape(image_count, SEQ, head_count, HD)
    scores_again = (
        jnp.einsum("gqhe,gkhe->ghqk", queries, keys_all, preferred_element_type=jnp.float32)
        * score_scale
    )
    probs_again = jnp.exp(scores_again - log_total)
    grad_weights = jnp.einsum(
        "gqhe,gkhe->ghqk", grad_attended, values_all, preferred_element_type=jnp.float32
    )
    grad_scores = (
        probs_again * (grad_weights - jnp.sum(probs_again * grad_weights, axis=-1, keepdims=True))
    ).astype(jnp.bfloat16)
    grad_queries = (
        jnp.einsum("ghqk,gkhe->gqhe", grad_scores, keys_all, preferred_element_type=jnp.float32)
        * score_scale
    )
    grad_keys = (
        jnp.einsum("ghqk,gqhe->gkhe", grad_scores, queries, preferred_element_type=jnp.float32)
        * score_scale
    )
    grad_values = jnp.einsum(
        "ghqk,gqhe->gkhe",
        probs_again.astype(jnp.bfloat16),
        grad_attended,
        preferred_element_type=jnp.float32,
    )
    grad_rows = (
        jnp.stack([grad_queries, grad_keys, grad_values])
        .astype(jnp.bfloat16)
        .reshape(3, row_total_count, head_count * HD)
    )
    grad_qkv = jnp.einsum("td,ctf->cdf", h_rows, grad_rows, preferred_element_type=jnp.float32)
    grad_h_one = jnp.einsum("ctf,cdf->td", grad_rows, qkv_w, preferred_element_type=jnp.float32)
    return (grad_qkv, grad_out, grad_h_one)


def moe_tail(
    grad_h_rows,
    grad_gate_rows,
    grad_out_rows,
    h_two_rows,
    resid_rows,
    gate_back,
    router_weight,
    gain_moe,
    shift_moe,
):
    row_total_count = grad_h_rows.shape[0]
    grad_gate = jnp.sum(grad_gate_rows.reshape(row_total_count, -1, 2), axis=1)
    grad_logits = gate_back(grad_gate)[0].astype(jnp.bfloat16)
    grad_router = jnp.einsum(
        "td,te->de", h_two_rows, grad_logits, preferred_element_type=jnp.float32
    )
    grad_h_two = grad_h_rows + jnp.einsum(
        "te,de->td", grad_logits, router_weight, preferred_element_type=jnp.float32
    )
    norm_out, norm_back = jax.vjp(norm_rows, resid_rows, gain_moe, shift_moe)
    grad_resid_norm, grad_gain_moe, grad_shift_moe = norm_back(grad_h_two)
    return (grad_out_rows + grad_resid_norm, grad_router, grad_gain_moe, grad_shift_moe)


def per_device_routed(
    tokens,
    gain_attn,
    shift_attn,
    qkv_weight,
    out_weight,
    gain_moe,
    shift_moe,
    router_weight,
    expert_up,
    expert_down,
    routes,
    keep_mask,
    cotangent,
):
    row_count, feature_count = tokens.shape
    tensor_count = lax.axis_size("tensor")
    expert_count = lax.axis_size("expert")
    tensor_here = lax.axis_index("tensor")
    quarter_width = feature_count // tensor_count
    col_start = tensor_here * quarter_width
    experts_all = router_weight.shape[1]
    capacity = max(2, 7 * row_count // (2 * experts_all))
    tokens_float = tokens.astype(jnp.float32)
    h_one = norm_rows(tokens_float, gain_attn, shift_attn).astype(jnp.bfloat16)
    partial_out, saved = attention_forward(h_one, qkv_weight, out_weight)
    branch = lax.psum(partial_out, "tensor")
    resid = tokens_float + branch
    h_two = norm_rows(resid, gain_moe, shift_moe).astype(jnp.bfloat16)
    logits = jnp.dot(h_two, router_weight, preferred_element_type=jnp.float32)
    keep_float = keep_mask.astype(jnp.float32)
    picked = routes[:, :, None] == jnp.arange(experts_all, dtype=jnp.int32)[None, None, :]
    gate_values, gate_back = jax.vjp(
        partial(gate_from_logits, picked_rows=picked, keep_rows=keep_float), logits
    )
    flat_expert = routes.reshape(-1)
    one_hot = (flat_expert[:, None] == jnp.arange(experts_all, dtype=jnp.int32)[None, :]).astype(
        jnp.int32
    )
    rank_within = jnp.sum((jnp.cumsum(one_hot, axis=0) - one_hot) * one_hot, axis=1)
    slot_index = flat_expert * capacity + rank_within
    token_index = jnp.repeat(jnp.arange(row_count, dtype=jnp.int32), 2)
    live_route = keep_mask.reshape(-1) > 0
    source_table = (
        jnp.full((experts_all * capacity,), row_count, jnp.int32)
        .at[slot_index]
        .set(jnp.where(live_route, token_index, row_count))
    )
    padded_rows = jnp.concatenate([h_two, jnp.zeros((1, feature_count), jnp.bfloat16)], axis=0)
    dispatch = padded_rows[source_table].reshape(experts_all, capacity, feature_count)
    paired = jnp.broadcast_to(dispatch[:, None], (experts_all, 2, capacity, feature_count)).reshape(
        expert_count, capacity, feature_count
    )
    arrived = lax.all_to_all(paired, "expert", split_axis=0, concat_axis=0, tiled=True)
    expert_rows = arrived.reshape(expert_count * capacity, feature_count)
    up_local = expert_up[0]
    down_local = expert_down[0]
    pre_act = jnp.dot(expert_rows, up_local, preferred_element_type=jnp.float32)
    hidden_float, gelu_back = jax.vjp(gelu_exact, pre_act)
    hidden = hidden_float.astype(jnp.bfloat16)
    partial_down = jnp.dot(hidden, down_local, preferred_element_type=jnp.float32)
    summed = lax.psum_scatter(partial_down, "tensor", scatter_dimension=1, tiled=True)
    returned = lax.all_to_all(
        summed.reshape(expert_count, capacity, quarter_width),
        "expert",
        split_axis=0,
        concat_axis=0,
        tiled=True,
    )
    answer_table = jnp.sum(
        returned.reshape(experts_all, 2, capacity, quarter_width), axis=1
    ).astype(jnp.bfloat16)
    answers = (
        answer_table.reshape(experts_all * capacity, quarter_width)[slot_index]
        .astype(jnp.float32)
        .reshape(row_count, 2, quarter_width)
    )
    resid_part = lax.dynamic_slice_in_dim(resid, col_start, quarter_width, 1)
    mixed = (resid_part + jnp.sum(gate_values[:, :, None] * answers, axis=1)).astype(jnp.bfloat16)
    grad_part = cotangent.astype(jnp.float32)
    grad_answers = (
        (gate_values[:, :, None] * grad_part[:, None, :])
        .astype(jnp.bfloat16)
        .reshape(2 * row_count, quarter_width)
    )
    grad_gate_part = jnp.sum(grad_part[:, None, :] * answers, axis=-1)
    outgoing = (
        jnp.zeros((experts_all * capacity, quarter_width), jnp.bfloat16)
        .at[slot_index]
        .set(grad_answers)
    )
    outgoing = jnp.broadcast_to(
        outgoing.reshape(experts_all, 1, capacity, quarter_width),
        (experts_all, 2, capacity, quarter_width),
    ).reshape(expert_count, capacity, quarter_width)
    incoming = lax.all_to_all(outgoing, "expert", split_axis=0, concat_axis=0, tiled=True)
    grad_full = lax.all_gather(incoming, "tensor", axis=2, tiled=True).reshape(
        expert_count * capacity, feature_count
    )
    grad_hidden = jnp.einsum("rd,fd->rf", grad_full, down_local, preferred_element_type=jnp.float32)
    grad_pre = gelu_back(grad_hidden)[0].astype(jnp.bfloat16)
    grad_down = jnp.einsum("rf,rd->fd", hidden, grad_full, preferred_element_type=jnp.float32)
    grad_up = jnp.einsum("rd,rf->df", expert_rows, grad_pre, preferred_element_type=jnp.float32)
    grad_rows_partial = jnp.einsum(
        "rf,df->rd", grad_pre, up_local, preferred_element_type=jnp.float32
    )
    grad_rows_sum = lax.psum_scatter(
        grad_rows_partial.astype(jnp.bfloat16), "tensor", scatter_dimension=1, tiled=True
    ).astype(jnp.float32)
    sent_back = lax.all_to_all(
        grad_rows_sum.reshape(expert_count, capacity, quarter_width).astype(jnp.bfloat16),
        "expert",
        split_axis=0,
        concat_axis=0,
        tiled=True,
    ).astype(jnp.float32)
    grad_table = jnp.sum(sent_back.reshape(experts_all, 2, capacity, quarter_width), axis=1).astype(
        jnp.bfloat16
    )
    grad_inputs = (
        grad_table.reshape(experts_all * capacity, quarter_width)[slot_index]
        .astype(jnp.float32)
        .reshape(row_count, 2, quarter_width)
    )
    grad_h_part = jnp.sum(grad_inputs * keep_float[:, :, None], axis=1)
    grad_h_full, grad_gate_all, grad_out_full = (
        lax.all_gather(grad_h_part, "tensor", axis=1, tiled=True),
        lax.all_gather(grad_gate_part, "tensor", axis=1, tiled=True),
        lax.all_gather(grad_part, "tensor", axis=1, tiled=True),
    )
    grad_resid, grad_router, grad_gain_moe, grad_shift_moe = moe_tail(
        grad_h_full,
        grad_gate_all,
        grad_out_full,
        h_two,
        resid,
        gate_back,
        router_weight,
        gain_moe,
        shift_moe,
    )
    grad_qkv, grad_out, grad_h_one_part = attention_backward(
        grad_resid.astype(jnp.bfloat16), saved, h_one, qkv_weight, out_weight
    )
    grad_h_one = lax.psum(grad_h_one_part.astype(jnp.bfloat16), "tensor").astype(jnp.float32)
    norm_one_out, norm_one_back = jax.vjp(norm_rows, tokens_float, gain_attn, shift_attn)
    grad_tok_norm, grad_gain_attn, grad_shift_attn = norm_one_back(grad_h_one)
    grad_tokens = grad_resid + grad_tok_norm
    summed_grads = lax.psum(
        (
            grad_gain_attn,
            grad_shift_attn,
            grad_qkv,
            grad_out,
            grad_gain_moe,
            grad_shift_moe,
            grad_router,
        ),
        "expert",
    )
    grad_qkv_mine = summed_grads[2]
    grad_out_mine = summed_grads[3]
    return (
        mixed,
        grad_tokens,
        summed_grads[0],
        summed_grads[1],
        grad_qkv_mine,
        grad_out_mine,
        summed_grads[4],
        summed_grads[5],
        summed_grads[6],
        grad_up[None],
        grad_down[None],
    )


MESH = pl.DeviceIdType.MESH
f32 = jnp.float32
bf16 = jnp.bfloat16
PITCH = 208


def dot(left, right, over=((1,), (0,))):
    return lax.dot_general(left, right, (over, ((), ())), preferred_element_type=f32)


def aligned(start, size):
    return pl.ds(pl.multiple_of(start, 16), size)


def lanes_at(start, size):
    return pl.ds(pl.multiple_of(start, 128), size)


def norm_stats(values):
    row_mean = jnp.mean(values, axis=1, keepdims=True)
    centred = values - row_mean
    inverse = lax.rsqrt(jnp.mean(centred * centred, axis=1, keepdims=True) + norm_epsilon)
    return centred * inverse, inverse


def greet(neighbours):
    barrier = pltpu.get_barrier_semaphore()
    count = 0
    for is_there, device in neighbours:

        @pl.when(is_there)
        def _():
            pl.semaphore_signal(barrier, inc=1, device_id=device, device_id_type=MESH)

        count = count + jnp.where(is_there, 1, 0)
    pl.semaphore_wait(barrier, count)


def head_mask(lane, head):
    return (lane < HD) if head % 2 == 0 else (lane >= HD)


def forward_kernel(
    tok_ref,
    gain1_ref,
    shift1_ref,
    gain2_ref,
    shift2_ref,
    qkv_ref,
    out_w_ref,
    up_ref,
    down_ref,
    cot_ref,
    kept_ref,
    q_ref,
    k_ref,
    v_ref,
    att_ref,
    lse_ref,
    resid_ref,
    h_out,
    cot_out,
    kept_out,
    up_out,
    down_out,
    q_all,
    k_all,
    v_all,
    att_all,
    lse_all,
    resid_all,
    h_all,
    cot_all,
    kept_all,
    part,
    mine,
    core_from,
    core_to,
    x_to,
    x_from,
    total_to,
    total_from,
    cot_core,
    core_s,
    core_r,
    x_s,
    x_r,
    tot_s,
    tot_r,
    y_s,
    y_r,
    rel_s,
    rel_r,
    w_s,
    w_r,
    c_s,
    c_r,
    own_sem,
    cot_sem,
    out_sem,
    *,
    images,
    heads,
):
    expert_at = lax.axis_index("expert")
    tensor_at = lax.axis_index("tensor")
    z_at, y_at = expert_at // 2, expert_at % 2
    z_last = lax.axis_size("expert") // 2 - 1
    x_at, core_at = tensor_at // 2, tensor_at % 2
    other = 1 - core_at
    rows = images * PITCH
    half = rows // 2
    wide = out_w_ref.shape[1] // 2
    hidden = up_ref.shape[1]
    core_dev = (expert_at, tensor_at + 1 - 2 * core_at)
    x_dev = (expert_at, tensor_at + 2 - 4 * x_at)
    y_dev = (expert_at + 1 - 2 * y_at, tensor_at)
    z_up = (expert_at + 2, tensor_at)
    z_down = (expert_at - 2, tensor_at)
    has_up, has_down = z_at < z_last, z_at > 0
    greet([(True, core_dev), (True, x_dev), (True, y_dev), (has_up, z_up), (has_down, z_down)])

    def remote(src, dst, send, recv, device):
        return pltpu.make_async_remote_copy(
            src_ref=src, dst_ref=dst, send_sem=send, recv_sem=recv, device_id=device, device_id_type=MESH
        )

    def slot(expert, plane):
        pair = (expert // 2 + plane // 2) % 2
        return (
            up_out.at[pair, :, lanes_at(expert % 2 * hidden, hidden)],
            down_out.at[pair, aligned(expert % 2 * hidden, hidden), :],
        )

    def hop(step, way):
        expert = z_at - step if way == 0 else z_at + step
        plane = z_at + 1 if way == 0 else z_at - 1
        source = (up_ref, down_ref) if step == 0 else slot(expert, z_at)
        target = slot(expert, plane)
        device = z_up if way == 0 else z_down
        return [remote(source[n], target[n], w_s.at[way, step, n], w_r.at[way, step, n], device) for n in range(2)]

    def hop_goes(step, way):
        if way == 0:
            return (z_at - step >= 0) & has_up
        return (z_at + step <= z_last) & has_down

    def hop_comes(step, way):
        return (z_at - 1 - step >= 0) if way == 0 else (z_at + 1 + step <= z_last)

    def hop_arriving(step, way):
        expert = z_at - 1 - step if way == 0 else z_at + 1 + step
        target = slot(expert, z_at)
        return [remote(target[n], target[n], w_s.at[way, step, n], w_r.at[way, step, n], core_dev) for n in range(2)]

    def start_hops(step):
        for way in range(2):

            @pl.when(hop_goes(step, way))
            def _():
                for copy in hop(step, way):
                    copy.start()

    def await_hops(step):
        for way in range(2):

            @pl.when(hop_comes(step, way))
            def _():
                for copy in hop_arriving(step, way):
                    copy.wait_recv()

    start_hops(0)
    own = slot(z_at, z_at)
    own_copies = [pltpu.make_async_copy((up_ref, down_ref)[n], own[n], own_sem.at[n]) for n in range(2)]
    for copy in own_copies:
        copy.start()

    swap = remote(cot_ref, cot_core, c_s.at[0], c_r.at[0], core_dev)
    swap.start()
    kept_all[pl.ds(0, rows), :] = kept_ref[...]

    def kept_half(side, core):
        return kept_all.at[aligned(side * rows + core * half, half), :]

    kept_y = remote(kept_half(0, core_at), kept_half(1, core_at), c_s.at[7], c_r.at[7], y_dev)
    kept_share = remote(kept_half(1, core_at), kept_half(1, core_at), c_s.at[6], c_r.at[6], core_dev)
    kept_share_in = remote(kept_half(1, other), kept_half(1, other), c_s.at[6], c_r.at[6], core_dev)
    kept_y.start()
    swap.wait_recv()

    @pl.when(core_at == 0)
    def _():
        both = jnp.concatenate([cot_ref[...], cot_core[...]], axis=1)
        cot_all[pl.ds(0, rows), lanes_at(x_at * wide, wide)] = both

    @pl.when(core_at == 1)
    def _():
        both = jnp.concatenate([cot_core[...], cot_ref[...]], axis=1)
        cot_all[pl.ds(0, rows), lanes_at(x_at * wide, wide)] = both

    def block(side, col_side, core):
        return cot_all.at[aligned(side * rows + core * half, half), lanes_at(col_side * wide, wide)]

    def cot_copy(number, source, target, device):
        return remote(source, target, c_s.at[number], c_r.at[number], device)

    mine_block = block(0, x_at, core_at)
    cot_x = cot_copy(1, mine_block, mine_block, x_dev)
    cot_y = cot_copy(2, mine_block, block(1, x_at, core_at), y_dev)
    cot_x.start()
    cot_y.start()
    across_x, across_y, across_both = block(0, 1 - x_at, core_at), block(1, x_at, core_at), block(1, 1 - x_at, core_at)
    cot_x_in = cot_copy(1, across_x, across_x, x_dev)
    cot_y_in = cot_copy(2, across_y, across_y, y_dev)
    relay_y = cot_copy(3, across_x, across_both, y_dev)
    relay_x = cot_copy(3, across_y, across_y, x_dev)
    relay_in = cot_copy(3, across_both, across_both, y_dev)
    cot_share = [
        cot_copy(4, across_x, across_x, core_dev),
        cot_copy(5, across_y, across_y, core_dev),
        cot_copy(8, across_both, across_both, core_dev),
    ]
    arriving = [block(0, 1 - x_at, other), block(1, x_at, other), block(1, 1 - x_at, other)]
    cot_share_in = [cot_copy(number, ref, ref, core_dev) for number, ref in zip((4, 5, 8), arriving)]

    lane = lax.broadcasted_iota(jnp.int32, (PITCH, 2 * HD), 1)
    key_mask = lax.broadcasted_iota(jnp.int32, (PITCH, PITCH), 1) < SEQ
    gain1, shift1 = gain1_ref[...], shift1_ref[...]
    gain2, shift2 = gain2_ref[...], shift2_ref[...]
    my_cols = lanes_at(core_at * wide, wide)
    their_cols = lanes_at(other * wide, wide)

    def attend(image):
        normed, _ = norm_stats(tok_ref[image].astype(f32))
        h_one = (normed * gain1 + shift1).astype(bf16)
        queries = dot(h_one, qkv_ref[0]).astype(bf16)
        keys = dot(h_one, qkv_ref[1]).astype(bf16)
        values = dot(h_one, qkv_ref[2]).astype(bf16)
        q_all[image] = queries
        k_all[image] = keys
        v_all[image] = values
        outs = []
        lse = jnp.zeros((PITCH, 2 * HD), f32)
        for head in range(heads):
            first = head // 2 * 2 * HD
            last = min(first + 2 * HD, heads * HD)
            q_head, k_head, v_head = queries[:, first:last], keys[:, first:last], values[:, first:last]
            if last - first == 2 * HD:
                q_head = jnp.where(head_mask(lane, head), q_head, jnp.zeros_like(q_head))
            scores = dot(q_head, k_head, ((1,), (1,))) * (HD**-0.5)
            scores = jnp.where(key_mask, scores, -1e30)
            peak = jnp.max(scores, axis=1, keepdims=True)
            powers = jnp.exp(scores - peak)
            row_sum = jnp.sum(powers, axis=1, keepdims=True)
            weights = (powers / row_sum).astype(bf16)
            outs.append(dot(weights, v_head))
            lse = jnp.where(lane == head, peak + jnp.log(row_sum), lse)
        lse_all[image] = lse
        joined = []
        for head in range(0, heads, 2):
            if head + 1 < heads:
                joined.append(jnp.where(lane < HD, outs[head], outs[head + 1]))
            else:
                joined.append(outs[head])
        attended = jnp.concatenate(joined, axis=1).astype(bf16)
        att_all[image] = attended
        part[...] = dot(attended, out_w_ref[...])
        mine[image] = part[:, my_cols]
        core_to[image] = part[:, their_cols].astype(bf16)

    def core_copy(image):
        return remote(core_to.at[image], core_from.at[image], core_s.at[image], core_r.at[image], core_dev)

    def x_copy(image):
        return remote(x_to.at[image], x_from.at[image], x_s.at[image], x_r.at[image], x_dev)

    def total_copy(image):
        return remote(total_to.at[image], total_from.at[image], tot_s.at[image], tot_r.at[image], core_dev)

    def h_block(side, image, core):
        return h_all.at[aligned(side * rows + image * PITCH, PITCH), lanes_at(core * wide, wide)]

    def y_copy(image):
        return remote(h_block(0, image, core_at), h_block(1, image, core_at), y_s.at[image], y_r.at[image], y_dev)

    def relay_copy(image):
        ref = h_block(1, image, core_at)
        return remote(ref, ref, rel_s.at[image], rel_r.at[image], core_dev)

    def relay_arriving(image):
        ref = h_block(1, image, other)
        return remote(ref, ref, rel_s.at[image], rel_r.at[image], core_dev)

    attend_outs = ((q_all, q_ref), (k_all, k_ref), (v_all, v_ref), (att_all, att_ref), (lse_all, lse_ref))

    def out_copies(image):
        copies = [
            pltpu.make_async_copy(kept.at[image], out.at[image], out_sem.at[n, image])
            for n, (kept, out) in enumerate(attend_outs)
        ]
        at = aligned(image * PITCH, PITCH)
        return copies, [
            pltpu.make_async_copy(resid_all.at[image], resid_ref.at[at, :], out_sem.at[5, image]),
            pltpu.make_async_copy(h_all.at[at, :], h_out.at[at, :], out_sem.at[6, image]),
        ]

    def other_copy(image):
        at = aligned(rows + image * PITCH, PITCH)
        return pltpu.make_async_copy(h_all.at[at, :], h_out.at[at, :], out_sem.at[7, image])

    def stage(tick, lag, run):
        image = tick - lag

        @pl.when((image >= 0) & (image < images))
        def _():
            run(image)

    def run_attend(image):
        attend(image)
        core_copy(image).start()
        for copy in out_copies(image)[0]:
            copy.start()

    def run_x(image):
        core_copy(image).wait_recv()
        x_to[image] = (mine[image] + core_from[image].astype(f32)).astype(bf16)
        x_copy(image).start()

    def run_total(image):
        x_copy(image).wait_recv()
        total_to[image] = (x_to[image].astype(f32) + x_from[image].astype(f32)).astype(bf16)
        total_copy(image).start()

    def run_norm(image):
        total_copy(image).wait_recv()
        part[:, my_cols] = total_to[image].astype(f32)
        part[:, their_cols] = total_from[image].astype(f32)
        resid = tok_ref[image].astype(f32) + part[...]
        resid_all[image] = resid
        normed, _ = norm_stats(resid)
        h_all[aligned(image * PITCH, PITCH), :] = (normed * gain2 + shift2).astype(bf16)
        y_copy(image).start()
        for copy in out_copies(image)[1]:
            copy.start()

    def run_relay(image):
        y_copy(image).wait_recv()
        relay_copy(image).start()

    def run_end(image):
        relay_arriving(image).wait_recv()
        other_copy(image).start()

    def at_tick(tick, when, run):
        @pl.when(tick == when)
        def _():
            run()

    def cot_step_one():
        cot_x_in.wait_recv()
        cot_share[0].start()

        @pl.when(core_at == 0)
        def _():
            relay_y.start()

        kept_y.wait_recv()
        kept_share.start()

    def cot_step_two():
        cot_y_in.wait_recv()
        cot_share[1].start()

        @pl.when(core_at == 1)
        def _():
            relay_x.start()

    def weights_step_one():
        await_hops(0)
        start_hops(1)

    def cot_step_three():
        relay_in.wait_recv()
        cot_share[2].start()

    def per_tick(tick, _):
        stage(tick, 0, run_attend)
        stage(tick, 1, run_x)
        stage(tick, 4, run_total)
        stage(tick, 5, run_norm)
        stage(tick, 9, run_relay)
        stage(tick, 10, run_end)
        at_tick(tick, 5, cot_step_one)
        at_tick(tick, 7, cot_step_two)
        at_tick(tick, 8, weights_step_one)
        at_tick(tick, 14, cot_step_three)
        return 0

    lax.fori_loop(0, images + 10, per_tick, 0)
    for copy in (*cot_share_in, kept_share_in):
        copy.wait_recv()
    outs = [
        pltpu.make_async_copy(cot_all, cot_out, cot_sem.at[0]),
        pltpu.make_async_copy(kept_all, kept_out, cot_sem.at[1]),
    ]
    for copy in outs:
        copy.start()
    for copy in (swap, kept_y, kept_share, cot_x, cot_y, *cot_share):
        copy.wait_send()

    @pl.when(core_at == 0)
    def _():
        relay_y.wait_send()

    @pl.when(core_at == 1)
    def _():
        relay_x.wait_send()

    def drain(image, _):
        for copy in (core_copy, x_copy, total_copy, y_copy, relay_copy):
            copy(image).wait_send()
        first, second = out_copies(image)
        for copy in (*first, *second, other_copy(image)):
            copy.wait()
        return 0

    lax.fori_loop(0, images, drain, 0)
    await_hops(1)
    for step in range(2):
        for way in range(2):

            @pl.when(hop_goes(step, way))
            def _():
                for copy in hop(step, way):
                    copy.wait_send()

    for copy in (*own_copies, *outs):
        copy.wait()


def run_forward(tok, gain1, shift1, gain2, shift2, qkv_w, out_w, up, down, cot, kept):
    images = tok.shape[0]
    rows = images * PITCH
    features = tok.shape[2]
    share = out_w.shape[0]
    heads = share // HD
    hidden = up.shape[1]
    wide = features // 2
    vmem = pl.BlockSpec(memory_space=pltpu.VMEM)
    anywhere = pl.BlockSpec(memory_space=pl.ANY)
    shape = jax.ShapeDtypeStruct
    block = (images, PITCH, wide)
    dma = pltpu.SemaphoreType.DMA
    return pl.pallas_call(
        partial(forward_kernel, images=images, heads=heads),
        out_shape=[
            shape((images, PITCH, share), bf16),
            shape((images, PITCH, share), bf16),
            shape((images, PITCH, share), bf16),
            shape((images, PITCH, share), bf16),
            shape((images, PITCH, 128), f32),
            shape((rows, features), f32),
            shape((2 * rows, features), bf16),
            shape((2 * rows, features), bf16),
            shape((2 * rows, 128), bf16),
            shape((2, features, 2 * hidden), bf16),
            shape((2, 2 * hidden, features), bf16),
        ],
        in_specs=[vmem] * 7 + [anywhere] * 2 + [vmem] * 2,
        out_specs=[anywhere] * 11,
        scratch_shapes=[
            *[pltpu.VMEM((images, PITCH, share), bf16)] * 4,
            pltpu.VMEM((images, PITCH, 128), f32),
            pltpu.VMEM((images, PITCH, features), f32),
            pltpu.VMEM((2 * rows, features), bf16),
            pltpu.VMEM((2 * rows, features), bf16),
            pltpu.VMEM((2 * rows, 128), bf16),
            pltpu.VMEM((PITCH, features), f32),
            pltpu.VMEM(block, f32),
            pltpu.VMEM(block, bf16),
            pltpu.VMEM(block, bf16),
            pltpu.VMEM(block, bf16),
            pltpu.VMEM(block, bf16),
            pltpu.VMEM(block, bf16),
            pltpu.VMEM(block, bf16),
            pltpu.VMEM((rows, share), bf16),
        ]
        + [dma((images,))] * 10
        + [dma((2, 2, 2))] * 2
        + [dma((9,))] * 2
        + [dma((2,)), dma((2,)), dma((8, images))],
        compiler_params=pltpu.CompilerParams(
            collective_id=1, has_side_effects=True, vmem_limit_bytes=60 << 20
        ),
    )(tok, gain1, shift1, gain2, shift2, qkv_w, out_w, up, down, cot, kept)


def expert_math(h_rows, cot_rows, kept, router, up, down, pair, experts):
    block = h_rows.shape[0]
    hidden = up.shape[1] // 2
    lane = lax.broadcasted_iota(jnp.int32, (block, 128), 1)
    logits = jnp.where(lane < experts, dot(h_rows, router), -1e30)
    powers = jnp.exp(logits - jnp.max(logits, axis=1, keepdims=True))
    probs = powers / jnp.sum(powers, axis=1, keepdims=True)
    gates = kept * probs
    pre_act = dot(h_rows, up)
    back = dot(cot_rows, down, ((1,), (1,)))
    normal_cdf = 0.5 + 0.5 * lax.erf(pre_act * 0.7071067811865476)
    gelu = pre_act * normal_cdf
    slope = normal_cdf + pre_act * (0.3989422804014327 * jnp.exp(-0.5 * pre_act * pre_act))
    product = gelu * back
    grad_gate = jnp.zeros((block, 128), f32)
    spread = []
    for side in range(2):
        chosen = lane == 2 * pair + side
        part = jnp.sum(product[:, side * hidden : (side + 1) * hidden], axis=1, keepdims=True)
        grad_gate = jnp.where(chosen, part, grad_gate)
        gate = jnp.sum(jnp.where(chosen, gates, 0.0), axis=1, keepdims=True)
        spread.append(jnp.broadcast_to(gate, (block, hidden)))
    gate = jnp.concatenate(spread, axis=1)
    hidden_rows = (gelu * gate).astype(bf16)
    grad_pre = (slope * back * gate).astype(bf16)
    return hidden_rows, grad_pre, probs, grad_gate


def first_pair_kernel(
    h_ref,
    cot_ref,
    kept_ref,
    router_ref,
    up_ref,
    down_ref,
    up_all,
    down_all,
    mixed_ref,
    grad_h_ref,
    gate_ref,
    grad_up_ref,
    grad_down_ref,
    up_late,
    down_late,
    up_sum,
    down_sum,
    late_s,
    late_r,
    *,
    experts,
    steps,
):
    expert_at = lax.axis_index("expert")
    tensor_at = lax.axis_index("tensor")
    z_at = expert_at // 2
    hidden = up_late.shape[1]
    partner = (jnp.where(z_at % 2 == 0, expert_at + 2, expert_at - 2), tensor_at)
    inner = (z_at == 1) | (z_at == 2)
    outer = (z_at == 0) | (z_at == 3)
    far = jnp.where(z_at == 1, hidden, 0)
    sources = (up_all.at[1, :, lanes_at(far, hidden)], down_all.at[1, aligned(far, hidden), :])
    hops = [
        pltpu.make_async_remote_copy(
            src_ref=source,
            dst_ref=target,
            send_sem=late_s.at[number],
            recv_sem=late_r.at[number],
            device_id=partner,
            device_id_type=MESH,
        )
        for number, (source, target) in enumerate(zip(sources, (up_late, down_late)))
    ]

    @pl.when(pl.program_id(0) == 0)
    def _():
        greet([(True, partner)])

        @pl.when(inner)
        def _():
            for copy in hops:
                copy.start()

        up_sum[...] = jnp.zeros_like(up_sum)
        down_sum[...] = jnp.zeros_like(down_sum)

    h_rows, cot_rows = h_ref[...], cot_ref[...]
    up, down = up_ref[0], down_ref[0]
    hidden_rows, grad_pre, _, grad_gate = expert_math(
        h_rows, cot_rows, kept_ref[...].astype(f32), router_ref[...], up, down, z_at // 2, experts
    )
    gate_ref[...] = grad_gate
    mixed_ref[...] = dot(hidden_rows, down).astype(bf16)
    grad_h_ref[...] = dot(grad_pre, up, ((1,), (1,))).astype(bf16)
    up_sum[...] += dot(h_rows.T, grad_pre)
    down_sum[...] += dot(cot_rows.T, hidden_rows)

    @pl.when(pl.program_id(0) == steps - 1)
    def _():
        grad_up_ref[...] = up_sum[...].astype(bf16)
        grad_down_ref[...] = down_sum[...].astype(bf16)

        @pl.when(inner)
        def _():
            for copy in hops:
                copy.wait_send()

        @pl.when(outer)
        def _():
            for copy in hops:
                copy.wait_recv()


BLOCK = 2 * PITCH


def run_first_pair(h_rows, cot_rows, kept, router, up, down, experts):
    rows, features = h_rows.shape
    width = up.shape[2]
    steps = rows // BLOCK
    anywhere = pl.BlockSpec(memory_space=pl.ANY)
    shape = jax.ShapeDtypeStruct

    def by_step(lanes):
        return pl.BlockSpec((BLOCK, lanes), lambda n: (n, 0))

    def whole(*dims):
        return pl.BlockSpec(dims, lambda n: (0,) * len(dims))

    return pl.pallas_call(
        partial(first_pair_kernel, experts=experts, steps=steps),
        grid=(steps,),
        out_shape=[
            shape((rows, features), bf16),
            shape((rows, features), bf16),
            shape((rows, 128), f32),
            shape((features, width), bf16),
            shape((features, width), bf16),
            shape((features, width // 2), bf16),
            shape((width // 2, features), bf16),
        ],
        in_specs=[
            by_step(features),
            by_step(features),
            by_step(128),
            whole(features, 128),
            whole(1, features, width),
            whole(1, width, features),
            anywhere,
            anywhere,
        ],
        out_specs=[
            by_step(features),
            by_step(features),
            by_step(128),
            whole(features, width),
            whole(features, width),
            anywhere,
            anywhere,
        ],
        scratch_shapes=[pltpu.VMEM((features, width), f32)] * 2 + [pltpu.SemaphoreType.DMA((2,))] * 2,
        compiler_params=pltpu.CompilerParams(
            collective_id=3, has_side_effects=True, vmem_limit_bytes=60 << 20
        ),
    )(h_rows, cot_rows, kept, router, up, down, up, down)


def turn_is_other(turn):
    return (turn == 0) | ((turn % 2 == 1) & (turn < 7))


def turn_block(turn):
    own = jnp.where(turn == 7, 3, turn // 2 - 1)
    return jnp.where(turn_is_other(turn), 4 + (turn + 1) // 2, own)


def second_pair_kernel(
    h_ref,
    cot_ref,
    kept_ref,
    router_ref,
    mixed_first,
    grad_h_first,
    gate_first,
    up_all,
    down_all,
    up_late,
    down_late,
    mixed_ref,
    grad_up_ref,
    grad_down_ref,
    grad_router_ref,
    grad_h_out,
    up_vm,
    down_vm,
    up_sum,
    down_sum,
    router_sum,
    ring,
    from_core,
    from_y,
    from_x,
    load,
    core_s,
    core_r,
    y_s,
    y_r,
    x_s,
    x_r,
    tot_s,
    tot_r,
    store,
    *,
    experts,
    steps,
):
    turn = pl.program_id(0)
    expert_at = lax.axis_index("expert")
    tensor_at = lax.axis_index("tensor")
    z_at, y_at = expert_at // 2, expert_at % 2
    x_at, core_at = tensor_at // 2, tensor_at % 2
    hidden = up_late.shape[1]
    wide = ring.shape[2] // 2
    core_dev = (expert_at, tensor_at + 1 - 2 * core_at)
    x_dev = (expert_at, tensor_at + 2 - 4 * x_at)
    y_dev = (expert_at + 1 - 2 * y_at, tensor_at)
    my_cols = lanes_at(core_at * wide, wide)
    their_cols = lanes_at((1 - core_at) * wide, wide)

    def remote(src, dst, send, recv, device):
        return pltpu.make_async_remote_copy(
            src_ref=src, dst_ref=dst, send_sem=send, recv_sem=recv, device_id=device, device_id_type=MESH
        )

    def core_copy(number):
        return remote(ring.at[number % 2, :, their_cols], from_core.at[number], core_s.at[number], core_r.at[number], core_dev)

    def y_copy(number, place):
        return remote(from_core.at[number], from_y.at[place], y_s.at[place], y_r.at[place], y_dev)

    def x_copy(number, place):
        return remote(from_core.at[number], from_x.at[place], x_s.at[place], x_r.at[place], x_dev)

    def out_rows(place):
        return grad_h_out.at[aligned(place * BLOCK, BLOCK), my_cols]

    def total_copy(place):
        return remote(from_x.at[place], out_rows(place), tot_s.at[place], tot_r.at[place], core_dev)

    def store_copy(place):
        return pltpu.make_async_copy(from_x.at[place], out_rows(place), store.at[place])

    def own_turn(place):
        return jnp.where(place == 3, 7, 2 * place + 2)

    def other_turn(place):
        return jnp.where(place == 0, 0, 2 * place - 1)

    def pass_other(number):
        core_copy(number).wait_recv()
        total = from_core[number].astype(f32) + ring[number % 2, :, my_cols].astype(f32)
        from_core[number] = total.astype(bf16)
        y_copy(number, (number + 1) // 2).start()

    def pass_own(number, place):
        core_copy(number).wait_recv()
        y_copy(number, place).wait_recv()
        total = from_core[number].astype(f32) + ring[number % 2, :, my_cols].astype(f32) + from_y[place].astype(f32)
        from_core[number] = total.astype(bf16)
        x_copy(number, place).start()

    def pass_total(place):
        number = own_turn(place)
        x_copy(number, place).wait_recv()
        from_x[place] = (from_core[number].astype(f32) + from_x[place].astype(f32)).astype(bf16)
        total_copy(place).start()
        store_copy(place).start()

    @pl.when(turn == 0)
    def _():
        greet([(True, core_dev), (True, x_dev), (True, y_dev)])
        late_expert = jnp.where(z_at == 0, 1, 0)
        late = late_expert * hidden
        is_outer = (z_at == 0) | (z_at == 3)
        whole = [
            pltpu.make_async_copy(up_all.at[1], up_vm, load.at[0]),
            pltpu.make_async_copy(down_all.at[1], down_vm, load.at[1]),
        ]
        for copy in whole:
            copy.start()
        up_sum[...] = jnp.zeros_like(up_sum)
        down_sum[...] = jnp.zeros_like(down_sum)
        router_sum[...] = jnp.zeros_like(router_sum)
        for copy in whole:
            copy.wait()

        @pl.when(is_outer)
        def _():
            parts = [
                pltpu.make_async_copy(up_late, up_vm.at[:, lanes_at(late, hidden)], load.at[0]),
                pltpu.make_async_copy(down_late, down_vm.at[aligned(late, hidden), :], load.at[1]),
            ]
            for copy in parts:
                copy.start()
            for copy in parts:
                copy.wait()

    h_rows, cot_rows = h_ref[...], cot_ref[...]
    up, down, router = up_vm[...], down_vm[...], router_ref[...]
    kept = kept_ref[...].astype(f32)
    hidden_rows, grad_pre, probs, grad_gate = expert_math(
        h_rows, cot_rows, kept, router, up, down, 1 - z_at // 2, experts
    )
    grad_gate = kept * (grad_gate + gate_first[...])
    grad_logits = (probs * (grad_gate - jnp.sum(probs * grad_gate, axis=1, keepdims=True))).astype(bf16)

    before = turn - 1

    @pl.when((turn >= 1) & turn_is_other(before))
    def _():
        pass_other(before)

    @pl.when((turn == 5) | (turn == 7))
    def _():
        pass_total((turn - 5) // 2)

    @pl.when((turn == 3) | (turn == 5) | (turn == 7))
    def _():
        pass_own(before, (turn - 3) // 2)

    mixed_ref[...] = (mixed_first[...].astype(f32) + dot(hidden_rows, down)).astype(bf16)

    @pl.when(turn >= 2)
    def _():
        core_copy(turn - 2).wait_send()

    ring[turn % 2] = (
        grad_h_first[...].astype(f32) + dot(grad_pre, up, ((1,), (1,))) + dot(grad_logits, router, ((1,), (1,)))
    ).astype(bf16)
    core_copy(turn).start()
    h_turned = h_rows.T
    up_sum[...] += dot(h_turned, grad_pre)
    router_sum[...] += dot(h_turned, grad_logits)
    down_sum[...] += dot(cot_rows.T, hidden_rows)

    @pl.when(turn == steps - 1)
    def _():
        pass_own(7, 3)
        pass_total(2)
        grad_up_ref[...] = up_sum[...].astype(bf16)
        grad_down_ref[...] = down_sum[...].astype(bf16)
        grad_router_ref[...] = router_sum[...].T[:8]
        pass_total(3)
        for number in (6, 7):
            core_copy(number).wait_send()
        for place in range(4):
            y_copy(other_turn(place), place).wait_send()
            x_copy(own_turn(place), place).wait_send()
            total_copy(place).wait_send()
            total_copy(place).wait_recv()
            store_copy(place).wait()


def run_second_pair(
    h_rows, cot_rows, kept, router, mixed_first, grad_h_first, gate_first, up, down, up_late, down_late, experts
):
    rows, features = h_rows.shape
    width = up.shape[2]
    steps = rows // BLOCK
    half = (BLOCK, features // 2)
    anywhere = pl.BlockSpec(memory_space=pl.ANY)
    shape = jax.ShapeDtypeStruct
    dma = pltpu.SemaphoreType.DMA

    def by_step(lanes):
        return pl.BlockSpec((BLOCK, lanes), lambda n: (turn_block(n), 0))

    def whole(*dims):
        return pl.BlockSpec(dims, lambda n: (0,) * len(dims))

    return pl.pallas_call(
        partial(second_pair_kernel, experts=experts, steps=steps),
        grid=(steps,),
        out_shape=[
            shape((rows, features), bf16),
            shape((features, width), bf16),
            shape((features, width), bf16),
            shape((8, features), f32),
            shape((rows // 2, features), bf16),
        ],
        in_specs=[
            by_step(features),
            by_step(features),
            by_step(128),
            whole(features, 128),
            by_step(features),
            by_step(features),
            by_step(128),
        ]
        + [anywhere] * 4,
        out_specs=[by_step(features), whole(features, width), whole(features, width), whole(8, features), anywhere],
        scratch_shapes=[
            pltpu.VMEM((features, width), bf16),
            pltpu.VMEM((width, features), bf16),
            pltpu.VMEM((features, width), f32),
            pltpu.VMEM((features, width), f32),
            pltpu.VMEM((features, 128), f32),
            pltpu.VMEM((2, BLOCK, features), bf16),
            pltpu.VMEM((8, *half), bf16),
            pltpu.VMEM((4, *half), bf16),
            pltpu.VMEM((4, *half), bf16),
            dma((2,)),
        ]
        + [dma((8,))] * 2
        + [dma((4,))] * 7,
        compiler_params=pltpu.CompilerParams(
            collective_id=4, has_side_effects=True, vmem_limit_bytes=60 << 20
        ),
    )(h_rows, cot_rows, kept, router, mixed_first, grad_h_first, gate_first, up, down, up_late, down_late)


def backward_kernel(
    tok_ref,
    gain1_ref,
    shift1_ref,
    gain2_ref,
    qkv_ref,
    out_w_ref,
    q_ref,
    k_ref,
    v_ref,
    att_ref,
    lse_ref,
    grad_h_ref,
    grad_router_ref,
    resid_ref,
    cot_ref,
    mixed_ref,
    up_first,
    up_second,
    down_first,
    down_second,
    up_out,
    down_out,
    tokens_out,
    weights_out,
    mixed_out,
    rows_kept,
    cot_rows,
    m_mine,
    m_core,
    m_y,
    m_x,
    m_out,
    m_resid,
    own_vm,
    one_mine,
    one_to,
    one_core,
    one_x,
    one_total,
    line,
    weight_sum,
    weight_half,
    shared,
    shared_y,
    shared_line,
    shared_all,
    route_core,
    route_x,
    whole,
    mc_s,
    mc_r,
    my_s,
    my_r,
    mx_s,
    mx_r,
    mq_s,
    mq_r,
    m_store,
    oc_s,
    oc_r,
    ox_s,
    ox_r,
    ot_s,
    ot_r,
    l_s,
    l_r,
    sy_s,
    sy_r,
    sl_s,
    sl_r,
    sg_s,
    sg_r,
    sz_s,
    sz_r,
    r_s,
    r_r,
    load,
    own_sem,
    weight_store,
    store,
    *,
    images,
    heads,
):
    expert_at = lax.axis_index("expert")
    tensor_at = lax.axis_index("tensor")
    z_at, y_at = expert_at // 2, expert_at % 2
    z_last = lax.axis_size("expert") // 2 - 1
    x_at, core_at = tensor_at // 2, tensor_at % 2
    other = 1 - core_at
    rows = images * PITCH
    features = tok_ref.shape[2]
    wide = features // 2
    share = out_w_ref.shape[0]
    hidden = line.shape[4]
    core_dev = (expert_at, tensor_at + 1 - 2 * core_at)
    x_dev = (expert_at, tensor_at + 2 - 4 * x_at)
    y_dev = (expert_at + 1 - 2 * y_at, tensor_at)
    z_devs = [(expert_at + 2, tensor_at), (expert_at - 2, tensor_at)]
    has_up, has_down = z_at < z_last, z_at > 0
    greet([(True, core_dev), (True, x_dev), (True, y_dev), (has_up, z_devs[0]), (has_down, z_devs[1])])
    my_cols = lanes_at(core_at * wide, wide)
    their_cols = lanes_at(other * wide, wide)

    def remote(src, dst, send, recv, device):
        return pltpu.make_async_remote_copy(
            src_ref=src, dst_ref=dst, send_sem=send, recv_sem=recv, device_id=device, device_id_type=MESH
        )

    def at_image(image):
        return aligned(image * PITCH, PITCH)

    part_count = m_y.shape[0]
    part_rows_m = rows // part_count

    def m_rows(side, part):
        return aligned(side * rows + part * part_rows_m, part_rows_m)

    def m_core_copy(side, part):
        at = m_rows(side, part)
        return remote(mixed_ref.at[at, their_cols], m_core.at[at, :], mc_s.at[side, part], mc_r.at[side, part], core_dev)

    for part in range(part_count):
        m_core_copy(1, part).start()
    for part in range(part_count):
        m_core_copy(0, part).start()
    loads = [
        pltpu.make_async_copy(resid_ref, rows_kept, load.at[0]),
        pltpu.make_async_copy(cot_ref.at[pl.ds(0, rows), :], cot_rows, load.at[1]),
        pltpu.make_async_copy(mixed_ref.at[:, my_cols], m_mine, load.at[2]),
    ]
    for copy in loads:
        copy.start()
    route_one = remote(grad_router_ref, route_core, r_s.at[0], r_r.at[0], core_dev)
    route_one.start()

    def place(way):
        return z_at if way == 0 else z_last - z_at

    def expert_of(step, at, way):
        mirrored = z_last - step + at
        return mirrored if way == 0 else z_last - mirrored

    def with_own(expert, run):
        lanes = lanes_at(expert % 2 * hidden, hidden)
        is_first = expert // 2 == z_at // 2

        @pl.when(is_first)
        def _():
            run([part.at[:, lanes] for part in (up_first, down_first)])

        @pl.when(jnp.logical_not(is_first))
        def _():
            run([part.at[:, lanes] for part in (up_second, down_second)])

    def load_own(expert):
        def load_from(sources):
            copies = [pltpu.make_async_copy(sources[n], own_vm.at[n], own_sem.at[n]) for n in range(2)]
            for copy in copies:
                copy.start()
            for copy in copies:
                copy.wait()

        with_own(expert, load_from)

    def line_copy(source, step, way, number):
        return remote(
            source, line.at[way, step, number], l_s.at[way, step, number], l_r.at[way, step, number], z_devs[way]
        )

    def line_send(step):
        for way in range(2):
            at = place(way)

            @pl.when(at == 0)
            def _():
                def send_from(sources):
                    for number in range(2):
                        line_copy(sources[number], step, way, number).start()

                with_own(expert_of(step, at, way), send_from)

            if step > 0:

                @pl.when((at > 0) & (at <= step) & (at < z_last))
                def _():
                    for number in range(2):
                        line_copy(line.at[way, step - 1, number], step, way, number).start()

    def line_await(step):
        for way in range(2):
            at = place(way)

            @pl.when((at > 0) & (at - 1 <= step))
            def _():
                for number in range(2):
                    line_copy(line.at[way, step, number], step, way, number).wait_recv()

    def line_add(step):
        for way in range(2):
            at = place(way)

            @pl.when((at > 0) & (at - 1 <= step))
            def _():
                load_own(expert_of(step, at - 1, way))
                for number in range(2):

                    def add(piece, _):
                        at_rows = aligned(piece * 96, 96)
                        total = line[way, step, number, at_rows, :].astype(f32) + own_vm[number, at_rows, :].astype(f32)
                        line[way, step, number, at_rows, :] = total.astype(bf16)
                        return 0

                    lax.fori_loop(0, features // 96, add, 0)

    line_send(0)
    for copy in loads:
        copy.wait()
    weight_sum[...] = jnp.zeros_like(weight_sum)

    def m_y_copy(part):
        return remote(m_core.at[m_rows(1, part), :], m_y.at[part], my_s.at[part], my_r.at[part], y_dev)

    def m_x_copy(part):
        return remote(m_core.at[m_rows(0, part), :], m_x.at[part], mx_s.at[part], mx_r.at[part], x_dev)

    def m_place(part):
        return mixed_out.at[aligned(part * part_rows_m, part_rows_m), :]

    def m_quarter_copy(part):
        return remote(m_out.at[part, other], m_place(part), mq_s.at[part], mq_r.at[part], core_dev)

    def m_store_copy(part):
        return pltpu.make_async_copy(m_out.at[part, core_at], m_place(part), m_store.at[part])

    def m_resid_copy(part):
        at = aligned(part * part_rows_m, part_rows_m)
        return pltpu.make_async_copy(resid_ref.at[at, lanes_at(x_at * wide, wide)], m_resid, load.at[3])

    keeps = x_at == core_at

    def run_m_y(part):
        m_core_copy(1, part).wait_recv()
        at = m_rows(1, part)
        m_core[at, :] = (m_core[at, :].astype(f32) + m_mine[at, :].astype(f32)).astype(bf16)
        m_y_copy(part).start()

    def run_m_x(part):
        m_core_copy(0, part).wait_recv()
        m_y_copy(part).wait_recv()
        at = m_rows(0, part)
        total = m_core[at, :].astype(f32) + m_mine[at, :].astype(f32) + m_y[part].astype(f32)
        m_core[at, :] = total.astype(bf16)

        @pl.when(jnp.logical_not(keeps))
        def _():
            m_x_copy(part).start()

    def run_m_out(part):
        @pl.when(keeps)
        def _():
            m_resid_copy(part).start()
            m_x_copy(part).wait_recv()
            m_resid_copy(part).wait()
            total = m_core[m_rows(0, part), :].astype(f32) + m_x[part].astype(f32)
            mixed = (m_resid[...] + total).astype(bf16)
            m_out[part, 0] = mixed[:, : wide // 2]
            m_out[part, 1] = mixed[:, wide // 2 :]
            m_quarter_copy(part).start()
            m_store_copy(part).start()

    for part in range(part_count):
        run_m_y(part)
    route_one.wait_recv()
    route_core[...] += grad_router_ref[...]
    route_two = remote(route_core, route_x, r_s.at[1], r_r.at[1], x_dev)
    route_two.start()

    def one_core_copy(image):
        return remote(one_to.at[image], one_core.at[image], oc_s.at[image], oc_r.at[image], core_dev)

    def one_x_copy(image):
        return remote(one_core.at[image], one_x.at[image], ox_s.at[image], ox_r.at[image], x_dev)

    def one_total_copy(image):
        return remote(one_x.at[image], one_total.at[image], ot_s.at[image], ot_r.at[image], core_dev)

    def store_copy(image):
        return pltpu.make_async_copy(rows_kept.at[at_image(image), :], tokens_out.at[at_image(image), :], store.at[image])

    lane = lax.broadcasted_iota(jnp.int32, (PITCH, 2 * HD), 1)
    key_mask = lax.broadcasted_iota(jnp.int32, (PITCH, PITCH), 1) < SEQ
    gain1, shift1, gain2 = gain1_ref[...], shift1_ref[...], gain2_ref[...]

    def norm_back(grad, gain, normed, inverse):
        scaled = grad * gain
        mean = jnp.mean(scaled, axis=1, keepdims=True)
        along = jnp.mean(scaled * normed, axis=1, keepdims=True)
        return (scaled - mean - normed * along) * inverse

    def add_sums(row, grad, normed):
        weight_sum[features + row : features + row + 1, :] += jnp.sum(grad * normed, axis=0, keepdims=True)
        weight_sum[features + row + 1 : features + row + 2, :] += jnp.sum(grad, axis=0, keepdims=True)

    def run_attention(image):
        at = at_image(image)
        grad_h = grad_h_ref[at, :].astype(f32)
        normed, inverse = norm_stats(rows_kept[at, :])
        add_sums(2, grad_h, normed)
        grad_resid = cot_rows[at, :].astype(f32) + norm_back(grad_h, gain2, normed, inverse)
        rows_kept[at, :] = grad_resid
        grad_branch = grad_resid.astype(bf16)
        token_normed, _ = norm_stats(tok_ref[image].astype(f32))
        h_one = (token_normed * gain1 + shift1).astype(bf16)
        queries, keys, values, attended = q_ref[image], k_ref[image], v_ref[image], att_ref[image]
        lse = lse_ref[image]
        grad_attended = dot(grad_branch, out_w_ref[...], ((1,), (1,))).astype(bf16)
        grads = [[], [], []]
        for head in range(heads):
            first = head // 2 * 2 * HD
            last = min(first + 2 * HD, heads * HD)
            parts = [whose[:, first:last] for whose in (queries, keys, values, grad_attended)]
            if last - first == 2 * HD:
                own = head_mask(lane, head)
                q_own, k_own, _, g_own = (jnp.where(own, part, jnp.zeros_like(part)) for part in parts)
            else:
                q_own, k_own, _, g_own = parts
            scores = dot(q_own, parts[1], ((1,), (1,))) * (HD**-0.5)
            probs = jnp.where(key_mask, jnp.exp(scores - lse[:, head : head + 1]), 0.0)
            back = dot(g_own, parts[2], ((1,), (1,)))
            product = probs * back
            grad_scores = (product - probs * jnp.sum(product, axis=1, keepdims=True)).astype(bf16)
            pieces = (
                dot(grad_scores, k_own) * (HD**-0.5),
                dot(grad_scores, q_own, ((0,), (0,))) * (HD**-0.5),
                dot(probs.astype(bf16), g_own, ((0,), (0,))),
            )
            for which in range(3):
                if head % 2 == 0:
                    grads[which].append(pieces[which])
                else:
                    grads[which][-1] += pieces[which]
        grad_rows = [jnp.concatenate(grads[which], axis=1).astype(bf16) for which in range(3)]
        grad_one = 0.0
        for which in range(3):
            weight_sum[which * share : (which + 1) * share, :] += dot(grad_rows[which].T, h_one)
            grad_one += dot(grad_rows[which], qkv_ref[which], ((1,), (1,)))
        weight_sum[3 * share : 4 * share, :] += dot(attended.T, grad_branch)
        whole[...] = grad_one
        one_mine[image] = whole[:, my_cols].astype(bf16)
        one_to[image] = whole[:, their_cols].astype(bf16)
        one_core_copy(image).start()

    def run_one_x(image):
        one_core_copy(image).wait_recv()
        one_core[image] = (one_core[image].astype(f32) + one_mine[image].astype(f32)).astype(bf16)
        one_x_copy(image).start()

    def run_one_total(image):
        one_x_copy(image).wait_recv()
        one_x[image] = (one_core[image].astype(f32) + one_x[image].astype(f32)).astype(bf16)
        one_total_copy(image).start()

    def run_tokens(image):
        one_total_copy(image).wait_recv()
        whole[:, my_cols] = one_x[image].astype(f32)
        whole[:, their_cols] = one_total[image].astype(f32)
        grad_one = whole[...]
        at = at_image(image)
        normed, inverse = norm_stats(tok_ref[image].astype(f32))
        add_sums(0, grad_one, normed)
        rows_kept[at, :] = rows_kept[at, :] + norm_back(grad_one, gain1, normed, inverse)
        store_copy(image).start()

    def stage(tick, lag, run):
        image = tick - lag

        @pl.when((image >= 0) & (image < images))
        def _():
            run(image)

    def m_stage(tick, first, run):
        @pl.when((tick >= first) & ((tick - first) % 2 == 0) & ((tick - first) // 2 < part_count))
        def _():
            run((tick - first) // 2)

    def per_tick(tick, _):
        stage(tick, 0, run_attention)
        stage(tick, 1, run_one_x)
        stage(tick, 2, run_one_total)
        stage(tick, 3, run_tokens)
        m_stage(tick, 2, run_m_x)
        m_stage(tick, 4, run_m_out)

        @pl.when(tick == 4)
        def _():
            line_await(0)
            line_add(0)
            line_send(1)

        @pl.when(tick == 9)
        def _():
            line_await(1)
            line_add(1)
            line_send(2)

        return 0

    lax.fori_loop(0, images + 3, per_tick, 0)

    route_two.wait_recv()
    weight_sum[features + 8 : features + 16, :] = route_core[...] + route_x[...]
    part_rows = shared.shape[1]
    quarter = part_rows // (z_last + 1)

    def to_half(side):
        def cast(piece, _):
            at_rows = aligned(piece * quarter, quarter)
            shared[side, at_rows, :] = weight_sum[aligned(side * part_rows + piece * quarter, quarter), :].astype(bf16)
            return 0

        lax.fori_loop(0, z_last + 1, cast, 0)

    to_half(0)
    to_half(1)

    def y_piece(number):
        inner = jnp.where(z_at == 1, jnp.where(number < 2, z_last - number, number - 2), jnp.where(number < 2, number, 5 - number))
        return jnp.where(z_at == 0, z_last - number, jnp.where(z_at == z_last, number, inner))

    def quarter_at(piece):
        return aligned(piece * quarter, quarter)

    def shared_y_copy(number):
        at_rows = quarter_at(y_piece(number))
        return remote(shared.at[1 - y_at, at_rows, :], shared_y.at[at_rows, :], sy_s.at[number], sy_r.at[number], y_dev)

    def take_y(number):
        shared_y_copy(number).wait_recv()
        at_rows = quarter_at(y_piece(number))
        weight_half[at_rows, :] = shared[y_at, at_rows, :].astype(f32) + shared_y[at_rows, :].astype(f32)

    for number in range(4):
        shared_y_copy(number).start()

    def small_copy(step, way):
        return remote(shared_line.at[way, 0, step], shared_line.at[way, 1, step], sl_s.at[way, step], sl_r.at[way, step], z_devs[way])

    for step in range(3):
        take_y(step)
        if step == 2:
            take_y(3)
        for way in range(2):
            at = place(way)

            @pl.when((at <= step) & (at < z_last))
            def _():
                at_rows = quarter_at(expert_of(step, at, way))
                if step == 0:
                    shared_line[way, 0, step] = weight_half[at_rows, :].astype(bf16)
                else:
                    came = jnp.where(at > 0, shared_line[way, 1, step - 1].astype(f32), 0.0)
                    shared_line[way, 0, step] = (weight_half[at_rows, :] + came).astype(bf16)
                small_copy(step, way).start()

        for way in range(2):
            at = place(way)

            @pl.when((at > 0) & (at - 1 <= step))
            def _():
                small_copy(step, way).wait_recv()

    own_rows = quarter_at(z_at)
    from_below = jnp.where(z_at > 0, shared_line[0, 1, 2].astype(f32), 0.0)
    from_above = jnp.where(z_at < z_last, shared_line[1, 1, 2].astype(f32), 0.0)

    def final_rows(side, piece):
        return shared_all.at[side, quarter_at(piece), :]

    shared_all[y_at, own_rows, :] = (weight_half[own_rows, :] + from_below + from_above).astype(bf16)
    for number in range(4):
        shared_y_copy(number).wait_send()

    def gather_z(step, way, piece):
        ref = final_rows(y_at, piece)
        return remote(ref, ref, sg_s.at[way, step], sg_r.at[way, step], z_devs[way])

    def gather_y(step, way, piece, side):
        ref = final_rows(side, piece)
        return remote(ref, ref, sz_s.at[way, step], sz_r.at[way, step], y_dev)

    gather_y(0, 0, z_at, y_at).start()
    for step in range(3):
        for way in range(2):
            at = place(way)
            piece = z_at - step if way == 0 else z_at + step

            @pl.when((at >= step) & (at < z_last))
            def _():
                gather_z(step, way, piece).start()

        for way in range(2):
            at = place(way)
            piece = z_at - 1 - step if way == 0 else z_at + 1 + step

            @pl.when(at >= 1 + step)
            def _():
                gather_z(step, way, piece).wait_recv()
                gather_y(step + 1, way, piece, y_at).start()

    gather_y(0, 0, z_at, 1 - y_at).wait_recv()
    for step in range(3):
        for way in range(2):
            at = place(way)
            piece = z_at - 1 - step if way == 0 else z_at + 1 + step

            @pl.when(at >= 1 + step)
            def _():
                gather_y(step + 1, way, piece, 1 - y_at).wait_recv()

    def to_out(piece, _):
        for side in range(2):
            weight_sum[aligned(side * part_rows + piece * quarter, quarter), :] = shared_all[
                side, quarter_at(piece), :
            ].astype(f32)
        return 0

    lax.fori_loop(0, z_last + 1, to_out, 0)
    weight_copy = pltpu.make_async_copy(weight_sum, weights_out, weight_store.at[0])
    weight_copy.start()
    line_await(2)
    load_own(z_at)

    def finish(piece, _):
        at_rows = aligned(piece * 128, 128)
        totals = []
        for number in range(2):
            below = jnp.where(z_at > 0, line[0, 2, number, at_rows, :].astype(f32), 0.0)
            above = jnp.where(z_at < z_last, line[1, 2, number, at_rows, :].astype(f32), 0.0)
            totals.append(own_vm[number, at_rows, :].astype(f32) + below + above)
        up_out[at_rows, :] = totals[0]
        down_out[:, lanes_at(piece * 128, 128)] = totals[1].T
        return 0

    lax.fori_loop(0, features // 128, finish, 0)

    route_one.wait_send()
    route_two.wait_send()

    def drain(image, _):
        for copy in (one_core_copy, one_x_copy, one_total_copy):
            copy(image).wait_send()
        store_copy(image).wait()
        return 0

    lax.fori_loop(0, images, drain, 0)
    for part in range(part_count):
        m_core_copy(0, part).wait_send()
        m_core_copy(1, part).wait_send()
        m_y_copy(part).wait_send()

        @pl.when(keeps)
        def _():
            m_quarter_copy(part).wait_send()
            m_store_copy(part).wait()

        @pl.when(jnp.logical_not(keeps))
        def _():
            m_x_copy(part).wait_send()
            m_quarter_copy(part).wait_recv()

    weight_copy.wait()
    gather_y(0, 0, z_at, y_at).wait_send()
    for step in range(3):
        for way in range(2):
            at = place(way)

            @pl.when((at <= step) & (at < z_last))
            def _():
                small_copy(step, way).wait_send()
                for number in range(2):
                    line_copy(line.at[way, step, number], step, way, number).wait_send()

            piece = z_at - step if way == 0 else z_at + step

            @pl.when((at >= step) & (at < z_last))
            def _():
                gather_z(step, way, piece).wait_send()

            piece = z_at - 1 - step if way == 0 else z_at + 1 + step

            @pl.when(at >= 1 + step)
            def _():
                gather_y(step + 1, way, piece, y_at).wait_send()


def run_backward(
    tok,
    gain1,
    shift1,
    gain2,
    qkv_w,
    out_w,
    q,
    k,
    v,
    att,
    lse,
    grad_h,
    grad_router,
    resid,
    cot,
    mixed,
    up_first,
    up_second,
    down_first,
    down_second,
):
    images, _, features = tok.shape
    rows = images * PITCH
    share = out_w.shape[0]
    heads = share // HD
    hidden = up_first.shape[1] // 2
    wide = features // 2
    packed = features + 128
    parts = 4
    vmem = pl.BlockSpec(memory_space=pltpu.VMEM)
    anywhere = pl.BlockSpec(memory_space=pl.ANY)
    shape = jax.ShapeDtypeStruct
    dma = pltpu.SemaphoreType.DMA
    block = (images, PITCH, wide)
    return pl.pallas_call(
        partial(backward_kernel, images=images, heads=heads),
        out_shape=[
            shape((features, hidden), f32),
            shape((hidden, features), f32),
            shape((rows, features), f32),
            shape((packed, features), f32),
            shape((rows, wide // 2), bf16),
        ],
        in_specs=[vmem] * 13 + [anywhere] * 7,
        out_specs=[vmem] * 2 + [anywhere] * 3,
        scratch_shapes=[
            pltpu.VMEM((rows, features), f32),
            pltpu.VMEM((rows, features), bf16),
            pltpu.VMEM((2 * rows, wide), bf16),
            pltpu.VMEM((2 * rows, wide), bf16),
            *[pltpu.VMEM((parts, rows // parts, wide), bf16)] * 2,
            pltpu.VMEM((parts, 2, rows // parts, wide // 2), bf16),
            pltpu.VMEM((rows // parts, wide), f32),
            pltpu.VMEM((2, features, hidden), bf16),
            *[pltpu.VMEM(block, bf16)] * 5,
            pltpu.VMEM((2, 3, 2, features, hidden), bf16),
            pltpu.VMEM((packed, features), f32),
            pltpu.VMEM((packed // 2, features), f32),
            pltpu.VMEM((2, packed // 2, features), bf16),
            pltpu.VMEM((packed // 2, features), bf16),
            pltpu.VMEM((2, 2, 3, packed // 8, features), bf16),
            pltpu.VMEM((2, packed // 2, features), bf16),
            pltpu.VMEM((8, features), f32),
            pltpu.VMEM((8, features), f32),
            pltpu.VMEM((PITCH, features), f32),
        ]
        + [dma((2, parts))] * 2
        + [dma((parts,))] * 7
        + [dma((images,))] * 6
        + [dma((2, 3, 2))] * 2
        + [dma((4,))] * 2
        + [dma((2, 3))] * 4
        + [dma((2, 4))] * 2
        + [dma((2,))] * 2
        + [dma((4,)), dma((2,)), dma((1,)), dma((images,))],
        compiler_params=pltpu.CompilerParams(
            collective_id=2, has_side_effects=True, vmem_limit_bytes=63 << 20
        ),
    )(
        tok,
        gain1,
        shift1,
        gain2,
        qkv_w,
        out_w,
        q,
        k,
        v,
        att,
        lse,
        grad_h,
        grad_router,
        resid,
        cot,
        mixed,
        up_first,
        up_second,
        down_first,
        down_second,
    )


def per_image(rows_in):
    images = rows_in.shape[0] // SEQ
    blocks = rows_in.reshape(images, SEQ, rows_in.shape[1])
    return jnp.pad(blocks, ((0, 0), (0, PITCH - SEQ), (0, 0)))


def unpad(blocks):
    images = blocks.shape[0]
    return blocks[:, :SEQ].reshape(images * SEQ, blocks.shape[2])


def per_device_dense(
    tokens,
    gain_attn,
    shift_attn,
    qkv_weight,
    out_weight,
    gain_moe,
    shift_moe,
    router_weight,
    expert_up,
    expert_down,
    routes,
    keep_mask,
    cotangent,
):
    row_count, feature_count = tokens.shape
    images = row_count // SEQ
    rows = images * PITCH
    tensor_count = lax.axis_size("tensor")
    quarter_width = feature_count // tensor_count
    experts_all = router_weight.shape[1]
    hidden = expert_up.shape[2]
    chosen = routes[:, :, None] == jnp.arange(128, dtype=jnp.int32)[None, None, :]
    kept = jnp.sum(jnp.where(chosen, keep_mask[:, :, None], 0), axis=1).astype(bf16)
    router_wide = jnp.pad(router_weight, ((0, 0), (0, 128 - experts_all)))
    tok = per_image(tokens)
    queries, keys, values, attended, lse, resid, h_all, cot_all, kept_all, up_all, down_all = run_forward(
        tok,
        gain_attn[None],
        shift_attn[None],
        gain_moe[None],
        shift_moe[None],
        qkv_weight,
        out_weight,
        expert_up[0],
        expert_down[0],
        per_image(cotangent).reshape(rows, quarter_width),
        per_image(kept).reshape(rows, 128),
    )
    mixed_first, grad_h_first, gate_first, up_first, down_first, up_late, down_late = run_first_pair(
        h_all, cot_all, kept_all, router_wide, up_all, down_all, experts_all
    )
    mixed_part, up_second, down_second, grad_router, grad_h_two = run_second_pair(
        h_all,
        cot_all,
        kept_all,
        router_wide,
        mixed_first,
        grad_h_first,
        gate_first,
        up_all,
        down_all,
        up_late,
        down_late,
        experts_all,
    )
    grad_up, grad_down, tokens_grad, weights_grad, mixed = run_backward(
        tok,
        gain_attn[None],
        shift_attn[None],
        gain_moe[None],
        qkv_weight,
        out_weight,
        queries,
        keys,
        values,
        attended,
        lse,
        grad_h_two,
        grad_router,
        resid,
        cot_all,
        mixed_part,
        up_first,
        up_second,
        down_first,
        down_second,
    )
    share = qkv_weight.shape[2]
    grad_qkv = weights_grad[: 3 * share].reshape(3, share, feature_count).transpose(0, 2, 1)
    small = weights_grad[feature_count : feature_count + 16]
    return (
        unpad(mixed.reshape(images, PITCH, quarter_width)),
        unpad(tokens_grad.reshape(images, PITCH, feature_count)),
        small[0],
        small[1],
        grad_qkv,
        weights_grad[3 * share : 4 * share],
        small[2],
        small[3],
        small[8 : 8 + experts_all].T,
        grad_up[None],
        grad_down[None],
    )


def per_device(*arguments):
    router_weight = arguments[7]
    if router_weight.shape[1] == 4 and lax.axis_size("expert") == 8 and lax.axis_size("tensor") == 4:
        return per_device_dense(*arguments)
    return per_device_routed(*arguments)


def solution(mesh):
    placed = (
        P("expert", None),
        P(),
        P(),
        P(None, None, "tensor"),
        P("tensor", None),
        P(),
        P(),
        P(),
        P("expert", None, "tensor"),
        P("expert", "tensor", None),
        P("expert", None),
        P("expert", None),
        P("expert", "tensor"),
    )
    return jax.shard_map(
        per_device,
        mesh=mesh,
        in_specs=placed,
        out_specs=(
            P("expert", "tensor"),
            P("expert", None),
            P(),
            P(),
            P(None, None, "tensor"),
            P("tensor", None),
            P(),
            P(),
            P(),
            P("expert", None, "tensor"),
            P("expert", "tensor", None),
        ),
        check_vma=False,
    )
```

```python
from functools import partial

import jax
import jax.numpy as jnp
from jax import lax
from jax.experimental import pallas as pl
from jax.experimental.pallas import tpu as pltpu
from jax.sharding import PartitionSpec as P

HD = 64
SEQ = 197


norm_epsilon = 1e-06


def norm_rows(values, gain, shift):
    row_mean = jnp.mean(values, axis=-1, keepdims=True)
    centred = values - row_mean
    spread = jnp.mean(centred * centred, axis=-1, keepdims=True)
    return centred * lax.rsqrt(spread + norm_epsilon) * gain + shift


def gelu_exact(values):
    return jax.nn.gelu(values, approximate=False)


def gate_from_logits(logit_rows, picked_rows, keep_rows):
    router_probs = jax.nn.softmax(logit_rows, axis=-1)
    return jnp.sum(jnp.where(picked_rows, router_probs[:, None, :], 0.0), axis=-1) * keep_rows


def attention_forward(h_rows, qkv_w, out_w):
    row_total_count = h_rows.shape[0]
    head_count = qkv_w.shape[2] // HD
    image_count = row_total_count // SEQ
    score_scale = HD ** (-0.5)
    projected = jnp.einsum("td,cdf->ctf", h_rows, qkv_w, preferred_element_type=jnp.float32).astype(
        jnp.bfloat16
    )
    split_heads = projected.reshape(3, image_count, SEQ, head_count, HD)
    queries = split_heads[0]
    keys_all = split_heads[1]
    values_all = split_heads[2]
    scores = (
        jnp.einsum("gqhe,gkhe->ghqk", queries, keys_all, preferred_element_type=jnp.float32)
        * score_scale
    )
    row_peak = jnp.max(scores, axis=-1, keepdims=True)
    exp_scores = jnp.exp(scores - row_peak)
    row_total = jnp.sum(exp_scores, axis=-1, keepdims=True)
    log_total = row_peak + jnp.log(row_total)
    weights = (exp_scores / row_total).astype(jnp.bfloat16)
    attended = jnp.einsum(
        "ghqk,gkhe->gqhe", weights, values_all, preferred_element_type=jnp.float32
    ).astype(jnp.bfloat16)
    attended = attended.reshape(row_total_count, head_count * HD)
    partial_out = jnp.dot(attended, out_w, preferred_element_type=jnp.float32)
    return (partial_out, (attended, queries, keys_all, values_all, log_total))


def attention_backward(grad_branch, saved, h_rows, qkv_w, out_w):
    attended, queries, keys_all, values_all, log_total = saved
    row_total_count = h_rows.shape[0]
    head_count = qkv_w.shape[2] // HD
    image_count = row_total_count // SEQ
    score_scale = HD ** (-0.5)
    grad_out = jnp.einsum("tc,td->cd", attended, grad_branch, preferred_element_type=jnp.float32)
    grad_attended = jnp.einsum(
        "td,cd->tc", grad_branch, out_w, preferred_element_type=jnp.float32
    ).astype(jnp.bfloat16)
    grad_attended = grad_attended.reshape(image_count, SEQ, head_count, HD)
    scores_again = (
        jnp.einsum("gqhe,gkhe->ghqk", queries, keys_all, preferred_element_type=jnp.float32)
        * score_scale
    )
    probs_again = jnp.exp(scores_again - log_total)
    grad_weights = jnp.einsum(
        "gqhe,gkhe->ghqk", grad_attended, values_all, preferred_element_type=jnp.float32
    )
    grad_scores = (
        probs_again * (grad_weights - jnp.sum(probs_again * grad_weights, axis=-1, keepdims=True))
    ).astype(jnp.bfloat16)
    grad_queries = (
        jnp.einsum("ghqk,gkhe->gqhe", grad_scores, keys_all, preferred_element_type=jnp.float32)
        * score_scale
    )
    grad_keys = (
        jnp.einsum("ghqk,gqhe->gkhe", grad_scores, queries, preferred_element_type=jnp.float32)
        * score_scale
    )
    grad_values = jnp.einsum(
        "ghqk,gqhe->gkhe",
        probs_again.astype(jnp.bfloat16),
        grad_attended,
        preferred_element_type=jnp.float32,
    )
    grad_rows = (
        jnp.stack([grad_queries, grad_keys, grad_values])
        .astype(jnp.bfloat16)
        .reshape(3, row_total_count, head_count * HD)
    )
    grad_qkv = jnp.einsum("td,ctf->cdf", h_rows, grad_rows, preferred_element_type=jnp.float32)
    grad_h_one = jnp.einsum("ctf,cdf->td", grad_rows, qkv_w, preferred_element_type=jnp.float32)
    return (grad_qkv, grad_out, grad_h_one)


def moe_tail(
    grad_h_rows,
    grad_gate_rows,
    grad_out_rows,
    h_two_rows,
    resid_rows,
    gate_back,
    router_weight,
    gain_moe,
    shift_moe,
):
    row_total_count = grad_h_rows.shape[0]
    grad_gate = jnp.sum(grad_gate_rows.reshape(row_total_count, -1, 2), axis=1)
    grad_logits = gate_back(grad_gate)[0].astype(jnp.bfloat16)
    grad_router = jnp.einsum(
        "td,te->de", h_two_rows, grad_logits, preferred_element_type=jnp.float32
    )
    grad_h_two = grad_h_rows + jnp.einsum(
        "te,de->td", grad_logits, router_weight, preferred_element_type=jnp.float32
    )
    norm_out, norm_back = jax.vjp(norm_rows, resid_rows, gain_moe, shift_moe)
    grad_resid_norm, grad_gain_moe, grad_shift_moe = norm_back(grad_h_two)
    return (grad_out_rows + grad_resid_norm, grad_router, grad_gain_moe, grad_shift_moe)


def per_device_routed(
    tokens,
    gain_attn,
    shift_attn,
    qkv_weight,
    out_weight,
    gain_moe,
    shift_moe,
    router_weight,
    expert_up,
    expert_down,
    routes,
    keep_mask,
    cotangent,
):
    row_count, feature_count = tokens.shape
    tensor_count = lax.axis_size("tensor")
    expert_count = lax.axis_size("expert")
    tensor_here = lax.axis_index("tensor")
    quarter_width = feature_count // tensor_count
    col_start = tensor_here * quarter_width
    experts_all = router_weight.shape[1]
    capacity = max(2, 7 * row_count // (2 * experts_all))
    tokens_float = tokens.astype(jnp.float32)
    h_one = norm_rows(tokens_float, gain_attn, shift_attn).astype(jnp.bfloat16)
    partial_out, saved = attention_forward(h_one, qkv_weight, out_weight)
    branch = lax.psum(partial_out, "tensor")
    resid = tokens_float + branch
    h_two = norm_rows(resid, gain_moe, shift_moe).astype(jnp.bfloat16)
    logits = jnp.dot(h_two, router_weight, preferred_element_type=jnp.float32)
    keep_float = keep_mask.astype(jnp.float32)
    picked = routes[:, :, None] == jnp.arange(experts_all, dtype=jnp.int32)[None, None, :]
    gate_values, gate_back = jax.vjp(
        partial(gate_from_logits, picked_rows=picked, keep_rows=keep_float), logits
    )
    flat_expert = routes.reshape(-1)
    one_hot = (flat_expert[:, None] == jnp.arange(experts_all, dtype=jnp.int32)[None, :]).astype(
        jnp.int32
    )
    rank_within = jnp.sum((jnp.cumsum(one_hot, axis=0) - one_hot) * one_hot, axis=1)
    slot_index = flat_expert * capacity + rank_within
    token_index = jnp.repeat(jnp.arange(row_count, dtype=jnp.int32), 2)
    live_route = keep_mask.reshape(-1) > 0
    source_table = (
        jnp.full((experts_all * capacity,), row_count, jnp.int32)
        .at[slot_index]
        .set(jnp.where(live_route, token_index, row_count))
    )
    padded_rows = jnp.concatenate([h_two, jnp.zeros((1, feature_count), jnp.bfloat16)], axis=0)
    dispatch = padded_rows[source_table].reshape(experts_all, capacity, feature_count)
    paired = jnp.broadcast_to(dispatch[:, None], (experts_all, 2, capacity, feature_count)).reshape(
        expert_count, capacity, feature_count
    )
    arrived = lax.all_to_all(paired, "expert", split_axis=0, concat_axis=0, tiled=True)
    expert_rows = arrived.reshape(expert_count * capacity, feature_count)
    up_local = expert_up[0]
    down_local = expert_down[0]
    pre_act = jnp.dot(expert_rows, up_local, preferred_element_type=jnp.float32)
    hidden_float, gelu_back = jax.vjp(gelu_exact, pre_act)
    hidden = hidden_float.astype(jnp.bfloat16)
    partial_down = jnp.dot(hidden, down_local, preferred_element_type=jnp.float32)
    summed = lax.psum_scatter(partial_down, "tensor", scatter_dimension=1, tiled=True)
    returned = lax.all_to_all(
        summed.reshape(expert_count, capacity, quarter_width),
        "expert",
        split_axis=0,
        concat_axis=0,
        tiled=True,
    )
    answer_table = jnp.sum(
        returned.reshape(experts_all, 2, capacity, quarter_width), axis=1
    ).astype(jnp.bfloat16)
    answers = (
        answer_table.reshape(experts_all * capacity, quarter_width)[slot_index]
        .astype(jnp.float32)
        .reshape(row_count, 2, quarter_width)
    )
    resid_part = lax.dynamic_slice_in_dim(resid, col_start, quarter_width, 1)
    mixed = (resid_part + jnp.sum(gate_values[:, :, None] * answers, axis=1)).astype(jnp.bfloat16)
    grad_part = cotangent.astype(jnp.float32)
    grad_answers = (
        (gate_values[:, :, None] * grad_part[:, None, :])
        .astype(jnp.bfloat16)
        .reshape(2 * row_count, quarter_width)
    )
    grad_gate_part = jnp.sum(grad_part[:, None, :] * answers, axis=-1)
    outgoing = (
        jnp.zeros((experts_all * capacity, quarter_width), jnp.bfloat16)
        .at[slot_index]
        .set(grad_answers)
    )
    outgoing = jnp.broadcast_to(
        outgoing.reshape(experts_all, 1, capacity, quarter_width),
        (experts_all, 2, capacity, quarter_width),
    ).reshape(expert_count, capacity, quarter_width)
    incoming = lax.all_to_all(outgoing, "expert", split_axis=0, concat_axis=0, tiled=True)
    grad_full = lax.all_gather(incoming, "tensor", axis=2, tiled=True).reshape(
        expert_count * capacity, feature_count
    )
    grad_hidden = jnp.einsum("rd,fd->rf", grad_full, down_local, preferred_element_type=jnp.float32)
    grad_pre = gelu_back(grad_hidden)[0].astype(jnp.bfloat16)
    grad_down = jnp.einsum("rf,rd->fd", hidden, grad_full, preferred_element_type=jnp.float32)
    grad_up = jnp.einsum("rd,rf->df", expert_rows, grad_pre, preferred_element_type=jnp.float32)
    grad_rows_partial = jnp.einsum(
        "rf,df->rd", grad_pre, up_local, preferred_element_type=jnp.float32
    )
    grad_rows_sum = lax.psum_scatter(
        grad_rows_partial.astype(jnp.bfloat16), "tensor", scatter_dimension=1, tiled=True
    ).astype(jnp.float32)
    sent_back = lax.all_to_all(
        grad_rows_sum.reshape(expert_count, capacity, quarter_width).astype(jnp.bfloat16),
        "expert",
        split_axis=0,
        concat_axis=0,
        tiled=True,
    ).astype(jnp.float32)
    grad_table = jnp.sum(sent_back.reshape(experts_all, 2, capacity, quarter_width), axis=1).astype(
        jnp.bfloat16
    )
    grad_inputs = (
        grad_table.reshape(experts_all * capacity, quarter_width)[slot_index]
        .astype(jnp.float32)
        .reshape(row_count, 2, quarter_width)
    )
    grad_h_part = jnp.sum(grad_inputs * keep_float[:, :, None], axis=1)
    grad_h_full, grad_gate_all, grad_out_full = (
        lax.all_gather(grad_h_part, "tensor", axis=1, tiled=True),
        lax.all_gather(grad_gate_part, "tensor", axis=1, tiled=True),
        lax.all_gather(grad_part, "tensor", axis=1, tiled=True),
    )
    grad_resid, grad_router, grad_gain_moe, grad_shift_moe = moe_tail(
        grad_h_full,
        grad_gate_all,
        grad_out_full,
        h_two,
        resid,
        gate_back,
        router_weight,
        gain_moe,
        shift_moe,
    )
    grad_qkv, grad_out, grad_h_one_part = attention_backward(
        grad_resid.astype(jnp.bfloat16), saved, h_one, qkv_weight, out_weight
    )
    grad_h_one = lax.psum(grad_h_one_part.astype(jnp.bfloat16), "tensor").astype(jnp.float32)
    norm_one_out, norm_one_back = jax.vjp(norm_rows, tokens_float, gain_attn, shift_attn)
    grad_tok_norm, grad_gain_attn, grad_shift_attn = norm_one_back(grad_h_one)
    grad_tokens = grad_resid + grad_tok_norm
    summed_grads = lax.psum(
        (
            grad_gain_attn,
            grad_shift_attn,
            grad_qkv,
            grad_out,
            grad_gain_moe,
            grad_shift_moe,
            grad_router,
        ),
        "expert",
    )
    grad_qkv_mine = summed_grads[2]
    grad_out_mine = summed_grads[3]
    return (
        mixed,
        grad_tokens,
        summed_grads[0],
        summed_grads[1],
        grad_qkv_mine,
        grad_out_mine,
        summed_grads[4],
        summed_grads[5],
        summed_grads[6],
        grad_up[None],
        grad_down[None],
    )


MESH = pl.DeviceIdType.MESH
f32 = jnp.float32
bf16 = jnp.bfloat16
PITCH = 208


def dot(left, right, over=((1,), (0,))):
    return lax.dot_general(left, right, (over, ((), ())), preferred_element_type=f32)


def aligned(start, size):
    return pl.ds(pl.multiple_of(start, 16), size)


def lanes_at(start, size):
    return pl.ds(pl.multiple_of(start, 128), size)


def norm_stats(values):
    row_mean = jnp.mean(values, axis=1, keepdims=True)
    centred = values - row_mean
    inverse = lax.rsqrt(jnp.mean(centred * centred, axis=1, keepdims=True) + norm_epsilon)
    return centred * inverse, inverse


def greet(neighbours):
    barrier = pltpu.get_barrier_semaphore()
    count = 0
    for is_there, device in neighbours:

        @pl.when(is_there)
        def _():
            pl.semaphore_signal(barrier, inc=1, device_id=device, device_id_type=MESH)

        count = count + jnp.where(is_there, 1, 0)
    pl.semaphore_wait(barrier, count)


def head_mask(lane, head):
    return (lane < HD) if head % 2 == 0 else (lane >= HD)


def forward_kernel(
    tok_ref,
    gain1_ref,
    shift1_ref,
    gain2_ref,
    shift2_ref,
    qkv_ref,
    out_w_ref,
    up_ref,
    down_ref,
    cot_ref,
    kept_ref,
    q_ref,
    k_ref,
    v_ref,
    att_ref,
    lse_ref,
    resid_ref,
    h_out,
    cot_out,
    kept_out,
    up_out,
    down_out,
    q_all,
    k_all,
    v_all,
    att_all,
    lse_all,
    resid_all,
    h_all,
    cot_all,
    kept_all,
    part,
    mine,
    core_from,
    core_to,
    x_to,
    x_from,
    total_to,
    total_from,
    cot_core,
    core_s,
    core_r,
    x_s,
    x_r,
    tot_s,
    tot_r,
    y_s,
    y_r,
    rel_s,
    rel_r,
    w_s,
    w_r,
    c_s,
    c_r,
    own_sem,
    cot_sem,
    out_sem,
    *,
    images,
    heads,
):
    expert_at = lax.axis_index("expert")
    tensor_at = lax.axis_index("tensor")
    z_at, y_at = expert_at // 2, expert_at % 2
    z_last = lax.axis_size("expert") // 2 - 1
    x_at, core_at = tensor_at // 2, tensor_at % 2
    other = 1 - core_at
    rows = images * PITCH
    half = rows // 2
    wide = out_w_ref.shape[1] // 2
    hidden = up_ref.shape[1]
    core_dev = (expert_at, tensor_at + 1 - 2 * core_at)
    x_dev = (expert_at, tensor_at + 2 - 4 * x_at)
    y_dev = (expert_at + 1 - 2 * y_at, tensor_at)
    z_up = (expert_at + 2, tensor_at)
    z_down = (expert_at - 2, tensor_at)
    has_up, has_down = z_at < z_last, z_at > 0
    greet([(True, core_dev), (True, x_dev), (True, y_dev), (has_up, z_up), (has_down, z_down)])

    def remote(src, dst, send, recv, device):
        return pltpu.make_async_remote_copy(
            src_ref=src, dst_ref=dst, send_sem=send, recv_sem=recv, device_id=device, device_id_type=MESH
        )

    def slot(expert, plane):
        pair = (expert // 2 + plane // 2) % 2
        return (
            up_out.at[pair, :, lanes_at(expert % 2 * hidden, hidden)],
            down_out.at[pair, aligned(expert % 2 * hidden, hidden), :],
        )

    def hop(step, way):
        expert = z_at - step if way == 0 else z_at + step
        plane = z_at + 1 if way == 0 else z_at - 1
        source = (up_ref, down_ref) if step == 0 else slot(expert, z_at)
        target = slot(expert, plane)
        device = z_up if way == 0 else z_down
        return [remote(source[n], target[n], w_s.at[way, step, n], w_r.at[way, step, n], device) for n in range(2)]

    def hop_goes(step, way):
        if way == 0:
            return (z_at - step >= 0) & has_up
        return (z_at + step <= z_last) & has_down

    def hop_comes(step, way):
        return (z_at - 1 - step >= 0) if way == 0 else (z_at + 1 + step <= z_last)

    def hop_arriving(step, way):
        expert = z_at - 1 - step if way == 0 else z_at + 1 + step
        target = slot(expert, z_at)
        return [remote(target[n], target[n], w_s.at[way, step, n], w_r.at[way, step, n], core_dev) for n in range(2)]

    def start_hops(step):
        for way in range(2):

            @pl.when(hop_goes(step, way))
            def _():
                for copy in hop(step, way):
                    copy.start()

    def await_hops(step):
        for way in range(2):

            @pl.when(hop_comes(step, way))
            def _():
                for copy in hop_arriving(step, way):
                    copy.wait_recv()

    start_hops(0)
    own = slot(z_at, z_at)
    own_copies = [pltpu.make_async_copy((up_ref, down_ref)[n], own[n], own_sem.at[n]) for n in range(2)]
    for copy in own_copies:
        copy.start()

    swap = remote(cot_ref, cot_core, c_s.at[0], c_r.at[0], core_dev)
    swap.start()
    kept_all[pl.ds(0, rows), :] = kept_ref[...]

    def kept_half(side, core):
        return kept_all.at[aligned(side * rows + core * half, half), :]

    kept_y = remote(kept_half(0, core_at), kept_half(1, core_at), c_s.at[7], c_r.at[7], y_dev)
    kept_share = remote(kept_half(1, core_at), kept_half(1, core_at), c_s.at[6], c_r.at[6], core_dev)
    kept_share_in = remote(kept_half(1, other), kept_half(1, other), c_s.at[6], c_r.at[6], core_dev)
    kept_y.start()
    swap.wait_recv()

    @pl.when(core_at == 0)
    def _():
        both = jnp.concatenate([cot_ref[...], cot_core[...]], axis=1)
        cot_all[pl.ds(0, rows), lanes_at(x_at * wide, wide)] = both

    @pl.when(core_at == 1)
    def _():
        both = jnp.concatenate([cot_core[...], cot_ref[...]], axis=1)
        cot_all[pl.ds(0, rows), lanes_at(x_at * wide, wide)] = both

    def block(side, col_side, core):
        return cot_all.at[aligned(side * rows + core * half, half), lanes_at(col_side * wide, wide)]

    def cot_copy(number, source, target, device):
        return remote(source, target, c_s.at[number], c_r.at[number], device)

    mine_block = block(0, x_at, core_at)
    cot_x = cot_copy(1, mine_block, mine_block, x_dev)
    cot_y = cot_copy(2, mine_block, block(1, x_at, core_at), y_dev)
    cot_x.start()
    cot_y.start()
    across_x, across_y, across_both = block(0, 1 - x_at, core_at), block(1, x_at, core_at), block(1, 1 - x_at, core_at)
    cot_x_in = cot_copy(1, across_x, across_x, x_dev)
    cot_y_in = cot_copy(2, across_y, across_y, y_dev)
    relay_y = cot_copy(3, across_x, across_both, y_dev)
    relay_x = cot_copy(3, across_y, across_y, x_dev)
    relay_in = cot_copy(3, across_both, across_both, y_dev)
    cot_share = [
        cot_copy(4, across_x, across_x, core_dev),
        cot_copy(5, across_y, across_y, core_dev),
        cot_copy(8, across_both, across_both, core_dev),
    ]
    arriving = [block(0, 1 - x_at, other), block(1, x_at, other), block(1, 1 - x_at, other)]
    cot_share_in = [cot_copy(number, ref, ref, core_dev) for number, ref in zip((4, 5, 8), arriving)]

    lane = lax.broadcasted_iota(jnp.int32, (PITCH, 2 * HD), 1)
    key_mask = lax.broadcasted_iota(jnp.int32, (PITCH, PITCH), 1) < SEQ
    gain1, shift1, gain2, shift2 = (ref[...].reshape(1, 2 * wide) for ref in (gain1_ref, shift1_ref, gain2_ref, shift2_ref))
    my_cols = lanes_at(core_at * wide, wide)
    their_cols = lanes_at(other * wide, wide)

    def attend(image):
        normed, _ = norm_stats(tok_ref[image].astype(f32))
        h_one = (normed * gain1 + shift1).astype(bf16)
        queries = dot(h_one, qkv_ref[0], ((1,), (1,))).astype(bf16)
        keys = dot(h_one, qkv_ref[1], ((1,), (1,))).astype(bf16)
        values = dot(h_one, qkv_ref[2], ((1,), (1,))).astype(bf16)
        q_all[image] = queries
        k_all[image] = keys
        v_all[image] = values
        outs = []
        lse = jnp.zeros((PITCH, 2 * HD), f32)
        for head in range(heads):
            first = head // 2 * 2 * HD
            last = min(first + 2 * HD, heads * HD)
            q_head, k_head, v_head = queries[:, first:last], keys[:, first:last], values[:, first:last]
            if last - first == 2 * HD:
                q_head = jnp.where(head_mask(lane, head), q_head, jnp.zeros_like(q_head))
            scores = dot(q_head, k_head, ((1,), (1,))) * (HD**-0.5)
            scores = jnp.where(key_mask, scores, -1e30)
            peak = jnp.max(scores, axis=1, keepdims=True)
            powers = jnp.exp(scores - peak)
            row_sum = jnp.sum(powers, axis=1, keepdims=True)
            weights = (powers / row_sum).astype(bf16)
            outs.append(dot(weights, v_head))
            lse = jnp.where(lane == head, peak + jnp.log(row_sum), lse)
        lse_all[image] = lse
        joined = []
        for head in range(0, heads, 2):
            if head + 1 < heads:
                joined.append(jnp.where(lane < HD, outs[head], outs[head + 1]))
            else:
                joined.append(outs[head])
        attended = jnp.concatenate(joined, axis=1).astype(bf16)
        att_all[image] = attended
        part[...] = dot(attended, out_w_ref[...])
        mine[image] = part[:, my_cols]
        core_to[image] = part[:, their_cols].astype(bf16)

    def core_copy(image):
        return remote(core_to.at[image], core_from.at[image], core_s.at[image], core_r.at[image], core_dev)

    def x_copy(image):
        return remote(x_to.at[image], x_from.at[image], x_s.at[image], x_r.at[image], x_dev)

    def total_copy(image):
        return remote(total_to.at[image], total_from.at[image], tot_s.at[image], tot_r.at[image], core_dev)

    def h_block(side, image, core):
        return h_all.at[aligned(side * rows + image * PITCH, PITCH), lanes_at(core * wide, wide)]

    def y_copy(image):
        return remote(h_block(0, image, core_at), h_block(1, image, core_at), y_s.at[image], y_r.at[image], y_dev)

    def relay_copy(image):
        ref = h_block(1, image, core_at)
        return remote(ref, ref, rel_s.at[image], rel_r.at[image], core_dev)

    def relay_arriving(image):
        ref = h_block(1, image, other)
        return remote(ref, ref, rel_s.at[image], rel_r.at[image], core_dev)

    attend_outs = ((q_all, q_ref), (k_all, k_ref), (v_all, v_ref), (att_all, att_ref), (lse_all, lse_ref))

    def out_copies(image):
        copies = [
            pltpu.make_async_copy(kept.at[image], out.at[image], out_sem.at[n, image])
            for n, (kept, out) in enumerate(attend_outs)
        ]
        at = aligned(image * PITCH, PITCH)
        return copies, [
            pltpu.make_async_copy(resid_all.at[image], resid_ref.at[at, :], out_sem.at[5, image]),
            pltpu.make_async_copy(h_all.at[at, :], h_out.at[at, :], out_sem.at[6, image]),
        ]

    def other_copy(image):
        at = aligned(rows + image * PITCH, PITCH)
        return pltpu.make_async_copy(h_all.at[at, :], h_out.at[at, :], out_sem.at[7, image])

    def stage(tick, lag, run):
        image = tick - lag

        @pl.when((image >= 0) & (image < images))
        def _():
            run(image)

    def run_attend(image):
        attend(image)
        core_copy(image).start()
        for copy in out_copies(image)[0]:
            copy.start()

    def run_x(image):
        core_copy(image).wait_recv()
        x_to[image] = (mine[image] + core_from[image].astype(f32)).astype(bf16)
        x_copy(image).start()

    def run_total(image):
        x_copy(image).wait_recv()
        total_to[image] = (x_to[image].astype(f32) + x_from[image].astype(f32)).astype(bf16)
        total_copy(image).start()

    def run_norm(image):
        total_copy(image).wait_recv()
        part[:, my_cols] = total_to[image].astype(f32)
        part[:, their_cols] = total_from[image].astype(f32)
        resid = tok_ref[image].astype(f32) + part[...]
        resid_all[image] = resid
        normed, _ = norm_stats(resid)
        h_all[aligned(image * PITCH, PITCH), :] = (normed * gain2 + shift2).astype(bf16)
        y_copy(image).start()
        for copy in out_copies(image)[1]:
            copy.start()

    def run_relay(image):
        y_copy(image).wait_recv()
        relay_copy(image).start()

    def run_end(image):
        relay_arriving(image).wait_recv()
        other_copy(image).start()

    def at_tick(tick, when, run):
        @pl.when(tick == when)
        def _():
            run()

    def cot_step_one():
        cot_x_in.wait_recv()
        cot_share[0].start()

        @pl.when(core_at == 0)
        def _():
            relay_y.start()

        kept_y.wait_recv()
        kept_share.start()

    def cot_step_two():
        cot_y_in.wait_recv()
        cot_share[1].start()

        @pl.when(core_at == 1)
        def _():
            relay_x.start()

    def weights_step_one():
        await_hops(0)
        start_hops(1)

    def cot_step_three():
        relay_in.wait_recv()
        cot_share[2].start()

    def per_tick(tick, _):
        stage(tick, 0, run_attend)
        stage(tick, 1, run_x)
        stage(tick, 4, run_total)
        stage(tick, 5, run_norm)
        stage(tick, 9, run_relay)
        stage(tick, 10, run_end)
        at_tick(tick, 5, cot_step_one)
        at_tick(tick, 7, cot_step_two)
        at_tick(tick, 8, weights_step_one)
        at_tick(tick, 14, cot_step_three)
        return 0

    lax.fori_loop(0, images + 10, per_tick, 0)
    for copy in (*cot_share_in, kept_share_in):
        copy.wait_recv()
    outs = [
        pltpu.make_async_copy(cot_all, cot_out, cot_sem.at[0]),
        pltpu.make_async_copy(kept_all, kept_out, cot_sem.at[1]),
    ]
    for copy in outs:
        copy.start()
    for copy in (swap, kept_y, kept_share, cot_x, cot_y, *cot_share):
        copy.wait_send()

    @pl.when(core_at == 0)
    def _():
        relay_y.wait_send()

    @pl.when(core_at == 1)
    def _():
        relay_x.wait_send()

    def drain(image, _):
        for copy in (core_copy, x_copy, total_copy, y_copy, relay_copy):
            copy(image).wait_send()
        first, second = out_copies(image)
        for copy in (*first, *second, other_copy(image)):
            copy.wait()
        return 0

    lax.fori_loop(0, images, drain, 0)
    await_hops(1)
    for step in range(2):
        for way in range(2):

            @pl.when(hop_goes(step, way))
            def _():
                for copy in hop(step, way):
                    copy.wait_send()

    for copy in (*own_copies, *outs):
        copy.wait()


def run_forward(tok, gain1, shift1, gain2, shift2, qkv_w, out_w, up, down, cot, kept):
    images = tok.shape[0]
    rows = images * PITCH
    features = tok.shape[2]
    share = out_w.shape[0]
    heads = share // HD
    hidden = up.shape[1]
    wide = features // 2
    vmem = pl.BlockSpec(memory_space=pltpu.VMEM)
    anywhere = pl.BlockSpec(memory_space=pl.ANY)
    shape = jax.ShapeDtypeStruct
    block = (images, PITCH, wide)
    dma = pltpu.SemaphoreType.DMA
    return pl.pallas_call(
        partial(forward_kernel, images=images, heads=heads),
        out_shape=[
            shape((images, PITCH, share), bf16),
            shape((images, PITCH, share), bf16),
            shape((images, PITCH, share), bf16),
            shape((images, PITCH, share), bf16),
            shape((images, PITCH, 128), f32),
            shape((rows, features), f32),
            shape((2 * rows, features), bf16),
            shape((2 * rows, features), bf16),
            shape((2 * rows, 128), bf16),
            shape((2, features, 2 * hidden), bf16),
            shape((2, 2 * hidden, features), bf16),
        ],
        in_specs=[vmem] * 7 + [anywhere] * 2 + [vmem] * 2,
        out_specs=[anywhere] * 11,
        scratch_shapes=[
            *[pltpu.VMEM((images, PITCH, share), bf16)] * 4,
            pltpu.VMEM((images, PITCH, 128), f32),
            pltpu.VMEM((images, PITCH, features), f32),
            pltpu.VMEM((2 * rows, features), bf16),
            pltpu.VMEM((2 * rows, features), bf16),
            pltpu.VMEM((2 * rows, 128), bf16),
            pltpu.VMEM((PITCH, features), f32),
            pltpu.VMEM(block, f32),
            pltpu.VMEM(block, bf16),
            pltpu.VMEM(block, bf16),
            pltpu.VMEM(block, bf16),
            pltpu.VMEM(block, bf16),
            pltpu.VMEM(block, bf16),
            pltpu.VMEM(block, bf16),
            pltpu.VMEM((rows, share), bf16),
        ]
        + [dma((images,))] * 10
        + [dma((2, 2, 2))] * 2
        + [dma((9,))] * 2
        + [dma((2,)), dma((2,)), dma((8, images))],
        compiler_params=pltpu.CompilerParams(
            collective_id=1, has_side_effects=True, vmem_limit_bytes=60 << 20
        ),
    )(tok, gain1, shift1, gain2, shift2, qkv_w, out_w, up, down, cot, kept)


def expert_math(h_rows, cot_rows, kept, router, up, down, pair, experts):
    block = h_rows.shape[0]
    hidden = up.shape[1] // 2
    lane = lax.broadcasted_iota(jnp.int32, (block, 128), 1)
    logits = jnp.where(lane < experts, dot(h_rows, router), -1e30)
    powers = jnp.exp(logits - jnp.max(logits, axis=1, keepdims=True))
    probs = powers / jnp.sum(powers, axis=1, keepdims=True)
    gates = kept * probs
    pre_act = dot(h_rows, up)
    back = dot(cot_rows, down, ((1,), (1,)))
    normal_cdf = 0.5 + 0.5 * lax.erf(pre_act * 0.7071067811865476)
    gelu = pre_act * normal_cdf
    slope = normal_cdf + pre_act * (0.3989422804014327 * jnp.exp(-0.5 * pre_act * pre_act))
    product = gelu * back
    grad_gate = jnp.zeros((block, 128), f32)
    spread = []
    for side in range(2):
        chosen = lane == 2 * pair + side
        part = jnp.sum(product[:, side * hidden : (side + 1) * hidden], axis=1, keepdims=True)
        grad_gate = jnp.where(chosen, part, grad_gate)
        gate = jnp.sum(jnp.where(chosen, gates, 0.0), axis=1, keepdims=True)
        spread.append(jnp.broadcast_to(gate, (block, hidden)))
    gate = jnp.concatenate(spread, axis=1)
    hidden_rows = (gelu * gate).astype(bf16)
    grad_pre = (slope * back * gate).astype(bf16)
    return hidden_rows, grad_pre, probs, grad_gate


def first_pair_kernel(
    h_ref,
    cot_ref,
    kept_ref,
    router_ref,
    up_ref,
    down_ref,
    up_all,
    down_all,
    mixed_ref,
    grad_h_ref,
    gate_ref,
    grad_up_ref,
    grad_down_ref,
    up_late,
    down_late,
    up_sum,
    down_sum,
    late_s,
    late_r,
    *,
    experts,
    steps,
):
    expert_at = lax.axis_index("expert")
    tensor_at = lax.axis_index("tensor")
    z_at = expert_at // 2
    hidden = up_late.shape[1]
    partner = (jnp.where(z_at % 2 == 0, expert_at + 2, expert_at - 2), tensor_at)
    inner = (z_at == 1) | (z_at == 2)
    outer = (z_at == 0) | (z_at == 3)
    far = jnp.where(z_at == 1, hidden, 0)
    sources = (up_all.at[1, :, lanes_at(far, hidden)], down_all.at[1, aligned(far, hidden), :])
    hops = [
        pltpu.make_async_remote_copy(
            src_ref=source,
            dst_ref=target,
            send_sem=late_s.at[number],
            recv_sem=late_r.at[number],
            device_id=partner,
            device_id_type=MESH,
        )
        for number, (source, target) in enumerate(zip(sources, (up_late, down_late)))
    ]

    @pl.when(pl.program_id(0) == 0)
    def _():
        greet([(True, partner)])

        @pl.when(inner)
        def _():
            for copy in hops:
                copy.start()

        up_sum[...] = jnp.zeros_like(up_sum)
        down_sum[...] = jnp.zeros_like(down_sum)

    h_rows, cot_rows = h_ref[...], cot_ref[...]
    up, down = up_ref[0], down_ref[0]
    hidden_rows, grad_pre, _, grad_gate = expert_math(
        h_rows, cot_rows, kept_ref[...].astype(f32), router_ref[...], up, down, z_at // 2, experts
    )
    gate_ref[...] = grad_gate
    mixed_ref[...] = dot(hidden_rows, down).astype(bf16)
    grad_h_ref[...] = dot(grad_pre, up, ((1,), (1,))).astype(bf16)
    up_sum[...] += dot(h_rows.T, grad_pre)
    down_sum[...] += dot(cot_rows.T, hidden_rows)

    @pl.when(pl.program_id(0) == steps - 1)
    def _():
        grad_up_ref[...] = up_sum[...].astype(bf16)
        grad_down_ref[...] = down_sum[...].astype(bf16)

        @pl.when(inner)
        def _():
            for copy in hops:
                copy.wait_send()

        @pl.when(outer)
        def _():
            for copy in hops:
                copy.wait_recv()


BLOCK = 2 * PITCH


def run_first_pair(h_rows, cot_rows, kept, router, up, down, experts):
    rows, features = h_rows.shape
    width = up.shape[2]
    steps = rows // BLOCK
    anywhere = pl.BlockSpec(memory_space=pl.ANY)
    shape = jax.ShapeDtypeStruct

    def by_step(lanes):
        return pl.BlockSpec((BLOCK, lanes), lambda n: (n, 0))

    def whole(*dims):
        return pl.BlockSpec(dims, lambda n: (0,) * len(dims))

    return pl.pallas_call(
        partial(first_pair_kernel, experts=experts, steps=steps),
        grid=(steps,),
        out_shape=[
            shape((rows, features), bf16),
            shape((rows, features), bf16),
            shape((rows, 128), f32),
            shape((features, width), bf16),
            shape((features, width), bf16),
            shape((features, width // 2), bf16),
            shape((width // 2, features), bf16),
        ],
        in_specs=[
            by_step(features),
            by_step(features),
            by_step(128),
            whole(features, 128),
            whole(1, features, width),
            whole(1, width, features),
            anywhere,
            anywhere,
        ],
        out_specs=[
            by_step(features),
            by_step(features),
            by_step(128),
            whole(features, width),
            whole(features, width),
            anywhere,
            anywhere,
        ],
        scratch_shapes=[pltpu.VMEM((features, width), f32)] * 2 + [pltpu.SemaphoreType.DMA((2,))] * 2,
        compiler_params=pltpu.CompilerParams(
            collective_id=3, has_side_effects=True, vmem_limit_bytes=60 << 20
        ),
    )(h_rows, cot_rows, kept, router, up, down, up, down)


def turn_is_other(turn):
    return (turn == 0) | ((turn % 2 == 1) & (turn < 7))


def turn_block(turn):
    own = jnp.where(turn == 7, 3, turn // 2 - 1)
    return jnp.where(turn_is_other(turn), 4 + (turn + 1) // 2, own)


def second_pair_kernel(
    h_ref,
    cot_ref,
    kept_ref,
    router_ref,
    mixed_first,
    grad_h_first,
    gate_first,
    up_all,
    down_all,
    up_late,
    down_late,
    up_first,
    down_first,
    mixed_ref,
    grad_up_ref,
    grad_down_ref,
    grad_router_ref,
    grad_h_out,
    up_pair,
    down_pair,
    up_vm,
    down_vm,
    up_sum,
    down_sum,
    router_sum,
    ring,
    from_core,
    from_y,
    from_x,
    load,
    core_s,
    core_r,
    y_s,
    y_r,
    x_s,
    x_r,
    tot_s,
    tot_r,
    store,
    pair_s,
    pair_r,
    *,
    experts,
    steps,
):
    turn = pl.program_id(0)
    expert_at = lax.axis_index("expert")
    tensor_at = lax.axis_index("tensor")
    z_at, y_at = expert_at // 2, expert_at % 2
    x_at, core_at = tensor_at // 2, tensor_at % 2
    hidden = up_late.shape[1]
    wide = ring.shape[2] // 2
    core_dev = (expert_at, tensor_at + 1 - 2 * core_at)
    x_dev = (expert_at, tensor_at + 2 - 4 * x_at)
    y_dev = (expert_at + 1 - 2 * y_at, tensor_at)
    my_cols = lanes_at(core_at * wide, wide)
    their_cols = lanes_at((1 - core_at) * wide, wide)

    def remote(src, dst, send, recv, device):
        return pltpu.make_async_remote_copy(
            src_ref=src, dst_ref=dst, send_sem=send, recv_sem=recv, device_id=device, device_id_type=MESH
        )

    def core_copy(number):
        return remote(ring.at[number % 2, :, their_cols], from_core.at[number], core_s.at[number], core_r.at[number], core_dev)

    def y_copy(number, place):
        return remote(from_core.at[number], from_y.at[place], y_s.at[place], y_r.at[place], y_dev)

    def x_copy(number, place):
        return remote(from_core.at[number], from_x.at[place], x_s.at[place], x_r.at[place], x_dev)

    def out_rows(place):
        return grad_h_out.at[aligned(place * BLOCK, BLOCK), my_cols]

    def total_copy(place):
        return remote(from_x.at[place], out_rows(place), tot_s.at[place], tot_r.at[place], core_dev)

    def store_copy(place):
        return pltpu.make_async_copy(from_x.at[place], out_rows(place), store.at[place])

    def own_turn(place):
        return jnp.where(place == 3, 7, 2 * place + 2)

    def other_turn(place):
        return jnp.where(place == 0, 0, 2 * place - 1)

    def pass_other(number):
        core_copy(number).wait_recv()
        total = from_core[number].astype(f32) + ring[number % 2, :, my_cols].astype(f32)
        from_core[number] = total.astype(bf16)
        y_copy(number, (number + 1) // 2).start()

    def pass_own(number, place):
        core_copy(number).wait_recv()
        y_copy(number, place).wait_recv()
        total = from_core[number].astype(f32) + ring[number % 2, :, my_cols].astype(f32) + from_y[place].astype(f32)
        from_core[number] = total.astype(bf16)
        x_copy(number, place).start()

    def pass_total(place):
        number = own_turn(place)
        x_copy(number, place).wait_recv()
        from_x[place] = (from_core[number].astype(f32) + from_x[place].astype(f32)).astype(bf16)
        total_copy(place).start()
        store_copy(place).start()

    z_dev = (jnp.where(z_at % 2 == 0, expert_at + 2, expert_at - 2), tensor_at)
    pair_lanes = lanes_at((1 - z_at % 2) * hidden, hidden)
    pair_copies = [
        remote(source.at[:, pair_lanes], target, pair_s.at[number], pair_r.at[number], z_dev)
        for number, (source, target) in enumerate(((up_first, up_pair), (down_first, down_pair)))
    ]

    @pl.when(turn == 0)
    def _():
        greet([(True, core_dev), (True, x_dev), (True, y_dev), (True, z_dev)])
        for copy in pair_copies:
            copy.start()
        late_expert = jnp.where(z_at == 0, 1, 0)
        late = late_expert * hidden
        is_outer = (z_at == 0) | (z_at == 3)
        whole = [
            pltpu.make_async_copy(up_all.at[1], up_vm, load.at[0]),
            pltpu.make_async_copy(down_all.at[1], down_vm, load.at[1]),
        ]
        for copy in whole:
            copy.start()
        up_sum[...] = jnp.zeros_like(up_sum)
        down_sum[...] = jnp.zeros_like(down_sum)
        router_sum[...] = jnp.zeros_like(router_sum)
        for copy in whole:
            copy.wait()

        @pl.when(is_outer)
        def _():
            parts = [
                pltpu.make_async_copy(up_late, up_vm.at[:, lanes_at(late, hidden)], load.at[0]),
                pltpu.make_async_copy(down_late, down_vm.at[aligned(late, hidden), :], load.at[1]),
            ]
            for copy in parts:
                copy.start()
            for copy in parts:
                copy.wait()

    h_rows, cot_rows = h_ref[...], cot_ref[...]
    up, down, router = up_vm[...], down_vm[...], router_ref[...]
    kept = kept_ref[...].astype(f32)
    hidden_rows, grad_pre, probs, grad_gate = expert_math(
        h_rows, cot_rows, kept, router, up, down, 1 - z_at // 2, experts
    )
    grad_gate = kept * (grad_gate + gate_first[...])
    grad_logits = (probs * (grad_gate - jnp.sum(probs * grad_gate, axis=1, keepdims=True))).astype(bf16)

    before = turn - 1

    @pl.when((turn >= 1) & turn_is_other(before))
    def _():
        pass_other(before)

    @pl.when((turn == 5) | (turn == 7))
    def _():
        pass_total((turn - 5) // 2)

    @pl.when((turn == 3) | (turn == 5) | (turn == 7))
    def _():
        pass_own(before, (turn - 3) // 2)

    mixed_ref[...] = (mixed_first[...].astype(f32) + dot(hidden_rows, down)).astype(bf16)

    @pl.when(turn >= 2)
    def _():
        core_copy(turn - 2).wait_send()

    ring[turn % 2] = (
        grad_h_first[...].astype(f32) + dot(grad_pre, up, ((1,), (1,))) + dot(grad_logits, router, ((1,), (1,)))
    ).astype(bf16)
    core_copy(turn).start()
    h_turned = h_rows.T
    up_sum[...] += dot(h_turned, grad_pre)
    router_sum[...] += dot(h_turned, grad_logits)
    down_sum[...] += dot(cot_rows.T, hidden_rows)

    @pl.when(turn == steps - 1)
    def _():
        pass_own(7, 3)
        pass_total(2)
        grad_up_ref[...] = up_sum[...].astype(bf16)
        grad_down_ref[...] = down_sum[...].astype(bf16)
        grad_router_ref[...] = router_sum[...].T[:8]
        pass_total(3)
        for copy in pair_copies:
            copy.wait()
        for number in (6, 7):
            core_copy(number).wait_send()
        for place in range(4):
            y_copy(other_turn(place), place).wait_send()
            x_copy(own_turn(place), place).wait_send()
            total_copy(place).wait_send()
            total_copy(place).wait_recv()
            store_copy(place).wait()


def run_second_pair(
    h_rows,
    cot_rows,
    kept,
    router,
    mixed_first,
    grad_h_first,
    gate_first,
    up,
    down,
    up_late,
    down_late,
    up_first,
    down_first,
    experts,
):
    rows, features = h_rows.shape
    width = up.shape[2]
    steps = rows // BLOCK
    half = (BLOCK, features // 2)
    anywhere = pl.BlockSpec(memory_space=pl.ANY)
    shape = jax.ShapeDtypeStruct
    dma = pltpu.SemaphoreType.DMA

    def by_step(lanes):
        return pl.BlockSpec((BLOCK, lanes), lambda n: (turn_block(n), 0))

    def whole(*dims):
        return pl.BlockSpec(dims, lambda n: (0,) * len(dims))

    return pl.pallas_call(
        partial(second_pair_kernel, experts=experts, steps=steps),
        grid=(steps,),
        out_shape=[
            shape((rows, features), bf16),
            shape((features, width), bf16),
            shape((features, width), bf16),
            shape((8, features), f32),
            shape((rows // 2, features), bf16),
            shape((features, width // 2), bf16),
            shape((features, width // 2), bf16),
        ],
        in_specs=[
            by_step(features),
            by_step(features),
            by_step(128),
            whole(features, 128),
            by_step(features),
            by_step(features),
            by_step(128),
        ]
        + [anywhere] * 6,
        out_specs=[by_step(features), whole(features, width), whole(features, width), whole(8, features)] + [anywhere] * 3,
        scratch_shapes=[
            pltpu.VMEM((features, width), bf16),
            pltpu.VMEM((width, features), bf16),
            pltpu.VMEM((features, width), f32),
            pltpu.VMEM((features, width), f32),
            pltpu.VMEM((features, 128), f32),
            pltpu.VMEM((2, BLOCK, features), bf16),
            pltpu.VMEM((8, *half), bf16),
            pltpu.VMEM((4, *half), bf16),
            pltpu.VMEM((4, *half), bf16),
            dma((2,)),
        ]
        + [dma((8,))] * 2
        + [dma((4,))] * 7
        + [dma((2,))] * 2,
        compiler_params=pltpu.CompilerParams(
            collective_id=4, has_side_effects=True, vmem_limit_bytes=60 << 20
        ),
    )(h_rows, cot_rows, kept, router, mixed_first, grad_h_first, gate_first, up, down, up_late, down_late, up_first, down_first)


def backward_kernel(
    tok_ref,
    gain1_ref,
    shift1_ref,
    gain2_ref,
    qkv_ref,
    out_w_ref,
    q_ref,
    k_ref,
    v_ref,
    att_ref,
    lse_ref,
    grad_h_ref,
    grad_router_ref,
    resid_ref,
    cot_ref,
    mixed_ref,
    up_first,
    down_first,
    up_pair,
    down_pair,
    up_second,
    down_second,
    up_out,
    down_out,
    tokens_out,
    qkv_out,
    out_w_out,
    sums_out,
    mixed_out,
    rows_kept,
    cot_rows,
    m_mine,
    m_core,
    m_y,
    m_x,
    m_out,
    m_resid,
    own_vm,
    pair_vm,
    far_vm,
    one_mine,
    one_to,
    one_core,
    one_x,
    one_total,
    line,
    weight_sum,
    weight_half,
    shared,
    shared_y,
    shared_line,
    shared_all,
    route_core,
    route_x,
    late_mine,
    late_y,
    late_z,
    whole,
    mc_s,
    mc_r,
    my_s,
    my_r,
    mx_s,
    mx_r,
    mq_s,
    mq_r,
    m_store,
    oc_s,
    oc_r,
    ox_s,
    ox_r,
    ot_s,
    ot_r,
    l_s,
    l_r,
    sy_s,
    sy_r,
    sl_s,
    sl_r,
    sg_s,
    sg_r,
    sz_s,
    sz_r,
    r_s,
    r_r,
    late_s,
    late_r,
    load,
    own_sem,
    weight_store,
    store,
    *,
    images,
    heads,
):
    expert_at = lax.axis_index("expert")
    tensor_at = lax.axis_index("tensor")
    z_at, y_at = expert_at // 2, expert_at % 2
    z_last = lax.axis_size("expert") // 2 - 1
    x_at, core_at = tensor_at // 2, tensor_at % 2
    other = 1 - core_at
    rows = images * PITCH
    features = tok_ref.shape[2]
    wide = features // 2
    share = out_w_ref.shape[0]
    hidden = line.shape[3]
    core_dev = (expert_at, tensor_at + 1 - 2 * core_at)
    x_dev = (expert_at, tensor_at + 2 - 4 * x_at)
    y_dev = (expert_at + 1 - 2 * y_at, tensor_at)
    z_devs = [(expert_at + 2, tensor_at), (expert_at - 2, tensor_at)]
    planes = z_last + 1
    z_others = [((z_at + hop) % planes * 2 + y_at, tensor_at) for hop in (1, 2, 3)]
    greet([(True, device) for device in (core_dev, x_dev, y_dev, *z_others)])
    my_cols = lanes_at(core_at * wide, wide)
    their_cols = lanes_at(other * wide, wide)

    def remote(src, dst, send, recv, device):
        return pltpu.make_async_remote_copy(
            src_ref=src, dst_ref=dst, send_sem=send, recv_sem=recv, device_id=device, device_id_type=MESH
        )

    def at_image(image):
        return aligned(image * PITCH, PITCH)

    part_count = m_y.shape[0]
    part_rows_m = rows // part_count

    def m_rows(side, part):
        return aligned(side * rows + part * part_rows_m, part_rows_m)

    def m_core_copy(side, part):
        at = m_rows(side, part)
        return remote(mixed_ref.at[at, their_cols], m_core.at[at, :], mc_s.at[side, part], mc_r.at[side, part], core_dev)

    for part in range(part_count):
        m_core_copy(1, part).start()
    for part in range(part_count):
        m_core_copy(0, part).start()
    loads = [
        pltpu.make_async_copy(resid_ref, rows_kept, load.at[0]),
        pltpu.make_async_copy(cot_ref.at[pl.ds(0, rows), :], cot_rows, load.at[1]),
        pltpu.make_async_copy(mixed_ref.at[:, my_cols], m_mine, load.at[2]),
    ]
    for copy in loads:
        copy.start()
    route_one = remote(grad_router_ref, route_core, r_s.at[0], r_r.at[0], core_dev)
    route_one.start()

    def place(way):
        return z_at if way == 0 else z_last - z_at

    def far_lanes(way, piece):
        expert = z_last - piece // 2 if way == 0 else piece // 2
        return pl.ds(expert % 2 * hidden, hidden)

    def line_copy(source, way, piece):
        return remote(source, line.at[way, piece], l_s.at[way, piece], l_r.at[way, piece], z_devs[way])

    def line_copy_on(way, piece):
        return line_copy(line.at[way, piece], way, piece)

    def line_start():
        for way in range(2):

            @pl.when(place(way) == 0)
            def _():
                for piece in range(4):
                    source = (up_second, down_second)[piece % 2]
                    line_copy(source.at[:, far_lanes(way, piece)], way, piece).start()

    def line_add(piece):
        for way in range(2):

            @pl.when(place(way) == 1)
            def _():
                line_copy_on(way, piece).wait_recv()
                lanes = far_lanes(way, piece)

                def add(part, _):
                    at_rows = aligned(part * 96, 96)
                    total = line[way, piece, at_rows, :].astype(f32) + far_vm[piece % 2, at_rows, lanes].astype(f32)
                    line[way, piece, at_rows, :] = total.astype(bf16)
                    return 0

                lax.fori_loop(0, features // 96, add, 0)
                line_copy_on(way, piece).start()

    def line_pass(piece):
        for way in range(2):

            @pl.when(place(way) == 2)
            def _():
                line_copy_on(way, piece).wait_recv()
                line_copy_on(way, piece).start()

    line_start()
    own_lanes = lanes_at(z_at % 2 * hidden, hidden)
    later = [
        pltpu.make_async_copy(source, target, own_sem.at[number])
        for number, (source, target) in enumerate(
            (
                (up_second, far_vm.at[0]),
                (down_second, far_vm.at[1]),
                (up_first.at[:, own_lanes], own_vm.at[0]),
                (down_first.at[:, own_lanes], own_vm.at[1]),
                (up_pair, pair_vm.at[0]),
                (down_pair, pair_vm.at[1]),
            )
        )
    ]
    for copy in loads:
        copy.wait()
    for copy in later:
        copy.start()
    weight_sum[...] = jnp.zeros_like(weight_sum)
    late_mine[...] = jnp.zeros_like(late_mine)

    def m_y_copy(part):
        return remote(m_core.at[m_rows(1, part), :], m_y.at[part], my_s.at[part], my_r.at[part], y_dev)

    def m_x_copy(part):
        return remote(m_core.at[m_rows(0, part), :], m_x.at[part], mx_s.at[part], mx_r.at[part], x_dev)

    def m_place(part):
        return mixed_out.at[aligned(part * part_rows_m, part_rows_m), :]

    def m_quarter_copy(part):
        return remote(m_out.at[part, other], m_place(part), mq_s.at[part], mq_r.at[part], core_dev)

    def m_store_copy(part):
        return pltpu.make_async_copy(m_out.at[part, core_at], m_place(part), m_store.at[part])

    def m_resid_copy(part):
        at = aligned(part * part_rows_m, part_rows_m)
        return pltpu.make_async_copy(resid_ref.at[at, lanes_at(x_at * wide, wide)], m_resid, load.at[3])

    keeps = x_at == core_at

    def run_m_y(part):
        m_core_copy(1, part).wait_recv()
        at = m_rows(1, part)
        m_core[at, :] = (m_core[at, :].astype(f32) + m_mine[at, :].astype(f32)).astype(bf16)
        m_y_copy(part).start()

    def run_m_x(part):
        m_core_copy(0, part).wait_recv()
        m_y_copy(part).wait_recv()
        at = m_rows(0, part)
        total = m_core[at, :].astype(f32) + m_mine[at, :].astype(f32) + m_y[part].astype(f32)
        m_core[at, :] = total.astype(bf16)

        @pl.when(jnp.logical_not(keeps))
        def _():
            m_x_copy(part).start()

    def run_m_out(part):
        @pl.when(keeps)
        def _():
            m_resid_copy(part).start()
            m_x_copy(part).wait_recv()
            m_resid_copy(part).wait()
            total = m_core[m_rows(0, part), :].astype(f32) + m_x[part].astype(f32)
            mixed = (m_resid[...] + total).astype(bf16)
            m_out[part, 0] = mixed[:, : wide // 2]
            m_out[part, 1] = mixed[:, wide // 2 :]
            m_quarter_copy(part).start()
            m_store_copy(part).start()

    for part in range(part_count):
        run_m_y(part)
    route_one.wait_recv()
    route_core[...] += grad_router_ref[...]
    route_two = remote(route_core, route_x, r_s.at[1], r_r.at[1], x_dev)
    route_two.start()

    def one_core_copy(image):
        return remote(one_to.at[image], one_core.at[image], oc_s.at[image], oc_r.at[image], core_dev)

    def one_x_copy(image):
        return remote(one_core.at[image], one_x.at[image], ox_s.at[image], ox_r.at[image], x_dev)

    def one_total_copy(image):
        return remote(one_x.at[image], one_total.at[image], ot_s.at[image], ot_r.at[image], core_dev)

    store_copy = pltpu.make_async_copy(rows_kept.at[pl.ds(0, images * SEQ), :], tokens_out, store.at[0])

    lane = lax.broadcasted_iota(jnp.int32, (PITCH, 2 * HD), 1)
    key_mask = lax.broadcasted_iota(jnp.int32, (PITCH, PITCH), 1) < SEQ
    gain1, shift1, gain2 = (ref[...].reshape(1, features) for ref in (gain1_ref, shift1_ref, gain2_ref))

    def norm_back(grad, gain, normed, inverse):
        scaled = grad * gain
        mean = jnp.mean(scaled, axis=1, keepdims=True)
        along = jnp.mean(scaled * normed, axis=1, keepdims=True)
        return (scaled - mean - normed * along) * inverse

    def add_sums(sums, row, grad, normed):
        sums[row : row + 1, :] += jnp.sum(grad * normed, axis=0, keepdims=True)
        sums[row + 1 : row + 2, :] += jnp.sum(grad, axis=0, keepdims=True)

    def run_attention(image):
        at = at_image(image)
        grad_h = grad_h_ref[at, :].astype(f32)
        normed, inverse = norm_stats(rows_kept[at, :])
        add_sums(weight_sum, features, grad_h, normed)
        grad_resid = cot_rows[at, :].astype(f32) + norm_back(grad_h, gain2, normed, inverse)
        rows_kept[at, :] = grad_resid
        grad_branch = grad_resid.astype(bf16)
        token_normed, _ = norm_stats(tok_ref[image].astype(f32))
        h_one = (token_normed * gain1 + shift1).astype(bf16)
        queries, keys, values, attended = q_ref[image], k_ref[image], v_ref[image], att_ref[image]
        lse = lse_ref[image]
        grad_attended = dot(grad_branch, out_w_ref[...], ((1,), (1,))).astype(bf16)
        grads = [[], [], []]
        for head in range(heads):
            first = head // 2 * 2 * HD
            last = min(first + 2 * HD, heads * HD)
            parts = [whose[:, first:last] for whose in (queries, keys, values, grad_attended)]
            if last - first == 2 * HD:
                own = head_mask(lane, head)
                q_own, k_own, _, g_own = (jnp.where(own, part, jnp.zeros_like(part)) for part in parts)
            else:
                q_own, k_own, _, g_own = parts
            scores = dot(q_own, parts[1], ((1,), (1,))) * (HD**-0.5)
            probs = jnp.where(key_mask, jnp.exp(scores - lse[:, head : head + 1]), 0.0)
            back = dot(g_own, parts[2], ((1,), (1,)))
            product = probs * back
            grad_scores = (product - probs * jnp.sum(product, axis=1, keepdims=True)).astype(bf16)
            pieces = (
                dot(grad_scores, k_own) * (HD**-0.5),
                dot(grad_scores, q_own, ((0,), (0,))) * (HD**-0.5),
                dot(probs.astype(bf16), g_own, ((0,), (0,))),
            )
            for which in range(3):
                if head % 2 == 0:
                    grads[which].append(pieces[which])
                else:
                    grads[which][-1] += pieces[which]
        grad_rows = [jnp.concatenate(grads[which], axis=1).astype(bf16) for which in range(3)]
        grad_one = 0.0
        for which in range(3):
            weight_sum[which * share : (which + 1) * share, :] += dot(grad_rows[which].T, h_one)
            grad_one += dot(grad_rows[which], qkv_ref[which])
        weight_sum[3 * share : 4 * share, :] += dot(attended.T, grad_branch)
        whole[...] = grad_one
        one_mine[image] = whole[:, my_cols].astype(bf16)
        one_to[image] = whole[:, their_cols].astype(bf16)
        one_core_copy(image).start()

    def run_one_x(image):
        one_core_copy(image).wait_recv()
        one_core[image] = (one_core[image].astype(f32) + one_mine[image].astype(f32)).astype(bf16)
        one_x_copy(image).start()

    def run_one_total(image):
        one_x_copy(image).wait_recv()
        one_x[image] = (one_core[image].astype(f32) + one_x[image].astype(f32)).astype(bf16)
        one_total_copy(image).start()

    def run_tokens(image):
        one_total_copy(image).wait_recv()
        whole[:, my_cols] = one_x[image].astype(f32)
        whole[:, their_cols] = one_total[image].astype(f32)
        grad_one = whole[...]
        at = at_image(image)
        normed, inverse = norm_stats(tok_ref[image].astype(f32))
        add_sums(late_mine, 0, grad_one, normed)
        total = rows_kept[at, :] + norm_back(grad_one, gain1, normed, inverse)
        whole[...] = total
        for number in range(images):

            @pl.when(image == number)
            def _():
                rows_kept[pl.ds(number * SEQ, SEQ), :] = whole[pl.ds(0, SEQ), :]


    def stage(tick, lag, run):
        image = tick - lag

        @pl.when((image >= 0) & (image < images))
        def _():
            run(image)

    def m_stage(tick, ticks, run):
        part = sum(jnp.where(tick > when, 1, 0) for when in ticks)
        falls = sum(jnp.where(tick == when, 1, 0) for when in ticks)

        @pl.when(falls == 1)
        def _():
            run(part)

    def per_tick(tick, _):
        stage(tick, 0, run_attention)
        stage(tick, 1, run_one_x)
        stage(tick, 2, run_one_total)
        stage(tick, 3, run_tokens)
        m_stage(tick, (2, 4, 5, 7), run_m_x)
        m_stage(tick, (4, 5, 7), run_m_out)

        @pl.when(tick == 2)
        def _():
            later[0].wait()
            later[1].wait()
            line_add(0)

        @pl.when(tick == 5)
        def _():
            line_add(1)
            line_pass(0)

        return 0

    lax.fori_loop(0, images, per_tick, 0)

    route_two.wait_recv()
    weight_sum[features + 8 : features + 16, :] = route_core[...] + route_x[...]
    part_rows = shared.shape[1]
    quarter = part_rows // (z_last + 1)

    def to_half(side):
        def cast(piece, _):
            at_rows = aligned(piece * quarter, quarter)
            shared[side, at_rows, :] = weight_sum[aligned(side * part_rows + piece * quarter, quarter), :].astype(bf16)
            return 0

        lax.fori_loop(0, z_last + 1, cast, 0)

    to_half(0)
    to_half(1)

    def y_piece(number):
        inner = jnp.where(z_at == 1, jnp.where(number < 2, z_last - number, number - 2), jnp.where(number < 2, number, 5 - number))
        return jnp.where(z_at == 0, z_last - number, jnp.where(z_at == z_last, number, inner))

    def quarter_at(piece):
        return aligned(piece * quarter, quarter)

    def shared_y_copy(number):
        at_rows = quarter_at(y_piece(number))
        return remote(shared.at[1 - y_at, at_rows, :], shared_y.at[at_rows, :], sy_s.at[number], sy_r.at[number], y_dev)

    def take_y(number):
        shared_y_copy(number).wait_recv()
        at_rows = quarter_at(y_piece(number))
        weight_half[at_rows, :] = shared[y_at, at_rows, :].astype(f32) + shared_y[at_rows, :].astype(f32)

    for number in range(4):
        shared_y_copy(number).start()
    run_one_x(images - 1)
    run_one_total(images - 2)
    run_tokens(images - 3)
    line_pass(1)
    line_add(2)

    def quarter_of(step, at, way):
        mirrored = z_last - step + at
        return mirrored if way == 0 else z_last - mirrored

    late_y_copy = remote(late_mine, late_y, late_s.at[0], late_r.at[0], y_dev)

    def late_copy(number):
        ref = late_z.at[z_at]
        return remote(ref, ref, late_s.at[number + 1], late_r.at[number + 1], z_others[number])

    def small_copy(step, way):
        return remote(shared_line.at[way, 0, step], shared_line.at[way, 1, step], sl_s.at[way, step], sl_r.at[way, step], z_devs[way])

    for step in range(3):
        take_y(step)
        if step == 2:
            take_y(3)
        for way in range(2):
            at = place(way)

            @pl.when((at <= step) & (at < z_last))
            def _():
                at_rows = quarter_at(quarter_of(step, at, way))
                if step == 0:
                    shared_line[way, 0, step] = weight_half[at_rows, :].astype(bf16)
                else:
                    came = jnp.where(at > 0, shared_line[way, 1, step - 1].astype(f32), 0.0)
                    shared_line[way, 0, step] = (weight_half[at_rows, :] + came).astype(bf16)
                small_copy(step, way).start()

        for way in range(2):
            at = place(way)

            @pl.when((at > 0) & (at - 1 <= step))
            def _():
                small_copy(step, way).wait_recv()

        if step == 0:
            run_one_total(images - 1)
            run_tokens(images - 2)
        if step == 1:
            run_tokens(images - 1)
            late_y_copy.start()
            store_copy.start()
            run_m_out(part_count - 1)
            line_add(3)

    late_y_copy.wait_recv()
    late_z[z_at] = late_mine[...] + late_y[...]
    for number in range(planes - 1):
        late_copy(number).start()
    own_rows = quarter_at(z_at)
    from_below = jnp.where(z_at > 0, shared_line[0, 1, 2].astype(f32), 0.0)
    from_above = jnp.where(z_at < z_last, shared_line[1, 1, 2].astype(f32), 0.0)

    def final_rows(side, piece):
        return shared_all.at[side, quarter_at(piece), :]

    shared_all[y_at, own_rows, :] = (weight_half[own_rows, :] + from_below + from_above).astype(bf16)
    for number in range(4):
        shared_y_copy(number).wait_send()

    def gather_z(step, way, piece):
        ref = final_rows(y_at, piece)
        return remote(ref, ref, sg_s.at[way, step], sg_r.at[way, step], z_devs[way])

    def gather_y(step, way, piece, side):
        ref = final_rows(side, piece)
        return remote(ref, ref, sz_s.at[way, step], sz_r.at[way, step], y_dev)

    gather_y(0, 0, z_at, y_at).start()
    for step in range(3):
        for way in range(2):
            at = place(way)
            piece = z_at - step if way == 0 else z_at + step

            @pl.when((at >= step) & (at < z_last))
            def _():
                gather_z(step, way, piece).start()

        for way in range(2):
            at = place(way)
            piece = z_at - 1 - step if way == 0 else z_at + 1 + step

            @pl.when(at >= 1 + step)
            def _():
                gather_z(step, way, piece).wait_recv()
                gather_y(step + 1, way, piece, y_at).start()

    gather_y(0, 0, z_at, 1 - y_at).wait_recv()
    for step in range(3):
        for way in range(2):
            at = place(way)
            piece = z_at - 1 - step if way == 0 else z_at + 1 + step

            @pl.when(at >= 1 + step)
            def _():
                gather_y(step + 1, way, piece, 1 - y_at).wait_recv()

    def to_out(piece, _):
        for side in range(2):
            weight_sum[aligned(side * part_rows + piece * quarter, quarter), :] = shared_all[
                side, quarter_at(piece), :
            ].astype(f32)
        return 0

    lax.fori_loop(0, z_last + 1, to_out, 0)
    for number in range(planes - 1):
        late_copy(number).wait_recv()
    late = late_z[0]
    for plane in range(1, planes):
        late += late_z[plane]
    weight_sum[features + 2 : features + 4, :] = late[:2]
    weight_copies = [
        *[
            pltpu.make_async_copy(weight_sum.at[pl.ds(n * share, share), :], qkv_out.at[n], weight_store.at[n])
            for n in range(3)
        ],
        pltpu.make_async_copy(weight_sum.at[pl.ds(3 * share, share), :], out_w_out, weight_store.at[3]),
        pltpu.make_async_copy(weight_sum.at[pl.ds(features, 16), :], sums_out, weight_store.at[4]),
    ]
    for copy in weight_copies:
        copy.start()
    for copy in later[2:]:
        copy.wait()
    for way in range(2):

        @pl.when(place(way) == 2)
        def _():
            line_copy_on(way, 2).wait_recv()
            line_copy_on(way, 3).wait_recv()

        @pl.when(place(way) == z_last)
        def _():
            line_copy_on(way, 0).wait_recv()
            line_copy_on(way, 1).wait_recv()

    from_far = 1 - z_at // 2
    first_piece = jnp.where((z_at == 0) | (z_at == z_last), 0, 2)

    def finish(piece, _):
        at_rows = aligned(piece * 128, 128)
        totals = [
            own_vm[n, at_rows, :].astype(f32)
            + pair_vm[n, at_rows, :].astype(f32)
            + line[from_far, first_piece + n, at_rows, :].astype(f32)
            for n in range(2)
        ]
        up_out[at_rows, :] = totals[0]
        down_out[:, lanes_at(piece * 128, 128)] = totals[1].T
        return 0

    lax.fori_loop(0, features // 128, finish, 0)

    route_one.wait_send()
    route_two.wait_send()

    def drain(image, _):
        for copy in (one_core_copy, one_x_copy, one_total_copy):
            copy(image).wait_send()
        return 0

    lax.fori_loop(0, images, drain, 0)
    for part in range(part_count):
        m_core_copy(0, part).wait_send()
        m_core_copy(1, part).wait_send()
        m_y_copy(part).wait_send()

        @pl.when(keeps)
        def _():
            m_quarter_copy(part).wait_send()
            m_store_copy(part).wait()

        @pl.when(jnp.logical_not(keeps))
        def _():
            m_x_copy(part).wait_send()
            m_quarter_copy(part).wait_recv()

    for copy in (*weight_copies, store_copy):
        copy.wait()
    late_y_copy.wait_send()
    for number in range(planes - 1):
        late_copy(number).wait_send()
    gather_y(0, 0, z_at, y_at).wait_send()
    for way in range(2):

        @pl.when(place(way) <= 1)
        def _():
            for piece in range(4):
                line_copy_on(way, piece).wait_send()

        @pl.when(place(way) == 2)
        def _():
            for piece in range(2):
                line_copy_on(way, piece).wait_send()

    for step in range(3):
        for way in range(2):
            at = place(way)

            @pl.when((at <= step) & (at < z_last))
            def _():
                small_copy(step, way).wait_send()

            piece = z_at - step if way == 0 else z_at + step

            @pl.when((at >= step) & (at < z_last))
            def _():
                gather_z(step, way, piece).wait_send()

            piece = z_at - 1 - step if way == 0 else z_at + 1 + step

            @pl.when(at >= 1 + step)
            def _():
                gather_y(step + 1, way, piece, y_at).wait_send()


def run_backward(
    tok,
    gain1,
    shift1,
    gain2,
    qkv_w,
    out_w,
    q,
    k,
    v,
    att,
    lse,
    grad_h,
    grad_router,
    resid,
    cot,
    mixed,
    up_first,
    down_first,
    up_pair,
    down_pair,
    up_second,
    down_second,
):
    images, _, features = tok.shape
    rows = images * PITCH
    share = out_w.shape[0]
    heads = share // HD
    hidden = up_first.shape[1] // 2
    wide = features // 2
    packed = features + 128
    parts = 4
    vmem = pl.BlockSpec(memory_space=pltpu.VMEM)
    anywhere = pl.BlockSpec(memory_space=pl.ANY)
    shape = jax.ShapeDtypeStruct
    dma = pltpu.SemaphoreType.DMA
    block = (images, PITCH, wide)
    return pl.pallas_call(
        partial(backward_kernel, images=images, heads=heads),
        out_shape=[
            shape((features, hidden), f32),
            shape((hidden, features), f32),
            shape((images * SEQ, features), f32),
            shape((3, share, features), f32),
            shape((share, features), f32),
            shape((16, features), f32),
            shape((rows, wide // 2), bf16),
        ],
        in_specs=[vmem] * 13 + [anywhere] * 9,
        out_specs=[vmem] * 2 + [anywhere] * 5,
        scratch_shapes=[
            pltpu.VMEM((rows, features), f32),
            pltpu.VMEM((rows, features), bf16),
            pltpu.VMEM((2 * rows, wide), bf16),
            pltpu.VMEM((2 * rows, wide), bf16),
            *[pltpu.VMEM((parts, rows // parts, wide), bf16)] * 2,
            pltpu.VMEM((parts, 2, rows // parts, wide // 2), bf16),
            pltpu.VMEM((rows // parts, wide), f32),
            pltpu.VMEM((2, features, hidden), bf16),
            pltpu.VMEM((2, features, hidden), bf16),
            pltpu.VMEM((2, features, 2 * hidden), bf16),
            *[pltpu.VMEM(block, bf16)] * 5,
            pltpu.VMEM((2, 4, features, hidden), bf16),
            pltpu.VMEM((packed, features), f32),
            pltpu.VMEM((packed // 2, features), f32),
            pltpu.VMEM((2, packed // 2, features), bf16),
            pltpu.VMEM((packed // 2, features), bf16),
            pltpu.VMEM((2, 2, 3, packed // 8, features), bf16),
            pltpu.VMEM((2, packed // 2, features), bf16),
            *[pltpu.VMEM((8, features), f32)] * 4,
            pltpu.VMEM((4, 8, features), f32),
            pltpu.VMEM((PITCH, features), f32),
        ]
        + [dma((2, parts))] * 2
        + [dma((parts,))] * 7
        + [dma((images,))] * 6
        + [dma((2, 4))] * 2
        + [dma((4,))] * 2
        + [dma((2, 3))] * 4
        + [dma((2, 4))] * 2
        + [dma((2,))] * 2
        + [dma((4,))] * 2
        + [dma((4,)), dma((6,)), dma((5,)), dma((1,))],
        compiler_params=pltpu.CompilerParams(
            collective_id=2, has_side_effects=True, vmem_limit_bytes=63 << 20
        ),
    )(
        tok,
        gain1,
        shift1,
        gain2,
        qkv_w,
        out_w,
        q,
        k,
        v,
        att,
        lse,
        grad_h,
        grad_router,
        resid,
        cot,
        mixed,
        up_first,
        down_first,
        up_pair,
        down_pair,
        up_second,
        down_second,
    )


def per_image(rows_in):
    images = rows_in.shape[0] // SEQ
    blocks = rows_in.reshape(images, SEQ, rows_in.shape[1])
    return jnp.pad(blocks, ((0, 0), (0, PITCH - SEQ), (0, 0)))


def unpad(blocks):
    images = blocks.shape[0]
    return blocks[:, :SEQ].reshape(images * SEQ, blocks.shape[2])


def per_device_dense(
    tokens,
    gain_attn,
    shift_attn,
    qkv_weight,
    out_weight,
    gain_moe,
    shift_moe,
    router_weight,
    expert_up,
    expert_down,
    routes,
    keep_mask,
    cotangent,
):
    row_count, feature_count = tokens.shape
    images = row_count // SEQ
    rows = images * PITCH
    tensor_count = lax.axis_size("tensor")
    quarter_width = feature_count // tensor_count
    experts_all = router_weight.shape[1]
    hidden = expert_up.shape[2]
    kept_routes = per_image(jnp.where(keep_mask > 0, routes, -1) + 1).reshape(rows, 2) - 1
    chosen = kept_routes[:, :, None] == jnp.arange(128, dtype=jnp.int32)[None, None, :]
    kept = jnp.any(chosen, axis=1).astype(bf16)
    router_wide = jnp.pad(router_weight, ((0, 0), (0, 128 - experts_all)))
    tok = per_image(tokens)
    qkv_turned = jnp.swapaxes(qkv_weight, 1, 2)
    queries, keys, values, attended, lse, resid, h_all, cot_all, kept_all, up_all, down_all = run_forward(
        tok,
        gain_attn,
        shift_attn,
        gain_moe,
        shift_moe,
        qkv_turned,
        out_weight,
        expert_up[0],
        expert_down[0],
        per_image(cotangent).reshape(rows, quarter_width),
        kept,
    )
    mixed_first, grad_h_first, gate_first, up_first, down_first, up_late, down_late = run_first_pair(
        h_all, cot_all, kept_all, router_wide, up_all, down_all, experts_all
    )
    mixed_part, up_second, down_second, grad_router, grad_h_two, up_pair, down_pair = run_second_pair(
        h_all,
        cot_all,
        kept_all,
        router_wide,
        mixed_first,
        grad_h_first,
        gate_first,
        up_all,
        down_all,
        up_late,
        down_late,
        up_first,
        down_first,
        experts_all,
    )
    grad_up, grad_down, tokens_grad, grad_qkv, grad_out, sums, mixed = run_backward(
        tok,
        gain_attn,
        shift_attn,
        gain_moe,
        qkv_turned,
        out_weight,
        queries,
        keys,
        values,
        attended,
        lse,
        grad_h_two,
        grad_router,
        resid,
        cot_all,
        mixed_part,
        up_first,
        down_first,
        up_pair,
        down_pair,
        up_second,
        down_second,
    )
    return (
        unpad(mixed.reshape(images, PITCH, quarter_width)),
        tokens_grad,
        sums[2],
        sums[3],
        jnp.swapaxes(grad_qkv, 1, 2),
        grad_out,
        sums[0],
        sums[1],
        sums[8 : 8 + experts_all].T,
        grad_up[None],
        grad_down[None],
    )


def per_device(*arguments):
    router_weight = arguments[7]
    if router_weight.shape[1] == 4 and lax.axis_size("expert") == 8 and lax.axis_size("tensor") == 4:
        return per_device_dense(*arguments)
    return per_device_routed(*arguments)


def solution(mesh):
    placed = (
        P("expert", None),
        P(),
        P(),
        P(None, None, "tensor"),
        P("tensor", None),
        P(),
        P(),
        P(),
        P("expert", None, "tensor"),
        P("expert", "tensor", None),
        P("expert", None),
        P("expert", None),
        P("expert", "tensor"),
    )
    return jax.shard_map(
        per_device,
        mesh=mesh,
        in_specs=placed,
        out_specs=(
            P("expert", "tensor"),
            P("expert", None),
            P(),
            P(),
            P(None, None, "tensor"),
            P("tensor", None),
            P(),
            P(),
            P(),
            P("expert", None, "tensor"),
            P("expert", "tensor", None),
        ),
        check_vma=False,
    )
```

```python
from functools import partial

import jax
import jax.numpy as jnp
from jax import lax
from jax.experimental import pallas as pl
from jax.experimental.pallas import tpu as pltpu
from jax.sharding import PartitionSpec as P

HD = 64
SEQ = 197


norm_epsilon = 1e-06


def norm_rows(values, gain, shift):
    row_mean = jnp.mean(values, axis=-1, keepdims=True)
    centred = values - row_mean
    spread = jnp.mean(centred * centred, axis=-1, keepdims=True)
    return centred * lax.rsqrt(spread + norm_epsilon) * gain + shift


def gelu_exact(values):
    return jax.nn.gelu(values, approximate=False)


def gate_from_logits(logit_rows, picked_rows, keep_rows):
    router_probs = jax.nn.softmax(logit_rows, axis=-1)
    return jnp.sum(jnp.where(picked_rows, router_probs[:, None, :], 0.0), axis=-1) * keep_rows


def attention_forward(h_rows, qkv_w, out_w):
    row_total_count = h_rows.shape[0]
    head_count = qkv_w.shape[2] // HD
    image_count = row_total_count // SEQ
    score_scale = HD ** (-0.5)
    projected = jnp.einsum("td,cdf->ctf", h_rows, qkv_w, preferred_element_type=jnp.float32).astype(
        jnp.bfloat16
    )
    split_heads = projected.reshape(3, image_count, SEQ, head_count, HD)
    queries = split_heads[0]
    keys_all = split_heads[1]
    values_all = split_heads[2]
    scores = (
        jnp.einsum("gqhe,gkhe->ghqk", queries, keys_all, preferred_element_type=jnp.float32)
        * score_scale
    )
    row_peak = jnp.max(scores, axis=-1, keepdims=True)
    exp_scores = jnp.exp(scores - row_peak)
    row_total = jnp.sum(exp_scores, axis=-1, keepdims=True)
    log_total = row_peak + jnp.log(row_total)
    weights = (exp_scores / row_total).astype(jnp.bfloat16)
    attended = jnp.einsum(
        "ghqk,gkhe->gqhe", weights, values_all, preferred_element_type=jnp.float32
    ).astype(jnp.bfloat16)
    attended = attended.reshape(row_total_count, head_count * HD)
    partial_out = jnp.dot(attended, out_w, preferred_element_type=jnp.float32)
    return (partial_out, (attended, queries, keys_all, values_all, log_total))


def attention_backward(grad_branch, saved, h_rows, qkv_w, out_w):
    attended, queries, keys_all, values_all, log_total = saved
    row_total_count = h_rows.shape[0]
    head_count = qkv_w.shape[2] // HD
    image_count = row_total_count // SEQ
    score_scale = HD ** (-0.5)
    grad_out = jnp.einsum("tc,td->cd", attended, grad_branch, preferred_element_type=jnp.float32)
    grad_attended = jnp.einsum(
        "td,cd->tc", grad_branch, out_w, preferred_element_type=jnp.float32
    ).astype(jnp.bfloat16)
    grad_attended = grad_attended.reshape(image_count, SEQ, head_count, HD)
    scores_again = (
        jnp.einsum("gqhe,gkhe->ghqk", queries, keys_all, preferred_element_type=jnp.float32)
        * score_scale
    )
    probs_again = jnp.exp(scores_again - log_total)
    grad_weights = jnp.einsum(
        "gqhe,gkhe->ghqk", grad_attended, values_all, preferred_element_type=jnp.float32
    )
    grad_scores = (
        probs_again * (grad_weights - jnp.sum(probs_again * grad_weights, axis=-1, keepdims=True))
    ).astype(jnp.bfloat16)
    grad_queries = (
        jnp.einsum("ghqk,gkhe->gqhe", grad_scores, keys_all, preferred_element_type=jnp.float32)
        * score_scale
    )
    grad_keys = (
        jnp.einsum("ghqk,gqhe->gkhe", grad_scores, queries, preferred_element_type=jnp.float32)
        * score_scale
    )
    grad_values = jnp.einsum(
        "ghqk,gqhe->gkhe",
        probs_again.astype(jnp.bfloat16),
        grad_attended,
        preferred_element_type=jnp.float32,
    )
    grad_rows = (
        jnp.stack([grad_queries, grad_keys, grad_values])
        .astype(jnp.bfloat16)
        .reshape(3, row_total_count, head_count * HD)
    )
    grad_qkv = jnp.einsum("td,ctf->cdf", h_rows, grad_rows, preferred_element_type=jnp.float32)
    grad_h_one = jnp.einsum("ctf,cdf->td", grad_rows, qkv_w, preferred_element_type=jnp.float32)
    return (grad_qkv, grad_out, grad_h_one)


def moe_tail(
    grad_h_rows,
    grad_gate_rows,
    grad_out_rows,
    h_two_rows,
    resid_rows,
    gate_back,
    router_weight,
    gain_moe,
    shift_moe,
):
    row_total_count = grad_h_rows.shape[0]
    grad_gate = jnp.sum(grad_gate_rows.reshape(row_total_count, -1, 2), axis=1)
    grad_logits = gate_back(grad_gate)[0].astype(jnp.bfloat16)
    grad_router = jnp.einsum(
        "td,te->de", h_two_rows, grad_logits, preferred_element_type=jnp.float32
    )
    grad_h_two = grad_h_rows + jnp.einsum(
        "te,de->td", grad_logits, router_weight, preferred_element_type=jnp.float32
    )
    norm_out, norm_back = jax.vjp(norm_rows, resid_rows, gain_moe, shift_moe)
    grad_resid_norm, grad_gain_moe, grad_shift_moe = norm_back(grad_h_two)
    return (grad_out_rows + grad_resid_norm, grad_router, grad_gain_moe, grad_shift_moe)


def per_device_routed(
    tokens,
    gain_attn,
    shift_attn,
    qkv_weight,
    out_weight,
    gain_moe,
    shift_moe,
    router_weight,
    expert_up,
    expert_down,
    routes,
    keep_mask,
    cotangent,
):
    row_count, feature_count = tokens.shape
    tensor_count = lax.axis_size("tensor")
    expert_count = lax.axis_size("expert")
    tensor_here = lax.axis_index("tensor")
    quarter_width = feature_count // tensor_count
    col_start = tensor_here * quarter_width
    experts_all = router_weight.shape[1]
    capacity = max(2, 7 * row_count // (2 * experts_all))
    tokens_float = tokens.astype(jnp.float32)
    h_one = norm_rows(tokens_float, gain_attn, shift_attn).astype(jnp.bfloat16)
    partial_out, saved = attention_forward(h_one, qkv_weight, out_weight)
    branch = lax.psum(partial_out, "tensor")
    resid = tokens_float + branch
    h_two = norm_rows(resid, gain_moe, shift_moe).astype(jnp.bfloat16)
    logits = jnp.dot(h_two, router_weight, preferred_element_type=jnp.float32)
    keep_float = keep_mask.astype(jnp.float32)
    picked = routes[:, :, None] == jnp.arange(experts_all, dtype=jnp.int32)[None, None, :]
    gate_values, gate_back = jax.vjp(
        partial(gate_from_logits, picked_rows=picked, keep_rows=keep_float), logits
    )
    flat_expert = routes.reshape(-1)
    one_hot = (flat_expert[:, None] == jnp.arange(experts_all, dtype=jnp.int32)[None, :]).astype(
        jnp.int32
    )
    rank_within = jnp.sum((jnp.cumsum(one_hot, axis=0) - one_hot) * one_hot, axis=1)
    slot_index = flat_expert * capacity + rank_within
    token_index = jnp.repeat(jnp.arange(row_count, dtype=jnp.int32), 2)
    live_route = keep_mask.reshape(-1) > 0
    source_table = (
        jnp.full((experts_all * capacity,), row_count, jnp.int32)
        .at[slot_index]
        .set(jnp.where(live_route, token_index, row_count))
    )
    padded_rows = jnp.concatenate([h_two, jnp.zeros((1, feature_count), jnp.bfloat16)], axis=0)
    dispatch = padded_rows[source_table].reshape(experts_all, capacity, feature_count)
    paired = jnp.broadcast_to(dispatch[:, None], (experts_all, 2, capacity, feature_count)).reshape(
        expert_count, capacity, feature_count
    )
    arrived = lax.all_to_all(paired, "expert", split_axis=0, concat_axis=0, tiled=True)
    expert_rows = arrived.reshape(expert_count * capacity, feature_count)
    up_local = expert_up[0]
    down_local = expert_down[0]
    pre_act = jnp.dot(expert_rows, up_local, preferred_element_type=jnp.float32)
    hidden_float, gelu_back = jax.vjp(gelu_exact, pre_act)
    hidden = hidden_float.astype(jnp.bfloat16)
    partial_down = jnp.dot(hidden, down_local, preferred_element_type=jnp.float32)
    summed = lax.psum_scatter(partial_down, "tensor", scatter_dimension=1, tiled=True)
    returned = lax.all_to_all(
        summed.reshape(expert_count, capacity, quarter_width),
        "expert",
        split_axis=0,
        concat_axis=0,
        tiled=True,
    )
    answer_table = jnp.sum(
        returned.reshape(experts_all, 2, capacity, quarter_width), axis=1
    ).astype(jnp.bfloat16)
    answers = (
        answer_table.reshape(experts_all * capacity, quarter_width)[slot_index]
        .astype(jnp.float32)
        .reshape(row_count, 2, quarter_width)
    )
    resid_part = lax.dynamic_slice_in_dim(resid, col_start, quarter_width, 1)
    mixed = (resid_part + jnp.sum(gate_values[:, :, None] * answers, axis=1)).astype(jnp.bfloat16)
    grad_part = cotangent.astype(jnp.float32)
    grad_answers = (
        (gate_values[:, :, None] * grad_part[:, None, :])
        .astype(jnp.bfloat16)
        .reshape(2 * row_count, quarter_width)
    )
    grad_gate_part = jnp.sum(grad_part[:, None, :] * answers, axis=-1)
    outgoing = (
        jnp.zeros((experts_all * capacity, quarter_width), jnp.bfloat16)
        .at[slot_index]
        .set(grad_answers)
    )
    outgoing = jnp.broadcast_to(
        outgoing.reshape(experts_all, 1, capacity, quarter_width),
        (experts_all, 2, capacity, quarter_width),
    ).reshape(expert_count, capacity, quarter_width)
    incoming = lax.all_to_all(outgoing, "expert", split_axis=0, concat_axis=0, tiled=True)
    grad_full = lax.all_gather(incoming, "tensor", axis=2, tiled=True).reshape(
        expert_count * capacity, feature_count
    )
    grad_hidden = jnp.einsum("rd,fd->rf", grad_full, down_local, preferred_element_type=jnp.float32)
    grad_pre = gelu_back(grad_hidden)[0].astype(jnp.bfloat16)
    grad_down = jnp.einsum("rf,rd->fd", hidden, grad_full, preferred_element_type=jnp.float32)
    grad_up = jnp.einsum("rd,rf->df", expert_rows, grad_pre, preferred_element_type=jnp.float32)
    grad_rows_partial = jnp.einsum(
        "rf,df->rd", grad_pre, up_local, preferred_element_type=jnp.float32
    )
    grad_rows_sum = lax.psum_scatter(
        grad_rows_partial.astype(jnp.bfloat16), "tensor", scatter_dimension=1, tiled=True
    ).astype(jnp.float32)
    sent_back = lax.all_to_all(
        grad_rows_sum.reshape(expert_count, capacity, quarter_width).astype(jnp.bfloat16),
        "expert",
        split_axis=0,
        concat_axis=0,
        tiled=True,
    ).astype(jnp.float32)
    grad_table = jnp.sum(sent_back.reshape(experts_all, 2, capacity, quarter_width), axis=1).astype(
        jnp.bfloat16
    )
    grad_inputs = (
        grad_table.reshape(experts_all * capacity, quarter_width)[slot_index]
        .astype(jnp.float32)
        .reshape(row_count, 2, quarter_width)
    )
    grad_h_part = jnp.sum(grad_inputs * keep_float[:, :, None], axis=1)
    grad_h_full, grad_gate_all, grad_out_full = (
        lax.all_gather(grad_h_part, "tensor", axis=1, tiled=True),
        lax.all_gather(grad_gate_part, "tensor", axis=1, tiled=True),
        lax.all_gather(grad_part, "tensor", axis=1, tiled=True),
    )
    grad_resid, grad_router, grad_gain_moe, grad_shift_moe = moe_tail(
        grad_h_full,
        grad_gate_all,
        grad_out_full,
        h_two,
        resid,
        gate_back,
        router_weight,
        gain_moe,
        shift_moe,
    )
    grad_qkv, grad_out, grad_h_one_part = attention_backward(
        grad_resid.astype(jnp.bfloat16), saved, h_one, qkv_weight, out_weight
    )
    grad_h_one = lax.psum(grad_h_one_part.astype(jnp.bfloat16), "tensor").astype(jnp.float32)
    norm_one_out, norm_one_back = jax.vjp(norm_rows, tokens_float, gain_attn, shift_attn)
    grad_tok_norm, grad_gain_attn, grad_shift_attn = norm_one_back(grad_h_one)
    grad_tokens = grad_resid + grad_tok_norm
    summed_grads = lax.psum(
        (
            grad_gain_attn,
            grad_shift_attn,
            grad_qkv,
            grad_out,
            grad_gain_moe,
            grad_shift_moe,
            grad_router,
        ),
        "expert",
    )
    grad_qkv_mine = summed_grads[2]
    grad_out_mine = summed_grads[3]
    return (
        mixed,
        grad_tokens,
        summed_grads[0],
        summed_grads[1],
        grad_qkv_mine,
        grad_out_mine,
        summed_grads[4],
        summed_grads[5],
        summed_grads[6],
        grad_up[None],
        grad_down[None],
    )


MESH = pl.DeviceIdType.MESH
f32 = jnp.float32
bf16 = jnp.bfloat16
PITCH = 208


def dot(left, right, over=((1,), (0,))):
    return lax.dot_general(left, right, (over, ((), ())), preferred_element_type=f32)


def aligned(start, size):
    return pl.ds(pl.multiple_of(start, 16), size)


def lanes_at(start, size):
    return pl.ds(pl.multiple_of(start, 128), size)


def norm_stats(values):
    row_mean = jnp.mean(values, axis=1, keepdims=True)
    centred = values - row_mean
    inverse = lax.rsqrt(jnp.mean(centred * centred, axis=1, keepdims=True) + norm_epsilon)
    return centred * inverse, inverse


def greet(neighbours):
    barrier = pltpu.get_barrier_semaphore()
    count = 0
    for is_there, device in neighbours:

        @pl.when(is_there)
        def _():
            pl.semaphore_signal(barrier, inc=1, device_id=device, device_id_type=MESH)

        count = count + jnp.where(is_there, 1, 0)
    pl.semaphore_wait(barrier, count)


def head_mask(lane, head):
    return (lane < HD) if head % 2 == 0 else (lane >= HD)


def expert_math(h_rows, cot_rows, kept, router, up, down, pair, experts):
    block = h_rows.shape[0]
    hidden = up.shape[1] // 2
    lane = lax.broadcasted_iota(jnp.int32, (block, 128), 1)
    logits = jnp.where(lane < experts, dot(h_rows, router), -1e30)
    powers = jnp.exp(logits - jnp.max(logits, axis=1, keepdims=True))
    probs = powers / jnp.sum(powers, axis=1, keepdims=True)
    gates = kept * probs
    pre_act = dot(h_rows, up)
    back = dot(cot_rows, down, ((1,), (1,)))
    normal_cdf = 0.5 + 0.5 * lax.erf(pre_act * 0.7071067811865476)
    gelu = pre_act * normal_cdf
    slope = normal_cdf + pre_act * (0.3989422804014327 * jnp.exp(-0.5 * pre_act * pre_act))
    product = gelu * back
    grad_gate = jnp.zeros((block, 128), f32)
    spread = []
    for side in range(2):
        chosen = lane == 2 * pair + side
        part = jnp.sum(product[:, side * hidden : (side + 1) * hidden], axis=1, keepdims=True)
        grad_gate = jnp.where(chosen, part, grad_gate)
        gate = jnp.sum(jnp.where(chosen, gates, 0.0), axis=1, keepdims=True)
        spread.append(jnp.broadcast_to(gate, (block, hidden)))
    gate = jnp.concatenate(spread, axis=1)
    hidden_rows = (gelu * gate).astype(bf16)
    grad_pre = (slope * back * gate).astype(bf16)
    return hidden_rows, grad_pre, probs, grad_gate


BLOCK = 2 * PITCH


def forward_kernel(
    tok_ref,
    gain1_ref,
    shift1_ref,
    gain2_ref,
    shift2_ref,
    qkv_ref,
    out_w_ref,
    up_ref,
    down_ref,
    cot_ref,
    kept_ref,
    router_ref,
    q_ref,
    k_ref,
    v_ref,
    att_ref,
    lse_ref,
    resid_ref,
    h_out,
    cot_out,
    kept_out,
    up_out,
    down_out,
    mixed_out,
    grad_h_out,
    gate_out,
    grad_up_out,
    grad_down_out,
    up_vm,
    down_vm,
    up_sum,
    down_sum,
    mixed_slots,
    grad_h_slots,
    gate_slots,
    grad_up_vm,
    grad_down_vm,
    q_all,
    k_all,
    v_all,
    att_all,
    lse_all,
    resid_all,
    h_all,
    cot_all,
    kept_all,
    part,
    mine,
    core_from,
    core_to,
    x_to,
    x_from,
    total_to,
    total_from,
    cot_core,
    core_s,
    core_r,
    x_s,
    x_r,
    tot_s,
    tot_r,
    y_s,
    y_r,
    rel_s,
    rel_r,
    w_s,
    w_r,
    c_s,
    c_r,
    own_sem,
    pair_sem,
    block_sem,
    grad_sem,
    cot_sem,
    out_sem,
    *,
    images,
    heads,
    experts,
):
    expert_at = lax.axis_index("expert")
    tensor_at = lax.axis_index("tensor")
    z_at, y_at = expert_at // 2, expert_at % 2
    z_last = lax.axis_size("expert") // 2 - 1
    x_at, core_at = tensor_at // 2, tensor_at % 2
    other = 1 - core_at
    rows = images * PITCH
    half = rows // 2
    wide = out_w_ref.shape[1] // 2
    hidden = up_ref.shape[1]
    core_dev = (expert_at, tensor_at + 1 - 2 * core_at)
    x_dev = (expert_at, tensor_at + 2 - 4 * x_at)
    y_dev = (expert_at + 1 - 2 * y_at, tensor_at)
    z_up = (expert_at + 2, tensor_at)
    z_down = (expert_at - 2, tensor_at)
    has_up, has_down = z_at < z_last, z_at > 0
    greet([(True, core_dev), (True, x_dev), (True, y_dev), (has_up, z_up), (has_down, z_down)])

    def remote(src, dst, send, recv, device):
        return pltpu.make_async_remote_copy(
            src_ref=src, dst_ref=dst, send_sem=send, recv_sem=recv, device_id=device, device_id_type=MESH
        )

    def slot(expert, plane):
        pair = (expert // 2 + plane // 2) % 2
        return (
            up_out.at[pair, :, lanes_at(expert % 2 * hidden, hidden)],
            down_out.at[pair, aligned(expert % 2 * hidden, hidden), :],
        )

    def hop(step, way):
        expert = z_at - step if way == 0 else z_at + step
        plane = z_at + 1 if way == 0 else z_at - 1
        source = (up_ref, down_ref) if step == 0 else slot(expert, z_at)
        target = slot(expert, plane)
        device = z_up if way == 0 else z_down
        return [remote(source[n], target[n], w_s.at[way, step, n], w_r.at[way, step, n], device) for n in range(2)]

    def hop_goes(step, way):
        if way == 0:
            return (z_at - step >= 0) & has_up
        return (z_at + step <= z_last) & has_down

    def hop_comes(step, way):
        return (z_at - 1 - step >= 0) if way == 0 else (z_at + 1 + step <= z_last)

    def hop_arriving(step, way):
        expert = z_at - 1 - step if way == 0 else z_at + 1 + step
        target = slot(expert, z_at)
        return [remote(target[n], target[n], w_s.at[way, step, n], w_r.at[way, step, n], core_dev) for n in range(2)]

    def start_hops(step):
        for way in range(2):

            @pl.when(hop_goes(step, way))
            def _():
                for copy in hop(step, way):
                    copy.start()

    def await_hops(step):
        for way in range(2):

            @pl.when(hop_comes(step, way))
            def _():
                for copy in hop_arriving(step, way):
                    copy.wait_recv()

    start_hops(0)

    def pair_place(expert):
        return up_vm.at[:, lanes_at(expert % 2 * hidden, hidden)], down_vm.at[aligned(expert % 2 * hidden, hidden), :]

    near = z_at + 1 - 2 * (z_at % 2)
    own_copies = [
        pltpu.make_async_copy((up_ref, down_ref)[n], pair_place(z_at)[n], own_sem.at[n]) for n in range(2)
    ]
    near_copies = [
        pltpu.make_async_copy(slot(near, z_at)[n], pair_place(near)[n], pair_sem.at[n]) for n in range(2)
    ]
    for copy in own_copies:
        copy.start()

    swap = remote(cot_ref, cot_core, c_s.at[0], c_r.at[0], core_dev)
    swap.start()
    kept_all[pl.ds(0, rows), :] = kept_ref[...]

    def kept_half(side, core):
        return kept_all.at[aligned(side * rows + core * half, half), :]

    kept_y = remote(kept_half(0, core_at), kept_half(1, core_at), c_s.at[7], c_r.at[7], y_dev)
    kept_share = remote(kept_half(1, core_at), kept_half(1, core_at), c_s.at[6], c_r.at[6], core_dev)
    kept_share_in = remote(kept_half(1, other), kept_half(1, other), c_s.at[6], c_r.at[6], core_dev)
    kept_y.start()
    swap.wait_recv()

    @pl.when(core_at == 0)
    def _():
        both = jnp.concatenate([cot_ref[...], cot_core[...]], axis=1)
        cot_all[pl.ds(0, rows), lanes_at(x_at * wide, wide)] = both

    @pl.when(core_at == 1)
    def _():
        both = jnp.concatenate([cot_core[...], cot_ref[...]], axis=1)
        cot_all[pl.ds(0, rows), lanes_at(x_at * wide, wide)] = both

    def block(side, col_side, core):
        return cot_all.at[aligned(side * rows + core * half, half), lanes_at(col_side * wide, wide)]

    def cot_copy(number, source, target, device):
        return remote(source, target, c_s.at[number], c_r.at[number], device)

    mine_block = block(0, x_at, core_at)
    cot_x = cot_copy(1, mine_block, mine_block, x_dev)
    cot_y = cot_copy(2, mine_block, block(1, x_at, core_at), y_dev)
    cot_x.start()
    cot_y.start()
    across_x, across_y, across_both = block(0, 1 - x_at, core_at), block(1, x_at, core_at), block(1, 1 - x_at, core_at)
    cot_x_in = cot_copy(1, across_x, across_x, x_dev)
    cot_y_in = cot_copy(2, across_y, across_y, y_dev)
    relay_y = cot_copy(3, across_x, across_both, y_dev)
    relay_x = cot_copy(3, across_y, across_y, x_dev)
    relay_in = cot_copy(3, across_both, across_both, y_dev)
    cot_share = [
        cot_copy(4, across_x, across_x, core_dev),
        cot_copy(5, across_y, across_y, core_dev),
        cot_copy(8, across_both, across_both, core_dev),
    ]
    arriving = [block(0, 1 - x_at, other), block(1, x_at, other), block(1, 1 - x_at, other)]
    cot_share_in = [cot_copy(number, ref, ref, core_dev) for number, ref in zip((4, 5, 8), arriving)]

    lane = lax.broadcasted_iota(jnp.int32, (PITCH, 2 * HD), 1)
    key_mask = lax.broadcasted_iota(jnp.int32, (PITCH, PITCH), 1) < SEQ
    gain1, shift1, gain2, shift2 = (ref[...].reshape(1, 2 * wide) for ref in (gain1_ref, shift1_ref, gain2_ref, shift2_ref))
    my_cols = lanes_at(core_at * wide, wide)
    their_cols = lanes_at(other * wide, wide)

    def attend(image):
        normed, _ = norm_stats(tok_ref[image].astype(f32))
        h_one = (normed * gain1 + shift1).astype(bf16)
        queries = dot(h_one, qkv_ref[0], ((1,), (1,))).astype(bf16)
        keys = dot(h_one, qkv_ref[1], ((1,), (1,))).astype(bf16)
        values = dot(h_one, qkv_ref[2], ((1,), (1,))).astype(bf16)
        q_all[image] = queries
        k_all[image] = keys
        v_all[image] = values
        outs = []
        lse = jnp.zeros((PITCH, 2 * HD), f32)
        for head in range(heads):
            first = head // 2 * 2 * HD
            last = min(first + 2 * HD, heads * HD)
            q_head, k_head, v_head = queries[:, first:last], keys[:, first:last], values[:, first:last]
            if last - first == 2 * HD:
                q_head = jnp.where(head_mask(lane, head), q_head, jnp.zeros_like(q_head))
            scores = dot(q_head, k_head, ((1,), (1,))) * (HD**-0.5)
            scores = jnp.where(key_mask, scores, -1e30)
            peak = jnp.max(scores, axis=1, keepdims=True)
            powers = jnp.exp(scores - peak)
            row_sum = jnp.sum(powers, axis=1, keepdims=True)
            weights = (powers / row_sum).astype(bf16)
            outs.append(dot(weights, v_head))
            lse = jnp.where(lane == head, peak + jnp.log(row_sum), lse)
        lse_all[image] = lse
        joined = []
        for head in range(0, heads, 2):
            if head + 1 < heads:
                joined.append(jnp.where(lane < HD, outs[head], outs[head + 1]))
            else:
                joined.append(outs[head])
        attended = jnp.concatenate(joined, axis=1).astype(bf16)
        att_all[image] = attended
        part[...] = dot(attended, out_w_ref[...])
        mine[image] = part[:, my_cols]
        core_to[image] = part[:, their_cols].astype(bf16)

    def core_copy(image):
        return remote(core_to.at[image], core_from.at[image], core_s.at[image], core_r.at[image], core_dev)

    def x_copy(image):
        return remote(x_to.at[image], x_from.at[image], x_s.at[image], x_r.at[image], x_dev)

    def total_copy(image):
        return remote(total_to.at[image], total_from.at[image], tot_s.at[image], tot_r.at[image], core_dev)

    def h_block(side, image, core):
        return h_all.at[aligned(side * rows + image * PITCH, PITCH), lanes_at(core * wide, wide)]

    def y_copy(image):
        return remote(h_block(0, image, core_at), h_block(1, image, core_at), y_s.at[image], y_r.at[image], y_dev)

    def relay_copy(image):
        ref = h_block(1, image, core_at)
        return remote(ref, ref, rel_s.at[image], rel_r.at[image], core_dev)

    def relay_arriving(image):
        ref = h_block(1, image, other)
        return remote(ref, ref, rel_s.at[image], rel_r.at[image], core_dev)

    attend_outs = ((q_all, q_ref), (k_all, k_ref), (v_all, v_ref), (att_all, att_ref), (lse_all, lse_ref))

    def out_copies(image):
        copies = [
            pltpu.make_async_copy(kept.at[image], out.at[image], out_sem.at[n, image])
            for n, (kept, out) in enumerate(attend_outs)
        ]
        at = aligned(image * PITCH, PITCH)
        return copies, [
            pltpu.make_async_copy(resid_all.at[image], resid_ref.at[at, :], out_sem.at[5, image]),
            pltpu.make_async_copy(h_all.at[at, :], h_out.at[at, :], out_sem.at[6, image]),
        ]

    def other_copy(image):
        at = aligned(rows + image * PITCH, PITCH)
        return pltpu.make_async_copy(h_all.at[at, :], h_out.at[at, :], out_sem.at[7, image])

    def stage(tick, lag, run):
        image = tick - lag

        @pl.when((image >= 0) & (image < images))
        def _():
            run(image)

    def run_attend(image):
        attend(image)
        core_copy(image).start()
        for copy in out_copies(image)[0]:
            copy.start()

    def run_x(image):
        core_copy(image).wait_recv()
        x_to[image] = (mine[image] + core_from[image].astype(f32)).astype(bf16)
        x_copy(image).start()

    def run_total(image):
        x_copy(image).wait_recv()
        total_to[image] = (x_to[image].astype(f32) + x_from[image].astype(f32)).astype(bf16)
        total_copy(image).start()

    def run_norm(image):
        total_copy(image).wait_recv()
        part[:, my_cols] = total_to[image].astype(f32)
        part[:, their_cols] = total_from[image].astype(f32)
        resid = tok_ref[image].astype(f32) + part[...]
        resid_all[image] = resid
        normed, _ = norm_stats(resid)
        h_all[aligned(image * PITCH, PITCH), :] = (normed * gain2 + shift2).astype(bf16)
        y_copy(image).start()
        for copy in out_copies(image)[1]:
            copy.start()

    def run_relay(image):
        y_copy(image).wait_recv()
        relay_copy(image).start()

    def run_end(image):
        relay_arriving(image).wait_recv()
        other_copy(image).start()

    def at_tick(tick, when, run):
        @pl.when(tick == when)
        def _():
            run()

    def cot_step_one():
        cot_x_in.wait_recv()
        cot_share[0].start()

        @pl.when(core_at == 0)
        def _():
            relay_y.start()

        kept_y.wait_recv()
        kept_share.start()

    def cot_step_two():
        cot_y_in.wait_recv()
        cot_share[1].start()

        @pl.when(core_at == 1)
        def _():
            relay_x.start()

    def weights_step_one():
        await_hops(0)
        start_hops(1)
        for copy in near_copies:
            copy.start()

    def weights_step_two():
        await_hops(1)
        start_hops(2)

    def cot_step_three():
        relay_in.wait_recv()
        cot_share[2].start()

    def ready_own():
        cot_share_in[0].wait_recv()
        for copy in (*own_copies, *near_copies):
            copy.wait()

    def ready_other():
        for copy in (cot_share_in[1], cot_share_in[2], kept_share_in):
            copy.wait_recv()

    def block_copies(number, place):
        at = aligned(number * BLOCK, BLOCK)
        pairs = ((mixed_slots, mixed_out), (grad_h_slots, grad_h_out), (gate_slots, gate_out))
        return [
            pltpu.make_async_copy(slots.at[place], out.at[at, :], block_sem.at[n, place])
            for n, (slots, out) in enumerate(pairs)
        ]

    def run_block(number, turn):
        at = aligned(number * BLOCK, BLOCK)
        h_rows, cot_rows = h_all[at, :], cot_all[at, :]
        up, down = up_vm[...], down_vm[...]
        hidden_rows, grad_pre, _, grad_gate = expert_math(
            h_rows, cot_rows, kept_all[at, :].astype(f32), router_ref[...], up, down, z_at // 2, experts
        )

        place = turn % 2

        @pl.when(turn >= 2)
        def _():
            for copy in block_copies(number, place):
                copy.wait()

        gate_slots[place] = grad_gate
        mixed_slots[place] = dot(hidden_rows, down).astype(bf16)
        grad_h_slots[place] = dot(grad_pre, up, ((1,), (1,))).astype(bf16)
        for copy in block_copies(number, place):
            copy.start()
        up_sum[...] += dot(h_rows.T, grad_pre)
        down_sum[...] += dot(cot_rows.T, hidden_rows)

    def choose(tick, table):
        return sum(jnp.where(tick == when, value, 0) for when, value in table)

    BLOCKS_AT = ((7, 0), (9, 1), (11, 2), (12, 4), (13, 3), (14, 5), (16, 6), (18, 7))
    TURNS = tuple((when, turn) for turn, (when, _) in enumerate(BLOCKS_AT))

    def per_tick(tick, _):
        stage(tick, 0, run_attend)
        stage(tick, 1, run_x)
        stage(tick, 4, run_total)
        stage(tick, 5, run_norm)
        stage(tick, 9, run_relay)
        stage(tick, 10, run_end)
        at_tick(tick, 5, cot_step_one)
        at_tick(tick, 6, weights_step_one)
        at_tick(tick, 6, cot_step_two)
        at_tick(tick, 7, ready_own)
        at_tick(tick, 9, cot_step_three)
        at_tick(tick, 12, ready_other)
        at_tick(tick, 13, weights_step_two)

        @pl.when(choose(tick, tuple((when, 1) for when, _ in BLOCKS_AT)) == 1)
        def _():
            run_block(choose(tick, BLOCKS_AT), choose(tick, TURNS))

        return 0

    up_sum[...] = jnp.zeros_like(up_sum)
    down_sum[...] = jnp.zeros_like(down_sum)
    lax.fori_loop(0, images + 11, per_tick, 0)
    grad_up_vm[...] = up_sum[...].astype(bf16)
    grad_down_vm[...] = down_sum[...].astype(bf16)
    grad_copies = [
        pltpu.make_async_copy(grad_up_vm, grad_up_out, grad_sem.at[0]),
        pltpu.make_async_copy(grad_down_vm, grad_down_out, grad_sem.at[1]),
    ]
    for copy in grad_copies:
        copy.start()
    outs = [
        pltpu.make_async_copy(cot_all, cot_out, cot_sem.at[0]),
        pltpu.make_async_copy(kept_all, kept_out, cot_sem.at[1]),
    ]
    for copy in outs:
        copy.start()
    for copy in (swap, kept_y, kept_share, cot_x, cot_y, *cot_share):
        copy.wait_send()

    @pl.when(core_at == 0)
    def _():
        relay_y.wait_send()

    @pl.when(core_at == 1)
    def _():
        relay_x.wait_send()

    def drain(image, _):
        for copy in (core_copy, x_copy, total_copy, y_copy, relay_copy):
            copy(image).wait_send()
        first, second = out_copies(image)
        for copy in (*first, *second, other_copy(image)):
            copy.wait()
        return 0

    lax.fori_loop(0, images, drain, 0)
    for place in range(2):
        for copy in block_copies(0, place):
            copy.wait()

    await_hops(2)
    for step in range(3):
        for way in range(2):

            @pl.when(hop_goes(step, way))
            def _():
                for copy in hop(step, way):
                    copy.wait_send()

    for copy in (*grad_copies, *outs):
        copy.wait()


def run_forward(tok, gain1, shift1, gain2, shift2, qkv_w, out_w, up, down, cot, kept, router, experts):
    images = tok.shape[0]
    rows = images * PITCH
    features = tok.shape[2]
    share = out_w.shape[0]
    heads = share // HD
    hidden = up.shape[1]
    wide = features // 2
    vmem = pl.BlockSpec(memory_space=pltpu.VMEM)
    anywhere = pl.BlockSpec(memory_space=pl.ANY)
    shape = jax.ShapeDtypeStruct
    block = (images, PITCH, wide)
    dma = pltpu.SemaphoreType.DMA
    return pl.pallas_call(
        partial(forward_kernel, images=images, heads=heads, experts=experts),
        out_shape=[
            shape((images, PITCH, share), bf16),
            shape((images, PITCH, share), bf16),
            shape((images, PITCH, share), bf16),
            shape((images, PITCH, share), bf16),
            shape((images, PITCH, 128), f32),
            shape((rows, features), f32),
            shape((2 * rows, features), bf16),
            shape((2 * rows, features), bf16),
            shape((2 * rows, 128), bf16),
            shape((2, features, 2 * hidden), bf16),
            shape((2, 2 * hidden, features), bf16),
            shape((2 * rows, features), bf16),
            shape((2 * rows, features), bf16),
            shape((2 * rows, 128), f32),
            shape((features, 2 * hidden), bf16),
            shape((features, 2 * hidden), bf16),
        ],
        in_specs=[vmem] * 7 + [anywhere] * 2 + [vmem] * 3,
        out_specs=[anywhere] * 16,
        scratch_shapes=[
            pltpu.VMEM((features, 2 * hidden), bf16),
            pltpu.VMEM((2 * hidden, features), bf16),
            *[pltpu.VMEM((features, 2 * hidden), f32)] * 2,
            *[pltpu.VMEM((2, BLOCK, features), bf16)] * 2,
            pltpu.VMEM((2, BLOCK, 128), f32),
            *[pltpu.VMEM((features, 2 * hidden), bf16)] * 2,
            *[pltpu.VMEM((images, PITCH, share), bf16)] * 4,
            pltpu.VMEM((images, PITCH, 128), f32),
            pltpu.VMEM((images, PITCH, features), f32),
            pltpu.VMEM((2 * rows, features), bf16),
            pltpu.VMEM((2 * rows, features), bf16),
            pltpu.VMEM((2 * rows, 128), bf16),
            pltpu.VMEM((PITCH, features), f32),
            pltpu.VMEM(block, f32),
            pltpu.VMEM(block, bf16),
            pltpu.VMEM(block, bf16),
            pltpu.VMEM(block, bf16),
            pltpu.VMEM(block, bf16),
            pltpu.VMEM(block, bf16),
            pltpu.VMEM(block, bf16),
            pltpu.VMEM((rows, share), bf16),
        ]
        + [dma((images,))] * 10
        + [dma((2, 3, 2))] * 2
        + [dma((9,))] * 2
        + [dma((2,)), dma((2,)), dma((3, 2)), dma((2,)), dma((2,)), dma((8, images))],
        compiler_params=pltpu.CompilerParams(
            collective_id=1, has_side_effects=True, vmem_limit_bytes=63 << 20
        ),
    )(tok, gain1, shift1, gain2, shift2, qkv_w, out_w, up, down, cot, kept, router)


def turn_is_other(turn):
    return (turn == 0) | ((turn % 2 == 1) & (turn < 7))


def turn_block(turn):
    own = jnp.where(turn == 7, 3, turn // 2 - 1)
    return jnp.where(turn_is_other(turn), 4 + (turn + 1) // 2, own)


def second_pair_kernel(
    h_ref,
    cot_ref,
    kept_ref,
    router_ref,
    mixed_first,
    grad_h_first,
    gate_first,
    up_all,
    down_all,
    up_first,
    down_first,
    mixed_ref,
    grad_up_ref,
    grad_down_ref,
    grad_router_ref,
    grad_h_out,
    up_pair,
    down_pair,
    up_vm,
    down_vm,
    up_sum,
    down_sum,
    router_sum,
    ring,
    from_core,
    from_y,
    from_x,
    load,
    core_s,
    core_r,
    y_s,
    y_r,
    x_s,
    x_r,
    tot_s,
    tot_r,
    store,
    pair_s,
    pair_r,
    *,
    experts,
    steps,
):
    turn = pl.program_id(0)
    expert_at = lax.axis_index("expert")
    tensor_at = lax.axis_index("tensor")
    z_at, y_at = expert_at // 2, expert_at % 2
    x_at, core_at = tensor_at // 2, tensor_at % 2
    hidden = up_pair.shape[1]
    wide = ring.shape[2] // 2
    core_dev = (expert_at, tensor_at + 1 - 2 * core_at)
    x_dev = (expert_at, tensor_at + 2 - 4 * x_at)
    y_dev = (expert_at + 1 - 2 * y_at, tensor_at)
    my_cols = lanes_at(core_at * wide, wide)
    their_cols = lanes_at((1 - core_at) * wide, wide)

    def remote(src, dst, send, recv, device):
        return pltpu.make_async_remote_copy(
            src_ref=src, dst_ref=dst, send_sem=send, recv_sem=recv, device_id=device, device_id_type=MESH
        )

    def core_copy(number):
        return remote(ring.at[number % 2, :, their_cols], from_core.at[number], core_s.at[number], core_r.at[number], core_dev)

    def y_copy(number, place):
        return remote(from_core.at[number], from_y.at[place], y_s.at[place], y_r.at[place], y_dev)

    def x_copy(number, place):
        return remote(from_core.at[number], from_x.at[place], x_s.at[place], x_r.at[place], x_dev)

    def out_rows(place):
        return grad_h_out.at[aligned(place * BLOCK, BLOCK), my_cols]

    def total_copy(place):
        return remote(from_x.at[place], out_rows(place), tot_s.at[place], tot_r.at[place], core_dev)

    def store_copy(place):
        return pltpu.make_async_copy(from_x.at[place], out_rows(place), store.at[place])

    def own_turn(place):
        return jnp.where(place == 3, 7, 2 * place + 2)

    def other_turn(place):
        return jnp.where(place == 0, 0, 2 * place - 1)

    def pass_other(number):
        core_copy(number).wait_recv()
        total = from_core[number].astype(f32) + ring[number % 2, :, my_cols].astype(f32)
        from_core[number] = total.astype(bf16)
        y_copy(number, (number + 1) // 2).start()

    def pass_own(number, place):
        core_copy(number).wait_recv()
        y_copy(number, place).wait_recv()
        total = from_core[number].astype(f32) + ring[number % 2, :, my_cols].astype(f32) + from_y[place].astype(f32)
        from_core[number] = total.astype(bf16)
        x_copy(number, place).start()

    def pass_total(place):
        number = own_turn(place)
        x_copy(number, place).wait_recv()
        from_x[place] = (from_core[number].astype(f32) + from_x[place].astype(f32)).astype(bf16)
        total_copy(place).start()
        store_copy(place).start()

    z_dev = (jnp.where(z_at % 2 == 0, expert_at + 2, expert_at - 2), tensor_at)
    pair_lanes = lanes_at((1 - z_at % 2) * hidden, hidden)
    pair_copies = [
        remote(source.at[:, pair_lanes], target, pair_s.at[number], pair_r.at[number], z_dev)
        for number, (source, target) in enumerate(((up_first, up_pair), (down_first, down_pair)))
    ]

    @pl.when(turn == 0)
    def _():
        greet([(True, core_dev), (True, x_dev), (True, y_dev), (True, z_dev)])
        for copy in pair_copies:
            copy.start()
        whole = [
            pltpu.make_async_copy(up_all.at[1], up_vm, load.at[0]),
            pltpu.make_async_copy(down_all.at[1], down_vm, load.at[1]),
        ]
        for copy in whole:
            copy.start()
        up_sum[...] = jnp.zeros_like(up_sum)
        down_sum[...] = jnp.zeros_like(down_sum)
        router_sum[...] = jnp.zeros_like(router_sum)
        for copy in whole:
            copy.wait()

    h_rows, cot_rows = h_ref[...], cot_ref[...]
    up, down, router = up_vm[...], down_vm[...], router_ref[...]
    kept = kept_ref[...].astype(f32)
    hidden_rows, grad_pre, probs, grad_gate = expert_math(
        h_rows, cot_rows, kept, router, up, down, 1 - z_at // 2, experts
    )
    grad_gate = kept * (grad_gate + gate_first[...])
    grad_logits = (probs * (grad_gate - jnp.sum(probs * grad_gate, axis=1, keepdims=True))).astype(bf16)

    before = turn - 1

    @pl.when((turn >= 1) & turn_is_other(before))
    def _():
        pass_other(before)

    @pl.when((turn == 5) | (turn == 7))
    def _():
        pass_total((turn - 5) // 2)

    @pl.when((turn == 3) | (turn == 5) | (turn == 7))
    def _():
        pass_own(before, (turn - 3) // 2)

    mixed_ref[...] = (mixed_first[...].astype(f32) + dot(hidden_rows, down)).astype(bf16)

    @pl.when(turn >= 2)
    def _():
        core_copy(turn - 2).wait_send()

    ring[turn % 2] = (
        grad_h_first[...].astype(f32) + dot(grad_pre, up, ((1,), (1,))) + dot(grad_logits, router, ((1,), (1,)))
    ).astype(bf16)
    core_copy(turn).start()
    h_turned = h_rows.T
    up_sum[...] += dot(h_turned, grad_pre)
    router_sum[...] += dot(h_turned, grad_logits)
    down_sum[...] += dot(cot_rows.T, hidden_rows)

    @pl.when(turn == steps - 1)
    def _():
        pass_own(7, 3)
        pass_total(2)
        grad_up_ref[...] = up_sum[...].astype(bf16)
        grad_down_ref[...] = down_sum[...].astype(bf16)
        grad_router_ref[...] = router_sum[...].T[:8]
        pass_total(3)
        for copy in pair_copies:
            copy.wait()
        for number in (6, 7):
            core_copy(number).wait_send()
        for place in range(4):
            y_copy(other_turn(place), place).wait_send()
            x_copy(own_turn(place), place).wait_send()
            total_copy(place).wait_send()
            total_copy(place).wait_recv()
            store_copy(place).wait()


def run_second_pair(
    h_rows,
    cot_rows,
    kept,
    router,
    mixed_first,
    grad_h_first,
    gate_first,
    up,
    down,
    up_first,
    down_first,
    experts,
):
    rows, features = h_rows.shape
    width = up.shape[2]
    steps = rows // BLOCK
    half = (BLOCK, features // 2)
    anywhere = pl.BlockSpec(memory_space=pl.ANY)
    shape = jax.ShapeDtypeStruct
    dma = pltpu.SemaphoreType.DMA

    def by_step(lanes):
        return pl.BlockSpec((BLOCK, lanes), lambda n: (turn_block(n), 0))

    def whole(*dims):
        return pl.BlockSpec(dims, lambda n: (0,) * len(dims))

    return pl.pallas_call(
        partial(second_pair_kernel, experts=experts, steps=steps),
        grid=(steps,),
        out_shape=[
            shape((rows, features), bf16),
            shape((features, width), bf16),
            shape((features, width), bf16),
            shape((8, features), f32),
            shape((rows // 2, features), bf16),
            shape((features, width // 2), bf16),
            shape((features, width // 2), bf16),
        ],
        in_specs=[
            by_step(features),
            by_step(features),
            by_step(128),
            whole(features, 128),
            by_step(features),
            by_step(features),
            by_step(128),
        ]
        + [anywhere] * 4,
        out_specs=[by_step(features), whole(features, width), whole(features, width), whole(8, features)] + [anywhere] * 3,
        scratch_shapes=[
            pltpu.VMEM((features, width), bf16),
            pltpu.VMEM((width, features), bf16),
            pltpu.VMEM((features, width), f32),
            pltpu.VMEM((features, width), f32),
            pltpu.VMEM((features, 128), f32),
            pltpu.VMEM((2, BLOCK, features), bf16),
            pltpu.VMEM((8, *half), bf16),
            pltpu.VMEM((4, *half), bf16),
            pltpu.VMEM((4, *half), bf16),
            dma((2,)),
        ]
        + [dma((8,))] * 2
        + [dma((4,))] * 7
        + [dma((2,))] * 2,
        compiler_params=pltpu.CompilerParams(
            collective_id=4, has_side_effects=True, vmem_limit_bytes=60 << 20
        ),
    )(h_rows, cot_rows, kept, router, mixed_first, grad_h_first, gate_first, up, down, up_first, down_first)


def backward_kernel(
    gain1_ref,
    shift1_ref,
    gain2_ref,
    qkv_ref,
    out_w_ref,
    grad_router_ref,
    tok_hbm,
    q_hbm,
    k_hbm,
    v_hbm,
    att_hbm,
    lse_hbm,
    grad_h_hbm,
    resid_ref,
    cot_ref,
    mixed_ref,
    up_first,
    down_first,
    up_pair,
    down_pair,
    up_second,
    down_second,
    up_out,
    down_out,
    tokens_out,
    qkv_out,
    out_w_out,
    sums_out,
    mixed_out,
    tok_ref,
    q_ref,
    k_ref,
    v_ref,
    att_ref,
    lse_ref,
    grad_h_ref,
    rows_kept,
    cot_rows,
    m_mine,
    m_core,
    m_y,
    m_x,
    m_out,
    m_resid,
    own_vm,
    pair_vm,
    far_vm,
    one_mine,
    one_to,
    one_core,
    one_x,
    one_total,
    line,
    weight_sum,
    weight_half,
    shared,
    shared_y,
    shared_line,
    shared_all,
    route_core,
    route_x,
    late_mine,
    late_y,
    late_z,
    up_total,
    down_total,
    sums_all,
    whole,
    mc_s,
    mc_r,
    my_s,
    my_r,
    mx_s,
    mx_r,
    mq_s,
    mq_r,
    m_store,
    oc_s,
    oc_r,
    ox_s,
    ox_r,
    ot_s,
    ot_r,
    l_s,
    l_r,
    sy_s,
    sy_r,
    sl_s,
    sl_r,
    sg_s,
    sg_r,
    sz_s,
    sz_r,
    r_s,
    r_r,
    late_s,
    late_r,
    load,
    image_load,
    own_sem,
    weight_store,
    store,
    *,
    images,
    heads,
):
    expert_at = lax.axis_index("expert")
    tensor_at = lax.axis_index("tensor")
    z_at, y_at = expert_at // 2, expert_at % 2
    z_last = lax.axis_size("expert") // 2 - 1
    x_at, core_at = tensor_at // 2, tensor_at % 2
    other = 1 - core_at
    rows = images * PITCH
    features = tok_hbm.shape[2]
    wide = features // 2
    share = out_w_ref.shape[0]
    hidden = line.shape[3]
    core_dev = (expert_at, tensor_at + 1 - 2 * core_at)
    x_dev = (expert_at, tensor_at + 2 - 4 * x_at)
    y_dev = (expert_at + 1 - 2 * y_at, tensor_at)
    z_devs = [(expert_at + 2, tensor_at), (expert_at - 2, tensor_at)]
    planes = z_last + 1
    z_others = [((z_at + hop) % planes * 2 + y_at, tensor_at) for hop in (1, 2, 3)]
    greet([(True, device) for device in (core_dev, x_dev, y_dev, *z_others)])
    my_cols = lanes_at(core_at * wide, wide)
    their_cols = lanes_at(other * wide, wide)

    def remote(src, dst, send, recv, device):
        return pltpu.make_async_remote_copy(
            src_ref=src, dst_ref=dst, send_sem=send, recv_sem=recv, device_id=device, device_id_type=MESH
        )

    def at_image(image):
        return aligned(image * PITCH, PITCH)

    part_count = m_y.shape[0]
    part_rows_m = rows // part_count

    def m_rows(side, part):
        return aligned(side * rows + part * part_rows_m, part_rows_m)

    def m_core_copy(side, part):
        at = m_rows(side, part)
        return remote(mixed_ref.at[at, their_cols], m_core.at[at, :], mc_s.at[side, part], mc_r.at[side, part], core_dev)

    for part in range(part_count):
        m_core_copy(1, part).start()
    for part in range(part_count):
        m_core_copy(0, part).start()
    m_loads = [
        pltpu.make_async_copy(mixed_ref.at[pl.ds(side * rows, rows), my_cols], m_mine.at[pl.ds(side * rows, rows), :], load.at[side])
        for side in range(2)
    ]

    def image_loads(image):
        at = at_image(image)
        by_image = ((tok_hbm, tok_ref), (q_hbm, q_ref), (k_hbm, k_ref), (v_hbm, v_ref), (att_hbm, att_ref), (lse_hbm, lse_ref))
        by_row = ((grad_h_hbm, grad_h_ref), (resid_ref, rows_kept), (cot_ref, cot_rows))
        pairs = [(source.at[image], target.at[image]) for source, target in by_image]
        pairs += [(source.at[at, :], target.at[at, :]) for source, target in by_row]
        return [pltpu.make_async_copy(source, target, image_load.at[n, image]) for n, (source, target) in enumerate(pairs)]

    def start_loads(image, _):
        for copy in image_loads(image):
            copy.start()
        return 0

    start_loads(0, 0)
    m_loads[1].start()
    lax.fori_loop(1, images, start_loads, 0)
    m_loads[0].start()
    route_one = remote(grad_router_ref, route_core, r_s.at[0], r_r.at[0], core_dev)
    route_one.start()

    def place(way):
        return z_at if way == 0 else z_last - z_at

    def far_lanes(way, piece):
        expert = z_last - piece // 2 if way == 0 else piece // 2
        return pl.ds(expert % 2 * hidden, hidden)

    def line_copy(source, way, piece):
        return remote(source, line.at[way, piece], l_s.at[way, piece], l_r.at[way, piece], z_devs[way])

    def line_copy_on(way, piece):
        return line_copy(line.at[way, piece], way, piece)

    def line_start():
        for way in range(2):

            @pl.when(place(way) == 0)
            def _():
                for piece in range(4):
                    source = (up_second, down_second)[piece % 2]
                    line_copy(source.at[:, far_lanes(way, piece)], way, piece).start()

    def line_add(piece):
        for way in range(2):

            @pl.when(place(way) == 1)
            def _():
                line_copy_on(way, piece).wait_recv()
                lanes = far_lanes(way, piece)

                def add(part, _):
                    at_rows = aligned(part * 96, 96)
                    total = line[way, piece, at_rows, :].astype(f32) + far_vm[piece % 2, at_rows, lanes].astype(f32)
                    line[way, piece, at_rows, :] = total.astype(bf16)
                    return 0

                lax.fori_loop(0, features // 96, add, 0)
                line_copy_on(way, piece).start()

    def line_pass(piece):
        for way in range(2):

            @pl.when(place(way) == 2)
            def _():
                line_copy_on(way, piece).wait_recv()
                line_copy_on(way, piece).start()

    line_start()
    own_lanes = lanes_at(z_at % 2 * hidden, hidden)
    later = [
        pltpu.make_async_copy(source, target, own_sem.at[number])
        for number, (source, target) in enumerate(
            (
                (up_second, far_vm.at[0]),
                (down_second, far_vm.at[1]),
                (up_first.at[:, own_lanes], own_vm.at[0]),
                (down_first.at[:, own_lanes], own_vm.at[1]),
                (up_pair, pair_vm.at[0]),
                (down_pair, pair_vm.at[1]),
            )
        )
    ]
    for copy in later:
        copy.start()
    weight_sum[...] = jnp.zeros_like(weight_sum)
    late_mine[...] = jnp.zeros_like(late_mine)

    def m_y_copy(part):
        return remote(m_core.at[m_rows(1, part), :], m_y.at[part], my_s.at[part], my_r.at[part], y_dev)

    def m_x_copy(part):
        return remote(m_core.at[m_rows(0, part), :], m_x.at[part], mx_s.at[part], mx_r.at[part], x_dev)

    def m_place(part):
        return mixed_out.at[aligned(part * part_rows_m, part_rows_m), :]

    def m_quarter_copy(part):
        return remote(m_out.at[part, other], m_place(part), mq_s.at[part], mq_r.at[part], core_dev)

    def m_store_copy(part):
        return pltpu.make_async_copy(m_out.at[part, core_at], m_place(part), m_store.at[part])

    def m_resid_copy(part):
        at = aligned(part * part_rows_m, part_rows_m)
        return pltpu.make_async_copy(resid_ref.at[at, lanes_at(x_at * wide, wide)], m_resid, load.at[3])

    keeps = x_at == core_at

    def run_m_y(part):
        m_core_copy(1, part).wait_recv()
        at = m_rows(1, part)
        m_core[at, :] = (m_core[at, :].astype(f32) + m_mine[at, :].astype(f32)).astype(bf16)
        m_y_copy(part).start()

    def run_m_x(part):
        if isinstance(part, int) and part == 0:
            m_loads[0].wait()
        m_core_copy(0, part).wait_recv()
        m_y_copy(part).wait_recv()
        at = m_rows(0, part)
        total = m_core[at, :].astype(f32) + m_mine[at, :].astype(f32) + m_y[part].astype(f32)
        m_core[at, :] = total.astype(bf16)

        @pl.when(jnp.logical_not(keeps))
        def _():
            m_x_copy(part).start()

    def run_m_out(part):
        @pl.when(keeps)
        def _():
            m_resid_copy(part).start()
            m_x_copy(part).wait_recv()
            m_resid_copy(part).wait()
            total = m_core[m_rows(0, part), :].astype(f32) + m_x[part].astype(f32)
            mixed = (m_resid[...] + total).astype(bf16)
            m_out[part, 0] = mixed[:, : wide // 2]
            m_out[part, 1] = mixed[:, wide // 2 :]
            m_quarter_copy(part).start()
            m_store_copy(part).start()

    m_loads[1].wait()
    for part in range(part_count):
        run_m_y(part)
    route_one.wait_recv()
    route_core[...] += grad_router_ref[...]
    route_two = remote(route_core, route_x, r_s.at[1], r_r.at[1], x_dev)
    route_two.start()

    def one_core_copy(image):
        return remote(one_to.at[image], one_core.at[image], oc_s.at[image], oc_r.at[image], core_dev)

    def one_x_copy(image):
        return remote(one_core.at[image], one_x.at[image], ox_s.at[image], ox_r.at[image], x_dev)

    def one_total_copy(image):
        return remote(one_x.at[image], one_total.at[image], ot_s.at[image], ot_r.at[image], core_dev)

    store_copy = pltpu.make_async_copy(rows_kept.at[pl.ds(0, images * SEQ), :], tokens_out, store.at[0])

    lane = lax.broadcasted_iota(jnp.int32, (PITCH, 2 * HD), 1)
    key_mask = lax.broadcasted_iota(jnp.int32, (PITCH, PITCH), 1) < SEQ
    gain1, shift1, gain2 = (ref[...].reshape(1, features) for ref in (gain1_ref, shift1_ref, gain2_ref))

    def norm_back(grad, gain, normed, inverse):
        scaled = grad * gain
        mean = jnp.mean(scaled, axis=1, keepdims=True)
        along = jnp.mean(scaled * normed, axis=1, keepdims=True)
        return (scaled - mean - normed * along) * inverse

    def add_sums(sums, row, grad, normed):
        sums[row : row + 1, :] += jnp.sum(grad * normed, axis=0, keepdims=True)
        sums[row + 1 : row + 2, :] += jnp.sum(grad, axis=0, keepdims=True)

    def run_attention(image):
        for copy in image_loads(image):
            copy.wait()
        at = at_image(image)
        grad_h = grad_h_ref[at, :].astype(f32)
        normed, inverse = norm_stats(rows_kept[at, :])
        add_sums(late_mine, 2, grad_h, normed)
        grad_resid = cot_rows[at, :].astype(f32) + norm_back(grad_h, gain2, normed, inverse)
        rows_kept[at, :] = grad_resid
        grad_branch = grad_resid.astype(bf16)
        token_normed, _ = norm_stats(tok_ref[image].astype(f32))
        h_one = (token_normed * gain1 + shift1).astype(bf16)
        queries, keys, values, attended = q_ref[image], k_ref[image], v_ref[image], att_ref[image]
        lse = lse_ref[image]
        grad_attended = dot(grad_branch, out_w_ref[...], ((1,), (1,))).astype(bf16)
        grads = [[], [], []]
        for head in range(heads):
            first = head // 2 * 2 * HD
            last = min(first + 2 * HD, heads * HD)
            parts = [whose[:, first:last] for whose in (queries, keys, values, grad_attended)]
            if last - first == 2 * HD:
                own = head_mask(lane, head)
                q_own, k_own, _, g_own = (jnp.where(own, part, jnp.zeros_like(part)) for part in parts)
            else:
                q_own, k_own, _, g_own = parts
            scores = dot(q_own, parts[1], ((1,), (1,))) * (HD**-0.5)
            probs = jnp.where(key_mask, jnp.exp(scores - lse[:, head : head + 1]), 0.0)
            back = dot(g_own, parts[2], ((1,), (1,)))
            product = probs * back
            grad_scores = (product - probs * jnp.sum(product, axis=1, keepdims=True)).astype(bf16)
            pieces = (
                dot(grad_scores, k_own) * (HD**-0.5),
                dot(grad_scores, q_own, ((0,), (0,))) * (HD**-0.5),
                dot(probs.astype(bf16), g_own, ((0,), (0,))),
            )
            for which in range(3):
                if head % 2 == 0:
                    grads[which].append(pieces[which])
                else:
                    grads[which][-1] += pieces[which]
        grad_rows = [jnp.concatenate(grads[which], axis=1).astype(bf16) for which in range(3)]
        grad_one = 0.0
        for which in range(3):
            weight_sum[which * share : (which + 1) * share, :] += dot(grad_rows[which].T, h_one)
            grad_one += dot(grad_rows[which], qkv_ref[which])
        weight_sum[3 * share : 4 * share, :] += dot(attended.T, grad_branch)
        whole[...] = grad_one
        one_mine[image] = whole[:, my_cols].astype(bf16)
        one_to[image] = whole[:, their_cols].astype(bf16)
        one_core_copy(image).start()

    def run_one_x(image):
        one_core_copy(image).wait_recv()
        one_core[image] = (one_core[image].astype(f32) + one_mine[image].astype(f32)).astype(bf16)
        one_x_copy(image).start()

    def run_one_total(image):
        one_x_copy(image).wait_recv()
        one_x[image] = (one_core[image].astype(f32) + one_x[image].astype(f32)).astype(bf16)
        one_total_copy(image).start()

    def run_tokens(image):
        one_total_copy(image).wait_recv()
        whole[:, my_cols] = one_x[image].astype(f32)
        whole[:, their_cols] = one_total[image].astype(f32)
        grad_one = whole[...]
        at = at_image(image)
        normed, inverse = norm_stats(tok_ref[image].astype(f32))
        add_sums(late_mine, 0, grad_one, normed)
        total = rows_kept[at, :] + norm_back(grad_one, gain1, normed, inverse)
        whole[...] = total
        for number in range(images):

            @pl.when(image == number)
            def _():
                rows_kept[pl.ds(number * SEQ, SEQ), :] = whole[pl.ds(0, SEQ), :]


    def stage(tick, lag, run):
        image = tick - lag

        @pl.when((image >= 0) & (image < images))
        def _():
            run(image)

    def at_tick(tick, when, run):
        @pl.when(tick == when)
        def _():
            run()

    def line_first():
        later[0].wait()
        later[1].wait()
        line_add(0)

    def line_second():
        line_add(1)
        line_pass(0)

    def per_tick(tick, _):
        stage(tick, 0, run_attention)
        stage(tick, 1, run_one_x)
        stage(tick, 4, run_one_total)
        stage(tick, 5, run_tokens)
        at_tick(tick, 3, line_first)
        at_tick(tick, 5, lambda: run_m_x(0))
        at_tick(tick, 6, line_second)
        at_tick(tick, 7, lambda: run_m_x(1))
        return 0

    lax.fori_loop(0, images, per_tick, 0)

    part_rows = shared.shape[1]
    quarter = part_rows // (z_last + 1)

    def to_half(side):
        def cast(piece, _):
            at_rows = aligned(piece * quarter, quarter)
            shared[side, at_rows, :] = weight_sum[aligned(side * part_rows + piece * quarter, quarter), :].astype(bf16)
            return 0

        lax.fori_loop(0, z_last + 1, cast, 0)

    to_half(0)
    to_half(1)

    def y_piece(number):
        inner = jnp.where(z_at == 1, jnp.where(number < 2, z_last - number, number - 2), jnp.where(number < 2, number, 5 - number))
        return jnp.where(z_at == 0, z_last - number, jnp.where(z_at == z_last, number, inner))

    def quarter_at(piece):
        return aligned(piece * quarter, quarter)

    def shared_y_copy(number):
        at_rows = quarter_at(y_piece(number))
        return remote(shared.at[1 - y_at, at_rows, :], shared_y.at[at_rows, :], sy_s.at[number], sy_r.at[number], y_dev)

    def take_y(number):
        shared_y_copy(number).wait_recv()
        at_rows = quarter_at(y_piece(number))
        weight_half[at_rows, :] = shared[y_at, at_rows, :].astype(f32) + shared_y[at_rows, :].astype(f32)

    for number in range(4):
        shared_y_copy(number).start()
    run_one_x(images - 1)
    run_m_x(part_count - 2)
    run_one_total(images - 4)
    run_tokens(images - 5)
    line_pass(1)
    line_add(2)

    def quarter_of(step, at, way):
        mirrored = z_last - step + at
        return mirrored if way == 0 else z_last - mirrored

    late_y_copy = remote(late_mine, late_y, late_s.at[0], late_r.at[0], y_dev)

    def late_copy(number):
        ref = late_z.at[z_at]
        return remote(ref, ref, late_s.at[number + 1], late_r.at[number + 1], z_others[number])

    def small_copy(step, way):
        return remote(shared_line.at[way, 0, step], shared_line.at[way, 1, step], sl_s.at[way, step], sl_r.at[way, step], z_devs[way])

    for step in range(3):
        take_y(step)
        if step == 2:
            take_y(3)
        for way in range(2):
            at = place(way)

            @pl.when((at <= step) & (at < z_last))
            def _():
                at_rows = quarter_at(quarter_of(step, at, way))
                if step == 0:
                    shared_line[way, 0, step] = weight_half[at_rows, :].astype(bf16)
                else:
                    came = jnp.where(at > 0, shared_line[way, 1, step - 1].astype(f32), 0.0)
                    shared_line[way, 0, step] = (weight_half[at_rows, :] + came).astype(bf16)
                small_copy(step, way).start()

        for way in range(2):
            at = place(way)

            @pl.when((at > 0) & (at - 1 <= step))
            def _():
                small_copy(step, way).wait_recv()

        if step == 0:
            run_m_x(part_count - 1)
            run_one_total(images - 3)
            run_tokens(images - 4)
            run_m_out(0)
        if step == 1:
            run_one_total(images - 2)
            run_tokens(images - 3)
            run_m_out(1)
            line_add(3)

    own_rows = quarter_at(z_at)
    from_below = jnp.where(z_at > 0, shared_line[0, 1, 2].astype(f32), 0.0)
    from_above = jnp.where(z_at < z_last, shared_line[1, 1, 2].astype(f32), 0.0)

    def final_rows(side, piece):
        return shared_all.at[side, quarter_at(piece), :]

    shared_all[y_at, own_rows, :] = (weight_half[own_rows, :] + from_below + from_above).astype(bf16)
    for number in range(4):
        shared_y_copy(number).wait_send()

    def gather_z(step, way, piece):
        ref = final_rows(y_at, piece)
        return remote(ref, ref, sg_s.at[way, step], sg_r.at[way, step], z_devs[way])

    def gather_y(step, way, piece, side):
        ref = final_rows(side, piece)
        return remote(ref, ref, sz_s.at[way, step], sz_r.at[way, step], y_dev)

    gather_y(0, 0, z_at, y_at).start()

    def between(step):
        if step == 0:
            run_one_total(images - 1)
            run_tokens(images - 2)
        if step == 1:
            run_tokens(images - 1)
            route_two.wait_recv()
            late_mine[8:16, :] = route_core[...] + route_x[...]
            late_y_copy.start()
            store_copy.start()
            run_m_out(part_count - 2)
        if step == 2:
            run_m_out(part_count - 1)
            late_y_copy.wait_recv()
            late_z[z_at] = late_mine[...] + late_y[...]
            for number in range(planes - 1):
                late_copy(number).start()

    for step in range(3):
        for way in range(2):
            at = place(way)
            piece = z_at - step if way == 0 else z_at + step

            @pl.when((at >= step) & (at < z_last))
            def _():
                gather_z(step, way, piece).start()

        between(step)
        for way in range(2):
            at = place(way)
            piece = z_at - 1 - step if way == 0 else z_at + 1 + step

            @pl.when(at >= 1 + step)
            def _():
                gather_z(step, way, piece).wait_recv()
                gather_y(step + 1, way, piece, y_at).start()

    for copy in later[2:]:
        copy.wait()
    for way in range(2):

        @pl.when(place(way) == 2)
        def _():
            line_copy_on(way, 2).wait_recv()
            line_copy_on(way, 3).wait_recv()

        @pl.when(place(way) == z_last)
        def _():
            line_copy_on(way, 0).wait_recv()
            line_copy_on(way, 1).wait_recv()

    from_far = 1 - z_at // 2
    first_piece = jnp.where((z_at == 0) | (z_at == z_last), 0, 2)

    def finish(piece, _):
        at_rows = aligned(piece * 128, 128)
        totals = [
            own_vm[n, at_rows, :].astype(f32)
            + pair_vm[n, at_rows, :].astype(f32)
            + line[from_far, first_piece + n, at_rows, :].astype(f32)
            for n in range(2)
        ]
        up_total[at_rows, :] = totals[0]
        down_total[:, lanes_at(piece * 128, 128)] = totals[1].T
        return 0

    lax.fori_loop(0, features // 128, finish, 0)
    expert_copies = [
        pltpu.make_async_copy(up_total, up_out, weight_store.at[5]),
        pltpu.make_async_copy(down_total, down_out, weight_store.at[6]),
    ]
    for copy in expert_copies:
        copy.start()

    gather_y(0, 0, z_at, 1 - y_at).wait_recv()
    for step in range(3):
        for way in range(2):
            at = place(way)
            piece = z_at - 1 - step if way == 0 else z_at + 1 + step

            @pl.when(at >= 1 + step)
            def _():
                gather_y(step + 1, way, piece, 1 - y_at).wait_recv()

    def to_out(piece, _):
        for side in range(2):
            weight_sum[aligned(side * part_rows + piece * quarter, quarter), :] = shared_all[
                side, quarter_at(piece), :
            ].astype(f32)
        return 0

    lax.fori_loop(0, z_last + 1, to_out, 0)
    for number in range(planes - 1):
        late_copy(number).wait_recv()
    late = late_z[0]
    for plane in range(1, planes):
        late += late_z[plane]
    sums_all[...] = late
    weight_copies = [
        *[
            pltpu.make_async_copy(weight_sum.at[pl.ds(n * share, share), :], qkv_out.at[n], weight_store.at[n])
            for n in range(3)
        ],
        pltpu.make_async_copy(weight_sum.at[pl.ds(3 * share, share), :], out_w_out, weight_store.at[3]),
        pltpu.make_async_copy(sums_all, sums_out, weight_store.at[4]),
    ]
    for copy in weight_copies:
        copy.start()
    route_one.wait_send()
    route_two.wait_send()

    def drain(image, _):
        for copy in (one_core_copy, one_x_copy, one_total_copy):
            copy(image).wait_send()
        return 0

    lax.fori_loop(0, images, drain, 0)
    for part in range(part_count):
        m_core_copy(0, part).wait_send()
        m_core_copy(1, part).wait_send()
        m_y_copy(part).wait_send()

        @pl.when(keeps)
        def _():
            m_quarter_copy(part).wait_send()
            m_store_copy(part).wait()

        @pl.when(jnp.logical_not(keeps))
        def _():
            m_x_copy(part).wait_send()
            m_quarter_copy(part).wait_recv()

    for copy in (*weight_copies, *expert_copies, store_copy):
        copy.wait()
    late_y_copy.wait_send()
    for number in range(planes - 1):
        late_copy(number).wait_send()
    gather_y(0, 0, z_at, y_at).wait_send()
    for way in range(2):

        @pl.when(place(way) <= 1)
        def _():
            for piece in range(4):
                line_copy_on(way, piece).wait_send()

        @pl.when(place(way) == 2)
        def _():
            for piece in range(2):
                line_copy_on(way, piece).wait_send()

    for step in range(3):
        for way in range(2):
            at = place(way)

            @pl.when((at <= step) & (at < z_last))
            def _():
                small_copy(step, way).wait_send()

            piece = z_at - step if way == 0 else z_at + step

            @pl.when((at >= step) & (at < z_last))
            def _():
                gather_z(step, way, piece).wait_send()

            piece = z_at - 1 - step if way == 0 else z_at + 1 + step

            @pl.when(at >= 1 + step)
            def _():
                gather_y(step + 1, way, piece, y_at).wait_send()


def run_backward(gain1, shift1, gain2, qkv_w, out_w, grad_router, tok, *streamed):
    images, _, features = tok.shape
    rows = images * PITCH
    share = out_w.shape[0]
    heads = share // HD
    hidden = streamed[-1].shape[1] // 2
    wide = features // 2
    parts = 4
    vmem = pl.BlockSpec(memory_space=pltpu.VMEM)
    anywhere = pl.BlockSpec(memory_space=pl.ANY)
    shape = jax.ShapeDtypeStruct
    dma = pltpu.SemaphoreType.DMA
    block = (images, PITCH, wide)
    return pl.pallas_call(
        partial(backward_kernel, images=images, heads=heads),
        out_shape=[
            shape((features, hidden), f32),
            shape((hidden, features), f32),
            shape((images * SEQ, features), f32),
            shape((3, share, features), f32),
            shape((share, features), f32),
            shape((16, features), f32),
            shape((rows, wide // 2), bf16),
        ],
        in_specs=[vmem] * 6 + [anywhere] * (1 + len(streamed)),
        out_specs=[anywhere] * 7,
        scratch_shapes=[
            pltpu.VMEM((images, PITCH, features), bf16),
            *[pltpu.VMEM((images, PITCH, share), bf16)] * 4,
            pltpu.VMEM((images, PITCH, 128), f32),
            pltpu.VMEM((rows, features), bf16),
            pltpu.VMEM((rows, features), f32),
            pltpu.VMEM((rows, features), bf16),
            pltpu.VMEM((2 * rows, wide), bf16),
            pltpu.VMEM((2 * rows, wide), bf16),
            *[pltpu.VMEM((parts, rows // parts, wide), bf16)] * 2,
            pltpu.VMEM((parts, 2, rows // parts, wide // 2), bf16),
            pltpu.VMEM((rows // parts, wide), f32),
            pltpu.VMEM((2, features, hidden), bf16),
            pltpu.VMEM((2, features, hidden), bf16),
            pltpu.VMEM((2, features, 2 * hidden), bf16),
            *[pltpu.VMEM(block, bf16)] * 5,
            pltpu.VMEM((2, 4, features, hidden), bf16),
            pltpu.VMEM((features, features), f32),
            pltpu.VMEM((features // 2, features), f32),
            pltpu.VMEM((2, features // 2, features), bf16),
            pltpu.VMEM((features // 2, features), bf16),
            pltpu.VMEM((2, 2, 3, features // 8, features), bf16),
            pltpu.VMEM((2, features // 2, features), bf16),
            *[pltpu.VMEM((8, features), f32)] * 2,
            *[pltpu.VMEM((16, features), f32)] * 2,
            pltpu.VMEM((4, 16, features), f32),
            pltpu.VMEM((features, hidden), f32),
            pltpu.VMEM((hidden, features), f32),
            pltpu.VMEM((16, features), f32),
            pltpu.VMEM((PITCH, features), f32),
        ]
        + [dma((2, parts))] * 2
        + [dma((parts,))] * 7
        + [dma((images,))] * 6
        + [dma((2, 4))] * 2
        + [dma((4,))] * 2
        + [dma((2, 3))] * 4
        + [dma((2, 4))] * 2
        + [dma((2,))] * 2
        + [dma((4,))] * 2
        + [dma((4,)), dma((9, images)), dma((6,)), dma((7,)), dma((1,))],
        compiler_params=pltpu.CompilerParams(
            collective_id=2, has_side_effects=True, vmem_limit_bytes=63 << 20
        ),
    )(gain1, shift1, gain2, qkv_w, out_w, grad_router, tok, *streamed)


def per_image(rows_in):
    images = rows_in.shape[0] // SEQ
    blocks = rows_in.reshape(images, SEQ, rows_in.shape[1])
    return jnp.pad(blocks, ((0, 0), (0, PITCH - SEQ), (0, 0)))


def unpad(blocks):
    images = blocks.shape[0]
    return blocks[:, :SEQ].reshape(images * SEQ, blocks.shape[2])


def per_device_dense(
    tokens,
    gain_attn,
    shift_attn,
    qkv_weight,
    out_weight,
    gain_moe,
    shift_moe,
    router_weight,
    expert_up,
    expert_down,
    routes,
    keep_mask,
    cotangent,
):
    row_count, feature_count = tokens.shape
    images = row_count // SEQ
    rows = images * PITCH
    tensor_count = lax.axis_size("tensor")
    quarter_width = feature_count // tensor_count
    experts_all = router_weight.shape[1]
    hidden = expert_up.shape[2]
    kept_routes = per_image(jnp.where(keep_mask > 0, routes, -1) + 1).reshape(rows, 2) - 1
    chosen = kept_routes[:, :, None] == jnp.arange(128, dtype=jnp.int32)[None, None, :]
    kept = jnp.any(chosen, axis=1).astype(bf16)
    router_wide = jnp.pad(router_weight, ((0, 0), (0, 128 - experts_all)))
    tok = per_image(tokens)
    qkv_turned = jnp.swapaxes(qkv_weight, 1, 2)
    (
        queries,
        keys,
        values,
        attended,
        lse,
        resid,
        h_all,
        cot_all,
        kept_all,
        up_all,
        down_all,
        mixed_first,
        grad_h_first,
        gate_first,
        up_first,
        down_first,
    ) = run_forward(
        tok,
        gain_attn,
        shift_attn,
        gain_moe,
        shift_moe,
        qkv_turned,
        out_weight,
        expert_up[0],
        expert_down[0],
        per_image(cotangent).reshape(rows, quarter_width),
        kept,
        router_wide,
        experts_all,
    )
    mixed_part, up_second, down_second, grad_router, grad_h_two, up_pair, down_pair = run_second_pair(
        h_all,
        cot_all,
        kept_all,
        router_wide,
        mixed_first,
        grad_h_first,
        gate_first,
        up_all,
        down_all,
        up_first,
        down_first,
        experts_all,
    )
    grad_up, grad_down, tokens_grad, grad_qkv, grad_out, sums, mixed = run_backward(
        gain_attn,
        shift_attn,
        gain_moe,
        qkv_turned,
        out_weight,
        grad_router,
        tok,
        queries,
        keys,
        values,
        attended,
        lse,
        grad_h_two,
        resid,
        cot_all,
        mixed_part,
        up_first,
        down_first,
        up_pair,
        down_pair,
        up_second,
        down_second,
    )
    return (
        unpad(mixed.reshape(images, PITCH, quarter_width)),
        tokens_grad,
        sums[0],
        sums[1],
        jnp.swapaxes(grad_qkv, 1, 2),
        grad_out,
        sums[2],
        sums[3],
        sums[8 : 8 + experts_all].T,
        grad_up[None],
        grad_down[None],
    )


def per_device(*arguments):
    router_weight = arguments[7]
    if router_weight.shape[1] == 4 and lax.axis_size("expert") == 8 and lax.axis_size("tensor") == 4:
        return per_device_dense(*arguments)
    return per_device_routed(*arguments)


def solution(mesh):
    placed = (
        P("expert", None),
        P(),
        P(),
        P(None, None, "tensor"),
        P("tensor", None),
        P(),
        P(),
        P(),
        P("expert", None, "tensor"),
        P("expert", "tensor", None),
        P("expert", None),
        P("expert", None),
        P("expert", "tensor"),
    )
    return jax.shard_map(
        per_device,
        mesh=mesh,
        in_specs=placed,
        out_specs=(
            P("expert", "tensor"),
            P("expert", None),
            P(),
            P(),
            P(None, None, "tensor"),
            P("tensor", None),
            P(),
            P(),
            P(),
            P("expert", None, "tensor"),
            P("expert", "tensor", None),
        ),
        check_vma=False,
    )
```

```python
from functools import partial

import jax
import jax.numpy as jnp
from jax import lax
from jax.experimental import pallas as pl
from jax.experimental.pallas import tpu as pltpu
from jax.sharding import PartitionSpec as P

HD = 64
SEQ = 197


norm_epsilon = 1e-06


def norm_rows(values, gain, shift):
    row_mean = jnp.mean(values, axis=-1, keepdims=True)
    centred = values - row_mean
    spread = jnp.mean(centred * centred, axis=-1, keepdims=True)
    return centred * lax.rsqrt(spread + norm_epsilon) * gain + shift


def gelu_exact(values):
    return jax.nn.gelu(values, approximate=False)


def gate_from_logits(logit_rows, picked_rows, keep_rows):
    router_probs = jax.nn.softmax(logit_rows, axis=-1)
    return jnp.sum(jnp.where(picked_rows, router_probs[:, None, :], 0.0), axis=-1) * keep_rows


def attention_forward(h_rows, qkv_w, out_w):
    row_total_count = h_rows.shape[0]
    head_count = qkv_w.shape[2] // HD
    image_count = row_total_count // SEQ
    score_scale = HD ** (-0.5)
    projected = jnp.einsum("td,cdf->ctf", h_rows, qkv_w, preferred_element_type=jnp.float32).astype(
        jnp.bfloat16
    )
    split_heads = projected.reshape(3, image_count, SEQ, head_count, HD)
    queries = split_heads[0]
    keys_all = split_heads[1]
    values_all = split_heads[2]
    scores = (
        jnp.einsum("gqhe,gkhe->ghqk", queries, keys_all, preferred_element_type=jnp.float32)
        * score_scale
    )
    row_peak = jnp.max(scores, axis=-1, keepdims=True)
    exp_scores = jnp.exp(scores - row_peak)
    row_total = jnp.sum(exp_scores, axis=-1, keepdims=True)
    log_total = row_peak + jnp.log(row_total)
    weights = (exp_scores / row_total).astype(jnp.bfloat16)
    attended = jnp.einsum(
        "ghqk,gkhe->gqhe", weights, values_all, preferred_element_type=jnp.float32
    ).astype(jnp.bfloat16)
    attended = attended.reshape(row_total_count, head_count * HD)
    partial_out = jnp.dot(attended, out_w, preferred_element_type=jnp.float32)
    return (partial_out, (attended, queries, keys_all, values_all, log_total))


def attention_backward(grad_branch, saved, h_rows, qkv_w, out_w):
    attended, queries, keys_all, values_all, log_total = saved
    row_total_count = h_rows.shape[0]
    head_count = qkv_w.shape[2] // HD
    image_count = row_total_count // SEQ
    score_scale = HD ** (-0.5)
    grad_out = jnp.einsum("tc,td->cd", attended, grad_branch, preferred_element_type=jnp.float32)
    grad_attended = jnp.einsum(
        "td,cd->tc", grad_branch, out_w, preferred_element_type=jnp.float32
    ).astype(jnp.bfloat16)
    grad_attended = grad_attended.reshape(image_count, SEQ, head_count, HD)
    scores_again = (
        jnp.einsum("gqhe,gkhe->ghqk", queries, keys_all, preferred_element_type=jnp.float32)
        * score_scale
    )
    probs_again = jnp.exp(scores_again - log_total)
    grad_weights = jnp.einsum(
        "gqhe,gkhe->ghqk", grad_attended, values_all, preferred_element_type=jnp.float32
    )
    grad_scores = (
        probs_again * (grad_weights - jnp.sum(probs_again * grad_weights, axis=-1, keepdims=True))
    ).astype(jnp.bfloat16)
    grad_queries = (
        jnp.einsum("ghqk,gkhe->gqhe", grad_scores, keys_all, preferred_element_type=jnp.float32)
        * score_scale
    )
    grad_keys = (
        jnp.einsum("ghqk,gqhe->gkhe", grad_scores, queries, preferred_element_type=jnp.float32)
        * score_scale
    )
    grad_values = jnp.einsum(
        "ghqk,gqhe->gkhe",
        probs_again.astype(jnp.bfloat16),
        grad_attended,
        preferred_element_type=jnp.float32,
    )
    grad_rows = (
        jnp.stack([grad_queries, grad_keys, grad_values])
        .astype(jnp.bfloat16)
        .reshape(3, row_total_count, head_count * HD)
    )
    grad_qkv = jnp.einsum("td,ctf->cdf", h_rows, grad_rows, preferred_element_type=jnp.float32)
    grad_h_one = jnp.einsum("ctf,cdf->td", grad_rows, qkv_w, preferred_element_type=jnp.float32)
    return (grad_qkv, grad_out, grad_h_one)


def moe_tail(
    grad_h_rows,
    grad_gate_rows,
    grad_out_rows,
    h_two_rows,
    resid_rows,
    gate_back,
    router_weight,
    gain_moe,
    shift_moe,
):
    row_total_count = grad_h_rows.shape[0]
    grad_gate = jnp.sum(grad_gate_rows.reshape(row_total_count, -1, 2), axis=1)
    grad_logits = gate_back(grad_gate)[0].astype(jnp.bfloat16)
    grad_router = jnp.einsum(
        "td,te->de", h_two_rows, grad_logits, preferred_element_type=jnp.float32
    )
    grad_h_two = grad_h_rows + jnp.einsum(
        "te,de->td", grad_logits, router_weight, preferred_element_type=jnp.float32
    )
    norm_out, norm_back = jax.vjp(norm_rows, resid_rows, gain_moe, shift_moe)
    grad_resid_norm, grad_gain_moe, grad_shift_moe = norm_back(grad_h_two)
    return (grad_out_rows + grad_resid_norm, grad_router, grad_gain_moe, grad_shift_moe)


def per_device_routed(
    tokens,
    gain_attn,
    shift_attn,
    qkv_weight,
    out_weight,
    gain_moe,
    shift_moe,
    router_weight,
    expert_up,
    expert_down,
    routes,
    keep_mask,
    cotangent,
):
    row_count, feature_count = tokens.shape
    tensor_count = lax.axis_size("tensor")
    expert_count = lax.axis_size("expert")
    tensor_here = lax.axis_index("tensor")
    quarter_width = feature_count // tensor_count
    col_start = tensor_here * quarter_width
    experts_all = router_weight.shape[1]
    capacity = max(2, 7 * row_count // (2 * experts_all))
    tokens_float = tokens.astype(jnp.float32)
    h_one = norm_rows(tokens_float, gain_attn, shift_attn).astype(jnp.bfloat16)
    partial_out, saved = attention_forward(h_one, qkv_weight, out_weight)
    branch = lax.psum(partial_out, "tensor")
    resid = tokens_float + branch
    h_two = norm_rows(resid, gain_moe, shift_moe).astype(jnp.bfloat16)
    logits = jnp.dot(h_two, router_weight, preferred_element_type=jnp.float32)
    keep_float = keep_mask.astype(jnp.float32)
    picked = routes[:, :, None] == jnp.arange(experts_all, dtype=jnp.int32)[None, None, :]
    gate_values, gate_back = jax.vjp(
        partial(gate_from_logits, picked_rows=picked, keep_rows=keep_float), logits
    )
    flat_expert = routes.reshape(-1)
    one_hot = (flat_expert[:, None] == jnp.arange(experts_all, dtype=jnp.int32)[None, :]).astype(
        jnp.int32
    )
    rank_within = jnp.sum((jnp.cumsum(one_hot, axis=0) - one_hot) * one_hot, axis=1)
    slot_index = flat_expert * capacity + rank_within
    token_index = jnp.repeat(jnp.arange(row_count, dtype=jnp.int32), 2)
    live_route = keep_mask.reshape(-1) > 0
    source_table = (
        jnp.full((experts_all * capacity,), row_count, jnp.int32)
        .at[slot_index]
        .set(jnp.where(live_route, token_index, row_count))
    )
    padded_rows = jnp.concatenate([h_two, jnp.zeros((1, feature_count), jnp.bfloat16)], axis=0)
    dispatch = padded_rows[source_table].reshape(experts_all, capacity, feature_count)
    paired = jnp.broadcast_to(dispatch[:, None], (experts_all, 2, capacity, feature_count)).reshape(
        expert_count, capacity, feature_count
    )
    arrived = lax.all_to_all(paired, "expert", split_axis=0, concat_axis=0, tiled=True)
    expert_rows = arrived.reshape(expert_count * capacity, feature_count)
    up_local = expert_up[0]
    down_local = expert_down[0]
    pre_act = jnp.dot(expert_rows, up_local, preferred_element_type=jnp.float32)
    hidden_float, gelu_back = jax.vjp(gelu_exact, pre_act)
    hidden = hidden_float.astype(jnp.bfloat16)
    partial_down = jnp.dot(hidden, down_local, preferred_element_type=jnp.float32)
    summed = lax.psum_scatter(partial_down, "tensor", scatter_dimension=1, tiled=True)
    returned = lax.all_to_all(
        summed.reshape(expert_count, capacity, quarter_width),
        "expert",
        split_axis=0,
        concat_axis=0,
        tiled=True,
    )
    answer_table = jnp.sum(
        returned.reshape(experts_all, 2, capacity, quarter_width), axis=1
    ).astype(jnp.bfloat16)
    answers = (
        answer_table.reshape(experts_all * capacity, quarter_width)[slot_index]
        .astype(jnp.float32)
        .reshape(row_count, 2, quarter_width)
    )
    resid_part = lax.dynamic_slice_in_dim(resid, col_start, quarter_width, 1)
    mixed = (resid_part + jnp.sum(gate_values[:, :, None] * answers, axis=1)).astype(jnp.bfloat16)
    grad_part = cotangent.astype(jnp.float32)
    grad_answers = (
        (gate_values[:, :, None] * grad_part[:, None, :])
        .astype(jnp.bfloat16)
        .reshape(2 * row_count, quarter_width)
    )
    grad_gate_part = jnp.sum(grad_part[:, None, :] * answers, axis=-1)
    outgoing = (
        jnp.zeros((experts_all * capacity, quarter_width), jnp.bfloat16)
        .at[slot_index]
        .set(grad_answers)
    )
    outgoing = jnp.broadcast_to(
        outgoing.reshape(experts_all, 1, capacity, quarter_width),
        (experts_all, 2, capacity, quarter_width),
    ).reshape(expert_count, capacity, quarter_width)
    incoming = lax.all_to_all(outgoing, "expert", split_axis=0, concat_axis=0, tiled=True)
    grad_full = lax.all_gather(incoming, "tensor", axis=2, tiled=True).reshape(
        expert_count * capacity, feature_count
    )
    grad_hidden = jnp.einsum("rd,fd->rf", grad_full, down_local, preferred_element_type=jnp.float32)
    grad_pre = gelu_back(grad_hidden)[0].astype(jnp.bfloat16)
    grad_down = jnp.einsum("rf,rd->fd", hidden, grad_full, preferred_element_type=jnp.float32)
    grad_up = jnp.einsum("rd,rf->df", expert_rows, grad_pre, preferred_element_type=jnp.float32)
    grad_rows_partial = jnp.einsum(
        "rf,df->rd", grad_pre, up_local, preferred_element_type=jnp.float32
    )
    grad_rows_sum = lax.psum_scatter(
        grad_rows_partial.astype(jnp.bfloat16), "tensor", scatter_dimension=1, tiled=True
    ).astype(jnp.float32)
    sent_back = lax.all_to_all(
        grad_rows_sum.reshape(expert_count, capacity, quarter_width).astype(jnp.bfloat16),
        "expert",
        split_axis=0,
        concat_axis=0,
        tiled=True,
    ).astype(jnp.float32)
    grad_table = jnp.sum(sent_back.reshape(experts_all, 2, capacity, quarter_width), axis=1).astype(
        jnp.bfloat16
    )
    grad_inputs = (
        grad_table.reshape(experts_all * capacity, quarter_width)[slot_index]
        .astype(jnp.float32)
        .reshape(row_count, 2, quarter_width)
    )
    grad_h_part = jnp.sum(grad_inputs * keep_float[:, :, None], axis=1)
    grad_h_full, grad_gate_all, grad_out_full = (
        lax.all_gather(grad_h_part, "tensor", axis=1, tiled=True),
        lax.all_gather(grad_gate_part, "tensor", axis=1, tiled=True),
        lax.all_gather(grad_part, "tensor", axis=1, tiled=True),
    )
    grad_resid, grad_router, grad_gain_moe, grad_shift_moe = moe_tail(
        grad_h_full,
        grad_gate_all,
        grad_out_full,
        h_two,
        resid,
        gate_back,
        router_weight,
        gain_moe,
        shift_moe,
    )
    grad_qkv, grad_out, grad_h_one_part = attention_backward(
        grad_resid.astype(jnp.bfloat16), saved, h_one, qkv_weight, out_weight
    )
    grad_h_one = lax.psum(grad_h_one_part.astype(jnp.bfloat16), "tensor").astype(jnp.float32)
    norm_one_out, norm_one_back = jax.vjp(norm_rows, tokens_float, gain_attn, shift_attn)
    grad_tok_norm, grad_gain_attn, grad_shift_attn = norm_one_back(grad_h_one)
    grad_tokens = grad_resid + grad_tok_norm
    summed_grads = lax.psum(
        (
            grad_gain_attn,
            grad_shift_attn,
            grad_qkv,
            grad_out,
            grad_gain_moe,
            grad_shift_moe,
            grad_router,
        ),
        "expert",
    )
    grad_qkv_mine = summed_grads[2]
    grad_out_mine = summed_grads[3]
    return (
        mixed,
        grad_tokens,
        summed_grads[0],
        summed_grads[1],
        grad_qkv_mine,
        grad_out_mine,
        summed_grads[4],
        summed_grads[5],
        summed_grads[6],
        grad_up[None],
        grad_down[None],
    )


MESH = pl.DeviceIdType.MESH
f32 = jnp.float32
bf16 = jnp.bfloat16
PITCH = 208


def dot(left, right, over=((1,), (0,))):
    return lax.dot_general(left, right, (over, ((), ())), preferred_element_type=f32)


def aligned(start, size):
    return pl.ds(pl.multiple_of(start, 16), size)


def lanes_at(start, size):
    return pl.ds(pl.multiple_of(start, 128), size)


def norm_stats(values):
    row_mean = jnp.mean(values, axis=1, keepdims=True)
    centred = values - row_mean
    inverse = lax.rsqrt(jnp.mean(centred * centred, axis=1, keepdims=True) + norm_epsilon)
    return centred * inverse, inverse


def greet(neighbours):
    barrier = pltpu.get_barrier_semaphore()
    count = 0
    for is_there, device in neighbours:

        @pl.when(is_there)
        def _():
            pl.semaphore_signal(barrier, inc=1, device_id=device, device_id_type=MESH)

        count = count + jnp.where(is_there, 1, 0)
    pl.semaphore_wait(barrier, count)


def head_mask(lane, head):
    return (lane < HD) if head % 2 == 0 else (lane >= HD)


def expert_math(h_rows, cot_rows, kept, router, up, down, pair, experts):
    block = h_rows.shape[0]
    hidden = up.shape[1] // 2
    lane = lax.broadcasted_iota(jnp.int32, (block, 128), 1)
    logits = jnp.where(lane < experts, dot(h_rows, router), -1e30)
    powers = jnp.exp(logits - jnp.max(logits, axis=1, keepdims=True))
    probs = powers / jnp.sum(powers, axis=1, keepdims=True)
    gates = kept * probs
    pre_act = dot(h_rows, up)
    back = dot(cot_rows, down, ((1,), (1,)))
    normal_cdf = 0.5 + 0.5 * lax.erf(pre_act * 0.7071067811865476)
    gelu = pre_act * normal_cdf
    slope = normal_cdf + pre_act * (0.3989422804014327 * jnp.exp(-0.5 * pre_act * pre_act))
    product = gelu * back
    grad_gate = jnp.zeros((block, 128), f32)
    spread = []
    for side in range(2):
        chosen = lane == 2 * pair + side
        part = jnp.sum(product[:, side * hidden : (side + 1) * hidden], axis=1, keepdims=True)
        grad_gate = jnp.where(chosen, part, grad_gate)
        gate = jnp.sum(jnp.where(chosen, gates, 0.0), axis=1, keepdims=True)
        spread.append(jnp.broadcast_to(gate, (block, hidden)))
    gate = jnp.concatenate(spread, axis=1)
    hidden_rows = (gelu * gate).astype(bf16)
    grad_pre = (slope * back * gate).astype(bf16)
    return hidden_rows, grad_pre, probs, grad_gate


BLOCK = 2 * PITCH


def forward_kernel(
    tok_ref,
    gain1_ref,
    shift1_ref,
    gain2_ref,
    shift2_ref,
    qkv_ref,
    out_w_ref,
    up_ref,
    down_ref,
    cot_ref,
    kept_ref,
    router_ref,
    q_ref,
    k_ref,
    v_ref,
    att_ref,
    lse_ref,
    resid_ref,
    h_out,
    cot_out,
    kept_out,
    up_out,
    down_out,
    mixed_out,
    grad_h_out,
    gate_out,
    grad_up_out,
    grad_down_out,
    up_vm,
    down_vm,
    up_sum,
    down_sum,
    mixed_slots,
    grad_h_slots,
    gate_slots,
    grad_up_vm,
    grad_down_vm,
    q_all,
    k_all,
    v_all,
    att_all,
    lse_all,
    resid_all,
    h_all,
    cot_all,
    kept_all,
    part,
    mine,
    core_from,
    core_to,
    x_to,
    x_from,
    total_to,
    total_from,
    cot_core,
    core_s,
    core_r,
    x_s,
    x_r,
    tot_s,
    tot_r,
    y_s,
    y_r,
    rel_s,
    rel_r,
    w_s,
    w_r,
    c_s,
    c_r,
    own_sem,
    pair_sem,
    block_sem,
    grad_sem,
    cot_sem,
    out_sem,
    *,
    images,
    heads,
    experts,
):
    expert_at = lax.axis_index("expert")
    tensor_at = lax.axis_index("tensor")
    z_at, y_at = expert_at // 2, expert_at % 2
    z_last = lax.axis_size("expert") // 2 - 1
    x_at, core_at = tensor_at // 2, tensor_at % 2
    other = 1 - core_at
    rows = images * PITCH
    half = rows // 2
    wide = out_w_ref.shape[1] // 2
    hidden = up_ref.shape[1]
    core_dev = (expert_at, tensor_at + 1 - 2 * core_at)
    x_dev = (expert_at, tensor_at + 2 - 4 * x_at)
    y_dev = (expert_at + 1 - 2 * y_at, tensor_at)
    z_up = (expert_at + 2, tensor_at)
    z_down = (expert_at - 2, tensor_at)
    has_up, has_down = z_at < z_last, z_at > 0
    greet([(True, core_dev), (True, x_dev), (True, y_dev), (has_up, z_up), (has_down, z_down)])

    def remote(src, dst, send, recv, device):
        return pltpu.make_async_remote_copy(
            src_ref=src, dst_ref=dst, send_sem=send, recv_sem=recv, device_id=device, device_id_type=MESH
        )

    def slot(expert, plane):
        pair = (expert // 2 + plane // 2) % 2
        return (
            up_out.at[pair, :, lanes_at(expert % 2 * hidden, hidden)],
            down_out.at[pair, aligned(expert % 2 * hidden, hidden), :],
        )

    def hop(step, way):
        expert = z_at - step if way == 0 else z_at + step
        plane = z_at + 1 if way == 0 else z_at - 1
        source = (up_ref, down_ref) if step == 0 else slot(expert, z_at)
        target = slot(expert, plane)
        device = z_up if way == 0 else z_down
        return [remote(source[n], target[n], w_s.at[way, step, n], w_r.at[way, step, n], device) for n in range(2)]

    def hop_goes(step, way):
        if way == 0:
            return (z_at - step >= 0) & has_up
        return (z_at + step <= z_last) & has_down

    def hop_comes(step, way):
        return (z_at - 1 - step >= 0) if way == 0 else (z_at + 1 + step <= z_last)

    def hop_arriving(step, way):
        expert = z_at - 1 - step if way == 0 else z_at + 1 + step
        target = slot(expert, z_at)
        return [remote(target[n], target[n], w_s.at[way, step, n], w_r.at[way, step, n], core_dev) for n in range(2)]

    def start_hops(step):
        for way in range(2):

            @pl.when(hop_goes(step, way))
            def _():
                for copy in hop(step, way):
                    copy.start()

    def await_hops(step):
        for way in range(2):

            @pl.when(hop_comes(step, way))
            def _():
                for copy in hop_arriving(step, way):
                    copy.wait_recv()

    start_hops(0)

    def pair_place(expert):
        return up_vm.at[:, lanes_at(expert % 2 * hidden, hidden)], down_vm.at[aligned(expert % 2 * hidden, hidden), :]

    near = z_at + 1 - 2 * (z_at % 2)
    own_copies = [
        pltpu.make_async_copy((up_ref, down_ref)[n], pair_place(z_at)[n], own_sem.at[n]) for n in range(2)
    ]
    near_copies = [
        pltpu.make_async_copy(slot(near, z_at)[n], pair_place(near)[n], pair_sem.at[n]) for n in range(2)
    ]
    for copy in own_copies:
        copy.start()

    swap = remote(cot_ref, cot_core, c_s.at[0], c_r.at[0], core_dev)
    swap.start()
    kept_all[pl.ds(0, rows), :] = kept_ref[...]

    def kept_half(side, core):
        return kept_all.at[aligned(side * rows + core * half, half), :]

    kept_y = remote(kept_half(0, core_at), kept_half(1, core_at), c_s.at[7], c_r.at[7], y_dev)
    kept_share = remote(kept_half(1, core_at), kept_half(1, core_at), c_s.at[6], c_r.at[6], core_dev)
    kept_share_in = remote(kept_half(1, other), kept_half(1, other), c_s.at[6], c_r.at[6], core_dev)
    kept_y.start()
    swap.wait_recv()

    @pl.when(core_at == 0)
    def _():
        both = jnp.concatenate([cot_ref[...], cot_core[...]], axis=1)
        cot_all[pl.ds(0, rows), lanes_at(x_at * wide, wide)] = both

    @pl.when(core_at == 1)
    def _():
        both = jnp.concatenate([cot_core[...], cot_ref[...]], axis=1)
        cot_all[pl.ds(0, rows), lanes_at(x_at * wide, wide)] = both

    def block(side, col_side, core):
        return cot_all.at[aligned(side * rows + core * half, half), lanes_at(col_side * wide, wide)]

    def cot_copy(number, source, target, device):
        return remote(source, target, c_s.at[number], c_r.at[number], device)

    mine_block = block(0, x_at, core_at)
    cot_x = cot_copy(1, mine_block, mine_block, x_dev)
    cot_y = cot_copy(2, mine_block, block(1, x_at, core_at), y_dev)
    cot_x.start()
    cot_y.start()
    across_x, across_y, across_both = block(0, 1 - x_at, core_at), block(1, x_at, core_at), block(1, 1 - x_at, core_at)
    cot_x_in = cot_copy(1, across_x, across_x, x_dev)
    cot_y_in = cot_copy(2, across_y, across_y, y_dev)
    relay_y = cot_copy(3, across_x, across_both, y_dev)
    relay_x = cot_copy(3, across_y, across_y, x_dev)
    relay_in = cot_copy(3, across_both, across_both, y_dev)
    cot_share = [
        cot_copy(4, across_x, across_x, core_dev),
        cot_copy(5, across_y, across_y, core_dev),
        cot_copy(8, across_both, across_both, core_dev),
    ]
    arriving = [block(0, 1 - x_at, other), block(1, x_at, other), block(1, 1 - x_at, other)]
    cot_share_in = [cot_copy(number, ref, ref, core_dev) for number, ref in zip((4, 5, 8), arriving)]

    lane = lax.broadcasted_iota(jnp.int32, (PITCH, 2 * HD), 1)
    key_mask = lax.broadcasted_iota(jnp.int32, (PITCH, PITCH), 1) < SEQ
    gain1, shift1, gain2, shift2 = (ref[...].reshape(1, 2 * wide) for ref in (gain1_ref, shift1_ref, gain2_ref, shift2_ref))
    my_cols = lanes_at(core_at * wide, wide)
    their_cols = lanes_at(other * wide, wide)

    def attend(image):
        normed, _ = norm_stats(tok_ref[image].astype(f32))
        h_one = (normed * gain1 + shift1).astype(bf16)
        queries = dot(h_one, qkv_ref[0], ((1,), (1,))).astype(bf16)
        keys = dot(h_one, qkv_ref[1], ((1,), (1,))).astype(bf16)
        values = dot(h_one, qkv_ref[2], ((1,), (1,))).astype(bf16)
        q_all[image] = queries
        k_all[image] = keys
        v_all[image] = values
        outs = []
        lse = jnp.zeros((PITCH, 2 * HD), f32)
        for head in range(heads):
            first = head // 2 * 2 * HD
            last = min(first + 2 * HD, heads * HD)
            q_head, k_head, v_head = queries[:, first:last], keys[:, first:last], values[:, first:last]
            if last - first == 2 * HD:
                q_head = jnp.where(head_mask(lane, head), q_head, jnp.zeros_like(q_head))
            scores = dot(q_head, k_head, ((1,), (1,))) * (HD**-0.5)
            scores = jnp.where(key_mask, scores, -1e30)
            peak = jnp.max(scores, axis=1, keepdims=True)
            powers = jnp.exp(scores - peak)
            row_sum = jnp.sum(powers, axis=1, keepdims=True)
            weights = (powers / row_sum).astype(bf16)
            outs.append(dot(weights, v_head))
            lse = jnp.where(lane == head, peak + jnp.log(row_sum), lse)
        lse_all[image] = lse
        joined = []
        for head in range(0, heads, 2):
            if head + 1 < heads:
                joined.append(jnp.where(lane < HD, outs[head], outs[head + 1]))
            else:
                joined.append(outs[head])
        attended = jnp.concatenate(joined, axis=1).astype(bf16)
        att_all[image] = attended
        part[...] = dot(attended, out_w_ref[...])
        mine[image] = part[:, my_cols]
        core_to[image] = part[:, their_cols].astype(bf16)

    def core_copy(image):
        return remote(core_to.at[image], core_from.at[image], core_s.at[image], core_r.at[image], core_dev)

    def x_copy(image):
        return remote(x_to.at[image], x_from.at[image], x_s.at[image], x_r.at[image], x_dev)

    def total_copy(image):
        return remote(total_to.at[image], total_from.at[image], tot_s.at[image], tot_r.at[image], core_dev)

    def h_block(side, image, core):
        return h_all.at[aligned(side * rows + image * PITCH, PITCH), lanes_at(core * wide, wide)]

    def y_copy(image):
        return remote(h_block(0, image, core_at), h_block(1, image, core_at), y_s.at[image], y_r.at[image], y_dev)

    def relay_copy(image):
        ref = h_block(1, image, core_at)
        return remote(ref, ref, rel_s.at[image], rel_r.at[image], core_dev)

    def relay_arriving(image):
        ref = h_block(1, image, other)
        return remote(ref, ref, rel_s.at[image], rel_r.at[image], core_dev)

    attend_outs = ((q_all, q_ref), (k_all, k_ref), (v_all, v_ref), (att_all, att_ref), (lse_all, lse_ref))

    def out_copies(image):
        copies = [
            pltpu.make_async_copy(kept.at[image], out.at[image], out_sem.at[n, image])
            for n, (kept, out) in enumerate(attend_outs)
        ]
        at = aligned(image * PITCH, PITCH)
        return copies, [
            pltpu.make_async_copy(resid_all.at[image], resid_ref.at[at, :], out_sem.at[5, image]),
            pltpu.make_async_copy(h_all.at[at, :], h_out.at[at, :], out_sem.at[6, image]),
        ]

    def other_copy(image):
        at = aligned(rows + image * PITCH, PITCH)
        return pltpu.make_async_copy(h_all.at[at, :], h_out.at[at, :], out_sem.at[7, image])

    def stage(tick, lag, run):
        image = tick - lag

        @pl.when((image >= 0) & (image < images))
        def _():
            run(image)

    def run_attend(image):
        attend(image)
        core_copy(image).start()
        for copy in out_copies(image)[0]:
            copy.start()

    def run_x(image):
        core_copy(image).wait_recv()
        x_to[image] = (mine[image] + core_from[image].astype(f32)).astype(bf16)
        x_copy(image).start()

    def run_total(image):
        x_copy(image).wait_recv()
        total_to[image] = (x_to[image].astype(f32) + x_from[image].astype(f32)).astype(bf16)
        total_copy(image).start()

    def run_norm(image):
        total_copy(image).wait_recv()
        part[:, my_cols] = total_to[image].astype(f32)
        part[:, their_cols] = total_from[image].astype(f32)
        resid = tok_ref[image].astype(f32) + part[...]
        resid_all[image] = resid
        normed, _ = norm_stats(resid)
        h_all[aligned(image * PITCH, PITCH), :] = (normed * gain2 + shift2).astype(bf16)
        y_copy(image).start()
        for copy in out_copies(image)[1]:
            copy.start()

    def run_relay(image):
        y_copy(image).wait_recv()
        relay_copy(image).start()

    def run_end(image):
        relay_arriving(image).wait_recv()
        other_copy(image).start()

    def cot_step_one():
        cot_x_in.wait_recv()
        cot_share[0].start()

        @pl.when(core_at == 0)
        def _():
            relay_y.start()

        kept_y.wait_recv()
        kept_share.start()

    def cot_step_two():
        cot_y_in.wait_recv()
        cot_share[1].start()

        @pl.when(core_at == 1)
        def _():
            relay_x.start()

    def weights_step_one():
        await_hops(0)
        start_hops(1)
        for copy in near_copies:
            copy.start()

    def weights_step_two():
        await_hops(1)
        start_hops(2)

    def cot_step_three():
        relay_in.wait_recv()
        cot_share[2].start()

    outs = [
        pltpu.make_async_copy(cot_all, cot_out, cot_sem.at[0]),
        pltpu.make_async_copy(kept_all, kept_out, cot_sem.at[1]),
    ]

    def ready_own():
        cot_share_in[0].wait_recv()
        for copy in (*own_copies, *near_copies):
            copy.wait()

    def ready_other():
        for copy in (cot_share_in[1], cot_share_in[2], kept_share_in):
            copy.wait_recv()
        for copy in outs:
            copy.start()

    def block_copies(number, place):
        at = aligned(number * BLOCK, BLOCK)
        pairs = ((mixed_slots, mixed_out), (grad_h_slots, grad_h_out), (gate_slots, gate_out))
        return [
            pltpu.make_async_copy(slots.at[place], out.at[at, :], block_sem.at[n, place])
            for n, (slots, out) in enumerate(pairs)
        ]

    def run_block(number, turn):
        at = aligned(number * BLOCK, BLOCK)
        h_rows, cot_rows = h_all[at, :], cot_all[at, :]
        up, down = up_vm[...], down_vm[...]
        hidden_rows, grad_pre, _, grad_gate = expert_math(
            h_rows, cot_rows, kept_all[at, :].astype(f32), router_ref[...], up, down, z_at // 2, experts
        )

        place = turn % 2

        @pl.when(turn >= 2)
        def _():
            for copy in block_copies(number, place):
                copy.wait()

        gate_slots[place] = grad_gate
        mixed_slots[place] = dot(hidden_rows, down).astype(bf16)
        grad_h_slots[place] = dot(grad_pre, up, ((1,), (1,))).astype(bf16)
        for copy in block_copies(number, place):
            copy.start()
        up_sum[...] += dot(h_rows.T, grad_pre)
        down_sum[...] += dot(cot_rows.T, hidden_rows)

    up_sum[...] = jnp.zeros_like(up_sum)
    down_sum[...] = jnp.zeros_like(down_sum)

    def first_ticks(tick, _):
        stage(tick, 0, run_attend)
        stage(tick, 1, run_x)
        return 0

    lax.fori_loop(0, images + 1, first_ticks, 0)
    pairs = images // 2

    def both(first, *runs):
        for run in runs:
            run(first)
            run(first + 1)

    cot_step_one()
    both(0, run_total, run_norm)
    cot_step_two()
    weights_step_one()
    ready_own()

    def per_turn(turn, _):
        @pl.when((turn <= 1) | (turn == 3))
        def _():
            both(jnp.where(turn == 3, 6, 2 * turn + 2), run_total, run_norm)

        @pl.when((turn >= 2) & (turn < pairs + 2))
        def _():
            both(2 * turn - 4, run_relay)

        @pl.when(turn == pairs)
        def _():
            weights_step_two()
            cot_step_three()
            ready_other()

        @pl.when(turn >= pairs)
        def _():
            both(2 * (turn - pairs), run_end)

        run_block(turn, turn)
        return 0

    lax.fori_loop(0, 2 * pairs, per_turn, 0)
    grad_up_vm[...] = up_sum[...].astype(bf16)
    grad_down_vm[...] = down_sum[...].astype(bf16)
    grad_copies = [
        pltpu.make_async_copy(grad_up_vm, grad_up_out, grad_sem.at[0]),
        pltpu.make_async_copy(grad_down_vm, grad_down_out, grad_sem.at[1]),
    ]
    for copy in grad_copies:
        copy.start()
    for copy in (swap, kept_y, kept_share, cot_x, cot_y, *cot_share):
        copy.wait_send()

    @pl.when(core_at == 0)
    def _():
        relay_y.wait_send()

    @pl.when(core_at == 1)
    def _():
        relay_x.wait_send()

    def drain(image, _):
        for copy in (core_copy, x_copy, total_copy, y_copy, relay_copy):
            copy(image).wait_send()
        first, second = out_copies(image)
        for copy in (*first, *second, other_copy(image)):
            copy.wait()
        return 0

    lax.fori_loop(0, images, drain, 0)
    for place in range(2):
        for copy in block_copies(0, place):
            copy.wait()

    await_hops(2)
    for step in range(3):
        for way in range(2):

            @pl.when(hop_goes(step, way))
            def _():
                for copy in hop(step, way):
                    copy.wait_send()

    for copy in (*grad_copies, *outs):
        copy.wait()


def run_forward(tok, gain1, shift1, gain2, shift2, qkv_w, out_w, up, down, cot, kept, router, experts):
    images = tok.shape[0]
    rows = images * PITCH
    features = tok.shape[2]
    share = out_w.shape[0]
    heads = share // HD
    hidden = up.shape[1]
    wide = features // 2
    vmem = pl.BlockSpec(memory_space=pltpu.VMEM)
    anywhere = pl.BlockSpec(memory_space=pl.ANY)
    shape = jax.ShapeDtypeStruct
    block = (images, PITCH, wide)
    dma = pltpu.SemaphoreType.DMA
    return pl.pallas_call(
        partial(forward_kernel, images=images, heads=heads, experts=experts),
        out_shape=[
            shape((images, PITCH, share), bf16),
            shape((images, PITCH, share), bf16),
            shape((images, PITCH, share), bf16),
            shape((images, PITCH, share), bf16),
            shape((images, PITCH, 128), f32),
            shape((rows, features), f32),
            shape((2 * rows, features), bf16),
            shape((2 * rows, features), bf16),
            shape((2 * rows, 128), bf16),
            shape((2, features, 2 * hidden), bf16),
            shape((2, 2 * hidden, features), bf16),
            shape((2 * rows, features), bf16),
            shape((2 * rows, features), bf16),
            shape((2 * rows, 128), f32),
            shape((features, 2 * hidden), bf16),
            shape((features, 2 * hidden), bf16),
        ],
        in_specs=[vmem] * 7 + [anywhere] * 2 + [vmem] * 3,
        out_specs=[anywhere] * 16,
        scratch_shapes=[
            pltpu.VMEM((features, 2 * hidden), bf16),
            pltpu.VMEM((2 * hidden, features), bf16),
            *[pltpu.VMEM((features, 2 * hidden), f32)] * 2,
            *[pltpu.VMEM((2, BLOCK, features), bf16)] * 2,
            pltpu.VMEM((2, BLOCK, 128), f32),
            *[pltpu.VMEM((features, 2 * hidden), bf16)] * 2,
            *[pltpu.VMEM((images, PITCH, share), bf16)] * 4,
            pltpu.VMEM((images, PITCH, 128), f32),
            pltpu.VMEM((images, PITCH, features), f32),
            pltpu.VMEM((2 * rows, features), bf16),
            pltpu.VMEM((2 * rows, features), bf16),
            pltpu.VMEM((2 * rows, 128), bf16),
            pltpu.VMEM((PITCH, features), f32),
            pltpu.VMEM(block, f32),
            pltpu.VMEM(block, bf16),
            pltpu.VMEM(block, bf16),
            pltpu.VMEM(block, bf16),
            pltpu.VMEM(block, bf16),
            pltpu.VMEM(block, bf16),
            pltpu.VMEM(block, bf16),
            pltpu.VMEM((rows, share), bf16),
        ]
        + [dma((images,))] * 10
        + [dma((2, 3, 2))] * 2
        + [dma((9,))] * 2
        + [dma((2,)), dma((2,)), dma((3, 2)), dma((2,)), dma((2,)), dma((8, images))],
        compiler_params=pltpu.CompilerParams(
            collective_id=1, has_side_effects=True, vmem_limit_bytes=63 << 20
        ),
    )(tok, gain1, shift1, gain2, shift2, qkv_w, out_w, up, down, cot, kept, router)


def turn_is_other(turn):
    return (turn == 0) | ((turn % 2 == 1) & (turn < 7))


def turn_block(turn):
    own = jnp.where(turn == 7, 3, turn // 2 - 1)
    return jnp.where(turn_is_other(turn), 4 + (turn + 1) // 2, own)


def second_pair_kernel(
    h_ref,
    cot_ref,
    kept_ref,
    router_ref,
    mixed_first,
    grad_h_first,
    gate_first,
    up_all,
    down_all,
    up_first,
    down_first,
    mixed_ref,
    grad_up_ref,
    grad_down_ref,
    grad_router_ref,
    grad_h_out,
    up_pair,
    down_pair,
    line_first,
    up_vm,
    down_vm,
    up_sum,
    down_sum,
    router_sum,
    ring,
    from_core,
    from_y,
    from_x,
    load,
    core_s,
    core_r,
    y_s,
    y_r,
    x_s,
    x_r,
    tot_s,
    tot_r,
    store,
    pair_s,
    pair_r,
    line_s,
    line_r,
    *,
    experts,
    steps,
):
    turn = pl.program_id(0)
    expert_at = lax.axis_index("expert")
    tensor_at = lax.axis_index("tensor")
    z_at, y_at = expert_at // 2, expert_at % 2
    x_at, core_at = tensor_at // 2, tensor_at % 2
    hidden = up_pair.shape[1]
    wide = ring.shape[2] // 2
    core_dev = (expert_at, tensor_at + 1 - 2 * core_at)
    x_dev = (expert_at, tensor_at + 2 - 4 * x_at)
    y_dev = (expert_at + 1 - 2 * y_at, tensor_at)
    my_cols = lanes_at(core_at * wide, wide)
    their_cols = lanes_at((1 - core_at) * wide, wide)

    def remote(src, dst, send, recv, device):
        return pltpu.make_async_remote_copy(
            src_ref=src, dst_ref=dst, send_sem=send, recv_sem=recv, device_id=device, device_id_type=MESH
        )

    def core_copy(number):
        return remote(ring.at[number % 2, :, their_cols], from_core.at[number], core_s.at[number], core_r.at[number], core_dev)

    def y_copy(number, place):
        return remote(from_core.at[number], from_y.at[place], y_s.at[place], y_r.at[place], y_dev)

    def x_copy(number, place):
        return remote(from_core.at[number], from_x.at[place], x_s.at[place], x_r.at[place], x_dev)

    def out_rows(place):
        return grad_h_out.at[aligned(place * BLOCK, BLOCK), my_cols]

    def total_copy(place):
        return remote(from_x.at[place], out_rows(place), tot_s.at[place], tot_r.at[place], core_dev)

    def store_copy(place):
        return pltpu.make_async_copy(from_x.at[place], out_rows(place), store.at[place])

    def own_turn(place):
        return jnp.where(place == 3, 7, 2 * place + 2)

    def other_turn(place):
        return jnp.where(place == 0, 0, 2 * place - 1)

    def pass_other(number):
        core_copy(number).wait_recv()
        total = from_core[number].astype(f32) + ring[number % 2, :, my_cols].astype(f32)
        from_core[number] = total.astype(bf16)
        y_copy(number, (number + 1) // 2).start()

    def pass_own(number, place):
        core_copy(number).wait_recv()
        y_copy(number, place).wait_recv()
        total = from_core[number].astype(f32) + ring[number % 2, :, my_cols].astype(f32) + from_y[place].astype(f32)
        from_core[number] = total.astype(bf16)
        x_copy(number, place).start()

    def pass_total(place):
        number = own_turn(place)
        x_copy(number, place).wait_recv()
        from_x[place] = (from_core[number].astype(f32) + from_x[place].astype(f32)).astype(bf16)
        total_copy(place).start()
        store_copy(place).start()

    z_dev = (jnp.where(z_at % 2 == 0, expert_at + 2, expert_at - 2), tensor_at)
    pair_lanes = lanes_at((1 - z_at % 2) * hidden, hidden)
    pair_copies = [
        remote(source.at[:, pair_lanes], target, pair_s.at[number], pair_r.at[number], z_dev)
        for number, (source, target) in enumerate(((up_first, up_pair), (down_first, down_pair)))
    ]

    far_lanes = lanes_at(jnp.where(z_at == 0, 1, 0) * hidden, hidden)
    line_copy = remote(grad_up_ref.at[:, far_lanes], line_first, line_s.at[0], line_r.at[0], z_dev)
    is_outer = (z_at == 0) | (z_at == lax.axis_size("expert") // 2 - 1)

    @pl.when(turn == 0)
    def _():
        greet([(True, core_dev), (True, x_dev), (True, y_dev), (True, z_dev)])
        for copy in pair_copies:
            copy.start()
        whole = [
            pltpu.make_async_copy(up_all.at[1], up_vm, load.at[0]),
            pltpu.make_async_copy(down_all.at[1], down_vm, load.at[1]),
        ]
        for copy in whole:
            copy.start()
        up_sum[...] = jnp.zeros_like(up_sum)
        down_sum[...] = jnp.zeros_like(down_sum)
        router_sum[...] = jnp.zeros_like(router_sum)
        for copy in whole:
            copy.wait()

    h_rows, cot_rows = h_ref[...], cot_ref[...]
    up, down, router = up_vm[...], down_vm[...], router_ref[...]
    kept = kept_ref[...].astype(f32)
    hidden_rows, grad_pre, probs, grad_gate = expert_math(
        h_rows, cot_rows, kept, router, up, down, 1 - z_at // 2, experts
    )
    grad_gate = kept * (grad_gate + gate_first[...])
    grad_logits = (probs * (grad_gate - jnp.sum(probs * grad_gate, axis=1, keepdims=True))).astype(bf16)

    before = turn - 1

    @pl.when((turn >= 1) & turn_is_other(before))
    def _():
        pass_other(before)

    @pl.when((turn == 5) | (turn == 7))
    def _():
        pass_total((turn - 5) // 2)

    @pl.when((turn == 3) | (turn == 5) | (turn == 7))
    def _():
        pass_own(before, (turn - 3) // 2)


    @pl.when(turn >= 2)
    def _():
        core_copy(turn - 2).wait_send()

    ring[turn % 2] = (
        grad_h_first[...].astype(f32) + dot(grad_pre, up, ((1,), (1,))) + dot(grad_logits, router, ((1,), (1,)))
    ).astype(bf16)
    core_copy(turn).start()
    mixed_ref[...] = (mixed_first[...].astype(f32) + dot(hidden_rows, down)).astype(bf16)
    h_turned = h_rows.T
    up_sum[...] += dot(h_turned, grad_pre)
    router_sum[...] += dot(h_turned, grad_logits)
    down_sum[...] += dot(cot_rows.T, hidden_rows)

    @pl.when(turn == steps - 1)
    def _():
        grad_up_ref[...] = up_sum[...].astype(bf16)

        @pl.when(is_outer)
        def _():
            line_copy.start()

        pass_own(7, 3)
        pass_total(2)
        grad_down_ref[...] = down_sum[...].astype(bf16)
        grad_router_ref[...] = router_sum[...].T[:8]
        pass_total(3)
        for copy in pair_copies:
            copy.wait()

        @pl.when(is_outer)
        def _():
            line_copy.wait_send()

        @pl.when(jnp.logical_not(is_outer))
        def _():
            line_copy.wait_recv()

        for number in (6, 7):
            core_copy(number).wait_send()
        for place in range(4):
            y_copy(other_turn(place), place).wait_send()
            x_copy(own_turn(place), place).wait_send()
            total_copy(place).wait_send()
            total_copy(place).wait_recv()
            store_copy(place).wait()


def run_second_pair(
    h_rows,
    cot_rows,
    kept,
    router,
    mixed_first,
    grad_h_first,
    gate_first,
    up,
    down,
    up_first,
    down_first,
    experts,
):
    rows, features = h_rows.shape
    width = up.shape[2]
    steps = rows // BLOCK
    half = (BLOCK, features // 2)
    anywhere = pl.BlockSpec(memory_space=pl.ANY)
    shape = jax.ShapeDtypeStruct
    dma = pltpu.SemaphoreType.DMA

    def by_step(lanes):
        return pl.BlockSpec((BLOCK, lanes), lambda n: (turn_block(n), 0))

    def whole(*dims):
        return pl.BlockSpec(dims, lambda n: (0,) * len(dims))

    return pl.pallas_call(
        partial(second_pair_kernel, experts=experts, steps=steps),
        grid=(steps,),
        out_shape=[
            shape((rows, features), bf16),
            shape((features, width), bf16),
            shape((features, width), bf16),
            shape((8, features), f32),
            shape((rows // 2, features), bf16),
            shape((features, width // 2), bf16),
            shape((features, width // 2), bf16),
            shape((features, width // 2), bf16),
        ],
        in_specs=[
            by_step(features),
            by_step(features),
            by_step(128),
            whole(features, 128),
            by_step(features),
            by_step(features),
            by_step(128),
        ]
        + [anywhere] * 4,
        out_specs=[by_step(features), whole(features, width), whole(features, width), whole(8, features)] + [anywhere] * 4,
        scratch_shapes=[
            pltpu.VMEM((features, width), bf16),
            pltpu.VMEM((width, features), bf16),
            pltpu.VMEM((features, width), f32),
            pltpu.VMEM((features, width), f32),
            pltpu.VMEM((features, 128), f32),
            pltpu.VMEM((2, BLOCK, features), bf16),
            pltpu.VMEM((8, *half), bf16),
            pltpu.VMEM((4, *half), bf16),
            pltpu.VMEM((4, *half), bf16),
            dma((2,)),
        ]
        + [dma((8,))] * 2
        + [dma((4,))] * 7
        + [dma((2,))] * 2
        + [dma((1,))] * 2,
        compiler_params=pltpu.CompilerParams(
            collective_id=4, has_side_effects=True, vmem_limit_bytes=60 << 20
        ),
    )(h_rows, cot_rows, kept, router, mixed_first, grad_h_first, gate_first, up, down, up_first, down_first)


def backward_kernel(
    gain1_ref,
    shift1_ref,
    gain2_ref,
    qkv_ref,
    out_w_ref,
    grad_router_ref,
    tok_hbm,
    q_hbm,
    k_hbm,
    v_hbm,
    att_hbm,
    lse_hbm,
    grad_h_hbm,
    resid_ref,
    cot_ref,
    mixed_ref,
    up_first,
    down_first,
    up_pair,
    down_pair,
    up_second,
    down_second,
    line_first,
    up_out,
    down_out,
    tokens_out,
    qkv_out,
    out_w_out,
    sums_out,
    mixed_out,
    tok_ref,
    q_ref,
    k_ref,
    v_ref,
    att_ref,
    lse_ref,
    grad_h_ref,
    rows_kept,
    cot_rows,
    m_mine,
    m_core,
    m_y,
    m_x,
    m_out,
    m_resid,
    own_vm,
    pair_vm,
    far_vm,
    one_mine,
    one_to,
    one_core,
    one_x,
    one_total,
    line,
    weight_sum,
    weight_half,
    shared,
    shared_y,
    shared_line,
    shared_all,
    route_core,
    route_x,
    late_mine,
    late_y,
    late_z,
    up_total,
    down_total,
    sums_all,
    whole,
    mc_s,
    mc_r,
    my_s,
    my_r,
    mx_s,
    mx_r,
    mq_s,
    mq_r,
    m_store,
    oc_s,
    oc_r,
    ox_s,
    ox_r,
    ot_s,
    ot_r,
    l_s,
    l_r,
    sy_s,
    sy_r,
    sl_s,
    sl_r,
    sg_s,
    sg_r,
    sz_s,
    sz_r,
    r_s,
    r_r,
    late_s,
    late_r,
    load,
    image_load,
    own_sem,
    weight_store,
    store,
    *,
    images,
    heads,
):
    expert_at = lax.axis_index("expert")
    tensor_at = lax.axis_index("tensor")
    z_at, y_at = expert_at // 2, expert_at % 2
    z_last = lax.axis_size("expert") // 2 - 1
    x_at, core_at = tensor_at // 2, tensor_at % 2
    other = 1 - core_at
    rows = images * PITCH
    features = tok_hbm.shape[2]
    wide = features // 2
    share = out_w_ref.shape[0]
    hidden = line.shape[3]
    core_dev = (expert_at, tensor_at + 1 - 2 * core_at)
    x_dev = (expert_at, tensor_at + 2 - 4 * x_at)
    y_dev = (expert_at + 1 - 2 * y_at, tensor_at)
    z_devs = [(expert_at + 2, tensor_at), (expert_at - 2, tensor_at)]
    planes = z_last + 1
    z_others = [((z_at + hop) % planes * 2 + y_at, tensor_at) for hop in (1, 2, 3)]
    greet([(True, device) for device in (core_dev, x_dev, y_dev, *z_others)])
    my_cols = lanes_at(core_at * wide, wide)
    their_cols = lanes_at(other * wide, wide)

    def remote(src, dst, send, recv, device):
        return pltpu.make_async_remote_copy(
            src_ref=src, dst_ref=dst, send_sem=send, recv_sem=recv, device_id=device, device_id_type=MESH
        )

    def at_image(image):
        return aligned(image * PITCH, PITCH)

    part_count = m_y.shape[0]
    part_rows_m = rows // part_count

    def m_rows(side, part):
        return aligned(side * rows + part * part_rows_m, part_rows_m)

    def m_core_copy(side, part):
        at = m_rows(side, part)
        return remote(mixed_ref.at[at, their_cols], m_core.at[at, :], mc_s.at[side, part], mc_r.at[side, part], core_dev)

    for part in range(part_count):
        m_core_copy(1, part).start()
    for part in range(part_count):
        m_core_copy(0, part).start()
    m_loads = [
        pltpu.make_async_copy(mixed_ref.at[pl.ds(side * rows, rows), my_cols], m_mine.at[pl.ds(side * rows, rows), :], load.at[side])
        for side in range(2)
    ]

    def image_loads(image):
        at = at_image(image)
        by_image = ((tok_hbm, tok_ref), (q_hbm, q_ref), (k_hbm, k_ref), (v_hbm, v_ref), (att_hbm, att_ref), (lse_hbm, lse_ref))
        by_row = ((grad_h_hbm, grad_h_ref), (resid_ref, rows_kept), (cot_ref, cot_rows))
        pairs = [(source.at[image], target.at[image]) for source, target in by_image]
        pairs += [(source.at[at, :], target.at[at, :]) for source, target in by_row]
        return [pltpu.make_async_copy(source, target, image_load.at[n, image]) for n, (source, target) in enumerate(pairs)]

    def start_loads(image, _):
        for copy in image_loads(image):
            copy.start()
        return 0

    start_loads(0, 0)
    m_loads[1].start()
    lax.fori_loop(1, images, start_loads, 0)
    m_loads[0].start()
    route_one = remote(grad_router_ref, route_core, r_s.at[0], r_r.at[0], core_dev)
    route_one.start()

    def place(way):
        return z_at if way == 0 else z_last - z_at

    def far_lanes(way, piece):
        expert = z_last - piece // 2 if way == 0 else piece // 2
        return pl.ds(expert % 2 * hidden, hidden)

    def line_copy(source, way, piece):
        return remote(source, line.at[way, piece], l_s.at[way, piece], l_r.at[way, piece], z_devs[way])

    def line_copy_on(way, piece):
        return line_copy(line.at[way, piece], way, piece)

    def line_start():
        for way in range(2):

            @pl.when(place(way) == 0)
            def _():
                for piece in range(1, 4):
                    source = (up_second, down_second)[piece % 2]
                    line_copy(source.at[:, far_lanes(way, piece)], way, piece).start()

    def line_add(piece):
        for way in range(2):

            @pl.when(place(way) == 1)
            def _():
                if piece > 0:
                    line_copy_on(way, piece).wait_recv()
                lanes = far_lanes(way, piece)

                def add(part, _):
                    at_rows = aligned(part * 96, 96)
                    total = line[way, piece, at_rows, :].astype(f32) + far_vm[piece % 2, at_rows, lanes].astype(f32)
                    line[way, piece, at_rows, :] = total.astype(bf16)
                    return 0

                lax.fori_loop(0, features // 96, add, 0)
                line_copy_on(way, piece).start()

    def line_pass(piece):
        for way in range(2):

            @pl.when(place(way) == 2)
            def _():
                line_copy_on(way, piece).wait_recv()
                line_copy_on(way, piece).start()

    line_start()
    own_lanes = lanes_at(z_at % 2 * hidden, hidden)
    later = [
        pltpu.make_async_copy(source, target, own_sem.at[number])
        for number, (source, target) in enumerate(
            (
                (up_second, far_vm.at[0]),
                (down_second, far_vm.at[1]),
                (up_first.at[:, own_lanes], own_vm.at[0]),
                (down_first.at[:, own_lanes], own_vm.at[1]),
                (up_pair, pair_vm.at[0]),
                (down_pair, pair_vm.at[1]),
            )
        )
    ]
    is_inner = (z_at == 1) | (z_at == z_last - 1)
    first_copy = pltpu.make_async_copy(line_first, line.at[jnp.where(z_at == 1, 0, 1), 0], own_sem.at[6])

    @pl.when(is_inner)
    def _():
        first_copy.start()

    for copy in later:
        copy.start()
    weight_sum[...] = jnp.zeros_like(weight_sum)
    late_mine[...] = jnp.zeros_like(late_mine)

    def m_y_copy(part):
        return remote(m_core.at[m_rows(1, part), :], m_y.at[part], my_s.at[part], my_r.at[part], y_dev)

    def m_x_copy(part):
        return remote(m_core.at[m_rows(0, part), :], m_x.at[part], mx_s.at[part], mx_r.at[part], x_dev)

    def m_place(part):
        return mixed_out.at[aligned(part * part_rows_m, part_rows_m), :]

    def m_quarter_copy(part):
        return remote(m_out.at[part, other], m_place(part), mq_s.at[part], mq_r.at[part], core_dev)

    def m_store_copy(part):
        return pltpu.make_async_copy(m_out.at[part, core_at], m_place(part), m_store.at[part])

    def m_resid_copy(part):
        at = aligned(part * part_rows_m, part_rows_m)
        return pltpu.make_async_copy(resid_ref.at[at, lanes_at(x_at * wide, wide)], m_resid, load.at[3])

    keeps = x_at == core_at

    def run_m_y(part):
        m_core_copy(1, part).wait_recv()
        at = m_rows(1, part)
        m_core[at, :] = (m_core[at, :].astype(f32) + m_mine[at, :].astype(f32)).astype(bf16)
        m_y_copy(part).start()

    def run_m_x(part):
        if isinstance(part, int) and part == 0:
            m_loads[0].wait()
        m_core_copy(0, part).wait_recv()
        m_y_copy(part).wait_recv()
        at = m_rows(0, part)
        total = m_core[at, :].astype(f32) + m_mine[at, :].astype(f32) + m_y[part].astype(f32)
        m_core[at, :] = total.astype(bf16)

        @pl.when(jnp.logical_not(keeps))
        def _():
            m_x_copy(part).start()

    def run_m_out(part):
        @pl.when(keeps)
        def _():
            m_resid_copy(part).start()
            m_x_copy(part).wait_recv()
            m_resid_copy(part).wait()
            total = m_core[m_rows(0, part), :].astype(f32) + m_x[part].astype(f32)
            mixed = (m_resid[...] + total).astype(bf16)
            m_out[part, 0] = mixed[:, : wide // 2]
            m_out[part, 1] = mixed[:, wide // 2 :]
            m_quarter_copy(part).start()
            m_store_copy(part).start()

    m_loads[1].wait()
    for part in range(part_count):
        run_m_y(part)
    later[0].wait()
    later[1].wait()

    @pl.when(is_inner)
    def _():
        first_copy.wait()

    line_add(0)
    route_one.wait_recv()
    route_core[...] += grad_router_ref[...]
    route_two = remote(route_core, route_x, r_s.at[1], r_r.at[1], x_dev)
    route_two.start()

    def one_core_copy(image):
        return remote(one_to.at[image], one_core.at[image], oc_s.at[image], oc_r.at[image], core_dev)

    def one_x_copy(image):
        return remote(one_core.at[image], one_x.at[image], ox_s.at[image], ox_r.at[image], x_dev)

    def one_total_copy(image):
        return remote(one_x.at[image], one_total.at[image], ot_s.at[image], ot_r.at[image], core_dev)

    store_copy = pltpu.make_async_copy(rows_kept.at[pl.ds(0, images * SEQ), :], tokens_out, store.at[0])

    lane = lax.broadcasted_iota(jnp.int32, (PITCH, 2 * HD), 1)
    key_mask = lax.broadcasted_iota(jnp.int32, (PITCH, PITCH), 1) < SEQ
    gain1, shift1, gain2 = (ref[...].reshape(1, features) for ref in (gain1_ref, shift1_ref, gain2_ref))

    def norm_back(grad, gain, normed, inverse):
        scaled = grad * gain
        mean = jnp.mean(scaled, axis=1, keepdims=True)
        along = jnp.mean(scaled * normed, axis=1, keepdims=True)
        return (scaled - mean - normed * along) * inverse

    def add_sums(sums, row, grad, normed):
        sums[row : row + 1, :] += jnp.sum(grad * normed, axis=0, keepdims=True)
        sums[row + 1 : row + 2, :] += jnp.sum(grad, axis=0, keepdims=True)

    def run_attention(image):
        for copy in image_loads(image):
            copy.wait()
        at = at_image(image)
        grad_h = grad_h_ref[at, :].astype(f32)
        normed, inverse = norm_stats(rows_kept[at, :])
        add_sums(late_mine, 2, grad_h, normed)
        grad_resid = cot_rows[at, :].astype(f32) + norm_back(grad_h, gain2, normed, inverse)
        rows_kept[at, :] = grad_resid
        grad_branch = grad_resid.astype(bf16)
        token_normed, _ = norm_stats(tok_ref[image].astype(f32))
        h_one = (token_normed * gain1 + shift1).astype(bf16)
        queries, keys, values, attended = q_ref[image], k_ref[image], v_ref[image], att_ref[image]
        lse = lse_ref[image]
        grad_attended = dot(grad_branch, out_w_ref[...], ((1,), (1,))).astype(bf16)
        grads = [[], [], []]
        for head in range(heads):
            first = head // 2 * 2 * HD
            last = min(first + 2 * HD, heads * HD)
            parts = [whose[:, first:last] for whose in (queries, keys, values, grad_attended)]
            if last - first == 2 * HD:
                own = head_mask(lane, head)
                q_own, k_own, _, g_own = (jnp.where(own, part, jnp.zeros_like(part)) for part in parts)
            else:
                q_own, k_own, _, g_own = parts
            scores = dot(q_own, parts[1], ((1,), (1,))) * (HD**-0.5)
            probs = jnp.where(key_mask, jnp.exp(scores - lse[:, head : head + 1]), 0.0)
            back = dot(g_own, parts[2], ((1,), (1,)))
            product = probs * back
            grad_scores = (product - probs * jnp.sum(product, axis=1, keepdims=True)).astype(bf16)
            pieces = (
                dot(grad_scores, k_own) * (HD**-0.5),
                dot(grad_scores, q_own, ((0,), (0,))) * (HD**-0.5),
                dot(probs.astype(bf16), g_own, ((0,), (0,))),
            )
            for which in range(3):
                if head % 2 == 0:
                    grads[which].append(pieces[which])
                else:
                    grads[which][-1] += pieces[which]
        grad_rows = [jnp.concatenate(grads[which], axis=1).astype(bf16) for which in range(3)]
        grad_one = 0.0
        for which in range(3):
            weight_sum[which * share : (which + 1) * share, :] += dot(grad_rows[which].T, h_one)
            grad_one += dot(grad_rows[which], qkv_ref[which])
        weight_sum[3 * share : 4 * share, :] += dot(attended.T, grad_branch)
        whole[...] = grad_one
        one_mine[image] = whole[:, my_cols].astype(bf16)
        one_to[image] = whole[:, their_cols].astype(bf16)
        one_core_copy(image).start()

    def run_one_x(image):
        one_core_copy(image).wait_recv()
        one_core[image] = (one_core[image].astype(f32) + one_mine[image].astype(f32)).astype(bf16)
        one_x_copy(image).start()

    def run_one_total(image):
        one_x_copy(image).wait_recv()
        one_x[image] = (one_core[image].astype(f32) + one_x[image].astype(f32)).astype(bf16)
        one_total_copy(image).start()

    def run_tokens(image):
        one_total_copy(image).wait_recv()
        whole[:, my_cols] = one_x[image].astype(f32)
        whole[:, their_cols] = one_total[image].astype(f32)
        grad_one = whole[...]
        at = at_image(image)
        normed, inverse = norm_stats(tok_ref[image].astype(f32))
        add_sums(late_mine, 0, grad_one, normed)
        total = rows_kept[at, :] + norm_back(grad_one, gain1, normed, inverse)
        whole[...] = total
        for number in range(images):

            @pl.when(image == number)
            def _():
                rows_kept[pl.ds(number * SEQ, SEQ), :] = whole[pl.ds(0, SEQ), :]


    def stage(tick, lag, run):
        image = tick - lag

        @pl.when((image >= 0) & (image < images))
        def _():
            run(image)

    def at_tick(tick, when, run):
        @pl.when(tick == when)
        def _():
            run()

    def line_second():
        line_add(1)
        line_pass(0)

    def line_third():
        line_add(2)
        line_pass(1)

    def per_tick(tick, _):
        stage(tick, 0, run_attention)
        stage(tick, 1, run_one_x)
        stage(tick, 4, run_one_total)
        stage(tick, 5, run_tokens)
        at_tick(tick, 5, lambda: run_m_x(0))
        at_tick(tick, 3, line_second)
        at_tick(tick, 6, line_third)
        at_tick(tick, 7, lambda: run_m_x(1))
        return 0

    lax.fori_loop(0, images, per_tick, 0)

    part_rows = shared.shape[1]
    quarter = part_rows // (z_last + 1)

    def to_half(side):
        def cast(piece, _):
            at_rows = aligned(piece * quarter, quarter)
            shared[side, at_rows, :] = weight_sum[aligned(side * part_rows + piece * quarter, quarter), :].astype(bf16)
            return 0

        lax.fori_loop(0, z_last + 1, cast, 0)

    to_half(0)
    to_half(1)

    def y_piece(number):
        inner = jnp.where(z_at == 1, jnp.where(number < 2, z_last - number, number - 2), jnp.where(number < 2, number, 5 - number))
        return jnp.where(z_at == 0, z_last - number, jnp.where(z_at == z_last, number, inner))

    def quarter_at(piece):
        return aligned(piece * quarter, quarter)

    def shared_y_copy(number):
        at_rows = quarter_at(y_piece(number))
        return remote(shared.at[1 - y_at, at_rows, :], shared_y.at[at_rows, :], sy_s.at[number], sy_r.at[number], y_dev)

    def take_y(number):
        shared_y_copy(number).wait_recv()
        at_rows = quarter_at(y_piece(number))
        weight_half[at_rows, :] = shared[y_at, at_rows, :].astype(f32) + shared_y[at_rows, :].astype(f32)

    for number in range(4):
        shared_y_copy(number).start()
    run_one_x(images - 1)
    run_m_x(part_count - 2)
    run_one_total(images - 4)
    run_tokens(images - 5)
    line_add(3)

    def quarter_of(step, at, way):
        mirrored = z_last - step + at
        return mirrored if way == 0 else z_last - mirrored

    late_y_copy = remote(late_mine, late_y, late_s.at[0], late_r.at[0], y_dev)

    def late_copy(number):
        ref = late_z.at[z_at]
        return remote(ref, ref, late_s.at[number + 1], late_r.at[number + 1], z_others[number])

    def small_copy(step, way):
        return remote(shared_line.at[way, 0, step], shared_line.at[way, 1, step], sl_s.at[way, step], sl_r.at[way, step], z_devs[way])

    for step in range(3):
        take_y(step)
        if step == 2:
            take_y(3)
        for way in range(2):
            at = place(way)

            @pl.when((at <= step) & (at < z_last))
            def _():
                at_rows = quarter_at(quarter_of(step, at, way))
                if step == 0:
                    shared_line[way, 0, step] = weight_half[at_rows, :].astype(bf16)
                else:
                    came = jnp.where(at > 0, shared_line[way, 1, step - 1].astype(f32), 0.0)
                    shared_line[way, 0, step] = (weight_half[at_rows, :] + came).astype(bf16)
                small_copy(step, way).start()

        for way in range(2):
            at = place(way)

            @pl.when((at > 0) & (at - 1 <= step))
            def _():
                small_copy(step, way).wait_recv()

        if step == 0:
            run_m_x(part_count - 1)
            run_one_total(images - 3)
            run_tokens(images - 4)
            run_m_out(0)
        if step == 1:
            run_one_total(images - 2)
            run_tokens(images - 3)
            run_m_out(1)

    own_rows = quarter_at(z_at)
    from_below = jnp.where(z_at > 0, shared_line[0, 1, 2].astype(f32), 0.0)
    from_above = jnp.where(z_at < z_last, shared_line[1, 1, 2].astype(f32), 0.0)

    def final_rows(side, piece):
        return shared_all.at[side, quarter_at(piece), :]

    shared_all[y_at, own_rows, :] = (weight_half[own_rows, :] + from_below + from_above).astype(bf16)
    for number in range(4):
        shared_y_copy(number).wait_send()

    def gather_z(step, way, piece):
        ref = final_rows(y_at, piece)
        return remote(ref, ref, sg_s.at[way, step], sg_r.at[way, step], z_devs[way])

    def gather_y(step, way, piece, side):
        ref = final_rows(side, piece)
        return remote(ref, ref, sz_s.at[way, step], sz_r.at[way, step], y_dev)

    gather_y(0, 0, z_at, y_at).start()

    def between(step):
        if step == 0:
            run_one_total(images - 1)
            run_tokens(images - 2)
        if step == 1:
            run_tokens(images - 1)
            route_two.wait_recv()
            late_mine[8:16, :] = route_core[...] + route_x[...]
            late_y_copy.start()
            store_copy.start()
            run_m_out(part_count - 2)
        if step == 2:
            run_m_out(part_count - 1)
            late_y_copy.wait_recv()
            late_z[z_at] = late_mine[...] + late_y[...]
            for number in range(planes - 1):
                late_copy(number).start()

    for step in range(3):
        for way in range(2):
            at = place(way)
            piece = z_at - step if way == 0 else z_at + step

            @pl.when((at >= step) & (at < z_last))
            def _():
                gather_z(step, way, piece).start()

        between(step)
        for way in range(2):
            at = place(way)
            piece = z_at - 1 - step if way == 0 else z_at + 1 + step

            @pl.when(at >= 1 + step)
            def _():
                gather_z(step, way, piece).wait_recv()
                gather_y(step + 1, way, piece, y_at).start()

    for copy in later[2:]:
        copy.wait()
    for way in range(2):

        @pl.when(place(way) == 2)
        def _():
            line_copy_on(way, 2).wait_recv()
            line_copy_on(way, 3).wait_recv()

        @pl.when(place(way) == z_last)
        def _():
            line_copy_on(way, 0).wait_recv()
            line_copy_on(way, 1).wait_recv()

    from_far = 1 - z_at // 2
    first_piece = jnp.where((z_at == 0) | (z_at == z_last), 0, 2)

    def finish(piece, _):
        at_rows = aligned(piece * 128, 128)
        totals = [
            own_vm[n, at_rows, :].astype(f32)
            + pair_vm[n, at_rows, :].astype(f32)
            + line[from_far, first_piece + n, at_rows, :].astype(f32)
            for n in range(2)
        ]
        up_total[at_rows, :] = totals[0]
        down_total[:, lanes_at(piece * 128, 128)] = totals[1].T
        return 0

    lax.fori_loop(0, features // 128, finish, 0)
    expert_copies = [
        pltpu.make_async_copy(up_total, up_out, weight_store.at[5]),
        pltpu.make_async_copy(down_total, down_out, weight_store.at[6]),
    ]
    for copy in expert_copies:
        copy.start()

    gather_y(0, 0, z_at, 1 - y_at).wait_recv()
    for step in range(3):
        for way in range(2):
            at = place(way)
            piece = z_at - 1 - step if way == 0 else z_at + 1 + step

            @pl.when(at >= 1 + step)
            def _():
                gather_y(step + 1, way, piece, 1 - y_at).wait_recv()

    def to_out(piece, _):
        for side in range(2):
            weight_sum[aligned(side * part_rows + piece * quarter, quarter), :] = shared_all[
                side, quarter_at(piece), :
            ].astype(f32)
        return 0

    lax.fori_loop(0, z_last + 1, to_out, 0)
    for number in range(planes - 1):
        late_copy(number).wait_recv()
    late = late_z[0]
    for plane in range(1, planes):
        late += late_z[plane]
    sums_all[...] = late
    weight_copies = [
        *[
            pltpu.make_async_copy(weight_sum.at[pl.ds(n * share, share), :], qkv_out.at[n], weight_store.at[n])
            for n in range(3)
        ],
        pltpu.make_async_copy(weight_sum.at[pl.ds(3 * share, share), :], out_w_out, weight_store.at[3]),
        pltpu.make_async_copy(sums_all, sums_out, weight_store.at[4]),
    ]
    for copy in weight_copies:
        copy.start()
    route_one.wait_send()
    route_two.wait_send()

    def drain(image, _):
        for copy in (one_core_copy, one_x_copy, one_total_copy):
            copy(image).wait_send()
        return 0

    lax.fori_loop(0, images, drain, 0)
    for part in range(part_count):
        m_core_copy(0, part).wait_send()
        m_core_copy(1, part).wait_send()
        m_y_copy(part).wait_send()

        @pl.when(keeps)
        def _():
            m_quarter_copy(part).wait_send()
            m_store_copy(part).wait()

        @pl.when(jnp.logical_not(keeps))
        def _():
            m_x_copy(part).wait_send()
            m_quarter_copy(part).wait_recv()

    for copy in (*weight_copies, *expert_copies, store_copy):
        copy.wait()
    late_y_copy.wait_send()
    for number in range(planes - 1):
        late_copy(number).wait_send()
    gather_y(0, 0, z_at, y_at).wait_send()
    for way in range(2):

        @pl.when(place(way) <= 1)
        def _():
            for piece in range(1, 4):
                line_copy_on(way, piece).wait_send()

        @pl.when(place(way) == 1)
        def _():
            line_copy_on(way, 0).wait_send()

        @pl.when(place(way) == 2)
        def _():
            for piece in range(2):
                line_copy_on(way, piece).wait_send()

    for step in range(3):
        for way in range(2):
            at = place(way)

            @pl.when((at <= step) & (at < z_last))
            def _():
                small_copy(step, way).wait_send()

            piece = z_at - step if way == 0 else z_at + step

            @pl.when((at >= step) & (at < z_last))
            def _():
                gather_z(step, way, piece).wait_send()

            piece = z_at - 1 - step if way == 0 else z_at + 1 + step

            @pl.when(at >= 1 + step)
            def _():
                gather_y(step + 1, way, piece, y_at).wait_send()


def run_backward(gain1, shift1, gain2, qkv_w, out_w, grad_router, tok, *streamed):
    images, _, features = tok.shape
    rows = images * PITCH
    share = out_w.shape[0]
    heads = share // HD
    hidden = streamed[-1].shape[1]
    wide = features // 2
    parts = 4
    vmem = pl.BlockSpec(memory_space=pltpu.VMEM)
    anywhere = pl.BlockSpec(memory_space=pl.ANY)
    shape = jax.ShapeDtypeStruct
    dma = pltpu.SemaphoreType.DMA
    block = (images, PITCH, wide)
    return pl.pallas_call(
        partial(backward_kernel, images=images, heads=heads),
        out_shape=[
            shape((features, hidden), f32),
            shape((hidden, features), f32),
            shape((images * SEQ, features), f32),
            shape((3, share, features), f32),
            shape((share, features), f32),
            shape((16, features), f32),
            shape((rows, wide // 2), bf16),
        ],
        in_specs=[vmem] * 6 + [anywhere] * (1 + len(streamed)),
        out_specs=[anywhere] * 7,
        scratch_shapes=[
            pltpu.VMEM((images, PITCH, features), bf16),
            *[pltpu.VMEM((images, PITCH, share), bf16)] * 4,
            pltpu.VMEM((images, PITCH, 128), f32),
            pltpu.VMEM((rows, features), bf16),
            pltpu.VMEM((rows, features), f32),
            pltpu.VMEM((rows, features), bf16),
            pltpu.VMEM((2 * rows, wide), bf16),
            pltpu.VMEM((2 * rows, wide), bf16),
            *[pltpu.VMEM((parts, rows // parts, wide), bf16)] * 2,
            pltpu.VMEM((parts, 2, rows // parts, wide // 2), bf16),
            pltpu.VMEM((rows // parts, wide), f32),
            pltpu.VMEM((2, features, hidden), bf16),
            pltpu.VMEM((2, features, hidden), bf16),
            pltpu.VMEM((2, features, 2 * hidden), bf16),
            *[pltpu.VMEM(block, bf16)] * 5,
            pltpu.VMEM((2, 4, features, hidden), bf16),
            pltpu.VMEM((features, features), f32),
            pltpu.VMEM((features // 2, features), f32),
            pltpu.VMEM((2, features // 2, features), bf16),
            pltpu.VMEM((features // 2, features), bf16),
            pltpu.VMEM((2, 2, 3, features // 8, features), bf16),
            pltpu.VMEM((2, features // 2, features), bf16),
            *[pltpu.VMEM((8, features), f32)] * 2,
            *[pltpu.VMEM((16, features), f32)] * 2,
            pltpu.VMEM((4, 16, features), f32),
            pltpu.VMEM((features, hidden), f32),
            pltpu.VMEM((hidden, features), f32),
            pltpu.VMEM((16, features), f32),
            pltpu.VMEM((PITCH, features), f32),
        ]
        + [dma((2, parts))] * 2
        + [dma((parts,))] * 7
        + [dma((images,))] * 6
        + [dma((2, 4))] * 2
        + [dma((4,))] * 2
        + [dma((2, 3))] * 4
        + [dma((2, 4))] * 2
        + [dma((2,))] * 2
        + [dma((4,))] * 2
        + [dma((4,)), dma((9, images)), dma((7,)), dma((7,)), dma((1,))],
        compiler_params=pltpu.CompilerParams(
            collective_id=2, has_side_effects=True, vmem_limit_bytes=63 << 20
        ),
    )(gain1, shift1, gain2, qkv_w, out_w, grad_router, tok, *streamed)


def per_image(rows_in):
    images = rows_in.shape[0] // SEQ
    blocks = rows_in.reshape(images, SEQ, rows_in.shape[1])
    return jnp.pad(blocks, ((0, 0), (0, PITCH - SEQ), (0, 0)))


def unpad(blocks):
    images = blocks.shape[0]
    return blocks[:, :SEQ].reshape(images * SEQ, blocks.shape[2])


def per_device_dense(
    tokens,
    gain_attn,
    shift_attn,
    qkv_weight,
    out_weight,
    gain_moe,
    shift_moe,
    router_weight,
    expert_up,
    expert_down,
    routes,
    keep_mask,
    cotangent,
):
    row_count, feature_count = tokens.shape
    images = row_count // SEQ
    rows = images * PITCH
    tensor_count = lax.axis_size("tensor")
    quarter_width = feature_count // tensor_count
    experts_all = router_weight.shape[1]
    hidden = expert_up.shape[2]
    kept_routes = per_image(jnp.where(keep_mask > 0, routes, -1) + 1).reshape(rows, 2) - 1
    chosen = kept_routes[:, :, None] == jnp.arange(128, dtype=jnp.int32)[None, None, :]
    kept = jnp.any(chosen, axis=1).astype(bf16)
    router_wide = jnp.pad(router_weight, ((0, 0), (0, 128 - experts_all)))
    tok = per_image(tokens)
    qkv_turned = jnp.swapaxes(qkv_weight, 1, 2)
    (
        queries,
        keys,
        values,
        attended,
        lse,
        resid,
        h_all,
        cot_all,
        kept_all,
        up_all,
        down_all,
        mixed_first,
        grad_h_first,
        gate_first,
        up_first,
        down_first,
    ) = run_forward(
        tok,
        gain_attn,
        shift_attn,
        gain_moe,
        shift_moe,
        qkv_turned,
        out_weight,
        expert_up[0],
        expert_down[0],
        per_image(cotangent).reshape(rows, quarter_width),
        kept,
        router_wide,
        experts_all,
    )
    mixed_part, up_second, down_second, grad_router, grad_h_two, up_pair, down_pair, line_first = run_second_pair(
        h_all,
        cot_all,
        kept_all,
        router_wide,
        mixed_first,
        grad_h_first,
        gate_first,
        up_all,
        down_all,
        up_first,
        down_first,
        experts_all,
    )
    grad_up, grad_down, tokens_grad, grad_qkv, grad_out, sums, mixed = run_backward(
        gain_attn,
        shift_attn,
        gain_moe,
        qkv_turned,
        out_weight,
        grad_router,
        tok,
        queries,
        keys,
        values,
        attended,
        lse,
        grad_h_two,
        resid,
        cot_all,
        mixed_part,
        up_first,
        down_first,
        up_pair,
        down_pair,
        up_second,
        down_second,
        line_first,
    )
    return (
        unpad(mixed.reshape(images, PITCH, quarter_width)),
        tokens_grad,
        sums[0],
        sums[1],
        jnp.swapaxes(grad_qkv, 1, 2),
        grad_out,
        sums[2],
        sums[3],
        sums[8 : 8 + experts_all].T,
        grad_up[None],
        grad_down[None],
    )


def per_device(*arguments):
    router_weight = arguments[7]
    if router_weight.shape[1] == 4 and lax.axis_size("expert") == 8 and lax.axis_size("tensor") == 4:
        return per_device_dense(*arguments)
    return per_device_routed(*arguments)


def solution(mesh):
    placed = (
        P("expert", None),
        P(),
        P(),
        P(None, None, "tensor"),
        P("tensor", None),
        P(),
        P(),
        P(),
        P("expert", None, "tensor"),
        P("expert", "tensor", None),
        P("expert", None),
        P("expert", None),
        P("expert", "tensor"),
    )
    return jax.shard_map(
        per_device,
        mesh=mesh,
        in_specs=placed,
        out_specs=(
            P("expert", "tensor"),
            P("expert", None),
            P(),
            P(),
            P(None, None, "tensor"),
            P("tensor", None),
            P(),
            P(),
            P(),
            P("expert", None, "tensor"),
            P("expert", "tensor", None),
        ),
        check_vma=False,
    )
```

```python
from functools import partial

import jax
import jax.numpy as jnp
from jax import lax
from jax.experimental import pallas as pl
from jax.experimental.pallas import tpu as pltpu
from jax.sharding import PartitionSpec as P

HD = 64
SEQ = 197


norm_epsilon = 1e-06


def norm_rows(values, gain, shift):
    row_mean = jnp.mean(values, axis=-1, keepdims=True)
    centred = values - row_mean
    spread = jnp.mean(centred * centred, axis=-1, keepdims=True)
    return centred * lax.rsqrt(spread + norm_epsilon) * gain + shift


def gelu_exact(values):
    return jax.nn.gelu(values, approximate=False)


def gate_from_logits(logit_rows, picked_rows, keep_rows):
    router_probs = jax.nn.softmax(logit_rows, axis=-1)
    return jnp.sum(jnp.where(picked_rows, router_probs[:, None, :], 0.0), axis=-1) * keep_rows


def attention_forward(h_rows, qkv_w, out_w):
    row_total_count = h_rows.shape[0]
    head_count = qkv_w.shape[2] // HD
    image_count = row_total_count // SEQ
    score_scale = HD ** (-0.5)
    projected = jnp.einsum("td,cdf->ctf", h_rows, qkv_w, preferred_element_type=jnp.float32).astype(
        jnp.bfloat16
    )
    split_heads = projected.reshape(3, image_count, SEQ, head_count, HD)
    queries = split_heads[0]
    keys_all = split_heads[1]
    values_all = split_heads[2]
    scores = (
        jnp.einsum("gqhe,gkhe->ghqk", queries, keys_all, preferred_element_type=jnp.float32)
        * score_scale
    )
    row_peak = jnp.max(scores, axis=-1, keepdims=True)
    exp_scores = jnp.exp(scores - row_peak)
    row_total = jnp.sum(exp_scores, axis=-1, keepdims=True)
    log_total = row_peak + jnp.log(row_total)
    weights = (exp_scores / row_total).astype(jnp.bfloat16)
    attended = jnp.einsum(
        "ghqk,gkhe->gqhe", weights, values_all, preferred_element_type=jnp.float32
    ).astype(jnp.bfloat16)
    attended = attended.reshape(row_total_count, head_count * HD)
    partial_out = jnp.dot(attended, out_w, preferred_element_type=jnp.float32)
    return (partial_out, (attended, queries, keys_all, values_all, log_total))


def attention_backward(grad_branch, saved, h_rows, qkv_w, out_w):
    attended, queries, keys_all, values_all, log_total = saved
    row_total_count = h_rows.shape[0]
    head_count = qkv_w.shape[2] // HD
    image_count = row_total_count // SEQ
    score_scale = HD ** (-0.5)
    grad_out = jnp.einsum("tc,td->cd", attended, grad_branch, preferred_element_type=jnp.float32)
    grad_attended = jnp.einsum(
        "td,cd->tc", grad_branch, out_w, preferred_element_type=jnp.float32
    ).astype(jnp.bfloat16)
    grad_attended = grad_attended.reshape(image_count, SEQ, head_count, HD)
    scores_again = (
        jnp.einsum("gqhe,gkhe->ghqk", queries, keys_all, preferred_element_type=jnp.float32)
        * score_scale
    )
    probs_again = jnp.exp(scores_again - log_total)
    grad_weights = jnp.einsum(
        "gqhe,gkhe->ghqk", grad_attended, values_all, preferred_element_type=jnp.float32
    )
    grad_scores = (
        probs_again * (grad_weights - jnp.sum(probs_again * grad_weights, axis=-1, keepdims=True))
    ).astype(jnp.bfloat16)
    grad_queries = (
        jnp.einsum("ghqk,gkhe->gqhe", grad_scores, keys_all, preferred_element_type=jnp.float32)
        * score_scale
    )
    grad_keys = (
        jnp.einsum("ghqk,gqhe->gkhe", grad_scores, queries, preferred_element_type=jnp.float32)
        * score_scale
    )
    grad_values = jnp.einsum(
        "ghqk,gqhe->gkhe",
        probs_again.astype(jnp.bfloat16),
        grad_attended,
        preferred_element_type=jnp.float32,
    )
    grad_rows = (
        jnp.stack([grad_queries, grad_keys, grad_values])
        .astype(jnp.bfloat16)
        .reshape(3, row_total_count, head_count * HD)
    )
    grad_qkv = jnp.einsum("td,ctf->cdf", h_rows, grad_rows, preferred_element_type=jnp.float32)
    grad_h_one = jnp.einsum("ctf,cdf->td", grad_rows, qkv_w, preferred_element_type=jnp.float32)
    return (grad_qkv, grad_out, grad_h_one)


def moe_tail(
    grad_h_rows,
    grad_gate_rows,
    grad_out_rows,
    h_two_rows,
    resid_rows,
    gate_back,
    router_weight,
    gain_moe,
    shift_moe,
):
    row_total_count = grad_h_rows.shape[0]
    grad_gate = jnp.sum(grad_gate_rows.reshape(row_total_count, -1, 2), axis=1)
    grad_logits = gate_back(grad_gate)[0].astype(jnp.bfloat16)
    grad_router = jnp.einsum(
        "td,te->de", h_two_rows, grad_logits, preferred_element_type=jnp.float32
    )
    grad_h_two = grad_h_rows + jnp.einsum(
        "te,de->td", grad_logits, router_weight, preferred_element_type=jnp.float32
    )
    norm_out, norm_back = jax.vjp(norm_rows, resid_rows, gain_moe, shift_moe)
    grad_resid_norm, grad_gain_moe, grad_shift_moe = norm_back(grad_h_two)
    return (grad_out_rows + grad_resid_norm, grad_router, grad_gain_moe, grad_shift_moe)


def per_device_routed(
    tokens,
    gain_attn,
    shift_attn,
    qkv_weight,
    out_weight,
    gain_moe,
    shift_moe,
    router_weight,
    expert_up,
    expert_down,
    routes,
    keep_mask,
    cotangent,
):
    row_count, feature_count = tokens.shape
    tensor_count = lax.axis_size("tensor")
    expert_count = lax.axis_size("expert")
    tensor_here = lax.axis_index("tensor")
    quarter_width = feature_count // tensor_count
    col_start = tensor_here * quarter_width
    experts_all = router_weight.shape[1]
    capacity = max(2, 7 * row_count // (2 * experts_all))
    tokens_float = tokens.astype(jnp.float32)
    h_one = norm_rows(tokens_float, gain_attn, shift_attn).astype(jnp.bfloat16)
    partial_out, saved = attention_forward(h_one, qkv_weight, out_weight)
    branch = lax.psum(partial_out, "tensor")
    resid = tokens_float + branch
    h_two = norm_rows(resid, gain_moe, shift_moe).astype(jnp.bfloat16)
    logits = jnp.dot(h_two, router_weight, preferred_element_type=jnp.float32)
    keep_float = keep_mask.astype(jnp.float32)
    picked = routes[:, :, None] == jnp.arange(experts_all, dtype=jnp.int32)[None, None, :]
    gate_values, gate_back = jax.vjp(
        partial(gate_from_logits, picked_rows=picked, keep_rows=keep_float), logits
    )
    flat_expert = routes.reshape(-1)
    one_hot = (flat_expert[:, None] == jnp.arange(experts_all, dtype=jnp.int32)[None, :]).astype(
        jnp.int32
    )
    rank_within = jnp.sum((jnp.cumsum(one_hot, axis=0) - one_hot) * one_hot, axis=1)
    slot_index = flat_expert * capacity + rank_within
    token_index = jnp.repeat(jnp.arange(row_count, dtype=jnp.int32), 2)
    live_route = keep_mask.reshape(-1) > 0
    source_table = (
        jnp.full((experts_all * capacity,), row_count, jnp.int32)
        .at[slot_index]
        .set(jnp.where(live_route, token_index, row_count))
    )
    padded_rows = jnp.concatenate([h_two, jnp.zeros((1, feature_count), jnp.bfloat16)], axis=0)
    dispatch = padded_rows[source_table].reshape(experts_all, capacity, feature_count)
    paired = jnp.broadcast_to(dispatch[:, None], (experts_all, 2, capacity, feature_count)).reshape(
        expert_count, capacity, feature_count
    )
    arrived = lax.all_to_all(paired, "expert", split_axis=0, concat_axis=0, tiled=True)
    expert_rows = arrived.reshape(expert_count * capacity, feature_count)
    up_local = expert_up[0]
    down_local = expert_down[0]
    pre_act = jnp.dot(expert_rows, up_local, preferred_element_type=jnp.float32)
    hidden_float, gelu_back = jax.vjp(gelu_exact, pre_act)
    hidden = hidden_float.astype(jnp.bfloat16)
    partial_down = jnp.dot(hidden, down_local, preferred_element_type=jnp.float32)
    summed = lax.psum_scatter(partial_down, "tensor", scatter_dimension=1, tiled=True)
    returned = lax.all_to_all(
        summed.reshape(expert_count, capacity, quarter_width),
        "expert",
        split_axis=0,
        concat_axis=0,
        tiled=True,
    )
    answer_table = jnp.sum(
        returned.reshape(experts_all, 2, capacity, quarter_width), axis=1
    ).astype(jnp.bfloat16)
    answers = (
        answer_table.reshape(experts_all * capacity, quarter_width)[slot_index]
        .astype(jnp.float32)
        .reshape(row_count, 2, quarter_width)
    )
    resid_part = lax.dynamic_slice_in_dim(resid, col_start, quarter_width, 1)
    mixed = (resid_part + jnp.sum(gate_values[:, :, None] * answers, axis=1)).astype(jnp.bfloat16)
    grad_part = cotangent.astype(jnp.float32)
    grad_answers = (
        (gate_values[:, :, None] * grad_part[:, None, :])
        .astype(jnp.bfloat16)
        .reshape(2 * row_count, quarter_width)
    )
    grad_gate_part = jnp.sum(grad_part[:, None, :] * answers, axis=-1)
    outgoing = (
        jnp.zeros((experts_all * capacity, quarter_width), jnp.bfloat16)
        .at[slot_index]
        .set(grad_answers)
    )
    outgoing = jnp.broadcast_to(
        outgoing.reshape(experts_all, 1, capacity, quarter_width),
        (experts_all, 2, capacity, quarter_width),
    ).reshape(expert_count, capacity, quarter_width)
    incoming = lax.all_to_all(outgoing, "expert", split_axis=0, concat_axis=0, tiled=True)
    grad_full = lax.all_gather(incoming, "tensor", axis=2, tiled=True).reshape(
        expert_count * capacity, feature_count
    )
    grad_hidden = jnp.einsum("rd,fd->rf", grad_full, down_local, preferred_element_type=jnp.float32)
    grad_pre = gelu_back(grad_hidden)[0].astype(jnp.bfloat16)
    grad_down = jnp.einsum("rf,rd->fd", hidden, grad_full, preferred_element_type=jnp.float32)
    grad_up = jnp.einsum("rd,rf->df", expert_rows, grad_pre, preferred_element_type=jnp.float32)
    grad_rows_partial = jnp.einsum(
        "rf,df->rd", grad_pre, up_local, preferred_element_type=jnp.float32
    )
    grad_rows_sum = lax.psum_scatter(
        grad_rows_partial.astype(jnp.bfloat16), "tensor", scatter_dimension=1, tiled=True
    ).astype(jnp.float32)
    sent_back = lax.all_to_all(
        grad_rows_sum.reshape(expert_count, capacity, quarter_width).astype(jnp.bfloat16),
        "expert",
        split_axis=0,
        concat_axis=0,
        tiled=True,
    ).astype(jnp.float32)
    grad_table = jnp.sum(sent_back.reshape(experts_all, 2, capacity, quarter_width), axis=1).astype(
        jnp.bfloat16
    )
    grad_inputs = (
        grad_table.reshape(experts_all * capacity, quarter_width)[slot_index]
        .astype(jnp.float32)
        .reshape(row_count, 2, quarter_width)
    )
    grad_h_part = jnp.sum(grad_inputs * keep_float[:, :, None], axis=1)
    grad_h_full, grad_gate_all, grad_out_full = (
        lax.all_gather(grad_h_part, "tensor", axis=1, tiled=True),
        lax.all_gather(grad_gate_part, "tensor", axis=1, tiled=True),
        lax.all_gather(grad_part, "tensor", axis=1, tiled=True),
    )
    grad_resid, grad_router, grad_gain_moe, grad_shift_moe = moe_tail(
        grad_h_full,
        grad_gate_all,
        grad_out_full,
        h_two,
        resid,
        gate_back,
        router_weight,
        gain_moe,
        shift_moe,
    )
    grad_qkv, grad_out, grad_h_one_part = attention_backward(
        grad_resid.astype(jnp.bfloat16), saved, h_one, qkv_weight, out_weight
    )
    grad_h_one = lax.psum(grad_h_one_part.astype(jnp.bfloat16), "tensor").astype(jnp.float32)
    norm_one_out, norm_one_back = jax.vjp(norm_rows, tokens_float, gain_attn, shift_attn)
    grad_tok_norm, grad_gain_attn, grad_shift_attn = norm_one_back(grad_h_one)
    grad_tokens = grad_resid + grad_tok_norm
    summed_grads = lax.psum(
        (
            grad_gain_attn,
            grad_shift_attn,
            grad_qkv,
            grad_out,
            grad_gain_moe,
            grad_shift_moe,
            grad_router,
        ),
        "expert",
    )
    grad_qkv_mine = summed_grads[2]
    grad_out_mine = summed_grads[3]
    return (
        mixed,
        grad_tokens,
        summed_grads[0],
        summed_grads[1],
        grad_qkv_mine,
        grad_out_mine,
        summed_grads[4],
        summed_grads[5],
        summed_grads[6],
        grad_up[None],
        grad_down[None],
    )


MESH = pl.DeviceIdType.MESH
f32 = jnp.float32
bf16 = jnp.bfloat16
PITCH = 208


def dot(left, right, over=((1,), (0,))):
    return lax.dot_general(left, right, (over, ((), ())), preferred_element_type=f32)


def aligned(start, size):
    return pl.ds(pl.multiple_of(start, 16), size)


def lanes_at(start, size):
    return pl.ds(pl.multiple_of(start, 128), size)


def norm_stats(values):
    row_mean = jnp.mean(values, axis=1, keepdims=True)
    centred = values - row_mean
    inverse = lax.rsqrt(jnp.mean(centred * centred, axis=1, keepdims=True) + norm_epsilon)
    return centred * inverse, inverse


def greet(neighbours):
    barrier = pltpu.get_barrier_semaphore()
    count = 0
    for is_there, device in neighbours:

        @pl.when(is_there)
        def _():
            pl.semaphore_signal(barrier, inc=1, device_id=device, device_id_type=MESH)

        count = count + jnp.where(is_there, 1, 0)
    pl.semaphore_wait(barrier, count)


def head_mask(lane, head):
    return (lane < HD) if head % 2 == 0 else (lane >= HD)


def expert_math(h_rows, cot_rows, kept, router, up, down, pair, experts):
    block = h_rows.shape[0]
    hidden = up.shape[1] // 2
    lane = lax.broadcasted_iota(jnp.int32, (block, 128), 1)
    logits = jnp.where(lane < experts, dot(h_rows, router, ((1,), (1,))), -1e30)
    powers = jnp.exp(logits - jnp.max(logits, axis=1, keepdims=True))
    probs = powers / jnp.sum(powers, axis=1, keepdims=True)
    gates = kept * probs
    pre_act = dot(h_rows, up)
    back = dot(cot_rows, down, ((1,), (1,)))
    normal_cdf = 0.5 + 0.5 * lax.erf(pre_act * 0.7071067811865476)
    gelu = pre_act * normal_cdf
    slope = normal_cdf + pre_act * (0.3989422804014327 * jnp.exp(-0.5 * pre_act * pre_act))
    product = gelu * back
    grad_gate = jnp.zeros((block, 128), f32)
    spread = []
    for side in range(2):
        chosen = lane == 2 * pair + side
        part = jnp.sum(product[:, side * hidden : (side + 1) * hidden], axis=1, keepdims=True)
        grad_gate = jnp.where(chosen, part, grad_gate)
        gate = jnp.sum(jnp.where(chosen, gates, 0.0), axis=1, keepdims=True)
        spread.append(jnp.broadcast_to(gate, (block, hidden)))
    gate = jnp.concatenate(spread, axis=1)
    hidden_rows = (gelu * gate).astype(bf16)
    grad_pre = (slope * back * gate).astype(bf16)
    return hidden_rows, grad_pre, probs, grad_gate


BLOCK = 2 * PITCH


def forward_kernel(
    tok_raw,
    gain1_ref,
    shift1_ref,
    gain2_ref,
    shift2_ref,
    qkv_ref,
    out_w_ref,
    up_ref,
    down_ref,
    cot_turned,
    kept_ref,
    router_ref,
    q_ref,
    k_ref,
    v_ref,
    att_ref,
    lse_ref,
    resid_ref,
    h_out,
    cot_out,
    kept_out,
    up_out,
    down_out,
    mixed_out,
    grad_h_out,
    gate_out,
    grad_up_out,
    grad_down_out,
    tok_out,
    tok_ref,
    cot_ref,
    up_vm,
    down_vm,
    up_sum,
    down_sum,
    mixed_slots,
    grad_h_slots,
    gate_slots,
    grad_up_vm,
    grad_down_vm,
    q_all,
    k_all,
    v_all,
    att_all,
    lse_all,
    resid_all,
    h_all,
    cot_all,
    kept_all,
    part,
    mine,
    core_from,
    core_to,
    x_to,
    x_from,
    total_to,
    total_from,
    cot_core,
    core_s,
    core_r,
    x_s,
    x_r,
    tot_s,
    tot_r,
    y_s,
    y_r,
    rel_s,
    rel_r,
    w_s,
    w_r,
    c_s,
    c_r,
    own_sem,
    pair_sem,
    block_sem,
    grad_sem,
    cot_sem,
    out_sem,
    *,
    images,
    heads,
    experts,
):
    expert_at = lax.axis_index("expert")
    tensor_at = lax.axis_index("tensor")
    z_at, y_at = expert_at // 2, expert_at % 2
    z_last = lax.axis_size("expert") // 2 - 1
    x_at, core_at = tensor_at // 2, tensor_at % 2
    other = 1 - core_at
    rows = images * PITCH
    half = rows // 2
    wide = out_w_ref.shape[1] // 2
    hidden = up_ref.shape[1]
    core_dev = (expert_at, tensor_at + 1 - 2 * core_at)
    x_dev = (expert_at, tensor_at + 2 - 4 * x_at)
    y_dev = (expert_at + 1 - 2 * y_at, tensor_at)
    z_up = (expert_at + 2, tensor_at)
    z_down = (expert_at - 2, tensor_at)
    has_up, has_down = z_at < z_last, z_at > 0
    greet([(True, core_dev), (True, x_dev), (True, y_dev), (has_up, z_up), (has_down, z_down)])

    def remote(src, dst, send, recv, device):
        return pltpu.make_async_remote_copy(
            src_ref=src, dst_ref=dst, send_sem=send, recv_sem=recv, device_id=device, device_id_type=MESH
        )

    def slot(expert, plane):
        pair = (expert // 2 + plane // 2) % 2
        return (
            up_out.at[pair, :, lanes_at(expert % 2 * hidden, hidden)],
            down_out.at[pair, aligned(expert % 2 * hidden, hidden), :],
        )

    def hop(step, way):
        expert = z_at - step if way == 0 else z_at + step
        plane = z_at + 1 if way == 0 else z_at - 1
        source = (up_ref, down_ref) if step == 0 else slot(expert, z_at)
        target = slot(expert, plane)
        device = z_up if way == 0 else z_down
        return [remote(source[n], target[n], w_s.at[way, step, n], w_r.at[way, step, n], device) for n in range(2)]

    def hop_goes(step, way):
        if way == 0:
            return (z_at - step >= 0) & has_up
        return (z_at + step <= z_last) & has_down

    def hop_comes(step, way):
        return (z_at - 1 - step >= 0) if way == 0 else (z_at + 1 + step <= z_last)

    def hop_arriving(step, way):
        expert = z_at - 1 - step if way == 0 else z_at + 1 + step
        target = slot(expert, z_at)
        return [remote(target[n], target[n], w_s.at[way, step, n], w_r.at[way, step, n], core_dev) for n in range(2)]

    def start_hops(step):
        for way in range(2):

            @pl.when(hop_goes(step, way))
            def _():
                for copy in hop(step, way):
                    copy.start()

    def await_hops(step):
        for way in range(2):

            @pl.when(hop_comes(step, way))
            def _():
                for copy in hop_arriving(step, way):
                    copy.wait_recv()

    start_hops(0)

    def pair_place(expert):
        return up_vm.at[:, lanes_at(expert % 2 * hidden, hidden)], down_vm.at[aligned(expert % 2 * hidden, hidden), :]

    near = z_at + 1 - 2 * (z_at % 2)
    own_copies = [
        pltpu.make_async_copy((up_ref, down_ref)[n], pair_place(z_at)[n], own_sem.at[n]) for n in range(2)
    ]
    near_copies = [
        pltpu.make_async_copy(slot(near, z_at)[n], pair_place(near)[n], pair_sem.at[n]) for n in range(2)
    ]
    for copy in own_copies:
        copy.start()

    for number in range(images):
        first = number * SEQ // 128 * 128
        skip = number * SEQ - first
        turned = cot_turned[:, first : first + 384].T.astype(f32)[skip : skip + SEQ]
        padded = jnp.concatenate([turned, jnp.zeros((PITCH - SEQ, turned.shape[1]), f32)], axis=0)
        cot_ref[number * PITCH : (number + 1) * PITCH, :] = padded.astype(bf16)
    swap = remote(cot_ref, cot_core, c_s.at[0], c_r.at[0], core_dev)
    swap.start()
    kept_all[pl.ds(0, rows), :] = kept_ref[...]

    def kept_half(side, core):
        return kept_all.at[aligned(side * rows + core * half, half), :]

    kept_y = remote(kept_half(0, core_at), kept_half(1, core_at), c_s.at[7], c_r.at[7], y_dev)
    kept_share = remote(kept_half(1, core_at), kept_half(1, core_at), c_s.at[6], c_r.at[6], core_dev)
    kept_share_in = remote(kept_half(1, other), kept_half(1, other), c_s.at[6], c_r.at[6], core_dev)
    kept_y.start()
    swap.wait_recv()

    @pl.when(core_at == 0)
    def _():
        both = jnp.concatenate([cot_ref[...], cot_core[...]], axis=1)
        cot_all[pl.ds(0, rows), lanes_at(x_at * wide, wide)] = both

    @pl.when(core_at == 1)
    def _():
        both = jnp.concatenate([cot_core[...], cot_ref[...]], axis=1)
        cot_all[pl.ds(0, rows), lanes_at(x_at * wide, wide)] = both

    def block(side, col_side, core):
        return cot_all.at[aligned(side * rows + core * half, half), lanes_at(col_side * wide, wide)]

    def cot_copy(number, source, target, device):
        return remote(source, target, c_s.at[number], c_r.at[number], device)

    mine_block = block(0, x_at, core_at)
    cot_x = cot_copy(1, mine_block, mine_block, x_dev)
    cot_y = cot_copy(2, mine_block, block(1, x_at, core_at), y_dev)
    cot_x.start()
    cot_y.start()
    across_x, across_y, across_both = block(0, 1 - x_at, core_at), block(1, x_at, core_at), block(1, 1 - x_at, core_at)
    cot_x_in = cot_copy(1, across_x, across_x, x_dev)
    cot_y_in = cot_copy(2, across_y, across_y, y_dev)
    relay_y = cot_copy(3, across_x, across_both, y_dev)
    relay_x = cot_copy(3, across_y, across_y, x_dev)
    relay_in = cot_copy(3, across_both, across_both, y_dev)
    cot_share = [
        cot_copy(4, across_x, across_x, core_dev),
        cot_copy(5, across_y, across_y, core_dev),
        cot_copy(8, across_both, across_both, core_dev),
    ]
    arriving = [block(0, 1 - x_at, other), block(1, x_at, other), block(1, 1 - x_at, other)]
    cot_share_in = [cot_copy(number, ref, ref, core_dev) for number, ref in zip((4, 5, 8), arriving)]

    lane = lax.broadcasted_iota(jnp.int32, (PITCH, 2 * HD), 1)
    key_mask = lax.broadcasted_iota(jnp.int32, (PITCH, PITCH), 1) < SEQ
    gain1, shift1, gain2, shift2 = (ref[...].reshape(1, 2 * wide) for ref in (gain1_ref, shift1_ref, gain2_ref, shift2_ref))
    my_cols = lanes_at(core_at * wide, wide)
    their_cols = lanes_at(other * wide, wide)

    def attend(image):
        normed, _ = norm_stats(tok_ref[image].astype(f32))
        h_one = (normed * gain1 + shift1).astype(bf16)
        queries = dot(h_one, qkv_ref[0], ((1,), (1,))).astype(bf16)
        keys = dot(h_one, qkv_ref[1], ((1,), (1,))).astype(bf16)
        values = dot(h_one, qkv_ref[2], ((1,), (1,))).astype(bf16)
        q_all[image] = queries
        k_all[image] = keys
        v_all[image] = values
        outs = []
        lse = jnp.zeros((PITCH, 2 * HD), f32)
        for head in range(heads):
            first = head // 2 * 2 * HD
            last = min(first + 2 * HD, heads * HD)
            q_head, k_head, v_head = queries[:, first:last], keys[:, first:last], values[:, first:last]
            if last - first == 2 * HD:
                q_head = jnp.where(head_mask(lane, head), q_head, jnp.zeros_like(q_head))
            scores = dot(q_head, k_head, ((1,), (1,))) * (HD**-0.5)
            scores = jnp.where(key_mask, scores, -1e30)
            peak = jnp.max(scores, axis=1, keepdims=True)
            powers = jnp.exp(scores - peak)
            row_sum = jnp.sum(powers, axis=1, keepdims=True)
            weights = (powers / row_sum).astype(bf16)
            outs.append(dot(weights, v_head))
            lse = jnp.where(lane == head, peak + jnp.log(row_sum), lse)
        lse_all[image] = lse
        joined = []
        for head in range(0, heads, 2):
            if head + 1 < heads:
                joined.append(jnp.where(lane < HD, outs[head], outs[head + 1]))
            else:
                joined.append(outs[head])
        attended = jnp.concatenate(joined, axis=1).astype(bf16)
        att_all[image] = attended
        part[...] = dot(attended, out_w_ref[...])
        mine[image] = part[:, my_cols]
        core_to[image] = part[:, their_cols].astype(bf16)

    def core_copy(image):
        return remote(core_to.at[image], core_from.at[image], core_s.at[image], core_r.at[image], core_dev)

    def x_copy(image):
        return remote(x_to.at[image], x_from.at[image], x_s.at[image], x_r.at[image], x_dev)

    def total_copy(image):
        return remote(total_to.at[image], total_from.at[image], tot_s.at[image], tot_r.at[image], core_dev)

    def h_block(side, image, core):
        return h_all.at[aligned(side * rows + image * PITCH, PITCH), lanes_at(core * wide, wide)]

    def y_copy(image):
        return remote(h_block(0, image, core_at), h_block(1, image, core_at), y_s.at[image], y_r.at[image], y_dev)

    def relay_copy(image):
        ref = h_block(1, image, core_at)
        return remote(ref, ref, rel_s.at[image], rel_r.at[image], core_dev)

    def relay_arriving(image):
        ref = h_block(1, image, other)
        return remote(ref, ref, rel_s.at[image], rel_r.at[image], core_dev)

    attend_outs = ((tok_ref, tok_out), (q_all, q_ref), (k_all, k_ref), (v_all, v_ref), (att_all, att_ref), (lse_all, lse_ref))

    def out_copies(image):
        copies = [
            pltpu.make_async_copy(kept.at[image], out.at[image], out_sem.at[n, image])
            for n, (kept, out) in enumerate(attend_outs)
        ]
        at = aligned(image * PITCH, PITCH)
        return copies, [
            pltpu.make_async_copy(resid_all.at[image], resid_ref.at[at, :], out_sem.at[6, image]),
            pltpu.make_async_copy(h_all.at[at, :], h_out.at[at, :], out_sem.at[7, image]),
        ]

    def other_copy(image):
        at = aligned(rows + image * PITCH, PITCH)
        return pltpu.make_async_copy(h_all.at[at, :], h_out.at[at, :], out_sem.at[8, image])

    def stage(tick, lag, run):
        image = tick - lag

        @pl.when((image >= 0) & (image < images))
        def _():
            run(image)

    def run_attend(image):
        attend(image)
        core_copy(image).start()
        for copy in out_copies(image)[0]:
            copy.start()

    def run_x(image):
        core_copy(image).wait_recv()
        x_to[image] = (mine[image] + core_from[image].astype(f32)).astype(bf16)
        x_copy(image).start()

    def run_total(image):
        x_copy(image).wait_recv()
        total_to[image] = (x_to[image].astype(f32) + x_from[image].astype(f32)).astype(bf16)
        total_copy(image).start()

    def run_norm(image):
        total_copy(image).wait_recv()
        part[:, my_cols] = total_to[image].astype(f32)
        part[:, their_cols] = total_from[image].astype(f32)
        resid = tok_ref[image].astype(f32) + part[...]
        resid_all[image] = resid
        normed, _ = norm_stats(resid)
        h_all[aligned(image * PITCH, PITCH), :] = (normed * gain2 + shift2).astype(bf16)
        y_copy(image).start()
        for copy in out_copies(image)[1]:
            copy.start()

    def run_relay(image):
        y_copy(image).wait_recv()
        relay_copy(image).start()

    def run_end(image):
        relay_arriving(image).wait_recv()
        other_copy(image).start()

    def cot_step_one():
        cot_x_in.wait_recv()
        cot_share[0].start()

        @pl.when(core_at == 0)
        def _():
            relay_y.start()

        kept_y.wait_recv()
        kept_share.start()

    def cot_step_two():
        cot_y_in.wait_recv()
        cot_share[1].start()

        @pl.when(core_at == 1)
        def _():
            relay_x.start()

    def weights_step_one():
        await_hops(0)
        start_hops(1)
        for copy in near_copies:
            copy.start()

    def weights_step_two():
        await_hops(1)
        start_hops(2)

    def cot_step_three():
        relay_in.wait_recv()
        cot_share[2].start()

    outs = [
        pltpu.make_async_copy(cot_all, cot_out, cot_sem.at[0]),
        pltpu.make_async_copy(kept_all, kept_out, cot_sem.at[1]),
    ]

    def ready_own():
        cot_share_in[0].wait_recv()
        for copy in (*own_copies, *near_copies):
            copy.wait()

    def ready_other():
        for copy in (cot_share_in[1], cot_share_in[2], kept_share_in):
            copy.wait_recv()
        for copy in outs:
            copy.start()

    def block_copies(number, place):
        at = aligned(number * BLOCK, BLOCK)
        pairs = ((mixed_slots, mixed_out), (grad_h_slots, grad_h_out), (gate_slots, gate_out))
        return [
            pltpu.make_async_copy(slots.at[place], out.at[at, :], block_sem.at[n, place])
            for n, (slots, out) in enumerate(pairs)
        ]

    def run_block(number, turn):
        at = aligned(number * BLOCK, BLOCK)
        h_rows, cot_rows = h_all[at, :], cot_all[at, :]
        up, down = up_vm[...], down_vm[...]
        hidden_rows, grad_pre, _, grad_gate = expert_math(
            h_rows, cot_rows, kept_all[at, :].astype(f32), router_ref[...], up, down, z_at // 2, experts
        )

        place = turn % 2

        @pl.when(turn >= 2)
        def _():
            for copy in block_copies(number, place):
                copy.wait()

        gate_slots[place] = grad_gate
        mixed_slots[place] = dot(hidden_rows, down).astype(bf16)
        grad_h_slots[place] = dot(grad_pre, up, ((1,), (1,))).astype(bf16)
        for copy in block_copies(number, place):
            copy.start()
        up_sum[...] += dot(h_rows.T, grad_pre)
        down_sum[...] += dot(cot_rows.T, hidden_rows)

    up_sum[...] = jnp.zeros_like(up_sum)
    down_sum[...] = jnp.zeros_like(down_sum)

    def take_tokens(number):
        first = number * SEQ // 16 * 16
        skip = number * SEQ - first
        taken = min(224, images * SEQ - first)
        rows_in = tok_raw[first : first + taken, :].astype(f32)[skip : skip + SEQ]
        padded = jnp.concatenate([rows_in, jnp.zeros((PITCH - SEQ, rows_in.shape[1]), f32)], axis=0)
        tok_ref[number] = padded.astype(bf16)

    def first_ticks(tick, _):
        for number in range(images):
            pl.when(tick == number)(partial(take_tokens, number))

        stage(tick, 0, run_attend)
        stage(tick, 1, run_x)
        return 0

    lax.fori_loop(0, images + 1, first_ticks, 0)
    pairs = images // 2

    def both(first, *runs):
        for run in runs:
            run(first)
            run(first + 1)

    cot_step_one()
    both(0, run_total, run_norm)
    cot_step_two()
    weights_step_one()
    ready_own()

    def per_turn(turn, _):
        @pl.when((turn <= 1) | (turn == 3))
        def _():
            both(jnp.where(turn == 3, 6, 2 * turn + 2), run_total, run_norm)

        @pl.when((turn >= 2) & (turn < pairs + 2))
        def _():
            both(2 * turn - 4, run_relay)

        @pl.when(turn == pairs)
        def _():
            weights_step_two()
            cot_step_three()
            ready_other()

        @pl.when(turn >= pairs)
        def _():
            both(2 * (turn - pairs), run_end)

        run_block(turn, turn)
        return 0

    lax.fori_loop(0, 2 * pairs, per_turn, 0)
    grad_up_vm[...] = up_sum[...].astype(bf16)
    grad_down_vm[...] = down_sum[...].astype(bf16)
    grad_copies = [
        pltpu.make_async_copy(grad_up_vm, grad_up_out, grad_sem.at[0]),
        pltpu.make_async_copy(grad_down_vm, grad_down_out, grad_sem.at[1]),
    ]
    for copy in grad_copies:
        copy.start()
    for copy in (swap, kept_y, kept_share, cot_x, cot_y, *cot_share):
        copy.wait_send()

    @pl.when(core_at == 0)
    def _():
        relay_y.wait_send()

    @pl.when(core_at == 1)
    def _():
        relay_x.wait_send()

    def drain(image, _):
        for copy in (core_copy, x_copy, total_copy, y_copy, relay_copy):
            copy(image).wait_send()
        first, second = out_copies(image)
        for copy in (*first, *second, other_copy(image)):
            copy.wait()
        return 0

    lax.fori_loop(0, images, drain, 0)
    for place in range(2):
        for copy in block_copies(0, place):
            copy.wait()

    await_hops(2)
    for step in range(3):
        for way in range(2):

            @pl.when(hop_goes(step, way))
            def _():
                for copy in hop(step, way):
                    copy.wait_send()

    for copy in (*grad_copies, *outs):
        copy.wait()


def run_forward(tok_raw, gain1, shift1, gain2, shift2, qkv_w, out_w, up, down, cot, kept, router, experts):
    images = tok_raw.shape[0] // SEQ
    rows = images * PITCH
    features = tok_raw.shape[1]
    share = out_w.shape[0]
    heads = share // HD
    hidden = up.shape[1]
    wide = features // 2
    vmem = pl.BlockSpec(memory_space=pltpu.VMEM)
    anywhere = pl.BlockSpec(memory_space=pl.ANY)
    shape = jax.ShapeDtypeStruct
    block = (images, PITCH, wide)
    dma = pltpu.SemaphoreType.DMA
    return pl.pallas_call(
        partial(forward_kernel, images=images, heads=heads, experts=experts),
        out_shape=[
            shape((images, PITCH, share), bf16),
            shape((images, PITCH, share), bf16),
            shape((images, PITCH, share), bf16),
            shape((images, PITCH, share), bf16),
            shape((images, PITCH, 128), f32),
            shape((rows, features), f32),
            shape((2 * rows, features), bf16),
            shape((2 * rows, features), bf16),
            shape((2 * rows, 128), bf16),
            shape((2, features, 2 * hidden), bf16),
            shape((2, 2 * hidden, features), bf16),
            shape((2 * rows, features), bf16),
            shape((2 * rows, features), bf16),
            shape((2 * rows, 128), f32),
            shape((features, 2 * hidden), bf16),
            shape((features, 2 * hidden), bf16),
            shape((images, PITCH, features), bf16),
        ],
        in_specs=[vmem] * 7 + [anywhere] * 2 + [vmem] * 3,
        out_specs=[anywhere] * 17,
        scratch_shapes=[
            pltpu.VMEM((images, PITCH, features), bf16),
            pltpu.VMEM((rows, share), bf16),
            pltpu.VMEM((features, 2 * hidden), bf16),
            pltpu.VMEM((2 * hidden, features), bf16),
            *[pltpu.VMEM((features, 2 * hidden), f32)] * 2,
            *[pltpu.VMEM((2, BLOCK, features), bf16)] * 2,
            pltpu.VMEM((2, BLOCK, 128), f32),
            *[pltpu.VMEM((features, 2 * hidden), bf16)] * 2,
            *[pltpu.VMEM((images, PITCH, share), bf16)] * 4,
            pltpu.VMEM((images, PITCH, 128), f32),
            pltpu.VMEM((images, PITCH, features), f32),
            pltpu.VMEM((2 * rows, features), bf16),
            pltpu.VMEM((2 * rows, features), bf16),
            pltpu.VMEM((2 * rows, 128), bf16),
            pltpu.VMEM((PITCH, features), f32),
            pltpu.VMEM(block, f32),
            pltpu.VMEM(block, bf16),
            pltpu.VMEM(block, bf16),
            pltpu.VMEM(block, bf16),
            pltpu.VMEM(block, bf16),
            pltpu.VMEM(block, bf16),
            pltpu.VMEM(block, bf16),
            pltpu.VMEM((rows, share), bf16),
        ]
        + [dma((images,))] * 10
        + [dma((2, 3, 2))] * 2
        + [dma((9,))] * 2
        + [dma((2,)), dma((2,)), dma((3, 2)), dma((2,)), dma((2,)), dma((9, images))],
        compiler_params=pltpu.CompilerParams(
            collective_id=1, has_side_effects=True, vmem_limit_bytes=63 << 20
        ),
    )(tok_raw, gain1, shift1, gain2, shift2, qkv_w, out_w, up, down, cot, kept, router)


def turn_is_other(turn):
    return (turn == 0) | ((turn % 2 == 1) & (turn < 7))


def turn_block(turn):
    own = jnp.where(turn == 7, 3, turn // 2 - 1)
    return jnp.where(turn_is_other(turn), 4 + (turn + 1) // 2, own)


def second_pair_kernel(
    h_ref,
    cot_ref,
    kept_ref,
    router_ref,
    mixed_first,
    grad_h_first,
    gate_first,
    up_all,
    down_all,
    up_first,
    down_first,
    mixed_ref,
    grad_up_ref,
    grad_down_ref,
    grad_router_ref,
    grad_h_out,
    up_pair,
    down_pair,
    line_first,
    up_vm,
    down_vm,
    up_sum,
    down_sum,
    router_sum,
    ring,
    from_core,
    from_y,
    from_x,
    load,
    core_s,
    core_r,
    y_s,
    y_r,
    x_s,
    x_r,
    tot_s,
    tot_r,
    store,
    pair_s,
    pair_r,
    line_s,
    line_r,
    *,
    experts,
    steps,
):
    turn = pl.program_id(0)
    expert_at = lax.axis_index("expert")
    tensor_at = lax.axis_index("tensor")
    z_at, y_at = expert_at // 2, expert_at % 2
    x_at, core_at = tensor_at // 2, tensor_at % 2
    hidden = up_pair.shape[1]
    wide = ring.shape[2] // 2
    core_dev = (expert_at, tensor_at + 1 - 2 * core_at)
    x_dev = (expert_at, tensor_at + 2 - 4 * x_at)
    y_dev = (expert_at + 1 - 2 * y_at, tensor_at)
    my_cols = lanes_at(core_at * wide, wide)
    their_cols = lanes_at((1 - core_at) * wide, wide)

    def remote(src, dst, send, recv, device):
        return pltpu.make_async_remote_copy(
            src_ref=src, dst_ref=dst, send_sem=send, recv_sem=recv, device_id=device, device_id_type=MESH
        )

    def core_copy(number):
        return remote(ring.at[number % 2, :, their_cols], from_core.at[number], core_s.at[number], core_r.at[number], core_dev)

    def y_copy(number, place):
        return remote(from_core.at[number], from_y.at[place], y_s.at[place], y_r.at[place], y_dev)

    def x_copy(number, place):
        return remote(from_core.at[number], from_x.at[place], x_s.at[place], x_r.at[place], x_dev)

    def out_rows(place):
        return grad_h_out.at[aligned(place * BLOCK, BLOCK), my_cols]

    def total_copy(place):
        return remote(from_x.at[place], out_rows(place), tot_s.at[place], tot_r.at[place], core_dev)

    def store_copy(place):
        return pltpu.make_async_copy(from_x.at[place], out_rows(place), store.at[place])

    def own_turn(place):
        return jnp.where(place == 3, 7, 2 * place + 2)

    def other_turn(place):
        return jnp.where(place == 0, 0, 2 * place - 1)

    def pass_other(number):
        core_copy(number).wait_recv()
        from_core[number] = from_core[number] + ring[number % 2, :, my_cols]
        y_copy(number, (number + 1) // 2).start()

    def pass_own(number, place):
        core_copy(number).wait_recv()
        y_copy(number, place).wait_recv()
        total = from_core[number].astype(f32) + ring[number % 2, :, my_cols].astype(f32) + from_y[place].astype(f32)
        from_core[number] = total.astype(bf16)
        x_copy(number, place).start()

    def pass_total(place):
        number = own_turn(place)
        x_copy(number, place).wait_recv()
        from_x[place] = from_core[number] + from_x[place]
        total_copy(place).start()
        store_copy(place).start()

    z_dev = (jnp.where(z_at % 2 == 0, expert_at + 2, expert_at - 2), tensor_at)
    pair_lanes = lanes_at((1 - z_at % 2) * hidden, hidden)
    pair_copies = [
        remote(source.at[:, pair_lanes], target, pair_s.at[number], pair_r.at[number], z_dev)
        for number, (source, target) in enumerate(((up_first, up_pair), (down_first, down_pair)))
    ]

    far_lanes = lanes_at(jnp.where(z_at == 0, 1, 0) * hidden, hidden)
    line_copy = remote(grad_up_ref.at[:, far_lanes], line_first, line_s.at[0], line_r.at[0], z_dev)
    is_outer = (z_at == 0) | (z_at == lax.axis_size("expert") // 2 - 1)

    @pl.when(turn == 0)
    def _():
        greet([(True, core_dev), (True, x_dev), (True, y_dev), (True, z_dev)])
        for copy in pair_copies:
            copy.start()
        whole = [
            pltpu.make_async_copy(up_all.at[1], up_vm, load.at[0]),
            pltpu.make_async_copy(down_all.at[1], down_vm, load.at[1]),
        ]
        for copy in whole:
            copy.start()
        up_sum[...] = jnp.zeros_like(up_sum)
        down_sum[...] = jnp.zeros_like(down_sum)
        router_sum[...] = jnp.zeros_like(router_sum)
        for copy in whole:
            copy.wait()

    h_rows, cot_rows = h_ref[...], cot_ref[...]
    up, down, router = up_vm[...], down_vm[...], router_ref[...]
    kept = kept_ref[...].astype(f32)
    hidden_rows, grad_pre, probs, grad_gate = expert_math(
        h_rows, cot_rows, kept, router, up, down, 1 - z_at // 2, experts
    )
    grad_gate = kept * (grad_gate + gate_first[...])
    grad_logits = (probs * (grad_gate - jnp.sum(probs * grad_gate, axis=1, keepdims=True))).astype(bf16)

    before = turn - 1

    @pl.when((turn >= 1) & turn_is_other(before))
    def _():
        pass_other(before)

    @pl.when((turn == 5) | (turn == 7))
    def _():
        pass_total((turn - 5) // 2)

    @pl.when((turn == 3) | (turn == 5) | (turn == 7))
    def _():
        pass_own(before, (turn - 3) // 2)


    @pl.when(turn >= 2)
    def _():
        core_copy(turn - 2).wait_send()

    ring[turn % 2] = (
        grad_h_first[...].astype(f32) + dot(grad_pre, up, ((1,), (1,))) + dot(grad_logits, router)
    ).astype(bf16)
    core_copy(turn).start()
    mixed_ref[...] = (mixed_first[...].astype(f32) + dot(hidden_rows, down)).astype(bf16)
    h_turned = h_rows.T
    up_sum[...] += dot(h_turned, grad_pre)
    router_sum[...] += dot(h_turned, grad_logits)
    down_sum[...] += dot(cot_rows.T, hidden_rows)

    @pl.when(turn == steps - 1)
    def _():
        grad_up_ref[...] = up_sum[...].astype(bf16)

        @pl.when(is_outer)
        def _():
            line_copy.start()

        pass_own(7, 3)
        pass_total(2)
        grad_down_ref[...] = down_sum[...].astype(bf16)
        grad_router_ref[...] = router_sum[...].T[:8]
        pass_total(3)
        for copy in pair_copies:
            copy.wait()

        @pl.when(is_outer)
        def _():
            line_copy.wait_send()

        @pl.when(jnp.logical_not(is_outer))
        def _():
            line_copy.wait_recv()

        for number in (6, 7):
            core_copy(number).wait_send()
        for place in range(4):
            y_copy(other_turn(place), place).wait_send()
            x_copy(own_turn(place), place).wait_send()
            total_copy(place).wait_send()
            total_copy(place).wait_recv()
            store_copy(place).wait()


def run_second_pair(
    h_rows,
    cot_rows,
    kept,
    router,
    mixed_first,
    grad_h_first,
    gate_first,
    up,
    down,
    up_first,
    down_first,
    experts,
):
    rows, features = h_rows.shape
    width = up.shape[2]
    steps = rows // BLOCK
    half = (BLOCK, features // 2)
    anywhere = pl.BlockSpec(memory_space=pl.ANY)
    shape = jax.ShapeDtypeStruct
    dma = pltpu.SemaphoreType.DMA

    def by_step(lanes):
        return pl.BlockSpec((BLOCK, lanes), lambda n: (turn_block(n), 0))

    def whole(*dims):
        return pl.BlockSpec(dims, lambda n: (0,) * len(dims))

    return pl.pallas_call(
        partial(second_pair_kernel, experts=experts, steps=steps),
        grid=(steps,),
        out_shape=[
            shape((rows, features), bf16),
            shape((features, width), bf16),
            shape((features, width), bf16),
            shape((8, features), f32),
            shape((rows // 2, features), bf16),
            shape((features, width // 2), bf16),
            shape((features, width // 2), bf16),
            shape((features, width // 2), bf16),
        ],
        in_specs=[
            by_step(features),
            by_step(features),
            by_step(128),
            whole(128, features),
            by_step(features),
            by_step(features),
            by_step(128),
        ]
        + [anywhere] * 4,
        out_specs=[by_step(features), whole(features, width), whole(features, width), whole(8, features)] + [anywhere] * 4,
        scratch_shapes=[
            pltpu.VMEM((features, width), bf16),
            pltpu.VMEM((width, features), bf16),
            pltpu.VMEM((features, width), f32),
            pltpu.VMEM((features, width), f32),
            pltpu.VMEM((features, 128), f32),
            pltpu.VMEM((2, BLOCK, features), bf16),
            pltpu.VMEM((8, *half), bf16),
            pltpu.VMEM((4, *half), bf16),
            pltpu.VMEM((4, *half), bf16),
            dma((2,)),
        ]
        + [dma((8,))] * 2
        + [dma((4,))] * 7
        + [dma((2,))] * 2
        + [dma((1,))] * 2,
        compiler_params=pltpu.CompilerParams(
            collective_id=4, has_side_effects=True, vmem_limit_bytes=60 << 20
        ),
    )(h_rows, cot_rows, kept, router, mixed_first, grad_h_first, gate_first, up, down, up_first, down_first)


def backward_kernel(
    gain1_ref,
    shift1_ref,
    gain2_ref,
    qkv_ref,
    out_w_ref,
    grad_router_ref,
    tok_hbm,
    q_hbm,
    k_hbm,
    v_hbm,
    att_hbm,
    lse_hbm,
    grad_h_hbm,
    resid_ref,
    cot_ref,
    mixed_ref,
    up_second,
    down_second,
    line_first,
    line_out,
    tokens_out,
    weights_out,
    sums_out,
    mixed_out,
    tok_ref,
    q_ref,
    k_ref,
    v_ref,
    att_ref,
    lse_ref,
    grad_h_ref,
    rows_kept,
    cot_rows,
    m_mine,
    m_core,
    m_y,
    m_x,
    m_out,
    m_resid,
    far_vm,
    one_mine,
    one_to,
    one_core,
    one_x,
    one_total,
    line,
    weight_sum,
    weight_half,
    shared,
    shared_y,
    shared_line,
    shared_all,
    route_core,
    route_x,
    late_mine,
    late_y,
    late_z,
    sums_all,
    tokens_low,
    whole,
    mc_s,
    mc_r,
    my_s,
    my_r,
    mx_s,
    mx_r,
    mq_s,
    mq_r,
    m_store,
    oc_s,
    oc_r,
    ox_s,
    ox_r,
    ot_s,
    ot_r,
    l_s,
    l_r,
    sy_s,
    sy_r,
    sl_s,
    sl_r,
    sg_s,
    sg_r,
    sz_s,
    sz_r,
    r_s,
    r_r,
    late_s,
    late_r,
    load,
    image_load,
    own_sem,
    weight_store,
    store,
    *,
    images,
    heads,
):
    expert_at = lax.axis_index("expert")
    tensor_at = lax.axis_index("tensor")
    z_at, y_at = expert_at // 2, expert_at % 2
    z_last = lax.axis_size("expert") // 2 - 1
    x_at, core_at = tensor_at // 2, tensor_at % 2
    other = 1 - core_at
    rows = images * PITCH
    features = tok_hbm.shape[2]
    wide = features // 2
    share = out_w_ref.shape[0]
    hidden = line.shape[3]
    core_dev = (expert_at, tensor_at + 1 - 2 * core_at)
    x_dev = (expert_at, tensor_at + 2 - 4 * x_at)
    y_dev = (expert_at + 1 - 2 * y_at, tensor_at)
    z_devs = [(expert_at + 2, tensor_at), (expert_at - 2, tensor_at)]
    planes = z_last + 1
    z_others = [((z_at + hop) % planes * 2 + y_at, tensor_at) for hop in (1, 2, 3)]
    greet([(True, device) for device in (core_dev, x_dev, y_dev, *z_others)])
    my_cols = lanes_at(core_at * wide, wide)
    their_cols = lanes_at(other * wide, wide)

    def remote(src, dst, send, recv, device):
        return pltpu.make_async_remote_copy(
            src_ref=src, dst_ref=dst, send_sem=send, recv_sem=recv, device_id=device, device_id_type=MESH
        )

    def at_image(image):
        return aligned(image * PITCH, PITCH)

    part_count = m_y.shape[0]
    part_rows_m = rows // part_count

    def m_rows(side, part):
        return aligned(side * rows + part * part_rows_m, part_rows_m)

    def m_core_copy(side, part):
        at = m_rows(side, part)
        return remote(mixed_ref.at[at, their_cols], m_core.at[at, :], mc_s.at[side, part], mc_r.at[side, part], core_dev)

    for part in range(part_count):
        m_core_copy(1, part).start()
    for part in range(part_count):
        m_core_copy(0, part).start()
    m_loads = [
        pltpu.make_async_copy(mixed_ref.at[pl.ds(side * rows, rows), my_cols], m_mine.at[pl.ds(side * rows, rows), :], load.at[side])
        for side in range(2)
    ]

    def image_loads(image):
        at = at_image(image)
        by_image = ((tok_hbm, tok_ref), (q_hbm, q_ref), (k_hbm, k_ref), (v_hbm, v_ref), (att_hbm, att_ref), (lse_hbm, lse_ref))
        by_row = ((grad_h_hbm, grad_h_ref), (resid_ref, rows_kept), (cot_ref, cot_rows))
        pairs = [(source.at[image], target.at[image]) for source, target in by_image]
        pairs += [(source.at[at, :], target.at[at, :]) for source, target in by_row]
        return [pltpu.make_async_copy(source, target, image_load.at[n, image]) for n, (source, target) in enumerate(pairs)]

    def start_loads(image, _):
        for copy in image_loads(image):
            copy.start()
        return 0

    start_loads(0, 0)
    m_loads[1].start()
    lax.fori_loop(1, images, start_loads, 0)
    m_loads[0].start()
    route_one = remote(grad_router_ref, route_core, r_s.at[0], r_r.at[0], core_dev)
    route_one.start()

    def place(way):
        return z_at if way == 0 else z_last - z_at

    def far_lanes(way, piece):
        expert = z_last - piece // 2 if way == 0 else piece // 2
        return pl.ds(expert % 2 * hidden, hidden)

    def line_copy(source, way, piece):
        return remote(source, line.at[way, piece], l_s.at[way, piece], l_r.at[way, piece], z_devs[way])

    def line_copy_on(way, piece):
        return line_copy(line.at[way, piece], way, piece)

    def line_start():
        for way in range(2):

            @pl.when(place(way) == 0)
            def _():
                for piece in range(1, 4):
                    source = (up_second, down_second)[piece % 2]
                    line_copy(source.at[:, far_lanes(way, piece)], way, piece).start()

    def line_add(piece):
        for way in range(2):

            @pl.when(place(way) == 1)
            def _():
                if piece > 0:
                    line_copy_on(way, piece).wait_recv()
                lanes = far_lanes(way, piece)

                def add(part, _):
                    at_rows = aligned(part * 96, 96)
                    total = line[way, piece, at_rows, :].astype(f32) + far_vm[piece % 2, at_rows, lanes].astype(f32)
                    line[way, piece, at_rows, :] = total.astype(bf16)
                    return 0

                lax.fori_loop(0, features // 96, add, 0)
                line_copy_on(way, piece).start()

    def line_pass(piece):
        for way in range(2):

            @pl.when(place(way) == 2)
            def _():
                line_copy_on(way, piece).wait_recv()
                line_copy_on(way, piece).start()

    line_start()
    later = [
        pltpu.make_async_copy((up_second, down_second)[number], far_vm.at[number], own_sem.at[number])
        for number in range(2)
    ]
    is_inner = (z_at == 1) | (z_at == z_last - 1)
    first_copy = pltpu.make_async_copy(line_first, line.at[jnp.where(z_at == 1, 0, 1), 0], own_sem.at[2])

    @pl.when(is_inner)
    def _():
        first_copy.start()

    for copy in later:
        copy.start()
    weight_sum[...] = jnp.zeros_like(weight_sum)
    late_mine[...] = jnp.zeros_like(late_mine)

    def m_y_copy(part):
        return remote(m_core.at[m_rows(1, part), :], m_y.at[part], my_s.at[part], my_r.at[part], y_dev)

    def m_x_copy(part):
        return remote(m_core.at[m_rows(0, part), :], m_x.at[part], mx_s.at[part], mx_r.at[part], x_dev)

    def m_place(part):
        return mixed_out.at[aligned(part * part_rows_m, part_rows_m), :]

    def m_quarter_copy(part):
        return remote(m_out.at[part, other], m_place(part), mq_s.at[part], mq_r.at[part], core_dev)

    def m_store_copy(part):
        return pltpu.make_async_copy(m_out.at[part, core_at], m_place(part), m_store.at[part])

    def m_resid_copy(part):
        at = aligned(part * part_rows_m, part_rows_m)
        return pltpu.make_async_copy(resid_ref.at[at, lanes_at(x_at * wide, wide)], m_resid, load.at[3])

    keeps = x_at == core_at

    def run_m_y(part):
        m_core_copy(1, part).wait_recv()
        at = m_rows(1, part)
        m_core[at, :] = (m_core[at, :].astype(f32) + m_mine[at, :].astype(f32)).astype(bf16)
        m_y_copy(part).start()

    def run_m_x(part):
        if isinstance(part, int) and part == 0:
            m_loads[0].wait()
        m_core_copy(0, part).wait_recv()
        m_y_copy(part).wait_recv()
        at = m_rows(0, part)
        total = m_core[at, :].astype(f32) + m_mine[at, :].astype(f32) + m_y[part].astype(f32)
        m_core[at, :] = total.astype(bf16)

        @pl.when(jnp.logical_not(keeps))
        def _():
            m_x_copy(part).start()

    def run_m_out(part):
        @pl.when(keeps)
        def _():
            m_resid_copy(part).start()
            m_x_copy(part).wait_recv()
            m_resid_copy(part).wait()
            total = m_core[m_rows(0, part), :].astype(f32) + m_x[part].astype(f32)
            mixed = (m_resid[...] + total).astype(bf16)
            m_out[part, 0] = mixed[:, : wide // 2]
            m_out[part, 1] = mixed[:, wide // 2 :]
            m_quarter_copy(part).start()
            m_store_copy(part).start()

    m_loads[1].wait()
    for part in range(part_count):
        run_m_y(part)
    later[0].wait()
    later[1].wait()

    @pl.when(is_inner)
    def _():
        first_copy.wait()

    line_add(0)
    route_one.wait_recv()
    route_core[...] += grad_router_ref[...]
    route_two = remote(route_core, route_x, r_s.at[1], r_r.at[1], x_dev)
    route_two.start()

    def one_core_copy(image):
        return remote(one_to.at[image], one_core.at[image], oc_s.at[image], oc_r.at[image], core_dev)

    def one_x_copy(image):
        return remote(one_core.at[image], one_x.at[image], ox_s.at[image], ox_r.at[image], x_dev)

    def one_total_copy(image):
        return remote(one_x.at[image], one_total.at[image], ot_s.at[image], ot_r.at[image], core_dev)

    store_copy = pltpu.make_async_copy(tokens_low, tokens_out, store.at[0])

    lane = lax.broadcasted_iota(jnp.int32, (PITCH, 2 * HD), 1)
    key_mask = lax.broadcasted_iota(jnp.int32, (PITCH, PITCH), 1) < SEQ
    gain1, shift1, gain2 = (ref[...].reshape(1, features) for ref in (gain1_ref, shift1_ref, gain2_ref))

    def norm_back(grad, gain, normed, inverse):
        scaled = grad * gain
        mean = jnp.mean(scaled, axis=1, keepdims=True)
        along = jnp.mean(scaled * normed, axis=1, keepdims=True)
        return (scaled - mean - normed * along) * inverse

    def add_sums(sums, row, grad, normed):
        sums[row : row + 1, :] += jnp.sum(grad * normed, axis=0, keepdims=True)
        sums[row + 1 : row + 2, :] += jnp.sum(grad, axis=0, keepdims=True)

    def run_attention(image):
        for copy in image_loads(image):
            copy.wait()
        at = at_image(image)
        grad_h = grad_h_ref[at, :].astype(f32)
        normed, inverse = norm_stats(rows_kept[at, :])
        add_sums(late_mine, 2, grad_h, normed)
        grad_resid = cot_rows[at, :].astype(f32) + norm_back(grad_h, gain2, normed, inverse)
        rows_kept[at, :] = grad_resid
        grad_branch = grad_resid.astype(bf16)
        token_normed, _ = norm_stats(tok_ref[image].astype(f32))
        h_one = (token_normed * gain1 + shift1).astype(bf16)
        queries, keys, values, attended = q_ref[image], k_ref[image], v_ref[image], att_ref[image]
        lse = lse_ref[image]
        grad_attended = dot(grad_branch, out_w_ref[...], ((1,), (1,))).astype(bf16)
        grads = [[], [], []]
        for head in range(heads):
            first = head // 2 * 2 * HD
            last = min(first + 2 * HD, heads * HD)
            parts = [whose[:, first:last] for whose in (queries, keys, values, grad_attended)]
            if last - first == 2 * HD:
                own = head_mask(lane, head)
                q_own, k_own, _, g_own = (jnp.where(own, part, jnp.zeros_like(part)) for part in parts)
            else:
                q_own, k_own, _, g_own = parts
            scores = dot(q_own, parts[1], ((1,), (1,))) * (HD**-0.5)
            probs = jnp.where(key_mask, jnp.exp(scores - lse[:, head : head + 1]), 0.0)
            back = dot(g_own, parts[2], ((1,), (1,)))
            product = probs * back
            grad_scores = (product - probs * jnp.sum(product, axis=1, keepdims=True)).astype(bf16)
            pieces = (
                dot(grad_scores, k_own) * (HD**-0.5),
                dot(grad_scores, q_own, ((0,), (0,))) * (HD**-0.5),
                dot(probs.astype(bf16), g_own, ((0,), (0,))),
            )
            for which in range(3):
                if head % 2 == 0:
                    grads[which].append(pieces[which])
                else:
                    grads[which][-1] += pieces[which]
        grad_rows = [jnp.concatenate(grads[which], axis=1).astype(bf16) for which in range(3)]
        grad_one = 0.0
        for which in range(3):
            weight_sum[which * share : (which + 1) * share, :] += dot(grad_rows[which].T, h_one)
            grad_one += dot(grad_rows[which], qkv_ref[which])
        weight_sum[3 * share : 4 * share, :] += dot(attended.T, grad_branch)
        whole[...] = grad_one
        one_mine[image] = whole[:, my_cols].astype(bf16)
        one_to[image] = whole[:, their_cols].astype(bf16)
        one_core_copy(image).start()

    def run_one_x(image):
        one_core_copy(image).wait_recv()
        one_core[image] = (one_core[image].astype(f32) + one_mine[image].astype(f32)).astype(bf16)
        one_x_copy(image).start()

    def run_one_total(image):
        one_x_copy(image).wait_recv()
        one_x[image] = (one_core[image].astype(f32) + one_x[image].astype(f32)).astype(bf16)
        one_total_copy(image).start()

    def run_tokens(image):
        one_total_copy(image).wait_recv()
        whole[:, my_cols] = one_x[image].astype(f32)
        whole[:, their_cols] = one_total[image].astype(f32)
        grad_one = whole[...]
        at = at_image(image)
        normed, inverse = norm_stats(tok_ref[image].astype(f32))
        add_sums(late_mine, 0, grad_one, normed)
        total = rows_kept[at, :] + norm_back(grad_one, gain1, normed, inverse)
        whole[...] = total
        for number in range(images):

            @pl.when(image == number)
            def _():
                rows_kept[pl.ds(number * SEQ, SEQ), :] = whole[pl.ds(0, SEQ), :]


    def stage(tick, lag, run):
        image = tick - lag

        @pl.when((image >= 0) & (image < images))
        def _():
            run(image)

    def at_tick(tick, when, run):
        @pl.when(tick == when)
        def _():
            run()

    def line_second():
        line_add(1)
        line_pass(0)

    def line_third():
        line_add(2)
        line_pass(1)

    def per_tick(tick, _):
        stage(tick, 0, run_attention)
        stage(tick, 1, run_one_x)
        stage(tick, 4, run_one_total)
        stage(tick, 5, run_tokens)
        at_tick(tick, 5, lambda: run_m_x(0))
        at_tick(tick, 3, line_second)
        at_tick(tick, 6, line_third)
        at_tick(tick, 7, lambda: run_m_x(1))
        return 0

    lax.fori_loop(0, images, per_tick, 0)

    part_rows = shared.shape[1]
    quarter = part_rows // (z_last + 1)

    def to_half(side):
        def cast(piece, _):
            at_rows = aligned(piece * quarter, quarter)
            shared[side, at_rows, :] = weight_sum[aligned(side * part_rows + piece * quarter, quarter), :].astype(bf16)
            return 0

        lax.fori_loop(0, z_last + 1, cast, 0)

    to_half(0)
    to_half(1)

    def y_piece(number):
        inner = jnp.where(z_at == 1, jnp.where(number < 2, z_last - number, number - 2), jnp.where(number < 2, number, 5 - number))
        return jnp.where(z_at == 0, z_last - number, jnp.where(z_at == z_last, number, inner))

    def quarter_at(piece):
        return aligned(piece * quarter, quarter)

    def shared_y_copy(number):
        at_rows = quarter_at(y_piece(number))
        return remote(shared.at[1 - y_at, at_rows, :], shared_y.at[at_rows, :], sy_s.at[number], sy_r.at[number], y_dev)

    def take_y(number):
        shared_y_copy(number).wait_recv()
        at_rows = quarter_at(y_piece(number))
        weight_half[at_rows, :] = shared[y_at, at_rows, :].astype(f32) + shared_y[at_rows, :].astype(f32)

    for number in range(4):
        shared_y_copy(number).start()
    run_one_x(images - 1)
    run_m_x(part_count - 2)
    run_one_total(images - 4)
    run_tokens(images - 5)

    def quarter_of(step, at, way):
        mirrored = z_last - step + at
        return mirrored if way == 0 else z_last - mirrored

    late_y_copy = remote(late_mine, late_y, late_s.at[0], late_r.at[0], y_dev)

    def late_copy(number):
        ref = late_z.at[z_at]
        return remote(ref, ref, late_s.at[number + 1], late_r.at[number + 1], z_others[number])

    def small_copy(step, way):
        return remote(shared_line.at[way, 0, step], shared_line.at[way, 1, step], sl_s.at[way, step], sl_r.at[way, step], z_devs[way])

    for step in range(3):
        take_y(step)
        if step == 2:
            take_y(3)
        for way in range(2):
            at = place(way)

            @pl.when((at <= step) & (at < z_last))
            def _():
                at_rows = quarter_at(quarter_of(step, at, way))
                if step == 0:
                    shared_line[way, 0, step] = weight_half[at_rows, :].astype(bf16)
                else:
                    came = jnp.where(at > 0, shared_line[way, 1, step - 1].astype(f32), 0.0)
                    shared_line[way, 0, step] = (weight_half[at_rows, :] + came).astype(bf16)
                small_copy(step, way).start()

        for way in range(2):
            at = place(way)

            @pl.when((at > 0) & (at - 1 <= step))
            def _():
                small_copy(step, way).wait_recv()

        if step == 0:
            run_m_x(part_count - 1)
            run_one_total(images - 3)
            run_tokens(images - 4)
            run_m_out(0)
        if step == 1:
            run_one_total(images - 2)
            run_tokens(images - 3)
            run_m_out(1)

    own_rows = quarter_at(z_at)
    from_below = jnp.where(z_at > 0, shared_line[0, 1, 2].astype(f32), 0.0)
    from_above = jnp.where(z_at < z_last, shared_line[1, 1, 2].astype(f32), 0.0)

    def final_rows(side, piece):
        return shared_all.at[side, quarter_at(piece), :]

    shared_all[y_at, own_rows, :] = (weight_half[own_rows, :] + from_below + from_above).astype(bf16)
    for number in range(4):
        shared_y_copy(number).wait_send()

    def gather_z(step, way, piece):
        ref = final_rows(y_at, piece)
        return remote(ref, ref, sg_s.at[way, step], sg_r.at[way, step], z_devs[way])

    def gather_y(step, way, piece, side):
        ref = final_rows(side, piece)
        return remote(ref, ref, sz_s.at[way, step], sz_r.at[way, step], y_dev)

    gather_y(0, 0, z_at, y_at).start()

    def between(step):
        if step == 0:
            run_one_total(images - 1)
            run_tokens(images - 2)
        if step == 1:
            run_tokens(images - 1)
            line_add(3)
            route_two.wait_recv()
            late_mine[8:16, :] = route_core[...] + route_x[...]
            late_y_copy.start()
            tokens_low[...] = rows_kept[pl.ds(0, images * SEQ), :].astype(bf16)
            store_copy.start()
            run_m_out(part_count - 2)
        if step == 2:
            run_m_out(part_count - 1)
            late_y_copy.wait_recv()
            late_z[z_at] = late_mine[...] + late_y[...]
            for number in range(planes - 1):
                late_copy(number).start()

    for step in range(3):
        for way in range(2):
            at = place(way)
            piece = z_at - step if way == 0 else z_at + step

            @pl.when((at >= step) & (at < z_last))
            def _():
                gather_z(step, way, piece).start()

        between(step)
        for way in range(2):
            at = place(way)
            piece = z_at - 1 - step if way == 0 else z_at + 1 + step

            @pl.when(at >= 1 + step)
            def _():
                gather_z(step, way, piece).wait_recv()
                gather_y(step + 1, way, piece, y_at).start()

    for way in range(2):

        @pl.when(place(way) == 2)
        def _():
            line_copy_on(way, 2).wait_recv()
            line_copy_on(way, 3).wait_recv()

        @pl.when(place(way) == z_last)
        def _():
            line_copy_on(way, 0).wait_recv()
            line_copy_on(way, 1).wait_recv()

    from_far = 1 - z_at // 2
    first_piece = jnp.where((z_at == 0) | (z_at == z_last), 0, 2)

    line_out_copies = [
        pltpu.make_async_copy(line.at[from_far, first_piece + n], line_out.at[n], weight_store.at[n]) for n in range(2)
    ]
    for copy in line_out_copies:
        copy.start()
    gather_y(0, 0, z_at, 1 - y_at).wait_recv()
    for step in range(3):
        for way in range(2):
            at = place(way)
            piece = z_at - 1 - step if way == 0 else z_at + 1 + step

            @pl.when(at >= 1 + step)
            def _():
                gather_y(step + 1, way, piece, 1 - y_at).wait_recv()

    for number in range(planes - 1):
        late_copy(number).wait_recv()
    late = late_z[0]
    for plane in range(1, planes):
        late += late_z[plane]
    sums_all[...] = late
    out_copies = [
        pltpu.make_async_copy(shared_all, weights_out, weight_store.at[2]),
        pltpu.make_async_copy(sums_all, sums_out, weight_store.at[3]),
    ]
    for copy in out_copies:
        copy.start()
    route_one.wait_send()
    route_two.wait_send()

    def drain(image, _):
        for copy in (one_core_copy, one_x_copy, one_total_copy):
            copy(image).wait_send()
        return 0

    lax.fori_loop(0, images, drain, 0)
    for part in range(part_count):
        m_core_copy(0, part).wait_send()
        m_core_copy(1, part).wait_send()
        m_y_copy(part).wait_send()

        @pl.when(keeps)
        def _():
            m_quarter_copy(part).wait_send()
            m_store_copy(part).wait()

        @pl.when(jnp.logical_not(keeps))
        def _():
            m_x_copy(part).wait_send()
            m_quarter_copy(part).wait_recv()

    for copy in (*line_out_copies, *out_copies, store_copy):
        copy.wait()
    late_y_copy.wait_send()
    for number in range(planes - 1):
        late_copy(number).wait_send()
    gather_y(0, 0, z_at, y_at).wait_send()
    for way in range(2):

        @pl.when(place(way) <= 1)
        def _():
            for piece in range(1, 4):
                line_copy_on(way, piece).wait_send()

        @pl.when(place(way) == 1)
        def _():
            line_copy_on(way, 0).wait_send()

        @pl.when(place(way) == 2)
        def _():
            for piece in range(2):
                line_copy_on(way, piece).wait_send()

    for step in range(3):
        for way in range(2):
            at = place(way)

            @pl.when((at <= step) & (at < z_last))
            def _():
                small_copy(step, way).wait_send()

            piece = z_at - step if way == 0 else z_at + step

            @pl.when((at >= step) & (at < z_last))
            def _():
                gather_z(step, way, piece).wait_send()

            piece = z_at - 1 - step if way == 0 else z_at + 1 + step

            @pl.when(at >= 1 + step)
            def _():
                gather_y(step + 1, way, piece, y_at).wait_send()


def run_backward(gain1, shift1, gain2, qkv_w, out_w, grad_router, tok, *streamed):
    images, _, features = tok.shape
    rows = images * PITCH
    share = out_w.shape[0]
    heads = share // HD
    hidden = streamed[-1].shape[1]
    wide = features // 2
    parts = 4
    vmem = pl.BlockSpec(memory_space=pltpu.VMEM)
    anywhere = pl.BlockSpec(memory_space=pl.ANY)
    shape = jax.ShapeDtypeStruct
    dma = pltpu.SemaphoreType.DMA
    block = (images, PITCH, wide)
    return pl.pallas_call(
        partial(backward_kernel, images=images, heads=heads),
        out_shape=[
            shape((2, features, hidden), bf16),
            shape((images * SEQ, features), bf16),
            shape((2, features // 2, features), bf16),
            shape((16, features), f32),
            shape((rows, wide // 2), bf16),
        ],
        in_specs=[vmem] * 6 + [anywhere] * (1 + len(streamed)),
        out_specs=[anywhere] * 5,
        scratch_shapes=[
            pltpu.VMEM((images, PITCH, features), bf16),
            *[pltpu.VMEM((images, PITCH, share), bf16)] * 4,
            pltpu.VMEM((images, PITCH, 128), f32),
            pltpu.VMEM((rows, features), bf16),
            pltpu.VMEM((rows, features), f32),
            pltpu.VMEM((rows, features), bf16),
            pltpu.VMEM((2 * rows, wide), bf16),
            pltpu.VMEM((2 * rows, wide), bf16),
            *[pltpu.VMEM((parts, rows // parts, wide), bf16)] * 2,
            pltpu.VMEM((parts, 2, rows // parts, wide // 2), bf16),
            pltpu.VMEM((rows // parts, wide), f32),
            pltpu.VMEM((2, features, 2 * hidden), bf16),
            *[pltpu.VMEM(block, bf16)] * 5,
            pltpu.VMEM((2, 4, features, hidden), bf16),
            pltpu.VMEM((features, features), f32),
            pltpu.VMEM((features // 2, features), f32),
            pltpu.VMEM((2, features // 2, features), bf16),
            pltpu.VMEM((features // 2, features), bf16),
            pltpu.VMEM((2, 2, 3, features // 8, features), bf16),
            pltpu.VMEM((2, features // 2, features), bf16),
            *[pltpu.VMEM((8, features), f32)] * 2,
            *[pltpu.VMEM((16, features), f32)] * 2,
            pltpu.VMEM((4, 16, features), f32),
            pltpu.VMEM((16, features), f32),
            pltpu.VMEM((images * SEQ, features), bf16),
            pltpu.VMEM((PITCH, features), f32),
        ]
        + [dma((2, parts))] * 2
        + [dma((parts,))] * 7
        + [dma((images,))] * 6
        + [dma((2, 4))] * 2
        + [dma((4,))] * 2
        + [dma((2, 3))] * 4
        + [dma((2, 4))] * 2
        + [dma((2,))] * 2
        + [dma((4,))] * 2
        + [dma((4,)), dma((9, images)), dma((3,)), dma((4,)), dma((1,))],
        compiler_params=pltpu.CompilerParams(
            collective_id=2, has_side_effects=True, vmem_limit_bytes=63 << 20
        ),
    )(gain1, shift1, gain2, qkv_w, out_w, grad_router, tok, *streamed)


def per_image(rows_in):
    images = rows_in.shape[0] // SEQ
    blocks = rows_in.reshape(images, SEQ, rows_in.shape[1])
    return jnp.pad(blocks, ((0, 0), (0, PITCH - SEQ), (0, 0)))


def unpad(blocks):
    images = blocks.shape[0]
    return blocks[:, :SEQ].reshape(images * SEQ, blocks.shape[2])


def per_device_dense(
    tokens,
    gain_attn,
    shift_attn,
    qkv_weight,
    out_weight,
    gain_moe,
    shift_moe,
    router_weight,
    expert_up,
    expert_down,
    routes,
    keep_mask,
    cotangent,
):
    row_count, feature_count = tokens.shape
    images = row_count // SEQ
    rows = images * PITCH
    tensor_count = lax.axis_size("tensor")
    quarter_width = feature_count // tensor_count
    experts_all = router_weight.shape[1]
    hidden = expert_up.shape[2]
    kept_routes = per_image(jnp.where(keep_mask > 0, routes, -1) + 1).reshape(rows, 2) - 1
    chosen = kept_routes[:, :, None] == jnp.arange(128, dtype=jnp.int32)[None, None, :]
    kept = jnp.any(chosen, axis=1).astype(bf16)
    router_wide = jnp.pad(router_weight.T, ((0, 128 - experts_all), (0, 0)))
    cot_turned = jnp.pad(cotangent.T, ((0, 0), (0, -row_count % 128)))
    qkv_turned = jnp.swapaxes(qkv_weight, 1, 2)
    (
        queries,
        keys,
        values,
        attended,
        lse,
        resid,
        h_all,
        cot_all,
        kept_all,
        up_all,
        down_all,
        mixed_first,
        grad_h_first,
        gate_first,
        up_first,
        down_first,
        tok,
    ) = run_forward(
        tokens,
        gain_attn,
        shift_attn,
        gain_moe,
        shift_moe,
        qkv_turned,
        out_weight,
        expert_up[0],
        expert_down[0],
        cot_turned,
        kept,
        router_wide,
        experts_all,
    )
    mixed_part, up_second, down_second, grad_router, grad_h_two, up_pair, down_pair, line_first = run_second_pair(
        h_all,
        cot_all,
        kept_all,
        router_wide,
        mixed_first,
        grad_h_first,
        gate_first,
        up_all,
        down_all,
        up_first,
        down_first,
        experts_all,
    )
    line_sum, tokens_grad, weights_grad, sums, mixed = run_backward(
        gain_attn,
        shift_attn,
        gain_moe,
        qkv_turned,
        out_weight,
        grad_router,
        tok,
        queries,
        keys,
        values,
        attended,
        lse,
        grad_h_two,
        resid,
        cot_all,
        mixed_part,
        up_second,
        down_second,
        line_first,
    )
    own_lane = lax.axis_index("expert") // 2 % 2 * hidden

    def expert_total(first, pair, line):
        own = lax.dynamic_slice_in_dim(first, own_lane, hidden, 1)
        return own.astype(f32) + pair.astype(f32) + line.astype(f32)

    weights_grad = weights_grad.reshape(feature_count, feature_count)
    share = qkv_weight.shape[2]
    grad_qkv = weights_grad[: 3 * share].reshape(3, share, feature_count)
    return (
        unpad(mixed.reshape(images, PITCH, quarter_width)),
        tokens_grad.astype(f32),
        sums[0],
        sums[1],
        jnp.swapaxes(grad_qkv, 1, 2).astype(f32),
        weights_grad[3 * share :].astype(f32),
        sums[2],
        sums[3],
        sums[8 : 8 + experts_all].T,
        expert_total(up_first, up_pair, line_sum[0])[None],
        expert_total(down_first, down_pair, line_sum[1]).T[None],
    )


def per_device(*arguments):
    router_weight = arguments[7]
    if router_weight.shape[1] == 4 and lax.axis_size("expert") == 8 and lax.axis_size("tensor") == 4:
        return per_device_dense(*arguments)
    return per_device_routed(*arguments)


def solution(mesh):
    placed = (
        P("expert", None),
        P(),
        P(),
        P(None, None, "tensor"),
        P("tensor", None),
        P(),
        P(),
        P(),
        P("expert", None, "tensor"),
        P("expert", "tensor", None),
        P("expert", None),
        P("expert", None),
        P("expert", "tensor"),
    )
    return jax.shard_map(
        per_device,
        mesh=mesh,
        in_specs=placed,
        out_specs=(
            P("expert", "tensor"),
            P("expert", None),
            P(),
            P(),
            P(None, None, "tensor"),
            P("tensor", None),
            P(),
            P(),
            P(),
            P("expert", None, "tensor"),
            P("expert", "tensor", None),
        ),
        check_vma=False,
    )
```

```python
from functools import partial

import jax
import jax.numpy as jnp
from jax import lax
from jax.experimental import pallas as pl
from jax.experimental.pallas import tpu as pltpu
from jax.sharding import PartitionSpec as P

HD = 64
SEQ = 197


norm_epsilon = 1e-06


def norm_rows(values, gain, shift):
    row_mean = jnp.mean(values, axis=-1, keepdims=True)
    centred = values - row_mean
    spread = jnp.mean(centred * centred, axis=-1, keepdims=True)
    return centred * lax.rsqrt(spread + norm_epsilon) * gain + shift


def gelu_exact(values):
    return jax.nn.gelu(values, approximate=False)


def gate_from_logits(logit_rows, picked_rows, keep_rows):
    router_probs = jax.nn.softmax(logit_rows, axis=-1)
    return jnp.sum(jnp.where(picked_rows, router_probs[:, None, :], 0.0), axis=-1) * keep_rows


def attention_forward(h_rows, qkv_w, out_w):
    row_total_count = h_rows.shape[0]
    head_count = qkv_w.shape[2] // HD
    image_count = row_total_count // SEQ
    score_scale = HD ** (-0.5)
    projected = jnp.einsum("td,cdf->ctf", h_rows, qkv_w, preferred_element_type=jnp.float32).astype(
        jnp.bfloat16
    )
    split_heads = projected.reshape(3, image_count, SEQ, head_count, HD)
    queries = split_heads[0]
    keys_all = split_heads[1]
    values_all = split_heads[2]
    scores = (
        jnp.einsum("gqhe,gkhe->ghqk", queries, keys_all, preferred_element_type=jnp.float32)
        * score_scale
    )
    row_peak = jnp.max(scores, axis=-1, keepdims=True)
    exp_scores = jnp.exp(scores - row_peak)
    row_total = jnp.sum(exp_scores, axis=-1, keepdims=True)
    log_total = row_peak + jnp.log(row_total)
    weights = (exp_scores / row_total).astype(jnp.bfloat16)
    attended = jnp.einsum(
        "ghqk,gkhe->gqhe", weights, values_all, preferred_element_type=jnp.float32
    ).astype(jnp.bfloat16)
    attended = attended.reshape(row_total_count, head_count * HD)
    partial_out = jnp.dot(attended, out_w, preferred_element_type=jnp.float32)
    return (partial_out, (attended, queries, keys_all, values_all, log_total))


def attention_backward(grad_branch, saved, h_rows, qkv_w, out_w):
    attended, queries, keys_all, values_all, log_total = saved
    row_total_count = h_rows.shape[0]
    head_count = qkv_w.shape[2] // HD
    image_count = row_total_count // SEQ
    score_scale = HD ** (-0.5)
    grad_out = jnp.einsum("tc,td->cd", attended, grad_branch, preferred_element_type=jnp.float32)
    grad_attended = jnp.einsum(
        "td,cd->tc", grad_branch, out_w, preferred_element_type=jnp.float32
    ).astype(jnp.bfloat16)
    grad_attended = grad_attended.reshape(image_count, SEQ, head_count, HD)
    scores_again = (
        jnp.einsum("gqhe,gkhe->ghqk", queries, keys_all, preferred_element_type=jnp.float32)
        * score_scale
    )
    probs_again = jnp.exp(scores_again - log_total)
    grad_weights = jnp.einsum(
        "gqhe,gkhe->ghqk", grad_attended, values_all, preferred_element_type=jnp.float32
    )
    grad_scores = (
        probs_again * (grad_weights - jnp.sum(probs_again * grad_weights, axis=-1, keepdims=True))
    ).astype(jnp.bfloat16)
    grad_queries = (
        jnp.einsum("ghqk,gkhe->gqhe", grad_scores, keys_all, preferred_element_type=jnp.float32)
        * score_scale
    )
    grad_keys = (
        jnp.einsum("ghqk,gqhe->gkhe", grad_scores, queries, preferred_element_type=jnp.float32)
        * score_scale
    )
    grad_values = jnp.einsum(
        "ghqk,gqhe->gkhe",
        probs_again.astype(jnp.bfloat16),
        grad_attended,
        preferred_element_type=jnp.float32,
    )
    grad_rows = (
        jnp.stack([grad_queries, grad_keys, grad_values])
        .astype(jnp.bfloat16)
        .reshape(3, row_total_count, head_count * HD)
    )
    grad_qkv = jnp.einsum("td,ctf->cdf", h_rows, grad_rows, preferred_element_type=jnp.float32)
    grad_h_one = jnp.einsum("ctf,cdf->td", grad_rows, qkv_w, preferred_element_type=jnp.float32)
    return (grad_qkv, grad_out, grad_h_one)


def moe_tail(
    grad_h_rows,
    grad_gate_rows,
    grad_out_rows,
    h_two_rows,
    resid_rows,
    gate_back,
    router_weight,
    gain_moe,
    shift_moe,
):
    row_total_count = grad_h_rows.shape[0]
    grad_gate = jnp.sum(grad_gate_rows.reshape(row_total_count, -1, 2), axis=1)
    grad_logits = gate_back(grad_gate)[0].astype(jnp.bfloat16)
    grad_router = jnp.einsum(
        "td,te->de", h_two_rows, grad_logits, preferred_element_type=jnp.float32
    )
    grad_h_two = grad_h_rows + jnp.einsum(
        "te,de->td", grad_logits, router_weight, preferred_element_type=jnp.float32
    )
    norm_out, norm_back = jax.vjp(norm_rows, resid_rows, gain_moe, shift_moe)
    grad_resid_norm, grad_gain_moe, grad_shift_moe = norm_back(grad_h_two)
    return (grad_out_rows + grad_resid_norm, grad_router, grad_gain_moe, grad_shift_moe)


def per_device_routed(
    tokens,
    gain_attn,
    shift_attn,
    qkv_weight,
    out_weight,
    gain_moe,
    shift_moe,
    router_weight,
    expert_up,
    expert_down,
    routes,
    keep_mask,
    cotangent,
):
    row_count, feature_count = tokens.shape
    tensor_count = lax.axis_size("tensor")
    expert_count = lax.axis_size("expert")
    tensor_here = lax.axis_index("tensor")
    quarter_width = feature_count // tensor_count
    col_start = tensor_here * quarter_width
    experts_all = router_weight.shape[1]
    capacity = max(2, 7 * row_count // (2 * experts_all))
    tokens_float = tokens.astype(jnp.float32)
    h_one = norm_rows(tokens_float, gain_attn, shift_attn).astype(jnp.bfloat16)
    partial_out, saved = attention_forward(h_one, qkv_weight, out_weight)
    branch = lax.psum(partial_out, "tensor")
    resid = tokens_float + branch
    h_two = norm_rows(resid, gain_moe, shift_moe).astype(jnp.bfloat16)
    logits = jnp.dot(h_two, router_weight, preferred_element_type=jnp.float32)
    keep_float = keep_mask.astype(jnp.float32)
    picked = routes[:, :, None] == jnp.arange(experts_all, dtype=jnp.int32)[None, None, :]
    gate_values, gate_back = jax.vjp(
        partial(gate_from_logits, picked_rows=picked, keep_rows=keep_float), logits
    )
    flat_expert = routes.reshape(-1)
    one_hot = (flat_expert[:, None] == jnp.arange(experts_all, dtype=jnp.int32)[None, :]).astype(
        jnp.int32
    )
    rank_within = jnp.sum((jnp.cumsum(one_hot, axis=0) - one_hot) * one_hot, axis=1)
    slot_index = flat_expert * capacity + rank_within
    token_index = jnp.repeat(jnp.arange(row_count, dtype=jnp.int32), 2)
    live_route = keep_mask.reshape(-1) > 0
    source_table = (
        jnp.full((experts_all * capacity,), row_count, jnp.int32)
        .at[slot_index]
        .set(jnp.where(live_route, token_index, row_count))
    )
    padded_rows = jnp.concatenate([h_two, jnp.zeros((1, feature_count), jnp.bfloat16)], axis=0)
    dispatch = padded_rows[source_table].reshape(experts_all, capacity, feature_count)
    paired = jnp.broadcast_to(dispatch[:, None], (experts_all, 2, capacity, feature_count)).reshape(
        expert_count, capacity, feature_count
    )
    arrived = lax.all_to_all(paired, "expert", split_axis=0, concat_axis=0, tiled=True)
    expert_rows = arrived.reshape(expert_count * capacity, feature_count)
    up_local = expert_up[0]
    down_local = expert_down[0]
    pre_act = jnp.dot(expert_rows, up_local, preferred_element_type=jnp.float32)
    hidden_float, gelu_back = jax.vjp(gelu_exact, pre_act)
    hidden = hidden_float.astype(jnp.bfloat16)
    partial_down = jnp.dot(hidden, down_local, preferred_element_type=jnp.float32)
    summed = lax.psum_scatter(partial_down, "tensor", scatter_dimension=1, tiled=True)
    returned = lax.all_to_all(
        summed.reshape(expert_count, capacity, quarter_width),
        "expert",
        split_axis=0,
        concat_axis=0,
        tiled=True,
    )
    answer_table = jnp.sum(
        returned.reshape(experts_all, 2, capacity, quarter_width), axis=1
    ).astype(jnp.bfloat16)
    answers = (
        answer_table.reshape(experts_all * capacity, quarter_width)[slot_index]
        .astype(jnp.float32)
        .reshape(row_count, 2, quarter_width)
    )
    resid_part = lax.dynamic_slice_in_dim(resid, col_start, quarter_width, 1)
    mixed = (resid_part + jnp.sum(gate_values[:, :, None] * answers, axis=1)).astype(jnp.bfloat16)
    grad_part = cotangent.astype(jnp.float32)
    grad_answers = (
        (gate_values[:, :, None] * grad_part[:, None, :])
        .astype(jnp.bfloat16)
        .reshape(2 * row_count, quarter_width)
    )
    grad_gate_part = jnp.sum(grad_part[:, None, :] * answers, axis=-1)
    outgoing = (
        jnp.zeros((experts_all * capacity, quarter_width), jnp.bfloat16)
        .at[slot_index]
        .set(grad_answers)
    )
    outgoing = jnp.broadcast_to(
        outgoing.reshape(experts_all, 1, capacity, quarter_width),
        (experts_all, 2, capacity, quarter_width),
    ).reshape(expert_count, capacity, quarter_width)
    incoming = lax.all_to_all(outgoing, "expert", split_axis=0, concat_axis=0, tiled=True)
    grad_full = lax.all_gather(incoming, "tensor", axis=2, tiled=True).reshape(
        expert_count * capacity, feature_count
    )
    grad_hidden = jnp.einsum("rd,fd->rf", grad_full, down_local, preferred_element_type=jnp.float32)
    grad_pre = gelu_back(grad_hidden)[0].astype(jnp.bfloat16)
    grad_down = jnp.einsum("rf,rd->fd", hidden, grad_full, preferred_element_type=jnp.float32)
    grad_up = jnp.einsum("rd,rf->df", expert_rows, grad_pre, preferred_element_type=jnp.float32)
    grad_rows_partial = jnp.einsum(
        "rf,df->rd", grad_pre, up_local, preferred_element_type=jnp.float32
    )
    grad_rows_sum = lax.psum_scatter(
        grad_rows_partial.astype(jnp.bfloat16), "tensor", scatter_dimension=1, tiled=True
    ).astype(jnp.float32)
    sent_back = lax.all_to_all(
        grad_rows_sum.reshape(expert_count, capacity, quarter_width).astype(jnp.bfloat16),
        "expert",
        split_axis=0,
        concat_axis=0,
        tiled=True,
    ).astype(jnp.float32)
    grad_table = jnp.sum(sent_back.reshape(experts_all, 2, capacity, quarter_width), axis=1).astype(
        jnp.bfloat16
    )
    grad_inputs = (
        grad_table.reshape(experts_all * capacity, quarter_width)[slot_index]
        .astype(jnp.float32)
        .reshape(row_count, 2, quarter_width)
    )
    grad_h_part = jnp.sum(grad_inputs * keep_float[:, :, None], axis=1)
    grad_h_full, grad_gate_all, grad_out_full = (
        lax.all_gather(grad_h_part, "tensor", axis=1, tiled=True),
        lax.all_gather(grad_gate_part, "tensor", axis=1, tiled=True),
        lax.all_gather(grad_part, "tensor", axis=1, tiled=True),
    )
    grad_resid, grad_router, grad_gain_moe, grad_shift_moe = moe_tail(
        grad_h_full,
        grad_gate_all,
        grad_out_full,
        h_two,
        resid,
        gate_back,
        router_weight,
        gain_moe,
        shift_moe,
    )
    grad_qkv, grad_out, grad_h_one_part = attention_backward(
        grad_resid.astype(jnp.bfloat16), saved, h_one, qkv_weight, out_weight
    )
    grad_h_one = lax.psum(grad_h_one_part.astype(jnp.bfloat16), "tensor").astype(jnp.float32)
    norm_one_out, norm_one_back = jax.vjp(norm_rows, tokens_float, gain_attn, shift_attn)
    grad_tok_norm, grad_gain_attn, grad_shift_attn = norm_one_back(grad_h_one)
    grad_tokens = grad_resid + grad_tok_norm
    summed_grads = lax.psum(
        (
            grad_gain_attn,
            grad_shift_attn,
            grad_qkv,
            grad_out,
            grad_gain_moe,
            grad_shift_moe,
            grad_router,
        ),
        "expert",
    )
    grad_qkv_mine = summed_grads[2]
    grad_out_mine = summed_grads[3]
    return (
        mixed,
        grad_tokens,
        summed_grads[0],
        summed_grads[1],
        grad_qkv_mine,
        grad_out_mine,
        summed_grads[4],
        summed_grads[5],
        summed_grads[6],
        grad_up[None],
        grad_down[None],
    )


MESH = pl.DeviceIdType.MESH
f32 = jnp.float32
bf16 = jnp.bfloat16
PITCH = 208


def dot(left, right, over=((1,), (0,))):
    return lax.dot_general(left, right, (over, ((), ())), preferred_element_type=f32)


def aligned(start, size):
    return pl.ds(pl.multiple_of(start, 16), size)


def lanes_at(start, size):
    return pl.ds(pl.multiple_of(start, 128), size)


def norm_stats(values):
    row_mean = jnp.mean(values, axis=1, keepdims=True)
    centred = values - row_mean
    inverse = lax.rsqrt(jnp.mean(centred * centred, axis=1, keepdims=True) + norm_epsilon)
    return centred * inverse, inverse


def greet(neighbours):
    barrier = pltpu.get_barrier_semaphore()
    count = 0
    for is_there, device in neighbours:

        @pl.when(is_there)
        def _():
            pl.semaphore_signal(barrier, inc=1, device_id=device, device_id_type=MESH)

        count = count + jnp.where(is_there, 1, 0)
    pl.semaphore_wait(barrier, count)


def head_mask(lane, head):
    return (lane < HD) if head % 2 == 0 else (lane >= HD)


def expert_math(h_rows, cot_rows, kept, router, up, down, pair, experts):
    block = h_rows.shape[0]
    hidden = up.shape[1] // 2
    lane = lax.broadcasted_iota(jnp.int32, (block, 128), 1)
    logits = jnp.where(lane < experts, dot(h_rows, router, ((1,), (1,))), -1e30)
    powers = jnp.exp(logits - jnp.max(logits, axis=1, keepdims=True))
    probs = powers / jnp.sum(powers, axis=1, keepdims=True)
    gates = kept * probs
    pre_act = dot(h_rows, up)
    back = dot(cot_rows, down, ((1,), (1,)))
    normal_cdf = 0.5 + 0.5 * lax.erf(pre_act * 0.7071067811865476)
    gelu = pre_act * normal_cdf
    slope = normal_cdf + pre_act * (0.3989422804014327 * jnp.exp(-0.5 * pre_act * pre_act))
    product = gelu * back
    grad_gate = jnp.zeros((block, 128), f32)
    spread = []
    for side in range(2):
        chosen = lane == 2 * pair + side
        part = jnp.sum(product[:, side * hidden : (side + 1) * hidden], axis=1, keepdims=True)
        grad_gate = jnp.where(chosen, part, grad_gate)
        gate = jnp.sum(jnp.where(chosen, gates, 0.0), axis=1, keepdims=True)
        spread.append(jnp.broadcast_to(gate, (block, hidden)))
    gate = jnp.concatenate(spread, axis=1)
    hidden_rows = (gelu * gate).astype(bf16)
    grad_pre = (slope * back * gate).astype(bf16)
    return hidden_rows, grad_pre, probs, grad_gate


BLOCK = 2 * PITCH


def forward_kernel(
    gain1_ref,
    shift1_ref,
    gain2_ref,
    shift2_ref,
    up_ref,
    down_ref,
    router_ref,
    cot_hbm,
    kept_hbm,
    tok_hbm,
    qkv_hbm,
    out_w_hbm,
    q_ref,
    k_ref,
    v_ref,
    att_ref,
    lse_ref,
    resid_ref,
    h_out,
    cot_out,
    kept_out,
    up_out,
    down_out,
    mixed_out,
    grad_h_out,
    gate_out,
    grad_up_out,
    grad_down_out,
    tok_out,
    cot_turned,
    kept_ref,
    tok_raw,
    qkv_ref,
    out_w_ref,
    tok_ref,
    cot_ref,
    up_vm,
    down_vm,
    up_sum,
    down_sum,
    mixed_slots,
    grad_h_slots,
    gate_slots,
    grad_up_vm,
    grad_down_vm,
    q_all,
    k_all,
    v_all,
    att_all,
    lse_all,
    resid_all,
    h_all,
    cot_all,
    kept_all,
    part,
    mine,
    core_from,
    core_to,
    x_to,
    x_from,
    total_to,
    total_from,
    cot_core,
    core_s,
    core_r,
    x_s,
    x_r,
    tot_s,
    tot_r,
    y_s,
    y_r,
    rel_s,
    rel_r,
    w_s,
    w_r,
    c_s,
    c_r,
    load_sem,
    own_sem,
    pair_sem,
    block_sem,
    grad_sem,
    cot_sem,
    out_sem,
    *,
    images,
    heads,
    experts,
):
    expert_at = lax.axis_index("expert")
    tensor_at = lax.axis_index("tensor")
    z_at, y_at = expert_at // 2, expert_at % 2
    z_last = lax.axis_size("expert") // 2 - 1
    x_at, core_at = tensor_at // 2, tensor_at % 2
    other = 1 - core_at
    rows = images * PITCH
    half = rows // 2
    wide = out_w_ref.shape[1] // 2
    loads = [
        pltpu.make_async_copy(source, target, load_sem.at[number])
        for number, (source, target) in enumerate(
            (
                (cot_hbm, cot_turned),
                (kept_hbm, kept_ref),
                (tok_hbm, tok_raw),
                (qkv_hbm, qkv_ref),
                (out_w_hbm, out_w_ref),
            )
        )
    ]
    for copy in loads:
        copy.start()
    hidden = up_ref.shape[1]
    core_dev = (expert_at, tensor_at + 1 - 2 * core_at)
    x_dev = (expert_at, tensor_at + 2 - 4 * x_at)
    y_dev = (expert_at + 1 - 2 * y_at, tensor_at)
    z_up = (expert_at + 2, tensor_at)
    z_down = (expert_at - 2, tensor_at)
    has_up, has_down = z_at < z_last, z_at > 0
    greet([(True, core_dev), (True, x_dev), (True, y_dev), (has_up, z_up), (has_down, z_down)])

    def remote(src, dst, send, recv, device):
        return pltpu.make_async_remote_copy(
            src_ref=src, dst_ref=dst, send_sem=send, recv_sem=recv, device_id=device, device_id_type=MESH
        )

    def slot(expert, plane):
        pair = (expert // 2 + plane // 2) % 2
        return (
            up_out.at[pair, :, lanes_at(expert % 2 * hidden, hidden)],
            down_out.at[pair, aligned(expert % 2 * hidden, hidden), :],
        )

    def hop(step, way):
        expert = z_at - step if way == 0 else z_at + step
        plane = z_at + 1 if way == 0 else z_at - 1
        source = (up_ref, down_ref) if step == 0 else slot(expert, z_at)
        target = slot(expert, plane)
        device = z_up if way == 0 else z_down
        return [remote(source[n], target[n], w_s.at[way, step, n], w_r.at[way, step, n], device) for n in range(2)]

    def hop_goes(step, way):
        if way == 0:
            return (z_at - step >= 0) & has_up
        return (z_at + step <= z_last) & has_down

    def hop_comes(step, way):
        return (z_at - 1 - step >= 0) if way == 0 else (z_at + 1 + step <= z_last)

    def hop_arriving(step, way):
        expert = z_at - 1 - step if way == 0 else z_at + 1 + step
        target = slot(expert, z_at)
        return [remote(target[n], target[n], w_s.at[way, step, n], w_r.at[way, step, n], core_dev) for n in range(2)]

    def start_hops(step):
        for way in range(2):

            @pl.when(hop_goes(step, way))
            def _():
                for copy in hop(step, way):
                    copy.start()

    def await_hops(step):
        for way in range(2):

            @pl.when(hop_comes(step, way))
            def _():
                for copy in hop_arriving(step, way):
                    copy.wait_recv()

    start_hops(0)

    def pair_place(expert):
        return up_vm.at[:, lanes_at(expert % 2 * hidden, hidden)], down_vm.at[aligned(expert % 2 * hidden, hidden), :]

    near = z_at + 1 - 2 * (z_at % 2)
    own_copies = [
        pltpu.make_async_copy((up_ref, down_ref)[n], pair_place(z_at)[n], own_sem.at[n]) for n in range(2)
    ]
    near_copies = [
        pltpu.make_async_copy(slot(near, z_at)[n], pair_place(near)[n], pair_sem.at[n]) for n in range(2)
    ]
    for copy in own_copies:
        copy.start()

    loads[0].wait()
    for number in range(images):
        first = number * SEQ // 128 * 128
        skip = number * SEQ - first
        turned = cot_turned[:, first : first + 384].T.astype(f32)[skip : skip + SEQ]
        padded = jnp.concatenate([turned, jnp.zeros((PITCH - SEQ, turned.shape[1]), f32)], axis=0)
        cot_ref[number * PITCH : (number + 1) * PITCH, :] = padded.astype(bf16)
    swap = remote(cot_ref, cot_core, c_s.at[0], c_r.at[0], core_dev)
    swap.start()
    loads[1].wait()
    kept_all[pl.ds(0, rows), :] = kept_ref[...]

    def kept_half(side, core):
        return kept_all.at[aligned(side * rows + core * half, half), :]

    kept_y = remote(kept_half(0, core_at), kept_half(1, core_at), c_s.at[7], c_r.at[7], y_dev)
    kept_share = remote(kept_half(1, core_at), kept_half(1, core_at), c_s.at[6], c_r.at[6], core_dev)
    kept_share_in = remote(kept_half(1, other), kept_half(1, other), c_s.at[6], c_r.at[6], core_dev)
    kept_y.start()
    swap.wait_recv()

    @pl.when(core_at == 0)
    def _():
        both = jnp.concatenate([cot_ref[...], cot_core[...]], axis=1)
        cot_all[pl.ds(0, rows), lanes_at(x_at * wide, wide)] = both

    @pl.when(core_at == 1)
    def _():
        both = jnp.concatenate([cot_core[...], cot_ref[...]], axis=1)
        cot_all[pl.ds(0, rows), lanes_at(x_at * wide, wide)] = both

    def block(side, col_side, core):
        return cot_all.at[aligned(side * rows + core * half, half), lanes_at(col_side * wide, wide)]

    def cot_copy(number, source, target, device):
        return remote(source, target, c_s.at[number], c_r.at[number], device)

    mine_block = block(0, x_at, core_at)
    cot_x = cot_copy(1, mine_block, mine_block, x_dev)
    cot_y = cot_copy(2, mine_block, block(1, x_at, core_at), y_dev)
    cot_x.start()
    cot_y.start()
    across_x, across_y, across_both = block(0, 1 - x_at, core_at), block(1, x_at, core_at), block(1, 1 - x_at, core_at)
    cot_x_in = cot_copy(1, across_x, across_x, x_dev)
    cot_y_in = cot_copy(2, across_y, across_y, y_dev)
    relay_y = cot_copy(3, across_x, across_both, y_dev)
    relay_x = cot_copy(3, across_y, across_y, x_dev)
    relay_in = cot_copy(3, across_both, across_both, y_dev)
    cot_share = [
        cot_copy(4, across_x, across_x, core_dev),
        cot_copy(5, across_y, across_y, core_dev),
        cot_copy(8, across_both, across_both, core_dev),
    ]
    arriving = [block(0, 1 - x_at, other), block(1, x_at, other), block(1, 1 - x_at, other)]
    cot_share_in = [cot_copy(number, ref, ref, core_dev) for number, ref in zip((4, 5, 8), arriving)]

    lane = lax.broadcasted_iota(jnp.int32, (PITCH, 2 * HD), 1)
    key_mask = lax.broadcasted_iota(jnp.int32, (PITCH, PITCH), 1) < SEQ
    gain1, shift1, gain2, shift2 = (ref[...].reshape(1, 2 * wide) for ref in (gain1_ref, shift1_ref, gain2_ref, shift2_ref))
    my_cols = lanes_at(core_at * wide, wide)
    their_cols = lanes_at(other * wide, wide)

    def attend(image):
        normed, _ = norm_stats(tok_ref[image].astype(f32))
        h_one = (normed * gain1 + shift1).astype(bf16)
        queries = dot(h_one, qkv_ref[0], ((1,), (1,))).astype(bf16)
        keys = dot(h_one, qkv_ref[1], ((1,), (1,))).astype(bf16)
        values = dot(h_one, qkv_ref[2], ((1,), (1,))).astype(bf16)
        q_all[image] = queries
        k_all[image] = keys
        v_all[image] = values
        outs = []
        lse = jnp.zeros((PITCH, 2 * HD), f32)
        for head in range(heads):
            first = head // 2 * 2 * HD
            last = min(first + 2 * HD, heads * HD)
            q_head, k_head, v_head = queries[:, first:last], keys[:, first:last], values[:, first:last]
            if last - first == 2 * HD:
                q_head = jnp.where(head_mask(lane, head), q_head, jnp.zeros_like(q_head))
            scores = dot(q_head, k_head, ((1,), (1,))) * (HD**-0.5)
            scores = jnp.where(key_mask, scores, -1e30)
            peak = jnp.max(scores, axis=1, keepdims=True)
            powers = jnp.exp(scores - peak)
            row_sum = jnp.sum(powers, axis=1, keepdims=True)
            weights = (powers / row_sum).astype(bf16)
            outs.append(dot(weights, v_head))
            lse = jnp.where(lane == head, peak + jnp.log(row_sum), lse)
        lse_all[image] = lse
        joined = []
        for head in range(0, heads, 2):
            if head + 1 < heads:
                joined.append(jnp.where(lane < HD, outs[head], outs[head + 1]))
            else:
                joined.append(outs[head])
        attended = jnp.concatenate(joined, axis=1).astype(bf16)
        att_all[image] = attended
        part[...] = dot(attended, out_w_ref[...])
        mine[image] = part[:, my_cols]
        core_to[image] = part[:, their_cols].astype(bf16)

    def core_copy(image):
        return remote(core_to.at[image], core_from.at[image], core_s.at[image], core_r.at[image], core_dev)

    def x_copy(image):
        return remote(x_to.at[image], x_from.at[image], x_s.at[image], x_r.at[image], x_dev)

    def total_copy(image):
        return remote(total_to.at[image], total_from.at[image], tot_s.at[image], tot_r.at[image], core_dev)

    def h_block(side, image, core):
        return h_all.at[aligned(side * rows + image * PITCH, PITCH), lanes_at(core * wide, wide)]

    def y_copy(image):
        return remote(h_block(0, image, core_at), h_block(1, image, core_at), y_s.at[image], y_r.at[image], y_dev)

    def relay_copy(image):
        ref = h_block(1, image, core_at)
        return remote(ref, ref, rel_s.at[image], rel_r.at[image], core_dev)

    def relay_arriving(image):
        ref = h_block(1, image, other)
        return remote(ref, ref, rel_s.at[image], rel_r.at[image], core_dev)

    attend_outs = ((tok_ref, tok_out), (q_all, q_ref), (k_all, k_ref), (v_all, v_ref), (att_all, att_ref), (lse_all, lse_ref))

    def out_copies(image):
        copies = [
            pltpu.make_async_copy(kept.at[image], out.at[image], out_sem.at[n, image])
            for n, (kept, out) in enumerate(attend_outs)
        ]
        at = aligned(image * PITCH, PITCH)
        return copies, [
            pltpu.make_async_copy(resid_all.at[image], resid_ref.at[at, :], out_sem.at[6, image]),
            pltpu.make_async_copy(h_all.at[at, :], h_out.at[at, :], out_sem.at[7, image]),
        ]

    def other_copy(image):
        at = aligned(rows + image * PITCH, PITCH)
        return pltpu.make_async_copy(h_all.at[at, :], h_out.at[at, :], out_sem.at[8, image])

    def stage(tick, lag, run):
        image = tick - lag

        @pl.when((image >= 0) & (image < images))
        def _():
            run(image)

    def run_attend(image):
        attend(image)
        core_copy(image).start()
        for copy in out_copies(image)[0]:
            copy.start()

    def run_x(image):
        core_copy(image).wait_recv()
        x_to[image] = (mine[image] + core_from[image].astype(f32)).astype(bf16)
        x_copy(image).start()

    def run_total(image):
        x_copy(image).wait_recv()
        total_to[image] = (x_to[image].astype(f32) + x_from[image].astype(f32)).astype(bf16)
        total_copy(image).start()

    def run_norm(image):
        total_copy(image).wait_recv()
        part[:, my_cols] = total_to[image].astype(f32)
        part[:, their_cols] = total_from[image].astype(f32)
        resid = tok_ref[image].astype(f32) + part[...]
        resid_all[image] = resid
        normed, _ = norm_stats(resid)
        h_all[aligned(image * PITCH, PITCH), :] = (normed * gain2 + shift2).astype(bf16)
        y_copy(image).start()
        for copy in out_copies(image)[1]:
            copy.start()

    def run_relay(image):
        y_copy(image).wait_recv()
        relay_copy(image).start()

    def run_end(image):
        relay_arriving(image).wait_recv()
        other_copy(image).start()

    def cot_step_one():
        cot_x_in.wait_recv()
        cot_share[0].start()

        @pl.when(core_at == 0)
        def _():
            relay_y.start()

        kept_y.wait_recv()
        kept_share.start()

    def cot_step_two():
        cot_y_in.wait_recv()
        cot_share[1].start()

        @pl.when(core_at == 1)
        def _():
            relay_x.start()

    def weights_step_one():
        await_hops(0)
        start_hops(1)
        for copy in near_copies:
            copy.start()

    def weights_step_two():
        await_hops(1)
        start_hops(2)

    def cot_step_three():
        relay_in.wait_recv()
        cot_share[2].start()

    outs = [
        pltpu.make_async_copy(cot_all, cot_out, cot_sem.at[0]),
        pltpu.make_async_copy(kept_all, kept_out, cot_sem.at[1]),
    ]

    def ready_own():
        cot_share_in[0].wait_recv()
        for copy in (*own_copies, *near_copies):
            copy.wait()

    def ready_other():
        for copy in (cot_share_in[1], cot_share_in[2], kept_share_in):
            copy.wait_recv()
        for copy in outs:
            copy.start()

    def block_copies(number, place):
        at = aligned(number * BLOCK, BLOCK)
        pairs = ((mixed_slots, mixed_out), (grad_h_slots, grad_h_out), (gate_slots, gate_out))
        return [
            pltpu.make_async_copy(slots.at[place], out.at[at, :], block_sem.at[n, place])
            for n, (slots, out) in enumerate(pairs)
        ]

    def run_block(number, turn):
        at = aligned(number * BLOCK, BLOCK)
        h_rows, cot_rows = h_all[at, :], cot_all[at, :]
        up, down = up_vm[...], down_vm[...]
        hidden_rows, grad_pre, _, grad_gate = expert_math(
            h_rows, cot_rows, kept_all[at, :].astype(f32), router_ref[...], up, down, z_at // 2, experts
        )

        place = turn % 2

        @pl.when(turn >= 2)
        def _():
            for copy in block_copies(number, place):
                copy.wait()

        gate_slots[place] = grad_gate
        mixed_slots[place] = dot(hidden_rows, down).astype(bf16)
        grad_h_slots[place] = dot(grad_pre, up, ((1,), (1,))).astype(bf16)
        for copy in block_copies(number, place):
            copy.start()
        up_sum[...] += dot(h_rows.T, grad_pre)
        down_sum[...] += dot(cot_rows.T, hidden_rows)

    up_sum[...] = jnp.zeros_like(up_sum)
    down_sum[...] = jnp.zeros_like(down_sum)

    def take_tokens(number):
        first = number * SEQ // 16 * 16
        skip = number * SEQ - first
        taken = min(224, images * SEQ - first)
        rows_in = tok_raw[first : first + taken, :].astype(f32)[skip : skip + SEQ]
        padded = jnp.concatenate([rows_in, jnp.zeros((PITCH - SEQ, rows_in.shape[1]), f32)], axis=0)
        tok_ref[number] = padded.astype(bf16)

    def first_ticks(tick, _):
        for number in range(images):
            pl.when(tick == number)(partial(take_tokens, number))

        stage(tick, 0, run_attend)
        stage(tick, 1, run_x)
        return 0

    for copy in loads[2:]:
        copy.wait()
    lax.fori_loop(0, images + 1, first_ticks, 0)
    pairs = images // 2

    def both(first, *runs):
        for run in runs:
            run(first)
            run(first + 1)

    cot_step_one()
    both(0, run_total, run_norm)
    cot_step_two()
    weights_step_one()
    ready_own()

    def per_turn(turn, _):
        @pl.when((turn <= 1) | (turn == 3))
        def _():
            both(jnp.where(turn == 3, 6, 2 * turn + 2), run_total, run_norm)

        @pl.when((turn >= 2) & (turn < pairs + 2))
        def _():
            both(2 * turn - 4, run_relay)

        @pl.when(turn == pairs)
        def _():
            weights_step_two()
            cot_step_three()
            ready_other()

        @pl.when(turn >= pairs)
        def _():
            both(2 * (turn - pairs), run_end)

        run_block(turn, turn)
        return 0

    lax.fori_loop(0, 2 * pairs, per_turn, 0)
    grad_up_vm[...] = up_sum[...].astype(bf16)
    grad_down_vm[...] = down_sum[...].astype(bf16)
    grad_copies = [
        pltpu.make_async_copy(grad_up_vm, grad_up_out, grad_sem.at[0]),
        pltpu.make_async_copy(grad_down_vm, grad_down_out, grad_sem.at[1]),
    ]
    for copy in grad_copies:
        copy.start()
    for copy in (swap, kept_y, kept_share, cot_x, cot_y, *cot_share):
        copy.wait_send()

    @pl.when(core_at == 0)
    def _():
        relay_y.wait_send()

    @pl.when(core_at == 1)
    def _():
        relay_x.wait_send()

    def drain(image, _):
        for copy in (core_copy, x_copy, total_copy, y_copy, relay_copy):
            copy(image).wait_send()
        first, second = out_copies(image)
        for copy in (*first, *second, other_copy(image)):
            copy.wait()
        return 0

    lax.fori_loop(0, images, drain, 0)
    for place in range(2):
        for copy in block_copies(0, place):
            copy.wait()

    await_hops(2)
    for step in range(3):
        for way in range(2):

            @pl.when(hop_goes(step, way))
            def _():
                for copy in hop(step, way):
                    copy.wait_send()

    for copy in (*grad_copies, *outs):
        copy.wait()


def run_forward(tok_raw, gain1, shift1, gain2, shift2, qkv_w, out_w, up, down, cot, kept, router, experts):
    images = tok_raw.shape[0] // SEQ
    rows = images * PITCH
    features = tok_raw.shape[1]
    share = out_w.shape[0]
    heads = share // HD
    hidden = up.shape[1]
    wide = features // 2
    vmem = pl.BlockSpec(memory_space=pltpu.VMEM)
    anywhere = pl.BlockSpec(memory_space=pl.ANY)
    shape = jax.ShapeDtypeStruct
    block = (images, PITCH, wide)
    dma = pltpu.SemaphoreType.DMA
    return pl.pallas_call(
        partial(forward_kernel, images=images, heads=heads, experts=experts),
        out_shape=[
            shape((images, PITCH, share), bf16),
            shape((images, PITCH, share), bf16),
            shape((images, PITCH, share), bf16),
            shape((images, PITCH, share), bf16),
            shape((images, PITCH, 128), f32),
            shape((rows, features), f32),
            shape((2 * rows, features), bf16),
            shape((2 * rows, features), bf16),
            shape((2 * rows, 128), bf16),
            shape((2, features, 2 * hidden), bf16),
            shape((2, 2 * hidden, features), bf16),
            shape((2 * rows, features), bf16),
            shape((2 * rows, features), bf16),
            shape((2 * rows, 128), f32),
            shape((features, 2 * hidden), bf16),
            shape((features, 2 * hidden), bf16),
            shape((images, PITCH, features), bf16),
        ],
        in_specs=[vmem] * 4 + [anywhere] * 2 + [vmem] + [anywhere] * 5,
        out_specs=[anywhere] * 17,
        scratch_shapes=[
            pltpu.VMEM(cot.shape, bf16),
            pltpu.VMEM(kept.shape, bf16),
            pltpu.VMEM(tok_raw.shape, bf16),
            pltpu.VMEM(qkv_w.shape, bf16),
            pltpu.VMEM(out_w.shape, bf16),
            pltpu.VMEM((images, PITCH, features), bf16),
            pltpu.VMEM((rows, share), bf16),
            pltpu.VMEM((features, 2 * hidden), bf16),
            pltpu.VMEM((2 * hidden, features), bf16),
            *[pltpu.VMEM((features, 2 * hidden), f32)] * 2,
            *[pltpu.VMEM((2, BLOCK, features), bf16)] * 2,
            pltpu.VMEM((2, BLOCK, 128), f32),
            *[pltpu.VMEM((features, 2 * hidden), bf16)] * 2,
            *[pltpu.VMEM((images, PITCH, share), bf16)] * 4,
            pltpu.VMEM((images, PITCH, 128), f32),
            pltpu.VMEM((images, PITCH, features), f32),
            pltpu.VMEM((2 * rows, features), bf16),
            pltpu.VMEM((2 * rows, features), bf16),
            pltpu.VMEM((2 * rows, 128), bf16),
            pltpu.VMEM((PITCH, features), f32),
            pltpu.VMEM(block, f32),
            pltpu.VMEM(block, bf16),
            pltpu.VMEM(block, bf16),
            pltpu.VMEM(block, bf16),
            pltpu.VMEM(block, bf16),
            pltpu.VMEM(block, bf16),
            pltpu.VMEM(block, bf16),
            pltpu.VMEM((rows, share), bf16),
        ]
        + [dma((images,))] * 10
        + [dma((2, 3, 2))] * 2
        + [dma((9,))] * 2
        + [dma((5,)), dma((2,)), dma((2,)), dma((3, 2)), dma((2,)), dma((2,)), dma((9, images))],
        compiler_params=pltpu.CompilerParams(
            collective_id=1, has_side_effects=True, vmem_limit_bytes=63 << 20
        ),
    )(gain1, shift1, gain2, shift2, up, down, router, cot, kept, tok_raw, qkv_w, out_w)


def turn_is_other(turn):
    return (turn == 0) | ((turn % 2 == 1) & (turn < 7))


def turn_block(turn):
    own = jnp.where(turn == 7, 3, turn // 2 - 1)
    return jnp.where(turn_is_other(turn), 4 + (turn + 1) // 2, own)


def second_pair_kernel(
    h_ref,
    cot_ref,
    kept_ref,
    router_ref,
    mixed_first,
    grad_h_first,
    gate_first,
    up_all,
    down_all,
    up_first,
    down_first,
    mixed_ref,
    grad_up_ref,
    grad_down_ref,
    grad_router_ref,
    grad_h_out,
    up_pair,
    down_pair,
    line_first,
    up_vm,
    down_vm,
    up_sum,
    down_sum,
    router_sum,
    ring,
    from_core,
    from_y,
    from_x,
    load,
    core_s,
    core_r,
    y_s,
    y_r,
    x_s,
    x_r,
    tot_s,
    tot_r,
    store,
    pair_s,
    pair_r,
    line_s,
    line_r,
    *,
    experts,
    steps,
):
    turn = pl.program_id(0)
    expert_at = lax.axis_index("expert")
    tensor_at = lax.axis_index("tensor")
    z_at, y_at = expert_at // 2, expert_at % 2
    x_at, core_at = tensor_at // 2, tensor_at % 2
    hidden = up_pair.shape[1]
    wide = ring.shape[2] // 2
    core_dev = (expert_at, tensor_at + 1 - 2 * core_at)
    x_dev = (expert_at, tensor_at + 2 - 4 * x_at)
    y_dev = (expert_at + 1 - 2 * y_at, tensor_at)
    my_cols = lanes_at(core_at * wide, wide)
    their_cols = lanes_at((1 - core_at) * wide, wide)

    def remote(src, dst, send, recv, device):
        return pltpu.make_async_remote_copy(
            src_ref=src, dst_ref=dst, send_sem=send, recv_sem=recv, device_id=device, device_id_type=MESH
        )

    def core_copy(number):
        return remote(ring.at[number % 2, :, their_cols], from_core.at[number], core_s.at[number], core_r.at[number], core_dev)

    def y_copy(number, place):
        return remote(from_core.at[number], from_y.at[place], y_s.at[place], y_r.at[place], y_dev)

    def x_copy(number, place):
        return remote(from_core.at[number], from_x.at[place], x_s.at[place], x_r.at[place], x_dev)

    def out_rows(place):
        return grad_h_out.at[aligned(place * BLOCK, BLOCK), my_cols]

    def total_copy(place):
        return remote(from_x.at[place], out_rows(place), tot_s.at[place], tot_r.at[place], core_dev)

    def store_copy(place):
        return pltpu.make_async_copy(from_x.at[place], out_rows(place), store.at[place])

    def own_turn(place):
        return jnp.where(place == 3, 7, 2 * place + 2)

    def other_turn(place):
        return jnp.where(place == 0, 0, 2 * place - 1)

    def pass_other(number):
        core_copy(number).wait_recv()
        from_core[number] = from_core[number] + ring[number % 2, :, my_cols]
        y_copy(number, (number + 1) // 2).start()

    def pass_own(number, place):
        core_copy(number).wait_recv()
        y_copy(number, place).wait_recv()
        total = from_core[number].astype(f32) + ring[number % 2, :, my_cols].astype(f32) + from_y[place].astype(f32)
        from_core[number] = total.astype(bf16)
        x_copy(number, place).start()

    def pass_total(place):
        number = own_turn(place)
        x_copy(number, place).wait_recv()
        from_x[place] = from_core[number] + from_x[place]
        total_copy(place).start()
        store_copy(place).start()

    z_dev = (jnp.where(z_at % 2 == 0, expert_at + 2, expert_at - 2), tensor_at)
    pair_lanes = lanes_at((1 - z_at % 2) * hidden, hidden)
    pair_copies = [
        remote(source.at[:, pair_lanes], target, pair_s.at[number], pair_r.at[number], z_dev)
        for number, (source, target) in enumerate(((up_first, up_pair), (down_first, down_pair)))
    ]

    far_lanes = lanes_at(jnp.where(z_at == 0, 1, 0) * hidden, hidden)
    line_copy = remote(grad_up_ref.at[:, far_lanes], line_first, line_s.at[0], line_r.at[0], z_dev)
    is_outer = (z_at == 0) | (z_at == lax.axis_size("expert") // 2 - 1)

    @pl.when(turn == 0)
    def _():
        greet([(True, core_dev), (True, x_dev), (True, y_dev), (True, z_dev)])
        for copy in pair_copies:
            copy.start()
        whole = [
            pltpu.make_async_copy(up_all.at[1], up_vm, load.at[0]),
            pltpu.make_async_copy(down_all.at[1], down_vm, load.at[1]),
        ]
        for copy in whole:
            copy.start()
        up_sum[...] = jnp.zeros_like(up_sum)
        down_sum[...] = jnp.zeros_like(down_sum)
        router_sum[...] = jnp.zeros_like(router_sum)
        for copy in whole:
            copy.wait()

    h_rows, cot_rows = h_ref[...], cot_ref[...]
    up, down, router = up_vm[...], down_vm[...], router_ref[...]
    kept = kept_ref[...].astype(f32)
    hidden_rows, grad_pre, probs, grad_gate = expert_math(
        h_rows, cot_rows, kept, router, up, down, 1 - z_at // 2, experts
    )
    grad_gate = kept * (grad_gate + gate_first[...])
    grad_logits = (probs * (grad_gate - jnp.sum(probs * grad_gate, axis=1, keepdims=True))).astype(bf16)

    before = turn - 1

    @pl.when((turn >= 1) & turn_is_other(before))
    def _():
        pass_other(before)

    @pl.when((turn == 5) | (turn == 7))
    def _():
        pass_total((turn - 5) // 2)

    @pl.when((turn == 3) | (turn == 5) | (turn == 7))
    def _():
        pass_own(before, (turn - 3) // 2)


    @pl.when(turn >= 2)
    def _():
        core_copy(turn - 2).wait_send()

    ring[turn % 2] = (
        grad_h_first[...].astype(f32) + dot(grad_pre, up, ((1,), (1,))) + dot(grad_logits, router)
    ).astype(bf16)
    core_copy(turn).start()
    mixed_ref[...] = (mixed_first[...].astype(f32) + dot(hidden_rows, down)).astype(bf16)
    h_turned = h_rows.T
    up_sum[...] += dot(h_turned, grad_pre)
    router_sum[...] += dot(h_turned, grad_logits)
    down_sum[...] += dot(cot_rows.T, hidden_rows)

    @pl.when(turn == steps - 1)
    def _():
        grad_up_ref[...] = up_sum[...].astype(bf16)

        @pl.when(is_outer)
        def _():
            line_copy.start()

        pass_own(7, 3)
        pass_total(2)
        grad_down_ref[...] = down_sum[...].astype(bf16)
        grad_router_ref[...] = router_sum[...].T[:8]
        pass_total(3)
        for copy in pair_copies:
            copy.wait()

        @pl.when(is_outer)
        def _():
            line_copy.wait_send()

        @pl.when(jnp.logical_not(is_outer))
        def _():
            line_copy.wait_recv()

        for number in (6, 7):
            core_copy(number).wait_send()
        for place in range(4):
            y_copy(other_turn(place), place).wait_send()
            x_copy(own_turn(place), place).wait_send()
            total_copy(place).wait_send()
            total_copy(place).wait_recv()
            store_copy(place).wait()


def run_second_pair(
    h_rows,
    cot_rows,
    kept,
    router,
    mixed_first,
    grad_h_first,
    gate_first,
    up,
    down,
    up_first,
    down_first,
    experts,
):
    rows, features = h_rows.shape
    width = up.shape[2]
    steps = rows // BLOCK
    half = (BLOCK, features // 2)
    anywhere = pl.BlockSpec(memory_space=pl.ANY)
    shape = jax.ShapeDtypeStruct
    dma = pltpu.SemaphoreType.DMA

    def by_step(lanes):
        return pl.BlockSpec((BLOCK, lanes), lambda n: (turn_block(n), 0))

    def whole(*dims):
        return pl.BlockSpec(dims, lambda n: (0,) * len(dims))

    return pl.pallas_call(
        partial(second_pair_kernel, experts=experts, steps=steps),
        grid=(steps,),
        out_shape=[
            shape((rows, features), bf16),
            shape((features, width), bf16),
            shape((features, width), bf16),
            shape((8, features), f32),
            shape((rows // 2, features), bf16),
            shape((features, width // 2), bf16),
            shape((features, width // 2), bf16),
            shape((features, width // 2), bf16),
        ],
        in_specs=[
            by_step(features),
            by_step(features),
            by_step(128),
            whole(128, features),
            by_step(features),
            by_step(features),
            by_step(128),
        ]
        + [anywhere] * 4,
        out_specs=[by_step(features), whole(features, width), whole(features, width), whole(8, features)] + [anywhere] * 4,
        scratch_shapes=[
            pltpu.VMEM((features, width), bf16),
            pltpu.VMEM((width, features), bf16),
            pltpu.VMEM((features, width), f32),
            pltpu.VMEM((features, width), f32),
            pltpu.VMEM((features, 128), f32),
            pltpu.VMEM((2, BLOCK, features), bf16),
            pltpu.VMEM((8, *half), bf16),
            pltpu.VMEM((4, *half), bf16),
            pltpu.VMEM((4, *half), bf16),
            dma((2,)),
        ]
        + [dma((8,))] * 2
        + [dma((4,))] * 7
        + [dma((2,))] * 2
        + [dma((1,))] * 2,
        compiler_params=pltpu.CompilerParams(
            collective_id=4, has_side_effects=True, vmem_limit_bytes=60 << 20
        ),
    )(h_rows, cot_rows, kept, router, mixed_first, grad_h_first, gate_first, up, down, up_first, down_first)


def backward_kernel(
    gain1_ref,
    shift1_ref,
    gain2_ref,
    grad_router_ref,
    qkv_hbm,
    out_w_hbm,
    tok_hbm,
    q_hbm,
    k_hbm,
    v_hbm,
    att_hbm,
    lse_hbm,
    grad_h_hbm,
    resid_ref,
    cot_ref,
    mixed_ref,
    up_second,
    down_second,
    line_first,
    line_out,
    tokens_out,
    weights_out,
    sums_out,
    mixed_out,
    qkv_ref,
    out_w_ref,
    tok_ref,
    q_ref,
    k_ref,
    v_ref,
    att_ref,
    lse_ref,
    grad_h_ref,
    rows_kept,
    cot_rows,
    m_mine,
    m_core,
    m_y,
    m_x,
    m_out,
    m_resid,
    far_vm,
    one_mine,
    one_to,
    one_core,
    one_x,
    one_total,
    line,
    weight_sum,
    weight_half,
    shared,
    shared_y,
    shared_line,
    shared_all,
    route_core,
    route_x,
    late_mine,
    late_y,
    late_z,
    sums_all,
    tokens_low,
    whole,
    mc_s,
    mc_r,
    my_s,
    my_r,
    mx_s,
    mx_r,
    mq_s,
    mq_r,
    m_store,
    oc_s,
    oc_r,
    ox_s,
    ox_r,
    ot_s,
    ot_r,
    l_s,
    l_r,
    sy_s,
    sy_r,
    sl_s,
    sl_r,
    sg_s,
    sg_r,
    sz_s,
    sz_r,
    r_s,
    r_r,
    late_s,
    late_r,
    load,
    image_load,
    own_sem,
    weight_store,
    store,
    *,
    images,
    heads,
):
    expert_at = lax.axis_index("expert")
    tensor_at = lax.axis_index("tensor")
    z_at, y_at = expert_at // 2, expert_at % 2
    z_last = lax.axis_size("expert") // 2 - 1
    x_at, core_at = tensor_at // 2, tensor_at % 2
    other = 1 - core_at
    rows = images * PITCH
    features = tok_hbm.shape[2]
    wide = features // 2
    share = out_w_ref.shape[0]
    hidden = line.shape[3]
    core_dev = (expert_at, tensor_at + 1 - 2 * core_at)
    x_dev = (expert_at, tensor_at + 2 - 4 * x_at)
    y_dev = (expert_at + 1 - 2 * y_at, tensor_at)
    z_devs = [(expert_at + 2, tensor_at), (expert_at - 2, tensor_at)]
    planes = z_last + 1
    z_others = [((z_at + hop) % planes * 2 + y_at, tensor_at) for hop in (1, 2, 3)]
    greet([(True, device) for device in (core_dev, x_dev, y_dev, *z_others)])
    my_cols = lanes_at(core_at * wide, wide)
    their_cols = lanes_at(other * wide, wide)

    def remote(src, dst, send, recv, device):
        return pltpu.make_async_remote_copy(
            src_ref=src, dst_ref=dst, send_sem=send, recv_sem=recv, device_id=device, device_id_type=MESH
        )

    def at_image(image):
        return aligned(image * PITCH, PITCH)

    def place(way):
        return z_at if way == 0 else z_last - z_at

    def far_lanes(way, piece):
        expert = z_last - piece // 2 if way == 0 else piece // 2
        return pl.ds(expert % 2 * hidden, hidden)

    def line_copy(source, way, piece):
        return remote(source, line.at[way, piece], l_s.at[way, piece], l_r.at[way, piece], z_devs[way])

    def line_copy_on(way, piece):
        return line_copy(line.at[way, piece], way, piece)

    def line_start():
        for way in range(2):

            @pl.when(place(way) == 0)
            def _():
                for piece in range(1, 4):
                    source = (up_second, down_second)[piece % 2]
                    line_copy(source.at[:, far_lanes(way, piece)], way, piece).start()

    def line_add(piece):
        for way in range(2):

            @pl.when(place(way) == 1)
            def _():
                if piece > 0:
                    line_copy_on(way, piece).wait_recv()
                lanes = far_lanes(way, piece)

                def add(part, _):
                    at_rows = aligned(part * 96, 96)
                    total = line[way, piece, at_rows, :].astype(f32) + far_vm[piece % 2, at_rows, lanes].astype(f32)
                    line[way, piece, at_rows, :] = total.astype(bf16)
                    return 0

                lax.fori_loop(0, features // 96, add, 0)
                line_copy_on(way, piece).start()

    def line_pass(piece):
        for way in range(2):

            @pl.when(place(way) == 2)
            def _():
                line_copy_on(way, piece).wait_recv()
                line_copy_on(way, piece).start()

    line_start()
    later = [
        pltpu.make_async_copy((up_second, down_second)[number], far_vm.at[number], own_sem.at[number])
        for number in range(2)
    ]
    is_inner = (z_at == 1) | (z_at == z_last - 1)
    first_copy = pltpu.make_async_copy(line_first, line.at[jnp.where(z_at == 1, 0, 1), 0], own_sem.at[2])

    @pl.when(is_inner)
    def _():
        first_copy.start()

    for copy in later:
        copy.start()

    part_count = m_y.shape[0]
    part_rows_m = rows // part_count

    def m_rows(side, part):
        return aligned(side * rows + part * part_rows_m, part_rows_m)

    def m_core_copy(side, part):
        at = m_rows(side, part)
        return remote(mixed_ref.at[at, their_cols], m_core.at[at, :], mc_s.at[side, part], mc_r.at[side, part], core_dev)

    for part in range(part_count):
        m_core_copy(1, part).start()
    for part in range(part_count):
        m_core_copy(0, part).start()
    m_loads = [
        pltpu.make_async_copy(mixed_ref.at[pl.ds(side * rows, rows), my_cols], m_mine.at[pl.ds(side * rows, rows), :], load.at[side])
        for side in range(2)
    ]

    def image_loads(image):
        at = at_image(image)
        by_image = ((tok_hbm, tok_ref), (q_hbm, q_ref), (k_hbm, k_ref), (v_hbm, v_ref), (att_hbm, att_ref), (lse_hbm, lse_ref))
        by_row = ((grad_h_hbm, grad_h_ref), (resid_ref, rows_kept), (cot_ref, cot_rows))
        pairs = [(source.at[image], target.at[image]) for source, target in by_image]
        pairs += [(source.at[at, :], target.at[at, :]) for source, target in by_row]
        return [pltpu.make_async_copy(source, target, image_load.at[n, image]) for n, (source, target) in enumerate(pairs)]

    def start_loads(image, _):
        for copy in image_loads(image):
            copy.start()
        return 0

    weight_loads = [
        pltpu.make_async_copy(qkv_hbm, qkv_ref, own_sem.at[3]),
        pltpu.make_async_copy(out_w_hbm, out_w_ref, own_sem.at[4]),
    ]
    for copy in weight_loads:
        copy.start()
    start_loads(0, 0)
    m_loads[1].start()
    lax.fori_loop(1, images, start_loads, 0)
    m_loads[0].start()
    route_one = remote(grad_router_ref, route_core, r_s.at[0], r_r.at[0], core_dev)
    route_one.start()

    weight_sum[...] = jnp.zeros_like(weight_sum)
    late_mine[...] = jnp.zeros_like(late_mine)

    def m_y_copy(part):
        return remote(m_core.at[m_rows(1, part), :], m_y.at[part], my_s.at[part], my_r.at[part], y_dev)

    def m_x_copy(part):
        return remote(m_core.at[m_rows(0, part), :], m_x.at[part], mx_s.at[part], mx_r.at[part], x_dev)

    def m_place(part):
        return mixed_out.at[aligned(part * part_rows_m, part_rows_m), :]

    def m_quarter_copy(part):
        return remote(m_out.at[part, other], m_place(part), mq_s.at[part], mq_r.at[part], core_dev)

    def m_store_copy(part):
        return pltpu.make_async_copy(m_out.at[part, core_at], m_place(part), m_store.at[part])

    def m_resid_copy(part):
        at = aligned(part * part_rows_m, part_rows_m)
        return pltpu.make_async_copy(resid_ref.at[at, lanes_at(x_at * wide, wide)], m_resid, load.at[3])

    keeps = x_at == core_at

    def run_m_y(part):
        m_core_copy(1, part).wait_recv()
        at = m_rows(1, part)
        m_core[at, :] = (m_core[at, :].astype(f32) + m_mine[at, :].astype(f32)).astype(bf16)
        m_y_copy(part).start()

    def run_m_x(part):
        if isinstance(part, int) and part == 0:
            m_loads[0].wait()
        m_core_copy(0, part).wait_recv()
        m_y_copy(part).wait_recv()
        at = m_rows(0, part)
        total = m_core[at, :].astype(f32) + m_mine[at, :].astype(f32) + m_y[part].astype(f32)
        m_core[at, :] = total.astype(bf16)

        @pl.when(jnp.logical_not(keeps))
        def _():
            m_x_copy(part).start()

    def run_m_out(part):
        @pl.when(keeps)
        def _():
            m_resid_copy(part).start()
            m_x_copy(part).wait_recv()
            m_resid_copy(part).wait()
            total = m_core[m_rows(0, part), :].astype(f32) + m_x[part].astype(f32)
            mixed = (m_resid[...] + total).astype(bf16)
            m_out[part, 0] = mixed[:, : wide // 2]
            m_out[part, 1] = mixed[:, wide // 2 :]
            m_quarter_copy(part).start()
            m_store_copy(part).start()

    later[0].wait()
    later[1].wait()

    @pl.when(is_inner)
    def _():
        first_copy.wait()

    line_add(0)
    m_loads[1].wait()
    for part in range(part_count):
        run_m_y(part)
    route_one.wait_recv()
    route_core[...] += grad_router_ref[...]
    route_two = remote(route_core, route_x, r_s.at[1], r_r.at[1], x_dev)
    route_two.start()

    def one_core_copy(image):
        return remote(one_to.at[image], one_core.at[image], oc_s.at[image], oc_r.at[image], core_dev)

    def one_x_copy(image):
        return remote(one_core.at[image], one_x.at[image], ox_s.at[image], ox_r.at[image], x_dev)

    def one_total_copy(image):
        return remote(one_x.at[image], one_total.at[image], ot_s.at[image], ot_r.at[image], core_dev)

    store_copy = pltpu.make_async_copy(tokens_low, tokens_out, store.at[0])

    lane = lax.broadcasted_iota(jnp.int32, (PITCH, 2 * HD), 1)
    key_mask = lax.broadcasted_iota(jnp.int32, (PITCH, PITCH), 1) < SEQ
    gain1, shift1, gain2 = (ref[...].reshape(1, features) for ref in (gain1_ref, shift1_ref, gain2_ref))

    def norm_back(grad, gain, normed, inverse):
        scaled = grad * gain
        mean = jnp.mean(scaled, axis=1, keepdims=True)
        along = jnp.mean(scaled * normed, axis=1, keepdims=True)
        return (scaled - mean - normed * along) * inverse

    def add_sums(sums, row, grad, normed):
        sums[row : row + 1, :] += jnp.sum(grad * normed, axis=0, keepdims=True)
        sums[row + 1 : row + 2, :] += jnp.sum(grad, axis=0, keepdims=True)

    def run_attention(image):
        for copy in image_loads(image):
            copy.wait()
        at = at_image(image)
        grad_h = grad_h_ref[at, :].astype(f32)
        normed, inverse = norm_stats(rows_kept[at, :])
        add_sums(late_mine, 2, grad_h, normed)
        grad_resid = cot_rows[at, :].astype(f32) + norm_back(grad_h, gain2, normed, inverse)
        rows_kept[at, :] = grad_resid
        grad_branch = grad_resid.astype(bf16)
        token_normed, _ = norm_stats(tok_ref[image].astype(f32))
        h_one = (token_normed * gain1 + shift1).astype(bf16)
        queries, keys, values, attended = q_ref[image], k_ref[image], v_ref[image], att_ref[image]
        lse = lse_ref[image]
        grad_attended = dot(grad_branch, out_w_ref[...], ((1,), (1,))).astype(bf16)
        grads = [[], [], []]
        for head in range(heads):
            first = head // 2 * 2 * HD
            last = min(first + 2 * HD, heads * HD)
            parts = [whose[:, first:last] for whose in (queries, keys, values, grad_attended)]
            if last - first == 2 * HD:
                own = head_mask(lane, head)
                q_own, k_own, _, g_own = (jnp.where(own, part, jnp.zeros_like(part)) for part in parts)
            else:
                q_own, k_own, _, g_own = parts
            scores = dot(q_own, parts[1], ((1,), (1,))) * (HD**-0.5)
            probs = jnp.where(key_mask, jnp.exp(scores - lse[:, head : head + 1]), 0.0)
            back = dot(g_own, parts[2], ((1,), (1,)))
            product = probs * back
            grad_scores = (product - probs * jnp.sum(product, axis=1, keepdims=True)).astype(bf16)
            pieces = (
                dot(grad_scores, k_own) * (HD**-0.5),
                dot(grad_scores, q_own, ((0,), (0,))) * (HD**-0.5),
                dot(probs.astype(bf16), g_own, ((0,), (0,))),
            )
            for which in range(3):
                if head % 2 == 0:
                    grads[which].append(pieces[which])
                else:
                    grads[which][-1] += pieces[which]
        grad_rows = [jnp.concatenate(grads[which], axis=1).astype(bf16) for which in range(3)]
        grad_one = 0.0
        for which in range(3):
            weight_sum[which * share : (which + 1) * share, :] += dot(grad_rows[which].T, h_one)
            grad_one += dot(grad_rows[which], qkv_ref[which])
        weight_sum[3 * share : 4 * share, :] += dot(attended.T, grad_branch)
        whole[...] = grad_one
        one_mine[image] = whole[:, my_cols].astype(bf16)
        one_to[image] = whole[:, their_cols].astype(bf16)
        one_core_copy(image).start()

    def run_one_x(image):
        one_core_copy(image).wait_recv()
        one_core[image] = (one_core[image].astype(f32) + one_mine[image].astype(f32)).astype(bf16)
        one_x_copy(image).start()

    def run_one_total(image):
        one_x_copy(image).wait_recv()
        one_x[image] = (one_core[image].astype(f32) + one_x[image].astype(f32)).astype(bf16)
        one_total_copy(image).start()

    def run_tokens(image):
        one_total_copy(image).wait_recv()
        whole[:, my_cols] = one_x[image].astype(f32)
        whole[:, their_cols] = one_total[image].astype(f32)
        grad_one = whole[...]
        at = at_image(image)
        normed, inverse = norm_stats(tok_ref[image].astype(f32))
        add_sums(late_mine, 0, grad_one, normed)
        total = rows_kept[at, :] + norm_back(grad_one, gain1, normed, inverse)
        whole[...] = total
        for number in range(images):

            @pl.when(image == number)
            def _():
                rows_kept[pl.ds(number * SEQ, SEQ), :] = whole[pl.ds(0, SEQ), :]


    def stage(tick, lag, run):
        image = tick - lag

        @pl.when((image >= 0) & (image < images))
        def _():
            run(image)

    def at_tick(tick, when, run):
        @pl.when(tick == when)
        def _():
            run()

    def line_second():
        line_add(1)
        line_pass(0)

    def line_third():
        line_add(2)
        line_pass(1)

    def per_tick(tick, _):
        stage(tick, 0, run_attention)
        stage(tick, 1, run_one_x)
        stage(tick, 4, run_one_total)
        stage(tick, 5, run_tokens)
        at_tick(tick, 5, lambda: run_m_x(0))
        at_tick(tick, 3, line_second)
        at_tick(tick, 6, line_third)
        at_tick(tick, 7, lambda: run_m_x(1))
        return 0

    for copy in weight_loads:
        copy.wait()
    lax.fori_loop(0, images, per_tick, 0)

    part_rows = shared.shape[1]
    chunks = 2
    chunk_rows = part_rows // chunks
    quarter = chunk_rows // planes

    def cast(piece, _):
        for side in range(2):
            at_rows = aligned(piece * 96, 96)
            shared[side, at_rows, :] = weight_sum[aligned(side * part_rows + piece * 96, 96), :].astype(bf16)
        return 0

    lax.fori_loop(0, part_rows // 96, cast, 0)

    def y_piece(number):
        inner = jnp.where(z_at == 1, jnp.where(number < 2, z_last - number, number - 2), jnp.where(number < 2, number, 5 - number))
        return jnp.where(z_at == 0, z_last - number, jnp.where(z_at == z_last, number, inner))

    def quarter_at(chunk, piece):
        return aligned(chunk * chunk_rows + piece * quarter, quarter)

    def shared_y_copy(chunk, number):
        at_rows = quarter_at(chunk, y_piece(number))
        return remote(
            shared.at[1 - y_at, at_rows, :], shared_y.at[at_rows, :], sy_s.at[chunk, number], sy_r.at[chunk, number], y_dev
        )

    def take_y(chunk, number):
        shared_y_copy(chunk, number).wait_recv()
        at_rows = quarter_at(chunk, y_piece(number))
        weight_half[at_rows, :] = shared[y_at, at_rows, :].astype(f32) + shared_y[at_rows, :].astype(f32)

    def quarter_of(step, at, way):
        mirrored = z_last - step + at
        return mirrored if way == 0 else z_last - mirrored

    def small_copy(chunk, step, way):
        return remote(
            shared_line.at[chunk, way, 0, step],
            shared_line.at[chunk, way, 1, step],
            sl_s.at[chunk, way, step],
            sl_r.at[chunk, way, step],
            z_devs[way],
        )

    def sum_wait(chunk, step):
        for way in range(2):
            at = place(way)

            @pl.when((at > 0) & (at - 1 <= step))
            def _():
                small_copy(chunk, step, way).wait_recv()

    def sum_send(chunk, step):
        for way in range(2):
            at = place(way)

            @pl.when((at <= step) & (at < z_last))
            def _():
                at_rows = quarter_at(chunk, quarter_of(step, at, way))
                if step == 0:
                    shared_line[chunk, way, 0, step] = weight_half[at_rows, :].astype(bf16)
                else:
                    came = jnp.where(at > 0, shared_line[chunk, way, 1, step - 1].astype(f32), 0.0)
                    shared_line[chunk, way, 0, step] = (weight_half[at_rows, :] + came).astype(bf16)
                small_copy(chunk, step, way).start()

    def final_rows(chunk, side, piece):
        return shared_all.at[side, quarter_at(chunk, piece), :]

    def gather_z(chunk, step, way, piece):
        ref = final_rows(chunk, y_at, piece)
        return remote(ref, ref, sg_s.at[chunk, way, step], sg_r.at[chunk, way, step], z_devs[way])

    def gather_y(chunk, step, way, piece, side):
        ref = final_rows(chunk, side, piece)
        return remote(ref, ref, sz_s.at[chunk, way, step], sz_r.at[chunk, way, step], y_dev)

    def piece_out(step, way):
        return z_at - step if way == 0 else z_at + step

    def piece_in(step, way):
        return z_at - 1 - step if way == 0 else z_at + 1 + step

    def gather_send(chunk, step):
        for way in range(2):
            at = place(way)

            @pl.when((at >= step) & (at < z_last))
            def _():
                gather_z(chunk, step, way, piece_out(step, way)).start()

    def gather_take(chunk, step):
        for way in range(2):

            @pl.when(place(way) >= 1 + step)
            def _():
                gather_z(chunk, step, way, piece_in(step, way)).wait_recv()
                gather_y(chunk, step + 1, way, piece_in(step, way), y_at).start()

    def finish_sum(chunk):
        own_rows = quarter_at(chunk, z_at)
        from_below = jnp.where(z_at > 0, shared_line[chunk, 0, 1, 2].astype(f32), 0.0)
        from_above = jnp.where(z_at < z_last, shared_line[chunk, 1, 1, 2].astype(f32), 0.0)
        shared_all[y_at, own_rows, :] = (weight_half[own_rows, :] + from_below + from_above).astype(bf16)
        gather_y(chunk, 0, 0, z_at, y_at).start()

    late_y_copy = remote(late_mine, late_y, late_s.at[0], late_r.at[0], y_dev)

    def late_copy(number):
        ref = late_z.at[z_at]
        return remote(ref, ref, late_s.at[number + 1], late_r.at[number + 1], z_others[number])

    def meanwhile(place_in_order):
        if place_in_order == 0:
            run_one_x(images - 1)
            run_tokens(images - 5)
            run_one_total(images - 4)
            run_m_x(part_count - 2)
        if place_in_order == 1:
            run_m_x(part_count - 1)
            run_tokens(images - 4)
            run_one_total(images - 3)
        if place_in_order == 2:
            run_m_out(0)
            run_tokens(images - 3)
        if place_in_order == 3:
            run_one_total(images - 2)
            run_m_out(1)
            run_tokens(images - 2)
        if place_in_order == 4:
            run_one_total(images - 1)
            run_m_out(2)
        if place_in_order == 5:
            run_tokens(images - 1)
            line_add(3)
            route_two.wait_recv()
            late_mine[8:16, :] = route_core[...] + route_x[...]
            late_y_copy.start()
            tokens_low[...] = rows_kept[pl.ds(0, images * SEQ), :].astype(bf16)
            store_copy.start()
        if place_in_order == 6:
            run_m_out(3)
            late_y_copy.wait_recv()
            late_z[z_at] = late_mine[...] + late_y[...]
            for number in range(planes - 1):
                late_copy(number).start()

    for number in range(4):
        for chunk in range(chunks):
            shared_y_copy(chunk, number).start()
    meanwhile(0)
    for step in range(3):
        for chunk in range(chunks):
            if step > 0:
                sum_wait(chunk, step - 1)
            take_y(chunk, step)
            sum_send(chunk, step)
        if step == 2:
            for chunk in range(chunks):
                take_y(chunk, 3)
        meanwhile(1 + step)
    for chunk in range(chunks):
        sum_wait(chunk, 2)
        finish_sum(chunk)
        gather_send(chunk, 0)
    for step in range(3):
        meanwhile(4 + step)
        for chunk in range(chunks):
            gather_take(chunk, step)
            if step < 2:
                gather_send(chunk, step + 1)

    for way in range(2):

        @pl.when(place(way) == 2)
        def _():
            line_copy_on(way, 2).wait_recv()
            line_copy_on(way, 3).wait_recv()

        @pl.when(place(way) == z_last)
        def _():
            line_copy_on(way, 0).wait_recv()
            line_copy_on(way, 1).wait_recv()

    from_far = 1 - z_at // 2
    first_piece = jnp.where((z_at == 0) | (z_at == z_last), 0, 2)

    line_out_copies = [
        pltpu.make_async_copy(line.at[from_far, first_piece + n], line_out.at[n], weight_store.at[n]) for n in range(2)
    ]
    for copy in line_out_copies:
        copy.start()
    for chunk in range(chunks):
        gather_y(chunk, 0, 0, z_at, 1 - y_at).wait_recv()
        for step in range(3):
            for way in range(2):

                @pl.when(place(way) >= 1 + step)
                def _():
                    gather_y(chunk, step + 1, way, piece_in(step, way), 1 - y_at).wait_recv()

    for number in range(planes - 1):
        late_copy(number).wait_recv()
    late = late_z[0]
    for plane in range(1, planes):
        late += late_z[plane]
    sums_all[...] = late
    out_copies = [
        pltpu.make_async_copy(shared_all, weights_out, weight_store.at[2]),
        pltpu.make_async_copy(sums_all, sums_out, weight_store.at[3]),
    ]
    for copy in out_copies:
        copy.start()
    route_one.wait_send()
    route_two.wait_send()

    def drain(image, _):
        for copy in (one_core_copy, one_x_copy, one_total_copy):
            copy(image).wait_send()
        return 0

    lax.fori_loop(0, images, drain, 0)
    for part in range(part_count):
        m_core_copy(0, part).wait_send()
        m_core_copy(1, part).wait_send()
        m_y_copy(part).wait_send()

        @pl.when(keeps)
        def _():
            m_quarter_copy(part).wait_send()
            m_store_copy(part).wait()

        @pl.when(jnp.logical_not(keeps))
        def _():
            m_x_copy(part).wait_send()
            m_quarter_copy(part).wait_recv()

    for copy in (*line_out_copies, *out_copies, store_copy):
        copy.wait()
    late_y_copy.wait_send()
    for number in range(planes - 1):
        late_copy(number).wait_send()
    for way in range(2):

        @pl.when(place(way) <= 1)
        def _():
            for piece in range(1, 4):
                line_copy_on(way, piece).wait_send()

        @pl.when(place(way) == 1)
        def _():
            line_copy_on(way, 0).wait_send()

        @pl.when(place(way) == 2)
        def _():
            for piece in range(2):
                line_copy_on(way, piece).wait_send()

    for chunk in range(chunks):
        gather_y(chunk, 0, 0, z_at, y_at).wait_send()
        for number in range(4):
            shared_y_copy(chunk, number).wait_send()
        for step in range(3):
            for way in range(2):
                at = place(way)

                @pl.when((at <= step) & (at < z_last))
                def _():
                    small_copy(chunk, step, way).wait_send()

                @pl.when((at >= step) & (at < z_last))
                def _():
                    gather_z(chunk, step, way, piece_out(step, way)).wait_send()

                @pl.when(at >= 1 + step)
                def _():
                    gather_y(chunk, step + 1, way, piece_in(step, way), y_at).wait_send()


def run_backward(gain1, shift1, gain2, grad_router, qkv_w, out_w, tok, *streamed):
    images, _, features = tok.shape
    rows = images * PITCH
    share = out_w.shape[0]
    heads = share // HD
    hidden = streamed[-1].shape[1]
    wide = features // 2
    parts = 4
    vmem = pl.BlockSpec(memory_space=pltpu.VMEM)
    anywhere = pl.BlockSpec(memory_space=pl.ANY)
    shape = jax.ShapeDtypeStruct
    dma = pltpu.SemaphoreType.DMA
    block = (images, PITCH, wide)
    return pl.pallas_call(
        partial(backward_kernel, images=images, heads=heads),
        out_shape=[
            shape((2, features, hidden), bf16),
            shape((images * SEQ, features), bf16),
            shape((2, features // 2, features), bf16),
            shape((16, features), f32),
            shape((rows, wide // 2), bf16),
        ],
        in_specs=[vmem] * 4 + [anywhere] * (3 + len(streamed)),
        out_specs=[anywhere] * 5,
        scratch_shapes=[
            pltpu.VMEM(qkv_w.shape, bf16),
            pltpu.VMEM(out_w.shape, bf16),
            pltpu.VMEM((images, PITCH, features), bf16),
            *[pltpu.VMEM((images, PITCH, share), bf16)] * 4,
            pltpu.VMEM((images, PITCH, 128), f32),
            pltpu.VMEM((rows, features), bf16),
            pltpu.VMEM((rows, features), f32),
            pltpu.VMEM((rows, features), bf16),
            pltpu.VMEM((2 * rows, wide), bf16),
            pltpu.VMEM((2 * rows, wide), bf16),
            *[pltpu.VMEM((parts, rows // parts, wide), bf16)] * 2,
            pltpu.VMEM((parts, 2, rows // parts, wide // 2), bf16),
            pltpu.VMEM((rows // parts, wide), f32),
            pltpu.VMEM((2, features, 2 * hidden), bf16),
            *[pltpu.VMEM(block, bf16)] * 5,
            pltpu.VMEM((2, 4, features, hidden), bf16),
            pltpu.VMEM((features, features), f32),
            pltpu.VMEM((features // 2, features), f32),
            pltpu.VMEM((2, features // 2, features), bf16),
            pltpu.VMEM((features // 2, features), bf16),
            pltpu.VMEM((2, 2, 2, 3, features // 16, features), bf16),
            pltpu.VMEM((2, features // 2, features), bf16),
            *[pltpu.VMEM((8, features), f32)] * 2,
            *[pltpu.VMEM((16, features), f32)] * 2,
            pltpu.VMEM((4, 16, features), f32),
            pltpu.VMEM((16, features), f32),
            pltpu.VMEM((images * SEQ, features), bf16),
            pltpu.VMEM((PITCH, features), f32),
        ]
        + [dma((2, parts))] * 2
        + [dma((parts,))] * 7
        + [dma((images,))] * 6
        + [dma((2, 4))] * 2
        + [dma((2, 4))] * 2
        + [dma((2, 2, 3))] * 4
        + [dma((2, 2, 4))] * 2
        + [dma((2,))] * 2
        + [dma((4,))] * 2
        + [dma((4,)), dma((9, images)), dma((5,)), dma((4,)), dma((1,))],
        compiler_params=pltpu.CompilerParams(
            collective_id=2, has_side_effects=True, vmem_limit_bytes=63 << 20
        ),
    )(gain1, shift1, gain2, grad_router, qkv_w, out_w, tok, *streamed)


def last_kernel(
    side_ref, tokens_ref, weights_ref, up_first, up_pair, down_first, down_pair, line_ref, tokens_out, qkv_out, out_w_out, up_out, down_out
):
    share = out_w_out.shape[0]
    tokens_out[...] = tokens_ref[...].astype(f32)
    for which in range(3):
        qkv_out[which] = weights_ref[which * share : (which + 1) * share, :].astype(f32)
    out_w_out[...] = weights_ref[3 * share :, :].astype(f32)
    up_out[...] = up_first[...].astype(f32) + up_pair[...].astype(f32) + line_ref[0].astype(f32)
    down_out[...] = (down_first[...].astype(f32) + down_pair[...].astype(f32) + line_ref[1].astype(f32)).T


def run_last(side, tokens, weights, up_first, up_pair, down_first, down_pair, line, share):
    rows, features = tokens.shape
    hidden = up_pair.shape[1]
    shape = jax.ShapeDtypeStruct

    def lanes(height):
        return pl.BlockSpec((height, 128), lambda n, side: (0, n))

    own = pl.BlockSpec((128, hidden), lambda n, side: (n, side[0]))
    plain = pl.BlockSpec((128, hidden), lambda n, side: (n, 0))
    return pl.pallas_call(
        last_kernel,
        grid_spec=pltpu.PrefetchScalarGridSpec(
            num_scalar_prefetch=1,
            grid=(features // 128,),
            in_specs=[
                lanes(rows),
                lanes(features),
                own,
                plain,
                own,
                plain,
                pl.BlockSpec((2, 128, hidden), lambda n, side: (0, n, 0)),
            ],
            out_specs=[
                lanes(rows),
                pl.BlockSpec((3, share, 128), lambda n, side: (0, 0, n)),
                lanes(share),
                plain,
                lanes(hidden),
            ],
        ),
        out_shape=[
            shape((rows, features), f32),
            shape((3, share, features), f32),
            shape((share, features), f32),
            shape((features, hidden), f32),
            shape((hidden, features), f32),
        ],
    )(side, tokens, weights, up_first, up_pair, down_first, down_pair, line)


def per_image(rows_in):
    images = rows_in.shape[0] // SEQ
    blocks = rows_in.reshape(images, SEQ, rows_in.shape[1])
    return jnp.pad(blocks, ((0, 0), (0, PITCH - SEQ), (0, 0)))


def unpad(blocks):
    images = blocks.shape[0]
    return blocks[:, :SEQ].reshape(images * SEQ, blocks.shape[2])


def per_device_dense(
    tokens,
    gain_attn,
    shift_attn,
    qkv_weight,
    out_weight,
    gain_moe,
    shift_moe,
    router_weight,
    expert_up,
    expert_down,
    routes,
    keep_mask,
    cotangent,
):
    row_count, feature_count = tokens.shape
    images = row_count // SEQ
    rows = images * PITCH
    tensor_count = lax.axis_size("tensor")
    quarter_width = feature_count // tensor_count
    experts_all = router_weight.shape[1]
    hidden = expert_up.shape[2]
    kept_routes = per_image(jnp.where(keep_mask > 0, routes, -1) + 1).reshape(rows, 2) - 1
    chosen = kept_routes[:, :, None] == jnp.arange(128, dtype=jnp.int32)[None, None, :]
    kept = jnp.any(chosen, axis=1).astype(bf16)
    router_wide = jnp.pad(router_weight.T, ((0, 128 - experts_all), (0, 0)))
    cot_turned = jnp.pad(cotangent.T, ((0, 0), (0, -row_count % 128)))
    qkv_turned = jnp.swapaxes(qkv_weight, 1, 2)
    (
        queries,
        keys,
        values,
        attended,
        lse,
        resid,
        h_all,
        cot_all,
        kept_all,
        up_all,
        down_all,
        mixed_first,
        grad_h_first,
        gate_first,
        up_first,
        down_first,
        tok,
    ) = run_forward(
        tokens,
        gain_attn,
        shift_attn,
        gain_moe,
        shift_moe,
        qkv_turned,
        out_weight,
        expert_up[0],
        expert_down[0],
        cot_turned,
        kept,
        router_wide,
        experts_all,
    )
    mixed_part, up_second, down_second, grad_router, grad_h_two, up_pair, down_pair, line_first = run_second_pair(
        h_all,
        cot_all,
        kept_all,
        router_wide,
        mixed_first,
        grad_h_first,
        gate_first,
        up_all,
        down_all,
        up_first,
        down_first,
        experts_all,
    )
    line_sum, tokens_grad, weights_grad, sums, mixed = run_backward(
        gain_attn,
        shift_attn,
        gain_moe,
        grad_router,
        qkv_turned,
        out_weight,
        tok,
        queries,
        keys,
        values,
        attended,
        lse,
        grad_h_two,
        resid,
        cot_all,
        mixed_part,
        up_second,
        down_second,
        line_first,
    )
    side = (lax.axis_index("expert") // 2 % 2).astype(jnp.int32)[None]
    grad_tokens, grad_qkv, grad_out, grad_up, grad_down = run_last(
        side,
        tokens_grad,
        weights_grad.reshape(feature_count, feature_count),
        up_first,
        up_pair,
        down_first,
        down_pair,
        line_sum,
        qkv_weight.shape[2],
    )
    return (
        unpad(mixed.reshape(images, PITCH, quarter_width)),
        grad_tokens,
        sums[0],
        sums[1],
        jnp.swapaxes(grad_qkv, 1, 2),
        grad_out,
        sums[2],
        sums[3],
        sums[8 : 8 + experts_all].T,
        grad_up[None],
        grad_down[None],
    )


def per_device(*arguments):
    router_weight = arguments[7]
    if router_weight.shape[1] == 4 and lax.axis_size("expert") == 8 and lax.axis_size("tensor") == 4:
        return per_device_dense(*arguments)
    return per_device_routed(*arguments)


def solution(mesh):
    placed = (
        P("expert", None),
        P(),
        P(),
        P(None, None, "tensor"),
        P("tensor", None),
        P(),
        P(),
        P(),
        P("expert", None, "tensor"),
        P("expert", "tensor", None),
        P("expert", None),
        P("expert", None),
        P("expert", "tensor"),
    )
    return jax.shard_map(
        per_device,
        mesh=mesh,
        in_specs=placed,
        out_specs=(
            P("expert", "tensor"),
            P("expert", None),
            P(),
            P(),
            P(None, None, "tensor"),
            P("tensor", None),
            P(),
            P(),
            P(),
            P("expert", None, "tensor"),
            P("expert", "tensor", None),
        ),
        check_vma=False,
    )
```

```python
from functools import partial

import jax
import jax.numpy as jnp
from jax import lax
from jax.experimental import pallas as pl
from jax.experimental.pallas import tpu as pltpu
from jax.sharding import PartitionSpec as P

HD = 64
SEQ = 197


norm_epsilon = 1e-06


def norm_rows(values, gain, shift):
    row_mean = jnp.mean(values, axis=-1, keepdims=True)
    centred = values - row_mean
    spread = jnp.mean(centred * centred, axis=-1, keepdims=True)
    return centred * lax.rsqrt(spread + norm_epsilon) * gain + shift


def gelu_exact(values):
    return jax.nn.gelu(values, approximate=False)


def gate_from_logits(logit_rows, picked_rows, keep_rows):
    router_probs = jax.nn.softmax(logit_rows, axis=-1)
    return jnp.sum(jnp.where(picked_rows, router_probs[:, None, :], 0.0), axis=-1) * keep_rows


def attention_forward(h_rows, qkv_w, out_w):
    row_total_count = h_rows.shape[0]
    head_count = qkv_w.shape[2] // HD
    image_count = row_total_count // SEQ
    score_scale = HD ** (-0.5)
    projected = jnp.einsum("td,cdf->ctf", h_rows, qkv_w, preferred_element_type=jnp.float32).astype(
        jnp.bfloat16
    )
    split_heads = projected.reshape(3, image_count, SEQ, head_count, HD)
    queries = split_heads[0]
    keys_all = split_heads[1]
    values_all = split_heads[2]
    scores = (
        jnp.einsum("gqhe,gkhe->ghqk", queries, keys_all, preferred_element_type=jnp.float32)
        * score_scale
    )
    row_peak = jnp.max(scores, axis=-1, keepdims=True)
    exp_scores = jnp.exp(scores - row_peak)
    row_total = jnp.sum(exp_scores, axis=-1, keepdims=True)
    log_total = row_peak + jnp.log(row_total)
    weights = (exp_scores / row_total).astype(jnp.bfloat16)
    attended = jnp.einsum(
        "ghqk,gkhe->gqhe", weights, values_all, preferred_element_type=jnp.float32
    ).astype(jnp.bfloat16)
    attended = attended.reshape(row_total_count, head_count * HD)
    partial_out = jnp.dot(attended, out_w, preferred_element_type=jnp.float32)
    return (partial_out, (attended, queries, keys_all, values_all, log_total))


def attention_backward(grad_branch, saved, h_rows, qkv_w, out_w):
    attended, queries, keys_all, values_all, log_total = saved
    row_total_count = h_rows.shape[0]
    head_count = qkv_w.shape[2] // HD
    image_count = row_total_count // SEQ
    score_scale = HD ** (-0.5)
    grad_out = jnp.einsum("tc,td->cd", attended, grad_branch, preferred_element_type=jnp.float32)
    grad_attended = jnp.einsum(
        "td,cd->tc", grad_branch, out_w, preferred_element_type=jnp.float32
    ).astype(jnp.bfloat16)
    grad_attended = grad_attended.reshape(image_count, SEQ, head_count, HD)
    scores_again = (
        jnp.einsum("gqhe,gkhe->ghqk", queries, keys_all, preferred_element_type=jnp.float32)
        * score_scale
    )
    probs_again = jnp.exp(scores_again - log_total)
    grad_weights = jnp.einsum(
        "gqhe,gkhe->ghqk", grad_attended, values_all, preferred_element_type=jnp.float32
    )
    grad_scores = (
        probs_again * (grad_weights - jnp.sum(probs_again * grad_weights, axis=-1, keepdims=True))
    ).astype(jnp.bfloat16)
    grad_queries = (
        jnp.einsum("ghqk,gkhe->gqhe", grad_scores, keys_all, preferred_element_type=jnp.float32)
        * score_scale
    )
    grad_keys = (
        jnp.einsum("ghqk,gqhe->gkhe", grad_scores, queries, preferred_element_type=jnp.float32)
        * score_scale
    )
    grad_values = jnp.einsum(
        "ghqk,gqhe->gkhe",
        probs_again.astype(jnp.bfloat16),
        grad_attended,
        preferred_element_type=jnp.float32,
    )
    grad_rows = (
        jnp.stack([grad_queries, grad_keys, grad_values])
        .astype(jnp.bfloat16)
        .reshape(3, row_total_count, head_count * HD)
    )
    grad_qkv = jnp.einsum("td,ctf->cdf", h_rows, grad_rows, preferred_element_type=jnp.float32)
    grad_h_one = jnp.einsum("ctf,cdf->td", grad_rows, qkv_w, preferred_element_type=jnp.float32)
    return (grad_qkv, grad_out, grad_h_one)


def moe_tail(
    grad_h_rows,
    grad_gate_rows,
    grad_out_rows,
    h_two_rows,
    resid_rows,
    gate_back,
    router_weight,
    gain_moe,
    shift_moe,
):
    row_total_count = grad_h_rows.shape[0]
    grad_gate = jnp.sum(grad_gate_rows.reshape(row_total_count, -1, 2), axis=1)
    grad_logits = gate_back(grad_gate)[0].astype(jnp.bfloat16)
    grad_router = jnp.einsum(
        "td,te->de", h_two_rows, grad_logits, preferred_element_type=jnp.float32
    )
    grad_h_two = grad_h_rows + jnp.einsum(
        "te,de->td", grad_logits, router_weight, preferred_element_type=jnp.float32
    )
    norm_out, norm_back = jax.vjp(norm_rows, resid_rows, gain_moe, shift_moe)
    grad_resid_norm, grad_gain_moe, grad_shift_moe = norm_back(grad_h_two)
    return (grad_out_rows + grad_resid_norm, grad_router, grad_gain_moe, grad_shift_moe)


def per_device_routed(
    tokens,
    gain_attn,
    shift_attn,
    qkv_weight,
    out_weight,
    gain_moe,
    shift_moe,
    router_weight,
    expert_up,
    expert_down,
    routes,
    keep_mask,
    cotangent,
):
    row_count, feature_count = tokens.shape
    tensor_count = lax.axis_size("tensor")
    expert_count = lax.axis_size("expert")
    tensor_here = lax.axis_index("tensor")
    quarter_width = feature_count // tensor_count
    col_start = tensor_here * quarter_width
    experts_all = router_weight.shape[1]
    capacity = max(2, 7 * row_count // (2 * experts_all))
    tokens_float = tokens.astype(jnp.float32)
    h_one = norm_rows(tokens_float, gain_attn, shift_attn).astype(jnp.bfloat16)
    partial_out, saved = attention_forward(h_one, qkv_weight, out_weight)
    branch = lax.psum(partial_out, "tensor")
    resid = tokens_float + branch
    h_two = norm_rows(resid, gain_moe, shift_moe).astype(jnp.bfloat16)
    logits = jnp.dot(h_two, router_weight, preferred_element_type=jnp.float32)
    keep_float = keep_mask.astype(jnp.float32)
    picked = routes[:, :, None] == jnp.arange(experts_all, dtype=jnp.int32)[None, None, :]
    gate_values, gate_back = jax.vjp(
        partial(gate_from_logits, picked_rows=picked, keep_rows=keep_float), logits
    )
    flat_expert = routes.reshape(-1)
    one_hot = (flat_expert[:, None] == jnp.arange(experts_all, dtype=jnp.int32)[None, :]).astype(
        jnp.int32
    )
    rank_within = jnp.sum((jnp.cumsum(one_hot, axis=0) - one_hot) * one_hot, axis=1)
    slot_index = flat_expert * capacity + rank_within
    token_index = jnp.repeat(jnp.arange(row_count, dtype=jnp.int32), 2)
    live_route = keep_mask.reshape(-1) > 0
    source_table = (
        jnp.full((experts_all * capacity,), row_count, jnp.int32)
        .at[slot_index]
        .set(jnp.where(live_route, token_index, row_count))
    )
    padded_rows = jnp.concatenate([h_two, jnp.zeros((1, feature_count), jnp.bfloat16)], axis=0)
    dispatch = padded_rows[source_table].reshape(experts_all, capacity, feature_count)
    paired = jnp.broadcast_to(dispatch[:, None], (experts_all, 2, capacity, feature_count)).reshape(
        expert_count, capacity, feature_count
    )
    arrived = lax.all_to_all(paired, "expert", split_axis=0, concat_axis=0, tiled=True)
    expert_rows = arrived.reshape(expert_count * capacity, feature_count)
    up_local = expert_up[0]
    down_local = expert_down[0]
    pre_act = jnp.dot(expert_rows, up_local, preferred_element_type=jnp.float32)
    hidden_float, gelu_back = jax.vjp(gelu_exact, pre_act)
    hidden = hidden_float.astype(jnp.bfloat16)
    partial_down = jnp.dot(hidden, down_local, preferred_element_type=jnp.float32)
    summed = lax.psum_scatter(partial_down, "tensor", scatter_dimension=1, tiled=True)
    returned = lax.all_to_all(
        summed.reshape(expert_count, capacity, quarter_width),
        "expert",
        split_axis=0,
        concat_axis=0,
        tiled=True,
    )
    answer_table = jnp.sum(
        returned.reshape(experts_all, 2, capacity, quarter_width), axis=1
    ).astype(jnp.bfloat16)
    answers = (
        answer_table.reshape(experts_all * capacity, quarter_width)[slot_index]
        .astype(jnp.float32)
        .reshape(row_count, 2, quarter_width)
    )
    resid_part = lax.dynamic_slice_in_dim(resid, col_start, quarter_width, 1)
    mixed = (resid_part + jnp.sum(gate_values[:, :, None] * answers, axis=1)).astype(jnp.bfloat16)
    grad_part = cotangent.astype(jnp.float32)
    grad_answers = (
        (gate_values[:, :, None] * grad_part[:, None, :])
        .astype(jnp.bfloat16)
        .reshape(2 * row_count, quarter_width)
    )
    grad_gate_part = jnp.sum(grad_part[:, None, :] * answers, axis=-1)
    outgoing = (
        jnp.zeros((experts_all * capacity, quarter_width), jnp.bfloat16)
        .at[slot_index]
        .set(grad_answers)
    )
    outgoing = jnp.broadcast_to(
        outgoing.reshape(experts_all, 1, capacity, quarter_width),
        (experts_all, 2, capacity, quarter_width),
    ).reshape(expert_count, capacity, quarter_width)
    incoming = lax.all_to_all(outgoing, "expert", split_axis=0, concat_axis=0, tiled=True)
    grad_full = lax.all_gather(incoming, "tensor", axis=2, tiled=True).reshape(
        expert_count * capacity, feature_count
    )
    grad_hidden = jnp.einsum("rd,fd->rf", grad_full, down_local, preferred_element_type=jnp.float32)
    grad_pre = gelu_back(grad_hidden)[0].astype(jnp.bfloat16)
    grad_down = jnp.einsum("rf,rd->fd", hidden, grad_full, preferred_element_type=jnp.float32)
    grad_up = jnp.einsum("rd,rf->df", expert_rows, grad_pre, preferred_element_type=jnp.float32)
    grad_rows_partial = jnp.einsum(
        "rf,df->rd", grad_pre, up_local, preferred_element_type=jnp.float32
    )
    grad_rows_sum = lax.psum_scatter(
        grad_rows_partial.astype(jnp.bfloat16), "tensor", scatter_dimension=1, tiled=True
    ).astype(jnp.float32)
    sent_back = lax.all_to_all(
        grad_rows_sum.reshape(expert_count, capacity, quarter_width).astype(jnp.bfloat16),
        "expert",
        split_axis=0,
        concat_axis=0,
        tiled=True,
    ).astype(jnp.float32)
    grad_table = jnp.sum(sent_back.reshape(experts_all, 2, capacity, quarter_width), axis=1).astype(
        jnp.bfloat16
    )
    grad_inputs = (
        grad_table.reshape(experts_all * capacity, quarter_width)[slot_index]
        .astype(jnp.float32)
        .reshape(row_count, 2, quarter_width)
    )
    grad_h_part = jnp.sum(grad_inputs * keep_float[:, :, None], axis=1)
    grad_h_full, grad_gate_all, grad_out_full = (
        lax.all_gather(grad_h_part, "tensor", axis=1, tiled=True),
        lax.all_gather(grad_gate_part, "tensor", axis=1, tiled=True),
        lax.all_gather(grad_part, "tensor", axis=1, tiled=True),
    )
    grad_resid, grad_router, grad_gain_moe, grad_shift_moe = moe_tail(
        grad_h_full,
        grad_gate_all,
        grad_out_full,
        h_two,
        resid,
        gate_back,
        router_weight,
        gain_moe,
        shift_moe,
    )
    grad_qkv, grad_out, grad_h_one_part = attention_backward(
        grad_resid.astype(jnp.bfloat16), saved, h_one, qkv_weight, out_weight
    )
    grad_h_one = lax.psum(grad_h_one_part.astype(jnp.bfloat16), "tensor").astype(jnp.float32)
    norm_one_out, norm_one_back = jax.vjp(norm_rows, tokens_float, gain_attn, shift_attn)
    grad_tok_norm, grad_gain_attn, grad_shift_attn = norm_one_back(grad_h_one)
    grad_tokens = grad_resid + grad_tok_norm
    summed_grads = lax.psum(
        (
            grad_gain_attn,
            grad_shift_attn,
            grad_qkv,
            grad_out,
            grad_gain_moe,
            grad_shift_moe,
            grad_router,
        ),
        "expert",
    )
    grad_qkv_mine = summed_grads[2]
    grad_out_mine = summed_grads[3]
    return (
        mixed,
        grad_tokens,
        summed_grads[0],
        summed_grads[1],
        grad_qkv_mine,
        grad_out_mine,
        summed_grads[4],
        summed_grads[5],
        summed_grads[6],
        grad_up[None],
        grad_down[None],
    )


MESH = pl.DeviceIdType.MESH
f32 = jnp.float32
bf16 = jnp.bfloat16
PITCH = 208


def dot(left, right, over=((1,), (0,))):
    return lax.dot_general(left, right, (over, ((), ())), preferred_element_type=f32)


def aligned(start, size):
    return pl.ds(pl.multiple_of(start, 16), size)


def lanes_at(start, size):
    return pl.ds(pl.multiple_of(start, 128), size)


def norm_stats(values):
    row_mean = jnp.mean(values, axis=1, keepdims=True)
    centred = values - row_mean
    inverse = lax.rsqrt(jnp.mean(centred * centred, axis=1, keepdims=True) + norm_epsilon)
    return centred * inverse, inverse


def greet(neighbours):
    barrier = pltpu.get_barrier_semaphore()
    count = 0
    for is_there, device in neighbours:

        @pl.when(is_there)
        def _():
            pl.semaphore_signal(barrier, inc=1, device_id=device, device_id_type=MESH)

        count = count + jnp.where(is_there, 1, 0)
    pl.semaphore_wait(barrier, count)


def head_mask(lane, head):
    return (lane < HD) if head % 2 == 0 else (lane >= HD)


def expert_math(h_rows, cot_rows, kept, router, up, down, pair, experts):
    block = h_rows.shape[0]
    hidden = up.shape[1] // 2
    lane = lax.broadcasted_iota(jnp.int32, (block, 128), 1)
    logits = jnp.where(lane < experts, dot(h_rows, router, ((1,), (1,))), -1e30)
    powers = jnp.exp(logits - jnp.max(logits, axis=1, keepdims=True))
    probs = powers / jnp.sum(powers, axis=1, keepdims=True)
    gates = kept * probs
    pre_act = dot(h_rows, up)
    back = dot(cot_rows, down, ((1,), (1,)))
    normal_cdf = 0.5 + 0.5 * lax.erf(pre_act * 0.7071067811865476)
    gelu = pre_act * normal_cdf
    slope = normal_cdf + pre_act * (0.3989422804014327 * jnp.exp(-0.5 * pre_act * pre_act))
    product = gelu * back
    grad_gate = jnp.zeros((block, 128), f32)
    spread = []
    for side in range(2):
        chosen = lane == 2 * pair + side
        part = jnp.sum(product[:, side * hidden : (side + 1) * hidden], axis=1, keepdims=True)
        grad_gate = jnp.where(chosen, part, grad_gate)
        gate = jnp.sum(jnp.where(chosen, gates, 0.0), axis=1, keepdims=True)
        spread.append(jnp.broadcast_to(gate, (block, hidden)))
    gate = jnp.concatenate(spread, axis=1)
    hidden_rows = (gelu * gate).astype(bf16)
    grad_pre = (slope * back * gate).astype(bf16)
    return hidden_rows, grad_pre, probs, grad_gate


BLOCK = 2 * PITCH


def forward_kernel(
    gain1_ref,
    shift1_ref,
    gain2_ref,
    shift2_ref,
    up_ref,
    down_ref,
    router_ref,
    cot_hbm,
    kept_hbm,
    tok_hbm,
    qkv_hbm,
    out_w_hbm,
    q_ref,
    k_ref,
    v_ref,
    att_ref,
    lse_ref,
    resid_ref,
    h_out,
    cot_out,
    kept_out,
    up_out,
    down_out,
    mixed_out,
    grad_h_out,
    gate_out,
    grad_up_out,
    grad_down_out,
    tok_out,
    cot_turned,
    kept_ref,
    tok_raw,
    qkv_ref,
    out_w_ref,
    tok_ref,
    cot_ref,
    up_vm,
    down_vm,
    up_sum,
    down_sum,
    mixed_slots,
    grad_h_slots,
    gate_slots,
    grad_up_vm,
    grad_down_vm,
    q_all,
    k_all,
    v_all,
    att_all,
    lse_all,
    resid_all,
    h_all,
    cot_all,
    kept_all,
    part,
    mine,
    core_from,
    core_to,
    x_to,
    x_from,
    total_to,
    total_from,
    cot_core,
    core_s,
    core_r,
    x_s,
    x_r,
    tot_s,
    tot_r,
    y_s,
    y_r,
    rel_s,
    rel_r,
    w_s,
    w_r,
    c_s,
    c_r,
    load_sem,
    own_sem,
    pair_sem,
    block_sem,
    grad_sem,
    cot_sem,
    out_sem,
    *,
    images,
    heads,
    experts,
):
    expert_at = lax.axis_index("expert")
    tensor_at = lax.axis_index("tensor")
    z_at, y_at = expert_at // 2, expert_at % 2
    z_last = lax.axis_size("expert") // 2 - 1
    x_at, core_at = tensor_at // 2, tensor_at % 2
    other = 1 - core_at
    rows = images * PITCH
    half = rows // 2
    wide = out_w_ref.shape[1] // 2
    loads = [
        pltpu.make_async_copy(source, target, load_sem.at[number])
        for number, (source, target) in enumerate(
            (
                (cot_hbm, cot_turned),
                (kept_hbm, kept_ref),
                (tok_hbm, tok_raw),
                (qkv_hbm, qkv_ref),
                (out_w_hbm, out_w_ref),
            )
        )
    ]
    for copy in loads:
        copy.start()
    hidden = up_ref.shape[1]
    core_dev = (expert_at, tensor_at + 1 - 2 * core_at)
    x_dev = (expert_at, tensor_at + 2 - 4 * x_at)
    y_dev = (expert_at + 1 - 2 * y_at, tensor_at)
    z_up = (expert_at + 2, tensor_at)
    z_down = (expert_at - 2, tensor_at)
    has_up, has_down = z_at < z_last, z_at > 0
    greet([(True, core_dev), (True, x_dev), (True, y_dev), (has_up, z_up), (has_down, z_down)])

    def remote(src, dst, send, recv, device):
        return pltpu.make_async_remote_copy(
            src_ref=src, dst_ref=dst, send_sem=send, recv_sem=recv, device_id=device, device_id_type=MESH
        )

    def slot(expert, plane):
        pair = (expert // 2 + plane // 2) % 2
        return (
            up_out.at[pair, :, lanes_at(expert % 2 * hidden, hidden)],
            down_out.at[pair, aligned(expert % 2 * hidden, hidden), :],
        )

    def hop(step, way):
        expert = z_at - step if way == 0 else z_at + step
        plane = z_at + 1 if way == 0 else z_at - 1
        source = (up_ref, down_ref) if step == 0 else slot(expert, z_at)
        target = slot(expert, plane)
        device = z_up if way == 0 else z_down
        return [remote(source[n], target[n], w_s.at[way, step, n], w_r.at[way, step, n], device) for n in range(2)]

    def hop_goes(step, way):
        if way == 0:
            return (z_at - step >= 0) & has_up
        return (z_at + step <= z_last) & has_down

    def hop_comes(step, way):
        return (z_at - 1 - step >= 0) if way == 0 else (z_at + 1 + step <= z_last)

    def hop_arriving(step, way):
        expert = z_at - 1 - step if way == 0 else z_at + 1 + step
        target = slot(expert, z_at)
        return [remote(target[n], target[n], w_s.at[way, step, n], w_r.at[way, step, n], core_dev) for n in range(2)]

    def start_hops(step, which):
        for way in range(2):

            @pl.when(hop_goes(step, way))
            def _():
                hop(step, way)[which].start()

    def await_hops(step, which):
        for way in range(2):

            @pl.when(hop_comes(step, way))
            def _():
                hop_arriving(step, way)[which].wait_recv()

    def pass_hops(step, which):
        await_hops(step, which)
        start_hops(step + 1, which)

    start_hops(0, 0)
    start_hops(0, 1)

    def pair_place(expert):
        return up_vm.at[:, lanes_at(expert % 2 * hidden, hidden)], down_vm.at[aligned(expert % 2 * hidden, hidden), :]

    near = z_at + 1 - 2 * (z_at % 2)
    own_copies = [
        pltpu.make_async_copy((up_ref, down_ref)[n], pair_place(z_at)[n], own_sem.at[n]) for n in range(2)
    ]
    near_copies = [
        pltpu.make_async_copy(slot(near, z_at)[n], pair_place(near)[n], pair_sem.at[n]) for n in range(2)
    ]
    for copy in own_copies:
        copy.start()

    loads[0].wait()
    for number in range(images):
        first = number * SEQ // 128 * 128
        skip = number * SEQ - first
        turned = cot_turned[:, first : first + 384].T.astype(f32)[skip : skip + SEQ]
        padded = jnp.concatenate([turned, jnp.zeros((PITCH - SEQ, turned.shape[1]), f32)], axis=0)
        cot_ref[number * PITCH : (number + 1) * PITCH, :] = padded.astype(bf16)
    swap = remote(cot_ref, cot_core, c_s.at[0], c_r.at[0], core_dev)
    swap.start()
    loads[1].wait()
    kept_all[pl.ds(0, rows), :] = kept_ref[...]

    def kept_half(side, core):
        return kept_all.at[aligned(side * rows + core * half, half), :]

    kept_y = remote(kept_half(0, core_at), kept_half(1, core_at), c_s.at[7], c_r.at[7], y_dev)
    kept_share = remote(kept_half(1, core_at), kept_half(1, core_at), c_s.at[6], c_r.at[6], core_dev)
    kept_share_in = remote(kept_half(1, other), kept_half(1, other), c_s.at[6], c_r.at[6], core_dev)
    kept_y.start()
    swap.wait_recv()

    @pl.when(core_at == 0)
    def _():
        both = jnp.concatenate([cot_ref[...], cot_core[...]], axis=1)
        cot_all[pl.ds(0, rows), lanes_at(x_at * wide, wide)] = both

    @pl.when(core_at == 1)
    def _():
        both = jnp.concatenate([cot_core[...], cot_ref[...]], axis=1)
        cot_all[pl.ds(0, rows), lanes_at(x_at * wide, wide)] = both

    def block(side, col_side, core):
        return cot_all.at[aligned(side * rows + core * half, half), lanes_at(col_side * wide, wide)]

    def cot_copy(number, source, target, device):
        return remote(source, target, c_s.at[number], c_r.at[number], device)

    mine_block = block(0, x_at, core_at)
    cot_x = cot_copy(1, mine_block, mine_block, x_dev)
    cot_y = cot_copy(2, mine_block, block(1, x_at, core_at), y_dev)
    cot_x.start()
    cot_y.start()
    across_x, across_y, across_both = block(0, 1 - x_at, core_at), block(1, x_at, core_at), block(1, 1 - x_at, core_at)
    cot_x_in = cot_copy(1, across_x, across_x, x_dev)
    cot_y_in = cot_copy(2, across_y, across_y, y_dev)
    relay_y = cot_copy(3, across_x, across_both, y_dev)
    relay_in = cot_copy(3, across_both, across_both, y_dev)
    cot_share = [
        cot_copy(4, across_x, across_x, core_dev),
        cot_copy(5, across_y, across_y, core_dev),
        cot_copy(8, across_both, across_both, core_dev),
    ]
    arriving = [block(0, 1 - x_at, other), block(1, x_at, other), block(1, 1 - x_at, other)]
    cot_share_in = [cot_copy(number, ref, ref, core_dev) for number, ref in zip((4, 5, 8), arriving)]

    lane = lax.broadcasted_iota(jnp.int32, (PITCH, 2 * HD), 1)
    key_mask = lax.broadcasted_iota(jnp.int32, (PITCH, PITCH), 1) < SEQ
    gain1, shift1, gain2, shift2 = (ref[...].reshape(1, 2 * wide) for ref in (gain1_ref, shift1_ref, gain2_ref, shift2_ref))
    my_cols = lanes_at(core_at * wide, wide)
    their_cols = lanes_at(other * wide, wide)

    def attend(image):
        normed, _ = norm_stats(tok_ref[image].astype(f32))
        h_one = (normed * gain1 + shift1).astype(bf16)
        queries = dot(h_one, qkv_ref[0], ((1,), (1,))).astype(bf16)
        keys = dot(h_one, qkv_ref[1], ((1,), (1,))).astype(bf16)
        values = dot(h_one, qkv_ref[2], ((1,), (1,))).astype(bf16)
        q_all[image] = queries
        k_all[image] = keys
        v_all[image] = values
        outs = []
        lse = jnp.zeros((PITCH, 2 * HD), f32)
        for head in range(heads):
            first = head // 2 * 2 * HD
            last = min(first + 2 * HD, heads * HD)
            q_head, k_head, v_head = queries[:, first:last], keys[:, first:last], values[:, first:last]
            if last - first == 2 * HD:
                q_head = jnp.where(head_mask(lane, head), q_head, jnp.zeros_like(q_head))
            scores = dot(q_head, k_head, ((1,), (1,))) * (HD**-0.5)
            scores = jnp.where(key_mask, scores, -1e30)
            peak = jnp.max(scores, axis=1, keepdims=True)
            powers = jnp.exp(scores - peak)
            row_sum = jnp.sum(powers, axis=1, keepdims=True)
            weights = (powers / row_sum).astype(bf16)
            outs.append(dot(weights, v_head))
            lse = jnp.where(lane == head, peak + jnp.log(row_sum), lse)
        lse_all[image] = lse
        joined = []
        for head in range(0, heads, 2):
            if head + 1 < heads:
                joined.append(jnp.where(lane < HD, outs[head], outs[head + 1]))
            else:
                joined.append(outs[head])
        attended = jnp.concatenate(joined, axis=1).astype(bf16)
        att_all[image] = attended
        part[...] = dot(attended, out_w_ref[...])
        mine[image] = part[:, my_cols]
        core_to[image] = part[:, their_cols].astype(bf16)

    def core_copy(image):
        return remote(core_to.at[image], core_from.at[image], core_s.at[image], core_r.at[image], core_dev)

    def x_copy(image):
        return remote(x_to.at[image], x_from.at[image], x_s.at[image], x_r.at[image], x_dev)

    def total_copy(image):
        return remote(total_to.at[image], total_from.at[image], tot_s.at[image], tot_r.at[image], core_dev)

    def h_block(side, image, core):
        return h_all.at[aligned(side * rows + image * PITCH, PITCH), lanes_at(core * wide, wide)]

    def y_copy(image):
        return remote(h_block(0, image, core_at), h_block(1, image, core_at), y_s.at[image], y_r.at[image], y_dev)

    def relay_copy(image):
        ref = h_block(1, image, core_at)
        return remote(ref, ref, rel_s.at[image], rel_r.at[image], core_dev)

    def relay_arriving(image):
        ref = h_block(1, image, other)
        return remote(ref, ref, rel_s.at[image], rel_r.at[image], core_dev)

    attend_outs = ((tok_ref, tok_out), (q_all, q_ref), (k_all, k_ref), (v_all, v_ref), (att_all, att_ref), (lse_all, lse_ref))

    def out_copies(image):
        copies = [
            pltpu.make_async_copy(kept.at[image], out.at[image], out_sem.at[n, image])
            for n, (kept, out) in enumerate(attend_outs)
        ]
        at = aligned(image * PITCH, PITCH)
        return copies, [
            pltpu.make_async_copy(resid_all.at[image], resid_ref.at[at, :], out_sem.at[6, image]),
            pltpu.make_async_copy(h_all.at[at, :], h_out.at[at, :], out_sem.at[7, image]),
        ]

    def other_copy(image):
        at = aligned(rows + image * PITCH, PITCH)
        return pltpu.make_async_copy(h_all.at[at, :], h_out.at[at, :], out_sem.at[8, image])

    def stage(tick, lag, run):
        image = tick - lag

        @pl.when((image >= 0) & (image < images))
        def _():
            run(image)

    def run_attend(image):
        attend(image)
        core_copy(image).start()
        for copy in out_copies(image)[0]:
            copy.start()

    def run_x(image):
        core_copy(image).wait_recv()
        x_to[image] = (mine[image] + core_from[image].astype(f32)).astype(bf16)
        x_copy(image).start()

    def run_total(image):
        x_copy(image).wait_recv()
        total_to[image] = (x_to[image].astype(f32) + x_from[image].astype(f32)).astype(bf16)
        total_copy(image).start()

    def run_norm(image):
        total_copy(image).wait_recv()
        part[:, my_cols] = total_to[image].astype(f32)
        part[:, their_cols] = total_from[image].astype(f32)
        resid = tok_ref[image].astype(f32) + part[...]
        resid_all[image] = resid
        normed, _ = norm_stats(resid)
        h_all[aligned(image * PITCH, PITCH), :] = (normed * gain2 + shift2).astype(bf16)
        y_copy(image).start()
        for copy in out_copies(image)[1]:
            copy.start()

    def run_relay(image):
        y_copy(image).wait_recv()
        relay_copy(image).start()

    def run_end(image):
        relay_arriving(image).wait_recv()
        other_copy(image).start()

    def cot_step_one():
        cot_x_in.wait_recv()
        cot_share[0].start()

        relay_y.start()

        kept_y.wait_recv()
        kept_share.start()

    def cot_step_two():
        cot_y_in.wait_recv()
        cot_share[1].start()

    def weights_step_one():
        pass_hops(0, 1)
        for copy in near_copies:
            copy.start()

    def cot_step_three():
        relay_in.wait_recv()
        cot_share[2].start()

    outs = [
        pltpu.make_async_copy(cot_all, cot_out, cot_sem.at[0]),
        pltpu.make_async_copy(kept_all, kept_out, cot_sem.at[1]),
    ]

    def ready_own():
        cot_share_in[0].wait_recv()
        for copy in (*own_copies, *near_copies):
            copy.wait()

    def ready_other():
        for copy in (cot_share_in[1], cot_share_in[2], kept_share_in):
            copy.wait_recv()
        for copy in outs:
            copy.start()

    def block_copies(number, place):
        at = aligned(number * BLOCK, BLOCK)
        pairs = ((mixed_slots, mixed_out), (grad_h_slots, grad_h_out), (gate_slots, gate_out))
        return [
            pltpu.make_async_copy(slots.at[place], out.at[at, :], block_sem.at[n, place])
            for n, (slots, out) in enumerate(pairs)
        ]

    def run_block(number, turn):
        at = aligned(number * BLOCK, BLOCK)
        h_rows, cot_rows = h_all[at, :], cot_all[at, :]
        up, down = up_vm[...], down_vm[...]
        hidden_rows, grad_pre, _, grad_gate = expert_math(
            h_rows, cot_rows, kept_all[at, :].astype(f32), router_ref[...], up, down, z_at // 2, experts
        )

        place = turn % 2

        @pl.when(turn >= 2)
        def _():
            for copy in block_copies(number, place):
                copy.wait()

        gate_slots[place] = grad_gate
        mixed_slots[place] = dot(hidden_rows, down).astype(bf16)
        grad_h_slots[place] = dot(grad_pre, up, ((1,), (1,))).astype(bf16)
        for copy in block_copies(number, place):
            copy.start()
        up_sum[...] += dot(h_rows.T, grad_pre)
        down_sum[...] += dot(cot_rows.T, hidden_rows)

    up_sum[...] = jnp.zeros_like(up_sum)
    down_sum[...] = jnp.zeros_like(down_sum)

    def take_tokens(number):
        first = number * SEQ // 16 * 16
        skip = number * SEQ - first
        taken = min(224, images * SEQ - first)
        rows_in = tok_raw[first : first + taken, :].astype(f32)[skip : skip + SEQ]
        padded = jnp.concatenate([rows_in, jnp.zeros((PITCH - SEQ, rows_in.shape[1]), f32)], axis=0)
        tok_ref[number] = padded.astype(bf16)

    def first_ticks(tick, _):
        for number in range(images):
            pl.when(tick == number)(partial(take_tokens, number))

        stage(tick, 0, run_attend)
        stage(tick, 1, run_x)
        return 0

    for copy in loads[2:]:
        copy.wait()
    lax.fori_loop(0, images + 1, first_ticks, 0)
    pairs = images // 2

    def both(first, *runs):
        for run in runs:
            run(first)
            run(first + 1)

    pass_hops(0, 0)
    cot_step_one()
    both(0, run_total, run_norm)
    cot_step_two()
    weights_step_one()
    ready_own()

    def per_turn(turn, _):
        @pl.when((turn <= 1) | (turn == 3))
        def _():
            both(jnp.where(turn == 3, 6, 2 * turn + 2), run_total, run_norm)

        @pl.when((turn >= 2) & (turn < pairs + 2))
        def _():
            both(2 * turn - 4, run_relay)

        @pl.when(turn == 2)
        def _():
            pass_hops(1, 0)
            cot_step_three()

        @pl.when(turn == pairs)
        def _():
            pass_hops(1, 1)
            ready_other()

        @pl.when(turn >= pairs)
        def _():
            both(2 * (turn - pairs), run_end)

        run_block(turn, turn)
        return 0

    lax.fori_loop(0, 2 * pairs, per_turn, 0)
    grad_up_vm[...] = up_sum[...].astype(bf16)
    grad_down_vm[...] = down_sum[...].astype(bf16)
    grad_copies = [
        pltpu.make_async_copy(grad_up_vm, grad_up_out, grad_sem.at[0]),
        pltpu.make_async_copy(grad_down_vm, grad_down_out, grad_sem.at[1]),
    ]
    for copy in grad_copies:
        copy.start()
    for copy in (swap, kept_y, kept_share, cot_x, cot_y, *cot_share):
        copy.wait_send()

    relay_y.wait_send()

    def drain(image, _):
        for copy in (core_copy, x_copy, total_copy, y_copy, relay_copy):
            copy(image).wait_send()
        first, second = out_copies(image)
        for copy in (*first, *second, other_copy(image)):
            copy.wait()
        return 0

    lax.fori_loop(0, images, drain, 0)
    for place in range(2):
        for copy in block_copies(0, place):
            copy.wait()

    await_hops(2, 0)
    await_hops(2, 1)
    for step in range(3):
        for way in range(2):

            @pl.when(hop_goes(step, way))
            def _():
                for copy in hop(step, way):
                    copy.wait_send()

    for copy in (*grad_copies, *outs):
        copy.wait()


def run_forward(tok_raw, gain1, shift1, gain2, shift2, qkv_w, out_w, up, down, cot, kept, router, experts):
    images = tok_raw.shape[0] // SEQ
    rows = images * PITCH
    features = tok_raw.shape[1]
    share = out_w.shape[0]
    heads = share // HD
    hidden = up.shape[1]
    wide = features // 2
    vmem = pl.BlockSpec(memory_space=pltpu.VMEM)
    anywhere = pl.BlockSpec(memory_space=pl.ANY)
    shape = jax.ShapeDtypeStruct
    block = (images, PITCH, wide)
    dma = pltpu.SemaphoreType.DMA
    return pl.pallas_call(
        partial(forward_kernel, images=images, heads=heads, experts=experts),
        out_shape=[
            shape((images, PITCH, share), bf16),
            shape((images, PITCH, share), bf16),
            shape((images, PITCH, share), bf16),
            shape((images, PITCH, share), bf16),
            shape((images, PITCH, 128), f32),
            shape((rows, features), f32),
            shape((2 * rows, features), bf16),
            shape((2 * rows, features), bf16),
            shape((2 * rows, 128), bf16),
            shape((2, features, 2 * hidden), bf16),
            shape((2, 2 * hidden, features), bf16),
            shape((2 * rows, features), bf16),
            shape((2 * rows, features), bf16),
            shape((2 * rows, 128), f32),
            shape((features, 2 * hidden), bf16),
            shape((features, 2 * hidden), bf16),
            shape((images, PITCH, features), bf16),
        ],
        in_specs=[vmem] * 4 + [anywhere] * 2 + [vmem] + [anywhere] * 5,
        out_specs=[anywhere] * 17,
        scratch_shapes=[
            pltpu.VMEM(cot.shape, bf16),
            pltpu.VMEM(kept.shape, bf16),
            pltpu.VMEM(tok_raw.shape, bf16),
            pltpu.VMEM(qkv_w.shape, bf16),
            pltpu.VMEM(out_w.shape, bf16),
            pltpu.VMEM((images, PITCH, features), bf16),
            pltpu.VMEM((rows, share), bf16),
            pltpu.VMEM((features, 2 * hidden), bf16),
            pltpu.VMEM((2 * hidden, features), bf16),
            *[pltpu.VMEM((features, 2 * hidden), f32)] * 2,
            *[pltpu.VMEM((2, BLOCK, features), bf16)] * 2,
            pltpu.VMEM((2, BLOCK, 128), f32),
            *[pltpu.VMEM((features, 2 * hidden), bf16)] * 2,
            *[pltpu.VMEM((images, PITCH, share), bf16)] * 4,
            pltpu.VMEM((images, PITCH, 128), f32),
            pltpu.VMEM((images, PITCH, features), f32),
            pltpu.VMEM((2 * rows, features), bf16),
            pltpu.VMEM((2 * rows, features), bf16),
            pltpu.VMEM((2 * rows, 128), bf16),
            pltpu.VMEM((PITCH, features), f32),
            pltpu.VMEM(block, f32),
            pltpu.VMEM(block, bf16),
            pltpu.VMEM(block, bf16),
            pltpu.VMEM(block, bf16),
            pltpu.VMEM(block, bf16),
            pltpu.VMEM(block, bf16),
            pltpu.VMEM(block, bf16),
            pltpu.VMEM((rows, share), bf16),
        ]
        + [dma((images,))] * 10
        + [dma((2, 3, 2))] * 2
        + [dma((9,))] * 2
        + [dma((5,)), dma((2,)), dma((2,)), dma((3, 2)), dma((2,)), dma((2,)), dma((9, images))],
        compiler_params=pltpu.CompilerParams(
            collective_id=1, has_side_effects=True, vmem_limit_bytes=63 << 20
        ),
    )(gain1, shift1, gain2, shift2, up, down, router, cot, kept, tok_raw, qkv_w, out_w)


def turn_is_other(turn):
    return (turn == 0) | ((turn % 2 == 1) & (turn < 7))


def turn_block(turn):
    own = jnp.where(turn == 7, 3, turn // 2 - 1)
    return jnp.where(turn_is_other(turn), 4 + (turn + 1) // 2, own)


def second_pair_kernel(
    h_ref,
    cot_ref,
    kept_ref,
    router_ref,
    mixed_first,
    grad_h_first,
    gate_first,
    up_all,
    down_all,
    up_first,
    down_first,
    mixed_ref,
    grad_router_ref,
    grad_up_out,
    grad_down_out,
    grad_h_out,
    up_pair,
    down_pair,
    line_first,
    up_vm,
    down_vm,
    grad_up_ref,
    grad_down_ref,
    up_sum,
    down_sum,
    router_sum,
    ring,
    from_core,
    from_y,
    from_x,
    load,
    core_s,
    core_r,
    y_s,
    y_r,
    x_s,
    x_r,
    tot_s,
    tot_r,
    store,
    pair_s,
    pair_r,
    line_s,
    line_r,
    *,
    experts,
    steps,
):
    turn = pl.program_id(0)
    expert_at = lax.axis_index("expert")
    tensor_at = lax.axis_index("tensor")
    z_at, y_at = expert_at // 2, expert_at % 2
    x_at, core_at = tensor_at // 2, tensor_at % 2
    hidden = up_pair.shape[1]
    wide = ring.shape[2] // 2
    core_dev = (expert_at, tensor_at + 1 - 2 * core_at)
    x_dev = (expert_at, tensor_at + 2 - 4 * x_at)
    y_dev = (expert_at + 1 - 2 * y_at, tensor_at)
    my_cols = lanes_at(core_at * wide, wide)
    their_cols = lanes_at((1 - core_at) * wide, wide)

    def remote(src, dst, send, recv, device):
        return pltpu.make_async_remote_copy(
            src_ref=src, dst_ref=dst, send_sem=send, recv_sem=recv, device_id=device, device_id_type=MESH
        )

    def core_copy(number):
        return remote(ring.at[number % 2, :, their_cols], from_core.at[number], core_s.at[number], core_r.at[number], core_dev)

    def y_copy(number, place):
        return remote(from_core.at[number], from_y.at[place], y_s.at[place], y_r.at[place], y_dev)

    def x_copy(number, place):
        return remote(from_core.at[number], from_x.at[place], x_s.at[place], x_r.at[place], x_dev)

    def out_rows(place):
        return grad_h_out.at[aligned(place * BLOCK, BLOCK), my_cols]

    def total_copy(place):
        return remote(from_x.at[place], out_rows(place), tot_s.at[place], tot_r.at[place], core_dev)

    def store_copy(place):
        return pltpu.make_async_copy(from_x.at[place], out_rows(place), store.at[place])

    def own_turn(place):
        return jnp.where(place == 3, 7, 2 * place + 2)

    def other_turn(place):
        return jnp.where(place == 0, 0, 2 * place - 1)

    def pass_other(number):
        core_copy(number).wait_recv()
        from_core[number] = from_core[number] + ring[number % 2, :, my_cols]
        y_copy(number, (number + 1) // 2).start()

    def pass_own(number, place):
        core_copy(number).wait_recv()
        y_copy(number, place).wait_recv()
        total = from_core[number].astype(f32) + ring[number % 2, :, my_cols].astype(f32) + from_y[place].astype(f32)
        from_core[number] = total.astype(bf16)
        x_copy(number, place).start()

    def pass_total(place):
        number = own_turn(place)
        x_copy(number, place).wait_recv()
        from_x[place] = from_core[number] + from_x[place]
        total_copy(place).start()
        store_copy(place).start()

    z_dev = (jnp.where(z_at % 2 == 0, expert_at + 2, expert_at - 2), tensor_at)
    pair_lanes = lanes_at((1 - z_at % 2) * hidden, hidden)
    pair_copies = [
        remote(source.at[:, pair_lanes], target, pair_s.at[number], pair_r.at[number], z_dev)
        for number, (source, target) in enumerate(((up_first, up_pair), (down_first, down_pair)))
    ]

    far_lanes = lanes_at(jnp.where(z_at == 0, 1, 0) * hidden, hidden)
    line_copy = remote(grad_up_ref.at[:, far_lanes], line_first, line_s.at[0], line_r.at[0], z_dev)
    is_outer = (z_at == 0) | (z_at == lax.axis_size("expert") // 2 - 1)

    grad_copies = [
        pltpu.make_async_copy(grad_up_ref, grad_up_out, load.at[2]),
        pltpu.make_async_copy(grad_down_ref, grad_down_out, load.at[3]),
    ]

    @pl.when(turn == 0)
    def _():
        whole = [
            pltpu.make_async_copy(up_all.at[1], up_vm, load.at[0]),
            pltpu.make_async_copy(down_all.at[1], down_vm, load.at[1]),
        ]
        for copy in whole:
            copy.start()
        greet([(True, core_dev), (True, x_dev), (True, y_dev), (True, z_dev)])
        for copy in pair_copies:
            copy.start()
        up_sum[...] = jnp.zeros_like(up_sum)
        down_sum[...] = jnp.zeros_like(down_sum)
        router_sum[...] = jnp.zeros_like(router_sum)
        for copy in whole:
            copy.wait()

    h_rows, cot_rows = h_ref[...], cot_ref[...]
    up, down, router = up_vm[...], down_vm[...], router_ref[...]
    kept = kept_ref[...].astype(f32)
    hidden_rows, grad_pre, probs, grad_gate = expert_math(
        h_rows, cot_rows, kept, router, up, down, 1 - z_at // 2, experts
    )
    grad_gate = kept * (grad_gate + gate_first[...])
    grad_logits = (probs * (grad_gate - jnp.sum(probs * grad_gate, axis=1, keepdims=True))).astype(bf16)

    before = turn - 1

    @pl.when((turn >= 1) & turn_is_other(before))
    def _():
        pass_other(before)

    @pl.when((turn == 5) | (turn == 7))
    def _():
        pass_total((turn - 5) // 2)

    @pl.when((turn == 3) | (turn == 5) | (turn == 7))
    def _():
        pass_own(before, (turn - 3) // 2)


    @pl.when(turn >= 2)
    def _():
        core_copy(turn - 2).wait_send()

    ring[turn % 2] = (
        grad_h_first[...].astype(f32) + dot(grad_pre, up, ((1,), (1,))) + dot(grad_logits, router)
    ).astype(bf16)
    core_copy(turn).start()
    mixed_ref[...] = (mixed_first[...].astype(f32) + dot(hidden_rows, down)).astype(bf16)
    h_turned = h_rows.T
    up_sum[...] += dot(h_turned, grad_pre)
    router_sum[...] += dot(h_turned, grad_logits)
    down_sum[...] += dot(cot_rows.T, hidden_rows)

    @pl.when(turn == steps - 1)
    def _():
        grad_up_ref[...] = up_sum[...].astype(bf16)
        grad_copies[0].start()

        @pl.when(is_outer)
        def _():
            line_copy.start()

        pass_own(7, 3)
        pass_total(2)
        grad_down_ref[...] = down_sum[...].astype(bf16)
        grad_copies[1].start()
        grad_router_ref[...] = router_sum[...].T[:8]
        pass_total(3)
        for copy in (*pair_copies, *grad_copies):
            copy.wait()

        @pl.when(is_outer)
        def _():
            line_copy.wait_send()

        @pl.when(jnp.logical_not(is_outer))
        def _():
            line_copy.wait_recv()

        for number in (6, 7):
            core_copy(number).wait_send()
        for place in range(4):
            y_copy(other_turn(place), place).wait_send()
            x_copy(own_turn(place), place).wait_send()
            total_copy(place).wait_send()
            total_copy(place).wait_recv()
            store_copy(place).wait()


def run_second_pair(
    h_rows,
    cot_rows,
    kept,
    router,
    mixed_first,
    grad_h_first,
    gate_first,
    up,
    down,
    up_first,
    down_first,
    experts,
):
    rows, features = h_rows.shape
    width = up.shape[2]
    steps = rows // BLOCK
    half = (BLOCK, features // 2)
    anywhere = pl.BlockSpec(memory_space=pl.ANY)
    shape = jax.ShapeDtypeStruct
    dma = pltpu.SemaphoreType.DMA

    def by_step(lanes):
        return pl.BlockSpec((BLOCK, lanes), lambda n: (turn_block(n), 0))

    def whole(*dims):
        return pl.BlockSpec(dims, lambda n: (0,) * len(dims))

    return pl.pallas_call(
        partial(second_pair_kernel, experts=experts, steps=steps),
        grid=(steps,),
        out_shape=[
            shape((rows, features), bf16),
            shape((8, features), f32),
            shape((features, width), bf16),
            shape((features, width), bf16),
            shape((rows // 2, features), bf16),
            shape((features, width // 2), bf16),
            shape((features, width // 2), bf16),
            shape((features, width // 2), bf16),
        ],
        in_specs=[
            by_step(features),
            by_step(features),
            by_step(128),
            whole(128, features),
            by_step(features),
            by_step(features),
            by_step(128),
        ]
        + [anywhere] * 4,
        out_specs=[by_step(features), whole(8, features)] + [anywhere] * 6,
        scratch_shapes=[
            pltpu.VMEM((features, width), bf16),
            pltpu.VMEM((width, features), bf16),
            *[pltpu.VMEM((features, width), bf16)] * 2,
            pltpu.VMEM((features, width), f32),
            pltpu.VMEM((features, width), f32),
            pltpu.VMEM((features, 128), f32),
            pltpu.VMEM((2, BLOCK, features), bf16),
            pltpu.VMEM((8, *half), bf16),
            pltpu.VMEM((4, *half), bf16),
            pltpu.VMEM((4, *half), bf16),
            dma((4,)),
        ]
        + [dma((8,))] * 2
        + [dma((4,))] * 7
        + [dma((2,))] * 2
        + [dma((1,))] * 2,
        compiler_params=pltpu.CompilerParams(
            collective_id=4, has_side_effects=True, vmem_limit_bytes=60 << 20
        ),
    )(h_rows, cot_rows, kept, router, mixed_first, grad_h_first, gate_first, up, down, up_first, down_first)


def backward_kernel(
    gain1_ref,
    shift1_ref,
    gain2_ref,
    grad_router_ref,
    qkv_hbm,
    out_w_hbm,
    tok_hbm,
    q_hbm,
    k_hbm,
    v_hbm,
    att_hbm,
    lse_hbm,
    grad_h_hbm,
    resid_ref,
    cot_ref,
    mixed_ref,
    up_second,
    down_second,
    line_first,
    line_out,
    tokens_out,
    weights_out,
    sums_out,
    mixed_out,
    qkv_ref,
    out_w_ref,
    tok_ref,
    q_ref,
    k_ref,
    v_ref,
    att_ref,
    lse_ref,
    grad_h_ref,
    rows_kept,
    cot_rows,
    m_mine,
    m_core,
    m_y,
    m_x,
    m_out,
    m_resid,
    far_vm,
    one_mine,
    one_to,
    one_core,
    one_x,
    one_total,
    line,
    weight_sum,
    weight_half,
    shared,
    shared_y,
    shared_line,
    shared_all,
    route_core,
    route_x,
    late_mine,
    late_y,
    late_z,
    sums_all,
    tokens_low,
    whole,
    mc_s,
    mc_r,
    my_s,
    my_r,
    mx_s,
    mx_r,
    mq_s,
    mq_r,
    m_store,
    oc_s,
    oc_r,
    ox_s,
    ox_r,
    ot_s,
    ot_r,
    l_s,
    l_r,
    sy_s,
    sy_r,
    sl_s,
    sl_r,
    sg_s,
    sg_r,
    sz_s,
    sz_r,
    r_s,
    r_r,
    late_s,
    late_r,
    load,
    image_load,
    own_sem,
    weight_store,
    store,
    *,
    images,
    heads,
):
    expert_at = lax.axis_index("expert")
    tensor_at = lax.axis_index("tensor")
    z_at, y_at = expert_at // 2, expert_at % 2
    z_last = lax.axis_size("expert") // 2 - 1
    x_at, core_at = tensor_at // 2, tensor_at % 2
    other = 1 - core_at
    rows = images * PITCH
    features = tok_hbm.shape[2]
    wide = features // 2
    share = out_w_ref.shape[0]
    hidden = line.shape[3]
    core_dev = (expert_at, tensor_at + 1 - 2 * core_at)
    x_dev = (expert_at, tensor_at + 2 - 4 * x_at)
    y_dev = (expert_at + 1 - 2 * y_at, tensor_at)
    z_devs = [(expert_at + 2, tensor_at), (expert_at - 2, tensor_at)]
    planes = z_last + 1
    z_others = [((z_at + hop) % planes * 2 + y_at, tensor_at) for hop in (1, 2, 3)]
    greet([(True, device) for device in (core_dev, x_dev, y_dev, *z_others)])
    my_cols = lanes_at(core_at * wide, wide)
    their_cols = lanes_at(other * wide, wide)

    def remote(src, dst, send, recv, device):
        return pltpu.make_async_remote_copy(
            src_ref=src, dst_ref=dst, send_sem=send, recv_sem=recv, device_id=device, device_id_type=MESH
        )

    def at_image(image):
        return aligned(image * PITCH, PITCH)

    def place(way):
        return z_at if way == 0 else z_last - z_at

    def far_lanes(way, piece):
        expert = z_last - piece // 2 if way == 0 else piece // 2
        return pl.ds(expert % 2 * hidden, hidden)

    def line_copy(source, way, piece):
        return remote(source, line.at[way, piece], l_s.at[way, piece], l_r.at[way, piece], z_devs[way])

    def line_copy_on(way, piece):
        return line_copy(line.at[way, piece], way, piece)

    def line_start():
        for way in range(2):

            @pl.when(place(way) == 0)
            def _():
                for piece in range(1, 4):
                    source = (up_second, down_second)[piece % 2]
                    line_copy(source.at[:, far_lanes(way, piece)], way, piece).start()

    def line_add(piece):
        for way in range(2):

            @pl.when(place(way) == 1)
            def _():
                if piece > 0:
                    line_copy_on(way, piece).wait_recv()
                lanes = far_lanes(way, piece)

                def add(part, _):
                    at_rows = aligned(part * 96, 96)
                    total = line[way, piece, at_rows, :].astype(f32) + far_vm[piece % 2, at_rows, lanes].astype(f32)
                    line[way, piece, at_rows, :] = total.astype(bf16)
                    return 0

                lax.fori_loop(0, features // 96, add, 0)
                line_copy_on(way, piece).start()

    def line_pass(piece):
        for way in range(2):

            @pl.when(place(way) == 2)
            def _():
                line_copy_on(way, piece).wait_recv()
                line_copy_on(way, piece).start()

    line_start()
    later = [
        pltpu.make_async_copy((up_second, down_second)[number], far_vm.at[number], own_sem.at[number])
        for number in range(2)
    ]
    is_inner = (z_at == 1) | (z_at == z_last - 1)
    first_copy = pltpu.make_async_copy(line_first, line.at[jnp.where(z_at == 1, 0, 1), 0], own_sem.at[2])

    @pl.when(is_inner)
    def _():
        first_copy.start()

    for copy in later:
        copy.start()

    part_count = m_y.shape[0]
    part_rows_m = rows // part_count

    def m_rows(side, part):
        return aligned(side * rows + part * part_rows_m, part_rows_m)

    def m_core_copy(side, part):
        at = m_rows(side, part)
        return remote(mixed_ref.at[at, their_cols], m_core.at[at, :], mc_s.at[side, part], mc_r.at[side, part], core_dev)

    for part in range(part_count):
        m_core_copy(1, part).start()
    for part in range(part_count):
        m_core_copy(0, part).start()
    m_loads = [
        pltpu.make_async_copy(mixed_ref.at[pl.ds(side * rows, rows), my_cols], m_mine.at[pl.ds(side * rows, rows), :], load.at[side])
        for side in range(2)
    ]

    def image_loads(image):
        at = at_image(image)
        by_image = ((tok_hbm, tok_ref), (q_hbm, q_ref), (k_hbm, k_ref), (v_hbm, v_ref), (att_hbm, att_ref), (lse_hbm, lse_ref))
        by_row = ((grad_h_hbm, grad_h_ref), (resid_ref, rows_kept), (cot_ref, cot_rows))
        pairs = [(source.at[image], target.at[image]) for source, target in by_image]
        pairs += [(source.at[at, :], target.at[at, :]) for source, target in by_row]
        return [pltpu.make_async_copy(source, target, image_load.at[n, image]) for n, (source, target) in enumerate(pairs)]

    def start_loads(image, _):
        for copy in image_loads(image):
            copy.start()
        return 0

    weight_loads = [
        pltpu.make_async_copy(qkv_hbm, qkv_ref, own_sem.at[3]),
        pltpu.make_async_copy(out_w_hbm, out_w_ref, own_sem.at[4]),
    ]
    for copy in weight_loads:
        copy.start()
    start_loads(0, 0)
    m_loads[1].start()
    lax.fori_loop(1, images, start_loads, 0)
    m_loads[0].start()
    route_one = remote(grad_router_ref, route_core, r_s.at[0], r_r.at[0], core_dev)
    route_one.start()

    weight_sum[...] = jnp.zeros_like(weight_sum)
    late_mine[...] = jnp.zeros_like(late_mine)

    def m_y_copy(part):
        return remote(m_core.at[m_rows(1, part), :], m_y.at[part], my_s.at[part], my_r.at[part], y_dev)

    def m_x_copy(part):
        return remote(m_core.at[m_rows(0, part), :], m_x.at[part], mx_s.at[part], mx_r.at[part], x_dev)

    def m_place(part):
        return mixed_out.at[aligned(part * part_rows_m, part_rows_m), :]

    def m_quarter_copy(part):
        return remote(m_out.at[part, other], m_place(part), mq_s.at[part], mq_r.at[part], core_dev)

    def m_store_copy(part):
        return pltpu.make_async_copy(m_out.at[part, core_at], m_place(part), m_store.at[part])

    def m_resid_copy(part):
        at = aligned(part * part_rows_m, part_rows_m)
        return pltpu.make_async_copy(resid_ref.at[at, lanes_at(x_at * wide, wide)], m_resid, load.at[3])

    keeps = x_at == core_at

    def run_m_y(part):
        m_core_copy(1, part).wait_recv()
        at = m_rows(1, part)
        m_core[at, :] = (m_core[at, :].astype(f32) + m_mine[at, :].astype(f32)).astype(bf16)
        m_y_copy(part).start()

    def run_m_x(part):
        if isinstance(part, int) and part == 0:
            m_loads[0].wait()
        m_core_copy(0, part).wait_recv()
        m_y_copy(part).wait_recv()
        at = m_rows(0, part)
        total = m_core[at, :].astype(f32) + m_mine[at, :].astype(f32) + m_y[part].astype(f32)
        m_core[at, :] = total.astype(bf16)

        @pl.when(jnp.logical_not(keeps))
        def _():
            m_x_copy(part).start()

    def run_m_out(part):
        @pl.when(keeps)
        def _():
            m_resid_copy(part).start()
            m_x_copy(part).wait_recv()
            m_resid_copy(part).wait()
            total = m_core[m_rows(0, part), :].astype(f32) + m_x[part].astype(f32)
            mixed = (m_resid[...] + total).astype(bf16)
            m_out[part, 0] = mixed[:, : wide // 2]
            m_out[part, 1] = mixed[:, wide // 2 :]
            m_quarter_copy(part).start()
            m_store_copy(part).start()

    later[0].wait()
    later[1].wait()

    @pl.when(is_inner)
    def _():
        first_copy.wait()

    line_add(0)
    m_loads[1].wait()
    for part in range(part_count):
        run_m_y(part)
    route_one.wait_recv()
    route_core[...] += grad_router_ref[...]
    route_two = remote(route_core, route_x, r_s.at[1], r_r.at[1], x_dev)
    route_two.start()

    def one_core_copy(image):
        return remote(one_to.at[image], one_core.at[image], oc_s.at[image], oc_r.at[image], core_dev)

    def one_x_copy(image):
        return remote(one_core.at[image], one_x.at[image], ox_s.at[image], ox_r.at[image], x_dev)

    def one_total_copy(image):
        return remote(one_x.at[image], one_total.at[image], ot_s.at[image], ot_r.at[image], core_dev)

    store_copy = pltpu.make_async_copy(tokens_low, tokens_out, store.at[0])

    lane = lax.broadcasted_iota(jnp.int32, (PITCH, 2 * HD), 1)
    key_mask = lax.broadcasted_iota(jnp.int32, (PITCH, PITCH), 1) < SEQ
    gain1, shift1, gain2 = (ref[...].reshape(1, features) for ref in (gain1_ref, shift1_ref, gain2_ref))

    def norm_back(grad, gain, normed, inverse):
        scaled = grad * gain
        mean = jnp.mean(scaled, axis=1, keepdims=True)
        along = jnp.mean(scaled * normed, axis=1, keepdims=True)
        return (scaled - mean - normed * along) * inverse

    def add_sums(sums, row, grad, normed):
        sums[row : row + 1, :] += jnp.sum(grad * normed, axis=0, keepdims=True)
        sums[row + 1 : row + 2, :] += jnp.sum(grad, axis=0, keepdims=True)

    def run_attention(image):
        for copy in image_loads(image):
            copy.wait()
        at = at_image(image)
        grad_h = grad_h_ref[at, :].astype(f32)
        normed, inverse = norm_stats(rows_kept[at, :])
        add_sums(late_mine, 2, grad_h, normed)
        grad_resid = cot_rows[at, :].astype(f32) + norm_back(grad_h, gain2, normed, inverse)
        rows_kept[at, :] = grad_resid
        grad_branch = grad_resid.astype(bf16)
        token_normed, _ = norm_stats(tok_ref[image].astype(f32))
        h_one = (token_normed * gain1 + shift1).astype(bf16)
        queries, keys, values, attended = q_ref[image], k_ref[image], v_ref[image], att_ref[image]
        lse = lse_ref[image]
        grad_attended = dot(grad_branch, out_w_ref[...], ((1,), (1,))).astype(bf16)
        grads = [[], [], []]
        for head in range(heads):
            first = head // 2 * 2 * HD
            last = min(first + 2 * HD, heads * HD)
            parts = [whose[:, first:last] for whose in (queries, keys, values, grad_attended)]
            if last - first == 2 * HD:
                own = head_mask(lane, head)
                q_own, k_own, _, g_own = (jnp.where(own, part, jnp.zeros_like(part)) for part in parts)
            else:
                q_own, k_own, _, g_own = parts
            scores = dot(q_own, parts[1], ((1,), (1,))) * (HD**-0.5)
            probs = jnp.where(key_mask, jnp.exp(scores - lse[:, head : head + 1]), 0.0)
            back = dot(g_own, parts[2], ((1,), (1,)))
            product = probs * back
            grad_scores = (product - probs * jnp.sum(product, axis=1, keepdims=True)).astype(bf16)
            pieces = (
                dot(grad_scores, k_own) * (HD**-0.5),
                dot(grad_scores, q_own, ((0,), (0,))) * (HD**-0.5),
                dot(probs.astype(bf16), g_own, ((0,), (0,))),
            )
            for which in range(3):
                if head % 2 == 0:
                    grads[which].append(pieces[which])
                else:
                    grads[which][-1] += pieces[which]
        grad_rows = [jnp.concatenate(grads[which], axis=1).astype(bf16) for which in range(3)]
        grad_one = 0.0
        for which in range(3):
            weight_sum[which * share : (which + 1) * share, :] += dot(grad_rows[which].T, h_one)
            grad_one += dot(grad_rows[which], qkv_ref[which])
        weight_sum[3 * share : 4 * share, :] += dot(attended.T, grad_branch)
        whole[...] = grad_one
        one_mine[image] = whole[:, my_cols].astype(bf16)
        one_to[image] = whole[:, their_cols].astype(bf16)
        one_core_copy(image).start()

    def run_one_x(image):
        one_core_copy(image).wait_recv()
        one_core[image] = (one_core[image].astype(f32) + one_mine[image].astype(f32)).astype(bf16)
        one_x_copy(image).start()

    def run_one_total(image):
        one_x_copy(image).wait_recv()
        one_x[image] = (one_core[image].astype(f32) + one_x[image].astype(f32)).astype(bf16)
        one_total_copy(image).start()

    def run_tokens(image):
        one_total_copy(image).wait_recv()
        whole[:, my_cols] = one_x[image].astype(f32)
        whole[:, their_cols] = one_total[image].astype(f32)
        grad_one = whole[...]
        at = at_image(image)
        normed, inverse = norm_stats(tok_ref[image].astype(f32))
        add_sums(late_mine, 0, grad_one, normed)
        total = rows_kept[at, :] + norm_back(grad_one, gain1, normed, inverse)
        whole[...] = total
        for number in range(images):

            @pl.when(image == number)
            def _():
                rows_kept[pl.ds(number * SEQ, SEQ), :] = whole[pl.ds(0, SEQ), :]


    def stage(tick, lag, run):
        image = tick - lag

        @pl.when((image >= 0) & (image < images))
        def _():
            run(image)

    def at_tick(tick, when, run):
        @pl.when(tick == when)
        def _():
            run()

    def line_second():
        line_add(1)
        line_pass(0)

    def line_third():
        line_add(2)
        line_pass(1)

    def per_tick(tick, _):
        stage(tick, 0, run_attention)
        stage(tick, 1, run_one_x)
        stage(tick, 4, run_one_total)
        stage(tick, 5, run_tokens)
        at_tick(tick, 5, lambda: run_m_x(0))
        at_tick(tick, 3, line_second)
        at_tick(tick, 6, line_third)
        at_tick(tick, 7, lambda: run_m_x(1))
        return 0

    for copy in weight_loads:
        copy.wait()
    lax.fori_loop(0, images, per_tick, 0)

    part_rows = shared.shape[1]
    chunks = 2
    chunk_rows = part_rows // chunks
    quarter = chunk_rows // planes

    def cast(piece, _):
        for side in range(2):
            at_rows = aligned(piece * 96, 96)
            shared[side, at_rows, :] = weight_sum[aligned(side * part_rows + piece * 96, 96), :].astype(bf16)
        return 0

    lax.fori_loop(0, part_rows // 96, cast, 0)

    def y_piece(number):
        inner = jnp.where(z_at == 1, jnp.where(number < 2, z_last - number, number - 2), jnp.where(number < 2, number, 5 - number))
        return jnp.where(z_at == 0, z_last - number, jnp.where(z_at == z_last, number, inner))

    def quarter_at(chunk, piece):
        return aligned(chunk * chunk_rows + piece * quarter, quarter)

    def shared_y_copy(chunk, number):
        at_rows = quarter_at(chunk, y_piece(number))
        return remote(
            shared.at[1 - y_at, at_rows, :], shared_y.at[at_rows, :], sy_s.at[chunk, number], sy_r.at[chunk, number], y_dev
        )

    def take_y(chunk, number):
        shared_y_copy(chunk, number).wait_recv()
        at_rows = quarter_at(chunk, y_piece(number))
        weight_half[at_rows, :] = shared[y_at, at_rows, :].astype(f32) + shared_y[at_rows, :].astype(f32)

    def quarter_of(step, at, way):
        mirrored = z_last - step + at
        return mirrored if way == 0 else z_last - mirrored

    def small_copy(chunk, step, way):
        return remote(
            shared_line.at[chunk, way, 0, step],
            shared_line.at[chunk, way, 1, step],
            sl_s.at[chunk, way, step],
            sl_r.at[chunk, way, step],
            z_devs[way],
        )

    def sum_wait(chunk, step):
        for way in range(2):
            at = place(way)

            @pl.when((at > 0) & (at - 1 <= step))
            def _():
                small_copy(chunk, step, way).wait_recv()

    def sum_send(chunk, step):
        for way in range(2):
            at = place(way)

            @pl.when((at <= step) & (at < z_last))
            def _():
                at_rows = quarter_at(chunk, quarter_of(step, at, way))
                if step == 0:
                    shared_line[chunk, way, 0, step] = weight_half[at_rows, :].astype(bf16)
                else:
                    came = jnp.where(at > 0, shared_line[chunk, way, 1, step - 1].astype(f32), 0.0)
                    shared_line[chunk, way, 0, step] = (weight_half[at_rows, :] + came).astype(bf16)
                small_copy(chunk, step, way).start()

    def final_rows(chunk, side, piece):
        return shared_all.at[side, quarter_at(chunk, piece), :]

    def gather_z(chunk, step, way, piece):
        ref = final_rows(chunk, y_at, piece)
        return remote(ref, ref, sg_s.at[chunk, way, step], sg_r.at[chunk, way, step], z_devs[way])

    def gather_y(chunk, step, way, piece, side):
        ref = final_rows(chunk, side, piece)
        return remote(ref, ref, sz_s.at[chunk, way, step], sz_r.at[chunk, way, step], y_dev)

    def piece_out(step, way):
        return z_at - step if way == 0 else z_at + step

    def piece_in(step, way):
        return z_at - 1 - step if way == 0 else z_at + 1 + step

    def gather_send(chunk, step):
        for way in range(2):
            at = place(way)

            @pl.when((at >= step) & (at < z_last))
            def _():
                gather_z(chunk, step, way, piece_out(step, way)).start()

    def gather_take(chunk, step):
        for way in range(2):

            @pl.when(place(way) >= 1 + step)
            def _():
                gather_z(chunk, step, way, piece_in(step, way)).wait_recv()
                gather_y(chunk, step + 1, way, piece_in(step, way), y_at).start()

    def finish_sum(chunk):
        own_rows = quarter_at(chunk, z_at)
        from_below = jnp.where(z_at > 0, shared_line[chunk, 0, 1, 2].astype(f32), 0.0)
        from_above = jnp.where(z_at < z_last, shared_line[chunk, 1, 1, 2].astype(f32), 0.0)
        shared_all[y_at, own_rows, :] = (weight_half[own_rows, :] + from_below + from_above).astype(bf16)
        gather_y(chunk, 0, 0, z_at, y_at).start()

    late_y_copy = remote(late_mine, late_y, late_s.at[0], late_r.at[0], y_dev)

    def late_copy(number):
        ref = late_z.at[z_at]
        return remote(ref, ref, late_s.at[number + 1], late_r.at[number + 1], z_others[number])

    def meanwhile(place_in_order):
        if place_in_order == 0:
            run_one_x(images - 1)
            run_tokens(images - 5)
            run_one_total(images - 4)
            run_m_x(part_count - 2)
        if place_in_order == 1:
            run_m_x(part_count - 1)
            run_tokens(images - 4)
            run_one_total(images - 3)
        if place_in_order == 2:
            run_m_out(0)
            run_tokens(images - 3)
        if place_in_order == 3:
            run_one_total(images - 2)
            run_m_out(1)
            run_tokens(images - 2)
        if place_in_order == 4:
            run_one_total(images - 1)
            run_m_out(2)
        if place_in_order == 5:
            run_tokens(images - 1)
            line_add(3)
            route_two.wait_recv()
            late_mine[8:16, :] = route_core[...] + route_x[...]
            late_y_copy.start()
            tokens_low[...] = rows_kept[pl.ds(0, images * SEQ), :].astype(bf16)
            store_copy.start()
        if place_in_order == 6:
            run_m_out(3)
            late_y_copy.wait_recv()
            late_z[z_at] = late_mine[...] + late_y[...]
            for number in range(planes - 1):
                late_copy(number).start()

    for number in range(4):
        for chunk in range(chunks):
            shared_y_copy(chunk, number).start()
    meanwhile(0)
    for step in range(3):
        for chunk in range(chunks):
            if step > 0:
                sum_wait(chunk, step - 1)
            take_y(chunk, step)
            sum_send(chunk, step)
        if step == 2:
            for chunk in range(chunks):
                take_y(chunk, 3)
        meanwhile(1 + step)
    for chunk in range(chunks):
        sum_wait(chunk, 2)
        finish_sum(chunk)
        gather_send(chunk, 0)
    for step in range(3):
        meanwhile(4 + step)
        for chunk in range(chunks):
            gather_take(chunk, step)
            if step < 2:
                gather_send(chunk, step + 1)

    for way in range(2):

        @pl.when(place(way) == 2)
        def _():
            line_copy_on(way, 2).wait_recv()
            line_copy_on(way, 3).wait_recv()

        @pl.when(place(way) == z_last)
        def _():
            line_copy_on(way, 0).wait_recv()
            line_copy_on(way, 1).wait_recv()

    from_far = 1 - z_at // 2
    first_piece = jnp.where((z_at == 0) | (z_at == z_last), 0, 2)

    line_out_copies = [
        pltpu.make_async_copy(line.at[from_far, first_piece + n], line_out.at[n], weight_store.at[n]) for n in range(2)
    ]
    for copy in line_out_copies:
        copy.start()
    for chunk in range(chunks):
        gather_y(chunk, 0, 0, z_at, 1 - y_at).wait_recv()
        for step in range(3):
            for way in range(2):

                @pl.when(place(way) >= 1 + step)
                def _():
                    gather_y(chunk, step + 1, way, piece_in(step, way), 1 - y_at).wait_recv()

    for number in range(planes - 1):
        late_copy(number).wait_recv()
    late = late_z[0]
    for plane in range(1, planes):
        late += late_z[plane]
    sums_all[...] = late
    out_copies = [
        pltpu.make_async_copy(shared_all, weights_out, weight_store.at[2]),
        pltpu.make_async_copy(sums_all, sums_out, weight_store.at[3]),
    ]
    for copy in out_copies:
        copy.start()
    route_one.wait_send()
    route_two.wait_send()

    def drain(image, _):
        for copy in (one_core_copy, one_x_copy, one_total_copy):
            copy(image).wait_send()
        return 0

    lax.fori_loop(0, images, drain, 0)
    for part in range(part_count):
        m_core_copy(0, part).wait_send()
        m_core_copy(1, part).wait_send()
        m_y_copy(part).wait_send()

        @pl.when(keeps)
        def _():
            m_quarter_copy(part).wait_send()
            m_store_copy(part).wait()

        @pl.when(jnp.logical_not(keeps))
        def _():
            m_x_copy(part).wait_send()
            m_quarter_copy(part).wait_recv()

    for copy in (*line_out_copies, *out_copies, store_copy):
        copy.wait()
    late_y_copy.wait_send()
    for number in range(planes - 1):
        late_copy(number).wait_send()
    for way in range(2):

        @pl.when(place(way) <= 1)
        def _():
            for piece in range(1, 4):
                line_copy_on(way, piece).wait_send()

        @pl.when(place(way) == 1)
        def _():
            line_copy_on(way, 0).wait_send()

        @pl.when(place(way) == 2)
        def _():
            for piece in range(2):
                line_copy_on(way, piece).wait_send()

    for chunk in range(chunks):
        gather_y(chunk, 0, 0, z_at, y_at).wait_send()
        for number in range(4):
            shared_y_copy(chunk, number).wait_send()
        for step in range(3):
            for way in range(2):
                at = place(way)

                @pl.when((at <= step) & (at < z_last))
                def _():
                    small_copy(chunk, step, way).wait_send()

                @pl.when((at >= step) & (at < z_last))
                def _():
                    gather_z(chunk, step, way, piece_out(step, way)).wait_send()

                @pl.when(at >= 1 + step)
                def _():
                    gather_y(chunk, step + 1, way, piece_in(step, way), y_at).wait_send()


def run_backward(gain1, shift1, gain2, grad_router, qkv_w, out_w, tok, *streamed):
    images, _, features = tok.shape
    rows = images * PITCH
    share = out_w.shape[0]
    heads = share // HD
    hidden = streamed[-1].shape[1]
    wide = features // 2
    parts = 4
    vmem = pl.BlockSpec(memory_space=pltpu.VMEM)
    anywhere = pl.BlockSpec(memory_space=pl.ANY)
    shape = jax.ShapeDtypeStruct
    dma = pltpu.SemaphoreType.DMA
    block = (images, PITCH, wide)
    return pl.pallas_call(
        partial(backward_kernel, images=images, heads=heads),
        out_shape=[
            shape((2, features, hidden), bf16),
            shape((images * SEQ, features), bf16),
            shape((2, features // 2, features), bf16),
            shape((16, features), f32),
            shape((rows, wide // 2), bf16),
        ],
        in_specs=[vmem] * 4 + [anywhere] * (3 + len(streamed)),
        out_specs=[anywhere] * 5,
        scratch_shapes=[
            pltpu.VMEM(qkv_w.shape, bf16),
            pltpu.VMEM(out_w.shape, bf16),
            pltpu.VMEM((images, PITCH, features), bf16),
            *[pltpu.VMEM((images, PITCH, share), bf16)] * 4,
            pltpu.VMEM((images, PITCH, 128), f32),
            pltpu.VMEM((rows, features), bf16),
            pltpu.VMEM((rows, features), f32),
            pltpu.VMEM((rows, features), bf16),
            pltpu.VMEM((2 * rows, wide), bf16),
            pltpu.VMEM((2 * rows, wide), bf16),
            *[pltpu.VMEM((parts, rows // parts, wide), bf16)] * 2,
            pltpu.VMEM((parts, 2, rows // parts, wide // 2), bf16),
            pltpu.VMEM((rows // parts, wide), f32),
            pltpu.VMEM((2, features, 2 * hidden), bf16),
            *[pltpu.VMEM(block, bf16)] * 5,
            pltpu.VMEM((2, 4, features, hidden), bf16),
            pltpu.VMEM((features, features), f32),
            pltpu.VMEM((features // 2, features), f32),
            pltpu.VMEM((2, features // 2, features), bf16),
            pltpu.VMEM((features // 2, features), bf16),
            pltpu.VMEM((2, 2, 2, 3, features // 16, features), bf16),
            pltpu.VMEM((2, features // 2, features), bf16),
            *[pltpu.VMEM((8, features), f32)] * 2,
            *[pltpu.VMEM((16, features), f32)] * 2,
            pltpu.VMEM((4, 16, features), f32),
            pltpu.VMEM((16, features), f32),
            pltpu.VMEM((images * SEQ, features), bf16),
            pltpu.VMEM((PITCH, features), f32),
        ]
        + [dma((2, parts))] * 2
        + [dma((parts,))] * 7
        + [dma((images,))] * 6
        + [dma((2, 4))] * 2
        + [dma((2, 4))] * 2
        + [dma((2, 2, 3))] * 4
        + [dma((2, 2, 4))] * 2
        + [dma((2,))] * 2
        + [dma((4,))] * 2
        + [dma((4,)), dma((9, images)), dma((5,)), dma((4,)), dma((1,))],
        compiler_params=pltpu.CompilerParams(
            collective_id=2, has_side_effects=True, vmem_limit_bytes=63 << 20
        ),
    )(gain1, shift1, gain2, grad_router, qkv_w, out_w, tok, *streamed)


def last_kernel(
    side_ref, tokens_ref, weights_ref, up_first, up_pair, down_first, down_pair, line_ref, tokens_out, qkv_out, out_w_out, up_out, down_out
):
    share = out_w_out.shape[0]
    tokens_out[...] = tokens_ref[...].astype(f32)
    for which in range(3):
        qkv_out[which] = weights_ref[which * share : (which + 1) * share, :].astype(f32)
    out_w_out[...] = weights_ref[3 * share :, :].astype(f32)
    up_out[...] = up_first[...].astype(f32) + up_pair[...].astype(f32) + line_ref[0].astype(f32)
    down_out[...] = (down_first[...].astype(f32) + down_pair[...].astype(f32) + line_ref[1].astype(f32)).T


def run_last(side, tokens, weights, up_first, up_pair, down_first, down_pair, line, share):
    rows, features = tokens.shape
    hidden = up_pair.shape[1]
    shape = jax.ShapeDtypeStruct

    def lanes(height):
        return pl.BlockSpec((height, 128), lambda n, side: (0, n))

    own = pl.BlockSpec((128, hidden), lambda n, side: (n, side[0]))
    plain = pl.BlockSpec((128, hidden), lambda n, side: (n, 0))
    return pl.pallas_call(
        last_kernel,
        grid_spec=pltpu.PrefetchScalarGridSpec(
            num_scalar_prefetch=1,
            grid=(features // 128,),
            in_specs=[
                lanes(rows),
                lanes(features),
                own,
                plain,
                own,
                plain,
                pl.BlockSpec((2, 128, hidden), lambda n, side: (0, n, 0)),
            ],
            out_specs=[
                lanes(rows),
                pl.BlockSpec((3, share, 128), lambda n, side: (0, 0, n)),
                lanes(share),
                plain,
                lanes(hidden),
            ],
        ),
        out_shape=[
            shape((rows, features), f32),
            shape((3, share, features), f32),
            shape((share, features), f32),
            shape((features, hidden), f32),
            shape((hidden, features), f32),
        ],
    )(side, tokens, weights, up_first, up_pair, down_first, down_pair, line)


def per_image(rows_in):
    images = rows_in.shape[0] // SEQ
    blocks = rows_in.reshape(images, SEQ, rows_in.shape[1])
    return jnp.pad(blocks, ((0, 0), (0, PITCH - SEQ), (0, 0)))


def unpad(blocks):
    images = blocks.shape[0]
    return blocks[:, :SEQ].reshape(images * SEQ, blocks.shape[2])


def per_device_dense(
    tokens,
    gain_attn,
    shift_attn,
    qkv_weight,
    out_weight,
    gain_moe,
    shift_moe,
    router_weight,
    expert_up,
    expert_down,
    routes,
    keep_mask,
    cotangent,
):
    row_count, feature_count = tokens.shape
    images = row_count // SEQ
    rows = images * PITCH
    tensor_count = lax.axis_size("tensor")
    quarter_width = feature_count // tensor_count
    experts_all = router_weight.shape[1]
    hidden = expert_up.shape[2]
    kept_routes = per_image(jnp.where(keep_mask > 0, routes, -1) + 1).reshape(rows, 2) - 1
    chosen = kept_routes[:, :, None] == jnp.arange(128, dtype=jnp.int32)[None, None, :]
    kept = jnp.any(chosen, axis=1).astype(bf16)
    router_wide = jnp.pad(router_weight.T, ((0, 128 - experts_all), (0, 0)))
    cot_turned = jnp.pad(cotangent.T, ((0, 0), (0, -row_count % 128)))
    qkv_turned = jnp.swapaxes(qkv_weight, 1, 2)
    (
        queries,
        keys,
        values,
        attended,
        lse,
        resid,
        h_all,
        cot_all,
        kept_all,
        up_all,
        down_all,
        mixed_first,
        grad_h_first,
        gate_first,
        up_first,
        down_first,
        tok,
    ) = run_forward(
        tokens,
        gain_attn,
        shift_attn,
        gain_moe,
        shift_moe,
        qkv_turned,
        out_weight,
        expert_up[0],
        expert_down[0],
        cot_turned,
        kept,
        router_wide,
        experts_all,
    )
    mixed_part, grad_router, up_second, down_second, grad_h_two, up_pair, down_pair, line_first = run_second_pair(
        h_all,
        cot_all,
        kept_all,
        router_wide,
        mixed_first,
        grad_h_first,
        gate_first,
        up_all,
        down_all,
        up_first,
        down_first,
        experts_all,
    )
    line_sum, tokens_grad, weights_grad, sums, mixed = run_backward(
        gain_attn,
        shift_attn,
        gain_moe,
        grad_router,
        qkv_turned,
        out_weight,
        tok,
        queries,
        keys,
        values,
        attended,
        lse,
        grad_h_two,
        resid,
        cot_all,
        mixed_part,
        up_second,
        down_second,
        line_first,
    )
    side = (lax.axis_index("expert") // 2 % 2).astype(jnp.int32)[None]
    grad_tokens, grad_qkv, grad_out, grad_up, grad_down = run_last(
        side,
        tokens_grad,
        weights_grad.reshape(feature_count, feature_count),
        up_first,
        up_pair,
        down_first,
        down_pair,
        line_sum,
        qkv_weight.shape[2],
    )
    return (
        unpad(mixed.reshape(images, PITCH, quarter_width)),
        grad_tokens,
        sums[0],
        sums[1],
        jnp.swapaxes(grad_qkv, 1, 2),
        grad_out,
        sums[2],
        sums[3],
        sums[8 : 8 + experts_all].T,
        grad_up[None],
        grad_down[None],
    )


def per_device(*arguments):
    router_weight = arguments[7]
    if router_weight.shape[1] == 4 and lax.axis_size("expert") == 8 and lax.axis_size("tensor") == 4:
        return per_device_dense(*arguments)
    return per_device_routed(*arguments)


def solution(mesh):
    placed = (
        P("expert", None),
        P(),
        P(),
        P(None, None, "tensor"),
        P("tensor", None),
        P(),
        P(),
        P(),
        P("expert", None, "tensor"),
        P("expert", "tensor", None),
        P("expert", None),
        P("expert", None),
        P("expert", "tensor"),
    )
    return jax.shard_map(
        per_device,
        mesh=mesh,
        in_specs=placed,
        out_specs=(
            P("expert", "tensor"),
            P("expert", None),
            P(),
            P(),
            P(None, None, "tensor"),
            P("tensor", None),
            P(),
            P(),
            P(),
            P("expert", None, "tensor"),
            P("expert", "tensor", None),
        ),
        check_vma=False,
    )
```

```python
from functools import partial

import jax
import jax.numpy as jnp
from jax import lax
from jax.experimental import pallas as pl
from jax.experimental.pallas import tpu as pltpu
from jax.sharding import PartitionSpec as P

HD = 64
SEQ = 197


norm_epsilon = 1e-06


def norm_rows(values, gain, shift):
    row_mean = jnp.mean(values, axis=-1, keepdims=True)
    centred = values - row_mean
    spread = jnp.mean(centred * centred, axis=-1, keepdims=True)
    return centred * lax.rsqrt(spread + norm_epsilon) * gain + shift


def gelu_exact(values):
    return jax.nn.gelu(values, approximate=False)


def gate_from_logits(logit_rows, picked_rows, keep_rows):
    router_probs = jax.nn.softmax(logit_rows, axis=-1)
    return jnp.sum(jnp.where(picked_rows, router_probs[:, None, :], 0.0), axis=-1) * keep_rows


def attention_forward(h_rows, qkv_w, out_w):
    row_total_count = h_rows.shape[0]
    head_count = qkv_w.shape[2] // HD
    image_count = row_total_count // SEQ
    score_scale = HD ** (-0.5)
    projected = jnp.einsum("td,cdf->ctf", h_rows, qkv_w, preferred_element_type=jnp.float32).astype(
        jnp.bfloat16
    )
    split_heads = projected.reshape(3, image_count, SEQ, head_count, HD)
    queries = split_heads[0]
    keys_all = split_heads[1]
    values_all = split_heads[2]
    scores = (
        jnp.einsum("gqhe,gkhe->ghqk", queries, keys_all, preferred_element_type=jnp.float32)
        * score_scale
    )
    row_peak = jnp.max(scores, axis=-1, keepdims=True)
    exp_scores = jnp.exp(scores - row_peak)
    row_total = jnp.sum(exp_scores, axis=-1, keepdims=True)
    log_total = row_peak + jnp.log(row_total)
    weights = (exp_scores / row_total).astype(jnp.bfloat16)
    attended = jnp.einsum(
        "ghqk,gkhe->gqhe", weights, values_all, preferred_element_type=jnp.float32
    ).astype(jnp.bfloat16)
    attended = attended.reshape(row_total_count, head_count * HD)
    partial_out = jnp.dot(attended, out_w, preferred_element_type=jnp.float32)
    return (partial_out, (attended, queries, keys_all, values_all, log_total))


def attention_backward(grad_branch, saved, h_rows, qkv_w, out_w):
    attended, queries, keys_all, values_all, log_total = saved
    row_total_count = h_rows.shape[0]
    head_count = qkv_w.shape[2] // HD
    image_count = row_total_count // SEQ
    score_scale = HD ** (-0.5)
    grad_out = jnp.einsum("tc,td->cd", attended, grad_branch, preferred_element_type=jnp.float32)
    grad_attended = jnp.einsum(
        "td,cd->tc", grad_branch, out_w, preferred_element_type=jnp.float32
    ).astype(jnp.bfloat16)
    grad_attended = grad_attended.reshape(image_count, SEQ, head_count, HD)
    scores_again = (
        jnp.einsum("gqhe,gkhe->ghqk", queries, keys_all, preferred_element_type=jnp.float32)
        * score_scale
    )
    probs_again = jnp.exp(scores_again - log_total)
    grad_weights = jnp.einsum(
        "gqhe,gkhe->ghqk", grad_attended, values_all, preferred_element_type=jnp.float32
    )
    grad_scores = (
        probs_again * (grad_weights - jnp.sum(probs_again * grad_weights, axis=-1, keepdims=True))
    ).astype(jnp.bfloat16)
    grad_queries = (
        jnp.einsum("ghqk,gkhe->gqhe", grad_scores, keys_all, preferred_element_type=jnp.float32)
        * score_scale
    )
    grad_keys = (
        jnp.einsum("ghqk,gqhe->gkhe", grad_scores, queries, preferred_element_type=jnp.float32)
        * score_scale
    )
    grad_values = jnp.einsum(
        "ghqk,gqhe->gkhe",
        probs_again.astype(jnp.bfloat16),
        grad_attended,
        preferred_element_type=jnp.float32,
    )
    grad_rows = (
        jnp.stack([grad_queries, grad_keys, grad_values])
        .astype(jnp.bfloat16)
        .reshape(3, row_total_count, head_count * HD)
    )
    grad_qkv = jnp.einsum("td,ctf->cdf", h_rows, grad_rows, preferred_element_type=jnp.float32)
    grad_h_one = jnp.einsum("ctf,cdf->td", grad_rows, qkv_w, preferred_element_type=jnp.float32)
    return (grad_qkv, grad_out, grad_h_one)


def moe_tail(
    grad_h_rows,
    grad_gate_rows,
    grad_out_rows,
    h_two_rows,
    resid_rows,
    gate_back,
    router_weight,
    gain_moe,
    shift_moe,
):
    row_total_count = grad_h_rows.shape[0]
    grad_gate = jnp.sum(grad_gate_rows.reshape(row_total_count, -1, 2), axis=1)
    grad_logits = gate_back(grad_gate)[0].astype(jnp.bfloat16)
    grad_router = jnp.einsum(
        "td,te->de", h_two_rows, grad_logits, preferred_element_type=jnp.float32
    )
    grad_h_two = grad_h_rows + jnp.einsum(
        "te,de->td", grad_logits, router_weight, preferred_element_type=jnp.float32
    )
    norm_out, norm_back = jax.vjp(norm_rows, resid_rows, gain_moe, shift_moe)
    grad_resid_norm, grad_gain_moe, grad_shift_moe = norm_back(grad_h_two)
    return (grad_out_rows + grad_resid_norm, grad_router, grad_gain_moe, grad_shift_moe)


def per_device_routed(
    tokens,
    gain_attn,
    shift_attn,
    qkv_weight,
    out_weight,
    gain_moe,
    shift_moe,
    router_weight,
    expert_up,
    expert_down,
    routes,
    keep_mask,
    cotangent,
):
    row_count, feature_count = tokens.shape
    tensor_count = lax.axis_size("tensor")
    expert_count = lax.axis_size("expert")
    tensor_here = lax.axis_index("tensor")
    quarter_width = feature_count // tensor_count
    col_start = tensor_here * quarter_width
    experts_all = router_weight.shape[1]
    capacity = max(2, 7 * row_count // (2 * experts_all))
    tokens_float = tokens.astype(jnp.float32)
    h_one = norm_rows(tokens_float, gain_attn, shift_attn).astype(jnp.bfloat16)
    partial_out, saved = attention_forward(h_one, qkv_weight, out_weight)
    branch = lax.psum(partial_out, "tensor")
    resid = tokens_float + branch
    h_two = norm_rows(resid, gain_moe, shift_moe).astype(jnp.bfloat16)
    logits = jnp.dot(h_two, router_weight, preferred_element_type=jnp.float32)
    keep_float = keep_mask.astype(jnp.float32)
    picked = routes[:, :, None] == jnp.arange(experts_all, dtype=jnp.int32)[None, None, :]
    gate_values, gate_back = jax.vjp(
        partial(gate_from_logits, picked_rows=picked, keep_rows=keep_float), logits
    )
    flat_expert = routes.reshape(-1)
    one_hot = (flat_expert[:, None] == jnp.arange(experts_all, dtype=jnp.int32)[None, :]).astype(
        jnp.int32
    )
    rank_within = jnp.sum((jnp.cumsum(one_hot, axis=0) - one_hot) * one_hot, axis=1)
    slot_index = flat_expert * capacity + rank_within
    token_index = jnp.repeat(jnp.arange(row_count, dtype=jnp.int32), 2)
    live_route = keep_mask.reshape(-1) > 0
    source_table = (
        jnp.full((experts_all * capacity,), row_count, jnp.int32)
        .at[slot_index]
        .set(jnp.where(live_route, token_index, row_count))
    )
    padded_rows = jnp.concatenate([h_two, jnp.zeros((1, feature_count), jnp.bfloat16)], axis=0)
    dispatch = padded_rows[source_table].reshape(experts_all, capacity, feature_count)
    paired = jnp.broadcast_to(dispatch[:, None], (experts_all, 2, capacity, feature_count)).reshape(
        expert_count, capacity, feature_count
    )
    arrived = lax.all_to_all(paired, "expert", split_axis=0, concat_axis=0, tiled=True)
    expert_rows = arrived.reshape(expert_count * capacity, feature_count)
    up_local = expert_up[0]
    down_local = expert_down[0]
    pre_act = jnp.dot(expert_rows, up_local, preferred_element_type=jnp.float32)
    hidden_float, gelu_back = jax.vjp(gelu_exact, pre_act)
    hidden = hidden_float.astype(jnp.bfloat16)
    partial_down = jnp.dot(hidden, down_local, preferred_element_type=jnp.float32)
    summed = lax.psum_scatter(partial_down, "tensor", scatter_dimension=1, tiled=True)
    returned = lax.all_to_all(
        summed.reshape(expert_count, capacity, quarter_width),
        "expert",
        split_axis=0,
        concat_axis=0,
        tiled=True,
    )
    answer_table = jnp.sum(
        returned.reshape(experts_all, 2, capacity, quarter_width), axis=1
    ).astype(jnp.bfloat16)
    answers = (
        answer_table.reshape(experts_all * capacity, quarter_width)[slot_index]
        .astype(jnp.float32)
        .reshape(row_count, 2, quarter_width)
    )
    resid_part = lax.dynamic_slice_in_dim(resid, col_start, quarter_width, 1)
    mixed = (resid_part + jnp.sum(gate_values[:, :, None] * answers, axis=1)).astype(jnp.bfloat16)
    grad_part = cotangent.astype(jnp.float32)
    grad_answers = (
        (gate_values[:, :, None] * grad_part[:, None, :])
        .astype(jnp.bfloat16)
        .reshape(2 * row_count, quarter_width)
    )
    grad_gate_part = jnp.sum(grad_part[:, None, :] * answers, axis=-1)
    outgoing = (
        jnp.zeros((experts_all * capacity, quarter_width), jnp.bfloat16)
        .at[slot_index]
        .set(grad_answers)
    )
    outgoing = jnp.broadcast_to(
        outgoing.reshape(experts_all, 1, capacity, quarter_width),
        (experts_all, 2, capacity, quarter_width),
    ).reshape(expert_count, capacity, quarter_width)
    incoming = lax.all_to_all(outgoing, "expert", split_axis=0, concat_axis=0, tiled=True)
    grad_full = lax.all_gather(incoming, "tensor", axis=2, tiled=True).reshape(
        expert_count * capacity, feature_count
    )
    grad_hidden = jnp.einsum("rd,fd->rf", grad_full, down_local, preferred_element_type=jnp.float32)
    grad_pre = gelu_back(grad_hidden)[0].astype(jnp.bfloat16)
    grad_down = jnp.einsum("rf,rd->fd", hidden, grad_full, preferred_element_type=jnp.float32)
    grad_up = jnp.einsum("rd,rf->df", expert_rows, grad_pre, preferred_element_type=jnp.float32)
    grad_rows_partial = jnp.einsum(
        "rf,df->rd", grad_pre, up_local, preferred_element_type=jnp.float32
    )
    grad_rows_sum = lax.psum_scatter(
        grad_rows_partial.astype(jnp.bfloat16), "tensor", scatter_dimension=1, tiled=True
    ).astype(jnp.float32)
    sent_back = lax.all_to_all(
        grad_rows_sum.reshape(expert_count, capacity, quarter_width).astype(jnp.bfloat16),
        "expert",
        split_axis=0,
        concat_axis=0,
        tiled=True,
    ).astype(jnp.float32)
    grad_table = jnp.sum(sent_back.reshape(experts_all, 2, capacity, quarter_width), axis=1).astype(
        jnp.bfloat16
    )
    grad_inputs = (
        grad_table.reshape(experts_all * capacity, quarter_width)[slot_index]
        .astype(jnp.float32)
        .reshape(row_count, 2, quarter_width)
    )
    grad_h_part = jnp.sum(grad_inputs * keep_float[:, :, None], axis=1)
    grad_h_full, grad_gate_all, grad_out_full = (
        lax.all_gather(grad_h_part, "tensor", axis=1, tiled=True),
        lax.all_gather(grad_gate_part, "tensor", axis=1, tiled=True),
        lax.all_gather(grad_part, "tensor", axis=1, tiled=True),
    )
    grad_resid, grad_router, grad_gain_moe, grad_shift_moe = moe_tail(
        grad_h_full,
        grad_gate_all,
        grad_out_full,
        h_two,
        resid,
        gate_back,
        router_weight,
        gain_moe,
        shift_moe,
    )
    grad_qkv, grad_out, grad_h_one_part = attention_backward(
        grad_resid.astype(jnp.bfloat16), saved, h_one, qkv_weight, out_weight
    )
    grad_h_one = lax.psum(grad_h_one_part.astype(jnp.bfloat16), "tensor").astype(jnp.float32)
    norm_one_out, norm_one_back = jax.vjp(norm_rows, tokens_float, gain_attn, shift_attn)
    grad_tok_norm, grad_gain_attn, grad_shift_attn = norm_one_back(grad_h_one)
    grad_tokens = grad_resid + grad_tok_norm
    summed_grads = lax.psum(
        (
            grad_gain_attn,
            grad_shift_attn,
            grad_qkv,
            grad_out,
            grad_gain_moe,
            grad_shift_moe,
            grad_router,
        ),
        "expert",
    )
    grad_qkv_mine = summed_grads[2]
    grad_out_mine = summed_grads[3]
    return (
        mixed,
        grad_tokens,
        summed_grads[0],
        summed_grads[1],
        grad_qkv_mine,
        grad_out_mine,
        summed_grads[4],
        summed_grads[5],
        summed_grads[6],
        grad_up[None],
        grad_down[None],
    )


MESH = pl.DeviceIdType.MESH
f32 = jnp.float32
bf16 = jnp.bfloat16
PITCH = 208


def dot(left, right, over=((1,), (0,))):
    return lax.dot_general(left, right, (over, ((), ())), preferred_element_type=f32)


def aligned(start, size):
    return pl.ds(pl.multiple_of(start, 16), size)


def lanes_at(start, size):
    return pl.ds(pl.multiple_of(start, 128), size)


def norm_stats(values):
    row_mean = jnp.mean(values, axis=1, keepdims=True)
    centred = values - row_mean
    inverse = lax.rsqrt(jnp.mean(centred * centred, axis=1, keepdims=True) + norm_epsilon)
    return centred * inverse, inverse


def greet(neighbours):
    barrier = pltpu.get_barrier_semaphore()
    count = 0
    for is_there, device in neighbours:

        @pl.when(is_there)
        def _():
            pl.semaphore_signal(barrier, inc=1, device_id=device, device_id_type=MESH)

        count = count + jnp.where(is_there, 1, 0)
    pl.semaphore_wait(barrier, count)


def head_mask(lane, head):
    return (lane < HD) if head % 2 == 0 else (lane >= HD)


def expert_math(h_rows, cot_rows, kept, router, up, down, pair, experts):
    block = h_rows.shape[0]
    hidden = up.shape[1] // 2
    lane = lax.broadcasted_iota(jnp.int32, (block, 128), 1)
    logits = jnp.where(lane < experts, dot(h_rows, router, ((1,), (1,))), -1e30)
    powers = jnp.exp(logits - jnp.max(logits, axis=1, keepdims=True))
    probs = powers / jnp.sum(powers, axis=1, keepdims=True)
    gates = kept * probs
    pre_act = dot(h_rows, up)
    back = dot(cot_rows, down, ((1,), (1,)))
    normal_cdf = 0.5 + 0.5 * lax.erf(pre_act * 0.7071067811865476)
    gelu = pre_act * normal_cdf
    slope = normal_cdf + pre_act * (0.3989422804014327 * jnp.exp(-0.5 * pre_act * pre_act))
    product = gelu * back
    grad_gate = jnp.zeros((block, 128), f32)
    spread = []
    for side in range(2):
        chosen = lane == 2 * pair + side
        part = jnp.sum(product[:, side * hidden : (side + 1) * hidden], axis=1, keepdims=True)
        grad_gate = jnp.where(chosen, part, grad_gate)
        gate = jnp.sum(jnp.where(chosen, gates, 0.0), axis=1, keepdims=True)
        spread.append(jnp.broadcast_to(gate, (block, hidden)))
    gate = jnp.concatenate(spread, axis=1)
    hidden_rows = (gelu * gate).astype(bf16)
    grad_pre = (slope * back * gate).astype(bf16)
    return hidden_rows, grad_pre, probs, grad_gate


BLOCK = 2 * PITCH


def forward_kernel(
    gain1_ref,
    shift1_ref,
    gain2_ref,
    shift2_ref,
    up_ref,
    down_ref,
    router_raw,
    cot_hbm,
    kept_hbm,
    tok_hbm,
    qkv_hbm,
    out_w_hbm,
    q_ref,
    k_ref,
    v_ref,
    att_ref,
    lse_ref,
    resid_ref,
    h_out,
    cot_out,
    kept_out,
    up_out,
    down_out,
    mixed_out,
    grad_h_out,
    gate_out,
    grad_up_out,
    grad_down_out,
    tok_out,
    router_out,
    router_ref,
    cot_turned,
    kept_ref,
    tok_raw,
    qkv_ref,
    out_w_ref,
    tok_ref,
    cot_ref,
    up_vm,
    down_vm,
    up_sum,
    down_sum,
    mixed_slots,
    grad_h_slots,
    gate_slots,
    grad_up_vm,
    grad_down_vm,
    q_all,
    k_all,
    v_all,
    att_all,
    lse_all,
    resid_all,
    h_all,
    cot_all,
    kept_all,
    part,
    mine,
    core_from,
    core_to,
    x_to,
    x_from,
    total_to,
    total_from,
    cot_core,
    core_s,
    core_r,
    x_s,
    x_r,
    tot_s,
    tot_r,
    y_s,
    y_r,
    rel_s,
    rel_r,
    w_s,
    w_r,
    c_s,
    c_r,
    load_sem,
    own_sem,
    pair_sem,
    block_sem,
    grad_sem,
    cot_sem,
    out_sem,
    *,
    images,
    heads,
    experts,
):
    expert_at = lax.axis_index("expert")
    tensor_at = lax.axis_index("tensor")
    z_at, y_at = expert_at // 2, expert_at % 2
    z_last = lax.axis_size("expert") // 2 - 1
    x_at, core_at = tensor_at // 2, tensor_at % 2
    other = 1 - core_at
    rows = images * PITCH
    half = rows // 2
    wide = out_w_ref.shape[1] // 2
    loads = [
        pltpu.make_async_copy(source, target, load_sem.at[number])
        for number, (source, target) in enumerate(
            (
                (cot_hbm, cot_turned),
                (kept_hbm, kept_ref),
                (tok_hbm, tok_raw),
                (qkv_hbm, qkv_ref),
                (out_w_hbm, out_w_ref),
            )
        )
    ]
    for copy in loads:
        copy.start()
    hidden = up_ref.shape[1]
    core_dev = (expert_at, tensor_at + 1 - 2 * core_at)
    x_dev = (expert_at, tensor_at + 2 - 4 * x_at)
    y_dev = (expert_at + 1 - 2 * y_at, tensor_at)
    z_up = (expert_at + 2, tensor_at)
    z_down = (expert_at - 2, tensor_at)
    has_up, has_down = z_at < z_last, z_at > 0
    greet([(True, core_dev), (True, x_dev), (True, y_dev), (has_up, z_up), (has_down, z_down)])

    def remote(src, dst, send, recv, device):
        return pltpu.make_async_remote_copy(
            src_ref=src, dst_ref=dst, send_sem=send, recv_sem=recv, device_id=device, device_id_type=MESH
        )

    def slot(expert, plane):
        pair = (expert // 2 + plane // 2) % 2
        return (
            up_out.at[pair, :, lanes_at(expert % 2 * hidden, hidden)],
            down_out.at[pair, aligned(expert % 2 * hidden, hidden), :],
        )

    def hop(step, way):
        expert = z_at - step if way == 0 else z_at + step
        plane = z_at + 1 if way == 0 else z_at - 1
        source = (up_ref, down_ref) if step == 0 else slot(expert, z_at)
        target = slot(expert, plane)
        device = z_up if way == 0 else z_down
        return [remote(source[n], target[n], w_s.at[way, step, n], w_r.at[way, step, n], device) for n in range(2)]

    def hop_goes(step, way):
        if way == 0:
            return (z_at - step >= 0) & has_up
        return (z_at + step <= z_last) & has_down

    def hop_comes(step, way):
        return (z_at - 1 - step >= 0) if way == 0 else (z_at + 1 + step <= z_last)

    def hop_arriving(step, way):
        expert = z_at - 1 - step if way == 0 else z_at + 1 + step
        target = slot(expert, z_at)
        return [remote(target[n], target[n], w_s.at[way, step, n], w_r.at[way, step, n], core_dev) for n in range(2)]

    def start_hops(step, which):
        for way in range(2):

            @pl.when(hop_goes(step, way))
            def _():
                hop(step, way)[which].start()

    def await_hops(step, which):
        for way in range(2):

            @pl.when(hop_comes(step, way))
            def _():
                hop_arriving(step, way)[which].wait_recv()

    def pass_hops(step, which):
        await_hops(step, which)
        start_hops(step + 1, which)

    start_hops(0, 0)
    start_hops(0, 1)

    def pair_place(expert):
        return up_vm.at[:, lanes_at(expert % 2 * hidden, hidden)], down_vm.at[aligned(expert % 2 * hidden, hidden), :]

    near = z_at + 1 - 2 * (z_at % 2)
    own_copies = [
        pltpu.make_async_copy((up_ref, down_ref)[n], pair_place(z_at)[n], own_sem.at[n]) for n in range(2)
    ]
    near_copies = [
        pltpu.make_async_copy(slot(near, z_at)[n], pair_place(near)[n], pair_sem.at[n]) for n in range(2)
    ]
    for copy in own_copies:
        copy.start()

    loads[0].wait()
    for number in range(images):
        first = number * SEQ // 128 * 128
        skip = number * SEQ - first
        turned = cot_turned[:, first : first + 384].T.astype(f32)[skip : skip + SEQ]
        padded = jnp.concatenate([turned, jnp.zeros((PITCH - SEQ, turned.shape[1]), f32)], axis=0)
        cot_ref[number * PITCH : (number + 1) * PITCH, :] = padded.astype(bf16)
    swap = remote(cot_ref, cot_core, c_s.at[0], c_r.at[0], core_dev)
    swap.start()

    narrow = router_raw[...].astype(f32)
    router_ref[0:16, :] = jnp.concatenate([narrow, jnp.zeros((16 - experts, narrow.shape[1]), f32)], axis=0).astype(bf16)
    router_ref[16:128, :] = jnp.zeros((112, narrow.shape[1]), bf16)

    def kept_half(side, core):
        return kept_all.at[aligned(side * rows + core * half, half), :]

    kept_y = remote(kept_half(0, core_at), kept_half(1, core_at), c_s.at[7], c_r.at[7], y_dev)
    kept_share = remote(kept_half(1, core_at), kept_half(1, core_at), c_s.at[6], c_r.at[6], core_dev)
    kept_share_in = remote(kept_half(1, other), kept_half(1, other), c_s.at[6], c_r.at[6], core_dev)
    loads[1].wait()
    kept_all[pl.ds(0, rows), :] = kept_ref[...]
    kept_y.start()
    swap.wait_recv()

    @pl.when(core_at == 0)
    def _():
        both = jnp.concatenate([cot_ref[...], cot_core[...]], axis=1)
        cot_all[pl.ds(0, rows), lanes_at(x_at * wide, wide)] = both

    @pl.when(core_at == 1)
    def _():
        both = jnp.concatenate([cot_core[...], cot_ref[...]], axis=1)
        cot_all[pl.ds(0, rows), lanes_at(x_at * wide, wide)] = both

    def block(side, col_side, core):
        return cot_all.at[aligned(side * rows + core * half, half), lanes_at(col_side * wide, wide)]

    def cot_copy(number, source, target, device):
        return remote(source, target, c_s.at[number], c_r.at[number], device)

    mine_block = block(0, x_at, core_at)
    cot_x = cot_copy(1, mine_block, mine_block, x_dev)
    cot_y = cot_copy(2, mine_block, block(1, x_at, core_at), y_dev)
    cot_x.start()
    cot_y.start()
    across_x, across_y, across_both = block(0, 1 - x_at, core_at), block(1, x_at, core_at), block(1, 1 - x_at, core_at)
    cot_x_in = cot_copy(1, across_x, across_x, x_dev)
    cot_y_in = cot_copy(2, across_y, across_y, y_dev)
    relay_y = cot_copy(3, across_x, across_both, y_dev)
    relay_in = cot_copy(3, across_both, across_both, y_dev)
    cot_share = [
        cot_copy(4, across_x, across_x, core_dev),
        cot_copy(5, across_y, across_y, core_dev),
        cot_copy(8, across_both, across_both, core_dev),
    ]
    arriving = [block(0, 1 - x_at, other), block(1, x_at, other), block(1, 1 - x_at, other)]
    cot_share_in = [cot_copy(number, ref, ref, core_dev) for number, ref in zip((4, 5, 8), arriving)]

    lane = lax.broadcasted_iota(jnp.int32, (PITCH, 2 * HD), 1)
    key_mask = lax.broadcasted_iota(jnp.int32, (PITCH, PITCH), 1) < SEQ
    gain1, shift1, gain2, shift2 = (ref[...].reshape(1, 2 * wide) for ref in (gain1_ref, shift1_ref, gain2_ref, shift2_ref))
    my_cols = lanes_at(core_at * wide, wide)
    their_cols = lanes_at(other * wide, wide)

    def attend(image):
        normed, _ = norm_stats(tok_ref[image].astype(f32))
        h_one = (normed * gain1 + shift1).astype(bf16)
        queries = dot(h_one, qkv_ref[0], ((1,), (1,))).astype(bf16)
        keys = dot(h_one, qkv_ref[1], ((1,), (1,))).astype(bf16)
        values = dot(h_one, qkv_ref[2], ((1,), (1,))).astype(bf16)
        q_all[image] = queries
        k_all[image] = keys
        v_all[image] = values
        outs = []
        lse = jnp.zeros((PITCH, 2 * HD), f32)
        for head in range(heads):
            first = head // 2 * 2 * HD
            last = min(first + 2 * HD, heads * HD)
            q_head, k_head, v_head = queries[:, first:last], keys[:, first:last], values[:, first:last]
            if last - first == 2 * HD:
                q_head = jnp.where(head_mask(lane, head), q_head, jnp.zeros_like(q_head))
            scores = dot(q_head, k_head, ((1,), (1,))) * (HD**-0.5)
            scores = jnp.where(key_mask, scores, -1e30)
            peak = jnp.max(scores, axis=1, keepdims=True)
            powers = jnp.exp(scores - peak)
            row_sum = jnp.sum(powers, axis=1, keepdims=True)
            weights = (powers / row_sum).astype(bf16)
            outs.append(dot(weights, v_head))
            lse = jnp.where(lane == head, peak + jnp.log(row_sum), lse)
        lse_all[image] = lse
        joined = []
        for head in range(0, heads, 2):
            if head + 1 < heads:
                joined.append(jnp.where(lane < HD, outs[head], outs[head + 1]))
            else:
                joined.append(outs[head])
        attended = jnp.concatenate(joined, axis=1).astype(bf16)
        att_all[image] = attended
        part[...] = dot(attended, out_w_ref[...])
        mine[image] = part[:, my_cols]
        core_to[image] = part[:, their_cols].astype(bf16)

    def core_copy(image):
        return remote(core_to.at[image], core_from.at[image], core_s.at[image], core_r.at[image], core_dev)

    def x_copy(image):
        return remote(x_to.at[image], x_from.at[image], x_s.at[image], x_r.at[image], x_dev)

    def total_copy(image):
        return remote(total_to.at[image], total_from.at[image], tot_s.at[image], tot_r.at[image], core_dev)

    def h_block(side, image, core):
        return h_all.at[aligned(side * rows + image * PITCH, PITCH), lanes_at(core * wide, wide)]

    def y_copy(image):
        return remote(h_block(0, image, core_at), h_block(1, image, core_at), y_s.at[image], y_r.at[image], y_dev)

    def relay_copy(image):
        ref = h_block(1, image, core_at)
        return remote(ref, ref, rel_s.at[image], rel_r.at[image], core_dev)

    def relay_arriving(image):
        ref = h_block(1, image, other)
        return remote(ref, ref, rel_s.at[image], rel_r.at[image], core_dev)

    attend_outs = ((tok_ref, tok_out), (q_all, q_ref), (k_all, k_ref), (v_all, v_ref), (att_all, att_ref), (lse_all, lse_ref))

    def out_copies(image):
        copies = [
            pltpu.make_async_copy(kept.at[image], out.at[image], out_sem.at[n, image])
            for n, (kept, out) in enumerate(attend_outs)
        ]
        at = aligned(image * PITCH, PITCH)
        return copies, [
            pltpu.make_async_copy(resid_all.at[image], resid_ref.at[at, :], out_sem.at[6, image]),
            pltpu.make_async_copy(h_all.at[at, :], h_out.at[at, :], out_sem.at[7, image]),
        ]

    def other_copy(image):
        at = aligned(rows + image * PITCH, PITCH)
        return pltpu.make_async_copy(h_all.at[at, :], h_out.at[at, :], out_sem.at[8, image])

    def stage(tick, lag, run):
        image = tick - lag

        @pl.when((image >= 0) & (image < images))
        def _():
            run(image)

    def run_attend(image):
        attend(image)
        core_copy(image).start()
        for copy in out_copies(image)[0]:
            copy.start()

    def run_x(image):
        core_copy(image).wait_recv()
        x_to[image] = (mine[image] + core_from[image].astype(f32)).astype(bf16)
        x_copy(image).start()

    def run_total(image):
        x_copy(image).wait_recv()
        total_to[image] = (x_to[image].astype(f32) + x_from[image].astype(f32)).astype(bf16)
        total_copy(image).start()

    def run_norm(image):
        total_copy(image).wait_recv()
        part[:, my_cols] = total_to[image].astype(f32)
        part[:, their_cols] = total_from[image].astype(f32)
        resid = tok_ref[image].astype(f32) + part[...]
        resid_all[image] = resid
        normed, _ = norm_stats(resid)
        h_all[aligned(image * PITCH, PITCH), :] = (normed * gain2 + shift2).astype(bf16)
        y_copy(image).start()
        for copy in out_copies(image)[1]:
            copy.start()

    def run_relay(image):
        y_copy(image).wait_recv()
        relay_copy(image).start()

    def run_end(image):
        relay_arriving(image).wait_recv()
        other_copy(image).start()

    def cot_step_one():
        cot_x_in.wait_recv()
        cot_share[0].start()

        relay_y.start()

    def cot_step_two():
        cot_y_in.wait_recv()
        cot_share[1].start()

    def weights_step_one():
        pass_hops(0, 1)
        for copy in near_copies:
            copy.start()

    def cot_step_three():
        kept_y.wait_recv()
        kept_share.start()
        relay_in.wait_recv()
        cot_share[2].start()

    outs = [
        pltpu.make_async_copy(cot_all, cot_out, cot_sem.at[0]),
        pltpu.make_async_copy(kept_all, kept_out, cot_sem.at[1]),
        pltpu.make_async_copy(router_ref, router_out, cot_sem.at[2]),
    ]

    def ready_own():
        cot_share_in[0].wait_recv()
        for copy in (*own_copies, *near_copies):
            copy.wait()

    def ready_other():
        for copy in (cot_share_in[1], cot_share_in[2], kept_share_in):
            copy.wait_recv()
        for copy in outs:
            copy.start()

    def block_copies(number, place):
        at = aligned(number * BLOCK, BLOCK)
        pairs = ((mixed_slots, mixed_out), (grad_h_slots, grad_h_out), (gate_slots, gate_out))
        return [
            pltpu.make_async_copy(slots.at[place], out.at[at, :], block_sem.at[n, place])
            for n, (slots, out) in enumerate(pairs)
        ]

    def run_block(number, turn):
        at = aligned(number * BLOCK, BLOCK)
        h_rows, cot_rows = h_all[at, :], cot_all[at, :]
        up, down = up_vm[...], down_vm[...]
        hidden_rows, grad_pre, _, grad_gate = expert_math(
            h_rows, cot_rows, kept_all[at, :].astype(f32), router_ref[...], up, down, z_at // 2, experts
        )

        place = turn % 2

        @pl.when(turn >= 2)
        def _():
            for copy in block_copies(number, place):
                copy.wait()

        gate_slots[place] = grad_gate
        mixed_slots[place] = dot(hidden_rows, down).astype(bf16)
        grad_h_slots[place] = dot(grad_pre, up, ((1,), (1,))).astype(bf16)
        for copy in block_copies(number, place):
            copy.start()
        up_sum[...] += dot(h_rows.T, grad_pre)
        down_sum[...] += dot(cot_rows.T, hidden_rows)

    up_sum[...] = jnp.zeros_like(up_sum)
    down_sum[...] = jnp.zeros_like(down_sum)

    def take_tokens(number):
        first = number * SEQ // 16 * 16
        skip = number * SEQ - first
        taken = min(224, images * SEQ - first)
        rows_in = tok_raw[first : first + taken, :].astype(f32)[skip : skip + SEQ]
        padded = jnp.concatenate([rows_in, jnp.zeros((PITCH - SEQ, rows_in.shape[1]), f32)], axis=0)
        tok_ref[number] = padded.astype(bf16)

    def first_ticks(tick, _):
        for number in range(images):
            pl.when(tick == number)(partial(take_tokens, number))

        stage(tick, 0, run_attend)
        stage(tick, 1, run_x)
        return 0

    for copy in loads[2:]:
        copy.wait()
    lax.fori_loop(0, images + 1, first_ticks, 0)
    pairs = images // 2

    def both(first, *runs):
        for run in runs:
            run(first)
            run(first + 1)

    pass_hops(0, 0)
    cot_step_one()
    both(0, run_total, run_norm)
    cot_step_two()
    weights_step_one()
    ready_own()

    def per_turn(turn, _):
        @pl.when((turn <= 1) | (turn == 3))
        def _():
            both(jnp.where(turn == 3, 6, 2 * turn + 2), run_total, run_norm)

        @pl.when((turn >= 2) & (turn < pairs + 2))
        def _():
            both(2 * turn - 4, run_relay)

        @pl.when(turn == 2)
        def _():
            pass_hops(1, 0)
            cot_step_three()

        @pl.when(turn == pairs)
        def _():
            pass_hops(1, 1)
            ready_other()

        @pl.when(turn >= pairs)
        def _():
            both(2 * (turn - pairs), run_end)

        run_block(turn, turn)
        return 0

    lax.fori_loop(0, 2 * pairs, per_turn, 0)
    grad_up_vm[...] = up_sum[...].astype(bf16)
    grad_down_vm[...] = down_sum[...].astype(bf16)
    grad_copies = [
        pltpu.make_async_copy(grad_up_vm, grad_up_out, grad_sem.at[0]),
        pltpu.make_async_copy(grad_down_vm, grad_down_out, grad_sem.at[1]),
    ]
    for copy in grad_copies:
        copy.start()
    for copy in (swap, kept_y, kept_share, cot_x, cot_y, *cot_share):
        copy.wait_send()

    relay_y.wait_send()

    def drain(image, _):
        for copy in (core_copy, x_copy, total_copy, y_copy, relay_copy):
            copy(image).wait_send()
        first, second = out_copies(image)
        for copy in (*first, *second, other_copy(image)):
            copy.wait()
        return 0

    lax.fori_loop(0, images, drain, 0)
    for place in range(2):
        for copy in block_copies(0, place):
            copy.wait()

    await_hops(2, 0)
    await_hops(2, 1)
    for step in range(3):
        for way in range(2):

            @pl.when(hop_goes(step, way))
            def _():
                for copy in hop(step, way):
                    copy.wait_send()

    for copy in (*grad_copies, *outs):
        copy.wait()


def run_forward(tok_raw, gain1, shift1, gain2, shift2, qkv_w, out_w, up, down, router, cot, kept, experts):
    images = tok_raw.shape[0] // SEQ
    rows = images * PITCH
    features = tok_raw.shape[1]
    share = out_w.shape[0]
    heads = share // HD
    hidden = up.shape[1]
    wide = features // 2
    vmem = pl.BlockSpec(memory_space=pltpu.VMEM)
    anywhere = pl.BlockSpec(memory_space=pl.ANY)
    shape = jax.ShapeDtypeStruct
    block = (images, PITCH, wide)
    dma = pltpu.SemaphoreType.DMA
    return pl.pallas_call(
        partial(forward_kernel, images=images, heads=heads, experts=experts),
        out_shape=[
            shape((images, PITCH, share), bf16),
            shape((images, PITCH, share), bf16),
            shape((images, PITCH, share), bf16),
            shape((images, PITCH, share), bf16),
            shape((images, PITCH, 128), f32),
            shape((rows, features), f32),
            shape((2 * rows, features), bf16),
            shape((2 * rows, features), bf16),
            shape((2 * rows, 128), bf16),
            shape((2, features, 2 * hidden), bf16),
            shape((2, 2 * hidden, features), bf16),
            shape((2 * rows, features), bf16),
            shape((2 * rows, features), bf16),
            shape((2 * rows, 128), f32),
            shape((features, 2 * hidden), bf16),
            shape((features, 2 * hidden), bf16),
            shape((images, PITCH, features), bf16),
            shape((128, features), bf16),
        ],
        in_specs=[vmem] * 4 + [anywhere] * 2 + [vmem] + [anywhere] * 5,
        out_specs=[anywhere] * 18,
        scratch_shapes=[
            pltpu.VMEM((128, features), bf16),
            pltpu.VMEM(cot.shape, bf16),
            pltpu.VMEM(kept.shape, bf16),
            pltpu.VMEM(tok_raw.shape, bf16),
            pltpu.VMEM(qkv_w.shape, bf16),
            pltpu.VMEM(out_w.shape, bf16),
            pltpu.VMEM((images, PITCH, features), bf16),
            pltpu.VMEM((rows, share), bf16),
            pltpu.VMEM((features, 2 * hidden), bf16),
            pltpu.VMEM((2 * hidden, features), bf16),
            *[pltpu.VMEM((features, 2 * hidden), f32)] * 2,
            *[pltpu.VMEM((2, BLOCK, features), bf16)] * 2,
            pltpu.VMEM((2, BLOCK, 128), f32),
            *[pltpu.VMEM((features, 2 * hidden), bf16)] * 2,
            *[pltpu.VMEM((images, PITCH, share), bf16)] * 4,
            pltpu.VMEM((images, PITCH, 128), f32),
            pltpu.VMEM((images, PITCH, features), f32),
            pltpu.VMEM((2 * rows, features), bf16),
            pltpu.VMEM((2 * rows, features), bf16),
            pltpu.VMEM((2 * rows, 128), bf16),
            pltpu.VMEM((PITCH, features), f32),
            pltpu.VMEM(block, f32),
            pltpu.VMEM(block, bf16),
            pltpu.VMEM(block, bf16),
            pltpu.VMEM(block, bf16),
            pltpu.VMEM(block, bf16),
            pltpu.VMEM(block, bf16),
            pltpu.VMEM(block, bf16),
            pltpu.VMEM((rows, share), bf16),
        ]
        + [dma((images,))] * 10
        + [dma((2, 3, 2))] * 2
        + [dma((9,))] * 2
        + [dma((5,)), dma((2,)), dma((2,)), dma((3, 2)), dma((2,)), dma((3,)), dma((9, images))],
        compiler_params=pltpu.CompilerParams(
            collective_id=1, has_side_effects=True, vmem_limit_bytes=63 << 20
        ),
    )(gain1, shift1, gain2, shift2, up, down, router, cot, kept, tok_raw, qkv_w, out_w)


def turn_is_other(turn):
    return (turn == 0) | ((turn % 2 == 1) & (turn < 7))


def turn_block(turn):
    own = jnp.where(turn == 7, 3, turn // 2 - 1)
    return jnp.where(turn_is_other(turn), 4 + (turn + 1) // 2, own)


def second_pair_kernel(
    h_ref,
    cot_ref,
    kept_ref,
    router_ref,
    mixed_first,
    grad_h_first,
    gate_first,
    up_all,
    down_all,
    up_first,
    down_first,
    mixed_ref,
    grad_router_ref,
    grad_up_out,
    grad_down_out,
    grad_h_out,
    up_pair,
    down_pair,
    line_first,
    up_vm,
    down_vm,
    grad_up_ref,
    grad_down_ref,
    up_sum,
    down_sum,
    router_sum,
    ring,
    from_core,
    from_y,
    from_x,
    load,
    core_s,
    core_r,
    y_s,
    y_r,
    x_s,
    x_r,
    tot_s,
    tot_r,
    store,
    pair_s,
    pair_r,
    line_s,
    line_r,
    *,
    experts,
    steps,
):
    turn = pl.program_id(0)
    expert_at = lax.axis_index("expert")
    tensor_at = lax.axis_index("tensor")
    z_at, y_at = expert_at // 2, expert_at % 2
    x_at, core_at = tensor_at // 2, tensor_at % 2
    hidden = up_pair.shape[1]
    wide = ring.shape[3]
    core_dev = (expert_at, tensor_at + 1 - 2 * core_at)
    x_dev = (expert_at, tensor_at + 2 - 4 * x_at)
    y_dev = (expert_at + 1 - 2 * y_at, tensor_at)
    my_cols = lanes_at(core_at * wide, wide)

    def remote(src, dst, send, recv, device):
        return pltpu.make_async_remote_copy(
            src_ref=src, dst_ref=dst, send_sem=send, recv_sem=recv, device_id=device, device_id_type=MESH
        )

    def core_copy(number):
        return remote(ring.at[number % 2, 1 - core_at], from_core.at[number], core_s.at[number], core_r.at[number], core_dev)

    def y_copy(number, place):
        return remote(from_core.at[number], from_y.at[place], y_s.at[place], y_r.at[place], y_dev)

    def x_copy(number, place):
        return remote(from_core.at[number], from_x.at[place], x_s.at[place], x_r.at[place], x_dev)

    def out_rows(place):
        return grad_h_out.at[aligned(place * BLOCK, BLOCK), my_cols]

    def total_copy(place):
        return remote(from_x.at[place], out_rows(place), tot_s.at[place], tot_r.at[place], core_dev)

    def store_copy(place):
        return pltpu.make_async_copy(from_x.at[place], out_rows(place), store.at[place])

    def own_turn(place):
        return jnp.where(place == 3, 7, 2 * place + 2)

    def other_turn(place):
        return jnp.where(place == 0, 0, 2 * place - 1)

    def pass_other(number):
        core_copy(number).wait_recv()
        from_core[number] = from_core[number] + ring[number % 2, core_at]
        y_copy(number, (number + 1) // 2).start()

    def pass_own(number, place):
        core_copy(number).wait_recv()
        y_copy(number, place).wait_recv()
        total = from_core[number].astype(f32) + ring[number % 2, core_at].astype(f32) + from_y[place].astype(f32)
        from_core[number] = total.astype(bf16)
        x_copy(number, place).start()

    def pass_total(place):
        number = own_turn(place)
        x_copy(number, place).wait_recv()
        from_x[place] = from_core[number] + from_x[place]
        total_copy(place).start()
        store_copy(place).start()

    z_dev = (jnp.where(z_at % 2 == 0, expert_at + 2, expert_at - 2), tensor_at)
    pair_lanes = lanes_at((1 - z_at % 2) * hidden, hidden)
    pair_copies = [
        remote(source.at[:, pair_lanes], target, pair_s.at[number], pair_r.at[number], z_dev)
        for number, (source, target) in enumerate(((up_first, up_pair), (down_first, down_pair)))
    ]

    far_lanes = lanes_at(jnp.where(z_at == 0, 1, 0) * hidden, hidden)
    line_copy = remote(grad_up_ref.at[:, far_lanes], line_first, line_s.at[0], line_r.at[0], z_dev)
    is_outer = (z_at == 0) | (z_at == lax.axis_size("expert") // 2 - 1)

    grad_copies = [
        pltpu.make_async_copy(grad_up_ref, grad_up_out, load.at[2]),
        pltpu.make_async_copy(grad_down_ref, grad_down_out, load.at[3]),
    ]

    @pl.when(turn == 0)
    def _():
        whole = [
            pltpu.make_async_copy(up_all.at[1], up_vm, load.at[0]),
            pltpu.make_async_copy(down_all.at[1], down_vm, load.at[1]),
        ]
        for copy in whole:
            copy.start()
        greet([(True, core_dev), (True, x_dev), (True, y_dev), (True, z_dev)])
        for copy in pair_copies:
            copy.start()
        up_sum[...] = jnp.zeros_like(up_sum)
        down_sum[...] = jnp.zeros_like(down_sum)
        router_sum[...] = jnp.zeros_like(router_sum)
        for copy in whole:
            copy.wait()

    h_rows, cot_rows = h_ref[...], cot_ref[...]
    up, down, router = up_vm[...], down_vm[...], router_ref[...]
    kept = kept_ref[...].astype(f32)
    hidden_rows, grad_pre, probs, grad_gate = expert_math(
        h_rows, cot_rows, kept, router, up, down, 1 - z_at // 2, experts
    )
    grad_gate = kept * (grad_gate + gate_first[...])
    grad_logits = (probs * (grad_gate - jnp.sum(probs * grad_gate, axis=1, keepdims=True))).astype(bf16)

    before = turn - 1

    @pl.when((turn >= 1) & turn_is_other(before))
    def _():
        pass_other(before)

    @pl.when((turn == 5) | (turn == 7))
    def _():
        pass_total((turn - 5) // 2)

    @pl.when((turn == 3) | (turn == 5) | (turn == 7))
    def _():
        pass_own(before, (turn - 3) // 2)


    @pl.when(turn >= 2)
    def _():
        core_copy(turn - 2).wait_send()

    grad_h = (
        grad_h_first[...].astype(f32) + dot(grad_pre, up, ((1,), (1,))) + dot(grad_logits, router)
    ).astype(bf16)
    ring[turn % 2, 0] = grad_h[:, :wide]
    ring[turn % 2, 1] = grad_h[:, wide:]
    core_copy(turn).start()
    mixed_ref[...] = (mixed_first[...].astype(f32) + dot(hidden_rows, down)).astype(bf16)
    h_turned = h_rows.T
    up_sum[...] += dot(h_turned, grad_pre)
    router_sum[...] += dot(h_turned, grad_logits)
    down_sum[...] += dot(cot_rows.T, hidden_rows)

    @pl.when(turn == steps - 1)
    def _():
        grad_up_ref[...] = up_sum[...].astype(bf16)
        grad_copies[0].start()

        @pl.when(is_outer)
        def _():
            line_copy.start()

        pass_own(7, 3)
        pass_total(2)
        grad_down_ref[...] = down_sum[...].astype(bf16)
        grad_copies[1].start()
        grad_router_ref[...] = router_sum[...].T[:8]
        pass_total(3)
        for copy in (*pair_copies, *grad_copies):
            copy.wait()

        @pl.when(is_outer)
        def _():
            line_copy.wait_send()

        @pl.when(jnp.logical_not(is_outer))
        def _():
            line_copy.wait_recv()

        for number in (6, 7):
            core_copy(number).wait_send()
        for place in range(4):
            y_copy(other_turn(place), place).wait_send()
            x_copy(own_turn(place), place).wait_send()
            total_copy(place).wait_send()
            total_copy(place).wait_recv()
            store_copy(place).wait()


def run_second_pair(
    h_rows,
    cot_rows,
    kept,
    router,
    mixed_first,
    grad_h_first,
    gate_first,
    up,
    down,
    up_first,
    down_first,
    experts,
):
    rows, features = h_rows.shape
    width = up.shape[2]
    steps = rows // BLOCK
    half = (BLOCK, features // 2)
    anywhere = pl.BlockSpec(memory_space=pl.ANY)
    shape = jax.ShapeDtypeStruct
    dma = pltpu.SemaphoreType.DMA

    def by_step(lanes):
        return pl.BlockSpec((BLOCK, lanes), lambda n: (turn_block(n), 0))

    def whole(*dims):
        return pl.BlockSpec(dims, lambda n: (0,) * len(dims))

    return pl.pallas_call(
        partial(second_pair_kernel, experts=experts, steps=steps),
        grid=(steps,),
        out_shape=[
            shape((rows, features), bf16),
            shape((8, features), f32),
            shape((features, width), bf16),
            shape((features, width), bf16),
            shape((rows // 2, features), bf16),
            shape((features, width // 2), bf16),
            shape((features, width // 2), bf16),
            shape((features, width // 2), bf16),
        ],
        in_specs=[
            by_step(features),
            by_step(features),
            by_step(128),
            whole(128, features),
            by_step(features),
            by_step(features),
            by_step(128),
        ]
        + [anywhere] * 4,
        out_specs=[by_step(features), whole(8, features)] + [anywhere] * 6,
        scratch_shapes=[
            pltpu.VMEM((features, width), bf16),
            pltpu.VMEM((width, features), bf16),
            *[pltpu.VMEM((features, width), bf16)] * 2,
            pltpu.VMEM((features, width), f32),
            pltpu.VMEM((features, width), f32),
            pltpu.VMEM((features, 128), f32),
            pltpu.VMEM((2, 2, *half), bf16),
            pltpu.VMEM((8, *half), bf16),
            pltpu.VMEM((4, *half), bf16),
            pltpu.VMEM((4, *half), bf16),
            dma((4,)),
        ]
        + [dma((8,))] * 2
        + [dma((4,))] * 7
        + [dma((2,))] * 2
        + [dma((1,))] * 2,
        compiler_params=pltpu.CompilerParams(
            collective_id=4, has_side_effects=True, vmem_limit_bytes=60 << 20
        ),
    )(h_rows, cot_rows, kept, router, mixed_first, grad_h_first, gate_first, up, down, up_first, down_first)


def backward_kernel(
    gain1_ref,
    shift1_ref,
    gain2_ref,
    grad_router_ref,
    qkv_hbm,
    out_w_hbm,
    tok_hbm,
    q_hbm,
    k_hbm,
    v_hbm,
    att_hbm,
    lse_hbm,
    grad_h_hbm,
    resid_ref,
    cot_ref,
    mixed_ref,
    up_second,
    down_second,
    line_first,
    line_out,
    tokens_out,
    weights_out,
    sums_out,
    mixed_out,
    qkv_ref,
    out_w_ref,
    tok_ref,
    q_ref,
    k_ref,
    v_ref,
    att_ref,
    lse_ref,
    grad_h_ref,
    rows_kept,
    cot_rows,
    m_mine,
    m_core,
    m_y,
    m_x,
    m_out,
    m_resid,
    far_vm,
    one_mine,
    one_to,
    one_core,
    one_x,
    one_total,
    line,
    weight_sum,
    weight_half,
    shared,
    shared_y,
    shared_line,
    shared_all,
    route_core,
    route_x,
    late_mine,
    late_y,
    late_z,
    sums_all,
    tokens_low,
    whole,
    mc_s,
    mc_r,
    my_s,
    my_r,
    mx_s,
    mx_r,
    mq_s,
    mq_r,
    m_store,
    oc_s,
    oc_r,
    ox_s,
    ox_r,
    ot_s,
    ot_r,
    l_s,
    l_r,
    sy_s,
    sy_r,
    sl_s,
    sl_r,
    sg_s,
    sg_r,
    sz_s,
    sz_r,
    r_s,
    r_r,
    late_s,
    late_r,
    load,
    image_load,
    own_sem,
    weight_store,
    store,
    *,
    images,
    heads,
):
    expert_at = lax.axis_index("expert")
    tensor_at = lax.axis_index("tensor")
    z_at, y_at = expert_at // 2, expert_at % 2
    z_last = lax.axis_size("expert") // 2 - 1
    x_at, core_at = tensor_at // 2, tensor_at % 2
    other = 1 - core_at
    rows = images * PITCH
    features = tok_hbm.shape[2]
    wide = features // 2
    share = out_w_ref.shape[0]
    hidden = line.shape[3]
    core_dev = (expert_at, tensor_at + 1 - 2 * core_at)
    x_dev = (expert_at, tensor_at + 2 - 4 * x_at)
    y_dev = (expert_at + 1 - 2 * y_at, tensor_at)
    z_devs = [(expert_at + 2, tensor_at), (expert_at - 2, tensor_at)]
    planes = z_last + 1
    z_others = [((z_at + hop) % planes * 2 + y_at, tensor_at) for hop in (1, 2, 3)]
    greet([(True, device) for device in (core_dev, x_dev, y_dev, *z_others)])
    my_cols = lanes_at(core_at * wide, wide)
    their_cols = lanes_at(other * wide, wide)

    def remote(src, dst, send, recv, device):
        return pltpu.make_async_remote_copy(
            src_ref=src, dst_ref=dst, send_sem=send, recv_sem=recv, device_id=device, device_id_type=MESH
        )

    def at_image(image):
        return aligned(image * PITCH, PITCH)

    def place(way):
        return z_at if way == 0 else z_last - z_at

    def far_lanes(way, piece):
        expert = z_last - piece // 2 if way == 0 else piece // 2
        return pl.ds(expert % 2 * hidden, hidden)

    def line_copy(source, way, piece):
        return remote(source, line.at[way, piece], l_s.at[way, piece], l_r.at[way, piece], z_devs[way])

    def line_copy_on(way, piece):
        return line_copy(line.at[way, piece], way, piece)

    def line_start():
        for way in range(2):

            @pl.when(place(way) == 0)
            def _():
                for piece in range(1, 4):
                    source = (up_second, down_second)[piece % 2]
                    line_copy(source.at[:, far_lanes(way, piece)], way, piece).start()

    def line_add(piece):
        for way in range(2):

            @pl.when(place(way) == 1)
            def _():
                if piece > 0:
                    line_copy_on(way, piece).wait_recv()
                lanes = far_lanes(way, piece)

                def add(part, _):
                    at_rows = aligned(part * 96, 96)
                    total = line[way, piece, at_rows, :].astype(f32) + far_vm[piece % 2, at_rows, lanes].astype(f32)
                    line[way, piece, at_rows, :] = total.astype(bf16)
                    return 0

                lax.fori_loop(0, features // 96, add, 0)
                line_copy_on(way, piece).start()

    part_height = line.shape[2] // 4

    def line_part_copy(way, part):
        ref = line.at[way, 3, pl.ds(part * part_height, part_height)]
        return remote(ref, ref, l_s.at[way, 3 + part], l_r.at[way, 3 + part], z_devs[way])

    def line_part(part):
        for way in range(2):

            @pl.when(place(way) == 1)
            def _():
                if part == 0:
                    line_copy_on(way, 3).wait_recv()
                lanes = far_lanes(way, 3)
                for piece in range(2):
                    at_rows = pl.ds(part * part_height + piece * part_height // 2, part_height // 2)
                    total = line[way, 3, at_rows, :].astype(f32) + far_vm[1, at_rows, lanes].astype(f32)
                    line[way, 3, at_rows, :] = total.astype(bf16)
                line_part_copy(way, part).start()

    def line_pass(piece):
        for way in range(2):

            @pl.when(place(way) == 2)
            def _():
                line_copy_on(way, piece).wait_recv()
                line_copy_on(way, piece).start()

    line_start()
    later = [
        pltpu.make_async_copy((up_second, down_second)[number], far_vm.at[number], own_sem.at[number])
        for number in range(2)
    ]
    is_inner = (z_at == 1) | (z_at == z_last - 1)
    first_copy = pltpu.make_async_copy(line_first, line.at[jnp.where(z_at == 1, 0, 1), 0], own_sem.at[2])

    @pl.when(is_inner)
    def _():
        first_copy.start()

    for copy in later:
        copy.start()

    part_count = m_y.shape[0]
    part_rows_m = rows // part_count

    def m_rows(side, part):
        return aligned(side * rows + part * part_rows_m, part_rows_m)

    def m_core_copy(side, part):
        at = m_rows(side, part)
        return remote(mixed_ref.at[at, their_cols], m_core.at[at, :], mc_s.at[side, part], mc_r.at[side, part], core_dev)

    for part in range(part_count):
        m_core_copy(1, part).start()
    for part in range(part_count):
        m_core_copy(0, part).start()
    m_loads = [
        pltpu.make_async_copy(mixed_ref.at[pl.ds(side * rows, rows), my_cols], m_mine.at[pl.ds(side * rows, rows), :], load.at[side])
        for side in range(2)
    ]

    def image_loads(image):
        at = at_image(image)
        by_image = ((tok_hbm, tok_ref), (q_hbm, q_ref), (k_hbm, k_ref), (v_hbm, v_ref), (att_hbm, att_ref), (lse_hbm, lse_ref))
        by_row = ((grad_h_hbm, grad_h_ref), (resid_ref, rows_kept), (cot_ref, cot_rows))
        pairs = [(source.at[image], target.at[image]) for source, target in by_image]
        pairs += [(source.at[at, :], target.at[at, :]) for source, target in by_row]
        return [pltpu.make_async_copy(source, target, image_load.at[n, image]) for n, (source, target) in enumerate(pairs)]

    def start_loads(image, _):
        for copy in image_loads(image):
            copy.start()
        return 0

    weight_loads = [
        pltpu.make_async_copy(qkv_hbm, qkv_ref, own_sem.at[3]),
        pltpu.make_async_copy(out_w_hbm, out_w_ref, own_sem.at[4]),
    ]
    for copy in weight_loads:
        copy.start()
    start_loads(0, 0)
    m_loads[1].start()
    lax.fori_loop(1, images, start_loads, 0)
    m_loads[0].start()
    route_one = remote(grad_router_ref, route_core, r_s.at[0], r_r.at[0], core_dev)
    route_one.start()

    weight_sum[...] = jnp.zeros_like(weight_sum)
    late_mine[...] = jnp.zeros_like(late_mine)

    def m_y_copy(part):
        return remote(m_core.at[m_rows(1, part), :], m_y.at[part], my_s.at[part], my_r.at[part], y_dev)

    def m_x_copy(part):
        return remote(m_core.at[m_rows(0, part), :], m_x.at[part], mx_s.at[part], mx_r.at[part], x_dev)

    def m_place(part):
        return mixed_out.at[aligned(part * part_rows_m, part_rows_m), :]

    def m_quarter_copy(part):
        return remote(m_out.at[part, other], m_place(part), mq_s.at[part], mq_r.at[part], core_dev)

    def m_store_copy(part):
        return pltpu.make_async_copy(m_out.at[part, core_at], m_place(part), m_store.at[part])

    def m_resid_copy(part):
        at = aligned(part * part_rows_m, part_rows_m)
        return pltpu.make_async_copy(resid_ref.at[at, lanes_at(x_at * wide, wide)], m_resid, load.at[3])

    keeps = x_at == core_at

    def run_m_y(part):
        m_core_copy(1, part).wait_recv()
        at = m_rows(1, part)
        m_core[at, :] = (m_core[at, :].astype(f32) + m_mine[at, :].astype(f32)).astype(bf16)
        m_y_copy(part).start()

    def run_m_x(part):
        if isinstance(part, int) and part == 0:
            m_loads[0].wait()
        m_core_copy(0, part).wait_recv()
        m_y_copy(part).wait_recv()
        at = m_rows(0, part)
        total = m_core[at, :].astype(f32) + m_mine[at, :].astype(f32) + m_y[part].astype(f32)
        m_core[at, :] = total.astype(bf16)

        @pl.when(jnp.logical_not(keeps))
        def _():
            m_x_copy(part).start()

    def run_m_out(part):
        @pl.when(keeps)
        def _():
            m_resid_copy(part).start()
            m_x_copy(part).wait_recv()
            m_resid_copy(part).wait()
            total = m_core[m_rows(0, part), :].astype(f32) + m_x[part].astype(f32)
            mixed = (m_resid[...] + total).astype(bf16)
            m_out[part, 0] = mixed[:, : wide // 2]
            m_out[part, 1] = mixed[:, wide // 2 :]
            m_quarter_copy(part).start()
            m_store_copy(part).start()

    later[0].wait()
    later[1].wait()

    @pl.when(is_inner)
    def _():
        first_copy.wait()

    line_add(0)
    m_loads[1].wait()
    for part in range(part_count):
        run_m_y(part)
    route_one.wait_recv()
    route_core[...] += grad_router_ref[...]
    route_two = remote(route_core, route_x, r_s.at[1], r_r.at[1], x_dev)
    route_two.start()

    def one_core_copy(image):
        return remote(one_to.at[image], one_core.at[image], oc_s.at[image], oc_r.at[image], core_dev)

    def one_x_copy(image):
        return remote(one_core.at[image], one_x.at[image], ox_s.at[image], ox_r.at[image], x_dev)

    def one_total_copy(image):
        return remote(one_x.at[image], one_total.at[image], ot_s.at[image], ot_r.at[image], core_dev)

    store_copy = pltpu.make_async_copy(tokens_low, tokens_out, store.at[0])

    lane = lax.broadcasted_iota(jnp.int32, (PITCH, 2 * HD), 1)
    key_mask = lax.broadcasted_iota(jnp.int32, (PITCH, PITCH), 1) < SEQ
    gain1, shift1, gain2 = (ref[...].reshape(1, features) for ref in (gain1_ref, shift1_ref, gain2_ref))

    def norm_back(grad, gain, normed, inverse):
        scaled = grad * gain
        mean = jnp.mean(scaled, axis=1, keepdims=True)
        along = jnp.mean(scaled * normed, axis=1, keepdims=True)
        return (scaled - mean - normed * along) * inverse

    def add_sums(sums, row, grad, normed):
        sums[row : row + 1, :] += jnp.sum(grad * normed, axis=0, keepdims=True)
        sums[row + 1 : row + 2, :] += jnp.sum(grad, axis=0, keepdims=True)

    def run_attention(image):
        for copy in image_loads(image):
            copy.wait()
        at = at_image(image)
        grad_h = grad_h_ref[at, :].astype(f32)
        normed, inverse = norm_stats(rows_kept[at, :])
        add_sums(late_mine, 2, grad_h, normed)
        grad_resid = cot_rows[at, :].astype(f32) + norm_back(grad_h, gain2, normed, inverse)
        rows_kept[at, :] = grad_resid
        grad_branch = grad_resid.astype(bf16)
        token_normed, _ = norm_stats(tok_ref[image].astype(f32))
        h_one = (token_normed * gain1 + shift1).astype(bf16)
        queries, keys, values, attended = q_ref[image], k_ref[image], v_ref[image], att_ref[image]
        lse = lse_ref[image]
        grad_attended = dot(grad_branch, out_w_ref[...], ((1,), (1,))).astype(bf16)
        grads = [[], [], []]
        for head in range(heads):
            first = head // 2 * 2 * HD
            last = min(first + 2 * HD, heads * HD)
            parts = [whose[:, first:last] for whose in (queries, keys, values, grad_attended)]
            if last - first == 2 * HD:
                own = head_mask(lane, head)
                q_own, k_own, _, g_own = (jnp.where(own, part, jnp.zeros_like(part)) for part in parts)
            else:
                q_own, k_own, _, g_own = parts
            scores = dot(q_own, parts[1], ((1,), (1,))) * (HD**-0.5)
            probs = jnp.where(key_mask, jnp.exp(scores - lse[:, head : head + 1]), 0.0)
            back = dot(g_own, parts[2], ((1,), (1,)))
            product = probs * back
            grad_scores = (product - probs * jnp.sum(product, axis=1, keepdims=True)).astype(bf16)
            pieces = (
                dot(grad_scores, k_own) * (HD**-0.5),
                dot(grad_scores, q_own, ((0,), (0,))) * (HD**-0.5),
                dot(probs.astype(bf16), g_own, ((0,), (0,))),
            )
            for which in range(3):
                if head % 2 == 0:
                    grads[which].append(pieces[which])
                else:
                    grads[which][-1] += pieces[which]
        grad_rows = [jnp.concatenate(grads[which], axis=1).astype(bf16) for which in range(3)]
        grad_one = 0.0
        for which in range(3):
            weight_sum[which * share : (which + 1) * share, :] += dot(grad_rows[which].T, h_one)
            grad_one += dot(grad_rows[which], qkv_ref[which])
        weight_sum[3 * share : 4 * share, :] += dot(attended.T, grad_branch)
        whole[...] = grad_one
        one_mine[image] = whole[:, my_cols].astype(bf16)
        one_to[image] = whole[:, their_cols].astype(bf16)
        one_core_copy(image).start()

    def run_one_x(image):
        one_core_copy(image).wait_recv()
        one_core[image] = (one_core[image].astype(f32) + one_mine[image].astype(f32)).astype(bf16)
        one_x_copy(image).start()

    def run_one_total(image):
        one_x_copy(image).wait_recv()
        one_x[image] = (one_core[image].astype(f32) + one_x[image].astype(f32)).astype(bf16)
        one_total_copy(image).start()

    def run_tokens(image):
        one_total_copy(image).wait_recv()
        whole[:, my_cols] = one_x[image].astype(f32)
        whole[:, their_cols] = one_total[image].astype(f32)
        grad_one = whole[...]
        at = at_image(image)
        normed, inverse = norm_stats(tok_ref[image].astype(f32))
        add_sums(late_mine, 0, grad_one, normed)
        total = rows_kept[at, :] + norm_back(grad_one, gain1, normed, inverse)
        whole[...] = total
        for number in range(images):

            @pl.when(image == number)
            def _():
                rows_kept[pl.ds(number * SEQ, SEQ), :] = whole[pl.ds(0, SEQ), :]


    def stage(tick, lag, run):
        image = tick - lag

        @pl.when((image >= 0) & (image < images))
        def _():
            run(image)

    def at_tick(tick, when, run):
        @pl.when(tick == when)
        def _():
            run()

    def line_second():
        line_add(1)
        line_pass(0)

    def line_third():
        line_add(2)
        line_pass(1)

    def per_tick(tick, _):
        stage(tick, 0, run_attention)
        stage(tick, 1, run_one_x)
        stage(tick, 4, run_one_total)
        stage(tick, 5, run_tokens)
        at_tick(tick, 5, lambda: run_m_x(0))
        at_tick(tick, 3, line_second)
        at_tick(tick, 6, line_third)
        at_tick(tick, 7, lambda: run_m_x(1))
        return 0

    for copy in weight_loads:
        copy.wait()
    lax.fori_loop(0, images, per_tick, 0)

    part_rows = shared.shape[1]
    chunks = 2
    chunk_rows = part_rows // chunks
    quarter = chunk_rows // planes

    def cast(piece, _):
        for side in range(2):
            at_rows = aligned(piece * 96, 96)
            shared[side, at_rows, :] = weight_sum[aligned(side * part_rows + piece * 96, 96), :].astype(bf16)
        return 0

    lax.fori_loop(0, part_rows // 96, cast, 0)

    def y_piece(number):
        inner = jnp.where(z_at == 1, jnp.where(number < 2, z_last - number, number - 2), jnp.where(number < 2, number, 5 - number))
        return jnp.where(z_at == 0, z_last - number, jnp.where(z_at == z_last, number, inner))

    def quarter_at(chunk, piece):
        return aligned(chunk * chunk_rows + piece * quarter, quarter)

    def shared_y_copy(chunk, number):
        at_rows = quarter_at(chunk, y_piece(number))
        return remote(
            shared.at[1 - y_at, at_rows, :], shared_y.at[at_rows, :], sy_s.at[chunk, number], sy_r.at[chunk, number], y_dev
        )

    def take_y(chunk, number):
        shared_y_copy(chunk, number).wait_recv()
        at_rows = quarter_at(chunk, y_piece(number))
        weight_half[at_rows, :] = shared[y_at, at_rows, :].astype(f32) + shared_y[at_rows, :].astype(f32)

    def quarter_of(step, at, way):
        mirrored = z_last - step + at
        return mirrored if way == 0 else z_last - mirrored

    def small_copy(chunk, step, way):
        return remote(
            shared_line.at[chunk, way, 0, step],
            shared_line.at[chunk, way, 1, step],
            sl_s.at[chunk, way, step],
            sl_r.at[chunk, way, step],
            z_devs[way],
        )

    def sum_wait(chunk, step):
        for way in range(2):
            at = place(way)

            @pl.when((at > 0) & (at - 1 <= step))
            def _():
                small_copy(chunk, step, way).wait_recv()

    def sum_send(chunk, step):
        for way in range(2):
            at = place(way)

            @pl.when((at <= step) & (at < z_last))
            def _():
                at_rows = quarter_at(chunk, quarter_of(step, at, way))
                if step == 0:
                    shared_line[chunk, way, 0, step] = weight_half[at_rows, :].astype(bf16)
                else:
                    came = jnp.where(at > 0, shared_line[chunk, way, 1, step - 1].astype(f32), 0.0)
                    shared_line[chunk, way, 0, step] = (weight_half[at_rows, :] + came).astype(bf16)
                small_copy(chunk, step, way).start()

    def final_rows(chunk, side, piece):
        return shared_all.at[side, quarter_at(chunk, piece), :]

    def gather_z(chunk, step, way, piece):
        ref = final_rows(chunk, y_at, piece)
        return remote(ref, ref, sg_s.at[chunk, way, step], sg_r.at[chunk, way, step], z_devs[way])

    def gather_y(chunk, step, way, piece, side):
        ref = final_rows(chunk, side, piece)
        return remote(ref, ref, sz_s.at[chunk, way, step], sz_r.at[chunk, way, step], y_dev)

    def piece_out(step, way):
        return z_at - step if way == 0 else z_at + step

    def piece_in(step, way):
        return z_at - 1 - step if way == 0 else z_at + 1 + step

    def gather_send(chunk, step):
        for way in range(2):
            at = place(way)

            @pl.when((at >= step) & (at < z_last))
            def _():
                gather_z(chunk, step, way, piece_out(step, way)).start()

    def gather_take(chunk, step):
        for way in range(2):

            @pl.when(place(way) >= 1 + step)
            def _():
                gather_z(chunk, step, way, piece_in(step, way)).wait_recv()
                gather_y(chunk, step + 1, way, piece_in(step, way), y_at).start()

    def finish_sum(chunk):
        own_rows = quarter_at(chunk, z_at)
        from_below = jnp.where(z_at > 0, shared_line[chunk, 0, 1, 2].astype(f32), 0.0)
        from_above = jnp.where(z_at < z_last, shared_line[chunk, 1, 1, 2].astype(f32), 0.0)
        shared_all[y_at, own_rows, :] = (weight_half[own_rows, :] + from_below + from_above).astype(bf16)
        gather_y(chunk, 0, 0, z_at, y_at).start()

    late_y_copy = remote(late_mine, late_y, late_s.at[0], late_r.at[0], y_dev)

    def late_copy(number):
        ref = late_z.at[z_at]
        return remote(ref, ref, late_s.at[number + 1], late_r.at[number + 1], z_others[number])

    def meanwhile(place_in_order):
        if place_in_order == 0:
            run_one_x(images - 1)
            run_tokens(images - 5)
            run_one_total(images - 4)
            run_m_x(part_count - 2)
        if place_in_order == 1:
            run_m_x(part_count - 1)
            run_tokens(images - 4)
            run_one_total(images - 3)
        if place_in_order == 2:
            run_m_out(0)
            run_tokens(images - 3)
        if place_in_order == 3:
            line_part(0)
            run_one_total(images - 2)
            run_m_out(1)
            run_tokens(images - 2)
        if place_in_order == 4:
            line_part(1)
            run_one_total(images - 1)
            run_m_out(2)
        if place_in_order == 5:
            line_part(2)
            run_tokens(images - 1)
            route_two.wait_recv()
            late_mine[8:16, :] = route_core[...] + route_x[...]
            late_y_copy.start()
            tokens_low[...] = rows_kept[pl.ds(0, images * SEQ), :].astype(bf16)
            store_copy.start()
        if place_in_order == 6:
            line_part(3)
            run_m_out(3)
            late_y_copy.wait_recv()
            late_z[z_at] = late_mine[...] + late_y[...]
            for number in range(planes - 1):
                late_copy(number).start()

    for number in range(4):
        for chunk in range(chunks):
            shared_y_copy(chunk, number).start()
    meanwhile(0)
    for step in range(3):
        for chunk in range(chunks):
            if step > 0:
                sum_wait(chunk, step - 1)
            take_y(chunk, step)
            sum_send(chunk, step)
        if step == 2:
            for chunk in range(chunks):
                take_y(chunk, 3)
        meanwhile(1 + step)
    for chunk in range(chunks):
        sum_wait(chunk, 2)
        finish_sum(chunk)
        gather_send(chunk, 0)
    for step in range(3):
        meanwhile(4 + step)
        for chunk in range(chunks):
            gather_take(chunk, step)
            if step < 2:
                gather_send(chunk, step + 1)

    for way in range(2):

        @pl.when(place(way) == 2)
        def _():
            line_copy_on(way, 2).wait_recv()
            for part in range(4):
                line_part_copy(way, part).wait_recv()

        @pl.when(place(way) == z_last)
        def _():
            line_copy_on(way, 0).wait_recv()
            line_copy_on(way, 1).wait_recv()

    from_far = 1 - z_at // 2
    first_piece = jnp.where((z_at == 0) | (z_at == z_last), 0, 2)

    line_out_copies = [
        pltpu.make_async_copy(line.at[from_far, first_piece + n], line_out.at[n], weight_store.at[n]) for n in range(2)
    ]
    for copy in line_out_copies:
        copy.start()
    for chunk in range(chunks):
        gather_y(chunk, 0, 0, z_at, 1 - y_at).wait_recv()
        for step in range(3):
            for way in range(2):

                @pl.when(place(way) >= 1 + step)
                def _():
                    gather_y(chunk, step + 1, way, piece_in(step, way), 1 - y_at).wait_recv()

    for number in range(planes - 1):
        late_copy(number).wait_recv()
    late = late_z[0]
    for plane in range(1, planes):
        late += late_z[plane]
    sums_all[...] = late
    out_copies = [
        pltpu.make_async_copy(shared_all, weights_out, weight_store.at[2]),
        pltpu.make_async_copy(sums_all, sums_out, weight_store.at[3]),
    ]
    for copy in out_copies:
        copy.start()
    route_one.wait_send()
    route_two.wait_send()

    def drain(image, _):
        for copy in (one_core_copy, one_x_copy, one_total_copy):
            copy(image).wait_send()
        return 0

    lax.fori_loop(0, images, drain, 0)
    for part in range(part_count):
        m_core_copy(0, part).wait_send()
        m_core_copy(1, part).wait_send()
        m_y_copy(part).wait_send()

        @pl.when(keeps)
        def _():
            m_quarter_copy(part).wait_send()
            m_store_copy(part).wait()

        @pl.when(jnp.logical_not(keeps))
        def _():
            m_x_copy(part).wait_send()
            m_quarter_copy(part).wait_recv()

    for copy in (*line_out_copies, *out_copies, store_copy):
        copy.wait()
    late_y_copy.wait_send()
    for number in range(planes - 1):
        late_copy(number).wait_send()
    for way in range(2):

        @pl.when(place(way) == 0)
        def _():
            for piece in range(1, 4):
                line_copy_on(way, piece).wait_send()

        @pl.when(place(way) == 1)
        def _():
            for piece in range(3):
                line_copy_on(way, piece).wait_send()
            for part in range(4):
                line_part_copy(way, part).wait_send()

        @pl.when(place(way) == 2)
        def _():
            for piece in range(2):
                line_copy_on(way, piece).wait_send()

    for chunk in range(chunks):
        gather_y(chunk, 0, 0, z_at, y_at).wait_send()
        for number in range(4):
            shared_y_copy(chunk, number).wait_send()
        for step in range(3):
            for way in range(2):
                at = place(way)

                @pl.when((at <= step) & (at < z_last))
                def _():
                    small_copy(chunk, step, way).wait_send()

                @pl.when((at >= step) & (at < z_last))
                def _():
                    gather_z(chunk, step, way, piece_out(step, way)).wait_send()

                @pl.when(at >= 1 + step)
                def _():
                    gather_y(chunk, step + 1, way, piece_in(step, way), y_at).wait_send()


def run_backward(gain1, shift1, gain2, grad_router, qkv_w, out_w, tok, *streamed):
    images, _, features = tok.shape
    rows = images * PITCH
    share = out_w.shape[0]
    heads = share // HD
    hidden = streamed[-1].shape[1]
    wide = features // 2
    parts = 4
    vmem = pl.BlockSpec(memory_space=pltpu.VMEM)
    anywhere = pl.BlockSpec(memory_space=pl.ANY)
    shape = jax.ShapeDtypeStruct
    dma = pltpu.SemaphoreType.DMA
    block = (images, PITCH, wide)
    return pl.pallas_call(
        partial(backward_kernel, images=images, heads=heads),
        out_shape=[
            shape((2, features, hidden), bf16),
            shape((images * SEQ, features), bf16),
            shape((2, features // 2, features), bf16),
            shape((16, features), f32),
            shape((rows, wide // 2), bf16),
        ],
        in_specs=[vmem] * 4 + [anywhere] * (3 + len(streamed)),
        out_specs=[anywhere] * 5,
        scratch_shapes=[
            pltpu.VMEM(qkv_w.shape, bf16),
            pltpu.VMEM(out_w.shape, bf16),
            pltpu.VMEM((images, PITCH, features), bf16),
            *[pltpu.VMEM((images, PITCH, share), bf16)] * 4,
            pltpu.VMEM((images, PITCH, 128), f32),
            pltpu.VMEM((rows, features), bf16),
            pltpu.VMEM((rows, features), f32),
            pltpu.VMEM((rows, features), bf16),
            pltpu.VMEM((2 * rows, wide), bf16),
            pltpu.VMEM((2 * rows, wide), bf16),
            *[pltpu.VMEM((parts, rows // parts, wide), bf16)] * 2,
            pltpu.VMEM((parts, 2, rows // parts, wide // 2), bf16),
            pltpu.VMEM((rows // parts, wide), f32),
            pltpu.VMEM((2, features, 2 * hidden), bf16),
            *[pltpu.VMEM(block, bf16)] * 5,
            pltpu.VMEM((2, 4, features, hidden), bf16),
            pltpu.VMEM((features, features), f32),
            pltpu.VMEM((features // 2, features), f32),
            pltpu.VMEM((2, features // 2, features), bf16),
            pltpu.VMEM((features // 2, features), bf16),
            pltpu.VMEM((2, 2, 2, 3, features // 16, features), bf16),
            pltpu.VMEM((2, features // 2, features), bf16),
            *[pltpu.VMEM((8, features), f32)] * 2,
            *[pltpu.VMEM((16, features), f32)] * 2,
            pltpu.VMEM((4, 16, features), f32),
            pltpu.VMEM((16, features), f32),
            pltpu.VMEM((images * SEQ, features), bf16),
            pltpu.VMEM((PITCH, features), f32),
        ]
        + [dma((2, parts))] * 2
        + [dma((parts,))] * 7
        + [dma((images,))] * 6
        + [dma((2, 7))] * 2
        + [dma((2, 4))] * 2
        + [dma((2, 2, 3))] * 4
        + [dma((2, 2, 4))] * 2
        + [dma((2,))] * 2
        + [dma((4,))] * 2
        + [dma((4,)), dma((9, images)), dma((5,)), dma((4,)), dma((1,))],
        compiler_params=pltpu.CompilerParams(
            collective_id=2, has_side_effects=True, vmem_limit_bytes=63 << 20
        ),
    )(gain1, shift1, gain2, grad_router, qkv_w, out_w, tok, *streamed)


def last_kernel(
    side_ref, tokens_ref, weights_ref, up_first, up_pair, down_first, down_pair, line_ref, tokens_out, qkv_out, out_w_out, up_out, down_out
):
    share = out_w_out.shape[0]
    tokens_out[...] = tokens_ref[...].astype(f32)
    for which in range(3):
        qkv_out[which] = weights_ref[which * share : (which + 1) * share, :].astype(f32)
    out_w_out[...] = weights_ref[3 * share :, :].astype(f32)
    up_out[...] = up_first[...].astype(f32) + up_pair[...].astype(f32) + line_ref[0].astype(f32)
    down_out[...] = (down_first[...].astype(f32) + down_pair[...].astype(f32) + line_ref[1].astype(f32)).T


def run_last(side, tokens, weights, up_first, up_pair, down_first, down_pair, line, share):
    rows, features = tokens.shape
    hidden = up_pair.shape[1]
    shape = jax.ShapeDtypeStruct

    steps = features // 128
    height = -(-rows // (16 * steps)) * 16
    by_rows = pl.BlockSpec((height, features), lambda n, side: (n, 0))

    def lanes(height):
        return pl.BlockSpec((height, 128), lambda n, side: (0, n))

    own = pl.BlockSpec((128, hidden), lambda n, side: (n, side[0]))
    plain = pl.BlockSpec((128, hidden), lambda n, side: (n, 0))
    return pl.pallas_call(
        last_kernel,
        grid_spec=pltpu.PrefetchScalarGridSpec(
            num_scalar_prefetch=1,
            grid=(features // 128,),
            in_specs=[
                by_rows,
                lanes(features),
                own,
                plain,
                own,
                plain,
                pl.BlockSpec((2, 128, hidden), lambda n, side: (0, n, 0)),
            ],
            out_specs=[
                by_rows,
                pl.BlockSpec((3, share, 128), lambda n, side: (0, 0, n)),
                lanes(share),
                plain,
                lanes(hidden),
            ],
        ),
        out_shape=[
            shape((rows, features), f32),
            shape((3, share, features), f32),
            shape((share, features), f32),
            shape((features, hidden), f32),
            shape((hidden, features), f32),
        ],
    )(side, tokens, weights, up_first, up_pair, down_first, down_pair, line)


def per_image(rows_in):
    images = rows_in.shape[0] // SEQ
    blocks = rows_in.reshape(images, SEQ, rows_in.shape[1])
    return jnp.pad(blocks, ((0, 0), (0, PITCH - SEQ), (0, 0)))


def unpad(blocks):
    images = blocks.shape[0]
    return blocks[:, :SEQ].reshape(images * SEQ, blocks.shape[2])


def per_device_dense(
    tokens,
    gain_attn,
    shift_attn,
    qkv_weight,
    out_weight,
    gain_moe,
    shift_moe,
    router_weight,
    expert_up,
    expert_down,
    routes,
    keep_mask,
    cotangent,
):
    row_count, feature_count = tokens.shape
    images = row_count // SEQ
    rows = images * PITCH
    tensor_count = lax.axis_size("tensor")
    quarter_width = feature_count // tensor_count
    experts_all = router_weight.shape[1]
    hidden = expert_up.shape[2]
    kept_routes = per_image(jnp.where(keep_mask > 0, routes, -1) + 1).reshape(rows, 2) - 1
    chosen = kept_routes[:, :, None] == jnp.arange(128, dtype=jnp.int32)[None, None, :]
    kept = jnp.any(chosen, axis=1).astype(bf16)
    cot_turned = jnp.pad(cotangent.T, ((0, 0), (0, -row_count % 128)))
    qkv_turned = jnp.swapaxes(qkv_weight, 1, 2)
    (
        queries,
        keys,
        values,
        attended,
        lse,
        resid,
        h_all,
        cot_all,
        kept_all,
        up_all,
        down_all,
        mixed_first,
        grad_h_first,
        gate_first,
        up_first,
        down_first,
        tok,
        router_wide,
    ) = run_forward(
        tokens,
        gain_attn,
        shift_attn,
        gain_moe,
        shift_moe,
        qkv_turned,
        out_weight,
        expert_up[0],
        expert_down[0],
        router_weight.T,
        cot_turned,
        kept,
        experts_all,
    )
    mixed_part, grad_router, up_second, down_second, grad_h_two, up_pair, down_pair, line_first = run_second_pair(
        h_all,
        cot_all,
        kept_all,
        router_wide,
        mixed_first,
        grad_h_first,
        gate_first,
        up_all,
        down_all,
        up_first,
        down_first,
        experts_all,
    )
    line_sum, tokens_grad, weights_grad, sums, mixed = run_backward(
        gain_attn,
        shift_attn,
        gain_moe,
        grad_router,
        qkv_turned,
        out_weight,
        tok,
        queries,
        keys,
        values,
        attended,
        lse,
        grad_h_two,
        resid,
        cot_all,
        mixed_part,
        up_second,
        down_second,
        line_first,
    )
    side = (lax.axis_index("expert") // 2 % 2).astype(jnp.int32)[None]
    grad_tokens, grad_qkv, grad_out, grad_up, grad_down = run_last(
        side,
        tokens_grad,
        weights_grad.reshape(feature_count, feature_count),
        up_first,
        up_pair,
        down_first,
        down_pair,
        line_sum,
        qkv_weight.shape[2],
    )
    return (
        unpad(mixed.reshape(images, PITCH, quarter_width)),
        grad_tokens,
        sums[0],
        sums[1],
        jnp.swapaxes(grad_qkv, 1, 2),
        grad_out,
        sums[2],
        sums[3],
        sums[8 : 8 + experts_all].T,
        grad_up[None],
        grad_down[None],
    )


def per_device(*arguments):
    router_weight = arguments[7]
    if router_weight.shape[1] == 4 and lax.axis_size("expert") == 8 and lax.axis_size("tensor") == 4:
        return per_device_dense(*arguments)
    return per_device_routed(*arguments)


def solution(mesh):
    placed = (
        P("expert", None),
        P(),
        P(),
        P(None, None, "tensor"),
        P("tensor", None),
        P(),
        P(),
        P(),
        P("expert", None, "tensor"),
        P("expert", "tensor", None),
        P("expert", None),
        P("expert", None),
        P("expert", "tensor"),
    )
    return jax.shard_map(
        per_device,
        mesh=mesh,
        in_specs=placed,
        out_specs=(
            P("expert", "tensor"),
            P("expert", None),
            P(),
            P(),
            P(None, None, "tensor"),
            P("tensor", None),
            P(),
            P(),
            P(),
            P("expert", None, "tensor"),
            P("expert", "tensor", None),
        ),
        check_vma=False,
    )
```

```python
from functools import partial

import jax
import jax.numpy as jnp
from jax import lax
from jax.experimental import pallas as pl
from jax.experimental.pallas import tpu as pltpu
from jax.sharding import PartitionSpec as P

HD = 64
SEQ = 197


norm_epsilon = 1e-06


def norm_rows(values, gain, shift):
    row_mean = jnp.mean(values, axis=-1, keepdims=True)
    centred = values - row_mean
    spread = jnp.mean(centred * centred, axis=-1, keepdims=True)
    return centred * lax.rsqrt(spread + norm_epsilon) * gain + shift


def gelu_exact(values):
    return jax.nn.gelu(values, approximate=False)


def gate_from_logits(logit_rows, picked_rows, keep_rows):
    router_probs = jax.nn.softmax(logit_rows, axis=-1)
    return jnp.sum(jnp.where(picked_rows, router_probs[:, None, :], 0.0), axis=-1) * keep_rows


def attention_forward(h_rows, qkv_w, out_w):
    row_total_count = h_rows.shape[0]
    head_count = qkv_w.shape[2] // HD
    image_count = row_total_count // SEQ
    score_scale = HD ** (-0.5)
    projected = jnp.einsum("td,cdf->ctf", h_rows, qkv_w, preferred_element_type=jnp.float32).astype(
        jnp.bfloat16
    )
    split_heads = projected.reshape(3, image_count, SEQ, head_count, HD)
    queries = split_heads[0]
    keys_all = split_heads[1]
    values_all = split_heads[2]
    scores = (
        jnp.einsum("gqhe,gkhe->ghqk", queries, keys_all, preferred_element_type=jnp.float32)
        * score_scale
    )
    row_peak = jnp.max(scores, axis=-1, keepdims=True)
    exp_scores = jnp.exp(scores - row_peak)
    row_total = jnp.sum(exp_scores, axis=-1, keepdims=True)
    log_total = row_peak + jnp.log(row_total)
    weights = (exp_scores / row_total).astype(jnp.bfloat16)
    attended = jnp.einsum(
        "ghqk,gkhe->gqhe", weights, values_all, preferred_element_type=jnp.float32
    ).astype(jnp.bfloat16)
    attended = attended.reshape(row_total_count, head_count * HD)
    partial_out = jnp.dot(attended, out_w, preferred_element_type=jnp.float32)
    return (partial_out, (attended, queries, keys_all, values_all, log_total))


def attention_backward(grad_branch, saved, h_rows, qkv_w, out_w):
    attended, queries, keys_all, values_all, log_total = saved
    row_total_count = h_rows.shape[0]
    head_count = qkv_w.shape[2] // HD
    image_count = row_total_count // SEQ
    score_scale = HD ** (-0.5)
    grad_out = jnp.einsum("tc,td->cd", attended, grad_branch, preferred_element_type=jnp.float32)
    grad_attended = jnp.einsum(
        "td,cd->tc", grad_branch, out_w, preferred_element_type=jnp.float32
    ).astype(jnp.bfloat16)
    grad_attended = grad_attended.reshape(image_count, SEQ, head_count, HD)
    scores_again = (
        jnp.einsum("gqhe,gkhe->ghqk", queries, keys_all, preferred_element_type=jnp.float32)
        * score_scale
    )
    probs_again = jnp.exp(scores_again - log_total)
    grad_weights = jnp.einsum(
        "gqhe,gkhe->ghqk", grad_attended, values_all, preferred_element_type=jnp.float32
    )
    grad_scores = (
        probs_again * (grad_weights - jnp.sum(probs_again * grad_weights, axis=-1, keepdims=True))
    ).astype(jnp.bfloat16)
    grad_queries = (
        jnp.einsum("ghqk,gkhe->gqhe", grad_scores, keys_all, preferred_element_type=jnp.float32)
        * score_scale
    )
    grad_keys = (
        jnp.einsum("ghqk,gqhe->gkhe", grad_scores, queries, preferred_element_type=jnp.float32)
        * score_scale
    )
    grad_values = jnp.einsum(
        "ghqk,gqhe->gkhe",
        probs_again.astype(jnp.bfloat16),
        grad_attended,
        preferred_element_type=jnp.float32,
    )
    grad_rows = (
        jnp.stack([grad_queries, grad_keys, grad_values])
        .astype(jnp.bfloat16)
        .reshape(3, row_total_count, head_count * HD)
    )
    grad_qkv = jnp.einsum("td,ctf->cdf", h_rows, grad_rows, preferred_element_type=jnp.float32)
    grad_h_one = jnp.einsum("ctf,cdf->td", grad_rows, qkv_w, preferred_element_type=jnp.float32)
    return (grad_qkv, grad_out, grad_h_one)


def moe_tail(
    grad_h_rows,
    grad_gate_rows,
    grad_out_rows,
    h_two_rows,
    resid_rows,
    gate_back,
    router_weight,
    gain_moe,
    shift_moe,
):
    row_total_count = grad_h_rows.shape[0]
    grad_gate = jnp.sum(grad_gate_rows.reshape(row_total_count, -1, 2), axis=1)
    grad_logits = gate_back(grad_gate)[0].astype(jnp.bfloat16)
    grad_router = jnp.einsum(
        "td,te->de", h_two_rows, grad_logits, preferred_element_type=jnp.float32
    )
    grad_h_two = grad_h_rows + jnp.einsum(
        "te,de->td", grad_logits, router_weight, preferred_element_type=jnp.float32
    )
    norm_out, norm_back = jax.vjp(norm_rows, resid_rows, gain_moe, shift_moe)
    grad_resid_norm, grad_gain_moe, grad_shift_moe = norm_back(grad_h_two)
    return (grad_out_rows + grad_resid_norm, grad_router, grad_gain_moe, grad_shift_moe)


def per_device_routed(
    tokens,
    gain_attn,
    shift_attn,
    qkv_weight,
    out_weight,
    gain_moe,
    shift_moe,
    router_weight,
    expert_up,
    expert_down,
    routes,
    keep_mask,
    cotangent,
):
    row_count, feature_count = tokens.shape
    tensor_count = lax.axis_size("tensor")
    expert_count = lax.axis_size("expert")
    tensor_here = lax.axis_index("tensor")
    quarter_width = feature_count // tensor_count
    col_start = tensor_here * quarter_width
    experts_all = router_weight.shape[1]
    capacity = max(2, 7 * row_count // (2 * experts_all))
    tokens_float = tokens.astype(jnp.float32)
    h_one = norm_rows(tokens_float, gain_attn, shift_attn).astype(jnp.bfloat16)
    partial_out, saved = attention_forward(h_one, qkv_weight, out_weight)
    branch = lax.psum(partial_out, "tensor")
    resid = tokens_float + branch
    h_two = norm_rows(resid, gain_moe, shift_moe).astype(jnp.bfloat16)
    logits = jnp.dot(h_two, router_weight, preferred_element_type=jnp.float32)
    keep_float = keep_mask.astype(jnp.float32)
    picked = routes[:, :, None] == jnp.arange(experts_all, dtype=jnp.int32)[None, None, :]
    gate_values, gate_back = jax.vjp(
        partial(gate_from_logits, picked_rows=picked, keep_rows=keep_float), logits
    )
    flat_expert = routes.reshape(-1)
    one_hot = (flat_expert[:, None] == jnp.arange(experts_all, dtype=jnp.int32)[None, :]).astype(
        jnp.int32
    )
    rank_within = jnp.sum((jnp.cumsum(one_hot, axis=0) - one_hot) * one_hot, axis=1)
    slot_index = flat_expert * capacity + rank_within
    token_index = jnp.repeat(jnp.arange(row_count, dtype=jnp.int32), 2)
    live_route = keep_mask.reshape(-1) > 0
    source_table = (
        jnp.full((experts_all * capacity,), row_count, jnp.int32)
        .at[slot_index]
        .set(jnp.where(live_route, token_index, row_count))
    )
    padded_rows = jnp.concatenate([h_two, jnp.zeros((1, feature_count), jnp.bfloat16)], axis=0)
    dispatch = padded_rows[source_table].reshape(experts_all, capacity, feature_count)
    paired = jnp.broadcast_to(dispatch[:, None], (experts_all, 2, capacity, feature_count)).reshape(
        expert_count, capacity, feature_count
    )
    arrived = lax.all_to_all(paired, "expert", split_axis=0, concat_axis=0, tiled=True)
    expert_rows = arrived.reshape(expert_count * capacity, feature_count)
    up_local = expert_up[0]
    down_local = expert_down[0]
    pre_act = jnp.dot(expert_rows, up_local, preferred_element_type=jnp.float32)
    hidden_float, gelu_back = jax.vjp(gelu_exact, pre_act)
    hidden = hidden_float.astype(jnp.bfloat16)
    partial_down = jnp.dot(hidden, down_local, preferred_element_type=jnp.float32)
    summed = lax.psum_scatter(partial_down, "tensor", scatter_dimension=1, tiled=True)
    returned = lax.all_to_all(
        summed.reshape(expert_count, capacity, quarter_width),
        "expert",
        split_axis=0,
        concat_axis=0,
        tiled=True,
    )
    answer_table = jnp.sum(
        returned.reshape(experts_all, 2, capacity, quarter_width), axis=1
    ).astype(jnp.bfloat16)
    answers = (
        answer_table.reshape(experts_all * capacity, quarter_width)[slot_index]
        .astype(jnp.float32)
        .reshape(row_count, 2, quarter_width)
    )
    resid_part = lax.dynamic_slice_in_dim(resid, col_start, quarter_width, 1)
    mixed = (resid_part + jnp.sum(gate_values[:, :, None] * answers, axis=1)).astype(jnp.bfloat16)
    grad_part = cotangent.astype(jnp.float32)
    grad_answers = (
        (gate_values[:, :, None] * grad_part[:, None, :])
        .astype(jnp.bfloat16)
        .reshape(2 * row_count, quarter_width)
    )
    grad_gate_part = jnp.sum(grad_part[:, None, :] * answers, axis=-1)
    outgoing = (
        jnp.zeros((experts_all * capacity, quarter_width), jnp.bfloat16)
        .at[slot_index]
        .set(grad_answers)
    )
    outgoing = jnp.broadcast_to(
        outgoing.reshape(experts_all, 1, capacity, quarter_width),
        (experts_all, 2, capacity, quarter_width),
    ).reshape(expert_count, capacity, quarter_width)
    incoming = lax.all_to_all(outgoing, "expert", split_axis=0, concat_axis=0, tiled=True)
    grad_full = lax.all_gather(incoming, "tensor", axis=2, tiled=True).reshape(
        expert_count * capacity, feature_count
    )
    grad_hidden = jnp.einsum("rd,fd->rf", grad_full, down_local, preferred_element_type=jnp.float32)
    grad_pre = gelu_back(grad_hidden)[0].astype(jnp.bfloat16)
    grad_down = jnp.einsum("rf,rd->fd", hidden, grad_full, preferred_element_type=jnp.float32)
    grad_up = jnp.einsum("rd,rf->df", expert_rows, grad_pre, preferred_element_type=jnp.float32)
    grad_rows_partial = jnp.einsum(
        "rf,df->rd", grad_pre, up_local, preferred_element_type=jnp.float32
    )
    grad_rows_sum = lax.psum_scatter(
        grad_rows_partial.astype(jnp.bfloat16), "tensor", scatter_dimension=1, tiled=True
    ).astype(jnp.float32)
    sent_back = lax.all_to_all(
        grad_rows_sum.reshape(expert_count, capacity, quarter_width).astype(jnp.bfloat16),
        "expert",
        split_axis=0,
        concat_axis=0,
        tiled=True,
    ).astype(jnp.float32)
    grad_table = jnp.sum(sent_back.reshape(experts_all, 2, capacity, quarter_width), axis=1).astype(
        jnp.bfloat16
    )
    grad_inputs = (
        grad_table.reshape(experts_all * capacity, quarter_width)[slot_index]
        .astype(jnp.float32)
        .reshape(row_count, 2, quarter_width)
    )
    grad_h_part = jnp.sum(grad_inputs * keep_float[:, :, None], axis=1)
    grad_h_full, grad_gate_all, grad_out_full = (
        lax.all_gather(grad_h_part, "tensor", axis=1, tiled=True),
        lax.all_gather(grad_gate_part, "tensor", axis=1, tiled=True),
        lax.all_gather(grad_part, "tensor", axis=1, tiled=True),
    )
    grad_resid, grad_router, grad_gain_moe, grad_shift_moe = moe_tail(
        grad_h_full,
        grad_gate_all,
        grad_out_full,
        h_two,
        resid,
        gate_back,
        router_weight,
        gain_moe,
        shift_moe,
    )
    grad_qkv, grad_out, grad_h_one_part = attention_backward(
        grad_resid.astype(jnp.bfloat16), saved, h_one, qkv_weight, out_weight
    )
    grad_h_one = lax.psum(grad_h_one_part.astype(jnp.bfloat16), "tensor").astype(jnp.float32)
    norm_one_out, norm_one_back = jax.vjp(norm_rows, tokens_float, gain_attn, shift_attn)
    grad_tok_norm, grad_gain_attn, grad_shift_attn = norm_one_back(grad_h_one)
    grad_tokens = grad_resid + grad_tok_norm
    summed_grads = lax.psum(
        (
            grad_gain_attn,
            grad_shift_attn,
            grad_qkv,
            grad_out,
            grad_gain_moe,
            grad_shift_moe,
            grad_router,
        ),
        "expert",
    )
    grad_qkv_mine = summed_grads[2]
    grad_out_mine = summed_grads[3]
    return (
        mixed,
        grad_tokens,
        summed_grads[0],
        summed_grads[1],
        grad_qkv_mine,
        grad_out_mine,
        summed_grads[4],
        summed_grads[5],
        summed_grads[6],
        grad_up[None],
        grad_down[None],
    )


MESH = pl.DeviceIdType.MESH
f32 = jnp.float32
bf16 = jnp.bfloat16
PITCH = 208


def dot(left, right, over=((1,), (0,))):
    return lax.dot_general(left, right, (over, ((), ())), preferred_element_type=f32)


def aligned(start, size):
    return pl.ds(pl.multiple_of(start, 16), size)


def lanes_at(start, size):
    return pl.ds(pl.multiple_of(start, 128), size)


def norm_stats(values):
    row_mean = jnp.mean(values, axis=1, keepdims=True)
    centred = values - row_mean
    inverse = lax.rsqrt(jnp.mean(centred * centred, axis=1, keepdims=True) + norm_epsilon)
    return centred * inverse, inverse


def greet(neighbours):
    barrier = pltpu.get_barrier_semaphore()
    count = 0
    for is_there, device in neighbours:

        @pl.when(is_there)
        def _():
            pl.semaphore_signal(barrier, inc=1, device_id=device, device_id_type=MESH)

        count = count + jnp.where(is_there, 1, 0)
    pl.semaphore_wait(barrier, count)


def head_mask(lane, head):
    return (lane < HD) if head % 2 == 0 else (lane >= HD)


def expert_math(h_rows, cot_rows, kept, router, up, down, pair, experts):
    block = h_rows.shape[0]
    hidden = up.shape[1] // 2
    lane = lax.broadcasted_iota(jnp.int32, (block, 128), 1)
    logits = jnp.where(lane < experts, dot(h_rows, router, ((1,), (1,))), -1e30)
    powers = jnp.exp(logits - jnp.max(logits, axis=1, keepdims=True))
    probs = powers / jnp.sum(powers, axis=1, keepdims=True)
    gates = kept * probs
    pre_act = dot(h_rows, up)
    back = dot(cot_rows, down, ((1,), (1,)))
    normal_cdf = 0.5 + 0.5 * lax.erf(pre_act * 0.7071067811865476)
    gelu = pre_act * normal_cdf
    slope = normal_cdf + pre_act * (0.3989422804014327 * jnp.exp(-0.5 * pre_act * pre_act))
    product = gelu * back
    grad_gate = jnp.zeros((block, 128), f32)
    spread = []
    for side in range(2):
        chosen = lane == 2 * pair + side
        part = jnp.sum(product[:, side * hidden : (side + 1) * hidden], axis=1, keepdims=True)
        grad_gate = jnp.where(chosen, part, grad_gate)
        gate = jnp.sum(jnp.where(chosen, gates, 0.0), axis=1, keepdims=True)
        spread.append(jnp.broadcast_to(gate, (block, hidden)))
    gate = jnp.concatenate(spread, axis=1)
    hidden_rows = (gelu * gate).astype(bf16)
    grad_pre = (slope * back * gate).astype(bf16)
    return hidden_rows, grad_pre, probs, grad_gate


BLOCK = 2 * PITCH


def forward_kernel(
    gain1_ref,
    shift1_ref,
    gain2_ref,
    shift2_ref,
    up_ref,
    down_ref,
    router_raw,
    cot_hbm,
    kept_hbm,
    tok_hbm,
    qkv_hbm,
    out_w_hbm,
    q_ref,
    k_ref,
    v_ref,
    att_ref,
    lse_ref,
    resid_ref,
    h_out,
    cot_out,
    kept_out,
    up_out,
    down_out,
    mixed_out,
    grad_h_out,
    gate_out,
    grad_up_out,
    grad_down_out,
    tok_out,
    router_out,
    router_ref,
    cot_turned,
    kept_ref,
    tok_raw,
    qkv_ref,
    out_w_ref,
    tok_ref,
    cot_ref,
    up_vm,
    down_vm,
    up_sum,
    down_sum,
    mixed_slots,
    grad_h_slots,
    gate_slots,
    grad_up_vm,
    grad_down_vm,
    q_all,
    k_all,
    v_all,
    att_all,
    lse_all,
    resid_all,
    h_all,
    cot_all,
    kept_all,
    part,
    mine,
    core_from,
    core_to,
    x_to,
    x_from,
    total_to,
    total_from,
    cot_core,
    core_s,
    core_r,
    x_s,
    x_r,
    tot_s,
    tot_r,
    y_s,
    y_r,
    rel_s,
    rel_r,
    w_s,
    w_r,
    c_s,
    c_r,
    load_sem,
    own_sem,
    pair_sem,
    block_sem,
    grad_sem,
    cot_sem,
    out_sem,
    *,
    images,
    heads,
    experts,
):
    expert_at = lax.axis_index("expert")
    tensor_at = lax.axis_index("tensor")
    z_at, y_at = expert_at // 2, expert_at % 2
    z_last = lax.axis_size("expert") // 2 - 1
    x_at, core_at = tensor_at // 2, tensor_at % 2
    other = 1 - core_at
    rows = images * PITCH
    half = rows // 2
    wide = out_w_ref.shape[1] // 2
    loads = [
        pltpu.make_async_copy(source, target, load_sem.at[number])
        for number, (source, target) in enumerate(
            (
                (cot_hbm, cot_turned),
                (kept_hbm, kept_ref),
                (tok_hbm, tok_raw),
                (qkv_hbm, qkv_ref),
                (out_w_hbm, out_w_ref),
            )
        )
    ]
    for copy in loads:
        copy.start()
    hidden = up_ref.shape[1]
    core_dev = (expert_at, tensor_at + 1 - 2 * core_at)
    x_dev = (expert_at, tensor_at + 2 - 4 * x_at)
    y_dev = (expert_at + 1 - 2 * y_at, tensor_at)
    z_up = (expert_at + 2, tensor_at)
    z_down = (expert_at - 2, tensor_at)
    has_up, has_down = z_at < z_last, z_at > 0
    greet([(True, core_dev), (True, x_dev), (True, y_dev), (has_up, z_up), (has_down, z_down)])

    def remote(src, dst, send, recv, device):
        return pltpu.make_async_remote_copy(
            src_ref=src, dst_ref=dst, send_sem=send, recv_sem=recv, device_id=device, device_id_type=MESH
        )

    def slot(expert, plane):
        pair = (expert // 2 + plane // 2) % 2
        return (
            up_out.at[pair, :, lanes_at(expert % 2 * hidden, hidden)],
            down_out.at[pair, aligned(expert % 2 * hidden, hidden), :],
        )

    def hop(step, way):
        expert = z_at - step if way == 0 else z_at + step
        plane = z_at + 1 if way == 0 else z_at - 1
        source = (up_ref, down_ref) if step == 0 else slot(expert, z_at)
        target = slot(expert, plane)
        device = z_up if way == 0 else z_down
        return [remote(source[n], target[n], w_s.at[way, step, n], w_r.at[way, step, n], device) for n in range(2)]

    def hop_goes(step, way):
        if way == 0:
            return (z_at - step >= 0) & has_up
        return (z_at + step <= z_last) & has_down

    def hop_comes(step, way):
        return (z_at - 1 - step >= 0) if way == 0 else (z_at + 1 + step <= z_last)

    def hop_arriving(step, way):
        expert = z_at - 1 - step if way == 0 else z_at + 1 + step
        target = slot(expert, z_at)
        return [remote(target[n], target[n], w_s.at[way, step, n], w_r.at[way, step, n], core_dev) for n in range(2)]

    def start_hops(step, which):
        for way in range(2):

            @pl.when(hop_goes(step, way))
            def _():
                hop(step, way)[which].start()

    def await_hops(step, which):
        for way in range(2):

            @pl.when(hop_comes(step, way))
            def _():
                hop_arriving(step, way)[which].wait_recv()

    def pass_hops(step, which):
        await_hops(step, which)
        start_hops(step + 1, which)

    start_hops(0, 0)
    start_hops(0, 1)

    def pair_place(expert):
        return up_vm.at[:, lanes_at(expert % 2 * hidden, hidden)], down_vm.at[aligned(expert % 2 * hidden, hidden), :]

    near = z_at + 1 - 2 * (z_at % 2)
    own_copies = [
        pltpu.make_async_copy((up_ref, down_ref)[n], pair_place(z_at)[n], own_sem.at[n]) for n in range(2)
    ]
    near_copies = [
        pltpu.make_async_copy(slot(near, z_at)[n], pair_place(near)[n], pair_sem.at[n]) for n in range(2)
    ]
    for copy in own_copies:
        copy.start()

    loads[0].wait()
    for number in range(images):
        first = number * SEQ // 128 * 128
        skip = number * SEQ - first
        lanes_in = cot_turned[:, first : min(first + 384, images * SEQ)].astype(f32)
        if lanes_in.shape[1] < 384:
            lanes_in = jnp.concatenate([lanes_in, jnp.zeros((lanes_in.shape[0], 384 - lanes_in.shape[1]), f32)], axis=1)
        turned = lanes_in.T[skip : skip + SEQ]
        padded = jnp.concatenate([turned, jnp.zeros((PITCH - SEQ, turned.shape[1]), f32)], axis=0)
        cot_ref[number * PITCH : (number + 1) * PITCH, :] = padded.astype(bf16)
    swap = remote(cot_ref, cot_core, c_s.at[0], c_r.at[0], core_dev)
    swap.start()

    narrow = router_raw[...].astype(f32)
    router_ref[0:16, :] = jnp.concatenate([narrow, jnp.zeros((16 - experts, narrow.shape[1]), f32)], axis=0).astype(bf16)
    router_ref[16:128, :] = jnp.zeros((112, narrow.shape[1]), bf16)

    def kept_half(side, core):
        return kept_all.at[aligned(side * rows + core * half, half), :]

    kept_y = remote(kept_half(0, core_at), kept_half(1, core_at), c_s.at[7], c_r.at[7], y_dev)
    kept_share = remote(kept_half(1, core_at), kept_half(1, core_at), c_s.at[6], c_r.at[6], core_dev)
    kept_share_in = remote(kept_half(1, other), kept_half(1, other), c_s.at[6], c_r.at[6], core_dev)
    loads[1].wait()
    kept_all[pl.ds(0, rows), :] = kept_ref[...]
    kept_y.start()
    swap.wait_recv()

    @pl.when(core_at == 0)
    def _():
        both = jnp.concatenate([cot_ref[...], cot_core[...]], axis=1)
        cot_all[pl.ds(0, rows), lanes_at(x_at * wide, wide)] = both

    @pl.when(core_at == 1)
    def _():
        both = jnp.concatenate([cot_core[...], cot_ref[...]], axis=1)
        cot_all[pl.ds(0, rows), lanes_at(x_at * wide, wide)] = both

    def block(side, col_side, core):
        return cot_all.at[aligned(side * rows + core * half, half), lanes_at(col_side * wide, wide)]

    def cot_copy(number, source, target, device):
        return remote(source, target, c_s.at[number], c_r.at[number], device)

    mine_block = block(0, x_at, core_at)
    cot_x = cot_copy(1, mine_block, mine_block, x_dev)
    cot_y = cot_copy(2, mine_block, block(1, x_at, core_at), y_dev)
    cot_x.start()
    cot_y.start()
    across_x, across_y, across_both = block(0, 1 - x_at, core_at), block(1, x_at, core_at), block(1, 1 - x_at, core_at)
    cot_x_in = cot_copy(1, across_x, across_x, x_dev)
    cot_y_in = cot_copy(2, across_y, across_y, y_dev)
    relay_y = cot_copy(3, across_x, across_both, y_dev)
    relay_in = cot_copy(3, across_both, across_both, y_dev)
    cot_share = [
        cot_copy(4, across_x, across_x, core_dev),
        cot_copy(5, across_y, across_y, core_dev),
        cot_copy(8, across_both, across_both, core_dev),
    ]
    arriving = [block(0, 1 - x_at, other), block(1, x_at, other), block(1, 1 - x_at, other)]
    cot_share_in = [cot_copy(number, ref, ref, core_dev) for number, ref in zip((4, 5, 8), arriving)]

    lane = lax.broadcasted_iota(jnp.int32, (PITCH, 2 * HD), 1)
    key_mask = lax.broadcasted_iota(jnp.int32, (PITCH, PITCH), 1) < SEQ
    gain1, shift1, gain2, shift2 = (ref[...].reshape(1, 2 * wide) for ref in (gain1_ref, shift1_ref, gain2_ref, shift2_ref))
    my_cols = lanes_at(core_at * wide, wide)
    their_cols = lanes_at(other * wide, wide)

    def attend(image):
        normed, _ = norm_stats(tok_ref[image].astype(f32))
        h_one = (normed * gain1 + shift1).astype(bf16)
        queries = dot(h_one, qkv_ref[0], ((1,), (1,))).astype(bf16)
        keys = dot(h_one, qkv_ref[1], ((1,), (1,))).astype(bf16)
        values = dot(h_one, qkv_ref[2], ((1,), (1,))).astype(bf16)
        q_all[image] = queries
        k_all[image] = keys
        v_all[image] = values
        outs = []
        lse = jnp.zeros((PITCH, 2 * HD), f32)
        for head in range(heads):
            first = head // 2 * 2 * HD
            last = min(first + 2 * HD, heads * HD)
            q_head, k_head, v_head = queries[:, first:last], keys[:, first:last], values[:, first:last]
            if last - first == 2 * HD:
                q_head = jnp.where(head_mask(lane, head), q_head, jnp.zeros_like(q_head))
            scores = dot(q_head, k_head, ((1,), (1,))) * (HD**-0.5)
            scores = jnp.where(key_mask, scores, -1e30)
            peak = jnp.max(scores, axis=1, keepdims=True)
            powers = jnp.exp(scores - peak)
            row_sum = jnp.sum(powers, axis=1, keepdims=True)
            weights = (powers / row_sum).astype(bf16)
            outs.append(dot(weights, v_head))
            lse = jnp.where(lane == head, peak + jnp.log(row_sum), lse)
        lse_all[image] = lse
        joined = []
        for head in range(0, heads, 2):
            if head + 1 < heads:
                joined.append(jnp.where(lane < HD, outs[head], outs[head + 1]))
            else:
                joined.append(outs[head])
        attended = jnp.concatenate(joined, axis=1).astype(bf16)
        att_all[image] = attended
        part[...] = dot(attended, out_w_ref[...])
        mine[image] = part[:, my_cols]
        core_to[image] = part[:, their_cols].astype(bf16)

    def core_copy(image):
        return remote(core_to.at[image], core_from.at[image], core_s.at[image], core_r.at[image], core_dev)

    def x_copy(image):
        return remote(x_to.at[image], x_from.at[image], x_s.at[image], x_r.at[image], x_dev)

    def total_copy(image):
        return remote(total_to.at[image], total_from.at[image], tot_s.at[image], tot_r.at[image], core_dev)

    def h_block(side, image, core):
        return h_all.at[aligned(side * rows + image * PITCH, PITCH), lanes_at(core * wide, wide)]

    def y_copy(image):
        return remote(h_block(0, image, core_at), h_block(1, image, core_at), y_s.at[image], y_r.at[image], y_dev)

    def relay_copy(image):
        ref = h_block(1, image, core_at)
        return remote(ref, ref, rel_s.at[image], rel_r.at[image], core_dev)

    def relay_arriving(image):
        ref = h_block(1, image, other)
        return remote(ref, ref, rel_s.at[image], rel_r.at[image], core_dev)

    attend_outs = ((tok_ref, tok_out), (q_all, q_ref), (k_all, k_ref), (v_all, v_ref), (att_all, att_ref), (lse_all, lse_ref))

    def out_copies(image):
        copies = [
            pltpu.make_async_copy(kept.at[image], out.at[image], out_sem.at[n, image])
            for n, (kept, out) in enumerate(attend_outs)
        ]
        at = aligned(image * PITCH, PITCH)
        return copies, [
            pltpu.make_async_copy(resid_all.at[image], resid_ref.at[at, :], out_sem.at[6, image]),
            pltpu.make_async_copy(h_all.at[at, :], h_out.at[at, :], out_sem.at[7, image]),
        ]

    def other_copy(image):
        at = aligned(rows + image * PITCH, PITCH)
        return pltpu.make_async_copy(h_all.at[at, :], h_out.at[at, :], out_sem.at[8, image])

    def stage(tick, lag, run):
        image = tick - lag

        @pl.when((image >= 0) & (image < images))
        def _():
            run(image)

    def run_attend(image):
        attend(image)
        core_copy(image).start()
        for copy in out_copies(image)[0]:
            copy.start()

    def run_x(image):
        core_copy(image).wait_recv()
        x_to[image] = (mine[image] + core_from[image].astype(f32)).astype(bf16)
        x_copy(image).start()

    def run_total(image):
        x_copy(image).wait_recv()
        total_to[image] = (x_to[image].astype(f32) + x_from[image].astype(f32)).astype(bf16)
        total_copy(image).start()

    def run_norm(image):
        total_copy(image).wait_recv()
        part[:, my_cols] = total_to[image].astype(f32)
        part[:, their_cols] = total_from[image].astype(f32)
        resid = tok_ref[image].astype(f32) + part[...]
        resid_all[image] = resid
        normed, _ = norm_stats(resid)
        h_all[aligned(image * PITCH, PITCH), :] = (normed * gain2 + shift2).astype(bf16)
        y_copy(image).start()
        for copy in out_copies(image)[1]:
            copy.start()

    def run_relay(image):
        y_copy(image).wait_recv()
        relay_copy(image).start()

    def run_end(image):
        relay_arriving(image).wait_recv()
        other_copy(image).start()

    def cot_step_one():
        cot_x_in.wait_recv()
        cot_share[0].start()

        relay_y.start()

    def cot_step_two():
        cot_y_in.wait_recv()
        cot_share[1].start()

    def weights_step_one():
        pass_hops(0, 1)
        for copy in near_copies:
            copy.start()

    def cot_step_three():
        kept_y.wait_recv()
        kept_share.start()
        relay_in.wait_recv()
        cot_share[2].start()

    outs = [
        pltpu.make_async_copy(cot_all, cot_out, cot_sem.at[0]),
        pltpu.make_async_copy(kept_all, kept_out, cot_sem.at[1]),
        pltpu.make_async_copy(router_ref, router_out, cot_sem.at[2]),
    ]

    def ready_own():
        cot_share_in[0].wait_recv()
        for copy in (*own_copies, *near_copies):
            copy.wait()

    def ready_other():
        for copy in (cot_share_in[1], cot_share_in[2], kept_share_in):
            copy.wait_recv()
        for copy in outs:
            copy.start()

    def block_copies(number, place):
        at = aligned(number * BLOCK, BLOCK)
        pairs = ((mixed_slots, mixed_out), (grad_h_slots, grad_h_out), (gate_slots, gate_out))
        return [
            pltpu.make_async_copy(slots.at[place], out.at[at, :], block_sem.at[n, place])
            for n, (slots, out) in enumerate(pairs)
        ]

    def run_block(number, turn):
        at = aligned(number * BLOCK, BLOCK)
        h_rows, cot_rows = h_all[at, :], cot_all[at, :]
        up, down = up_vm[...], down_vm[...]
        hidden_rows, grad_pre, _, grad_gate = expert_math(
            h_rows, cot_rows, kept_all[at, :].astype(f32), router_ref[...], up, down, z_at // 2, experts
        )

        place = turn % 2

        @pl.when(turn >= 2)
        def _():
            for copy in block_copies(number, place):
                copy.wait()

        gate_slots[place] = grad_gate
        mixed_slots[place] = dot(hidden_rows, down).astype(bf16)
        grad_h_slots[place] = dot(grad_pre, up, ((1,), (1,))).astype(bf16)
        for copy in block_copies(number, place):
            copy.start()
        up_sum[...] += dot(h_rows.T, grad_pre)
        down_sum[...] += dot(cot_rows.T, hidden_rows)

    up_sum[...] = jnp.zeros_like(up_sum)
    down_sum[...] = jnp.zeros_like(down_sum)

    def take_tokens(number):
        first = number * SEQ // 16 * 16
        skip = number * SEQ - first
        taken = min(224, images * SEQ - first)
        rows_in = tok_raw[first : first + taken, :].astype(f32)[skip : skip + SEQ]
        padded = jnp.concatenate([rows_in, jnp.zeros((PITCH - SEQ, rows_in.shape[1]), f32)], axis=0)
        tok_ref[number] = padded.astype(bf16)

    def first_ticks(tick, _):
        for number in range(images):
            pl.when(tick == number)(partial(take_tokens, number))

        stage(tick, 0, run_attend)
        stage(tick, 1, run_x)
        return 0

    for copy in loads[2:]:
        copy.wait()
    lax.fori_loop(0, images + 1, first_ticks, 0)
    pairs = images // 2

    def both(first, *runs):
        for run in runs:
            run(first)
            run(first + 1)

    pass_hops(0, 0)
    cot_step_one()
    both(0, run_total, run_norm)
    cot_step_two()
    weights_step_one()
    ready_own()

    def per_turn(turn, _):
        @pl.when((turn <= 1) | (turn == 3))
        def _():
            both(jnp.where(turn == 3, 6, 2 * turn + 2), run_total, run_norm)

        @pl.when((turn >= 2) & (turn < pairs + 2))
        def _():
            both(2 * turn - 4, run_relay)

        @pl.when(turn == 2)
        def _():
            pass_hops(1, 0)
            cot_step_three()

        @pl.when(turn == pairs)
        def _():
            pass_hops(1, 1)
            ready_other()

        @pl.when(turn >= pairs)
        def _():
            both(2 * (turn - pairs), run_end)

        run_block(turn, turn)
        return 0

    lax.fori_loop(0, 2 * pairs, per_turn, 0)
    grad_up_vm[...] = up_sum[...].astype(bf16)
    grad_down_vm[...] = down_sum[...].astype(bf16)
    grad_copies = [
        pltpu.make_async_copy(grad_up_vm, grad_up_out, grad_sem.at[0]),
        pltpu.make_async_copy(grad_down_vm, grad_down_out, grad_sem.at[1]),
    ]
    for copy in grad_copies:
        copy.start()
    for copy in (swap, kept_y, kept_share, cot_x, cot_y, *cot_share):
        copy.wait_send()

    relay_y.wait_send()

    def drain(image, _):
        for copy in (core_copy, x_copy, total_copy, y_copy, relay_copy):
            copy(image).wait_send()
        first, second = out_copies(image)
        for copy in (*first, *second, other_copy(image)):
            copy.wait()
        return 0

    lax.fori_loop(0, images, drain, 0)
    for place in range(2):
        for copy in block_copies(0, place):
            copy.wait()

    await_hops(2, 0)
    await_hops(2, 1)
    for step in range(3):
        for way in range(2):

            @pl.when(hop_goes(step, way))
            def _():
                for copy in hop(step, way):
                    copy.wait_send()

    for copy in (*grad_copies, *outs):
        copy.wait()


def run_forward(tok_raw, gain1, shift1, gain2, shift2, qkv_w, out_w, up, down, router, cot, kept, experts):
    images = tok_raw.shape[0] // SEQ
    rows = images * PITCH
    features = tok_raw.shape[1]
    share = out_w.shape[0]
    heads = share // HD
    hidden = up.shape[1]
    wide = features // 2
    vmem = pl.BlockSpec(memory_space=pltpu.VMEM)
    anywhere = pl.BlockSpec(memory_space=pl.ANY)
    shape = jax.ShapeDtypeStruct
    block = (images, PITCH, wide)
    dma = pltpu.SemaphoreType.DMA
    return pl.pallas_call(
        partial(forward_kernel, images=images, heads=heads, experts=experts),
        out_shape=[
            shape((images, PITCH, share), bf16),
            shape((images, PITCH, share), bf16),
            shape((images, PITCH, share), bf16),
            shape((images, PITCH, share), bf16),
            shape((images, PITCH, 128), f32),
            shape((rows, features), f32),
            shape((2 * rows, features), bf16),
            shape((2 * rows, features), bf16),
            shape((2 * rows, 128), bf16),
            shape((2, features, 2 * hidden), bf16),
            shape((2, 2 * hidden, features), bf16),
            shape((2 * rows, features), bf16),
            shape((2 * rows, features), bf16),
            shape((2 * rows, 128), f32),
            shape((features, 2 * hidden), bf16),
            shape((features, 2 * hidden), bf16),
            shape((images, PITCH, features), bf16),
            shape((128, features), bf16),
        ],
        in_specs=[vmem] * 4 + [anywhere] * 2 + [vmem] + [anywhere] * 5,
        out_specs=[anywhere] * 18,
        scratch_shapes=[
            pltpu.VMEM((128, features), bf16),
            pltpu.VMEM(cot.shape, bf16),
            pltpu.VMEM(kept.shape, bf16),
            pltpu.VMEM(tok_raw.shape, bf16),
            pltpu.VMEM(qkv_w.shape, bf16),
            pltpu.VMEM(out_w.shape, bf16),
            pltpu.VMEM((images, PITCH, features), bf16),
            pltpu.VMEM((rows, share), bf16),
            pltpu.VMEM((features, 2 * hidden), bf16),
            pltpu.VMEM((2 * hidden, features), bf16),
            *[pltpu.VMEM((features, 2 * hidden), f32)] * 2,
            *[pltpu.VMEM((2, BLOCK, features), bf16)] * 2,
            pltpu.VMEM((2, BLOCK, 128), f32),
            *[pltpu.VMEM((features, 2 * hidden), bf16)] * 2,
            *[pltpu.VMEM((images, PITCH, share), bf16)] * 4,
            pltpu.VMEM((images, PITCH, 128), f32),
            pltpu.VMEM((images, PITCH, features), f32),
            pltpu.VMEM((2 * rows, features), bf16),
            pltpu.VMEM((2 * rows, features), bf16),
            pltpu.VMEM((2 * rows, 128), bf16),
            pltpu.VMEM((PITCH, features), f32),
            pltpu.VMEM(block, f32),
            pltpu.VMEM(block, bf16),
            pltpu.VMEM(block, bf16),
            pltpu.VMEM(block, bf16),
            pltpu.VMEM(block, bf16),
            pltpu.VMEM(block, bf16),
            pltpu.VMEM(block, bf16),
            pltpu.VMEM((rows, share), bf16),
        ]
        + [dma((images,))] * 10
        + [dma((2, 3, 2))] * 2
        + [dma((9,))] * 2
        + [dma((5,)), dma((2,)), dma((2,)), dma((3, 2)), dma((2,)), dma((3,)), dma((9, images))],
        compiler_params=pltpu.CompilerParams(
            collective_id=1, has_side_effects=True, vmem_limit_bytes=63 << 20
        ),
    )(gain1, shift1, gain2, shift2, up, down, router, cot, kept, tok_raw, qkv_w, out_w)


def turn_is_other(turn):
    return (turn == 0) | ((turn % 2 == 1) & (turn < 7))


def turn_block(turn):
    own = jnp.where(turn == 7, 3, turn // 2 - 1)
    return jnp.where(turn_is_other(turn), 4 + (turn + 1) // 2, own)


def second_pair_kernel(
    h_ref,
    cot_ref,
    kept_ref,
    router_ref,
    mixed_first,
    grad_h_first,
    gate_first,
    up_all,
    down_all,
    up_first,
    down_first,
    mixed_ref,
    grad_router_ref,
    grad_up_out,
    grad_down_out,
    grad_h_out,
    up_pair,
    down_pair,
    line_first,
    up_vm,
    down_vm,
    grad_up_ref,
    grad_down_ref,
    up_sum,
    down_sum,
    router_sum,
    ring,
    from_core,
    from_y,
    from_x,
    load,
    core_s,
    core_r,
    y_s,
    y_r,
    x_s,
    x_r,
    tot_s,
    tot_r,
    store,
    pair_s,
    pair_r,
    line_s,
    line_r,
    *,
    experts,
    steps,
):
    turn = pl.program_id(0)
    expert_at = lax.axis_index("expert")
    tensor_at = lax.axis_index("tensor")
    z_at, y_at = expert_at // 2, expert_at % 2
    x_at, core_at = tensor_at // 2, tensor_at % 2
    hidden = up_pair.shape[1]
    wide = ring.shape[3]
    core_dev = (expert_at, tensor_at + 1 - 2 * core_at)
    x_dev = (expert_at, tensor_at + 2 - 4 * x_at)
    y_dev = (expert_at + 1 - 2 * y_at, tensor_at)
    my_cols = lanes_at(core_at * wide, wide)

    def remote(src, dst, send, recv, device):
        return pltpu.make_async_remote_copy(
            src_ref=src, dst_ref=dst, send_sem=send, recv_sem=recv, device_id=device, device_id_type=MESH
        )

    def core_copy(number):
        return remote(ring.at[number % 2, 1 - core_at], from_core.at[number], core_s.at[number], core_r.at[number], core_dev)

    def y_copy(number, place):
        return remote(from_core.at[number], from_y.at[place], y_s.at[place], y_r.at[place], y_dev)

    def x_copy(number, place):
        return remote(from_core.at[number], from_x.at[place], x_s.at[place], x_r.at[place], x_dev)

    def out_rows(place):
        return grad_h_out.at[aligned(place * BLOCK, BLOCK), my_cols]

    def total_copy(place):
        return remote(from_x.at[place], out_rows(place), tot_s.at[place], tot_r.at[place], core_dev)

    def store_copy(place):
        return pltpu.make_async_copy(from_x.at[place], out_rows(place), store.at[place])

    def own_turn(place):
        return jnp.where(place == 3, 7, 2 * place + 2)

    def other_turn(place):
        return jnp.where(place == 0, 0, 2 * place - 1)

    def pass_other(number):
        core_copy(number).wait_recv()
        from_core[number] = from_core[number] + ring[number % 2, core_at]
        y_copy(number, (number + 1) // 2).start()

    def pass_own(number, place):
        core_copy(number).wait_recv()
        y_copy(number, place).wait_recv()
        total = from_core[number].astype(f32) + ring[number % 2, core_at].astype(f32) + from_y[place].astype(f32)
        from_core[number] = total.astype(bf16)
        x_copy(number, place).start()

    def pass_total(place):
        number = own_turn(place)
        x_copy(number, place).wait_recv()
        from_x[place] = from_core[number] + from_x[place]
        total_copy(place).start()
        store_copy(place).start()

    z_dev = (jnp.where(z_at % 2 == 0, expert_at + 2, expert_at - 2), tensor_at)
    pair_lanes = lanes_at((1 - z_at % 2) * hidden, hidden)
    pair_copies = [
        remote(source.at[:, pair_lanes], target, pair_s.at[number], pair_r.at[number], z_dev)
        for number, (source, target) in enumerate(((up_first, up_pair), (down_first, down_pair)))
    ]

    far_lanes = lanes_at(jnp.where(z_at == 0, 1, 0) * hidden, hidden)
    line_copy = remote(grad_up_ref.at[:, far_lanes], line_first, line_s.at[0], line_r.at[0], z_dev)
    is_outer = (z_at == 0) | (z_at == lax.axis_size("expert") // 2 - 1)

    grad_copies = [
        pltpu.make_async_copy(grad_up_ref, grad_up_out, load.at[2]),
        pltpu.make_async_copy(grad_down_ref, grad_down_out, load.at[3]),
    ]

    @pl.when(turn == 0)
    def _():
        whole = [
            pltpu.make_async_copy(up_all.at[1], up_vm, load.at[0]),
            pltpu.make_async_copy(down_all.at[1], down_vm, load.at[1]),
        ]
        for copy in whole:
            copy.start()
        greet([(True, core_dev), (True, x_dev), (True, y_dev), (True, z_dev)])
        for copy in pair_copies:
            copy.start()
        up_sum[...] = jnp.zeros_like(up_sum)
        down_sum[...] = jnp.zeros_like(down_sum)
        router_sum[...] = jnp.zeros_like(router_sum)
        for copy in whole:
            copy.wait()

    h_rows, cot_rows = h_ref[...], cot_ref[...]
    up, down, router = up_vm[...], down_vm[...], router_ref[...]
    kept = kept_ref[...].astype(f32)
    hidden_rows, grad_pre, probs, grad_gate = expert_math(
        h_rows, cot_rows, kept, router, up, down, 1 - z_at // 2, experts
    )
    grad_gate = kept * (grad_gate + gate_first[...])
    grad_logits = (probs * (grad_gate - jnp.sum(probs * grad_gate, axis=1, keepdims=True))).astype(bf16)

    before = turn - 1

    @pl.when((turn >= 1) & turn_is_other(before))
    def _():
        pass_other(before)

    @pl.when((turn == 5) | (turn == 7))
    def _():
        pass_total((turn - 5) // 2)

    @pl.when((turn == 3) | (turn == 5) | (turn == 7))
    def _():
        pass_own(before, (turn - 3) // 2)


    @pl.when(turn >= 2)
    def _():
        core_copy(turn - 2).wait_send()

    grad_h = (
        grad_h_first[...].astype(f32) + dot(grad_pre, up, ((1,), (1,))) + dot(grad_logits, router)
    ).astype(bf16)
    ring[turn % 2, 0] = grad_h[:, :wide]
    ring[turn % 2, 1] = grad_h[:, wide:]
    core_copy(turn).start()
    mixed_ref[...] = (mixed_first[...].astype(f32) + dot(hidden_rows, down)).astype(bf16)
    h_turned = h_rows.T
    up_sum[...] += dot(h_turned, grad_pre)
    router_sum[...] += dot(h_turned, grad_logits)
    down_sum[...] += dot(cot_rows.T, hidden_rows)

    @pl.when(turn == steps - 1)
    def _():
        grad_up_ref[...] = up_sum[...].astype(bf16)
        grad_copies[0].start()

        @pl.when(is_outer)
        def _():
            line_copy.start()

        pass_own(7, 3)
        pass_total(2)
        grad_down_ref[...] = down_sum[...].astype(bf16)
        grad_copies[1].start()
        grad_router_ref[...] = router_sum[...].T[:8]
        pass_total(3)
        for copy in (*pair_copies, *grad_copies):
            copy.wait()

        @pl.when(is_outer)
        def _():
            line_copy.wait_send()

        @pl.when(jnp.logical_not(is_outer))
        def _():
            line_copy.wait_recv()

        for number in (6, 7):
            core_copy(number).wait_send()
        for place in range(4):
            y_copy(other_turn(place), place).wait_send()
            x_copy(own_turn(place), place).wait_send()
            total_copy(place).wait_send()
            total_copy(place).wait_recv()
            store_copy(place).wait()


def run_second_pair(
    h_rows,
    cot_rows,
    kept,
    router,
    mixed_first,
    grad_h_first,
    gate_first,
    up,
    down,
    up_first,
    down_first,
    experts,
):
    rows, features = h_rows.shape
    width = up.shape[2]
    steps = rows // BLOCK
    half = (BLOCK, features // 2)
    anywhere = pl.BlockSpec(memory_space=pl.ANY)
    shape = jax.ShapeDtypeStruct
    dma = pltpu.SemaphoreType.DMA

    def by_step(lanes):
        return pl.BlockSpec((BLOCK, lanes), lambda n: (turn_block(n), 0))

    def whole(*dims):
        return pl.BlockSpec(dims, lambda n: (0,) * len(dims))

    return pl.pallas_call(
        partial(second_pair_kernel, experts=experts, steps=steps),
        grid=(steps,),
        out_shape=[
            shape((rows, features), bf16),
            shape((8, features), f32),
            shape((features, width), bf16),
            shape((features, width), bf16),
            shape((rows // 2, features), bf16),
            shape((features, width // 2), bf16),
            shape((features, width // 2), bf16),
            shape((features, width // 2), bf16),
        ],
        in_specs=[
            by_step(features),
            by_step(features),
            by_step(128),
            whole(128, features),
            by_step(features),
            by_step(features),
            by_step(128),
        ]
        + [anywhere] * 4,
        out_specs=[by_step(features), whole(8, features)] + [anywhere] * 6,
        scratch_shapes=[
            pltpu.VMEM((features, width), bf16),
            pltpu.VMEM((width, features), bf16),
            *[pltpu.VMEM((features, width), bf16)] * 2,
            pltpu.VMEM((features, width), f32),
            pltpu.VMEM((features, width), f32),
            pltpu.VMEM((features, 128), f32),
            pltpu.VMEM((2, 2, *half), bf16),
            pltpu.VMEM((8, *half), bf16),
            pltpu.VMEM((4, *half), bf16),
            pltpu.VMEM((4, *half), bf16),
            dma((4,)),
        ]
        + [dma((8,))] * 2
        + [dma((4,))] * 7
        + [dma((2,))] * 2
        + [dma((1,))] * 2,
        compiler_params=pltpu.CompilerParams(
            collective_id=4, has_side_effects=True, vmem_limit_bytes=60 << 20
        ),
    )(h_rows, cot_rows, kept, router, mixed_first, grad_h_first, gate_first, up, down, up_first, down_first)


def backward_kernel(
    gain1_ref,
    shift1_ref,
    gain2_ref,
    grad_router_ref,
    qkv_hbm,
    out_w_hbm,
    tok_hbm,
    q_hbm,
    k_hbm,
    v_hbm,
    att_hbm,
    lse_hbm,
    grad_h_hbm,
    resid_ref,
    cot_ref,
    mixed_ref,
    up_second,
    down_second,
    line_first,
    line_out,
    tokens_out,
    weights_out,
    sums_out,
    mixed_out,
    qkv_ref,
    out_w_ref,
    tok_ref,
    q_ref,
    k_ref,
    v_ref,
    att_ref,
    lse_ref,
    grad_h_ref,
    rows_kept,
    cot_rows,
    m_mine,
    m_core,
    m_y,
    m_x,
    m_out,
    m_resid,
    far_vm,
    one_mine,
    one_to,
    one_core,
    one_x,
    one_total,
    line,
    weight_sum,
    weight_half,
    shared,
    shared_y,
    shared_line,
    shared_all,
    route_core,
    route_x,
    late_mine,
    late_y,
    late_z,
    sums_all,
    tokens_low,
    whole,
    mc_s,
    mc_r,
    my_s,
    my_r,
    mx_s,
    mx_r,
    mq_s,
    mq_r,
    m_store,
    oc_s,
    oc_r,
    ox_s,
    ox_r,
    ot_s,
    ot_r,
    l_s,
    l_r,
    sy_s,
    sy_r,
    sl_s,
    sl_r,
    sg_s,
    sg_r,
    sz_s,
    sz_r,
    r_s,
    r_r,
    late_s,
    late_r,
    load,
    image_load,
    own_sem,
    weight_store,
    store,
    *,
    images,
    heads,
):
    expert_at = lax.axis_index("expert")
    tensor_at = lax.axis_index("tensor")
    z_at, y_at = expert_at // 2, expert_at % 2
    z_last = lax.axis_size("expert") // 2 - 1
    x_at, core_at = tensor_at // 2, tensor_at % 2
    other = 1 - core_at
    rows = images * PITCH
    features = tok_hbm.shape[2]
    wide = features // 2
    share = out_w_ref.shape[0]
    hidden = line.shape[3]
    core_dev = (expert_at, tensor_at + 1 - 2 * core_at)
    x_dev = (expert_at, tensor_at + 2 - 4 * x_at)
    y_dev = (expert_at + 1 - 2 * y_at, tensor_at)
    z_devs = [(expert_at + 2, tensor_at), (expert_at - 2, tensor_at)]
    planes = z_last + 1
    z_others = [((z_at + hop) % planes * 2 + y_at, tensor_at) for hop in (1, 2, 3)]
    greet([(True, device) for device in (core_dev, x_dev, y_dev, *z_others)])
    my_cols = lanes_at(core_at * wide, wide)
    their_cols = lanes_at(other * wide, wide)

    def remote(src, dst, send, recv, device):
        return pltpu.make_async_remote_copy(
            src_ref=src, dst_ref=dst, send_sem=send, recv_sem=recv, device_id=device, device_id_type=MESH
        )

    def at_image(image):
        return aligned(image * PITCH, PITCH)

    def place(way):
        return z_at if way == 0 else z_last - z_at

    def far_lanes(way, piece):
        expert = z_last - piece // 2 if way == 0 else piece // 2
        return pl.ds(expert % 2 * hidden, hidden)

    def line_copy(source, way, piece):
        return remote(source, line.at[way, piece], l_s.at[way, piece], l_r.at[way, piece], z_devs[way])

    def line_copy_on(way, piece):
        return line_copy(line.at[way, piece], way, piece)

    def line_start():
        for way in range(2):

            @pl.when(place(way) == 0)
            def _():
                for piece in range(1, 4):
                    source = (up_second, down_second)[piece % 2]
                    line_copy(source.at[:, far_lanes(way, piece)], way, piece).start()

    def line_add(piece):
        for way in range(2):

            @pl.when(place(way) == 1)
            def _():
                if piece > 0:
                    line_copy_on(way, piece).wait_recv()
                lanes = far_lanes(way, piece)

                def add(part, _):
                    at_rows = aligned(part * 96, 96)
                    total = line[way, piece, at_rows, :].astype(f32) + far_vm[piece % 2, at_rows, lanes].astype(f32)
                    line[way, piece, at_rows, :] = total.astype(bf16)
                    return 0

                lax.fori_loop(0, features // 96, add, 0)
                line_copy_on(way, piece).start()

    part_height = line.shape[2] // 4

    def line_part_copy(way, part):
        ref = line.at[way, 3, pl.ds(part * part_height, part_height)]
        return remote(ref, ref, l_s.at[way, 3 + part], l_r.at[way, 3 + part], z_devs[way])

    def line_part(part):
        for way in range(2):

            @pl.when(place(way) == 1)
            def _():
                if part == 0:
                    line_copy_on(way, 3).wait_recv()
                lanes = far_lanes(way, 3)
                for piece in range(2):
                    at_rows = pl.ds(part * part_height + piece * part_height // 2, part_height // 2)
                    total = line[way, 3, at_rows, :].astype(f32) + far_vm[1, at_rows, lanes].astype(f32)
                    line[way, 3, at_rows, :] = total.astype(bf16)
                line_part_copy(way, part).start()

    def line_pass(piece):
        for way in range(2):

            @pl.when(place(way) == 2)
            def _():
                line_copy_on(way, piece).wait_recv()
                line_copy_on(way, piece).start()

    line_start()
    later = [
        pltpu.make_async_copy((up_second, down_second)[number], far_vm.at[number], own_sem.at[number])
        for number in range(2)
    ]
    is_inner = (z_at == 1) | (z_at == z_last - 1)
    first_copy = pltpu.make_async_copy(line_first, line.at[jnp.where(z_at == 1, 0, 1), 0], own_sem.at[2])

    @pl.when(is_inner)
    def _():
        first_copy.start()

    for copy in later:
        copy.start()

    part_count = m_y.shape[0]
    part_rows_m = rows // part_count

    def m_rows(side, part):
        return aligned(side * rows + part * part_rows_m, part_rows_m)

    def m_core_copy(side, part):
        at = m_rows(side, part)
        return remote(mixed_ref.at[at, their_cols], m_core.at[at, :], mc_s.at[side, part], mc_r.at[side, part], core_dev)

    for part in range(part_count):
        m_core_copy(1, part).start()
    for part in range(part_count):
        m_core_copy(0, part).start()
    m_loads = [
        pltpu.make_async_copy(mixed_ref.at[pl.ds(side * rows, rows), my_cols], m_mine.at[pl.ds(side * rows, rows), :], load.at[side])
        for side in range(2)
    ]

    def image_loads(image):
        at = at_image(image)
        by_image = ((tok_hbm, tok_ref), (q_hbm, q_ref), (k_hbm, k_ref), (v_hbm, v_ref), (att_hbm, att_ref), (lse_hbm, lse_ref))
        by_row = ((grad_h_hbm, grad_h_ref), (resid_ref, rows_kept), (cot_ref, cot_rows))
        pairs = [(source.at[image], target.at[image]) for source, target in by_image]
        pairs += [(source.at[at, :], target.at[at, :]) for source, target in by_row]
        return [pltpu.make_async_copy(source, target, image_load.at[n, image]) for n, (source, target) in enumerate(pairs)]

    def start_loads(image, _):
        for copy in image_loads(image):
            copy.start()
        return 0

    weight_loads = [
        pltpu.make_async_copy(qkv_hbm, qkv_ref, own_sem.at[3]),
        pltpu.make_async_copy(out_w_hbm, out_w_ref, own_sem.at[4]),
    ]
    for copy in weight_loads:
        copy.start()
    start_loads(0, 0)
    m_loads[1].start()
    lax.fori_loop(1, images, start_loads, 0)
    m_loads[0].start()
    route_one = remote(grad_router_ref, route_core, r_s.at[0], r_r.at[0], core_dev)
    route_one.start()

    weight_sum[...] = jnp.zeros_like(weight_sum)
    late_mine[...] = jnp.zeros_like(late_mine)

    def m_y_copy(part):
        return remote(m_core.at[m_rows(1, part), :], m_y.at[part], my_s.at[part], my_r.at[part], y_dev)

    def m_x_copy(part):
        return remote(m_core.at[m_rows(0, part), :], m_x.at[part], mx_s.at[part], mx_r.at[part], x_dev)

    def m_place(part):
        return mixed_out.at[aligned(part * part_rows_m, part_rows_m), :]

    def m_quarter_copy(part):
        return remote(m_out.at[part, other], m_place(part), mq_s.at[part], mq_r.at[part], core_dev)

    def m_store_copy(part):
        return pltpu.make_async_copy(m_out.at[part, core_at], m_place(part), m_store.at[part])

    def m_resid_copy(part):
        at = aligned(part * part_rows_m, part_rows_m)
        return pltpu.make_async_copy(resid_ref.at[at, lanes_at(x_at * wide, wide)], m_resid, load.at[3])

    keeps = x_at == core_at

    def run_m_y(part):
        m_core_copy(1, part).wait_recv()
        at = m_rows(1, part)
        m_core[at, :] = (m_core[at, :].astype(f32) + m_mine[at, :].astype(f32)).astype(bf16)
        m_y_copy(part).start()

    def run_m_x(part):
        if isinstance(part, int) and part == 0:
            m_loads[0].wait()
        m_core_copy(0, part).wait_recv()
        m_y_copy(part).wait_recv()
        at = m_rows(0, part)
        total = m_core[at, :].astype(f32) + m_mine[at, :].astype(f32) + m_y[part].astype(f32)
        m_core[at, :] = total.astype(bf16)

        @pl.when(jnp.logical_not(keeps))
        def _():
            m_x_copy(part).start()

    def run_m_out(part):
        @pl.when(keeps)
        def _():
            m_resid_copy(part).start()
            m_x_copy(part).wait_recv()
            m_resid_copy(part).wait()
            total = m_core[m_rows(0, part), :].astype(f32) + m_x[part].astype(f32)
            mixed = (m_resid[...] + total).astype(bf16)
            m_out[part, 0] = mixed[:, : wide // 2]
            m_out[part, 1] = mixed[:, wide // 2 :]
            m_quarter_copy(part).start()
            m_store_copy(part).start()

    later[0].wait()
    later[1].wait()

    @pl.when(is_inner)
    def _():
        first_copy.wait()

    line_add(0)
    m_loads[1].wait()
    for part in range(part_count):
        run_m_y(part)
    route_one.wait_recv()
    route_core[...] += grad_router_ref[...]
    route_two = remote(route_core, route_x, r_s.at[1], r_r.at[1], x_dev)
    route_two.start()

    def one_core_copy(image):
        return remote(one_to.at[image], one_core.at[image], oc_s.at[image], oc_r.at[image], core_dev)

    def one_x_copy(image):
        return remote(one_core.at[image], one_x.at[image], ox_s.at[image], ox_r.at[image], x_dev)

    def one_total_copy(image):
        return remote(one_x.at[image], one_total.at[image], ot_s.at[image], ot_r.at[image], core_dev)

    store_copy = pltpu.make_async_copy(tokens_low, tokens_out, store.at[0])

    lane = lax.broadcasted_iota(jnp.int32, (PITCH, 2 * HD), 1)
    key_mask = lax.broadcasted_iota(jnp.int32, (PITCH, PITCH), 1) < SEQ
    gain1, shift1, gain2 = (ref[...].reshape(1, features) for ref in (gain1_ref, shift1_ref, gain2_ref))

    def norm_back(grad, gain, normed, inverse):
        scaled = grad * gain
        mean = jnp.mean(scaled, axis=1, keepdims=True)
        along = jnp.mean(scaled * normed, axis=1, keepdims=True)
        return (scaled - mean - normed * along) * inverse

    def add_sums(sums, row, grad, normed):
        sums[row : row + 1, :] += jnp.sum(grad * normed, axis=0, keepdims=True)
        sums[row + 1 : row + 2, :] += jnp.sum(grad, axis=0, keepdims=True)

    def run_attention(image):
        for copy in image_loads(image):
            copy.wait()
        at = at_image(image)
        grad_h = grad_h_ref[at, :].astype(f32)
        normed, inverse = norm_stats(rows_kept[at, :])
        add_sums(late_mine, 2, grad_h, normed)
        grad_resid = cot_rows[at, :].astype(f32) + norm_back(grad_h, gain2, normed, inverse)
        rows_kept[at, :] = grad_resid
        grad_branch = grad_resid.astype(bf16)
        token_normed, _ = norm_stats(tok_ref[image].astype(f32))
        h_one = (token_normed * gain1 + shift1).astype(bf16)
        queries, keys, values, attended = q_ref[image], k_ref[image], v_ref[image], att_ref[image]
        lse = lse_ref[image]
        grad_attended = dot(grad_branch, out_w_ref[...], ((1,), (1,))).astype(bf16)
        grads = [[], [], []]
        for head in range(heads):
            first = head // 2 * 2 * HD
            last = min(first + 2 * HD, heads * HD)
            parts = [whose[:, first:last] for whose in (queries, keys, values, grad_attended)]
            if last - first == 2 * HD:
                own = head_mask(lane, head)
                q_own, k_own, _, g_own = (jnp.where(own, part, jnp.zeros_like(part)) for part in parts)
            else:
                q_own, k_own, _, g_own = parts
            scores = dot(q_own, parts[1], ((1,), (1,))) * (HD**-0.5)
            probs = jnp.where(key_mask, jnp.exp(scores - lse[:, head : head + 1]), 0.0)
            back = dot(g_own, parts[2], ((1,), (1,)))
            product = probs * back
            grad_scores = (product - probs * jnp.sum(product, axis=1, keepdims=True)).astype(bf16)
            pieces = (
                dot(grad_scores, k_own) * (HD**-0.5),
                dot(grad_scores, q_own, ((0,), (0,))) * (HD**-0.5),
                dot(probs.astype(bf16), g_own, ((0,), (0,))),
            )
            for which in range(3):
                if head % 2 == 0:
                    grads[which].append(pieces[which])
                else:
                    grads[which][-1] += pieces[which]
        grad_rows = [jnp.concatenate(grads[which], axis=1).astype(bf16) for which in range(3)]
        grad_one = 0.0
        for which in range(3):
            weight_sum[which * share : (which + 1) * share, :] += dot(grad_rows[which].T, h_one)
            grad_one += dot(grad_rows[which], qkv_ref[which])
        weight_sum[3 * share : 4 * share, :] += dot(attended.T, grad_branch)
        whole[...] = grad_one
        one_mine[image] = whole[:, my_cols].astype(bf16)
        one_to[image] = whole[:, their_cols].astype(bf16)
        one_core_copy(image).start()

    def run_one_x(image):
        one_core_copy(image).wait_recv()
        one_core[image] = (one_core[image].astype(f32) + one_mine[image].astype(f32)).astype(bf16)
        one_x_copy(image).start()

    def run_one_total(image):
        one_x_copy(image).wait_recv()
        one_x[image] = (one_core[image].astype(f32) + one_x[image].astype(f32)).astype(bf16)
        one_total_copy(image).start()

    def run_tokens(image):
        one_total_copy(image).wait_recv()
        whole[:, my_cols] = one_x[image].astype(f32)
        whole[:, their_cols] = one_total[image].astype(f32)
        grad_one = whole[...]
        at = at_image(image)
        normed, inverse = norm_stats(tok_ref[image].astype(f32))
        add_sums(late_mine, 0, grad_one, normed)
        total = rows_kept[at, :] + norm_back(grad_one, gain1, normed, inverse)
        whole[...] = total
        for number in range(images):

            @pl.when(image == number)
            def _():
                rows_kept[pl.ds(number * SEQ, SEQ), :] = whole[pl.ds(0, SEQ), :]


    def stage(tick, lag, run):
        image = tick - lag

        @pl.when((image >= 0) & (image < images))
        def _():
            run(image)

    def at_tick(tick, when, run):
        @pl.when(tick == when)
        def _():
            run()

    def line_second():
        line_add(1)
        line_pass(0)

    def line_third():
        line_add(2)
        line_pass(1)

    def per_tick(tick, _):
        stage(tick, 0, run_attention)
        stage(tick, 1, run_one_x)
        stage(tick, 4, run_one_total)
        stage(tick, 5, run_tokens)
        at_tick(tick, 5, lambda: run_m_x(0))
        at_tick(tick, 3, line_second)
        at_tick(tick, 6, line_third)
        at_tick(tick, 7, lambda: run_m_x(1))
        return 0

    for copy in weight_loads:
        copy.wait()
    lax.fori_loop(0, images, per_tick, 0)

    part_rows = shared.shape[1]
    chunks = 2
    chunk_rows = part_rows // chunks
    quarter = chunk_rows // planes

    def cast(piece, _):
        for side in range(2):
            at_rows = aligned(piece * 96, 96)
            shared[side, at_rows, :] = weight_sum[aligned(side * part_rows + piece * 96, 96), :].astype(bf16)
        return 0

    lax.fori_loop(0, part_rows // 96, cast, 0)

    def y_piece(number):
        inner = jnp.where(z_at == 1, jnp.where(number < 2, z_last - number, number - 2), jnp.where(number < 2, number, 5 - number))
        return jnp.where(z_at == 0, z_last - number, jnp.where(z_at == z_last, number, inner))

    def quarter_at(chunk, piece):
        return aligned(chunk * chunk_rows + piece * quarter, quarter)

    def shared_y_copy(chunk, number):
        at_rows = quarter_at(chunk, y_piece(number))
        return remote(
            shared.at[1 - y_at, at_rows, :], shared_y.at[at_rows, :], sy_s.at[chunk, number], sy_r.at[chunk, number], y_dev
        )

    def take_y(chunk, number):
        shared_y_copy(chunk, number).wait_recv()
        at_rows = quarter_at(chunk, y_piece(number))
        weight_half[at_rows, :] = shared[y_at, at_rows, :].astype(f32) + shared_y[at_rows, :].astype(f32)

    def quarter_of(step, at, way):
        mirrored = z_last - step + at
        return mirrored if way == 0 else z_last - mirrored

    def small_copy(chunk, step, way):
        return remote(
            shared_line.at[chunk, way, 0, step],
            shared_line.at[chunk, way, 1, step],
            sl_s.at[chunk, way, step],
            sl_r.at[chunk, way, step],
            z_devs[way],
        )

    def sum_wait(chunk, step):
        for way in range(2):
            at = place(way)

            @pl.when((at > 0) & (at - 1 <= step))
            def _():
                small_copy(chunk, step, way).wait_recv()

    def sum_send(chunk, step):
        for way in range(2):
            at = place(way)

            @pl.when((at <= step) & (at < z_last))
            def _():
                at_rows = quarter_at(chunk, quarter_of(step, at, way))
                if step == 0:
                    shared_line[chunk, way, 0, step] = weight_half[at_rows, :].astype(bf16)
                else:
                    came = jnp.where(at > 0, shared_line[chunk, way, 1, step - 1].astype(f32), 0.0)
                    shared_line[chunk, way, 0, step] = (weight_half[at_rows, :] + came).astype(bf16)
                small_copy(chunk, step, way).start()

    def final_rows(chunk, side, piece):
        return shared_all.at[side, quarter_at(chunk, piece), :]

    def gather_z(chunk, step, way, piece):
        ref = final_rows(chunk, y_at, piece)
        return remote(ref, ref, sg_s.at[chunk, way, step], sg_r.at[chunk, way, step], z_devs[way])

    def gather_y(chunk, step, way, piece, side):
        ref = final_rows(chunk, side, piece)
        return remote(ref, ref, sz_s.at[chunk, way, step], sz_r.at[chunk, way, step], y_dev)

    def piece_out(step, way):
        return z_at - step if way == 0 else z_at + step

    def piece_in(step, way):
        return z_at - 1 - step if way == 0 else z_at + 1 + step

    def gather_send(chunk, step):
        for way in range(2):
            at = place(way)

            @pl.when((at >= step) & (at < z_last))
            def _():
                gather_z(chunk, step, way, piece_out(step, way)).start()

    def gather_take(chunk, step):
        for way in range(2):

            @pl.when(place(way) >= 1 + step)
            def _():
                gather_z(chunk, step, way, piece_in(step, way)).wait_recv()
                gather_y(chunk, step + 1, way, piece_in(step, way), y_at).start()

    def finish_sum(chunk):
        own_rows = quarter_at(chunk, z_at)
        from_below = jnp.where(z_at > 0, shared_line[chunk, 0, 1, 2].astype(f32), 0.0)
        from_above = jnp.where(z_at < z_last, shared_line[chunk, 1, 1, 2].astype(f32), 0.0)
        shared_all[y_at, own_rows, :] = (weight_half[own_rows, :] + from_below + from_above).astype(bf16)
        gather_y(chunk, 0, 0, z_at, y_at).start()

    late_y_copy = remote(late_mine, late_y, late_s.at[0], late_r.at[0], y_dev)

    def late_copy(number):
        ref = late_z.at[z_at]
        return remote(ref, ref, late_s.at[number + 1], late_r.at[number + 1], z_others[number])

    def meanwhile(place_in_order):
        if place_in_order == 0:
            run_one_x(images - 1)
            run_tokens(images - 5)
            run_one_total(images - 4)
            run_m_x(part_count - 2)
        if place_in_order == 1:
            run_m_x(part_count - 1)
            run_tokens(images - 4)
            run_one_total(images - 3)
        if place_in_order == 2:
            run_m_out(0)
            run_tokens(images - 3)
        if place_in_order == 3:
            line_part(0)
            run_one_total(images - 2)
            run_m_out(1)
            run_tokens(images - 2)
        if place_in_order == 4:
            line_part(1)
            run_one_total(images - 1)
            run_m_out(2)
        if place_in_order == 5:
            line_part(2)
            run_tokens(images - 1)
            route_two.wait_recv()
            late_mine[8:16, :] = route_core[...] + route_x[...]
            late_y_copy.start()
            tokens_low[...] = rows_kept[pl.ds(0, images * SEQ), :].astype(bf16)
            store_copy.start()
        if place_in_order == 6:
            line_part(3)
            run_m_out(3)
            late_y_copy.wait_recv()
            late_z[z_at] = late_mine[...] + late_y[...]
            for number in range(planes - 1):
                late_copy(number).start()

    for number in range(4):
        for chunk in range(chunks):
            shared_y_copy(chunk, number).start()
    meanwhile(0)
    for step in range(3):
        for chunk in range(chunks):
            if step > 0:
                sum_wait(chunk, step - 1)
            take_y(chunk, step)
            sum_send(chunk, step)
        if step == 2:
            for chunk in range(chunks):
                take_y(chunk, 3)
        meanwhile(1 + step)
    for chunk in range(chunks):
        sum_wait(chunk, 2)
        finish_sum(chunk)
        gather_send(chunk, 0)
    for step in range(3):
        meanwhile(4 + step)
        for chunk in range(chunks):
            gather_take(chunk, step)
            if step < 2:
                gather_send(chunk, step + 1)

    for way in range(2):

        @pl.when(place(way) == 2)
        def _():
            line_copy_on(way, 2).wait_recv()
            for part in range(4):
                line_part_copy(way, part).wait_recv()

        @pl.when(place(way) == z_last)
        def _():
            line_copy_on(way, 0).wait_recv()
            line_copy_on(way, 1).wait_recv()

    from_far = 1 - z_at // 2
    first_piece = jnp.where((z_at == 0) | (z_at == z_last), 0, 2)

    line_out_copies = [
        pltpu.make_async_copy(line.at[from_far, first_piece + n], line_out.at[n], weight_store.at[n]) for n in range(2)
    ]
    for copy in line_out_copies:
        copy.start()
    for chunk in range(chunks):
        gather_y(chunk, 0, 0, z_at, 1 - y_at).wait_recv()
        for step in range(3):
            for way in range(2):

                @pl.when(place(way) >= 1 + step)
                def _():
                    gather_y(chunk, step + 1, way, piece_in(step, way), 1 - y_at).wait_recv()

    for number in range(planes - 1):
        late_copy(number).wait_recv()
    late = late_z[0]
    for plane in range(1, planes):
        late += late_z[plane]
    sums_all[...] = late
    out_copies = [
        pltpu.make_async_copy(shared_all, weights_out, weight_store.at[2]),
        pltpu.make_async_copy(sums_all, sums_out, weight_store.at[3]),
    ]
    for copy in out_copies:
        copy.start()
    route_one.wait_send()
    route_two.wait_send()

    def drain(image, _):
        for copy in (one_core_copy, one_x_copy, one_total_copy):
            copy(image).wait_send()
        return 0

    lax.fori_loop(0, images, drain, 0)
    for part in range(part_count):
        m_core_copy(0, part).wait_send()
        m_core_copy(1, part).wait_send()
        m_y_copy(part).wait_send()

        @pl.when(keeps)
        def _():
            m_quarter_copy(part).wait_send()
            m_store_copy(part).wait()

        @pl.when(jnp.logical_not(keeps))
        def _():
            m_x_copy(part).wait_send()
            m_quarter_copy(part).wait_recv()

    for copy in (*line_out_copies, *out_copies, store_copy):
        copy.wait()
    late_y_copy.wait_send()
    for number in range(planes - 1):
        late_copy(number).wait_send()
    for way in range(2):

        @pl.when(place(way) == 0)
        def _():
            for piece in range(1, 4):
                line_copy_on(way, piece).wait_send()

        @pl.when(place(way) == 1)
        def _():
            for piece in range(3):
                line_copy_on(way, piece).wait_send()
            for part in range(4):
                line_part_copy(way, part).wait_send()

        @pl.when(place(way) == 2)
        def _():
            for piece in range(2):
                line_copy_on(way, piece).wait_send()

    for chunk in range(chunks):
        gather_y(chunk, 0, 0, z_at, y_at).wait_send()
        for number in range(4):
            shared_y_copy(chunk, number).wait_send()
        for step in range(3):
            for way in range(2):
                at = place(way)

                @pl.when((at <= step) & (at < z_last))
                def _():
                    small_copy(chunk, step, way).wait_send()

                @pl.when((at >= step) & (at < z_last))
                def _():
                    gather_z(chunk, step, way, piece_out(step, way)).wait_send()

                @pl.when(at >= 1 + step)
                def _():
                    gather_y(chunk, step + 1, way, piece_in(step, way), y_at).wait_send()


def run_backward(gain1, shift1, gain2, grad_router, qkv_w, out_w, tok, *streamed):
    images, _, features = tok.shape
    rows = images * PITCH
    share = out_w.shape[0]
    heads = share // HD
    hidden = streamed[-1].shape[1]
    wide = features // 2
    parts = 4
    vmem = pl.BlockSpec(memory_space=pltpu.VMEM)
    anywhere = pl.BlockSpec(memory_space=pl.ANY)
    shape = jax.ShapeDtypeStruct
    dma = pltpu.SemaphoreType.DMA
    block = (images, PITCH, wide)
    return pl.pallas_call(
        partial(backward_kernel, images=images, heads=heads),
        out_shape=[
            shape((2, features, hidden), bf16),
            shape((images * SEQ, features), bf16),
            shape((2, features // 2, features), bf16),
            shape((16, features), f32),
            shape((rows, wide // 2), bf16),
        ],
        in_specs=[vmem] * 4 + [anywhere] * (3 + len(streamed)),
        out_specs=[anywhere] * 5,
        scratch_shapes=[
            pltpu.VMEM(qkv_w.shape, bf16),
            pltpu.VMEM(out_w.shape, bf16),
            pltpu.VMEM((images, PITCH, features), bf16),
            *[pltpu.VMEM((images, PITCH, share), bf16)] * 4,
            pltpu.VMEM((images, PITCH, 128), f32),
            pltpu.VMEM((rows, features), bf16),
            pltpu.VMEM((rows, features), f32),
            pltpu.VMEM((rows, features), bf16),
            pltpu.VMEM((2 * rows, wide), bf16),
            pltpu.VMEM((2 * rows, wide), bf16),
            *[pltpu.VMEM((parts, rows // parts, wide), bf16)] * 2,
            pltpu.VMEM((parts, 2, rows // parts, wide // 2), bf16),
            pltpu.VMEM((rows // parts, wide), f32),
            pltpu.VMEM((2, features, 2 * hidden), bf16),
            *[pltpu.VMEM(block, bf16)] * 5,
            pltpu.VMEM((2, 4, features, hidden), bf16),
            pltpu.VMEM((features, features), f32),
            pltpu.VMEM((features // 2, features), f32),
            pltpu.VMEM((2, features // 2, features), bf16),
            pltpu.VMEM((features // 2, features), bf16),
            pltpu.VMEM((2, 2, 2, 3, features // 16, features), bf16),
            pltpu.VMEM((2, features // 2, features), bf16),
            *[pltpu.VMEM((8, features), f32)] * 2,
            *[pltpu.VMEM((16, features), f32)] * 2,
            pltpu.VMEM((4, 16, features), f32),
            pltpu.VMEM((16, features), f32),
            pltpu.VMEM((images * SEQ, features), bf16),
            pltpu.VMEM((PITCH, features), f32),
        ]
        + [dma((2, parts))] * 2
        + [dma((parts,))] * 7
        + [dma((images,))] * 6
        + [dma((2, 7))] * 2
        + [dma((2, 4))] * 2
        + [dma((2, 2, 3))] * 4
        + [dma((2, 2, 4))] * 2
        + [dma((2,))] * 2
        + [dma((4,))] * 2
        + [dma((4,)), dma((9, images)), dma((5,)), dma((4,)), dma((1,))],
        compiler_params=pltpu.CompilerParams(
            collective_id=2, has_side_effects=True, vmem_limit_bytes=63 << 20
        ),
    )(gain1, shift1, gain2, grad_router, qkv_w, out_w, tok, *streamed)


def last_kernel(
    side_ref, tokens_ref, weights_ref, up_first, up_pair, down_first, down_pair, line_ref, tokens_out, qkv_out, out_w_out, up_out, down_out
):
    share = out_w_out.shape[0]
    tokens_out[...] = tokens_ref[...].astype(f32)
    for which in range(3):
        qkv_out[which] = weights_ref[which * share : (which + 1) * share, :].astype(f32)
    out_w_out[...] = weights_ref[3 * share :, :].astype(f32)
    up_out[...] = up_first[...].astype(f32) + up_pair[...].astype(f32) + line_ref[0].astype(f32)
    down_out[...] = (down_first[...].astype(f32) + down_pair[...].astype(f32) + line_ref[1].astype(f32)).T


def run_last(side, tokens, weights, up_first, up_pair, down_first, down_pair, line, share):
    rows, features = tokens.shape
    hidden = up_pair.shape[1]
    shape = jax.ShapeDtypeStruct

    steps = features // 128
    height = -(-rows // (16 * steps)) * 16
    by_rows = pl.BlockSpec((height, features), lambda n, side: (n, 0))

    def lanes(height):
        return pl.BlockSpec((height, 128), lambda n, side: (0, n))

    own = pl.BlockSpec((128, hidden), lambda n, side: (n, side[0]))
    plain = pl.BlockSpec((128, hidden), lambda n, side: (n, 0))
    return pl.pallas_call(
        last_kernel,
        grid_spec=pltpu.PrefetchScalarGridSpec(
            num_scalar_prefetch=1,
            grid=(features // 128,),
            in_specs=[
                by_rows,
                lanes(features),
                own,
                plain,
                own,
                plain,
                pl.BlockSpec((2, 128, hidden), lambda n, side: (0, n, 0)),
            ],
            out_specs=[
                by_rows,
                pl.BlockSpec((3, share, 128), lambda n, side: (0, 0, n)),
                lanes(share),
                plain,
                lanes(hidden),
            ],
        ),
        out_shape=[
            shape((rows, features), f32),
            shape((3, share, features), f32),
            shape((share, features), f32),
            shape((features, hidden), f32),
            shape((hidden, features), f32),
        ],
    )(side, tokens, weights, up_first, up_pair, down_first, down_pair, line)


def per_image(rows_in):
    images = rows_in.shape[0] // SEQ
    blocks = rows_in.reshape(images, SEQ, rows_in.shape[1])
    return jnp.pad(blocks, ((0, 0), (0, PITCH - SEQ), (0, 0)))


def unpad(blocks):
    images = blocks.shape[0]
    return blocks[:, :SEQ].reshape(images * SEQ, blocks.shape[2])


def per_device_dense(
    tokens,
    gain_attn,
    shift_attn,
    qkv_weight,
    out_weight,
    gain_moe,
    shift_moe,
    router_weight,
    expert_up,
    expert_down,
    routes,
    keep_mask,
    cotangent,
):
    row_count, feature_count = tokens.shape
    images = row_count // SEQ
    rows = images * PITCH
    tensor_count = lax.axis_size("tensor")
    quarter_width = feature_count // tensor_count
    experts_all = router_weight.shape[1]
    hidden = expert_up.shape[2]
    kept_routes = per_image(jnp.where(keep_mask > 0, routes, -1) + 1).reshape(rows, 2) - 1
    expert_lane = jnp.arange(128, dtype=jnp.int32)[None, :]
    kept = ((kept_routes[:, 0:1] == expert_lane) | (kept_routes[:, 1:2] == expert_lane)).astype(bf16)
    cot_turned = cotangent.T
    qkv_turned = jnp.swapaxes(qkv_weight, 1, 2)
    (
        queries,
        keys,
        values,
        attended,
        lse,
        resid,
        h_all,
        cot_all,
        kept_all,
        up_all,
        down_all,
        mixed_first,
        grad_h_first,
        gate_first,
        up_first,
        down_first,
        tok,
        router_wide,
    ) = run_forward(
        tokens,
        gain_attn,
        shift_attn,
        gain_moe,
        shift_moe,
        qkv_turned,
        out_weight,
        expert_up[0],
        expert_down[0],
        router_weight.T,
        cot_turned,
        kept,
        experts_all,
    )
    mixed_part, grad_router, up_second, down_second, grad_h_two, up_pair, down_pair, line_first = run_second_pair(
        h_all,
        cot_all,
        kept_all,
        router_wide,
        mixed_first,
        grad_h_first,
        gate_first,
        up_all,
        down_all,
        up_first,
        down_first,
        experts_all,
    )
    line_sum, tokens_grad, weights_grad, sums, mixed = run_backward(
        gain_attn,
        shift_attn,
        gain_moe,
        grad_router,
        qkv_turned,
        out_weight,
        tok,
        queries,
        keys,
        values,
        attended,
        lse,
        grad_h_two,
        resid,
        cot_all,
        mixed_part,
        up_second,
        down_second,
        line_first,
    )
    side = (lax.axis_index("expert") // 2 % 2).astype(jnp.int32)[None]
    grad_tokens, grad_qkv, grad_out, grad_up, grad_down = run_last(
        side,
        tokens_grad,
        weights_grad.reshape(feature_count, feature_count),
        up_first,
        up_pair,
        down_first,
        down_pair,
        line_sum,
        qkv_weight.shape[2],
    )
    return (
        unpad(mixed.reshape(images, PITCH, quarter_width)),
        grad_tokens,
        sums[0],
        sums[1],
        jnp.swapaxes(grad_qkv, 1, 2),
        grad_out,
        sums[2],
        sums[3],
        sums[8 : 8 + experts_all].T,
        grad_up[None],
        grad_down[None],
    )


def per_device(*arguments):
    router_weight = arguments[7]
    if router_weight.shape[1] == 4 and lax.axis_size("expert") == 8 and lax.axis_size("tensor") == 4:
        return per_device_dense(*arguments)
    return per_device_routed(*arguments)


def solution(mesh):
    placed = (
        P("expert", None),
        P(),
        P(),
        P(None, None, "tensor"),
        P("tensor", None),
        P(),
        P(),
        P(),
        P("expert", None, "tensor"),
        P("expert", "tensor", None),
        P("expert", None),
        P("expert", None),
        P("expert", "tensor"),
    )
    return jax.shard_map(
        per_device,
        mesh=mesh,
        in_specs=placed,
        out_specs=(
            P("expert", "tensor"),
            P("expert", None),
            P(),
            P(),
            P(None, None, "tensor"),
            P("tensor", None),
            P(),
            P(),
            P(),
            P("expert", None, "tensor"),
            P("expert", "tensor", None),
        ),
        check_vma=False,
    )
```

```python
from functools import partial

import jax
import jax.numpy as jnp
from jax import lax
from jax.experimental import pallas as pl
from jax.experimental.pallas import tpu as pltpu
from jax.sharding import PartitionSpec as P

HD = 64
SEQ = 197


norm_epsilon = 1e-06


def norm_rows(values, gain, shift):
    row_mean = jnp.mean(values, axis=-1, keepdims=True)
    centred = values - row_mean
    spread = jnp.mean(centred * centred, axis=-1, keepdims=True)
    return centred * lax.rsqrt(spread + norm_epsilon) * gain + shift


def gelu_exact(values):
    return jax.nn.gelu(values, approximate=False)


def gate_from_logits(logit_rows, picked_rows, keep_rows):
    router_probs = jax.nn.softmax(logit_rows, axis=-1)
    return jnp.sum(jnp.where(picked_rows, router_probs[:, None, :], 0.0), axis=-1) * keep_rows


def attention_forward(h_rows, qkv_w, out_w):
    row_total_count = h_rows.shape[0]
    head_count = qkv_w.shape[2] // HD
    image_count = row_total_count // SEQ
    score_scale = HD ** (-0.5)
    projected = jnp.einsum("td,cdf->ctf", h_rows, qkv_w, preferred_element_type=jnp.float32).astype(
        jnp.bfloat16
    )
    split_heads = projected.reshape(3, image_count, SEQ, head_count, HD)
    queries = split_heads[0]
    keys_all = split_heads[1]
    values_all = split_heads[2]
    scores = (
        jnp.einsum("gqhe,gkhe->ghqk", queries, keys_all, preferred_element_type=jnp.float32)
        * score_scale
    )
    row_peak = jnp.max(scores, axis=-1, keepdims=True)
    exp_scores = jnp.exp(scores - row_peak)
    row_total = jnp.sum(exp_scores, axis=-1, keepdims=True)
    log_total = row_peak + jnp.log(row_total)
    weights = (exp_scores / row_total).astype(jnp.bfloat16)
    attended = jnp.einsum(
        "ghqk,gkhe->gqhe", weights, values_all, preferred_element_type=jnp.float32
    ).astype(jnp.bfloat16)
    attended = attended.reshape(row_total_count, head_count * HD)
    partial_out = jnp.dot(attended, out_w, preferred_element_type=jnp.float32)
    return (partial_out, (attended, queries, keys_all, values_all, log_total))


def attention_backward(grad_branch, saved, h_rows, qkv_w, out_w):
    attended, queries, keys_all, values_all, log_total = saved
    row_total_count = h_rows.shape[0]
    head_count = qkv_w.shape[2] // HD
    image_count = row_total_count // SEQ
    score_scale = HD ** (-0.5)
    grad_out = jnp.einsum("tc,td->cd", attended, grad_branch, preferred_element_type=jnp.float32)
    grad_attended = jnp.einsum(
        "td,cd->tc", grad_branch, out_w, preferred_element_type=jnp.float32
    ).astype(jnp.bfloat16)
    grad_attended = grad_attended.reshape(image_count, SEQ, head_count, HD)
    scores_again = (
        jnp.einsum("gqhe,gkhe->ghqk", queries, keys_all, preferred_element_type=jnp.float32)
        * score_scale
    )
    probs_again = jnp.exp(scores_again - log_total)
    grad_weights = jnp.einsum(
        "gqhe,gkhe->ghqk", grad_attended, values_all, preferred_element_type=jnp.float32
    )
    grad_scores = (
        probs_again * (grad_weights - jnp.sum(probs_again * grad_weights, axis=-1, keepdims=True))
    ).astype(jnp.bfloat16)
    grad_queries = (
        jnp.einsum("ghqk,gkhe->gqhe", grad_scores, keys_all, preferred_element_type=jnp.float32)
        * score_scale
    )
    grad_keys = (
        jnp.einsum("ghqk,gqhe->gkhe", grad_scores, queries, preferred_element_type=jnp.float32)
        * score_scale
    )
    grad_values = jnp.einsum(
        "ghqk,gqhe->gkhe",
        probs_again.astype(jnp.bfloat16),
        grad_attended,
        preferred_element_type=jnp.float32,
    )
    grad_rows = (
        jnp.stack([grad_queries, grad_keys, grad_values])
        .astype(jnp.bfloat16)
        .reshape(3, row_total_count, head_count * HD)
    )
    grad_qkv = jnp.einsum("td,ctf->cdf", h_rows, grad_rows, preferred_element_type=jnp.float32)
    grad_h_one = jnp.einsum("ctf,cdf->td", grad_rows, qkv_w, preferred_element_type=jnp.float32)
    return (grad_qkv, grad_out, grad_h_one)


def moe_tail(
    grad_h_rows,
    grad_gate_rows,
    grad_out_rows,
    h_two_rows,
    resid_rows,
    gate_back,
    router_weight,
    gain_moe,
    shift_moe,
):
    row_total_count = grad_h_rows.shape[0]
    grad_gate = jnp.sum(grad_gate_rows.reshape(row_total_count, -1, 2), axis=1)
    grad_logits = gate_back(grad_gate)[0].astype(jnp.bfloat16)
    grad_router = jnp.einsum(
        "td,te->de", h_two_rows, grad_logits, preferred_element_type=jnp.float32
    )
    grad_h_two = grad_h_rows + jnp.einsum(
        "te,de->td", grad_logits, router_weight, preferred_element_type=jnp.float32
    )
    norm_out, norm_back = jax.vjp(norm_rows, resid_rows, gain_moe, shift_moe)
    grad_resid_norm, grad_gain_moe, grad_shift_moe = norm_back(grad_h_two)
    return (grad_out_rows + grad_resid_norm, grad_router, grad_gain_moe, grad_shift_moe)


def per_device_routed(
    tokens,
    gain_attn,
    shift_attn,
    qkv_weight,
    out_weight,
    gain_moe,
    shift_moe,
    router_weight,
    expert_up,
    expert_down,
    routes,
    keep_mask,
    cotangent,
):
    row_count, feature_count = tokens.shape
    tensor_count = lax.axis_size("tensor")
    expert_count = lax.axis_size("expert")
    tensor_here = lax.axis_index("tensor")
    quarter_width = feature_count // tensor_count
    col_start = tensor_here * quarter_width
    experts_all = router_weight.shape[1]
    capacity = max(2, 7 * row_count // (2 * experts_all))
    tokens_float = tokens.astype(jnp.float32)
    h_one = norm_rows(tokens_float, gain_attn, shift_attn).astype(jnp.bfloat16)
    partial_out, saved = attention_forward(h_one, qkv_weight, out_weight)
    branch = lax.psum(partial_out, "tensor")
    resid = tokens_float + branch
    h_two = norm_rows(resid, gain_moe, shift_moe).astype(jnp.bfloat16)
    logits = jnp.dot(h_two, router_weight, preferred_element_type=jnp.float32)
    keep_float = keep_mask.astype(jnp.float32)
    picked = routes[:, :, None] == jnp.arange(experts_all, dtype=jnp.int32)[None, None, :]
    gate_values, gate_back = jax.vjp(
        partial(gate_from_logits, picked_rows=picked, keep_rows=keep_float), logits
    )
    flat_expert = routes.reshape(-1)
    one_hot = (flat_expert[:, None] == jnp.arange(experts_all, dtype=jnp.int32)[None, :]).astype(
        jnp.int32
    )
    rank_within = jnp.sum((jnp.cumsum(one_hot, axis=0) - one_hot) * one_hot, axis=1)
    slot_index = flat_expert * capacity + rank_within
    token_index = jnp.repeat(jnp.arange(row_count, dtype=jnp.int32), 2)
    live_route = keep_mask.reshape(-1) > 0
    source_table = (
        jnp.full((experts_all * capacity,), row_count, jnp.int32)
        .at[slot_index]
        .set(jnp.where(live_route, token_index, row_count))
    )
    padded_rows = jnp.concatenate([h_two, jnp.zeros((1, feature_count), jnp.bfloat16)], axis=0)
    dispatch = padded_rows[source_table].reshape(experts_all, capacity, feature_count)
    paired = jnp.broadcast_to(dispatch[:, None], (experts_all, 2, capacity, feature_count)).reshape(
        expert_count, capacity, feature_count
    )
    arrived = lax.all_to_all(paired, "expert", split_axis=0, concat_axis=0, tiled=True)
    expert_rows = arrived.reshape(expert_count * capacity, feature_count)
    up_local = expert_up[0]
    down_local = expert_down[0]
    pre_act = jnp.dot(expert_rows, up_local, preferred_element_type=jnp.float32)
    hidden_float, gelu_back = jax.vjp(gelu_exact, pre_act)
    hidden = hidden_float.astype(jnp.bfloat16)
    partial_down = jnp.dot(hidden, down_local, preferred_element_type=jnp.float32)
    summed = lax.psum_scatter(partial_down, "tensor", scatter_dimension=1, tiled=True)
    returned = lax.all_to_all(
        summed.reshape(expert_count, capacity, quarter_width),
        "expert",
        split_axis=0,
        concat_axis=0,
        tiled=True,
    )
    answer_table = jnp.sum(
        returned.reshape(experts_all, 2, capacity, quarter_width), axis=1
    ).astype(jnp.bfloat16)
    answers = (
        answer_table.reshape(experts_all * capacity, quarter_width)[slot_index]
        .astype(jnp.float32)
        .reshape(row_count, 2, quarter_width)
    )
    resid_part = lax.dynamic_slice_in_dim(resid, col_start, quarter_width, 1)
    mixed = (resid_part + jnp.sum(gate_values[:, :, None] * answers, axis=1)).astype(jnp.bfloat16)
    grad_part = cotangent.astype(jnp.float32)
    grad_answers = (
        (gate_values[:, :, None] * grad_part[:, None, :])
        .astype(jnp.bfloat16)
        .reshape(2 * row_count, quarter_width)
    )
    grad_gate_part = jnp.sum(grad_part[:, None, :] * answers, axis=-1)
    outgoing = (
        jnp.zeros((experts_all * capacity, quarter_width), jnp.bfloat16)
        .at[slot_index]
        .set(grad_answers)
    )
    outgoing = jnp.broadcast_to(
        outgoing.reshape(experts_all, 1, capacity, quarter_width),
        (experts_all, 2, capacity, quarter_width),
    ).reshape(expert_count, capacity, quarter_width)
    incoming = lax.all_to_all(outgoing, "expert", split_axis=0, concat_axis=0, tiled=True)
    grad_full = lax.all_gather(incoming, "tensor", axis=2, tiled=True).reshape(
        expert_count * capacity, feature_count
    )
    grad_hidden = jnp.einsum("rd,fd->rf", grad_full, down_local, preferred_element_type=jnp.float32)
    grad_pre = gelu_back(grad_hidden)[0].astype(jnp.bfloat16)
    grad_down = jnp.einsum("rf,rd->fd", hidden, grad_full, preferred_element_type=jnp.float32)
    grad_up = jnp.einsum("rd,rf->df", expert_rows, grad_pre, preferred_element_type=jnp.float32)
    grad_rows_partial = jnp.einsum(
        "rf,df->rd", grad_pre, up_local, preferred_element_type=jnp.float32
    )
    grad_rows_sum = lax.psum_scatter(
        grad_rows_partial.astype(jnp.bfloat16), "tensor", scatter_dimension=1, tiled=True
    ).astype(jnp.float32)
    sent_back = lax.all_to_all(
        grad_rows_sum.reshape(expert_count, capacity, quarter_width).astype(jnp.bfloat16),
        "expert",
        split_axis=0,
        concat_axis=0,
        tiled=True,
    ).astype(jnp.float32)
    grad_table = jnp.sum(sent_back.reshape(experts_all, 2, capacity, quarter_width), axis=1).astype(
        jnp.bfloat16
    )
    grad_inputs = (
        grad_table.reshape(experts_all * capacity, quarter_width)[slot_index]
        .astype(jnp.float32)
        .reshape(row_count, 2, quarter_width)
    )
    grad_h_part = jnp.sum(grad_inputs * keep_float[:, :, None], axis=1)
    grad_h_full, grad_gate_all, grad_out_full = (
        lax.all_gather(grad_h_part, "tensor", axis=1, tiled=True),
        lax.all_gather(grad_gate_part, "tensor", axis=1, tiled=True),
        lax.all_gather(grad_part, "tensor", axis=1, tiled=True),
    )
    grad_resid, grad_router, grad_gain_moe, grad_shift_moe = moe_tail(
        grad_h_full,
        grad_gate_all,
        grad_out_full,
        h_two,
        resid,
        gate_back,
        router_weight,
        gain_moe,
        shift_moe,
    )
    grad_qkv, grad_out, grad_h_one_part = attention_backward(
        grad_resid.astype(jnp.bfloat16), saved, h_one, qkv_weight, out_weight
    )
    grad_h_one = lax.psum(grad_h_one_part.astype(jnp.bfloat16), "tensor").astype(jnp.float32)
    norm_one_out, norm_one_back = jax.vjp(norm_rows, tokens_float, gain_attn, shift_attn)
    grad_tok_norm, grad_gain_attn, grad_shift_attn = norm_one_back(grad_h_one)
    grad_tokens = grad_resid + grad_tok_norm
    summed_grads = lax.psum(
        (
            grad_gain_attn,
            grad_shift_attn,
            grad_qkv,
            grad_out,
            grad_gain_moe,
            grad_shift_moe,
            grad_router,
        ),
        "expert",
    )
    grad_qkv_mine = summed_grads[2]
    grad_out_mine = summed_grads[3]
    return (
        mixed,
        grad_tokens,
        summed_grads[0],
        summed_grads[1],
        grad_qkv_mine,
        grad_out_mine,
        summed_grads[4],
        summed_grads[5],
        summed_grads[6],
        grad_up[None],
        grad_down[None],
    )


MESH = pl.DeviceIdType.MESH
f32 = jnp.float32
bf16 = jnp.bfloat16
PITCH = 208


def dot(left, right, over=((1,), (0,))):
    return lax.dot_general(left, right, (over, ((), ())), preferred_element_type=f32)


def aligned(start, size):
    return pl.ds(pl.multiple_of(start, 16), size)


def lanes_at(start, size):
    return pl.ds(pl.multiple_of(start, 128), size)


def norm_stats(values):
    row_mean = jnp.mean(values, axis=1, keepdims=True)
    centred = values - row_mean
    inverse = lax.rsqrt(jnp.mean(centred * centred, axis=1, keepdims=True) + norm_epsilon)
    return centred * inverse, inverse


def greet(neighbours):
    barrier = pltpu.get_barrier_semaphore()
    count = 0
    for is_there, device in neighbours:

        @pl.when(is_there)
        def _():
            pl.semaphore_signal(barrier, inc=1, device_id=device, device_id_type=MESH)

        count = count + jnp.where(is_there, 1, 0)
    pl.semaphore_wait(barrier, count)


def head_mask(lane, head):
    return (lane < HD) if head % 2 == 0 else (lane >= HD)


def expert_math(h_rows, cot_rows, kept, router, up, down, pair, experts):
    block = h_rows.shape[0]
    hidden = up.shape[1] // 2
    lane = lax.broadcasted_iota(jnp.int32, (block, 128), 1)
    logits = jnp.where(lane < experts, dot(h_rows, router, ((1,), (1,))), -1e30)
    powers = jnp.exp(logits - jnp.max(logits, axis=1, keepdims=True))
    probs = powers / jnp.sum(powers, axis=1, keepdims=True)
    gates = kept * probs
    pre_act = dot(h_rows, up)
    back = dot(cot_rows, down, ((1,), (1,)))
    normal_cdf = 0.5 + 0.5 * lax.erf(pre_act * 0.7071067811865476)
    gelu = pre_act * normal_cdf
    slope = normal_cdf + pre_act * (0.3989422804014327 * jnp.exp(-0.5 * pre_act * pre_act))
    product = gelu * back
    grad_gate = jnp.zeros((block, 128), f32)
    spread = []
    for side in range(2):
        chosen = lane == 2 * pair + side
        part = jnp.sum(product[:, side * hidden : (side + 1) * hidden], axis=1, keepdims=True)
        grad_gate = jnp.where(chosen, part, grad_gate)
        gate = jnp.sum(jnp.where(chosen, gates, 0.0), axis=1, keepdims=True)
        spread.append(jnp.broadcast_to(gate, (block, hidden)))
    gate = jnp.concatenate(spread, axis=1)
    hidden_rows = (gelu * gate).astype(bf16)
    grad_pre = (slope * back * gate).astype(bf16)
    return hidden_rows, grad_pre, probs, grad_gate


BLOCK = 2 * PITCH


def forward_kernel(
    gain1_ref,
    shift1_ref,
    gain2_ref,
    shift2_ref,
    up_ref,
    down_ref,
    router_raw,
    cot_hbm,
    kept_hbm,
    tok_hbm,
    qkv_hbm,
    out_w_hbm,
    q_ref,
    k_ref,
    v_ref,
    att_ref,
    lse_ref,
    resid_ref,
    h_out,
    cot_out,
    kept_out,
    up_out,
    down_out,
    mixed_out,
    grad_h_out,
    gate_out,
    grad_up_out,
    grad_down_out,
    tok_out,
    router_out,
    router_ref,
    cot_turned,
    kept_ref,
    tok_raw,
    qkv_ref,
    out_w_ref,
    tok_ref,
    cot_ref,
    up_vm,
    down_vm,
    up_sum,
    down_sum,
    mixed_slots,
    grad_h_slots,
    gate_slots,
    grad_up_vm,
    grad_down_vm,
    q_all,
    k_all,
    v_all,
    att_all,
    lse_all,
    resid_all,
    h_all,
    cot_all,
    kept_all,
    part,
    mine,
    core_from,
    core_to,
    x_to,
    x_from,
    total_to,
    total_from,
    cot_core,
    core_s,
    core_r,
    x_s,
    x_r,
    tot_s,
    tot_r,
    y_s,
    y_r,
    rel_s,
    rel_r,
    w_s,
    w_r,
    c_s,
    c_r,
    load_sem,
    own_sem,
    pair_sem,
    block_sem,
    grad_sem,
    cot_sem,
    out_sem,
    *,
    images,
    heads,
    experts,
):
    expert_at = lax.axis_index("expert")
    tensor_at = lax.axis_index("tensor")
    z_at, y_at = expert_at // 2, expert_at % 2
    z_last = lax.axis_size("expert") // 2 - 1
    x_at, core_at = tensor_at // 2, tensor_at % 2
    other = 1 - core_at
    rows = images * PITCH
    half = rows // 2
    wide = out_w_ref.shape[1] // 2
    loads = [
        pltpu.make_async_copy(source, target, load_sem.at[number])
        for number, (source, target) in enumerate(
            (
                (cot_hbm, cot_turned),
                (kept_hbm, kept_ref),
                (tok_hbm, tok_raw),
                (qkv_hbm, qkv_ref),
                (out_w_hbm, out_w_ref),
            )
        )
    ]
    for copy in loads:
        copy.start()
    hidden = up_ref.shape[1]
    core_dev = (expert_at, tensor_at + 1 - 2 * core_at)
    x_dev = (expert_at, tensor_at + 2 - 4 * x_at)
    y_dev = (expert_at + 1 - 2 * y_at, tensor_at)
    z_up = (expert_at + 2, tensor_at)
    z_down = (expert_at - 2, tensor_at)
    has_up, has_down = z_at < z_last, z_at > 0
    greet([(True, core_dev), (True, x_dev), (True, y_dev), (has_up, z_up), (has_down, z_down)])

    def remote(src, dst, send, recv, device):
        return pltpu.make_async_remote_copy(
            src_ref=src, dst_ref=dst, send_sem=send, recv_sem=recv, device_id=device, device_id_type=MESH
        )

    def slot(expert, plane):
        pair = (expert // 2 + plane // 2) % 2
        return (
            up_out.at[pair, :, lanes_at(expert % 2 * hidden, hidden)],
            down_out.at[pair, aligned(expert % 2 * hidden, hidden), :],
        )

    def hop(step, way):
        expert = z_at - step if way == 0 else z_at + step
        plane = z_at + 1 if way == 0 else z_at - 1
        source = (up_ref, down_ref) if step == 0 else slot(expert, z_at)
        target = slot(expert, plane)
        device = z_up if way == 0 else z_down
        return [remote(source[n], target[n], w_s.at[way, step, n], w_r.at[way, step, n], device) for n in range(2)]

    def hop_goes(step, way):
        if way == 0:
            return (z_at - step >= 0) & has_up
        return (z_at + step <= z_last) & has_down

    def hop_comes(step, way):
        return (z_at - 1 - step >= 0) if way == 0 else (z_at + 1 + step <= z_last)

    def hop_arriving(step, way):
        expert = z_at - 1 - step if way == 0 else z_at + 1 + step
        target = slot(expert, z_at)
        return [remote(target[n], target[n], w_s.at[way, step, n], w_r.at[way, step, n], core_dev) for n in range(2)]

    def start_hops(step, which):
        for way in range(2):

            @pl.when(hop_goes(step, way))
            def _():
                hop(step, way)[which].start()

    def await_hops(step, which):
        for way in range(2):

            @pl.when(hop_comes(step, way))
            def _():
                hop_arriving(step, way)[which].wait_recv()

    def pass_hops(step, which):
        await_hops(step, which)
        start_hops(step + 1, which)

    start_hops(0, 0)
    start_hops(0, 1)

    def pair_place(expert):
        return up_vm.at[:, lanes_at(expert % 2 * hidden, hidden)], down_vm.at[aligned(expert % 2 * hidden, hidden), :]

    near = z_at + 1 - 2 * (z_at % 2)
    own_copies = [
        pltpu.make_async_copy((up_ref, down_ref)[n], pair_place(z_at)[n], own_sem.at[n]) for n in range(2)
    ]
    near_copies = [
        pltpu.make_async_copy(slot(near, z_at)[n], pair_place(near)[n], pair_sem.at[n]) for n in range(2)
    ]
    for copy in own_copies:
        copy.start()

    loads[0].wait()
    for number in range(images):
        first = number * SEQ // 128 * 128
        skip = number * SEQ - first
        lanes_in = cot_turned[:, first : min(first + 384, images * SEQ)].astype(f32)
        if lanes_in.shape[1] < 384:
            lanes_in = jnp.concatenate([lanes_in, jnp.zeros((lanes_in.shape[0], 384 - lanes_in.shape[1]), f32)], axis=1)
        turned = lanes_in.T[skip : skip + SEQ]
        padded = jnp.concatenate([turned, jnp.zeros((PITCH - SEQ, turned.shape[1]), f32)], axis=0)
        cot_ref[number * PITCH : (number + 1) * PITCH, :] = padded.astype(bf16)
    swap = remote(cot_ref, cot_core, c_s.at[0], c_r.at[0], core_dev)
    swap.start()

    narrow = router_raw[...].astype(f32)
    router_ref[0:16, :] = jnp.concatenate([narrow, jnp.zeros((16 - experts, narrow.shape[1]), f32)], axis=0).astype(bf16)
    router_ref[16:128, :] = jnp.zeros((112, narrow.shape[1]), bf16)

    def kept_half(side, core):
        return kept_all.at[aligned(side * rows + core * half, half), :]

    kept_y = remote(kept_half(0, core_at), kept_half(1, core_at), c_s.at[7], c_r.at[7], y_dev)
    kept_share = remote(kept_half(1, core_at), kept_half(1, core_at), c_s.at[6], c_r.at[6], core_dev)
    kept_share_in = remote(kept_half(1, other), kept_half(1, other), c_s.at[6], c_r.at[6], core_dev)
    loads[1].wait()
    kept_all[pl.ds(0, rows), :] = kept_ref[...]
    kept_y.start()
    swap.wait_recv()

    @pl.when(core_at == 0)
    def _():
        both = jnp.concatenate([cot_ref[...], cot_core[...]], axis=1)
        cot_all[pl.ds(0, rows), lanes_at(x_at * wide, wide)] = both

    @pl.when(core_at == 1)
    def _():
        both = jnp.concatenate([cot_core[...], cot_ref[...]], axis=1)
        cot_all[pl.ds(0, rows), lanes_at(x_at * wide, wide)] = both

    def block(side, col_side, core):
        return cot_all.at[aligned(side * rows + core * half, half), lanes_at(col_side * wide, wide)]

    def cot_copy(number, source, target, device):
        return remote(source, target, c_s.at[number], c_r.at[number], device)

    mine_block = block(0, x_at, core_at)
    cot_x = cot_copy(1, mine_block, mine_block, x_dev)
    cot_y = cot_copy(2, mine_block, block(1, x_at, core_at), y_dev)
    cot_x.start()
    cot_y.start()
    across_x, across_y, across_both = block(0, 1 - x_at, core_at), block(1, x_at, core_at), block(1, 1 - x_at, core_at)
    cot_x_in = cot_copy(1, across_x, across_x, x_dev)
    cot_y_in = cot_copy(2, across_y, across_y, y_dev)
    relay_y = cot_copy(3, across_x, across_both, y_dev)
    relay_in = cot_copy(3, across_both, across_both, y_dev)
    cot_share = [
        cot_copy(4, across_x, across_x, core_dev),
        cot_copy(5, across_y, across_y, core_dev),
        cot_copy(8, across_both, across_both, core_dev),
    ]
    arriving = [block(0, 1 - x_at, other), block(1, x_at, other), block(1, 1 - x_at, other)]
    cot_share_in = [cot_copy(number, ref, ref, core_dev) for number, ref in zip((4, 5, 8), arriving)]

    lane = lax.broadcasted_iota(jnp.int32, (PITCH, 2 * HD), 1)
    key_mask = lax.broadcasted_iota(jnp.int32, (PITCH, PITCH), 1) < SEQ
    gain1, shift1, gain2, shift2 = (ref[...].reshape(1, 2 * wide) for ref in (gain1_ref, shift1_ref, gain2_ref, shift2_ref))
    my_cols = lanes_at(core_at * wide, wide)
    their_cols = lanes_at(other * wide, wide)

    def attend(image):
        normed, _ = norm_stats(tok_ref[image].astype(f32))
        h_one = (normed * gain1 + shift1).astype(bf16)
        queries = dot(h_one, qkv_ref[0], ((1,), (1,))).astype(bf16)
        keys = dot(h_one, qkv_ref[1], ((1,), (1,))).astype(bf16)
        values = dot(h_one, qkv_ref[2], ((1,), (1,))).astype(bf16)
        q_all[image] = queries
        k_all[image] = keys
        v_all[image] = values
        outs = []
        lse = jnp.zeros((PITCH, 2 * HD), f32)
        for head in range(heads):
            first = head // 2 * 2 * HD
            last = min(first + 2 * HD, heads * HD)
            q_head, k_head, v_head = queries[:, first:last], keys[:, first:last], values[:, first:last]
            if last - first == 2 * HD:
                q_head = jnp.where(head_mask(lane, head), q_head, jnp.zeros_like(q_head))
            scores = dot(q_head, k_head, ((1,), (1,))) * (HD**-0.5)
            scores = jnp.where(key_mask, scores, -1e30)
            peak = jnp.max(scores, axis=1, keepdims=True)
            powers = jnp.exp(scores - peak)
            row_sum = jnp.sum(powers, axis=1, keepdims=True)
            weights = (powers / row_sum).astype(bf16)
            outs.append(dot(weights, v_head))
            lse = jnp.where(lane == head, peak + jnp.log(row_sum), lse)
        lse_all[image] = lse
        joined = []
        for head in range(0, heads, 2):
            if head + 1 < heads:
                joined.append(jnp.where(lane < HD, outs[head], outs[head + 1]))
            else:
                joined.append(outs[head])
        attended = jnp.concatenate(joined, axis=1).astype(bf16)
        att_all[image] = attended
        part[...] = dot(attended, out_w_ref[...])
        mine[image] = part[:, my_cols]
        core_to[image] = part[:, their_cols].astype(bf16)

    def core_copy(image):
        return remote(core_to.at[image], core_from.at[image], core_s.at[image], core_r.at[image], core_dev)

    def x_copy(image):
        return remote(x_to.at[image], x_from.at[image], x_s.at[image], x_r.at[image], x_dev)

    def total_copy(image):
        return remote(total_to.at[image], total_from.at[image], tot_s.at[image], tot_r.at[image], core_dev)

    def h_block(side, image, core):
        return h_all.at[aligned(side * rows + image * PITCH, PITCH), lanes_at(core * wide, wide)]

    def y_copy(image):
        return remote(h_block(0, image, core_at), h_block(1, image, core_at), y_s.at[image], y_r.at[image], y_dev)

    def relay_copy(image):
        ref = h_block(1, image, core_at)
        return remote(ref, ref, rel_s.at[image], rel_r.at[image], core_dev)

    def relay_arriving(image):
        ref = h_block(1, image, other)
        return remote(ref, ref, rel_s.at[image], rel_r.at[image], core_dev)

    attend_outs = ((tok_ref, tok_out), (q_all, q_ref), (k_all, k_ref), (v_all, v_ref), (att_all, att_ref), (lse_all, lse_ref))

    def out_copies(image):
        copies = [
            pltpu.make_async_copy(kept.at[image], out.at[image], out_sem.at[n, image])
            for n, (kept, out) in enumerate(attend_outs)
        ]
        at = aligned(image * PITCH, PITCH)
        return copies, [
            pltpu.make_async_copy(resid_all.at[image], resid_ref.at[at, :], out_sem.at[6, image]),
            pltpu.make_async_copy(h_all.at[at, :], h_out.at[at, :], out_sem.at[7, image]),
        ]

    def other_copy(image):
        at = aligned(rows + image * PITCH, PITCH)
        return pltpu.make_async_copy(h_all.at[at, :], h_out.at[at, :], out_sem.at[8, image])

    def stage(tick, lag, run):
        image = tick - lag

        @pl.when((image >= 0) & (image < images))
        def _():
            run(image)

    def run_attend(image):
        attend(image)
        core_copy(image).start()
        for copy in out_copies(image)[0]:
            copy.start()

    def run_x(image):
        core_copy(image).wait_recv()
        x_to[image] = (mine[image] + core_from[image].astype(f32)).astype(bf16)
        x_copy(image).start()

    def run_total(image):
        x_copy(image).wait_recv()
        total_to[image] = (x_to[image].astype(f32) + x_from[image].astype(f32)).astype(bf16)
        total_copy(image).start()

    def run_norm(image):
        total_copy(image).wait_recv()
        part[:, my_cols] = total_to[image].astype(f32)
        part[:, their_cols] = total_from[image].astype(f32)
        resid = tok_ref[image].astype(f32) + part[...]
        resid_all[image] = resid
        normed, _ = norm_stats(resid)
        h_all[aligned(image * PITCH, PITCH), :] = (normed * gain2 + shift2).astype(bf16)
        y_copy(image).start()
        for copy in out_copies(image)[1]:
            copy.start()

    def run_relay(image):
        y_copy(image).wait_recv()
        relay_copy(image).start()

    def run_end(image):
        relay_arriving(image).wait_recv()
        other_copy(image).start()

    def cot_step_one():
        cot_x_in.wait_recv()
        cot_share[0].start()

        relay_y.start()

    def cot_step_two():
        cot_y_in.wait_recv()
        cot_share[1].start()

    def weights_step_one():
        pass_hops(0, 1)
        for copy in near_copies:
            copy.start()

    def cot_step_three():
        kept_y.wait_recv()
        kept_share.start()
        relay_in.wait_recv()
        cot_share[2].start()

    outs = [
        pltpu.make_async_copy(cot_all, cot_out, cot_sem.at[0]),
        pltpu.make_async_copy(kept_all, kept_out, cot_sem.at[1]),
        pltpu.make_async_copy(router_ref, router_out, cot_sem.at[2]),
    ]

    def ready_own():
        cot_share_in[0].wait_recv()
        for copy in (*own_copies, *near_copies):
            copy.wait()

    def ready_other():
        for copy in (cot_share_in[1], cot_share_in[2], kept_share_in):
            copy.wait_recv()
        for copy in outs:
            copy.start()

    def block_copies(number, place):
        at = aligned(number * BLOCK, BLOCK)
        pairs = ((mixed_slots, mixed_out), (grad_h_slots, grad_h_out), (gate_slots, gate_out))
        return [
            pltpu.make_async_copy(slots.at[place], out.at[at, :], block_sem.at[n, place])
            for n, (slots, out) in enumerate(pairs)
        ]

    def run_block(number, turn):
        at = aligned(number * BLOCK, BLOCK)
        h_rows, cot_rows = h_all[at, :], cot_all[at, :]
        up, down = up_vm[...], down_vm[...]
        hidden_rows, grad_pre, _, grad_gate = expert_math(
            h_rows, cot_rows, kept_all[at, :].astype(f32), router_ref[...], up, down, z_at // 2, experts
        )

        place = turn % 2

        @pl.when(turn >= 2)
        def _():
            for copy in block_copies(number, place):
                copy.wait()

        gate_slots[place] = grad_gate
        mixed_slots[place] = dot(hidden_rows, down).astype(bf16)
        grad_h_slots[place] = dot(grad_pre, up, ((1,), (1,))).astype(bf16)
        for copy in block_copies(number, place):
            copy.start()
        up_sum[...] += dot(h_rows.T, grad_pre)
        down_sum[...] += dot(cot_rows.T, hidden_rows)

    up_sum[...] = jnp.zeros_like(up_sum)
    down_sum[...] = jnp.zeros_like(down_sum)

    def take_tokens(number):
        first = number * SEQ // 16 * 16
        skip = number * SEQ - first
        taken = min(224, images * SEQ - first)
        rows_in = tok_raw[first : first + taken, :].astype(f32)[skip : skip + SEQ]
        padded = jnp.concatenate([rows_in, jnp.zeros((PITCH - SEQ, rows_in.shape[1]), f32)], axis=0)
        tok_ref[number] = padded.astype(bf16)

    def first_ticks(tick, _):
        for number in range(images):
            pl.when(tick == number)(partial(take_tokens, number))

        stage(tick, 0, run_attend)
        stage(tick, 1, run_x)
        return 0

    for copy in loads[2:]:
        copy.wait()
    lax.fori_loop(0, images + 1, first_ticks, 0)
    pairs = images // 2

    def both(first, *runs):
        for run in runs:
            run(first)
            run(first + 1)

    pass_hops(0, 0)
    cot_step_one()
    both(0, run_total, run_norm)
    cot_step_two()
    weights_step_one()
    ready_own()

    def per_turn(turn, _):
        @pl.when((turn <= 1) | (turn == 3))
        def _():
            both(jnp.where(turn == 3, 6, 2 * turn + 2), run_total, run_norm)

        @pl.when((turn >= 2) & (turn < pairs + 2))
        def _():
            both(2 * turn - 4, run_relay)

        @pl.when(turn == 2)
        def _():
            pass_hops(1, 0)
            cot_step_three()

        @pl.when(turn == pairs)
        def _():
            pass_hops(1, 1)
            ready_other()

        @pl.when(turn >= pairs)
        def _():
            both(2 * (turn - pairs), run_end)

        run_block(turn, turn)
        return 0

    lax.fori_loop(0, 2 * pairs, per_turn, 0)
    grad_up_vm[...] = up_sum[...].astype(bf16)
    grad_down_vm[...] = down_sum[...].astype(bf16)
    grad_copies = [
        pltpu.make_async_copy(grad_up_vm, grad_up_out, grad_sem.at[0]),
        pltpu.make_async_copy(grad_down_vm, grad_down_out, grad_sem.at[1]),
    ]
    for copy in grad_copies:
        copy.start()
    for copy in (swap, kept_y, kept_share, cot_x, cot_y, *cot_share):
        copy.wait_send()

    relay_y.wait_send()

    def drain(image, _):
        for copy in (core_copy, x_copy, total_copy, y_copy, relay_copy):
            copy(image).wait_send()
        first, second = out_copies(image)
        for copy in (*first, *second, other_copy(image)):
            copy.wait()
        return 0

    lax.fori_loop(0, images, drain, 0)
    for place in range(2):
        for copy in block_copies(0, place):
            copy.wait()

    await_hops(2, 0)
    await_hops(2, 1)
    for step in range(3):
        for way in range(2):

            @pl.when(hop_goes(step, way))
            def _():
                for copy in hop(step, way):
                    copy.wait_send()

    for copy in (*grad_copies, *outs):
        copy.wait()


def run_forward(tok_raw, gain1, shift1, gain2, shift2, qkv_w, out_w, up, down, router, cot, kept, experts):
    images = tok_raw.shape[0] // SEQ
    rows = images * PITCH
    features = tok_raw.shape[1]
    share = out_w.shape[0]
    heads = share // HD
    hidden = up.shape[1]
    wide = features // 2
    vmem = pl.BlockSpec(memory_space=pltpu.VMEM)
    anywhere = pl.BlockSpec(memory_space=pl.ANY)
    shape = jax.ShapeDtypeStruct
    block = (images, PITCH, wide)
    dma = pltpu.SemaphoreType.DMA
    return pl.pallas_call(
        partial(forward_kernel, images=images, heads=heads, experts=experts),
        out_shape=[
            shape((images, PITCH, share), bf16),
            shape((images, PITCH, share), bf16),
            shape((images, PITCH, share), bf16),
            shape((images, PITCH, share), bf16),
            shape((images, PITCH, 128), f32),
            shape((rows, features), f32),
            shape((2 * rows, features), bf16),
            shape((2 * rows, features), bf16),
            shape((2 * rows, 128), bf16),
            shape((2, features, 2 * hidden), bf16),
            shape((2, 2 * hidden, features), bf16),
            shape((2 * rows, features), bf16),
            shape((2 * rows, features), bf16),
            shape((2 * rows, 128), f32),
            shape((features, 2 * hidden), bf16),
            shape((features, 2 * hidden), bf16),
            shape((images, PITCH, features), bf16),
            shape((128, features), bf16),
        ],
        in_specs=[vmem] * 4 + [anywhere] * 2 + [vmem] + [anywhere] * 5,
        out_specs=[anywhere] * 18,
        scratch_shapes=[
            pltpu.VMEM((128, features), bf16),
            pltpu.VMEM(cot.shape, bf16),
            pltpu.VMEM(kept.shape, bf16),
            pltpu.VMEM(tok_raw.shape, bf16),
            pltpu.VMEM(qkv_w.shape, bf16),
            pltpu.VMEM(out_w.shape, bf16),
            pltpu.VMEM((images, PITCH, features), bf16),
            pltpu.VMEM((rows, share), bf16),
            pltpu.VMEM((features, 2 * hidden), bf16),
            pltpu.VMEM((2 * hidden, features), bf16),
            *[pltpu.VMEM((features, 2 * hidden), f32)] * 2,
            *[pltpu.VMEM((2, BLOCK, features), bf16)] * 2,
            pltpu.VMEM((2, BLOCK, 128), f32),
            *[pltpu.VMEM((features, 2 * hidden), bf16)] * 2,
            *[pltpu.VMEM((images, PITCH, share), bf16)] * 4,
            pltpu.VMEM((images, PITCH, 128), f32),
            pltpu.VMEM((images, PITCH, features), f32),
            pltpu.VMEM((2 * rows, features), bf16),
            pltpu.VMEM((2 * rows, features), bf16),
            pltpu.VMEM((2 * rows, 128), bf16),
            pltpu.VMEM((PITCH, features), f32),
            pltpu.VMEM(block, f32),
            pltpu.VMEM(block, bf16),
            pltpu.VMEM(block, bf16),
            pltpu.VMEM(block, bf16),
            pltpu.VMEM(block, bf16),
            pltpu.VMEM(block, bf16),
            pltpu.VMEM(block, bf16),
            pltpu.VMEM((rows, share), bf16),
        ]
        + [dma((images,))] * 10
        + [dma((2, 3, 2))] * 2
        + [dma((9,))] * 2
        + [dma((5,)), dma((2,)), dma((2,)), dma((3, 2)), dma((2,)), dma((3,)), dma((9, images))],
        compiler_params=pltpu.CompilerParams(
            collective_id=1, has_side_effects=True, vmem_limit_bytes=63 << 20
        ),
    )(gain1, shift1, gain2, shift2, up, down, router, cot, kept, tok_raw, qkv_w, out_w)


def turn_is_other(turn):
    return (turn == 0) | ((turn % 2 == 1) & (turn < 7))


def turn_block(turn):
    own = jnp.where(turn == 7, 3, turn // 2 - 1)
    return jnp.where(turn_is_other(turn), 4 + (turn + 1) // 2, own)


def second_pair_kernel(
    h_ref,
    cot_ref,
    kept_ref,
    router_ref,
    mixed_first,
    grad_h_first,
    gate_first,
    up_all,
    down_all,
    up_first,
    down_first,
    mixed_ref,
    grad_router_ref,
    grad_up_out,
    grad_down_out,
    grad_h_out,
    up_pair,
    down_pair,
    line_first,
    up_vm,
    down_vm,
    grad_up_ref,
    grad_down_ref,
    up_sum,
    down_sum,
    router_sum,
    ring,
    from_core,
    from_y,
    from_x,
    load,
    core_s,
    core_r,
    y_s,
    y_r,
    x_s,
    x_r,
    tot_s,
    tot_r,
    store,
    pair_s,
    pair_r,
    line_s,
    line_r,
    *,
    experts,
    steps,
):
    turn = pl.program_id(0)
    expert_at = lax.axis_index("expert")
    tensor_at = lax.axis_index("tensor")
    z_at, y_at = expert_at // 2, expert_at % 2
    x_at, core_at = tensor_at // 2, tensor_at % 2
    hidden = up_pair.shape[1]
    wide = ring.shape[3]
    core_dev = (expert_at, tensor_at + 1 - 2 * core_at)
    x_dev = (expert_at, tensor_at + 2 - 4 * x_at)
    y_dev = (expert_at + 1 - 2 * y_at, tensor_at)
    my_cols = lanes_at(core_at * wide, wide)

    def remote(src, dst, send, recv, device):
        return pltpu.make_async_remote_copy(
            src_ref=src, dst_ref=dst, send_sem=send, recv_sem=recv, device_id=device, device_id_type=MESH
        )

    def core_copy(number):
        return remote(ring.at[number % 2, 1 - core_at], from_core.at[number], core_s.at[number], core_r.at[number], core_dev)

    def y_copy(number, place):
        return remote(from_core.at[number], from_y.at[place], y_s.at[place], y_r.at[place], y_dev)

    def x_copy(number, place):
        return remote(from_core.at[number], from_x.at[place], x_s.at[place], x_r.at[place], x_dev)

    def out_rows(place):
        return grad_h_out.at[aligned(place * BLOCK, BLOCK), my_cols]

    def total_copy(place):
        return remote(from_x.at[place], out_rows(place), tot_s.at[place], tot_r.at[place], core_dev)

    def store_copy(place):
        return pltpu.make_async_copy(from_x.at[place], out_rows(place), store.at[place])

    def own_turn(place):
        return jnp.where(place == 3, 7, 2 * place + 2)

    def other_turn(place):
        return jnp.where(place == 0, 0, 2 * place - 1)

    def pass_other(number):
        core_copy(number).wait_recv()
        from_core[number] = from_core[number] + ring[number % 2, core_at]
        y_copy(number, (number + 1) // 2).start()

    def pass_own(number, place):
        core_copy(number).wait_recv()
        y_copy(number, place).wait_recv()
        total = from_core[number].astype(f32) + ring[number % 2, core_at].astype(f32) + from_y[place].astype(f32)
        from_core[number] = total.astype(bf16)
        x_copy(number, place).start()

    def pass_total(place):
        number = own_turn(place)
        x_copy(number, place).wait_recv()
        from_x[place] = from_core[number] + from_x[place]
        total_copy(place).start()
        store_copy(place).start()

    z_dev = (jnp.where(z_at % 2 == 0, expert_at + 2, expert_at - 2), tensor_at)
    pair_lanes = lanes_at((1 - z_at % 2) * hidden, hidden)
    pair_copies = [
        remote(source.at[:, pair_lanes], target, pair_s.at[number], pair_r.at[number], z_dev)
        for number, (source, target) in enumerate(((up_first, up_pair), (down_first, down_pair)))
    ]

    far_lanes = lanes_at(jnp.where(z_at == 0, 1, 0) * hidden, hidden)
    line_copy = remote(grad_up_ref.at[:, far_lanes], line_first, line_s.at[0], line_r.at[0], z_dev)
    is_outer = (z_at == 0) | (z_at == lax.axis_size("expert") // 2 - 1)

    grad_copies = [
        pltpu.make_async_copy(grad_up_ref, grad_up_out, load.at[2]),
        pltpu.make_async_copy(grad_down_ref, grad_down_out, load.at[3]),
    ]

    @pl.when(turn == 0)
    def _():
        whole = [
            pltpu.make_async_copy(up_all.at[1], up_vm, load.at[0]),
            pltpu.make_async_copy(down_all.at[1], down_vm, load.at[1]),
        ]
        for copy in whole:
            copy.start()
        greet([(True, core_dev), (True, x_dev), (True, y_dev), (True, z_dev)])
        for copy in pair_copies:
            copy.start()
        up_sum[...] = jnp.zeros_like(up_sum)
        down_sum[...] = jnp.zeros_like(down_sum)
        router_sum[...] = jnp.zeros_like(router_sum)
        for copy in whole:
            copy.wait()

    h_rows, cot_rows = h_ref[...], cot_ref[...]
    up, down, router = up_vm[...], down_vm[...], router_ref[...]
    kept = kept_ref[...].astype(f32)
    hidden_rows, grad_pre, probs, grad_gate = expert_math(
        h_rows, cot_rows, kept, router, up, down, 1 - z_at // 2, experts
    )
    grad_gate = kept * (grad_gate + gate_first[...])
    grad_logits = (probs * (grad_gate - jnp.sum(probs * grad_gate, axis=1, keepdims=True))).astype(bf16)

    before = turn - 1

    @pl.when((turn >= 1) & turn_is_other(before))
    def _():
        pass_other(before)

    @pl.when((turn == 5) | (turn == 7))
    def _():
        pass_total((turn - 5) // 2)

    @pl.when((turn == 3) | (turn == 5) | (turn == 7))
    def _():
        pass_own(before, (turn - 3) // 2)


    @pl.when(turn >= 2)
    def _():
        core_copy(turn - 2).wait_send()

    grad_h = (
        grad_h_first[...].astype(f32) + dot(grad_pre, up, ((1,), (1,))) + dot(grad_logits, router)
    ).astype(bf16)
    ring[turn % 2, 0] = grad_h[:, :wide]
    ring[turn % 2, 1] = grad_h[:, wide:]
    core_copy(turn).start()
    mixed_ref[...] = (mixed_first[...].astype(f32) + dot(hidden_rows, down)).astype(bf16)
    h_turned = h_rows.T
    up_sum[...] += dot(h_turned, grad_pre)
    router_sum[...] += dot(h_turned, grad_logits)
    down_sum[...] += dot(cot_rows.T, hidden_rows)

    @pl.when(turn == steps - 1)
    def _():
        grad_up_ref[...] = up_sum[...].astype(bf16)
        grad_copies[0].start()

        @pl.when(is_outer)
        def _():
            line_copy.start()

        pass_own(7, 3)
        pass_total(2)
        grad_down_ref[...] = down_sum[...].astype(bf16)
        grad_copies[1].start()
        grad_router_ref[...] = router_sum[...].T[:8]
        pass_total(3)
        for copy in (*pair_copies, *grad_copies):
            copy.wait()

        @pl.when(is_outer)
        def _():
            line_copy.wait_send()

        @pl.when(jnp.logical_not(is_outer))
        def _():
            line_copy.wait_recv()

        for number in (6, 7):
            core_copy(number).wait_send()
        for place in range(4):
            y_copy(other_turn(place), place).wait_send()
            x_copy(own_turn(place), place).wait_send()
            total_copy(place).wait_send()
            total_copy(place).wait_recv()
            store_copy(place).wait()


def run_second_pair(
    h_rows,
    cot_rows,
    kept,
    router,
    mixed_first,
    grad_h_first,
    gate_first,
    up,
    down,
    up_first,
    down_first,
    experts,
):
    rows, features = h_rows.shape
    width = up.shape[2]
    steps = rows // BLOCK
    half = (BLOCK, features // 2)
    anywhere = pl.BlockSpec(memory_space=pl.ANY)
    shape = jax.ShapeDtypeStruct
    dma = pltpu.SemaphoreType.DMA

    def by_step(lanes):
        return pl.BlockSpec((BLOCK, lanes), lambda n: (turn_block(n), 0))

    def whole(*dims):
        return pl.BlockSpec(dims, lambda n: (0,) * len(dims))

    return pl.pallas_call(
        partial(second_pair_kernel, experts=experts, steps=steps),
        grid=(steps,),
        out_shape=[
            shape((rows, features), bf16),
            shape((8, features), f32),
            shape((features, width), bf16),
            shape((features, width), bf16),
            shape((rows // 2, features), bf16),
            shape((features, width // 2), bf16),
            shape((features, width // 2), bf16),
            shape((features, width // 2), bf16),
        ],
        in_specs=[
            by_step(features),
            by_step(features),
            by_step(128),
            whole(128, features),
            by_step(features),
            by_step(features),
            by_step(128),
        ]
        + [anywhere] * 4,
        out_specs=[by_step(features), whole(8, features)] + [anywhere] * 6,
        scratch_shapes=[
            pltpu.VMEM((features, width), bf16),
            pltpu.VMEM((width, features), bf16),
            *[pltpu.VMEM((features, width), bf16)] * 2,
            pltpu.VMEM((features, width), f32),
            pltpu.VMEM((features, width), f32),
            pltpu.VMEM((features, 128), f32),
            pltpu.VMEM((2, 2, *half), bf16),
            pltpu.VMEM((8, *half), bf16),
            pltpu.VMEM((4, *half), bf16),
            pltpu.VMEM((4, *half), bf16),
            dma((4,)),
        ]
        + [dma((8,))] * 2
        + [dma((4,))] * 7
        + [dma((2,))] * 2
        + [dma((1,))] * 2,
        compiler_params=pltpu.CompilerParams(
            collective_id=4, has_side_effects=True, vmem_limit_bytes=60 << 20
        ),
    )(h_rows, cot_rows, kept, router, mixed_first, grad_h_first, gate_first, up, down, up_first, down_first)


def backward_kernel(
    gain1_ref,
    shift1_ref,
    gain2_ref,
    grad_router_ref,
    qkv_hbm,
    out_w_hbm,
    tok_hbm,
    q_hbm,
    k_hbm,
    v_hbm,
    att_hbm,
    lse_hbm,
    grad_h_hbm,
    resid_ref,
    cot_ref,
    mixed_ref,
    up_second,
    down_second,
    line_first,
    line_out,
    tokens_out,
    weights_out,
    sums_out,
    mixed_out,
    qkv_ref,
    out_w_ref,
    tok_ref,
    q_ref,
    k_ref,
    v_ref,
    att_ref,
    lse_ref,
    grad_h_ref,
    rows_kept,
    cot_rows,
    m_mine,
    m_core,
    m_y,
    m_x,
    m_out,
    m_resid,
    far_vm,
    one_mine,
    one_to,
    one_core,
    one_x,
    one_total,
    line,
    weight_sum,
    weight_half,
    shared,
    shared_y,
    shared_line,
    shared_all,
    route_core,
    route_x,
    late_mine,
    late_y,
    late_z,
    sums_all,
    tokens_low,
    whole,
    mc_s,
    mc_r,
    my_s,
    my_r,
    mx_s,
    mx_r,
    mq_s,
    mq_r,
    m_store,
    oc_s,
    oc_r,
    ox_s,
    ox_r,
    ot_s,
    ot_r,
    l_s,
    l_r,
    sy_s,
    sy_r,
    sl_s,
    sl_r,
    sg_s,
    sg_r,
    sz_s,
    sz_r,
    r_s,
    r_r,
    late_s,
    late_r,
    load,
    image_load,
    own_sem,
    weight_store,
    store,
    *,
    images,
    heads,
):
    expert_at = lax.axis_index("expert")
    tensor_at = lax.axis_index("tensor")
    z_at, y_at = expert_at // 2, expert_at % 2
    z_last = lax.axis_size("expert") // 2 - 1
    x_at, core_at = tensor_at // 2, tensor_at % 2
    other = 1 - core_at
    rows = images * PITCH
    features = tok_hbm.shape[2]
    wide = features // 2
    share = out_w_ref.shape[0]
    hidden = line.shape[3]
    core_dev = (expert_at, tensor_at + 1 - 2 * core_at)
    x_dev = (expert_at, tensor_at + 2 - 4 * x_at)
    y_dev = (expert_at + 1 - 2 * y_at, tensor_at)
    z_devs = [(expert_at + 2, tensor_at), (expert_at - 2, tensor_at)]
    planes = z_last + 1
    z_others = [((z_at + hop) % planes * 2 + y_at, tensor_at) for hop in (1, 2, 3)]
    greet([(True, device) for device in (core_dev, x_dev, y_dev, *z_others)])
    my_cols = lanes_at(core_at * wide, wide)
    their_cols = lanes_at(other * wide, wide)

    def remote(src, dst, send, recv, device):
        return pltpu.make_async_remote_copy(
            src_ref=src, dst_ref=dst, send_sem=send, recv_sem=recv, device_id=device, device_id_type=MESH
        )

    def at_image(image):
        return aligned(image * PITCH, PITCH)

    def place(way):
        return z_at if way == 0 else z_last - z_at

    def far_lanes(way, piece):
        expert = z_last - piece // 2 if way == 0 else piece // 2
        return pl.ds(expert % 2 * hidden, hidden)

    def line_copy(source, way, piece):
        return remote(source, line.at[way, piece], l_s.at[way, piece], l_r.at[way, piece], z_devs[way])

    def line_copy_on(way, piece):
        return line_copy(line.at[way, piece], way, piece)

    def line_start():
        for way in range(2):

            @pl.when(place(way) == 0)
            def _():
                for piece in range(1, 4):
                    source = (up_second, down_second)[piece % 2]
                    line_copy(source.at[:, far_lanes(way, piece)], way, piece).start()

    def line_add(piece):
        for way in range(2):

            @pl.when(place(way) == 1)
            def _():
                if piece > 0:
                    line_copy_on(way, piece).wait_recv()
                lanes = far_lanes(way, piece)

                def add(part, _):
                    at_rows = aligned(part * 96, 96)
                    total = line[way, piece, at_rows, :].astype(f32) + far_vm[piece % 2, at_rows, lanes].astype(f32)
                    line[way, piece, at_rows, :] = total.astype(bf16)
                    return 0

                lax.fori_loop(0, features // 96, add, 0)
                line_copy_on(way, piece).start()

    part_height = line.shape[2] // 4

    def line_part_copy(way, part):
        ref = line.at[way, 3, pl.ds(part * part_height, part_height)]
        return remote(ref, ref, l_s.at[way, 3 + part], l_r.at[way, 3 + part], z_devs[way])

    def line_part(part):
        for way in range(2):

            @pl.when(place(way) == 1)
            def _():
                if part == 0:
                    line_copy_on(way, 3).wait_recv()
                lanes = far_lanes(way, 3)
                for piece in range(2):
                    at_rows = pl.ds(part * part_height + piece * part_height // 2, part_height // 2)
                    total = line[way, 3, at_rows, :].astype(f32) + far_vm[1, at_rows, lanes].astype(f32)
                    line[way, 3, at_rows, :] = total.astype(bf16)
                line_part_copy(way, part).start()

    def line_pass(piece):
        for way in range(2):

            @pl.when(place(way) == 2)
            def _():
                line_copy_on(way, piece).wait_recv()
                line_copy_on(way, piece).start()

    line_start()
    later = [
        pltpu.make_async_copy((up_second, down_second)[number], far_vm.at[number], own_sem.at[number])
        for number in range(2)
    ]
    is_inner = (z_at == 1) | (z_at == z_last - 1)
    first_copy = pltpu.make_async_copy(line_first, line.at[jnp.where(z_at == 1, 0, 1), 0], own_sem.at[2])

    @pl.when(is_inner)
    def _():
        first_copy.start()

    for copy in later:
        copy.start()

    part_count = m_y.shape[0]
    part_rows_m = rows // part_count

    def m_rows(side, part):
        return aligned(side * rows + part * part_rows_m, part_rows_m)

    def m_core_copy(side, part):
        at = m_rows(side, part)
        return remote(mixed_ref.at[at, their_cols], m_core.at[at, :], mc_s.at[side, part], mc_r.at[side, part], core_dev)

    for part in range(part_count):
        m_core_copy(1, part).start()
    for part in range(part_count):
        m_core_copy(0, part).start()
    m_loads = [
        pltpu.make_async_copy(mixed_ref.at[pl.ds(side * rows, rows), my_cols], m_mine.at[pl.ds(side * rows, rows), :], load.at[side])
        for side in range(2)
    ]

    def image_loads(image):
        at = at_image(image)
        by_image = ((tok_hbm, tok_ref), (q_hbm, q_ref), (k_hbm, k_ref), (v_hbm, v_ref), (att_hbm, att_ref), (lse_hbm, lse_ref))
        by_row = ((grad_h_hbm, grad_h_ref), (resid_ref, rows_kept), (cot_ref, cot_rows))
        pairs = [(source.at[image], target.at[image]) for source, target in by_image]
        pairs += [(source.at[at, :], target.at[at, :]) for source, target in by_row]
        return [pltpu.make_async_copy(source, target, image_load.at[n, image]) for n, (source, target) in enumerate(pairs)]

    def start_loads(image, _):
        for copy in image_loads(image):
            copy.start()
        return 0

    weight_loads = [
        pltpu.make_async_copy(qkv_hbm, qkv_ref, own_sem.at[3]),
        pltpu.make_async_copy(out_w_hbm, out_w_ref, own_sem.at[4]),
    ]
    for copy in weight_loads:
        copy.start()
    start_loads(0, 0)
    m_loads[1].start()
    lax.fori_loop(1, images, start_loads, 0)
    m_loads[0].start()
    route_one = remote(grad_router_ref, route_core, r_s.at[0], r_r.at[0], core_dev)
    route_one.start()

    weight_sum[...] = jnp.zeros_like(weight_sum)
    late_mine[...] = jnp.zeros_like(late_mine)

    def m_y_copy(part):
        return remote(m_core.at[m_rows(1, part), :], m_y.at[part], my_s.at[part], my_r.at[part], y_dev)

    def m_x_copy(part):
        return remote(m_core.at[m_rows(0, part), :], m_x.at[part], mx_s.at[part], mx_r.at[part], x_dev)

    def m_place(part):
        return mixed_out.at[aligned(part * part_rows_m, part_rows_m), :]

    def m_quarter_copy(part):
        return remote(m_out.at[part, other], m_place(part), mq_s.at[part], mq_r.at[part], core_dev)

    def m_store_copy(part):
        return pltpu.make_async_copy(m_out.at[part, core_at], m_place(part), m_store.at[part])

    def m_resid_copy(part):
        at = aligned(part * part_rows_m, part_rows_m)
        return pltpu.make_async_copy(resid_ref.at[at, lanes_at(x_at * wide, wide)], m_resid, load.at[3])

    keeps = x_at == core_at

    def run_m_y(part):
        m_core_copy(1, part).wait_recv()
        at = m_rows(1, part)
        m_core[at, :] = (m_core[at, :].astype(f32) + m_mine[at, :].astype(f32)).astype(bf16)
        m_y_copy(part).start()

    def run_m_x(part):
        if isinstance(part, int) and part == 0:
            m_loads[0].wait()
        m_core_copy(0, part).wait_recv()
        m_y_copy(part).wait_recv()
        at = m_rows(0, part)
        total = m_core[at, :].astype(f32) + m_mine[at, :].astype(f32) + m_y[part].astype(f32)
        m_core[at, :] = total.astype(bf16)

        @pl.when(jnp.logical_not(keeps))
        def _():
            m_x_copy(part).start()

    def run_m_out(part):
        @pl.when(keeps)
        def _():
            m_resid_copy(part).start()
            m_x_copy(part).wait_recv()
            m_resid_copy(part).wait()
            total = m_core[m_rows(0, part), :].astype(f32) + m_x[part].astype(f32)
            mixed = (m_resid[...] + total).astype(bf16)
            m_out[part, 0] = mixed[:, : wide // 2]
            m_out[part, 1] = mixed[:, wide // 2 :]
            m_quarter_copy(part).start()
            m_store_copy(part).start()

    later[0].wait()
    later[1].wait()

    @pl.when(is_inner)
    def _():
        first_copy.wait()

    line_add(0)
    m_loads[1].wait()
    for part in range(part_count):
        run_m_y(part)
    route_one.wait_recv()
    route_core[...] += grad_router_ref[...]
    route_two = remote(route_core, route_x, r_s.at[1], r_r.at[1], x_dev)
    route_two.start()

    def one_core_copy(image):
        return remote(one_to.at[image], one_core.at[image], oc_s.at[image], oc_r.at[image], core_dev)

    def one_x_copy(image):
        return remote(one_core.at[image], one_x.at[image], ox_s.at[image], ox_r.at[image], x_dev)

    def one_total_copy(image):
        return remote(one_x.at[image], one_total.at[image], ot_s.at[image], ot_r.at[image], core_dev)

    store_copy = pltpu.make_async_copy(tokens_low, tokens_out, store.at[0])

    lane = lax.broadcasted_iota(jnp.int32, (PITCH, 2 * HD), 1)
    key_mask = lax.broadcasted_iota(jnp.int32, (PITCH, PITCH), 1) < SEQ
    gain1, shift1, gain2 = (ref[...].reshape(1, features) for ref in (gain1_ref, shift1_ref, gain2_ref))

    def norm_back(grad, gain, normed, inverse):
        scaled = grad * gain
        mean = jnp.mean(scaled, axis=1, keepdims=True)
        along = jnp.mean(scaled * normed, axis=1, keepdims=True)
        return (scaled - mean - normed * along) * inverse

    def add_sums(sums, row, grad, normed):
        sums[row : row + 1, :] += jnp.sum(grad * normed, axis=0, keepdims=True)
        sums[row + 1 : row + 2, :] += jnp.sum(grad, axis=0, keepdims=True)

    def run_attention(image):
        for copy in image_loads(image):
            copy.wait()
        at = at_image(image)
        grad_h = grad_h_ref[at, :].astype(f32)
        normed, inverse = norm_stats(rows_kept[at, :])
        add_sums(late_mine, 2, grad_h, normed)
        grad_resid = cot_rows[at, :].astype(f32) + norm_back(grad_h, gain2, normed, inverse)
        rows_kept[at, :] = grad_resid
        grad_branch = grad_resid.astype(bf16)
        token_normed, _ = norm_stats(tok_ref[image].astype(f32))
        h_one = (token_normed * gain1 + shift1).astype(bf16)
        queries, keys, values, attended = q_ref[image], k_ref[image], v_ref[image], att_ref[image]
        lse = lse_ref[image]
        grad_attended = dot(grad_branch, out_w_ref[...], ((1,), (1,))).astype(bf16)
        grads = [[], [], []]
        for head in range(heads):
            first = head // 2 * 2 * HD
            last = min(first + 2 * HD, heads * HD)
            parts = [whose[:, first:last] for whose in (queries, keys, values, grad_attended)]
            if last - first == 2 * HD:
                own = head_mask(lane, head)
                q_own, k_own, _, g_own = (jnp.where(own, part, jnp.zeros_like(part)) for part in parts)
            else:
                q_own, k_own, _, g_own = parts
            scores = dot(q_own, parts[1], ((1,), (1,))) * (HD**-0.5)
            probs = jnp.where(key_mask, jnp.exp(scores - lse[:, head : head + 1]), 0.0)
            back = dot(g_own, parts[2], ((1,), (1,)))
            product = probs * back
            grad_scores = (product - probs * jnp.sum(product, axis=1, keepdims=True)).astype(bf16)
            pieces = (
                dot(grad_scores, k_own) * (HD**-0.5),
                dot(grad_scores, q_own, ((0,), (0,))) * (HD**-0.5),
                dot(probs.astype(bf16), g_own, ((0,), (0,))),
            )
            for which in range(3):
                if head % 2 == 0:
                    grads[which].append(pieces[which])
                else:
                    grads[which][-1] += pieces[which]
        grad_rows = [jnp.concatenate(grads[which], axis=1).astype(bf16) for which in range(3)]
        grad_one = 0.0
        for which in range(3):
            weight_sum[which * share : (which + 1) * share, :] += dot(grad_rows[which].T, h_one)
            grad_one += dot(grad_rows[which], qkv_ref[which])
        weight_sum[3 * share : 4 * share, :] += dot(attended.T, grad_branch)
        whole[...] = grad_one
        one_mine[image] = whole[:, my_cols].astype(bf16)
        one_to[image] = whole[:, their_cols].astype(bf16)
        one_core_copy(image).start()

    def run_one_x(image):
        one_core_copy(image).wait_recv()
        one_core[image] = (one_core[image].astype(f32) + one_mine[image].astype(f32)).astype(bf16)
        one_x_copy(image).start()

    def run_one_total(image):
        one_x_copy(image).wait_recv()
        one_x[image] = (one_core[image].astype(f32) + one_x[image].astype(f32)).astype(bf16)
        one_total_copy(image).start()

    def run_tokens(image):
        one_total_copy(image).wait_recv()
        whole[:, my_cols] = one_x[image].astype(f32)
        whole[:, their_cols] = one_total[image].astype(f32)
        grad_one = whole[...]
        at = at_image(image)
        normed, inverse = norm_stats(tok_ref[image].astype(f32))
        add_sums(late_mine, 0, grad_one, normed)
        total = rows_kept[at, :] + norm_back(grad_one, gain1, normed, inverse)
        whole[...] = total
        for number in range(images):

            @pl.when(image == number)
            def _():
                rows_kept[pl.ds(number * SEQ, SEQ), :] = whole[pl.ds(0, SEQ), :]


    def stage(tick, lag, run):
        image = tick - lag

        @pl.when((image >= 0) & (image < images))
        def _():
            run(image)

    def at_tick(tick, when, run):
        @pl.when(tick == when)
        def _():
            run()

    def line_second():
        line_add(1)
        line_pass(0)

    def line_third():
        line_add(2)
        line_pass(1)

    def per_tick(tick, _):
        stage(tick, 0, run_attention)
        stage(tick, 1, run_one_x)
        stage(tick, 4, run_one_total)
        stage(tick, 5, run_tokens)
        at_tick(tick, 5, lambda: run_m_x(0))
        at_tick(tick, 3, line_second)
        at_tick(tick, 6, line_third)
        at_tick(tick, 7, lambda: run_m_x(1))
        return 0

    for copy in weight_loads:
        copy.wait()
    lax.fori_loop(0, images, per_tick, 0)

    part_rows = shared.shape[1]
    chunks = 2
    chunk_rows = part_rows // chunks
    quarter = chunk_rows // planes

    def cast(piece, _):
        for side in range(2):
            at_rows = aligned(piece * 96, 96)
            shared[side, at_rows, :] = weight_sum[aligned(side * part_rows + piece * 96, 96), :].astype(bf16)
        return 0

    lax.fori_loop(0, part_rows // 96, cast, 0)

    def y_piece(number):
        inner = jnp.where(z_at == 1, jnp.where(number < 2, z_last - number, number - 2), jnp.where(number < 2, number, 5 - number))
        return jnp.where(z_at == 0, z_last - number, jnp.where(z_at == z_last, number, inner))

    def quarter_at(chunk, piece):
        return aligned(chunk * chunk_rows + piece * quarter, quarter)

    def shared_y_copy(chunk, number):
        at_rows = quarter_at(chunk, y_piece(number))
        return remote(
            shared.at[1 - y_at, at_rows, :], shared_y.at[at_rows, :], sy_s.at[chunk, number], sy_r.at[chunk, number], y_dev
        )

    def take_y(chunk, number):
        shared_y_copy(chunk, number).wait_recv()
        at_rows = quarter_at(chunk, y_piece(number))
        weight_half[at_rows, :] = shared[y_at, at_rows, :].astype(f32) + shared_y[at_rows, :].astype(f32)

    def quarter_of(step, at, way):
        mirrored = z_last - step + at
        return mirrored if way == 0 else z_last - mirrored

    def small_copy(chunk, step, way):
        return remote(
            shared_line.at[chunk, way, 0, step],
            shared_line.at[chunk, way, 1, step],
            sl_s.at[chunk, way, step],
            sl_r.at[chunk, way, step],
            z_devs[way],
        )

    def sum_wait(chunk, step):
        for way in range(2):
            at = place(way)

            @pl.when((at > 0) & (at - 1 <= step))
            def _():
                small_copy(chunk, step, way).wait_recv()

    def sum_send(chunk, step):
        for way in range(2):
            at = place(way)

            @pl.when((at <= step) & (at < z_last))
            def _():
                at_rows = quarter_at(chunk, quarter_of(step, at, way))
                if step == 0:
                    shared_line[chunk, way, 0, step] = weight_half[at_rows, :].astype(bf16)
                else:
                    came = jnp.where(at > 0, shared_line[chunk, way, 1, step - 1].astype(f32), 0.0)
                    shared_line[chunk, way, 0, step] = (weight_half[at_rows, :] + came).astype(bf16)
                small_copy(chunk, step, way).start()

    def final_rows(chunk, side, piece):
        return shared_all.at[side, quarter_at(chunk, piece), :]

    def gather_z(chunk, step, way, piece):
        ref = final_rows(chunk, y_at, piece)
        return remote(ref, ref, sg_s.at[chunk, way, step], sg_r.at[chunk, way, step], z_devs[way])

    def gather_y(chunk, step, way, piece, side):
        ref = final_rows(chunk, side, piece)
        return remote(ref, ref, sz_s.at[chunk, way, step], sz_r.at[chunk, way, step], y_dev)

    def piece_out(step, way):
        return z_at - step if way == 0 else z_at + step

    def piece_in(step, way):
        return z_at - 1 - step if way == 0 else z_at + 1 + step

    def gather_send(chunk, step):
        for way in range(2):
            at = place(way)

            @pl.when((at >= step) & (at < z_last))
            def _():
                gather_z(chunk, step, way, piece_out(step, way)).start()

    def gather_take(chunk, step):
        for way in range(2):

            @pl.when(place(way) >= 1 + step)
            def _():
                gather_z(chunk, step, way, piece_in(step, way)).wait_recv()
                gather_y(chunk, step + 1, way, piece_in(step, way), y_at).start()

    def finish_sum(chunk):
        own_rows = quarter_at(chunk, z_at)
        from_below = jnp.where(z_at > 0, shared_line[chunk, 0, 1, 2].astype(f32), 0.0)
        from_above = jnp.where(z_at < z_last, shared_line[chunk, 1, 1, 2].astype(f32), 0.0)
        shared_all[y_at, own_rows, :] = (weight_half[own_rows, :] + from_below + from_above).astype(bf16)
        gather_y(chunk, 0, 0, z_at, y_at).start()

    late_y_copy = remote(late_mine, late_y, late_s.at[0], late_r.at[0], y_dev)

    def late_copy(number):
        ref = late_z.at[z_at]
        return remote(ref, ref, late_s.at[number + 1], late_r.at[number + 1], z_others[number])

    def meanwhile(place_in_order):
        if place_in_order == 0:
            run_one_x(images - 1)
            run_tokens(images - 5)
            run_one_total(images - 4)
            run_m_x(part_count - 2)
        if place_in_order == 1:
            run_m_x(part_count - 1)
            run_tokens(images - 4)
            run_one_total(images - 3)
        if place_in_order == 2:
            run_m_out(0)
            run_tokens(images - 3)
        if place_in_order == 3:
            line_part(0)
            run_one_total(images - 2)
            run_m_out(1)
            run_tokens(images - 2)
        if place_in_order == 4:
            line_part(1)
            run_one_total(images - 1)
            run_m_out(2)
        if place_in_order == 5:
            line_part(2)
            run_tokens(images - 1)
            route_two.wait_recv()
            late_mine[8:16, :] = route_core[...] + route_x[...]
            late_y_copy.start()
            tokens_low[...] = rows_kept[pl.ds(0, images * SEQ), :].astype(bf16)
            store_copy.start()
        if place_in_order == 6:
            line_part(3)
            run_m_out(3)
            late_y_copy.wait_recv()
            late_z[z_at] = late_mine[...] + late_y[...]
            for number in range(planes - 1):
                late_copy(number).start()

    for number in range(4):
        for chunk in range(chunks):
            shared_y_copy(chunk, number).start()
    meanwhile(0)
    for step in range(3):
        for chunk in range(chunks):
            if step > 0:
                sum_wait(chunk, step - 1)
            take_y(chunk, step)
            sum_send(chunk, step)
        if step == 2:
            for chunk in range(chunks):
                take_y(chunk, 3)
        meanwhile(1 + step)
    for chunk in range(chunks):
        sum_wait(chunk, 2)
        finish_sum(chunk)
        gather_send(chunk, 0)
    for step in range(3):
        meanwhile(4 + step)
        for chunk in range(chunks):
            gather_take(chunk, step)
            if step < 2:
                gather_send(chunk, step + 1)

    for way in range(2):

        @pl.when(place(way) == 2)
        def _():
            line_copy_on(way, 2).wait_recv()
            for part in range(4):
                line_part_copy(way, part).wait_recv()

        @pl.when(place(way) == z_last)
        def _():
            line_copy_on(way, 0).wait_recv()
            line_copy_on(way, 1).wait_recv()

    from_far = 1 - z_at // 2
    first_piece = jnp.where((z_at == 0) | (z_at == z_last), 0, 2)

    line_out_copies = [
        pltpu.make_async_copy(line.at[from_far, first_piece + n], line_out.at[n], weight_store.at[n]) for n in range(2)
    ]
    for copy in line_out_copies:
        copy.start()
    for chunk in range(chunks):
        gather_y(chunk, 0, 0, z_at, 1 - y_at).wait_recv()
        for step in range(3):
            for way in range(2):

                @pl.when(place(way) >= 1 + step)
                def _():
                    gather_y(chunk, step + 1, way, piece_in(step, way), 1 - y_at).wait_recv()

    for number in range(planes - 1):
        late_copy(number).wait_recv()
    late = late_z[0]
    for plane in range(1, planes):
        late += late_z[plane]
    sums_all[...] = late
    out_copies = [
        pltpu.make_async_copy(shared_all, weights_out, weight_store.at[2]),
        pltpu.make_async_copy(sums_all, sums_out, weight_store.at[3]),
    ]
    for copy in out_copies:
        copy.start()
    route_one.wait_send()
    route_two.wait_send()

    def drain(image, _):
        for copy in (one_core_copy, one_x_copy, one_total_copy):
            copy(image).wait_send()
        return 0

    lax.fori_loop(0, images, drain, 0)
    for part in range(part_count):
        m_core_copy(0, part).wait_send()
        m_core_copy(1, part).wait_send()
        m_y_copy(part).wait_send()

        @pl.when(keeps)
        def _():
            m_quarter_copy(part).wait_send()
            m_store_copy(part).wait()

        @pl.when(jnp.logical_not(keeps))
        def _():
            m_x_copy(part).wait_send()
            m_quarter_copy(part).wait_recv()

    for copy in (*line_out_copies, *out_copies, store_copy):
        copy.wait()
    late_y_copy.wait_send()
    for number in range(planes - 1):
        late_copy(number).wait_send()
    for way in range(2):

        @pl.when(place(way) == 0)
        def _():
            for piece in range(1, 4):
                line_copy_on(way, piece).wait_send()

        @pl.when(place(way) == 1)
        def _():
            for piece in range(3):
                line_copy_on(way, piece).wait_send()
            for part in range(4):
                line_part_copy(way, part).wait_send()

        @pl.when(place(way) == 2)
        def _():
            for piece in range(2):
                line_copy_on(way, piece).wait_send()

    for chunk in range(chunks):
        gather_y(chunk, 0, 0, z_at, y_at).wait_send()
        for number in range(4):
            shared_y_copy(chunk, number).wait_send()
        for step in range(3):
            for way in range(2):
                at = place(way)

                @pl.when((at <= step) & (at < z_last))
                def _():
                    small_copy(chunk, step, way).wait_send()

                @pl.when((at >= step) & (at < z_last))
                def _():
                    gather_z(chunk, step, way, piece_out(step, way)).wait_send()

                @pl.when(at >= 1 + step)
                def _():
                    gather_y(chunk, step + 1, way, piece_in(step, way), y_at).wait_send()


def run_backward(gain1, shift1, gain2, grad_router, qkv_w, out_w, tok, *streamed):
    images, _, features = tok.shape
    rows = images * PITCH
    share = out_w.shape[0]
    heads = share // HD
    hidden = streamed[-1].shape[1]
    wide = features // 2
    parts = 4
    vmem = pl.BlockSpec(memory_space=pltpu.VMEM)
    anywhere = pl.BlockSpec(memory_space=pl.ANY)
    shape = jax.ShapeDtypeStruct
    dma = pltpu.SemaphoreType.DMA
    block = (images, PITCH, wide)
    return pl.pallas_call(
        partial(backward_kernel, images=images, heads=heads),
        out_shape=[
            shape((2, features, hidden), bf16),
            shape((images * SEQ, features), bf16),
            shape((2, features // 2, features), bf16),
            shape((16, features), f32),
            shape((rows, wide // 2), bf16),
        ],
        in_specs=[vmem] * 4 + [anywhere] * (3 + len(streamed)),
        out_specs=[anywhere] * 5,
        scratch_shapes=[
            pltpu.VMEM(qkv_w.shape, bf16),
            pltpu.VMEM(out_w.shape, bf16),
            pltpu.VMEM((images, PITCH, features), bf16),
            *[pltpu.VMEM((images, PITCH, share), bf16)] * 4,
            pltpu.VMEM((images, PITCH, 128), f32),
            pltpu.VMEM((rows, features), bf16),
            pltpu.VMEM((rows, features), f32),
            pltpu.VMEM((rows, features), bf16),
            pltpu.VMEM((2 * rows, wide), bf16),
            pltpu.VMEM((2 * rows, wide), bf16),
            *[pltpu.VMEM((parts, rows // parts, wide), bf16)] * 2,
            pltpu.VMEM((parts, 2, rows // parts, wide // 2), bf16),
            pltpu.VMEM((rows // parts, wide), f32),
            pltpu.VMEM((2, features, 2 * hidden), bf16),
            *[pltpu.VMEM(block, bf16)] * 5,
            pltpu.VMEM((2, 4, features, hidden), bf16),
            pltpu.VMEM((features, features), f32),
            pltpu.VMEM((features // 2, features), f32),
            pltpu.VMEM((2, features // 2, features), bf16),
            pltpu.VMEM((features // 2, features), bf16),
            pltpu.VMEM((2, 2, 2, 3, features // 16, features), bf16),
            pltpu.VMEM((2, features // 2, features), bf16),
            *[pltpu.VMEM((8, features), f32)] * 2,
            *[pltpu.VMEM((16, features), f32)] * 2,
            pltpu.VMEM((4, 16, features), f32),
            pltpu.VMEM((16, features), f32),
            pltpu.VMEM((images * SEQ, features), bf16),
            pltpu.VMEM((PITCH, features), f32),
        ]
        + [dma((2, parts))] * 2
        + [dma((parts,))] * 7
        + [dma((images,))] * 6
        + [dma((2, 7))] * 2
        + [dma((2, 4))] * 2
        + [dma((2, 2, 3))] * 4
        + [dma((2, 2, 4))] * 2
        + [dma((2,))] * 2
        + [dma((4,))] * 2
        + [dma((4,)), dma((9, images)), dma((5,)), dma((4,)), dma((1,))],
        compiler_params=pltpu.CompilerParams(
            collective_id=2, has_side_effects=True, vmem_limit_bytes=63 << 20
        ),
    )(gain1, shift1, gain2, grad_router, qkv_w, out_w, tok, *streamed)


def last_kernel(
    side_ref, tokens_ref, weights_ref, up_first, up_pair, down_first, down_pair, line_ref, tokens_out, qkv_out, out_w_out, up_out, down_out
):
    share = out_w_out.shape[0]
    tokens_out[...] = tokens_ref[...].astype(f32)
    for which in range(3):
        qkv_out[which] = weights_ref[which * share : (which + 1) * share, :].astype(f32)
    out_w_out[...] = weights_ref[3 * share :, :].astype(f32)
    up_out[...] = up_first[...].astype(f32) + up_pair[...].astype(f32) + line_ref[0].astype(f32)
    down_out[...] = (down_first[...].astype(f32) + down_pair[...].astype(f32) + line_ref[1].astype(f32)).T


def run_last(side, tokens, weights, up_first, up_pair, down_first, down_pair, line, share):
    rows, features = tokens.shape
    hidden = up_pair.shape[1]
    shape = jax.ShapeDtypeStruct

    def lanes(height):
        return pl.BlockSpec((height, 128), lambda n, side: (0, n))

    own = pl.BlockSpec((128, hidden), lambda n, side: (n, side[0]))
    plain = pl.BlockSpec((128, hidden), lambda n, side: (n, 0))
    return pl.pallas_call(
        last_kernel,
        grid_spec=pltpu.PrefetchScalarGridSpec(
            num_scalar_prefetch=1,
            grid=(features // 128,),
            in_specs=[
                lanes(rows),
                lanes(features),
                own,
                plain,
                own,
                plain,
                pl.BlockSpec((2, 128, hidden), lambda n, side: (0, n, 0)),
            ],
            out_specs=[
                lanes(rows),
                pl.BlockSpec((3, share, 128), lambda n, side: (0, 0, n)),
                lanes(share),
                plain,
                lanes(hidden),
            ],
        ),
        out_shape=[
            shape((rows, features), f32),
            shape((3, share, features), f32),
            shape((share, features), f32),
            shape((features, hidden), f32),
            shape((hidden, features), f32),
        ],
    )(side, tokens, weights, up_first, up_pair, down_first, down_pair, line)


def per_image(rows_in):
    images = rows_in.shape[0] // SEQ
    blocks = rows_in.reshape(images, SEQ, rows_in.shape[1])
    return jnp.pad(blocks, ((0, 0), (0, PITCH - SEQ), (0, 0)))


def unpad(blocks):
    images = blocks.shape[0]
    return blocks[:, :SEQ].reshape(images * SEQ, blocks.shape[2])


def per_device_dense(
    tokens,
    gain_attn,
    shift_attn,
    qkv_weight,
    out_weight,
    gain_moe,
    shift_moe,
    router_weight,
    expert_up,
    expert_down,
    routes,
    keep_mask,
    cotangent,
):
    row_count, feature_count = tokens.shape
    images = row_count // SEQ
    rows = images * PITCH
    tensor_count = lax.axis_size("tensor")
    quarter_width = feature_count // tensor_count
    experts_all = router_weight.shape[1]
    hidden = expert_up.shape[2]
    kept_routes = per_image(jnp.where(keep_mask > 0, routes, -1) + 1).reshape(rows, 2) - 1
    expert_lane = jnp.arange(128, dtype=jnp.int32)[None, :]
    kept = ((kept_routes[:, 0:1] == expert_lane) | (kept_routes[:, 1:2] == expert_lane)).astype(bf16)
    cot_turned = cotangent.T
    qkv_turned = jnp.swapaxes(qkv_weight, 1, 2)
    (
        queries,
        keys,
        values,
        attended,
        lse,
        resid,
        h_all,
        cot_all,
        kept_all,
        up_all,
        down_all,
        mixed_first,
        grad_h_first,
        gate_first,
        up_first,
        down_first,
        tok,
        router_wide,
    ) = run_forward(
        tokens,
        gain_attn,
        shift_attn,
        gain_moe,
        shift_moe,
        qkv_turned,
        out_weight,
        expert_up[0],
        expert_down[0],
        router_weight.T,
        cot_turned,
        kept,
        experts_all,
    )
    mixed_part, grad_router, up_second, down_second, grad_h_two, up_pair, down_pair, line_first = run_second_pair(
        h_all,
        cot_all,
        kept_all,
        router_wide,
        mixed_first,
        grad_h_first,
        gate_first,
        up_all,
        down_all,
        up_first,
        down_first,
        experts_all,
    )
    line_sum, tokens_grad, weights_grad, sums, mixed = run_backward(
        gain_attn,
        shift_attn,
        gain_moe,
        grad_router,
        qkv_turned,
        out_weight,
        tok,
        queries,
        keys,
        values,
        attended,
        lse,
        grad_h_two,
        resid,
        cot_all,
        mixed_part,
        up_second,
        down_second,
        line_first,
    )
    side = (lax.axis_index("expert") // 2 % 2).astype(jnp.int32)[None]
    grad_tokens, grad_qkv, grad_out, grad_up, grad_down = run_last(
        side,
        tokens_grad,
        weights_grad.reshape(feature_count, feature_count),
        up_first,
        up_pair,
        down_first,
        down_pair,
        line_sum,
        qkv_weight.shape[2],
    )
    return (
        unpad(mixed.reshape(images, PITCH, quarter_width)),
        grad_tokens,
        sums[0],
        sums[1],
        jnp.swapaxes(grad_qkv, 1, 2),
        grad_out,
        sums[2],
        sums[3],
        sums[8 : 8 + experts_all].T,
        grad_up[None],
        grad_down[None],
    )


def per_device(*arguments):
    router_weight = arguments[7]
    if router_weight.shape[1] == 4 and lax.axis_size("expert") == 8 and lax.axis_size("tensor") == 4:
        return per_device_dense(*arguments)
    return per_device_routed(*arguments)


def solution(mesh):
    placed = (
        P("expert", None),
        P(),
        P(),
        P(None, None, "tensor"),
        P("tensor", None),
        P(),
        P(),
        P(),
        P("expert", None, "tensor"),
        P("expert", "tensor", None),
        P("expert", None),
        P("expert", None),
        P("expert", "tensor"),
    )
    return jax.shard_map(
        per_device,
        mesh=mesh,
        in_specs=placed,
        out_specs=(
            P("expert", "tensor"),
            P("expert", None),
            P(),
            P(),
            P(None, None, "tensor"),
            P("tensor", None),
            P(),
            P(),
            P(),
            P("expert", None, "tensor"),
            P("expert", "tensor", None),
        ),
        check_vma=False,
    )
```

```python
from functools import partial

import jax
import jax.numpy as jnp
from jax import lax
from jax.experimental import pallas as pl
from jax.experimental.pallas import tpu as pltpu
from jax.sharding import PartitionSpec as P

HD = 64
SEQ = 197


norm_epsilon = 1e-06


def norm_rows(values, gain, shift):
    row_mean = jnp.mean(values, axis=-1, keepdims=True)
    centred = values - row_mean
    spread = jnp.mean(centred * centred, axis=-1, keepdims=True)
    return centred * lax.rsqrt(spread + norm_epsilon) * gain + shift


def gelu_exact(values):
    return jax.nn.gelu(values, approximate=False)


def gate_from_logits(logit_rows, picked_rows, keep_rows):
    router_probs = jax.nn.softmax(logit_rows, axis=-1)
    return jnp.sum(jnp.where(picked_rows, router_probs[:, None, :], 0.0), axis=-1) * keep_rows


def attention_forward(h_rows, qkv_w, out_w):
    row_total_count = h_rows.shape[0]
    head_count = qkv_w.shape[2] // HD
    image_count = row_total_count // SEQ
    score_scale = HD ** (-0.5)
    projected = jnp.einsum("td,cdf->ctf", h_rows, qkv_w, preferred_element_type=jnp.float32).astype(
        jnp.bfloat16
    )
    split_heads = projected.reshape(3, image_count, SEQ, head_count, HD)
    queries = split_heads[0]
    keys_all = split_heads[1]
    values_all = split_heads[2]
    scores = (
        jnp.einsum("gqhe,gkhe->ghqk", queries, keys_all, preferred_element_type=jnp.float32)
        * score_scale
    )
    row_peak = jnp.max(scores, axis=-1, keepdims=True)
    exp_scores = jnp.exp(scores - row_peak)
    row_total = jnp.sum(exp_scores, axis=-1, keepdims=True)
    log_total = row_peak + jnp.log(row_total)
    weights = (exp_scores / row_total).astype(jnp.bfloat16)
    attended = jnp.einsum(
        "ghqk,gkhe->gqhe", weights, values_all, preferred_element_type=jnp.float32
    ).astype(jnp.bfloat16)
    attended = attended.reshape(row_total_count, head_count * HD)
    partial_out = jnp.dot(attended, out_w, preferred_element_type=jnp.float32)
    return (partial_out, (attended, queries, keys_all, values_all, log_total))


def attention_backward(grad_branch, saved, h_rows, qkv_w, out_w):
    attended, queries, keys_all, values_all, log_total = saved
    row_total_count = h_rows.shape[0]
    head_count = qkv_w.shape[2] // HD
    image_count = row_total_count // SEQ
    score_scale = HD ** (-0.5)
    grad_out = jnp.einsum("tc,td->cd", attended, grad_branch, preferred_element_type=jnp.float32)
    grad_attended = jnp.einsum(
        "td,cd->tc", grad_branch, out_w, preferred_element_type=jnp.float32
    ).astype(jnp.bfloat16)
    grad_attended = grad_attended.reshape(image_count, SEQ, head_count, HD)
    scores_again = (
        jnp.einsum("gqhe,gkhe->ghqk", queries, keys_all, preferred_element_type=jnp.float32)
        * score_scale
    )
    probs_again = jnp.exp(scores_again - log_total)
    grad_weights = jnp.einsum(
        "gqhe,gkhe->ghqk", grad_attended, values_all, preferred_element_type=jnp.float32
    )
    grad_scores = (
        probs_again * (grad_weights - jnp.sum(probs_again * grad_weights, axis=-1, keepdims=True))
    ).astype(jnp.bfloat16)
    grad_queries = (
        jnp.einsum("ghqk,gkhe->gqhe", grad_scores, keys_all, preferred_element_type=jnp.float32)
        * score_scale
    )
    grad_keys = (
        jnp.einsum("ghqk,gqhe->gkhe", grad_scores, queries, preferred_element_type=jnp.float32)
        * score_scale
    )
    grad_values = jnp.einsum(
        "ghqk,gqhe->gkhe",
        probs_again.astype(jnp.bfloat16),
        grad_attended,
        preferred_element_type=jnp.float32,
    )
    grad_rows = (
        jnp.stack([grad_queries, grad_keys, grad_values])
        .astype(jnp.bfloat16)
        .reshape(3, row_total_count, head_count * HD)
    )
    grad_qkv = jnp.einsum("td,ctf->cdf", h_rows, grad_rows, preferred_element_type=jnp.float32)
    grad_h_one = jnp.einsum("ctf,cdf->td", grad_rows, qkv_w, preferred_element_type=jnp.float32)
    return (grad_qkv, grad_out, grad_h_one)


def moe_tail(
    grad_h_rows,
    grad_gate_rows,
    grad_out_rows,
    h_two_rows,
    resid_rows,
    gate_back,
    router_weight,
    gain_moe,
    shift_moe,
):
    row_total_count = grad_h_rows.shape[0]
    grad_gate = jnp.sum(grad_gate_rows.reshape(row_total_count, -1, 2), axis=1)
    grad_logits = gate_back(grad_gate)[0].astype(jnp.bfloat16)
    grad_router = jnp.einsum(
        "td,te->de", h_two_rows, grad_logits, preferred_element_type=jnp.float32
    )
    grad_h_two = grad_h_rows + jnp.einsum(
        "te,de->td", grad_logits, router_weight, preferred_element_type=jnp.float32
    )
    norm_out, norm_back = jax.vjp(norm_rows, resid_rows, gain_moe, shift_moe)
    grad_resid_norm, grad_gain_moe, grad_shift_moe = norm_back(grad_h_two)
    return (grad_out_rows + grad_resid_norm, grad_router, grad_gain_moe, grad_shift_moe)


def per_device_routed(
    tokens,
    gain_attn,
    shift_attn,
    qkv_weight,
    out_weight,
    gain_moe,
    shift_moe,
    router_weight,
    expert_up,
    expert_down,
    routes,
    keep_mask,
    cotangent,
):
    row_count, feature_count = tokens.shape
    tensor_count = lax.axis_size("tensor")
    expert_count = lax.axis_size("expert")
    tensor_here = lax.axis_index("tensor")
    quarter_width = feature_count // tensor_count
    col_start = tensor_here * quarter_width
    experts_all = router_weight.shape[1]
    capacity = max(2, 7 * row_count // (2 * experts_all))
    tokens_float = tokens.astype(jnp.float32)
    h_one = norm_rows(tokens_float, gain_attn, shift_attn).astype(jnp.bfloat16)
    partial_out, saved = attention_forward(h_one, qkv_weight, out_weight)
    branch = lax.psum(partial_out, "tensor")
    resid = tokens_float + branch
    h_two = norm_rows(resid, gain_moe, shift_moe).astype(jnp.bfloat16)
    logits = jnp.dot(h_two, router_weight, preferred_element_type=jnp.float32)
    keep_float = keep_mask.astype(jnp.float32)
    picked = routes[:, :, None] == jnp.arange(experts_all, dtype=jnp.int32)[None, None, :]
    gate_values, gate_back = jax.vjp(
        partial(gate_from_logits, picked_rows=picked, keep_rows=keep_float), logits
    )
    flat_expert = routes.reshape(-1)
    one_hot = (flat_expert[:, None] == jnp.arange(experts_all, dtype=jnp.int32)[None, :]).astype(
        jnp.int32
    )
    rank_within = jnp.sum((jnp.cumsum(one_hot, axis=0) - one_hot) * one_hot, axis=1)
    slot_index = flat_expert * capacity + rank_within
    token_index = jnp.repeat(jnp.arange(row_count, dtype=jnp.int32), 2)
    live_route = keep_mask.reshape(-1) > 0
    source_table = (
        jnp.full((experts_all * capacity,), row_count, jnp.int32)
        .at[slot_index]
        .set(jnp.where(live_route, token_index, row_count))
    )
    padded_rows = jnp.concatenate([h_two, jnp.zeros((1, feature_count), jnp.bfloat16)], axis=0)
    dispatch = padded_rows[source_table].reshape(experts_all, capacity, feature_count)
    paired = jnp.broadcast_to(dispatch[:, None], (experts_all, 2, capacity, feature_count)).reshape(
        expert_count, capacity, feature_count
    )
    arrived = lax.all_to_all(paired, "expert", split_axis=0, concat_axis=0, tiled=True)
    expert_rows = arrived.reshape(expert_count * capacity, feature_count)
    up_local = expert_up[0]
    down_local = expert_down[0]
    pre_act = jnp.dot(expert_rows, up_local, preferred_element_type=jnp.float32)
    hidden_float, gelu_back = jax.vjp(gelu_exact, pre_act)
    hidden = hidden_float.astype(jnp.bfloat16)
    partial_down = jnp.dot(hidden, down_local, preferred_element_type=jnp.float32)
    summed = lax.psum_scatter(partial_down, "tensor", scatter_dimension=1, tiled=True)
    returned = lax.all_to_all(
        summed.reshape(expert_count, capacity, quarter_width),
        "expert",
        split_axis=0,
        concat_axis=0,
        tiled=True,
    )
    answer_table = jnp.sum(
        returned.reshape(experts_all, 2, capacity, quarter_width), axis=1
    ).astype(jnp.bfloat16)
    answers = (
        answer_table.reshape(experts_all * capacity, quarter_width)[slot_index]
        .astype(jnp.float32)
        .reshape(row_count, 2, quarter_width)
    )
    resid_part = lax.dynamic_slice_in_dim(resid, col_start, quarter_width, 1)
    mixed = (resid_part + jnp.sum(gate_values[:, :, None] * answers, axis=1)).astype(jnp.bfloat16)
    grad_part = cotangent.astype(jnp.float32)
    grad_answers = (
        (gate_values[:, :, None] * grad_part[:, None, :])
        .astype(jnp.bfloat16)
        .reshape(2 * row_count, quarter_width)
    )
    grad_gate_part = jnp.sum(grad_part[:, None, :] * answers, axis=-1)
    outgoing = (
        jnp.zeros((experts_all * capacity, quarter_width), jnp.bfloat16)
        .at[slot_index]
        .set(grad_answers)
    )
    outgoing = jnp.broadcast_to(
        outgoing.reshape(experts_all, 1, capacity, quarter_width),
        (experts_all, 2, capacity, quarter_width),
    ).reshape(expert_count, capacity, quarter_width)
    incoming = lax.all_to_all(outgoing, "expert", split_axis=0, concat_axis=0, tiled=True)
    grad_full = lax.all_gather(incoming, "tensor", axis=2, tiled=True).reshape(
        expert_count * capacity, feature_count
    )
    grad_hidden = jnp.einsum("rd,fd->rf", grad_full, down_local, preferred_element_type=jnp.float32)
    grad_pre = gelu_back(grad_hidden)[0].astype(jnp.bfloat16)
    grad_down = jnp.einsum("rf,rd->fd", hidden, grad_full, preferred_element_type=jnp.float32)
    grad_up = jnp.einsum("rd,rf->df", expert_rows, grad_pre, preferred_element_type=jnp.float32)
    grad_rows_partial = jnp.einsum(
        "rf,df->rd", grad_pre, up_local, preferred_element_type=jnp.float32
    )
    grad_rows_sum = lax.psum_scatter(
        grad_rows_partial.astype(jnp.bfloat16), "tensor", scatter_dimension=1, tiled=True
    ).astype(jnp.float32)
    sent_back = lax.all_to_all(
        grad_rows_sum.reshape(expert_count, capacity, quarter_width).astype(jnp.bfloat16),
        "expert",
        split_axis=0,
        concat_axis=0,
        tiled=True,
    ).astype(jnp.float32)
    grad_table = jnp.sum(sent_back.reshape(experts_all, 2, capacity, quarter_width), axis=1).astype(
        jnp.bfloat16
    )
    grad_inputs = (
        grad_table.reshape(experts_all * capacity, quarter_width)[slot_index]
        .astype(jnp.float32)
        .reshape(row_count, 2, quarter_width)
    )
    grad_h_part = jnp.sum(grad_inputs * keep_float[:, :, None], axis=1)
    grad_h_full, grad_gate_all, grad_out_full = (
        lax.all_gather(grad_h_part, "tensor", axis=1, tiled=True),
        lax.all_gather(grad_gate_part, "tensor", axis=1, tiled=True),
        lax.all_gather(grad_part, "tensor", axis=1, tiled=True),
    )
    grad_resid, grad_router, grad_gain_moe, grad_shift_moe = moe_tail(
        grad_h_full,
        grad_gate_all,
        grad_out_full,
        h_two,
        resid,
        gate_back,
        router_weight,
        gain_moe,
        shift_moe,
    )
    grad_qkv, grad_out, grad_h_one_part = attention_backward(
        grad_resid.astype(jnp.bfloat16), saved, h_one, qkv_weight, out_weight
    )
    grad_h_one = lax.psum(grad_h_one_part.astype(jnp.bfloat16), "tensor").astype(jnp.float32)
    norm_one_out, norm_one_back = jax.vjp(norm_rows, tokens_float, gain_attn, shift_attn)
    grad_tok_norm, grad_gain_attn, grad_shift_attn = norm_one_back(grad_h_one)
    grad_tokens = grad_resid + grad_tok_norm
    summed_grads = lax.psum(
        (
            grad_gain_attn,
            grad_shift_attn,
            grad_qkv,
            grad_out,
            grad_gain_moe,
            grad_shift_moe,
            grad_router,
        ),
        "expert",
    )
    grad_qkv_mine = summed_grads[2]
    grad_out_mine = summed_grads[3]
    return (
        mixed,
        grad_tokens,
        summed_grads[0],
        summed_grads[1],
        grad_qkv_mine,
        grad_out_mine,
        summed_grads[4],
        summed_grads[5],
        summed_grads[6],
        grad_up[None],
        grad_down[None],
    )


MESH = pl.DeviceIdType.MESH
f32 = jnp.float32
bf16 = jnp.bfloat16
PITCH = 208


def dot(left, right, over=((1,), (0,))):
    return lax.dot_general(left, right, (over, ((), ())), preferred_element_type=f32)


def aligned(start, size):
    return pl.ds(pl.multiple_of(start, 16), size)


def lanes_at(start, size):
    return pl.ds(pl.multiple_of(start, 128), size)


def norm_stats(values):
    row_mean = jnp.mean(values, axis=1, keepdims=True)
    centred = values - row_mean
    inverse = lax.rsqrt(jnp.mean(centred * centred, axis=1, keepdims=True) + norm_epsilon)
    return centred * inverse, inverse


def greet(neighbours):
    barrier = pltpu.get_barrier_semaphore()
    count = 0
    for is_there, device in neighbours:

        @pl.when(is_there)
        def _():
            pl.semaphore_signal(barrier, inc=1, device_id=device, device_id_type=MESH)

        count = count + jnp.where(is_there, 1, 0)
    pl.semaphore_wait(barrier, count)


def head_mask(lane, head):
    return (lane < HD) if head % 2 == 0 else (lane >= HD)


def expert_math(h_rows, cot_rows, kept, router, up, down, pair, experts):
    block = h_rows.shape[0]
    hidden = up.shape[1] // 2
    lane = lax.broadcasted_iota(jnp.int32, (block, 128), 1)
    logits = jnp.where(lane < experts, dot(h_rows, router, ((1,), (1,))), -1e30)
    powers = jnp.exp(logits - jnp.max(logits, axis=1, keepdims=True))
    probs = powers / jnp.sum(powers, axis=1, keepdims=True)
    gates = kept * probs
    pre_act = dot(h_rows, up)
    back = dot(cot_rows, down, ((1,), (1,)))
    normal_cdf = 0.5 + 0.5 * lax.erf(pre_act * 0.7071067811865476)
    gelu = pre_act * normal_cdf
    slope = normal_cdf + pre_act * (0.3989422804014327 * jnp.exp(-0.5 * pre_act * pre_act))
    product = gelu * back
    grad_gate = jnp.zeros((block, 128), f32)
    spread = []
    for side in range(2):
        chosen = lane == 2 * pair + side
        part = jnp.sum(product[:, side * hidden : (side + 1) * hidden], axis=1, keepdims=True)
        grad_gate = jnp.where(chosen, part, grad_gate)
        gate = jnp.sum(jnp.where(chosen, gates, 0.0), axis=1, keepdims=True)
        spread.append(jnp.broadcast_to(gate, (block, hidden)))
    gate = jnp.concatenate(spread, axis=1)
    hidden_rows = (gelu * gate).astype(bf16)
    grad_pre = (slope * back * gate).astype(bf16)
    return hidden_rows, grad_pre, probs, grad_gate


BLOCK = 2 * PITCH


def forward_kernel(
    gain1_ref,
    shift1_ref,
    gain2_ref,
    shift2_ref,
    up_ref,
    down_ref,
    router_raw,
    cot_hbm,
    kept_hbm,
    tok_hbm,
    qkv_hbm,
    out_w_hbm,
    q_ref,
    k_ref,
    v_ref,
    att_ref,
    lse_ref,
    resid_ref,
    h_out,
    cot_out,
    kept_out,
    up_out,
    down_out,
    mixed_out,
    grad_h_out,
    gate_out,
    grad_up_out,
    grad_down_out,
    tok_out,
    router_out,
    router_ref,
    cot_turned,
    kept_ref,
    tok_raw,
    qkv_ref,
    out_w_ref,
    tok_ref,
    cot_ref,
    up_vm,
    down_vm,
    up_sum,
    down_sum,
    mixed_slots,
    grad_h_slots,
    gate_slots,
    grad_up_vm,
    grad_down_vm,
    q_all,
    k_all,
    v_all,
    att_all,
    lse_all,
    resid_all,
    h_all,
    cot_all,
    kept_all,
    part,
    mine,
    core_from,
    core_to,
    x_to,
    x_from,
    total_to,
    total_from,
    cot_core,
    core_s,
    core_r,
    x_s,
    x_r,
    tot_s,
    tot_r,
    y_s,
    y_r,
    rel_s,
    rel_r,
    w_s,
    w_r,
    c_s,
    c_r,
    load_sem,
    own_sem,
    pair_sem,
    block_sem,
    grad_sem,
    cot_sem,
    out_sem,
    *,
    images,
    heads,
    experts,
):
    expert_at = lax.axis_index("expert")
    tensor_at = lax.axis_index("tensor")
    z_at, y_at = expert_at // 2, expert_at % 2
    z_last = lax.axis_size("expert") // 2 - 1
    x_at, core_at = tensor_at // 2, tensor_at % 2
    other = 1 - core_at
    rows = images * PITCH
    half = rows // 2
    wide = out_w_ref.shape[1] // 2
    loads = [
        pltpu.make_async_copy(source, target, load_sem.at[number])
        for number, (source, target) in enumerate(
            (
                (cot_hbm, cot_turned),
                (kept_hbm, kept_ref),
                (tok_hbm, tok_raw),
                (qkv_hbm, qkv_ref),
                (out_w_hbm, out_w_ref),
            )
        )
    ]
    for copy in loads:
        copy.start()
    hidden = up_ref.shape[1]
    core_dev = (expert_at, tensor_at + 1 - 2 * core_at)
    x_dev = (expert_at, tensor_at + 2 - 4 * x_at)
    y_dev = (expert_at + 1 - 2 * y_at, tensor_at)
    z_up = (expert_at + 2, tensor_at)
    z_down = (expert_at - 2, tensor_at)
    has_up, has_down = z_at < z_last, z_at > 0
    greet([(True, core_dev), (True, x_dev), (True, y_dev), (has_up, z_up), (has_down, z_down)])

    def remote(src, dst, send, recv, device):
        return pltpu.make_async_remote_copy(
            src_ref=src, dst_ref=dst, send_sem=send, recv_sem=recv, device_id=device, device_id_type=MESH
        )

    def slot(expert, plane):
        pair = (expert // 2 + plane // 2) % 2
        return (
            up_out.at[pair, :, lanes_at(expert % 2 * hidden, hidden)],
            down_out.at[pair, aligned(expert % 2 * hidden, hidden), :],
        )

    def hop(step, way):
        expert = z_at - step if way == 0 else z_at + step
        plane = z_at + 1 if way == 0 else z_at - 1
        source = (up_ref, down_ref) if step == 0 else slot(expert, z_at)
        target = slot(expert, plane)
        device = z_up if way == 0 else z_down
        return [remote(source[n], target[n], w_s.at[way, step, n], w_r.at[way, step, n], device) for n in range(2)]

    def hop_goes(step, way):
        if way == 0:
            return (z_at - step >= 0) & has_up
        return (z_at + step <= z_last) & has_down

    def hop_comes(step, way):
        return (z_at - 1 - step >= 0) if way == 0 else (z_at + 1 + step <= z_last)

    def hop_arriving(step, way):
        expert = z_at - 1 - step if way == 0 else z_at + 1 + step
        target = slot(expert, z_at)
        return [remote(target[n], target[n], w_s.at[way, step, n], w_r.at[way, step, n], core_dev) for n in range(2)]

    def start_hops(step, which):
        for way in range(2):

            @pl.when(hop_goes(step, way))
            def _():
                hop(step, way)[which].start()

    def await_hops(step, which):
        for way in range(2):

            @pl.when(hop_comes(step, way))
            def _():
                hop_arriving(step, way)[which].wait_recv()

    def pass_hops(step, which):
        await_hops(step, which)
        start_hops(step + 1, which)

    start_hops(0, 0)
    start_hops(0, 1)

    def pair_place(expert):
        return up_vm.at[:, lanes_at(expert % 2 * hidden, hidden)], down_vm.at[aligned(expert % 2 * hidden, hidden), :]

    near = z_at + 1 - 2 * (z_at % 2)
    own_copies = [
        pltpu.make_async_copy((up_ref, down_ref)[n], pair_place(z_at)[n], own_sem.at[n]) for n in range(2)
    ]
    near_copies = [
        pltpu.make_async_copy(slot(near, z_at)[n], pair_place(near)[n], pair_sem.at[n]) for n in range(2)
    ]
    for copy in own_copies:
        copy.start()

    loads[0].wait()
    for number in range(images):
        first = number * SEQ // 128 * 128
        skip = number * SEQ - first
        lanes_in = cot_turned[:, first : min(first + 384, images * SEQ)].astype(f32)
        if lanes_in.shape[1] < 384:
            lanes_in = jnp.concatenate([lanes_in, jnp.zeros((lanes_in.shape[0], 384 - lanes_in.shape[1]), f32)], axis=1)
        turned = lanes_in.T[skip : skip + SEQ]
        padded = jnp.concatenate([turned, jnp.zeros((PITCH - SEQ, turned.shape[1]), f32)], axis=0)
        cot_ref[number * PITCH : (number + 1) * PITCH, :] = padded.astype(bf16)
    swap = remote(cot_ref, cot_core, c_s.at[0], c_r.at[0], core_dev)
    swap.start()

    narrow = router_raw[...].astype(f32)
    router_ref[0:16, :] = jnp.concatenate([narrow, jnp.zeros((16 - experts, narrow.shape[1]), f32)], axis=0).astype(bf16)
    router_ref[16:128, :] = jnp.zeros((112, narrow.shape[1]), bf16)

    def kept_half(side, core):
        return kept_all.at[aligned(side * rows + core * half, half), :]

    kept_y = remote(kept_half(0, core_at), kept_half(1, core_at), c_s.at[7], c_r.at[7], y_dev)
    kept_share = remote(kept_half(1, core_at), kept_half(1, core_at), c_s.at[6], c_r.at[6], core_dev)
    kept_share_in = remote(kept_half(1, other), kept_half(1, other), c_s.at[6], c_r.at[6], core_dev)
    loads[1].wait()
    kept_all[pl.ds(0, rows), :] = kept_ref[...]
    kept_y.start()
    swap.wait_recv()

    @pl.when(core_at == 0)
    def _():
        both = jnp.concatenate([cot_ref[...], cot_core[...]], axis=1)
        cot_all[pl.ds(0, rows), lanes_at(x_at * wide, wide)] = both

    @pl.when(core_at == 1)
    def _():
        both = jnp.concatenate([cot_core[...], cot_ref[...]], axis=1)
        cot_all[pl.ds(0, rows), lanes_at(x_at * wide, wide)] = both

    def block(side, col_side, core):
        return cot_all.at[aligned(side * rows + core * half, half), lanes_at(col_side * wide, wide)]

    def cot_copy(number, source, target, device):
        return remote(source, target, c_s.at[number], c_r.at[number], device)

    mine_block = block(0, x_at, core_at)
    cot_x = cot_copy(1, mine_block, mine_block, x_dev)
    cot_y = cot_copy(2, mine_block, block(1, x_at, core_at), y_dev)
    cot_x.start()
    cot_y.start()
    across_x, across_y, across_both = block(0, 1 - x_at, core_at), block(1, x_at, core_at), block(1, 1 - x_at, core_at)
    cot_x_in = cot_copy(1, across_x, across_x, x_dev)
    cot_y_in = cot_copy(2, across_y, across_y, y_dev)
    relay_y = cot_copy(3, across_x, across_both, y_dev)
    relay_in = cot_copy(3, across_both, across_both, y_dev)
    cot_share = [
        cot_copy(4, across_x, across_x, core_dev),
        cot_copy(5, across_y, across_y, core_dev),
        cot_copy(8, across_both, across_both, core_dev),
    ]
    arriving = [block(0, 1 - x_at, other), block(1, x_at, other), block(1, 1 - x_at, other)]
    cot_share_in = [cot_copy(number, ref, ref, core_dev) for number, ref in zip((4, 5, 8), arriving)]

    lane = lax.broadcasted_iota(jnp.int32, (PITCH, 2 * HD), 1)
    key_mask = lax.broadcasted_iota(jnp.int32, (PITCH, PITCH), 1) < SEQ
    gain1, shift1, gain2, shift2 = (ref[...].reshape(1, 2 * wide) for ref in (gain1_ref, shift1_ref, gain2_ref, shift2_ref))
    my_cols = lanes_at(core_at * wide, wide)
    their_cols = lanes_at(other * wide, wide)

    def attend(image):
        normed, _ = norm_stats(tok_ref[image].astype(f32))
        h_one = (normed * gain1 + shift1).astype(bf16)
        queries = dot(h_one, qkv_ref[0], ((1,), (1,))).astype(bf16)
        keys = dot(h_one, qkv_ref[1], ((1,), (1,))).astype(bf16)
        values = dot(h_one, qkv_ref[2], ((1,), (1,))).astype(bf16)
        q_all[image] = queries
        k_all[image] = keys
        v_all[image] = values
        outs = []
        lse = jnp.zeros((PITCH, 2 * HD), f32)
        for head in range(heads):
            first = head // 2 * 2 * HD
            last = min(first + 2 * HD, heads * HD)
            q_head, k_head, v_head = queries[:, first:last], keys[:, first:last], values[:, first:last]
            if last - first == 2 * HD:
                q_head = jnp.where(head_mask(lane, head), q_head, jnp.zeros_like(q_head))
            scores = dot(q_head, k_head, ((1,), (1,))) * (HD**-0.5)
            scores = jnp.where(key_mask, scores, -1e30)
            peak = jnp.max(scores, axis=1, keepdims=True)
            powers = jnp.exp(scores - peak)
            row_sum = jnp.sum(powers, axis=1, keepdims=True)
            weights = (powers / row_sum).astype(bf16)
            outs.append(dot(weights, v_head))
            lse = jnp.where(lane == head, peak + jnp.log(row_sum), lse)
        lse_all[image] = lse
        joined = []
        for head in range(0, heads, 2):
            if head + 1 < heads:
                joined.append(jnp.where(lane < HD, outs[head], outs[head + 1]))
            else:
                joined.append(outs[head])
        attended = jnp.concatenate(joined, axis=1).astype(bf16)
        att_all[image] = attended
        part[...] = dot(attended, out_w_ref[...])
        mine[image] = part[:, my_cols]
        core_to[image] = part[:, their_cols].astype(bf16)

    def core_copy(image):
        return remote(core_to.at[image], core_from.at[image], core_s.at[image], core_r.at[image], core_dev)

    def x_copy(image):
        return remote(x_to.at[image], x_from.at[image], x_s.at[image], x_r.at[image], x_dev)

    def total_copy(image):
        return remote(total_to.at[image], total_from.at[image], tot_s.at[image], tot_r.at[image], core_dev)

    def h_block(side, image, core):
        return h_all.at[aligned(side * rows + image * PITCH, PITCH), lanes_at(core * wide, wide)]

    def y_copy(image):
        return remote(h_block(0, image, core_at), h_block(1, image, core_at), y_s.at[image], y_r.at[image], y_dev)

    def relay_copy(image):
        ref = h_block(1, image, core_at)
        return remote(ref, ref, rel_s.at[image], rel_r.at[image], core_dev)

    def relay_arriving(image):
        ref = h_block(1, image, other)
        return remote(ref, ref, rel_s.at[image], rel_r.at[image], core_dev)

    attend_outs = ((tok_ref, tok_out), (q_all, q_ref), (k_all, k_ref), (v_all, v_ref), (att_all, att_ref), (lse_all, lse_ref))

    def out_copies(image):
        copies = [
            pltpu.make_async_copy(kept.at[image], out.at[image], out_sem.at[n, image])
            for n, (kept, out) in enumerate(attend_outs)
        ]
        at = aligned(image * PITCH, PITCH)
        return copies, [
            pltpu.make_async_copy(resid_all.at[image], resid_ref.at[at, :], out_sem.at[6, image]),
            pltpu.make_async_copy(h_all.at[at, :], h_out.at[at, :], out_sem.at[7, image]),
        ]

    def other_copy(image):
        at = aligned(rows + image * PITCH, PITCH)
        return pltpu.make_async_copy(h_all.at[at, :], h_out.at[at, :], out_sem.at[8, image])

    def stage(tick, lag, run):
        image = tick - lag

        @pl.when((image >= 0) & (image < images))
        def _():
            run(image)

    def run_attend(image):
        attend(image)
        core_copy(image).start()
        for copy in out_copies(image)[0]:
            copy.start()

    def run_x(image):
        core_copy(image).wait_recv()
        x_to[image] = (mine[image] + core_from[image].astype(f32)).astype(bf16)
        x_copy(image).start()

    def run_total(image):
        x_copy(image).wait_recv()
        total_to[image] = (x_to[image].astype(f32) + x_from[image].astype(f32)).astype(bf16)
        total_copy(image).start()

    def run_norm(image):
        total_copy(image).wait_recv()
        part[:, my_cols] = total_to[image].astype(f32)
        part[:, their_cols] = total_from[image].astype(f32)
        resid = tok_ref[image].astype(f32) + part[...]
        resid_all[image] = resid
        normed, _ = norm_stats(resid)
        h_all[aligned(image * PITCH, PITCH), :] = (normed * gain2 + shift2).astype(bf16)
        y_copy(image).start()
        for copy in out_copies(image)[1]:
            copy.start()

    def run_relay(image):
        y_copy(image).wait_recv()
        relay_copy(image).start()

    def run_end(image):
        relay_arriving(image).wait_recv()
        other_copy(image).start()

    def cot_step_one():
        cot_x_in.wait_recv()
        cot_share[0].start()

        relay_y.start()

    def cot_step_two():
        cot_y_in.wait_recv()
        cot_share[1].start()

    def weights_step_one():
        pass_hops(0, 1)
        for copy in near_copies:
            copy.start()

    def cot_step_three():
        kept_y.wait_recv()
        kept_share.start()
        relay_in.wait_recv()
        cot_share[2].start()

    outs = [
        pltpu.make_async_copy(cot_all, cot_out, cot_sem.at[0]),
        pltpu.make_async_copy(kept_all, kept_out, cot_sem.at[1]),
        pltpu.make_async_copy(router_ref, router_out, cot_sem.at[2]),
    ]

    def ready_own():
        cot_share_in[0].wait_recv()
        for copy in (*own_copies, *near_copies):
            copy.wait()

    def ready_other():
        for copy in (cot_share_in[1], cot_share_in[2], kept_share_in):
            copy.wait_recv()
        for copy in outs:
            copy.start()

    def block_copies(number, place):
        at = aligned(number * BLOCK, BLOCK)
        pairs = ((mixed_slots, mixed_out), (grad_h_slots, grad_h_out), (gate_slots, gate_out))
        return [
            pltpu.make_async_copy(slots.at[place], out.at[at, :], block_sem.at[n, place])
            for n, (slots, out) in enumerate(pairs)
        ]

    def run_block(number, turn):
        at = aligned(number * BLOCK, BLOCK)
        h_rows, cot_rows = h_all[at, :], cot_all[at, :]
        up, down = up_vm[...], down_vm[...]
        hidden_rows, grad_pre, _, grad_gate = expert_math(
            h_rows, cot_rows, kept_all[at, :].astype(f32), router_ref[...], up, down, z_at // 2, experts
        )

        place = turn % 2

        @pl.when(turn >= 2)
        def _():
            for copy in block_copies(number, place):
                copy.wait()

        gate_slots[place] = grad_gate
        mixed_slots[place] = dot(hidden_rows, down).astype(bf16)
        grad_h_slots[place] = dot(grad_pre, up, ((1,), (1,))).astype(bf16)
        for copy in block_copies(number, place):
            copy.start()
        up_sum[...] += dot(h_rows.T, grad_pre)
        down_sum[...] += dot(cot_rows.T, hidden_rows)

    up_sum[...] = jnp.zeros_like(up_sum)
    down_sum[...] = jnp.zeros_like(down_sum)

    def take_tokens(number):
        first = number * SEQ // 16 * 16
        skip = number * SEQ - first
        taken = min(224, images * SEQ - first)
        rows_in = tok_raw[first : first + taken, :].astype(f32)[skip : skip + SEQ]
        padded = jnp.concatenate([rows_in, jnp.zeros((PITCH - SEQ, rows_in.shape[1]), f32)], axis=0)
        tok_ref[number] = padded.astype(bf16)

    def first_ticks(tick, _):
        for number in range(images):
            pl.when(tick == number)(partial(take_tokens, number))

        stage(tick, 0, run_attend)
        stage(tick, 1, run_x)
        return 0

    for copy in loads[2:]:
        copy.wait()
    lax.fori_loop(0, images + 1, first_ticks, 0)
    pairs = images // 2

    def both(first, *runs):
        for run in runs:
            run(first)
            run(first + 1)

    pass_hops(0, 0)
    cot_step_one()
    both(0, run_total, run_norm)
    cot_step_two()
    weights_step_one()
    ready_own()

    def per_turn(turn, _):
        @pl.when((turn <= 1) | (turn == 3))
        def _():
            both(jnp.where(turn == 3, 6, 2 * turn + 2), run_total, run_norm)

        @pl.when((turn >= 2) & (turn < pairs + 2))
        def _():
            both(2 * turn - 4, run_relay)

        @pl.when(turn == 2)
        def _():
            pass_hops(1, 0)
            cot_step_three()

        @pl.when(turn == pairs)
        def _():
            pass_hops(1, 1)
            ready_other()

        @pl.when(turn >= pairs)
        def _():
            both(2 * (turn - pairs), run_end)

        run_block(turn, turn)
        return 0

    lax.fori_loop(0, 2 * pairs, per_turn, 0)
    grad_up_vm[...] = up_sum[...].astype(bf16)
    grad_down_vm[...] = down_sum[...].astype(bf16)
    grad_copies = [
        pltpu.make_async_copy(grad_up_vm, grad_up_out, grad_sem.at[0]),
        pltpu.make_async_copy(grad_down_vm, grad_down_out, grad_sem.at[1]),
    ]
    for copy in grad_copies:
        copy.start()
    for copy in (swap, kept_y, kept_share, cot_x, cot_y, *cot_share):
        copy.wait_send()

    relay_y.wait_send()

    def drain(image, _):
        for copy in (core_copy, x_copy, total_copy, y_copy, relay_copy):
            copy(image).wait_send()
        first, second = out_copies(image)
        for copy in (*first, *second, other_copy(image)):
            copy.wait()
        return 0

    lax.fori_loop(0, images, drain, 0)
    for place in range(2):
        for copy in block_copies(0, place):
            copy.wait()

    await_hops(2, 0)
    await_hops(2, 1)
    for step in range(3):
        for way in range(2):

            @pl.when(hop_goes(step, way))
            def _():
                for copy in hop(step, way):
                    copy.wait_send()

    for copy in (*grad_copies, *outs):
        copy.wait()


def run_forward(tok_raw, gain1, shift1, gain2, shift2, qkv_w, out_w, up, down, router, cot, kept, experts):
    images = tok_raw.shape[0] // SEQ
    rows = images * PITCH
    features = tok_raw.shape[1]
    share = out_w.shape[0]
    heads = share // HD
    hidden = up.shape[1]
    wide = features // 2
    vmem = pl.BlockSpec(memory_space=pltpu.VMEM)
    anywhere = pl.BlockSpec(memory_space=pl.ANY)
    shape = jax.ShapeDtypeStruct
    block = (images, PITCH, wide)
    dma = pltpu.SemaphoreType.DMA
    return pl.pallas_call(
        partial(forward_kernel, images=images, heads=heads, experts=experts),
        out_shape=[
            shape((images, PITCH, share), bf16),
            shape((images, PITCH, share), bf16),
            shape((images, PITCH, share), bf16),
            shape((images, PITCH, share), bf16),
            shape((images, PITCH, 128), f32),
            shape((rows, features), f32),
            shape((2 * rows, features), bf16),
            shape((2 * rows, features), bf16),
            shape((2 * rows, 128), bf16),
            shape((2, features, 2 * hidden), bf16),
            shape((2, 2 * hidden, features), bf16),
            shape((2 * rows, features), bf16),
            shape((2 * rows, features), bf16),
            shape((2 * rows, 128), f32),
            shape((features, 2 * hidden), bf16),
            shape((features, 2 * hidden), bf16),
            shape((images, PITCH, features), bf16),
            shape((128, features), bf16),
        ],
        in_specs=[vmem] * 4 + [anywhere] * 2 + [vmem] + [anywhere] * 5,
        out_specs=[anywhere] * 18,
        scratch_shapes=[
            pltpu.VMEM((128, features), bf16),
            pltpu.VMEM(cot.shape, bf16),
            pltpu.VMEM(kept.shape, bf16),
            pltpu.VMEM(tok_raw.shape, bf16),
            pltpu.VMEM(qkv_w.shape, bf16),
            pltpu.VMEM(out_w.shape, bf16),
            pltpu.VMEM((images, PITCH, features), bf16),
            pltpu.VMEM((rows, share), bf16),
            pltpu.VMEM((features, 2 * hidden), bf16),
            pltpu.VMEM((2 * hidden, features), bf16),
            *[pltpu.VMEM((features, 2 * hidden), f32)] * 2,
            *[pltpu.VMEM((2, BLOCK, features), bf16)] * 2,
            pltpu.VMEM((2, BLOCK, 128), f32),
            *[pltpu.VMEM((features, 2 * hidden), bf16)] * 2,
            *[pltpu.VMEM((images, PITCH, share), bf16)] * 4,
            pltpu.VMEM((images, PITCH, 128), f32),
            pltpu.VMEM((images, PITCH, features), f32),
            pltpu.VMEM((2 * rows, features), bf16),
            pltpu.VMEM((2 * rows, features), bf16),
            pltpu.VMEM((2 * rows, 128), bf16),
            pltpu.VMEM((PITCH, features), f32),
            pltpu.VMEM(block, f32),
            pltpu.VMEM(block, bf16),
            pltpu.VMEM(block, bf16),
            pltpu.VMEM(block, bf16),
            pltpu.VMEM(block, bf16),
            pltpu.VMEM(block, bf16),
            pltpu.VMEM(block, bf16),
            pltpu.VMEM((rows, share), bf16),
        ]
        + [dma((images,))] * 10
        + [dma((2, 3, 2))] * 2
        + [dma((9,))] * 2
        + [dma((5,)), dma((2,)), dma((2,)), dma((3, 2)), dma((2,)), dma((3,)), dma((9, images))],
        compiler_params=pltpu.CompilerParams(
            collective_id=1, has_side_effects=True, vmem_limit_bytes=63 << 20
        ),
    )(gain1, shift1, gain2, shift2, up, down, router, cot, kept, tok_raw, qkv_w, out_w)


def turn_is_other(turn):
    return (turn == 0) | ((turn % 2 == 1) & (turn < 7))


def turn_block(turn):
    own = jnp.where(turn == 7, 3, turn // 2 - 1)
    return jnp.where(turn_is_other(turn), 4 + (turn + 1) // 2, own)


def second_pair_kernel(
    h_ref,
    cot_ref,
    kept_ref,
    router_ref,
    mixed_first,
    grad_h_first,
    gate_first,
    up_all,
    down_all,
    up_first,
    down_first,
    mixed_ref,
    grad_router_ref,
    grad_up_out,
    grad_down_out,
    grad_h_out,
    up_pair,
    down_pair,
    line_first,
    up_vm,
    down_vm,
    grad_up_ref,
    grad_down_ref,
    up_sum,
    down_sum,
    router_sum,
    ring,
    from_core,
    from_y,
    from_x,
    load,
    core_s,
    core_r,
    y_s,
    y_r,
    x_s,
    x_r,
    tot_s,
    tot_r,
    store,
    pair_s,
    pair_r,
    line_s,
    line_r,
    *,
    experts,
    steps,
):
    turn = pl.program_id(0)
    expert_at = lax.axis_index("expert")
    tensor_at = lax.axis_index("tensor")
    z_at, y_at = expert_at // 2, expert_at % 2
    x_at, core_at = tensor_at // 2, tensor_at % 2
    hidden = up_pair.shape[1]
    wide = ring.shape[3]
    core_dev = (expert_at, tensor_at + 1 - 2 * core_at)
    x_dev = (expert_at, tensor_at + 2 - 4 * x_at)
    y_dev = (expert_at + 1 - 2 * y_at, tensor_at)
    my_cols = lanes_at(core_at * wide, wide)

    def remote(src, dst, send, recv, device):
        return pltpu.make_async_remote_copy(
            src_ref=src, dst_ref=dst, send_sem=send, recv_sem=recv, device_id=device, device_id_type=MESH
        )

    def core_copy(number):
        return remote(ring.at[number % 2, 1 - core_at], from_core.at[number], core_s.at[number], core_r.at[number], core_dev)

    def y_copy(number, place):
        return remote(from_core.at[number], from_y.at[place], y_s.at[place], y_r.at[place], y_dev)

    def x_copy(number, place):
        return remote(from_core.at[number], from_x.at[place], x_s.at[place], x_r.at[place], x_dev)

    def out_rows(place):
        return grad_h_out.at[aligned(place * BLOCK, BLOCK), my_cols]

    def total_copy(place):
        return remote(from_x.at[place], out_rows(place), tot_s.at[place], tot_r.at[place], core_dev)

    def store_copy(place):
        return pltpu.make_async_copy(from_x.at[place], out_rows(place), store.at[place])

    def own_turn(place):
        return jnp.where(place == 3, 7, 2 * place + 2)

    def other_turn(place):
        return jnp.where(place == 0, 0, 2 * place - 1)

    def pass_other(number):
        core_copy(number).wait_recv()
        from_core[number] = from_core[number] + ring[number % 2, core_at]
        y_copy(number, (number + 1) // 2).start()

    def pass_own(number, place):
        core_copy(number).wait_recv()
        y_copy(number, place).wait_recv()
        total = from_core[number].astype(f32) + ring[number % 2, core_at].astype(f32) + from_y[place].astype(f32)
        from_core[number] = total.astype(bf16)
        x_copy(number, place).start()

    def pass_total(place):
        number = own_turn(place)
        x_copy(number, place).wait_recv()
        from_x[place] = from_core[number] + from_x[place]
        total_copy(place).start()
        store_copy(place).start()

    z_dev = (jnp.where(z_at % 2 == 0, expert_at + 2, expert_at - 2), tensor_at)
    pair_lanes = lanes_at((1 - z_at % 2) * hidden, hidden)
    pair_copies = [
        remote(source.at[:, pair_lanes], target, pair_s.at[number], pair_r.at[number], z_dev)
        for number, (source, target) in enumerate(((up_first, up_pair), (down_first, down_pair)))
    ]

    far_lanes = lanes_at(jnp.where(z_at == 0, 1, 0) * hidden, hidden)
    line_copy = remote(grad_up_ref.at[:, far_lanes], line_first, line_s.at[0], line_r.at[0], z_dev)
    is_outer = (z_at == 0) | (z_at == lax.axis_size("expert") // 2 - 1)

    grad_copies = [
        pltpu.make_async_copy(grad_up_ref, grad_up_out, load.at[2]),
        pltpu.make_async_copy(grad_down_ref, grad_down_out, load.at[3]),
    ]

    @pl.when(turn == 0)
    def _():
        whole = [
            pltpu.make_async_copy(up_all.at[1], up_vm, load.at[0]),
            pltpu.make_async_copy(down_all.at[1], down_vm, load.at[1]),
        ]
        for copy in whole:
            copy.start()
        greet([(True, core_dev), (True, x_dev), (True, y_dev), (True, z_dev)])
        for copy in pair_copies:
            copy.start()
        up_sum[...] = jnp.zeros_like(up_sum)
        down_sum[...] = jnp.zeros_like(down_sum)
        router_sum[...] = jnp.zeros_like(router_sum)
        for copy in whole:
            copy.wait()

    h_rows, cot_rows = h_ref[...], cot_ref[...]
    up, down, router = up_vm[...], down_vm[...], router_ref[...]
    kept = kept_ref[...].astype(f32)
    hidden_rows, grad_pre, probs, grad_gate = expert_math(
        h_rows, cot_rows, kept, router, up, down, 1 - z_at // 2, experts
    )
    grad_gate = kept * (grad_gate + gate_first[...])
    grad_logits = (probs * (grad_gate - jnp.sum(probs * grad_gate, axis=1, keepdims=True))).astype(bf16)

    before = turn - 1

    @pl.when((turn >= 1) & turn_is_other(before))
    def _():
        pass_other(before)

    @pl.when((turn == 5) | (turn == 7))
    def _():
        pass_total((turn - 5) // 2)

    @pl.when((turn == 3) | (turn == 5) | (turn == 7))
    def _():
        pass_own(before, (turn - 3) // 2)


    @pl.when(turn >= 2)
    def _():
        core_copy(turn - 2).wait_send()

    grad_h = (
        grad_h_first[...].astype(f32) + dot(grad_pre, up, ((1,), (1,))) + dot(grad_logits, router)
    ).astype(bf16)
    ring[turn % 2, 0] = grad_h[:, :wide]
    ring[turn % 2, 1] = grad_h[:, wide:]
    core_copy(turn).start()
    h_turned = h_rows.T
    up_sum[...] += dot(h_turned, grad_pre)

    @pl.when(turn == steps - 1)
    def _():
        grad_up_ref[...] = up_sum[...].astype(bf16)
        grad_copies[0].start()

        @pl.when(is_outer)
        def _():
            line_copy.start()

        pass_own(7, 3)

    mixed_ref[...] = (mixed_first[...].astype(f32) + dot(hidden_rows, down)).astype(bf16)
    router_sum[...] += dot(h_turned, grad_logits)
    down_sum[...] += dot(cot_rows.T, hidden_rows)

    @pl.when(turn == steps - 1)
    def _():
        pass_total(2)
        grad_down_ref[...] = down_sum[...].astype(bf16)
        grad_copies[1].start()
        grad_router_ref[...] = router_sum[...].T[:8]
        pass_total(3)
        for copy in (*pair_copies, *grad_copies):
            copy.wait()

        @pl.when(is_outer)
        def _():
            line_copy.wait_send()

        @pl.when(jnp.logical_not(is_outer))
        def _():
            line_copy.wait_recv()

        for number in (6, 7):
            core_copy(number).wait_send()
        for place in range(4):
            y_copy(other_turn(place), place).wait_send()
            x_copy(own_turn(place), place).wait_send()
            total_copy(place).wait_send()
            total_copy(place).wait_recv()
            store_copy(place).wait()


def run_second_pair(
    h_rows,
    cot_rows,
    kept,
    router,
    mixed_first,
    grad_h_first,
    gate_first,
    up,
    down,
    up_first,
    down_first,
    experts,
):
    rows, features = h_rows.shape
    width = up.shape[2]
    steps = rows // BLOCK
    half = (BLOCK, features // 2)
    anywhere = pl.BlockSpec(memory_space=pl.ANY)
    shape = jax.ShapeDtypeStruct
    dma = pltpu.SemaphoreType.DMA

    def by_step(lanes):
        return pl.BlockSpec((BLOCK, lanes), lambda n: (turn_block(n), 0))

    def whole(*dims):
        return pl.BlockSpec(dims, lambda n: (0,) * len(dims))

    return pl.pallas_call(
        partial(second_pair_kernel, experts=experts, steps=steps),
        grid=(steps,),
        out_shape=[
            shape((rows, features), bf16),
            shape((8, features), f32),
            shape((features, width), bf16),
            shape((features, width), bf16),
            shape((rows // 2, features), bf16),
            shape((features, width // 2), bf16),
            shape((features, width // 2), bf16),
            shape((features, width // 2), bf16),
        ],
        in_specs=[
            by_step(features),
            by_step(features),
            by_step(128),
            whole(128, features),
            by_step(features),
            by_step(features),
            by_step(128),
        ]
        + [anywhere] * 4,
        out_specs=[by_step(features), whole(8, features)] + [anywhere] * 6,
        scratch_shapes=[
            pltpu.VMEM((features, width), bf16),
            pltpu.VMEM((width, features), bf16),
            *[pltpu.VMEM((features, width), bf16)] * 2,
            pltpu.VMEM((features, width), f32),
            pltpu.VMEM((features, width), f32),
            pltpu.VMEM((features, 128), f32),
            pltpu.VMEM((2, 2, *half), bf16),
            pltpu.VMEM((8, *half), bf16),
            pltpu.VMEM((4, *half), bf16),
            pltpu.VMEM((4, *half), bf16),
            dma((4,)),
        ]
        + [dma((8,))] * 2
        + [dma((4,))] * 7
        + [dma((2,))] * 2
        + [dma((1,))] * 2,
        compiler_params=pltpu.CompilerParams(
            collective_id=4, has_side_effects=True, vmem_limit_bytes=60 << 20
        ),
    )(h_rows, cot_rows, kept, router, mixed_first, grad_h_first, gate_first, up, down, up_first, down_first)


def backward_kernel(
    gain1_ref,
    shift1_ref,
    gain2_ref,
    grad_router_ref,
    qkv_hbm,
    out_w_hbm,
    tok_hbm,
    q_hbm,
    k_hbm,
    v_hbm,
    att_hbm,
    lse_hbm,
    grad_h_hbm,
    resid_ref,
    cot_ref,
    mixed_ref,
    up_second,
    down_second,
    line_first,
    line_out,
    tokens_out,
    weights_out,
    sums_out,
    mixed_out,
    qkv_ref,
    out_w_ref,
    tok_ref,
    q_ref,
    k_ref,
    v_ref,
    att_ref,
    lse_ref,
    grad_h_ref,
    rows_kept,
    cot_rows,
    m_mine,
    m_core,
    m_y,
    m_x,
    m_out,
    m_resid,
    far_vm,
    one_mine,
    one_to,
    one_core,
    one_x,
    one_total,
    line,
    weight_sum,
    weight_half,
    shared,
    shared_y,
    shared_line,
    shared_all,
    route_core,
    route_x,
    late_mine,
    late_y,
    late_z,
    sums_all,
    tokens_low,
    whole,
    mc_s,
    mc_r,
    my_s,
    my_r,
    mx_s,
    mx_r,
    mq_s,
    mq_r,
    m_store,
    oc_s,
    oc_r,
    ox_s,
    ox_r,
    ot_s,
    ot_r,
    l_s,
    l_r,
    sy_s,
    sy_r,
    sl_s,
    sl_r,
    sg_s,
    sg_r,
    sz_s,
    sz_r,
    r_s,
    r_r,
    late_s,
    late_r,
    load,
    image_load,
    own_sem,
    weight_store,
    store,
    *,
    images,
    heads,
):
    expert_at = lax.axis_index("expert")
    tensor_at = lax.axis_index("tensor")
    z_at, y_at = expert_at // 2, expert_at % 2
    z_last = lax.axis_size("expert") // 2 - 1
    x_at, core_at = tensor_at // 2, tensor_at % 2
    other = 1 - core_at
    rows = images * PITCH
    features = tok_hbm.shape[2]
    wide = features // 2
    share = out_w_ref.shape[0]
    hidden = line.shape[3]
    core_dev = (expert_at, tensor_at + 1 - 2 * core_at)
    x_dev = (expert_at, tensor_at + 2 - 4 * x_at)
    y_dev = (expert_at + 1 - 2 * y_at, tensor_at)
    z_devs = [(expert_at + 2, tensor_at), (expert_at - 2, tensor_at)]
    planes = z_last + 1
    z_others = [((z_at + hop) % planes * 2 + y_at, tensor_at) for hop in (1, 2, 3)]
    greet([(True, device) for device in (core_dev, x_dev, y_dev, *z_others)])
    my_cols = lanes_at(core_at * wide, wide)
    their_cols = lanes_at(other * wide, wide)

    def remote(src, dst, send, recv, device):
        return pltpu.make_async_remote_copy(
            src_ref=src, dst_ref=dst, send_sem=send, recv_sem=recv, device_id=device, device_id_type=MESH
        )

    def at_image(image):
        return aligned(image * PITCH, PITCH)

    def place(way):
        return z_at if way == 0 else z_last - z_at

    def far_lanes(way, piece):
        expert = z_last - piece // 2 if way == 0 else piece // 2
        return pl.ds(expert % 2 * hidden, hidden)

    def line_copy(source, way, piece):
        return remote(source, line.at[way, piece], l_s.at[way, piece], l_r.at[way, piece], z_devs[way])

    def line_copy_on(way, piece):
        return line_copy(line.at[way, piece], way, piece)

    def line_start():
        for way in range(2):

            @pl.when(place(way) == 0)
            def _():
                for piece in range(1, 4):
                    source = (up_second, down_second)[piece % 2]
                    line_copy(source.at[:, far_lanes(way, piece)], way, piece).start()

    def line_add(piece):
        for way in range(2):

            @pl.when(place(way) == 1)
            def _():
                if piece > 0:
                    line_copy_on(way, piece).wait_recv()
                lanes = far_lanes(way, piece)

                def add(part, _):
                    at_rows = aligned(part * 96, 96)
                    total = line[way, piece, at_rows, :].astype(f32) + far_vm[piece % 2, at_rows, lanes].astype(f32)
                    line[way, piece, at_rows, :] = total.astype(bf16)
                    return 0

                lax.fori_loop(0, features // 96, add, 0)
                line_copy_on(way, piece).start()

    part_height = line.shape[2] // 4

    def line_part_copy(way, part):
        ref = line.at[way, 3, pl.ds(part * part_height, part_height)]
        return remote(ref, ref, l_s.at[way, 3 + part], l_r.at[way, 3 + part], z_devs[way])

    def line_part(part):
        for way in range(2):

            @pl.when(place(way) == 1)
            def _():
                if part == 0:
                    line_copy_on(way, 3).wait_recv()
                lanes = far_lanes(way, 3)
                for piece in range(2):
                    at_rows = pl.ds(part * part_height + piece * part_height // 2, part_height // 2)
                    total = line[way, 3, at_rows, :].astype(f32) + far_vm[1, at_rows, lanes].astype(f32)
                    line[way, 3, at_rows, :] = total.astype(bf16)
                line_part_copy(way, part).start()

    def line_pass(piece):
        for way in range(2):

            @pl.when(place(way) == 2)
            def _():
                line_copy_on(way, piece).wait_recv()
                line_copy_on(way, piece).start()

    line_start()
    later = [
        pltpu.make_async_copy((up_second, down_second)[number], far_vm.at[number], own_sem.at[number])
        for number in range(2)
    ]
    is_inner = (z_at == 1) | (z_at == z_last - 1)
    first_copy = pltpu.make_async_copy(line_first, line.at[jnp.where(z_at == 1, 0, 1), 0], own_sem.at[2])

    @pl.when(is_inner)
    def _():
        first_copy.start()

    for copy in later:
        copy.start()

    part_count = m_y.shape[0]
    part_rows_m = rows // part_count

    def m_rows(side, part):
        return aligned(side * rows + part * part_rows_m, part_rows_m)

    def m_core_copy(side, part):
        at = m_rows(side, part)
        return remote(mixed_ref.at[at, their_cols], m_core.at[at, :], mc_s.at[side, part], mc_r.at[side, part], core_dev)

    for part in range(part_count):
        m_core_copy(1, part).start()
    for part in range(part_count):
        m_core_copy(0, part).start()
    m_loads = [
        pltpu.make_async_copy(mixed_ref.at[pl.ds(side * rows, rows), my_cols], m_mine.at[pl.ds(side * rows, rows), :], load.at[side])
        for side in range(2)
    ]

    def image_loads(image):
        at = at_image(image)
        by_image = ((tok_hbm, tok_ref), (q_hbm, q_ref), (k_hbm, k_ref), (v_hbm, v_ref), (att_hbm, att_ref), (lse_hbm, lse_ref))
        by_row = ((grad_h_hbm, grad_h_ref), (resid_ref, rows_kept), (cot_ref, cot_rows))
        pairs = [(source.at[image], target.at[image]) for source, target in by_image]
        pairs += [(source.at[at, :], target.at[at, :]) for source, target in by_row]
        return [pltpu.make_async_copy(source, target, image_load.at[n, image]) for n, (source, target) in enumerate(pairs)]

    def start_loads(image, _):
        for copy in image_loads(image):
            copy.start()
        return 0

    weight_loads = [
        pltpu.make_async_copy(qkv_hbm, qkv_ref, own_sem.at[3]),
        pltpu.make_async_copy(out_w_hbm, out_w_ref, own_sem.at[4]),
    ]
    for copy in weight_loads:
        copy.start()
    start_loads(0, 0)
    m_loads[1].start()
    lax.fori_loop(1, images, start_loads, 0)
    m_loads[0].start()
    route_one = remote(grad_router_ref, route_core, r_s.at[0], r_r.at[0], core_dev)
    route_one.start()

    weight_sum[...] = jnp.zeros_like(weight_sum)
    late_mine[...] = jnp.zeros_like(late_mine)

    def m_y_copy(part):
        return remote(m_core.at[m_rows(1, part), :], m_y.at[part], my_s.at[part], my_r.at[part], y_dev)

    def m_x_copy(part):
        return remote(m_core.at[m_rows(0, part), :], m_x.at[part], mx_s.at[part], mx_r.at[part], x_dev)

    def m_place(part):
        return mixed_out.at[aligned(part * part_rows_m, part_rows_m), :]

    def m_quarter_copy(part):
        return remote(m_out.at[part, other], m_place(part), mq_s.at[part], mq_r.at[part], core_dev)

    def m_store_copy(part):
        return pltpu.make_async_copy(m_out.at[part, core_at], m_place(part), m_store.at[part])

    def m_resid_copy(part):
        at = aligned(part * part_rows_m, part_rows_m)
        return pltpu.make_async_copy(resid_ref.at[at, lanes_at(x_at * wide, wide)], m_resid, load.at[3])

    keeps = x_at == core_at

    def run_m_y(part):
        m_core_copy(1, part).wait_recv()
        at = m_rows(1, part)
        m_core[at, :] = (m_core[at, :].astype(f32) + m_mine[at, :].astype(f32)).astype(bf16)
        m_y_copy(part).start()

    def run_m_x(part):
        if isinstance(part, int) and part == 0:
            m_loads[0].wait()
        m_core_copy(0, part).wait_recv()
        m_y_copy(part).wait_recv()
        at = m_rows(0, part)
        total = m_core[at, :].astype(f32) + m_mine[at, :].astype(f32) + m_y[part].astype(f32)
        m_core[at, :] = total.astype(bf16)

        @pl.when(jnp.logical_not(keeps))
        def _():
            m_x_copy(part).start()

    def run_m_out(part):
        @pl.when(keeps)
        def _():
            m_resid_copy(part).start()
            m_x_copy(part).wait_recv()
            m_resid_copy(part).wait()
            total = m_core[m_rows(0, part), :].astype(f32) + m_x[part].astype(f32)
            mixed = (m_resid[...] + total).astype(bf16)
            m_out[part, 0] = mixed[:, : wide // 2]
            m_out[part, 1] = mixed[:, wide // 2 :]
            m_quarter_copy(part).start()
            m_store_copy(part).start()

    later[0].wait()
    later[1].wait()

    @pl.when(is_inner)
    def _():
        first_copy.wait()

    line_add(0)
    m_loads[1].wait()
    for part in range(part_count):
        run_m_y(part)
    route_one.wait_recv()
    route_core[...] += grad_router_ref[...]
    route_two = remote(route_core, route_x, r_s.at[1], r_r.at[1], x_dev)
    route_two.start()

    def one_core_copy(image):
        return remote(one_to.at[image], one_core.at[image], oc_s.at[image], oc_r.at[image], core_dev)

    def one_x_copy(image):
        return remote(one_core.at[image], one_x.at[image], ox_s.at[image], ox_r.at[image], x_dev)

    def one_total_copy(image):
        return remote(one_x.at[image], one_total.at[image], ot_s.at[image], ot_r.at[image], core_dev)

    store_copy = pltpu.make_async_copy(tokens_low, tokens_out, store.at[0])

    lane = lax.broadcasted_iota(jnp.int32, (PITCH, 2 * HD), 1)
    key_mask = lax.broadcasted_iota(jnp.int32, (PITCH, PITCH), 1) < SEQ
    gain1, shift1, gain2 = (ref[...].reshape(1, features) for ref in (gain1_ref, shift1_ref, gain2_ref))

    def norm_back(grad, gain, normed, inverse):
        scaled = grad * gain
        mean = jnp.mean(scaled, axis=1, keepdims=True)
        along = jnp.mean(scaled * normed, axis=1, keepdims=True)
        return (scaled - mean - normed * along) * inverse

    def add_sums(sums, row, grad, normed):
        sums[row : row + 1, :] += jnp.sum(grad * normed, axis=0, keepdims=True)
        sums[row + 1 : row + 2, :] += jnp.sum(grad, axis=0, keepdims=True)

    def run_attention(image):
        for copy in image_loads(image):
            copy.wait()
        at = at_image(image)
        grad_h = grad_h_ref[at, :].astype(f32)
        normed, inverse = norm_stats(rows_kept[at, :])
        add_sums(late_mine, 2, grad_h, normed)
        grad_resid = cot_rows[at, :].astype(f32) + norm_back(grad_h, gain2, normed, inverse)
        rows_kept[at, :] = grad_resid
        grad_branch = grad_resid.astype(bf16)
        token_normed, _ = norm_stats(tok_ref[image].astype(f32))
        h_one = (token_normed * gain1 + shift1).astype(bf16)
        queries, keys, values, attended = q_ref[image], k_ref[image], v_ref[image], att_ref[image]
        lse = lse_ref[image]
        grad_attended = dot(grad_branch, out_w_ref[...], ((1,), (1,))).astype(bf16)
        grads = [[], [], []]
        for head in range(heads):
            first = head // 2 * 2 * HD
            last = min(first + 2 * HD, heads * HD)
            parts = [whose[:, first:last] for whose in (queries, keys, values, grad_attended)]
            if last - first == 2 * HD:
                own = head_mask(lane, head)
                q_own, k_own, _, g_own = (jnp.where(own, part, jnp.zeros_like(part)) for part in parts)
            else:
                q_own, k_own, _, g_own = parts
            scores = dot(q_own, parts[1], ((1,), (1,))) * (HD**-0.5)
            probs = jnp.where(key_mask, jnp.exp(scores - lse[:, head : head + 1]), 0.0)
            back = dot(g_own, parts[2], ((1,), (1,)))
            product = probs * back
            grad_scores = (product - probs * jnp.sum(product, axis=1, keepdims=True)).astype(bf16)
            pieces = (
                dot(grad_scores, k_own) * (HD**-0.5),
                dot(grad_scores, q_own, ((0,), (0,))) * (HD**-0.5),
                dot(probs.astype(bf16), g_own, ((0,), (0,))),
            )
            for which in range(3):
                if head % 2 == 0:
                    grads[which].append(pieces[which])
                else:
                    grads[which][-1] += pieces[which]
        grad_rows = [jnp.concatenate(grads[which], axis=1).astype(bf16) for which in range(3)]
        grad_one = 0.0
        for which in range(3):
            weight_sum[which * share : (which + 1) * share, :] += dot(grad_rows[which].T, h_one)
            grad_one += dot(grad_rows[which], qkv_ref[which])
        weight_sum[3 * share : 4 * share, :] += dot(attended.T, grad_branch)
        whole[...] = grad_one
        one_mine[image] = whole[:, my_cols].astype(bf16)
        one_to[image] = whole[:, their_cols].astype(bf16)
        one_core_copy(image).start()

    def run_one_x(image):
        one_core_copy(image).wait_recv()
        one_core[image] = (one_core[image].astype(f32) + one_mine[image].astype(f32)).astype(bf16)
        one_x_copy(image).start()

    def run_one_total(image):
        one_x_copy(image).wait_recv()
        one_x[image] = (one_core[image].astype(f32) + one_x[image].astype(f32)).astype(bf16)
        one_total_copy(image).start()

    def run_tokens(image):
        one_total_copy(image).wait_recv()
        whole[:, my_cols] = one_x[image].astype(f32)
        whole[:, their_cols] = one_total[image].astype(f32)
        grad_one = whole[...]
        at = at_image(image)
        normed, inverse = norm_stats(tok_ref[image].astype(f32))
        add_sums(late_mine, 0, grad_one, normed)
        total = rows_kept[at, :] + norm_back(grad_one, gain1, normed, inverse)
        whole[...] = total
        for number in range(images):

            @pl.when(image == number)
            def _():
                rows_kept[pl.ds(number * SEQ, SEQ), :] = whole[pl.ds(0, SEQ), :]


    def stage(tick, lag, run):
        image = tick - lag

        @pl.when((image >= 0) & (image < images))
        def _():
            run(image)

    def at_tick(tick, when, run):
        @pl.when(tick == when)
        def _():
            run()

    def line_second():
        line_add(1)
        line_pass(0)

    def line_third():
        line_add(2)
        line_pass(1)

    def per_tick(tick, _):
        stage(tick, 0, run_attention)
        stage(tick, 1, run_one_x)
        stage(tick, 4, run_one_total)
        stage(tick, 5, run_tokens)
        at_tick(tick, 5, lambda: run_m_x(0))
        at_tick(tick, 2, line_second)
        at_tick(tick, 6, line_third)
        at_tick(tick, 7, lambda: run_m_x(1))
        return 0

    for copy in weight_loads:
        copy.wait()
    lax.fori_loop(0, images, per_tick, 0)

    part_rows = shared.shape[1]
    chunks = 2
    chunk_rows = part_rows // chunks
    quarter = chunk_rows // planes

    def cast(piece, _):
        for side in range(2):
            at_rows = aligned(piece * 96, 96)
            shared[side, at_rows, :] = weight_sum[aligned(side * part_rows + piece * 96, 96), :].astype(bf16)
        return 0

    lax.fori_loop(0, part_rows // 96, cast, 0)

    def y_piece(number):
        inner = jnp.where(z_at == 1, jnp.where(number < 2, z_last - number, number - 2), jnp.where(number < 2, number, 5 - number))
        return jnp.where(z_at == 0, z_last - number, jnp.where(z_at == z_last, number, inner))

    def quarter_at(chunk, piece):
        return aligned(chunk * chunk_rows + piece * quarter, quarter)

    def shared_y_copy(chunk, number):
        at_rows = quarter_at(chunk, y_piece(number))
        return remote(
            shared.at[1 - y_at, at_rows, :], shared_y.at[at_rows, :], sy_s.at[chunk, number], sy_r.at[chunk, number], y_dev
        )

    def take_y(chunk, number):
        shared_y_copy(chunk, number).wait_recv()
        at_rows = quarter_at(chunk, y_piece(number))
        weight_half[at_rows, :] = shared[y_at, at_rows, :].astype(f32) + shared_y[at_rows, :].astype(f32)

    def quarter_of(step, at, way):
        mirrored = z_last - step + at
        return mirrored if way == 0 else z_last - mirrored

    def small_copy(chunk, step, way):
        return remote(
            shared_line.at[chunk, way, 0, step],
            shared_line.at[chunk, way, 1, step],
            sl_s.at[chunk, way, step],
            sl_r.at[chunk, way, step],
            z_devs[way],
        )

    def sum_wait(chunk, step):
        for way in range(2):
            at = place(way)

            @pl.when((at > 0) & (at - 1 <= step))
            def _():
                small_copy(chunk, step, way).wait_recv()

    def sum_send(chunk, step):
        for way in range(2):
            at = place(way)

            @pl.when((at <= step) & (at < z_last))
            def _():
                at_rows = quarter_at(chunk, quarter_of(step, at, way))
                if step == 0:
                    shared_line[chunk, way, 0, step] = weight_half[at_rows, :].astype(bf16)
                else:
                    came = jnp.where(at > 0, shared_line[chunk, way, 1, step - 1].astype(f32), 0.0)
                    shared_line[chunk, way, 0, step] = (weight_half[at_rows, :] + came).astype(bf16)
                small_copy(chunk, step, way).start()

    def final_rows(chunk, side, piece):
        return shared_all.at[side, quarter_at(chunk, piece), :]

    def gather_z(chunk, step, way, piece):
        ref = final_rows(chunk, y_at, piece)
        return remote(ref, ref, sg_s.at[chunk, way, step], sg_r.at[chunk, way, step], z_devs[way])

    def gather_y(chunk, step, way, piece, side):
        ref = final_rows(chunk, side, piece)
        return remote(ref, ref, sz_s.at[chunk, way, step], sz_r.at[chunk, way, step], y_dev)

    def piece_out(step, way):
        return z_at - step if way == 0 else z_at + step

    def piece_in(step, way):
        return z_at - 1 - step if way == 0 else z_at + 1 + step

    def gather_send(chunk, step):
        for way in range(2):
            at = place(way)

            @pl.when((at >= step) & (at < z_last))
            def _():
                gather_z(chunk, step, way, piece_out(step, way)).start()

    def gather_take(chunk, step):
        for way in range(2):

            @pl.when(place(way) >= 1 + step)
            def _():
                gather_z(chunk, step, way, piece_in(step, way)).wait_recv()
                gather_y(chunk, step + 1, way, piece_in(step, way), y_at).start()

    def finish_sum(chunk):
        own_rows = quarter_at(chunk, z_at)
        from_below = jnp.where(z_at > 0, shared_line[chunk, 0, 1, 2].astype(f32), 0.0)
        from_above = jnp.where(z_at < z_last, shared_line[chunk, 1, 1, 2].astype(f32), 0.0)
        shared_all[y_at, own_rows, :] = (weight_half[own_rows, :] + from_below + from_above).astype(bf16)
        gather_y(chunk, 0, 0, z_at, y_at).start()

    late_y_copy = remote(late_mine, late_y, late_s.at[0], late_r.at[0], y_dev)

    def late_copy(number):
        ref = late_z.at[z_at]
        return remote(ref, ref, late_s.at[number + 1], late_r.at[number + 1], z_others[number])

    def meanwhile(place_in_order):
        if place_in_order == 0:
            run_one_x(images - 1)
            run_tokens(images - 5)
            run_one_total(images - 4)
            run_m_x(part_count - 2)
        if place_in_order == 1:
            run_m_x(part_count - 1)
            run_tokens(images - 4)
            run_one_total(images - 3)
        if place_in_order == 2:
            run_m_out(0)
            run_tokens(images - 3)
        if place_in_order == 3:
            line_part(0)
            run_one_total(images - 2)
            run_m_out(1)
            run_tokens(images - 2)
        if place_in_order == 4:
            line_part(1)
            run_one_total(images - 1)
            run_m_out(2)
        if place_in_order == 5:
            line_part(2)
            run_tokens(images - 1)
            route_two.wait_recv()
            late_mine[8:16, :] = route_core[...] + route_x[...]
            late_y_copy.start()
            tokens_low[...] = rows_kept[pl.ds(0, images * SEQ), :].astype(bf16)
            store_copy.start()
        if place_in_order == 6:
            line_part(3)
            run_m_out(3)
            late_y_copy.wait_recv()
            late_z[z_at] = late_mine[...] + late_y[...]
            for number in range(planes - 1):
                late_copy(number).start()

    for number in range(4):
        for chunk in range(chunks):
            shared_y_copy(chunk, number).start()
    meanwhile(0)
    for step in range(3):
        for chunk in range(chunks):
            if step > 0:
                sum_wait(chunk, step - 1)
            take_y(chunk, step)
            sum_send(chunk, step)
        if step == 2:
            for chunk in range(chunks):
                take_y(chunk, 3)
        meanwhile(1 + step)
    for chunk in range(chunks):
        sum_wait(chunk, 2)
        finish_sum(chunk)
        gather_send(chunk, 0)
    for step in range(3):
        meanwhile(4 + step)
        for chunk in range(chunks):
            gather_take(chunk, step)
            if step < 2:
                gather_send(chunk, step + 1)

    for way in range(2):

        @pl.when(place(way) == 2)
        def _():
            line_copy_on(way, 2).wait_recv()
            for part in range(4):
                line_part_copy(way, part).wait_recv()

        @pl.when(place(way) == z_last)
        def _():
            line_copy_on(way, 0).wait_recv()
            line_copy_on(way, 1).wait_recv()

    from_far = 1 - z_at // 2
    first_piece = jnp.where((z_at == 0) | (z_at == z_last), 0, 2)

    line_out_copies = [
        pltpu.make_async_copy(line.at[from_far, first_piece + n], line_out.at[n], weight_store.at[n]) for n in range(2)
    ]
    for copy in line_out_copies:
        copy.start()
    for chunk in range(chunks):
        gather_y(chunk, 0, 0, z_at, 1 - y_at).wait_recv()
        for step in range(3):
            for way in range(2):

                @pl.when(place(way) >= 1 + step)
                def _():
                    gather_y(chunk, step + 1, way, piece_in(step, way), 1 - y_at).wait_recv()

    for number in range(planes - 1):
        late_copy(number).wait_recv()
    late = late_z[0]
    for plane in range(1, planes):
        late += late_z[plane]
    sums_all[...] = late
    out_copies = [
        pltpu.make_async_copy(shared_all, weights_out, weight_store.at[2]),
        pltpu.make_async_copy(sums_all, sums_out, weight_store.at[3]),
    ]
    for copy in out_copies:
        copy.start()
    route_one.wait_send()
    route_two.wait_send()

    def drain(image, _):
        for copy in (one_core_copy, one_x_copy, one_total_copy):
            copy(image).wait_send()
        return 0

    lax.fori_loop(0, images, drain, 0)
    for part in range(part_count):
        m_core_copy(0, part).wait_send()
        m_core_copy(1, part).wait_send()
        m_y_copy(part).wait_send()

        @pl.when(keeps)
        def _():
            m_quarter_copy(part).wait_send()
            m_store_copy(part).wait()

        @pl.when(jnp.logical_not(keeps))
        def _():
            m_x_copy(part).wait_send()
            m_quarter_copy(part).wait_recv()

    for copy in (*line_out_copies, *out_copies, store_copy):
        copy.wait()
    late_y_copy.wait_send()
    for number in range(planes - 1):
        late_copy(number).wait_send()
    for way in range(2):

        @pl.when(place(way) == 0)
        def _():
            for piece in range(1, 4):
                line_copy_on(way, piece).wait_send()

        @pl.when(place(way) == 1)
        def _():
            for piece in range(3):
                line_copy_on(way, piece).wait_send()
            for part in range(4):
                line_part_copy(way, part).wait_send()

        @pl.when(place(way) == 2)
        def _():
            for piece in range(2):
                line_copy_on(way, piece).wait_send()

    for chunk in range(chunks):
        gather_y(chunk, 0, 0, z_at, y_at).wait_send()
        for number in range(4):
            shared_y_copy(chunk, number).wait_send()
        for step in range(3):
            for way in range(2):
                at = place(way)

                @pl.when((at <= step) & (at < z_last))
                def _():
                    small_copy(chunk, step, way).wait_send()

                @pl.when((at >= step) & (at < z_last))
                def _():
                    gather_z(chunk, step, way, piece_out(step, way)).wait_send()

                @pl.when(at >= 1 + step)
                def _():
                    gather_y(chunk, step + 1, way, piece_in(step, way), y_at).wait_send()


def run_backward(gain1, shift1, gain2, grad_router, qkv_w, out_w, tok, *streamed):
    images, _, features = tok.shape
    rows = images * PITCH
    share = out_w.shape[0]
    heads = share // HD
    hidden = streamed[-1].shape[1]
    wide = features // 2
    parts = 4
    vmem = pl.BlockSpec(memory_space=pltpu.VMEM)
    anywhere = pl.BlockSpec(memory_space=pl.ANY)
    shape = jax.ShapeDtypeStruct
    dma = pltpu.SemaphoreType.DMA
    block = (images, PITCH, wide)
    return pl.pallas_call(
        partial(backward_kernel, images=images, heads=heads),
        out_shape=[
            shape((2, features, hidden), bf16),
            shape((images * SEQ, features), bf16),
            shape((2, features // 2, features), bf16),
            shape((16, features), f32),
            shape((rows, wide // 2), bf16),
        ],
        in_specs=[vmem] * 4 + [anywhere] * (3 + len(streamed)),
        out_specs=[anywhere] * 5,
        scratch_shapes=[
            pltpu.VMEM(qkv_w.shape, bf16),
            pltpu.VMEM(out_w.shape, bf16),
            pltpu.VMEM((images, PITCH, features), bf16),
            *[pltpu.VMEM((images, PITCH, share), bf16)] * 4,
            pltpu.VMEM((images, PITCH, 128), f32),
            pltpu.VMEM((rows, features), bf16),
            pltpu.VMEM((rows, features), f32),
            pltpu.VMEM((rows, features), bf16),
            pltpu.VMEM((2 * rows, wide), bf16),
            pltpu.VMEM((2 * rows, wide), bf16),
            *[pltpu.VMEM((parts, rows // parts, wide), bf16)] * 2,
            pltpu.VMEM((parts, 2, rows // parts, wide // 2), bf16),
            pltpu.VMEM((rows // parts, wide), f32),
            pltpu.VMEM((2, features, 2 * hidden), bf16),
            *[pltpu.VMEM(block, bf16)] * 5,
            pltpu.VMEM((2, 4, features, hidden), bf16),
            pltpu.VMEM((features, features), f32),
            pltpu.VMEM((features // 2, features), f32),
            pltpu.VMEM((2, features // 2, features), bf16),
            pltpu.VMEM((features // 2, features), bf16),
            pltpu.VMEM((2, 2, 2, 3, features // 16, features), bf16),
            pltpu.VMEM((2, features // 2, features), bf16),
            *[pltpu.VMEM((8, features), f32)] * 2,
            *[pltpu.VMEM((16, features), f32)] * 2,
            pltpu.VMEM((4, 16, features), f32),
            pltpu.VMEM((16, features), f32),
            pltpu.VMEM((images * SEQ, features), bf16),
            pltpu.VMEM((PITCH, features), f32),
        ]
        + [dma((2, parts))] * 2
        + [dma((parts,))] * 7
        + [dma((images,))] * 6
        + [dma((2, 7))] * 2
        + [dma((2, 4))] * 2
        + [dma((2, 2, 3))] * 4
        + [dma((2, 2, 4))] * 2
        + [dma((2,))] * 2
        + [dma((4,))] * 2
        + [dma((4,)), dma((9, images)), dma((5,)), dma((4,)), dma((1,))],
        compiler_params=pltpu.CompilerParams(
            collective_id=2, has_side_effects=True, vmem_limit_bytes=63 << 20
        ),
    )(gain1, shift1, gain2, grad_router, qkv_w, out_w, tok, *streamed)


def last_kernel(
    side_ref, tokens_ref, weights_ref, up_first, up_pair, down_first, down_pair, line_ref, tokens_out, qkv_out, out_w_out, up_out, down_out
):
    share = out_w_out.shape[0]
    tokens_out[...] = tokens_ref[...].astype(f32)
    for which in range(3):
        qkv_out[which] = weights_ref[which * share : (which + 1) * share, :].astype(f32)
    out_w_out[...] = weights_ref[3 * share :, :].astype(f32)
    up_out[...] = up_first[...].astype(f32) + up_pair[...].astype(f32) + line_ref[0].astype(f32)
    down_out[...] = (down_first[...].astype(f32) + down_pair[...].astype(f32) + line_ref[1].astype(f32)).T


def run_last(side, tokens, weights, up_first, up_pair, down_first, down_pair, line, share):
    rows, features = tokens.shape
    hidden = up_pair.shape[1]
    shape = jax.ShapeDtypeStruct

    def lanes(height):
        return pl.BlockSpec((height, 128), lambda n, side: (0, n))

    own = pl.BlockSpec((128, hidden), lambda n, side: (n, side[0]))
    plain = pl.BlockSpec((128, hidden), lambda n, side: (n, 0))
    return pl.pallas_call(
        last_kernel,
        grid_spec=pltpu.PrefetchScalarGridSpec(
            num_scalar_prefetch=1,
            grid=(features // 128,),
            in_specs=[
                lanes(rows),
                lanes(features),
                own,
                plain,
                own,
                plain,
                pl.BlockSpec((2, 128, hidden), lambda n, side: (0, n, 0)),
            ],
            out_specs=[
                lanes(rows),
                pl.BlockSpec((3, share, 128), lambda n, side: (0, 0, n)),
                lanes(share),
                plain,
                lanes(hidden),
            ],
        ),
        out_shape=[
            shape((rows, features), f32),
            shape((3, share, features), f32),
            shape((share, features), f32),
            shape((features, hidden), f32),
            shape((hidden, features), f32),
        ],
    )(side, tokens, weights, up_first, up_pair, down_first, down_pair, line)


def per_image(rows_in):
    images = rows_in.shape[0] // SEQ
    blocks = rows_in.reshape(images, SEQ, rows_in.shape[1])
    return jnp.pad(blocks, ((0, 0), (0, PITCH - SEQ), (0, 0)))


def unpad(blocks):
    images = blocks.shape[0]
    return blocks[:, :SEQ].reshape(images * SEQ, blocks.shape[2])


def per_device_dense(
    tokens,
    gain_attn,
    shift_attn,
    qkv_weight,
    out_weight,
    gain_moe,
    shift_moe,
    router_weight,
    expert_up,
    expert_down,
    routes,
    keep_mask,
    cotangent,
):
    row_count, feature_count = tokens.shape
    images = row_count // SEQ
    rows = images * PITCH
    tensor_count = lax.axis_size("tensor")
    quarter_width = feature_count // tensor_count
    experts_all = router_weight.shape[1]
    hidden = expert_up.shape[2]
    kept_routes = per_image(jnp.where(keep_mask > 0, routes, -1) + 1).reshape(rows, 2) - 1
    expert_lane = jnp.arange(128, dtype=jnp.int32)[None, :]
    kept = ((kept_routes[:, 0:1] == expert_lane) | (kept_routes[:, 1:2] == expert_lane)).astype(bf16)
    cot_turned = cotangent.T
    qkv_turned = jnp.swapaxes(qkv_weight, 1, 2)
    (
        queries,
        keys,
        values,
        attended,
        lse,
        resid,
        h_all,
        cot_all,
        kept_all,
        up_all,
        down_all,
        mixed_first,
        grad_h_first,
        gate_first,
        up_first,
        down_first,
        tok,
        router_wide,
    ) = run_forward(
        tokens,
        gain_attn,
        shift_attn,
        gain_moe,
        shift_moe,
        qkv_turned,
        out_weight,
        expert_up[0],
        expert_down[0],
        router_weight.T,
        cot_turned,
        kept,
        experts_all,
    )
    mixed_part, grad_router, up_second, down_second, grad_h_two, up_pair, down_pair, line_first = run_second_pair(
        h_all,
        cot_all,
        kept_all,
        router_wide,
        mixed_first,
        grad_h_first,
        gate_first,
        up_all,
        down_all,
        up_first,
        down_first,
        experts_all,
    )
    line_sum, tokens_grad, weights_grad, sums, mixed = run_backward(
        gain_attn,
        shift_attn,
        gain_moe,
        grad_router,
        qkv_turned,
        out_weight,
        tok,
        queries,
        keys,
        values,
        attended,
        lse,
        grad_h_two,
        resid,
        cot_all,
        mixed_part,
        up_second,
        down_second,
        line_first,
    )
    side = (lax.axis_index("expert") // 2 % 2).astype(jnp.int32)[None]
    grad_tokens, grad_qkv, grad_out, grad_up, grad_down = run_last(
        side,
        tokens_grad,
        weights_grad.reshape(feature_count, feature_count),
        up_first,
        up_pair,
        down_first,
        down_pair,
        line_sum,
        qkv_weight.shape[2],
    )
    return (
        unpad(mixed.reshape(images, PITCH, quarter_width)),
        grad_tokens,
        sums[0],
        sums[1],
        jnp.swapaxes(grad_qkv, 1, 2),
        grad_out,
        sums[2],
        sums[3],
        sums[8 : 8 + experts_all].T,
        grad_up[None],
        grad_down[None],
    )


def per_device(*arguments):
    router_weight = arguments[7]
    if router_weight.shape[1] == 4 and lax.axis_size("expert") == 8 and lax.axis_size("tensor") == 4:
        return per_device_dense(*arguments)
    return per_device_routed(*arguments)


def solution(mesh):
    placed = (
        P("expert", None),
        P(),
        P(),
        P(None, None, "tensor"),
        P("tensor", None),
        P(),
        P(),
        P(),
        P("expert", None, "tensor"),
        P("expert", "tensor", None),
        P("expert", None),
        P("expert", None),
        P("expert", "tensor"),
    )
    return jax.shard_map(
        per_device,
        mesh=mesh,
        in_specs=placed,
        out_specs=(
            P("expert", "tensor"),
            P("expert", None),
            P(),
            P(),
            P(None, None, "tensor"),
            P("tensor", None),
            P(),
            P(),
            P(),
            P("expert", None, "tensor"),
            P("expert", "tensor", None),
        ),
        check_vma=False,
    )
```

```python
from functools import partial

import jax
import jax.numpy as jnp
from jax import lax
from jax.experimental import pallas as pl
from jax.experimental.pallas import tpu as pltpu
from jax.sharding import PartitionSpec as P

HD = 64
SEQ = 197


norm_epsilon = 1e-06


def norm_rows(values, gain, shift):
    row_mean = jnp.mean(values, axis=-1, keepdims=True)
    centred = values - row_mean
    spread = jnp.mean(centred * centred, axis=-1, keepdims=True)
    return centred * lax.rsqrt(spread + norm_epsilon) * gain + shift


def gelu_exact(values):
    return jax.nn.gelu(values, approximate=False)


def gate_from_logits(logit_rows, picked_rows, keep_rows):
    router_probs = jax.nn.softmax(logit_rows, axis=-1)
    return jnp.sum(jnp.where(picked_rows, router_probs[:, None, :], 0.0), axis=-1) * keep_rows


def attention_forward(h_rows, qkv_w, out_w):
    row_total_count = h_rows.shape[0]
    head_count = qkv_w.shape[2] // HD
    image_count = row_total_count // SEQ
    score_scale = HD ** (-0.5)
    projected = jnp.einsum("td,cdf->ctf", h_rows, qkv_w, preferred_element_type=jnp.float32).astype(
        jnp.bfloat16
    )
    split_heads = projected.reshape(3, image_count, SEQ, head_count, HD)
    queries = split_heads[0]
    keys_all = split_heads[1]
    values_all = split_heads[2]
    scores = (
        jnp.einsum("gqhe,gkhe->ghqk", queries, keys_all, preferred_element_type=jnp.float32)
        * score_scale
    )
    row_peak = jnp.max(scores, axis=-1, keepdims=True)
    exp_scores = jnp.exp(scores - row_peak)
    row_total = jnp.sum(exp_scores, axis=-1, keepdims=True)
    log_total = row_peak + jnp.log(row_total)
    weights = (exp_scores / row_total).astype(jnp.bfloat16)
    attended = jnp.einsum(
        "ghqk,gkhe->gqhe", weights, values_all, preferred_element_type=jnp.float32
    ).astype(jnp.bfloat16)
    attended = attended.reshape(row_total_count, head_count * HD)
    partial_out = jnp.dot(attended, out_w, preferred_element_type=jnp.float32)
    return (partial_out, (attended, queries, keys_all, values_all, log_total))


def attention_backward(grad_branch, saved, h_rows, qkv_w, out_w):
    attended, queries, keys_all, values_all, log_total = saved
    row_total_count = h_rows.shape[0]
    head_count = qkv_w.shape[2] // HD
    image_count = row_total_count // SEQ
    score_scale = HD ** (-0.5)
    grad_out = jnp.einsum("tc,td->cd", attended, grad_branch, preferred_element_type=jnp.float32)
    grad_attended = jnp.einsum(
        "td,cd->tc", grad_branch, out_w, preferred_element_type=jnp.float32
    ).astype(jnp.bfloat16)
    grad_attended = grad_attended.reshape(image_count, SEQ, head_count, HD)
    scores_again = (
        jnp.einsum("gqhe,gkhe->ghqk", queries, keys_all, preferred_element_type=jnp.float32)
        * score_scale
    )
    probs_again = jnp.exp(scores_again - log_total)
    grad_weights = jnp.einsum(
        "gqhe,gkhe->ghqk", grad_attended, values_all, preferred_element_type=jnp.float32
    )
    grad_scores = (
        probs_again * (grad_weights - jnp.sum(probs_again * grad_weights, axis=-1, keepdims=True))
    ).astype(jnp.bfloat16)
    grad_queries = (
        jnp.einsum("ghqk,gkhe->gqhe", grad_scores, keys_all, preferred_element_type=jnp.float32)
        * score_scale
    )
    grad_keys = (
        jnp.einsum("ghqk,gqhe->gkhe", grad_scores, queries, preferred_element_type=jnp.float32)
        * score_scale
    )
    grad_values = jnp.einsum(
        "ghqk,gqhe->gkhe",
        probs_again.astype(jnp.bfloat16),
        grad_attended,
        preferred_element_type=jnp.float32,
    )
    grad_rows = (
        jnp.stack([grad_queries, grad_keys, grad_values])
        .astype(jnp.bfloat16)
        .reshape(3, row_total_count, head_count * HD)
    )
    grad_qkv = jnp.einsum("td,ctf->cdf", h_rows, grad_rows, preferred_element_type=jnp.float32)
    grad_h_one = jnp.einsum("ctf,cdf->td", grad_rows, qkv_w, preferred_element_type=jnp.float32)
    return (grad_qkv, grad_out, grad_h_one)


def moe_tail(
    grad_h_rows,
    grad_gate_rows,
    grad_out_rows,
    h_two_rows,
    resid_rows,
    gate_back,
    router_weight,
    gain_moe,
    shift_moe,
):
    row_total_count = grad_h_rows.shape[0]
    grad_gate = jnp.sum(grad_gate_rows.reshape(row_total_count, -1, 2), axis=1)
    grad_logits = gate_back(grad_gate)[0].astype(jnp.bfloat16)
    grad_router = jnp.einsum(
        "td,te->de", h_two_rows, grad_logits, preferred_element_type=jnp.float32
    )
    grad_h_two = grad_h_rows + jnp.einsum(
        "te,de->td", grad_logits, router_weight, preferred_element_type=jnp.float32
    )
    norm_out, norm_back = jax.vjp(norm_rows, resid_rows, gain_moe, shift_moe)
    grad_resid_norm, grad_gain_moe, grad_shift_moe = norm_back(grad_h_two)
    return (grad_out_rows + grad_resid_norm, grad_router, grad_gain_moe, grad_shift_moe)


def per_device_routed(
    tokens,
    gain_attn,
    shift_attn,
    qkv_weight,
    out_weight,
    gain_moe,
    shift_moe,
    router_weight,
    expert_up,
    expert_down,
    routes,
    keep_mask,
    cotangent,
):
    row_count, feature_count = tokens.shape
    tensor_count = lax.axis_size("tensor")
    expert_count = lax.axis_size("expert")
    tensor_here = lax.axis_index("tensor")
    quarter_width = feature_count // tensor_count
    col_start = tensor_here * quarter_width
    experts_all = router_weight.shape[1]
    capacity = max(2, 7 * row_count // (2 * experts_all))
    tokens_float = tokens.astype(jnp.float32)
    h_one = norm_rows(tokens_float, gain_attn, shift_attn).astype(jnp.bfloat16)
    partial_out, saved = attention_forward(h_one, qkv_weight, out_weight)
    branch = lax.psum(partial_out, "tensor")
    resid = tokens_float + branch
    h_two = norm_rows(resid, gain_moe, shift_moe).astype(jnp.bfloat16)
    logits = jnp.dot(h_two, router_weight, preferred_element_type=jnp.float32)
    keep_float = keep_mask.astype(jnp.float32)
    picked = routes[:, :, None] == jnp.arange(experts_all, dtype=jnp.int32)[None, None, :]
    gate_values, gate_back = jax.vjp(
        partial(gate_from_logits, picked_rows=picked, keep_rows=keep_float), logits
    )
    flat_expert = routes.reshape(-1)
    one_hot = (flat_expert[:, None] == jnp.arange(experts_all, dtype=jnp.int32)[None, :]).astype(
        jnp.int32
    )
    rank_within = jnp.sum((jnp.cumsum(one_hot, axis=0) - one_hot) * one_hot, axis=1)
    slot_index = flat_expert * capacity + rank_within
    token_index = jnp.repeat(jnp.arange(row_count, dtype=jnp.int32), 2)
    live_route = keep_mask.reshape(-1) > 0
    source_table = (
        jnp.full((experts_all * capacity,), row_count, jnp.int32)
        .at[slot_index]
        .set(jnp.where(live_route, token_index, row_count))
    )
    padded_rows = jnp.concatenate([h_two, jnp.zeros((1, feature_count), jnp.bfloat16)], axis=0)
    dispatch = padded_rows[source_table].reshape(experts_all, capacity, feature_count)
    paired = jnp.broadcast_to(dispatch[:, None], (experts_all, 2, capacity, feature_count)).reshape(
        expert_count, capacity, feature_count
    )
    arrived = lax.all_to_all(paired, "expert", split_axis=0, concat_axis=0, tiled=True)
    expert_rows = arrived.reshape(expert_count * capacity, feature_count)
    up_local = expert_up[0]
    down_local = expert_down[0]
    pre_act = jnp.dot(expert_rows, up_local, preferred_element_type=jnp.float32)
    hidden_float, gelu_back = jax.vjp(gelu_exact, pre_act)
    hidden = hidden_float.astype(jnp.bfloat16)
    partial_down = jnp.dot(hidden, down_local, preferred_element_type=jnp.float32)
    summed = lax.psum_scatter(partial_down, "tensor", scatter_dimension=1, tiled=True)
    returned = lax.all_to_all(
        summed.reshape(expert_count, capacity, quarter_width),
        "expert",
        split_axis=0,
        concat_axis=0,
        tiled=True,
    )
    answer_table = jnp.sum(
        returned.reshape(experts_all, 2, capacity, quarter_width), axis=1
    ).astype(jnp.bfloat16)
    answers = (
        answer_table.reshape(experts_all * capacity, quarter_width)[slot_index]
        .astype(jnp.float32)
        .reshape(row_count, 2, quarter_width)
    )
    resid_part = lax.dynamic_slice_in_dim(resid, col_start, quarter_width, 1)
    mixed = (resid_part + jnp.sum(gate_values[:, :, None] * answers, axis=1)).astype(jnp.bfloat16)
    grad_part = cotangent.astype(jnp.float32)
    grad_answers = (
        (gate_values[:, :, None] * grad_part[:, None, :])
        .astype(jnp.bfloat16)
        .reshape(2 * row_count, quarter_width)
    )
    grad_gate_part = jnp.sum(grad_part[:, None, :] * answers, axis=-1)
    outgoing = (
        jnp.zeros((experts_all * capacity, quarter_width), jnp.bfloat16)
        .at[slot_index]
        .set(grad_answers)
    )
    outgoing = jnp.broadcast_to(
        outgoing.reshape(experts_all, 1, capacity, quarter_width),
        (experts_all, 2, capacity, quarter_width),
    ).reshape(expert_count, capacity, quarter_width)
    incoming = lax.all_to_all(outgoing, "expert", split_axis=0, concat_axis=0, tiled=True)
    grad_full = lax.all_gather(incoming, "tensor", axis=2, tiled=True).reshape(
        expert_count * capacity, feature_count
    )
    grad_hidden = jnp.einsum("rd,fd->rf", grad_full, down_local, preferred_element_type=jnp.float32)
    grad_pre = gelu_back(grad_hidden)[0].astype(jnp.bfloat16)
    grad_down = jnp.einsum("rf,rd->fd", hidden, grad_full, preferred_element_type=jnp.float32)
    grad_up = jnp.einsum("rd,rf->df", expert_rows, grad_pre, preferred_element_type=jnp.float32)
    grad_rows_partial = jnp.einsum(
        "rf,df->rd", grad_pre, up_local, preferred_element_type=jnp.float32
    )
    grad_rows_sum = lax.psum_scatter(
        grad_rows_partial.astype(jnp.bfloat16), "tensor", scatter_dimension=1, tiled=True
    ).astype(jnp.float32)
    sent_back = lax.all_to_all(
        grad_rows_sum.reshape(expert_count, capacity, quarter_width).astype(jnp.bfloat16),
        "expert",
        split_axis=0,
        concat_axis=0,
        tiled=True,
    ).astype(jnp.float32)
    grad_table = jnp.sum(sent_back.reshape(experts_all, 2, capacity, quarter_width), axis=1).astype(
        jnp.bfloat16
    )
    grad_inputs = (
        grad_table.reshape(experts_all * capacity, quarter_width)[slot_index]
        .astype(jnp.float32)
        .reshape(row_count, 2, quarter_width)
    )
    grad_h_part = jnp.sum(grad_inputs * keep_float[:, :, None], axis=1)
    grad_h_full, grad_gate_all, grad_out_full = (
        lax.all_gather(grad_h_part, "tensor", axis=1, tiled=True),
        lax.all_gather(grad_gate_part, "tensor", axis=1, tiled=True),
        lax.all_gather(grad_part, "tensor", axis=1, tiled=True),
    )
    grad_resid, grad_router, grad_gain_moe, grad_shift_moe = moe_tail(
        grad_h_full,
        grad_gate_all,
        grad_out_full,
        h_two,
        resid,
        gate_back,
        router_weight,
        gain_moe,
        shift_moe,
    )
    grad_qkv, grad_out, grad_h_one_part = attention_backward(
        grad_resid.astype(jnp.bfloat16), saved, h_one, qkv_weight, out_weight
    )
    grad_h_one = lax.psum(grad_h_one_part.astype(jnp.bfloat16), "tensor").astype(jnp.float32)
    norm_one_out, norm_one_back = jax.vjp(norm_rows, tokens_float, gain_attn, shift_attn)
    grad_tok_norm, grad_gain_attn, grad_shift_attn = norm_one_back(grad_h_one)
    grad_tokens = grad_resid + grad_tok_norm
    summed_grads = lax.psum(
        (
            grad_gain_attn,
            grad_shift_attn,
            grad_qkv,
            grad_out,
            grad_gain_moe,
            grad_shift_moe,
            grad_router,
        ),
        "expert",
    )
    grad_qkv_mine = summed_grads[2]
    grad_out_mine = summed_grads[3]
    return (
        mixed,
        grad_tokens,
        summed_grads[0],
        summed_grads[1],
        grad_qkv_mine,
        grad_out_mine,
        summed_grads[4],
        summed_grads[5],
        summed_grads[6],
        grad_up[None],
        grad_down[None],
    )


MESH = pl.DeviceIdType.MESH
f32 = jnp.float32
bf16 = jnp.bfloat16
PITCH = 208


def dot(left, right, over=((1,), (0,))):
    return lax.dot_general(left, right, (over, ((), ())), preferred_element_type=f32)


def aligned(start, size):
    return pl.ds(pl.multiple_of(start, 16), size)


def lanes_at(start, size):
    return pl.ds(pl.multiple_of(start, 128), size)


def norm_stats(values):
    row_mean = jnp.mean(values, axis=1, keepdims=True)
    centred = values - row_mean
    inverse = lax.rsqrt(jnp.mean(centred * centred, axis=1, keepdims=True) + norm_epsilon)
    return centred * inverse, inverse


def greet(neighbours):
    barrier = pltpu.get_barrier_semaphore()
    count = 0
    for is_there, device in neighbours:

        @pl.when(is_there)
        def _():
            pl.semaphore_signal(barrier, inc=1, device_id=device, device_id_type=MESH)

        count = count + jnp.where(is_there, 1, 0)
    pl.semaphore_wait(barrier, count)


def head_mask(lane, head):
    return (lane < HD) if head % 2 == 0 else (lane >= HD)


def expert_math(h_rows, cot_rows, kept, router, up, down, pair, experts):
    block = h_rows.shape[0]
    hidden = up.shape[1] // 2
    lane = lax.broadcasted_iota(jnp.int32, (block, 128), 1)
    logits = jnp.where(lane < experts, dot(h_rows, router, ((1,), (1,))), -1e30)
    powers = jnp.exp(logits - jnp.max(logits, axis=1, keepdims=True))
    probs = powers / jnp.sum(powers, axis=1, keepdims=True)
    gates = kept * probs
    pre_act = dot(h_rows, up)
    back = dot(cot_rows, down, ((1,), (1,)))
    normal_cdf = 0.5 + 0.5 * lax.erf(pre_act * 0.7071067811865476)
    gelu = pre_act * normal_cdf
    slope = normal_cdf + pre_act * (0.3989422804014327 * jnp.exp(-0.5 * pre_act * pre_act))
    product = gelu * back
    grad_gate = jnp.zeros((block, 128), f32)
    spread = []
    for side in range(2):
        chosen = lane == 2 * pair + side
        part = jnp.sum(product[:, side * hidden : (side + 1) * hidden], axis=1, keepdims=True)
        grad_gate = jnp.where(chosen, part, grad_gate)
        gate = jnp.sum(jnp.where(chosen, gates, 0.0), axis=1, keepdims=True)
        spread.append(jnp.broadcast_to(gate, (block, hidden)))
    gate = jnp.concatenate(spread, axis=1)
    hidden_rows = (gelu * gate).astype(bf16)
    grad_pre = (slope * back * gate).astype(bf16)
    return hidden_rows, grad_pre, probs, grad_gate


BLOCK = 2 * PITCH


def forward_kernel(
    gain1_ref,
    shift1_ref,
    gain2_ref,
    shift2_ref,
    up_ref,
    down_ref,
    router_raw,
    cot_hbm,
    kept_hbm,
    tok_hbm,
    qkv_hbm,
    out_w_hbm,
    q_ref,
    k_ref,
    v_ref,
    att_ref,
    lse_ref,
    resid_ref,
    h_out,
    cot_out,
    kept_out,
    up_out,
    down_out,
    mixed_out,
    grad_h_out,
    gate_out,
    grad_up_out,
    grad_down_out,
    tok_out,
    router_out,
    router_ref,
    cot_turned,
    kept_ref,
    tok_raw,
    qkv_ref,
    out_w_ref,
    tok_ref,
    cot_ref,
    up_vm,
    down_vm,
    up_sum,
    down_sum,
    mixed_slots,
    grad_h_slots,
    gate_slots,
    grad_up_vm,
    grad_down_vm,
    q_all,
    k_all,
    v_all,
    att_all,
    lse_all,
    resid_all,
    h_all,
    cot_all,
    kept_all,
    part,
    mine,
    core_from,
    core_to,
    x_to,
    x_from,
    total_to,
    total_from,
    cot_core,
    core_s,
    core_r,
    x_s,
    x_r,
    tot_s,
    tot_r,
    y_s,
    y_r,
    rel_s,
    rel_r,
    w_s,
    w_r,
    c_s,
    c_r,
    load_sem,
    own_sem,
    pair_sem,
    block_sem,
    grad_sem,
    cot_sem,
    out_sem,
    *,
    images,
    heads,
    experts,
):
    expert_at = lax.axis_index("expert")
    tensor_at = lax.axis_index("tensor")
    z_at, y_at = expert_at // 2, expert_at % 2
    z_last = lax.axis_size("expert") // 2 - 1
    x_at, core_at = tensor_at // 2, tensor_at % 2
    other = 1 - core_at
    rows = images * PITCH
    half = rows // 2
    wide = out_w_ref.shape[1] // 2
    loads = [
        pltpu.make_async_copy(source, target, load_sem.at[number])
        for number, (source, target) in enumerate(
            (
                (cot_hbm, cot_turned),
                (kept_hbm, kept_ref),
                (tok_hbm, tok_raw),
                (qkv_hbm, qkv_ref),
                (out_w_hbm, out_w_ref),
            )
        )
    ]
    for copy in loads:
        copy.start()
    hidden = up_ref.shape[1]
    core_dev = (expert_at, tensor_at + 1 - 2 * core_at)
    x_dev = (expert_at, tensor_at + 2 - 4 * x_at)
    y_dev = (expert_at + 1 - 2 * y_at, tensor_at)
    z_up = (expert_at + 2, tensor_at)
    z_down = (expert_at - 2, tensor_at)
    has_up, has_down = z_at < z_last, z_at > 0
    greet([(True, core_dev), (True, x_dev), (True, y_dev), (has_up, z_up), (has_down, z_down)])

    def remote(src, dst, send, recv, device):
        return pltpu.make_async_remote_copy(
            src_ref=src, dst_ref=dst, send_sem=send, recv_sem=recv, device_id=device, device_id_type=MESH
        )

    def slot(expert, plane):
        pair = (expert // 2 + plane // 2) % 2
        return (
            up_out.at[pair, :, lanes_at(expert % 2 * hidden, hidden)],
            down_out.at[pair, aligned(expert % 2 * hidden, hidden), :],
        )

    def hop(step, way):
        expert = z_at - step if way == 0 else z_at + step
        plane = z_at + 1 if way == 0 else z_at - 1
        source = (up_ref, down_ref) if step == 0 else slot(expert, z_at)
        target = slot(expert, plane)
        device = z_up if way == 0 else z_down
        return [remote(source[n], target[n], w_s.at[way, step, n], w_r.at[way, step, n], device) for n in range(2)]

    def hop_goes(step, way):
        if way == 0:
            return (z_at - step >= 0) & has_up
        return (z_at + step <= z_last) & has_down

    def hop_comes(step, way):
        return (z_at - 1 - step >= 0) if way == 0 else (z_at + 1 + step <= z_last)

    def hop_arriving(step, way):
        expert = z_at - 1 - step if way == 0 else z_at + 1 + step
        target = slot(expert, z_at)
        return [remote(target[n], target[n], w_s.at[way, step, n], w_r.at[way, step, n], core_dev) for n in range(2)]

    def start_hops(step, which):
        for way in range(2):

            @pl.when(hop_goes(step, way))
            def _():
                hop(step, way)[which].start()

    def await_hops(step, which):
        for way in range(2):

            @pl.when(hop_comes(step, way))
            def _():
                hop_arriving(step, way)[which].wait_recv()

    def pass_hops(step, which):
        await_hops(step, which)
        start_hops(step + 1, which)

    start_hops(0, 0)
    start_hops(0, 1)

    def pair_place(expert):
        return up_vm.at[:, lanes_at(expert % 2 * hidden, hidden)], down_vm.at[aligned(expert % 2 * hidden, hidden), :]

    near = z_at + 1 - 2 * (z_at % 2)
    own_copies = [
        pltpu.make_async_copy((up_ref, down_ref)[n], pair_place(z_at)[n], own_sem.at[n]) for n in range(2)
    ]
    near_copies = [
        pltpu.make_async_copy(slot(near, z_at)[n], pair_place(near)[n], pair_sem.at[n]) for n in range(2)
    ]
    for copy in own_copies:
        copy.start()

    loads[0].wait()
    for number in range(images):
        first = number * SEQ // 128 * 128
        skip = number * SEQ - first
        lanes_in = cot_turned[:, first : min(first + 384, images * SEQ)].astype(f32)
        if lanes_in.shape[1] < 384:
            lanes_in = jnp.concatenate([lanes_in, jnp.zeros((lanes_in.shape[0], 384 - lanes_in.shape[1]), f32)], axis=1)
        turned = lanes_in.T[skip : skip + SEQ]
        padded = jnp.concatenate([turned, jnp.zeros((PITCH - SEQ, turned.shape[1]), f32)], axis=0)
        cot_ref[number * PITCH : (number + 1) * PITCH, :] = padded.astype(bf16)
    swap = remote(cot_ref, cot_core, c_s.at[0], c_r.at[0], core_dev)
    swap.start()

    narrow = router_raw[...].astype(f32)
    router_ref[0:16, :] = jnp.concatenate([narrow, jnp.zeros((16 - experts, narrow.shape[1]), f32)], axis=0).astype(bf16)
    router_ref[16:128, :] = jnp.zeros((112, narrow.shape[1]), bf16)

    def kept_half(side, core):
        return kept_all.at[aligned(side * rows + core * half, half), :]

    kept_y = remote(kept_half(0, core_at), kept_half(1, core_at), c_s.at[7], c_r.at[7], y_dev)
    kept_share = remote(kept_half(1, core_at), kept_half(1, core_at), c_s.at[6], c_r.at[6], core_dev)
    kept_share_in = remote(kept_half(1, other), kept_half(1, other), c_s.at[6], c_r.at[6], core_dev)
    loads[1].wait()
    kept_all[pl.ds(0, rows), :] = kept_ref[...]
    kept_y.start()
    swap.wait_recv()

    @pl.when(core_at == 0)
    def _():
        both = jnp.concatenate([cot_ref[...], cot_core[...]], axis=1)
        cot_all[pl.ds(0, rows), lanes_at(x_at * wide, wide)] = both

    @pl.when(core_at == 1)
    def _():
        both = jnp.concatenate([cot_core[...], cot_ref[...]], axis=1)
        cot_all[pl.ds(0, rows), lanes_at(x_at * wide, wide)] = both

    def block(side, col_side, core):
        return cot_all.at[aligned(side * rows + core * half, half), lanes_at(col_side * wide, wide)]

    def cot_copy(number, source, target, device):
        return remote(source, target, c_s.at[number], c_r.at[number], device)

    mine_block = block(0, x_at, core_at)
    cot_x = cot_copy(1, mine_block, mine_block, x_dev)
    cot_y = cot_copy(2, mine_block, block(1, x_at, core_at), y_dev)
    cot_x.start()
    cot_y.start()
    across_x, across_y, across_both = block(0, 1 - x_at, core_at), block(1, x_at, core_at), block(1, 1 - x_at, core_at)
    cot_x_in = cot_copy(1, across_x, across_x, x_dev)
    cot_y_in = cot_copy(2, across_y, across_y, y_dev)
    relay_y = cot_copy(3, across_x, across_both, y_dev)
    relay_in = cot_copy(3, across_both, across_both, y_dev)
    cot_share = [
        cot_copy(4, across_x, across_x, core_dev),
        cot_copy(5, across_y, across_y, core_dev),
        cot_copy(8, across_both, across_both, core_dev),
    ]
    arriving = [block(0, 1 - x_at, other), block(1, x_at, other), block(1, 1 - x_at, other)]
    cot_share_in = [cot_copy(number, ref, ref, core_dev) for number, ref in zip((4, 5, 8), arriving)]

    lane = lax.broadcasted_iota(jnp.int32, (PITCH, 2 * HD), 1)
    key_mask = lax.broadcasted_iota(jnp.int32, (PITCH, PITCH), 1) < SEQ
    gain1, shift1, gain2, shift2 = (ref[...].reshape(1, 2 * wide) for ref in (gain1_ref, shift1_ref, gain2_ref, shift2_ref))
    my_cols = lanes_at(core_at * wide, wide)
    their_cols = lanes_at(other * wide, wide)

    def attend(image):
        normed, _ = norm_stats(tok_ref[image].astype(f32))
        h_one = (normed * gain1 + shift1).astype(bf16)
        queries = dot(h_one, qkv_ref[0], ((1,), (1,))).astype(bf16)
        keys = dot(h_one, qkv_ref[1], ((1,), (1,))).astype(bf16)
        values = dot(h_one, qkv_ref[2], ((1,), (1,))).astype(bf16)
        q_all[image] = queries
        k_all[image] = keys
        v_all[image] = values
        outs = []
        lse = jnp.zeros((PITCH, 2 * HD), f32)
        for head in range(heads):
            first = head // 2 * 2 * HD
            last = min(first + 2 * HD, heads * HD)
            q_head, k_head, v_head = queries[:, first:last], keys[:, first:last], values[:, first:last]
            if last - first == 2 * HD:
                q_head = jnp.where(head_mask(lane, head), q_head, jnp.zeros_like(q_head))
            scores = dot(q_head, k_head, ((1,), (1,))) * (HD**-0.5)
            scores = jnp.where(key_mask, scores, -1e30)
            peak = jnp.max(scores, axis=1, keepdims=True)
            powers = jnp.exp(scores - peak)
            row_sum = jnp.sum(powers, axis=1, keepdims=True)
            weights = (powers / row_sum).astype(bf16)
            outs.append(dot(weights, v_head))
            lse = jnp.where(lane == head, peak + jnp.log(row_sum), lse)
        lse_all[image] = lse
        joined = []
        for head in range(0, heads, 2):
            if head + 1 < heads:
                joined.append(jnp.where(lane < HD, outs[head], outs[head + 1]))
            else:
                joined.append(outs[head])
        attended = jnp.concatenate(joined, axis=1).astype(bf16)
        att_all[image] = attended
        part[...] = dot(attended, out_w_ref[...])
        mine[image] = part[:, my_cols]
        core_to[image] = part[:, their_cols].astype(bf16)

    def core_copy(image):
        return remote(core_to.at[image], core_from.at[image], core_s.at[image], core_r.at[image], core_dev)

    def x_copy(image):
        return remote(x_to.at[image], x_from.at[image], x_s.at[image], x_r.at[image], x_dev)

    def total_copy(image):
        return remote(total_to.at[image], total_from.at[image], tot_s.at[image], tot_r.at[image], core_dev)

    def h_block(side, image, core):
        return h_all.at[aligned(side * rows + image * PITCH, PITCH), lanes_at(core * wide, wide)]

    def y_copy(image):
        return remote(h_block(0, image, core_at), h_block(1, image, core_at), y_s.at[image], y_r.at[image], y_dev)

    def relay_copy(image):
        ref = h_block(1, image, core_at)
        return remote(ref, ref, rel_s.at[image], rel_r.at[image], core_dev)

    def relay_arriving(image):
        ref = h_block(1, image, other)
        return remote(ref, ref, rel_s.at[image], rel_r.at[image], core_dev)

    attend_outs = ((tok_ref, tok_out), (q_all, q_ref), (k_all, k_ref), (v_all, v_ref), (att_all, att_ref), (lse_all, lse_ref))

    def out_copies(image):
        copies = [
            pltpu.make_async_copy(kept.at[image], out.at[image], out_sem.at[n, image])
            for n, (kept, out) in enumerate(attend_outs)
        ]
        at = aligned(image * PITCH, PITCH)
        return copies, [
            pltpu.make_async_copy(resid_all.at[image], resid_ref.at[at, :], out_sem.at[6, image]),
            pltpu.make_async_copy(h_all.at[at, :], h_out.at[at, :], out_sem.at[7, image]),
        ]

    def other_copy(image):
        at = aligned(rows + image * PITCH, PITCH)
        return pltpu.make_async_copy(h_all.at[at, :], h_out.at[at, :], out_sem.at[8, image])

    def stage(tick, lag, run):
        image = tick - lag

        @pl.when((image >= 0) & (image < images))
        def _():
            run(image)

    def run_attend(image):
        attend(image)
        core_copy(image).start()
        for copy in out_copies(image)[0]:
            copy.start()

    def run_x(image):
        core_copy(image).wait_recv()
        x_to[image] = (mine[image] + core_from[image].astype(f32)).astype(bf16)
        x_copy(image).start()

    def run_total(image):
        x_copy(image).wait_recv()
        total_to[image] = (x_to[image].astype(f32) + x_from[image].astype(f32)).astype(bf16)
        total_copy(image).start()

    def run_norm(image):
        total_copy(image).wait_recv()
        part[:, my_cols] = total_to[image].astype(f32)
        part[:, their_cols] = total_from[image].astype(f32)
        resid = tok_ref[image].astype(f32) + part[...]
        resid_all[image] = resid
        normed, _ = norm_stats(resid)
        h_all[aligned(image * PITCH, PITCH), :] = (normed * gain2 + shift2).astype(bf16)
        y_copy(image).start()
        for copy in out_copies(image)[1]:
            copy.start()

    def run_relay(image):
        y_copy(image).wait_recv()
        relay_copy(image).start()

    def run_end(image):
        relay_arriving(image).wait_recv()
        other_copy(image).start()

    def cot_step_one():
        cot_x_in.wait_recv()
        cot_share[0].start()

        relay_y.start()

    def cot_step_two():
        cot_y_in.wait_recv()
        cot_share[1].start()

    def weights_step_one():
        pass_hops(0, 1)
        for copy in near_copies:
            copy.start()

    def cot_step_three():
        kept_y.wait_recv()
        kept_share.start()
        relay_in.wait_recv()
        cot_share[2].start()

    outs = [
        pltpu.make_async_copy(cot_all, cot_out, cot_sem.at[0]),
        pltpu.make_async_copy(kept_all, kept_out, cot_sem.at[1]),
        pltpu.make_async_copy(router_ref, router_out, cot_sem.at[2]),
    ]

    def ready_own():
        cot_share_in[0].wait_recv()
        for copy in (*own_copies, *near_copies):
            copy.wait()

    def ready_other():
        for copy in (cot_share_in[1], cot_share_in[2], kept_share_in):
            copy.wait_recv()
        for copy in outs:
            copy.start()

    def block_copies(number, place):
        at = aligned(number * BLOCK, BLOCK)
        pairs = ((mixed_slots, mixed_out), (grad_h_slots, grad_h_out), (gate_slots, gate_out))
        return [
            pltpu.make_async_copy(slots.at[place], out.at[at, :], block_sem.at[n, place])
            for n, (slots, out) in enumerate(pairs)
        ]

    def run_block(number, turn):
        at = aligned(number * BLOCK, BLOCK)
        h_rows, cot_rows = h_all[at, :], cot_all[at, :]
        up, down = up_vm[...], down_vm[...]
        hidden_rows, grad_pre, _, grad_gate = expert_math(
            h_rows, cot_rows, kept_all[at, :].astype(f32), router_ref[...], up, down, z_at // 2, experts
        )

        place = turn % 2

        @pl.when(turn >= 2)
        def _():
            for copy in block_copies(number, place):
                copy.wait()

        gate_slots[place] = grad_gate
        mixed_slots[place] = dot(hidden_rows, down).astype(bf16)
        grad_h_slots[place] = dot(grad_pre, up, ((1,), (1,))).astype(bf16)
        for copy in block_copies(number, place):
            copy.start()
        up_sum[...] += dot(h_rows.T, grad_pre)
        down_sum[...] += dot(cot_rows.T, hidden_rows)

    up_sum[...] = jnp.zeros_like(up_sum)
    down_sum[...] = jnp.zeros_like(down_sum)

    def take_tokens(number):
        first = number * SEQ // 16 * 16
        skip = number * SEQ - first
        taken = min(224, images * SEQ - first)
        rows_in = tok_raw[first : first + taken, :].astype(f32)[skip : skip + SEQ]
        padded = jnp.concatenate([rows_in, jnp.zeros((PITCH - SEQ, rows_in.shape[1]), f32)], axis=0)
        tok_ref[number] = padded.astype(bf16)

    def first_ticks(tick, _):
        for number in range(images):
            pl.when(tick == number)(partial(take_tokens, number))

        stage(tick, 0, run_attend)
        stage(tick, 1, run_x)
        return 0

    for copy in loads[2:]:
        copy.wait()
    lax.fori_loop(0, images + 1, first_ticks, 0)
    pairs = images // 2

    def both(first, *runs):
        for run in runs:
            run(first)
            run(first + 1)

    pass_hops(0, 0)
    cot_step_one()
    both(0, run_total, run_norm)
    cot_step_two()
    weights_step_one()
    ready_own()

    def per_turn(turn, _):
        @pl.when((turn <= 1) | (turn == 3))
        def _():
            both(jnp.where(turn == 3, 6, 2 * turn + 2), run_total, run_norm)

        @pl.when((turn >= 2) & (turn < pairs + 2))
        def _():
            both(2 * turn - 4, run_relay)

        @pl.when(turn == 2)
        def _():
            pass_hops(1, 0)
            cot_step_three()

        @pl.when(turn == pairs)
        def _():
            pass_hops(1, 1)
            ready_other()

        @pl.when(turn >= pairs)
        def _():
            both(2 * (turn - pairs), run_end)

        run_block(turn, turn)
        return 0

    lax.fori_loop(0, 2 * pairs, per_turn, 0)
    grad_up_vm[...] = up_sum[...].astype(bf16)
    grad_down_vm[...] = down_sum[...].astype(bf16)
    grad_copies = [
        pltpu.make_async_copy(grad_up_vm, grad_up_out, grad_sem.at[0]),
        pltpu.make_async_copy(grad_down_vm, grad_down_out, grad_sem.at[1]),
    ]
    for copy in grad_copies:
        copy.start()
    for copy in (swap, kept_y, kept_share, cot_x, cot_y, *cot_share):
        copy.wait_send()

    relay_y.wait_send()

    def drain(image, _):
        for copy in (core_copy, x_copy, total_copy, y_copy, relay_copy):
            copy(image).wait_send()
        first, second = out_copies(image)
        for copy in (*first, *second, other_copy(image)):
            copy.wait()
        return 0

    lax.fori_loop(0, images, drain, 0)
    for place in range(2):
        for copy in block_copies(0, place):
            copy.wait()

    await_hops(2, 0)
    await_hops(2, 1)
    for step in range(3):
        for way in range(2):

            @pl.when(hop_goes(step, way))
            def _():
                for copy in hop(step, way):
                    copy.wait_send()

    for copy in (*grad_copies, *outs):
        copy.wait()


def run_forward(tok_raw, gain1, shift1, gain2, shift2, qkv_w, out_w, up, down, router, cot, kept, experts):
    images = tok_raw.shape[0] // SEQ
    rows = images * PITCH
    features = tok_raw.shape[1]
    share = out_w.shape[0]
    heads = share // HD
    hidden = up.shape[1]
    wide = features // 2
    vmem = pl.BlockSpec(memory_space=pltpu.VMEM)
    anywhere = pl.BlockSpec(memory_space=pl.ANY)
    shape = jax.ShapeDtypeStruct
    block = (images, PITCH, wide)
    dma = pltpu.SemaphoreType.DMA
    return pl.pallas_call(
        partial(forward_kernel, images=images, heads=heads, experts=experts),
        out_shape=[
            shape((images, PITCH, share), bf16),
            shape((images, PITCH, share), bf16),
            shape((images, PITCH, share), bf16),
            shape((images, PITCH, share), bf16),
            shape((images, PITCH, 128), f32),
            shape((rows, features), f32),
            shape((2 * rows, features), bf16),
            shape((2 * rows, features), bf16),
            shape((2 * rows, 128), bf16),
            shape((2, features, 2 * hidden), bf16),
            shape((2, 2 * hidden, features), bf16),
            shape((2 * rows, features), bf16),
            shape((2 * rows, features), bf16),
            shape((2 * rows, 128), f32),
            shape((features, 2 * hidden), bf16),
            shape((features, 2 * hidden), bf16),
            shape((images, PITCH, features), bf16),
            shape((128, features), bf16),
        ],
        in_specs=[vmem] * 4 + [anywhere] * 2 + [vmem] + [anywhere] * 5,
        out_specs=[anywhere] * 18,
        scratch_shapes=[
            pltpu.VMEM((128, features), bf16),
            pltpu.VMEM(cot.shape, bf16),
            pltpu.VMEM(kept.shape, bf16),
            pltpu.VMEM(tok_raw.shape, bf16),
            pltpu.VMEM(qkv_w.shape, bf16),
            pltpu.VMEM(out_w.shape, bf16),
            pltpu.VMEM((images, PITCH, features), bf16),
            pltpu.VMEM((rows, share), bf16),
            pltpu.VMEM((features, 2 * hidden), bf16),
            pltpu.VMEM((2 * hidden, features), bf16),
            *[pltpu.VMEM((features, 2 * hidden), f32)] * 2,
            *[pltpu.VMEM((2, BLOCK, features), bf16)] * 2,
            pltpu.VMEM((2, BLOCK, 128), f32),
            *[pltpu.VMEM((features, 2 * hidden), bf16)] * 2,
            *[pltpu.VMEM((images, PITCH, share), bf16)] * 4,
            pltpu.VMEM((images, PITCH, 128), f32),
            pltpu.VMEM((images, PITCH, features), f32),
            pltpu.VMEM((2 * rows, features), bf16),
            pltpu.VMEM((2 * rows, features), bf16),
            pltpu.VMEM((2 * rows, 128), bf16),
            pltpu.VMEM((PITCH, features), f32),
            pltpu.VMEM(block, f32),
            pltpu.VMEM(block, bf16),
            pltpu.VMEM(block, bf16),
            pltpu.VMEM(block, bf16),
            pltpu.VMEM(block, bf16),
            pltpu.VMEM(block, bf16),
            pltpu.VMEM(block, bf16),
            pltpu.VMEM((rows, share), bf16),
        ]
        + [dma((images,))] * 10
        + [dma((2, 3, 2))] * 2
        + [dma((9,))] * 2
        + [dma((5,)), dma((2,)), dma((2,)), dma((3, 2)), dma((2,)), dma((3,)), dma((9, images))],
        compiler_params=pltpu.CompilerParams(
            collective_id=1, has_side_effects=True, vmem_limit_bytes=63 << 20
        ),
    )(gain1, shift1, gain2, shift2, up, down, router, cot, kept, tok_raw, qkv_w, out_w)


def turn_is_other(turn):
    return (turn == 0) | ((turn % 2 == 1) & (turn < 7))


def turn_block(turn):
    own = jnp.where(turn == 7, 3, turn // 2 - 1)
    return jnp.where(turn_is_other(turn), 4 + (turn + 1) // 2, own)


def second_pair_kernel(
    h_ref,
    cot_ref,
    kept_ref,
    router_ref,
    mixed_first,
    grad_h_first,
    gate_first,
    up_all,
    down_all,
    up_first,
    down_first,
    mixed_ref,
    grad_router_ref,
    grad_up_out,
    grad_down_out,
    grad_h_out,
    up_pair,
    down_pair,
    line_first,
    up_vm,
    down_vm,
    grad_up_ref,
    grad_down_ref,
    up_sum,
    down_sum,
    router_sum,
    ring,
    from_core,
    from_y,
    from_x,
    load,
    core_s,
    core_r,
    y_s,
    y_r,
    x_s,
    x_r,
    tot_s,
    tot_r,
    store,
    pair_s,
    pair_r,
    line_s,
    line_r,
    *,
    experts,
    steps,
):
    turn = pl.program_id(0)
    expert_at = lax.axis_index("expert")
    tensor_at = lax.axis_index("tensor")
    z_at, y_at = expert_at // 2, expert_at % 2
    x_at, core_at = tensor_at // 2, tensor_at % 2
    hidden = up_pair.shape[1]
    wide = ring.shape[3]
    core_dev = (expert_at, tensor_at + 1 - 2 * core_at)
    x_dev = (expert_at, tensor_at + 2 - 4 * x_at)
    y_dev = (expert_at + 1 - 2 * y_at, tensor_at)
    my_cols = lanes_at(core_at * wide, wide)

    def remote(src, dst, send, recv, device):
        return pltpu.make_async_remote_copy(
            src_ref=src, dst_ref=dst, send_sem=send, recv_sem=recv, device_id=device, device_id_type=MESH
        )

    def core_copy(number):
        return remote(ring.at[number % 2, 1 - core_at], from_core.at[number], core_s.at[number], core_r.at[number], core_dev)

    def y_copy(number, place):
        return remote(from_core.at[number], from_y.at[place], y_s.at[place], y_r.at[place], y_dev)

    def x_copy(number, place):
        return remote(from_core.at[number], from_x.at[place], x_s.at[place], x_r.at[place], x_dev)

    def out_rows(place):
        return grad_h_out.at[aligned(place * BLOCK, BLOCK), my_cols]

    def total_copy(place):
        return remote(from_x.at[place], out_rows(place), tot_s.at[place], tot_r.at[place], core_dev)

    def store_copy(place):
        return pltpu.make_async_copy(from_x.at[place], out_rows(place), store.at[place])

    def own_turn(place):
        return jnp.where(place == 3, 7, 2 * place + 2)

    def other_turn(place):
        return jnp.where(place == 0, 0, 2 * place - 1)

    def pass_other(number):
        core_copy(number).wait_recv()
        from_core[number] = from_core[number] + ring[number % 2, core_at]
        y_copy(number, (number + 1) // 2).start()

    def pass_own(number, place):
        core_copy(number).wait_recv()
        y_copy(number, place).wait_recv()
        total = from_core[number].astype(f32) + ring[number % 2, core_at].astype(f32) + from_y[place].astype(f32)
        from_core[number] = total.astype(bf16)
        x_copy(number, place).start()

    def pass_total(place):
        number = own_turn(place)
        x_copy(number, place).wait_recv()
        from_x[place] = from_core[number] + from_x[place]
        total_copy(place).start()
        store_copy(place).start()

    z_dev = (jnp.where(z_at % 2 == 0, expert_at + 2, expert_at - 2), tensor_at)
    pair_lanes = lanes_at((1 - z_at % 2) * hidden, hidden)
    pair_copies = [
        remote(source.at[:, pair_lanes], target, pair_s.at[number], pair_r.at[number], z_dev)
        for number, (source, target) in enumerate(((up_first, up_pair), (down_first, down_pair)))
    ]

    far_lanes = lanes_at(jnp.where(z_at == 0, 1, 0) * hidden, hidden)
    line_copy = remote(grad_up_ref.at[:, far_lanes], line_first, line_s.at[0], line_r.at[0], z_dev)
    is_outer = (z_at == 0) | (z_at == lax.axis_size("expert") // 2 - 1)

    grad_copies = [
        pltpu.make_async_copy(grad_up_ref, grad_up_out, load.at[2]),
        pltpu.make_async_copy(grad_down_ref, grad_down_out, load.at[3]),
    ]

    @pl.when(turn == 0)
    def _():
        whole = [
            pltpu.make_async_copy(up_all.at[1], up_vm, load.at[0]),
            pltpu.make_async_copy(down_all.at[1], down_vm, load.at[1]),
        ]
        for copy in whole:
            copy.start()
        greet([(True, core_dev), (True, x_dev), (True, y_dev), (True, z_dev)])
        for copy in pair_copies:
            copy.start()
        up_sum[...] = jnp.zeros_like(up_sum)
        down_sum[...] = jnp.zeros_like(down_sum)
        router_sum[...] = jnp.zeros_like(router_sum)
        for copy in whole:
            copy.wait()

    before = turn - 1

    @pl.when((turn >= 1) & turn_is_other(before))
    def _():
        pass_other(before)

    @pl.when((turn == 5) | (turn == 7))
    def _():
        pass_total((turn - 5) // 2)

    @pl.when((turn == 3) | (turn == 5) | (turn == 7))
    def _():
        pass_own(before, (turn - 3) // 2)


    h_rows, cot_rows = h_ref[...], cot_ref[...]
    up, down, router = up_vm[...], down_vm[...], router_ref[...]
    kept = kept_ref[...].astype(f32)
    hidden_rows, grad_pre, probs, grad_gate = expert_math(
        h_rows, cot_rows, kept, router, up, down, 1 - z_at // 2, experts
    )
    grad_gate = kept * (grad_gate + gate_first[...])
    grad_logits = (probs * (grad_gate - jnp.sum(probs * grad_gate, axis=1, keepdims=True))).astype(bf16)

    @pl.when(turn >= 2)
    def _():
        core_copy(turn - 2).wait_send()

    grad_h = (
        grad_h_first[...].astype(f32) + dot(grad_pre, up, ((1,), (1,))) + dot(grad_logits, router)
    ).astype(bf16)
    ring[turn % 2, 0] = grad_h[:, :wide]
    ring[turn % 2, 1] = grad_h[:, wide:]
    core_copy(turn).start()
    mixed_ref[...] = (mixed_first[...].astype(f32) + dot(hidden_rows, down)).astype(bf16)
    h_turned = h_rows.T
    up_sum[...] += dot(h_turned, grad_pre)
    router_sum[...] += dot(h_turned, grad_logits)
    down_sum[...] += dot(cot_rows.T, hidden_rows)

    @pl.when(turn == steps - 1)
    def _():
        grad_up_ref[...] = up_sum[...].astype(bf16)
        grad_copies[0].start()

        @pl.when(is_outer)
        def _():
            line_copy.start()

        pass_own(7, 3)
        pass_total(2)
        grad_down_ref[...] = down_sum[...].astype(bf16)
        grad_copies[1].start()
        grad_router_ref[...] = router_sum[...].T[:8]
        pass_total(3)
        for copy in (*pair_copies, *grad_copies):
            copy.wait()

        @pl.when(is_outer)
        def _():
            line_copy.wait_send()

        @pl.when(jnp.logical_not(is_outer))
        def _():
            line_copy.wait_recv()

        for number in (6, 7):
            core_copy(number).wait_send()
        for place in range(4):
            y_copy(other_turn(place), place).wait_send()
            x_copy(own_turn(place), place).wait_send()
            total_copy(place).wait_send()
            total_copy(place).wait_recv()
            store_copy(place).wait()


def run_second_pair(
    h_rows,
    cot_rows,
    kept,
    router,
    mixed_first,
    grad_h_first,
    gate_first,
    up,
    down,
    up_first,
    down_first,
    experts,
):
    rows, features = h_rows.shape
    width = up.shape[2]
    steps = rows // BLOCK
    half = (BLOCK, features // 2)
    anywhere = pl.BlockSpec(memory_space=pl.ANY)
    shape = jax.ShapeDtypeStruct
    dma = pltpu.SemaphoreType.DMA

    def by_step(lanes):
        return pl.BlockSpec((BLOCK, lanes), lambda n: (turn_block(n), 0))

    def whole(*dims):
        return pl.BlockSpec(dims, lambda n: (0,) * len(dims))

    return pl.pallas_call(
        partial(second_pair_kernel, experts=experts, steps=steps),
        grid=(steps,),
        out_shape=[
            shape((rows, features), bf16),
            shape((8, features), f32),
            shape((features, width), bf16),
            shape((features, width), bf16),
            shape((rows // 2, features), bf16),
            shape((features, width // 2), bf16),
            shape((features, width // 2), bf16),
            shape((features, width // 2), bf16),
        ],
        in_specs=[
            by_step(features),
            by_step(features),
            by_step(128),
            whole(128, features),
            by_step(features),
            by_step(features),
            by_step(128),
        ]
        + [anywhere] * 4,
        out_specs=[by_step(features), whole(8, features)] + [anywhere] * 6,
        scratch_shapes=[
            pltpu.VMEM((features, width), bf16),
            pltpu.VMEM((width, features), bf16),
            *[pltpu.VMEM((features, width), bf16)] * 2,
            pltpu.VMEM((features, width), f32),
            pltpu.VMEM((features, width), f32),
            pltpu.VMEM((features, 128), f32),
            pltpu.VMEM((2, 2, *half), bf16),
            pltpu.VMEM((8, *half), bf16),
            pltpu.VMEM((4, *half), bf16),
            pltpu.VMEM((4, *half), bf16),
            dma((4,)),
        ]
        + [dma((8,))] * 2
        + [dma((4,))] * 7
        + [dma((2,))] * 2
        + [dma((1,))] * 2,
        compiler_params=pltpu.CompilerParams(
            collective_id=4, has_side_effects=True, vmem_limit_bytes=60 << 20
        ),
    )(h_rows, cot_rows, kept, router, mixed_first, grad_h_first, gate_first, up, down, up_first, down_first)


def backward_kernel(
    gain1_ref,
    shift1_ref,
    gain2_ref,
    grad_router_ref,
    qkv_hbm,
    out_w_hbm,
    tok_hbm,
    q_hbm,
    k_hbm,
    v_hbm,
    att_hbm,
    lse_hbm,
    grad_h_hbm,
    resid_ref,
    cot_ref,
    mixed_ref,
    up_second,
    down_second,
    line_first,
    line_out,
    tokens_out,
    weights_out,
    sums_out,
    mixed_out,
    qkv_ref,
    out_w_ref,
    tok_ref,
    q_ref,
    k_ref,
    v_ref,
    att_ref,
    lse_ref,
    grad_h_ref,
    rows_kept,
    cot_rows,
    m_mine,
    m_core,
    m_y,
    m_x,
    m_out,
    m_resid,
    far_vm,
    one_mine,
    one_to,
    one_core,
    one_x,
    one_total,
    line,
    weight_sum,
    weight_half,
    shared,
    shared_y,
    shared_line,
    shared_all,
    route_core,
    route_x,
    late_mine,
    late_y,
    late_z,
    sums_all,
    tokens_low,
    whole,
    mc_s,
    mc_r,
    my_s,
    my_r,
    mx_s,
    mx_r,
    mq_s,
    mq_r,
    m_store,
    oc_s,
    oc_r,
    ox_s,
    ox_r,
    ot_s,
    ot_r,
    l_s,
    l_r,
    sy_s,
    sy_r,
    sl_s,
    sl_r,
    sg_s,
    sg_r,
    sz_s,
    sz_r,
    r_s,
    r_r,
    late_s,
    late_r,
    load,
    image_load,
    own_sem,
    weight_store,
    store,
    *,
    images,
    heads,
):
    expert_at = lax.axis_index("expert")
    tensor_at = lax.axis_index("tensor")
    z_at, y_at = expert_at // 2, expert_at % 2
    z_last = lax.axis_size("expert") // 2 - 1
    x_at, core_at = tensor_at // 2, tensor_at % 2
    other = 1 - core_at
    rows = images * PITCH
    features = tok_hbm.shape[2]
    wide = features // 2
    share = out_w_ref.shape[0]
    hidden = line.shape[3]
    core_dev = (expert_at, tensor_at + 1 - 2 * core_at)
    x_dev = (expert_at, tensor_at + 2 - 4 * x_at)
    y_dev = (expert_at + 1 - 2 * y_at, tensor_at)
    z_devs = [(expert_at + 2, tensor_at), (expert_at - 2, tensor_at)]
    planes = z_last + 1
    z_others = [((z_at + hop) % planes * 2 + y_at, tensor_at) for hop in (1, 2, 3)]
    greet([(True, device) for device in (core_dev, x_dev, y_dev, *z_others)])
    my_cols = lanes_at(core_at * wide, wide)
    their_cols = lanes_at(other * wide, wide)

    def remote(src, dst, send, recv, device):
        return pltpu.make_async_remote_copy(
            src_ref=src, dst_ref=dst, send_sem=send, recv_sem=recv, device_id=device, device_id_type=MESH
        )

    def at_image(image):
        return aligned(image * PITCH, PITCH)

    def place(way):
        return z_at if way == 0 else z_last - z_at

    def far_lanes(way, piece):
        expert = z_last - piece // 2 if way == 0 else piece // 2
        return pl.ds(expert % 2 * hidden, hidden)

    def line_copy(source, way, piece):
        return remote(source, line.at[way, piece], l_s.at[way, piece], l_r.at[way, piece], z_devs[way])

    def line_copy_on(way, piece):
        return line_copy(line.at[way, piece], way, piece)

    def line_start():
        for way in range(2):

            @pl.when(place(way) == 0)
            def _():
                for piece in range(1, 4):
                    source = (up_second, down_second)[piece % 2]
                    line_copy(source.at[:, far_lanes(way, piece)], way, piece).start()

    def line_add(piece):
        for way in range(2):

            @pl.when(place(way) == 1)
            def _():
                if piece > 0:
                    line_copy_on(way, piece).wait_recv()
                lanes = far_lanes(way, piece)

                def add(part, _):
                    at_rows = aligned(part * 96, 96)
                    total = line[way, piece, at_rows, :].astype(f32) + far_vm[piece % 2, at_rows, lanes].astype(f32)
                    line[way, piece, at_rows, :] = total.astype(bf16)
                    return 0

                lax.fori_loop(0, features // 96, add, 0)
                line_copy_on(way, piece).start()

    part_height = line.shape[2] // 4

    def line_part_copy(way, part):
        ref = line.at[way, 3, pl.ds(part * part_height, part_height)]
        return remote(ref, ref, l_s.at[way, 3 + part], l_r.at[way, 3 + part], z_devs[way])

    def line_part(part):
        for way in range(2):

            @pl.when(place(way) == 1)
            def _():
                if part == 0:
                    line_copy_on(way, 3).wait_recv()
                lanes = far_lanes(way, 3)
                for piece in range(2):
                    at_rows = pl.ds(part * part_height + piece * part_height // 2, part_height // 2)
                    total = line[way, 3, at_rows, :].astype(f32) + far_vm[1, at_rows, lanes].astype(f32)
                    line[way, 3, at_rows, :] = total.astype(bf16)
                line_part_copy(way, part).start()

    def line_pass(piece):
        for way in range(2):

            @pl.when(place(way) == 2)
            def _():
                line_copy_on(way, piece).wait_recv()
                line_copy_on(way, piece).start()

    line_start()
    later = [
        pltpu.make_async_copy((up_second, down_second)[number], far_vm.at[number], own_sem.at[number])
        for number in range(2)
    ]
    is_inner = (z_at == 1) | (z_at == z_last - 1)
    first_copy = pltpu.make_async_copy(line_first, line.at[jnp.where(z_at == 1, 0, 1), 0], own_sem.at[2])

    @pl.when(is_inner)
    def _():
        first_copy.start()

    for copy in later:
        copy.start()

    part_count = m_y.shape[0]
    part_rows_m = rows // part_count

    def m_rows(side, part):
        return aligned(side * rows + part * part_rows_m, part_rows_m)

    def m_core_copy(side, part):
        at = m_rows(side, part)
        return remote(mixed_ref.at[at, their_cols], m_core.at[at, :], mc_s.at[side, part], mc_r.at[side, part], core_dev)

    for part in range(part_count):
        m_core_copy(1, part).start()
    for part in range(part_count):
        m_core_copy(0, part).start()
    m_loads = [
        pltpu.make_async_copy(mixed_ref.at[pl.ds(side * rows, rows), my_cols], m_mine.at[pl.ds(side * rows, rows), :], load.at[side])
        for side in range(2)
    ]

    def image_loads(image):
        at = at_image(image)
        by_image = ((tok_hbm, tok_ref), (q_hbm, q_ref), (k_hbm, k_ref), (v_hbm, v_ref), (att_hbm, att_ref), (lse_hbm, lse_ref))
        by_row = ((grad_h_hbm, grad_h_ref), (resid_ref, rows_kept), (cot_ref, cot_rows))
        pairs = [(source.at[image], target.at[image]) for source, target in by_image]
        pairs += [(source.at[at, :], target.at[at, :]) for source, target in by_row]
        return [pltpu.make_async_copy(source, target, image_load.at[n, image]) for n, (source, target) in enumerate(pairs)]

    def start_loads(image, _):
        for copy in image_loads(image):
            copy.start()
        return 0

    weight_loads = [
        pltpu.make_async_copy(qkv_hbm, qkv_ref, own_sem.at[3]),
        pltpu.make_async_copy(out_w_hbm, out_w_ref, own_sem.at[4]),
    ]
    for copy in weight_loads:
        copy.start()
    start_loads(0, 0)
    m_loads[1].start()
    lax.fori_loop(1, images, start_loads, 0)
    m_loads[0].start()
    route_one = remote(grad_router_ref, route_core, r_s.at[0], r_r.at[0], core_dev)
    route_one.start()

    weight_sum[...] = jnp.zeros_like(weight_sum)
    late_mine[...] = jnp.zeros_like(late_mine)

    def m_y_copy(part):
        return remote(m_core.at[m_rows(1, part), :], m_y.at[part], my_s.at[part], my_r.at[part], y_dev)

    def m_x_copy(part):
        return remote(m_core.at[m_rows(0, part), :], m_x.at[part], mx_s.at[part], mx_r.at[part], x_dev)

    def m_place(part):
        return mixed_out.at[aligned(part * part_rows_m, part_rows_m), :]

    def m_quarter_copy(part):
        return remote(m_out.at[part, other], m_place(part), mq_s.at[part], mq_r.at[part], core_dev)

    def m_store_copy(part):
        return pltpu.make_async_copy(m_out.at[part, core_at], m_place(part), m_store.at[part])

    def m_resid_copy(part):
        at = aligned(part * part_rows_m, part_rows_m)
        return pltpu.make_async_copy(resid_ref.at[at, lanes_at(x_at * wide, wide)], m_resid, load.at[3])

    keeps = x_at == core_at

    def run_m_y(part):
        m_core_copy(1, part).wait_recv()
        at = m_rows(1, part)
        m_core[at, :] = (m_core[at, :].astype(f32) + m_mine[at, :].astype(f32)).astype(bf16)
        m_y_copy(part).start()

    def run_m_x(part):
        if isinstance(part, int) and part == 0:
            m_loads[0].wait()
        m_core_copy(0, part).wait_recv()
        m_y_copy(part).wait_recv()
        at = m_rows(0, part)
        total = m_core[at, :].astype(f32) + m_mine[at, :].astype(f32) + m_y[part].astype(f32)
        m_core[at, :] = total.astype(bf16)

        @pl.when(jnp.logical_not(keeps))
        def _():
            m_x_copy(part).start()

    def run_m_out(part):
        @pl.when(keeps)
        def _():
            m_resid_copy(part).start()
            m_x_copy(part).wait_recv()
            m_resid_copy(part).wait()
            total = m_core[m_rows(0, part), :].astype(f32) + m_x[part].astype(f32)
            mixed = (m_resid[...] + total).astype(bf16)
            m_out[part, 0] = mixed[:, : wide // 2]
            m_out[part, 1] = mixed[:, wide // 2 :]
            m_quarter_copy(part).start()
            m_store_copy(part).start()

    later[0].wait()
    later[1].wait()

    @pl.when(is_inner)
    def _():
        first_copy.wait()

    line_add(0)
    m_loads[1].wait()
    for part in range(part_count):
        run_m_y(part)
    route_one.wait_recv()
    route_core[...] += grad_router_ref[...]
    route_two = remote(route_core, route_x, r_s.at[1], r_r.at[1], x_dev)
    route_two.start()

    def one_core_copy(image):
        return remote(one_to.at[image], one_core.at[image], oc_s.at[image], oc_r.at[image], core_dev)

    def one_x_copy(image):
        return remote(one_core.at[image], one_x.at[image], ox_s.at[image], ox_r.at[image], x_dev)

    def one_total_copy(image):
        return remote(one_x.at[image], one_total.at[image], ot_s.at[image], ot_r.at[image], core_dev)

    store_copy = pltpu.make_async_copy(tokens_low, tokens_out, store.at[0])

    lane = lax.broadcasted_iota(jnp.int32, (PITCH, 2 * HD), 1)
    key_mask = lax.broadcasted_iota(jnp.int32, (PITCH, PITCH), 1) < SEQ
    gain1, shift1, gain2 = (ref[...].reshape(1, features) for ref in (gain1_ref, shift1_ref, gain2_ref))

    def norm_back(grad, gain, normed, inverse):
        scaled = grad * gain
        mean = jnp.mean(scaled, axis=1, keepdims=True)
        along = jnp.mean(scaled * normed, axis=1, keepdims=True)
        return (scaled - mean - normed * along) * inverse

    def add_sums(sums, row, grad, normed):
        sums[row : row + 1, :] += jnp.sum(grad * normed, axis=0, keepdims=True)
        sums[row + 1 : row + 2, :] += jnp.sum(grad, axis=0, keepdims=True)

    def run_attention(image):
        for copy in image_loads(image):
            copy.wait()
        at = at_image(image)
        grad_h = grad_h_ref[at, :].astype(f32)
        normed, inverse = norm_stats(rows_kept[at, :])
        add_sums(late_mine, 2, grad_h, normed)
        grad_resid = cot_rows[at, :].astype(f32) + norm_back(grad_h, gain2, normed, inverse)
        rows_kept[at, :] = grad_resid
        grad_branch = grad_resid.astype(bf16)
        token_normed, _ = norm_stats(tok_ref[image].astype(f32))
        h_one = (token_normed * gain1 + shift1).astype(bf16)
        queries, keys, values, attended = q_ref[image], k_ref[image], v_ref[image], att_ref[image]
        lse = lse_ref[image]
        grad_attended = dot(grad_branch, out_w_ref[...], ((1,), (1,))).astype(bf16)
        grads = [[], [], []]
        for head in range(heads):
            first = head // 2 * 2 * HD
            last = min(first + 2 * HD, heads * HD)
            parts = [whose[:, first:last] for whose in (queries, keys, values, grad_attended)]
            if last - first == 2 * HD:
                own = head_mask(lane, head)
                q_own, k_own, _, g_own = (jnp.where(own, part, jnp.zeros_like(part)) for part in parts)
            else:
                q_own, k_own, _, g_own = parts
            scores = dot(q_own, parts[1], ((1,), (1,))) * (HD**-0.5)
            probs = jnp.where(key_mask, jnp.exp(scores - lse[:, head : head + 1]), 0.0)
            back = dot(g_own, parts[2], ((1,), (1,)))
            product = probs * back
            grad_scores = (product - probs * jnp.sum(product, axis=1, keepdims=True)).astype(bf16)
            pieces = (
                dot(grad_scores, k_own) * (HD**-0.5),
                dot(grad_scores, q_own, ((0,), (0,))) * (HD**-0.5),
                dot(probs.astype(bf16), g_own, ((0,), (0,))),
            )
            for which in range(3):
                if head % 2 == 0:
                    grads[which].append(pieces[which])
                else:
                    grads[which][-1] += pieces[which]
        grad_rows = [jnp.concatenate(grads[which], axis=1).astype(bf16) for which in range(3)]
        grad_one = 0.0
        for which in range(3):
            weight_sum[which * share : (which + 1) * share, :] += dot(grad_rows[which].T, h_one)
            grad_one += dot(grad_rows[which], qkv_ref[which])
        weight_sum[3 * share : 4 * share, :] += dot(attended.T, grad_branch)
        whole[...] = grad_one
        one_mine[image] = whole[:, my_cols].astype(bf16)
        one_to[image] = whole[:, their_cols].astype(bf16)
        one_core_copy(image).start()

    def run_one_x(image):
        one_core_copy(image).wait_recv()
        one_core[image] = (one_core[image].astype(f32) + one_mine[image].astype(f32)).astype(bf16)
        one_x_copy(image).start()

    def run_one_total(image):
        one_x_copy(image).wait_recv()
        one_x[image] = (one_core[image].astype(f32) + one_x[image].astype(f32)).astype(bf16)
        one_total_copy(image).start()

    def run_tokens(image):
        one_total_copy(image).wait_recv()
        whole[:, my_cols] = one_x[image].astype(f32)
        whole[:, their_cols] = one_total[image].astype(f32)
        grad_one = whole[...]
        at = at_image(image)
        normed, inverse = norm_stats(tok_ref[image].astype(f32))
        add_sums(late_mine, 0, grad_one, normed)
        total = rows_kept[at, :] + norm_back(grad_one, gain1, normed, inverse)
        whole[...] = total
        for number in range(images):

            @pl.when(image == number)
            def _():
                rows_kept[pl.ds(number * SEQ, SEQ), :] = whole[pl.ds(0, SEQ), :]


    def stage(tick, lag, run):
        image = tick - lag

        @pl.when((image >= 0) & (image < images))
        def _():
            run(image)

    def at_tick(tick, when, run):
        @pl.when(tick == when)
        def _():
            run()

    def line_second():
        line_add(1)
        line_pass(0)

    def line_third():
        line_add(2)
        line_pass(1)

    def per_tick(tick, _):
        stage(tick, 0, run_attention)
        stage(tick, 1, run_one_x)
        stage(tick, 4, run_one_total)
        stage(tick, 5, run_tokens)
        at_tick(tick, 5, lambda: run_m_x(0))
        at_tick(tick, 3, line_second)
        at_tick(tick, 6, line_third)
        at_tick(tick, 7, lambda: run_m_x(1))
        return 0

    for copy in weight_loads:
        copy.wait()
    lax.fori_loop(0, images, per_tick, 0)

    part_rows = shared.shape[1]
    chunks = 2
    chunk_rows = part_rows // chunks
    quarter = chunk_rows // planes

    def cast(piece, _):
        for side in range(2):
            at_rows = aligned(piece * 96, 96)
            shared[side, at_rows, :] = weight_sum[aligned(side * part_rows + piece * 96, 96), :].astype(bf16)
        return 0

    lax.fori_loop(0, part_rows // 96, cast, 0)

    def y_piece(number):
        inner = jnp.where(z_at == 1, jnp.where(number < 2, z_last - number, number - 2), jnp.where(number < 2, number, 5 - number))
        return jnp.where(z_at == 0, z_last - number, jnp.where(z_at == z_last, number, inner))

    def quarter_at(chunk, piece):
        return aligned(chunk * chunk_rows + piece * quarter, quarter)

    def shared_y_copy(chunk, number):
        at_rows = quarter_at(chunk, y_piece(number))
        return remote(
            shared.at[1 - y_at, at_rows, :], shared_y.at[at_rows, :], sy_s.at[chunk, number], sy_r.at[chunk, number], y_dev
        )

    def take_y(chunk, number):
        shared_y_copy(chunk, number).wait_recv()
        at_rows = quarter_at(chunk, y_piece(number))
        weight_half[at_rows, :] = shared[y_at, at_rows, :].astype(f32) + shared_y[at_rows, :].astype(f32)

    def quarter_of(step, at, way):
        mirrored = z_last - step + at
        return mirrored if way == 0 else z_last - mirrored

    def small_copy(chunk, step, way):
        return remote(
            shared_line.at[chunk, way, 0, step],
            shared_line.at[chunk, way, 1, step],
            sl_s.at[chunk, way, step],
            sl_r.at[chunk, way, step],
            z_devs[way],
        )

    def sum_wait(chunk, step):
        for way in range(2):
            at = place(way)

            @pl.when((at > 0) & (at - 1 <= step))
            def _():
                small_copy(chunk, step, way).wait_recv()

    def sum_send(chunk, step):
        for way in range(2):
            at = place(way)

            @pl.when((at <= step) & (at < z_last))
            def _():
                at_rows = quarter_at(chunk, quarter_of(step, at, way))
                if step == 0:
                    shared_line[chunk, way, 0, step] = weight_half[at_rows, :].astype(bf16)
                else:
                    came = jnp.where(at > 0, shared_line[chunk, way, 1, step - 1].astype(f32), 0.0)
                    shared_line[chunk, way, 0, step] = (weight_half[at_rows, :] + came).astype(bf16)
                small_copy(chunk, step, way).start()

    def final_rows(chunk, side, piece):
        return shared_all.at[side, quarter_at(chunk, piece), :]

    def gather_z(chunk, step, way, piece):
        ref = final_rows(chunk, y_at, piece)
        return remote(ref, ref, sg_s.at[chunk, way, step], sg_r.at[chunk, way, step], z_devs[way])

    def gather_y(chunk, step, way, piece, side):
        ref = final_rows(chunk, side, piece)
        return remote(ref, ref, sz_s.at[chunk, way, step], sz_r.at[chunk, way, step], y_dev)

    def piece_out(step, way):
        return z_at - step if way == 0 else z_at + step

    def piece_in(step, way):
        return z_at - 1 - step if way == 0 else z_at + 1 + step

    def gather_send(chunk, step):
        for way in range(2):
            at = place(way)

            @pl.when((at >= step) & (at < z_last))
            def _():
                gather_z(chunk, step, way, piece_out(step, way)).start()

    def gather_take(chunk, step):
        for way in range(2):

            @pl.when(place(way) >= 1 + step)
            def _():
                gather_z(chunk, step, way, piece_in(step, way)).wait_recv()
                gather_y(chunk, step + 1, way, piece_in(step, way), y_at).start()

    def finish_sum(chunk):
        own_rows = quarter_at(chunk, z_at)
        from_below = jnp.where(z_at > 0, shared_line[chunk, 0, 1, 2].astype(f32), 0.0)
        from_above = jnp.where(z_at < z_last, shared_line[chunk, 1, 1, 2].astype(f32), 0.0)
        shared_all[y_at, own_rows, :] = (weight_half[own_rows, :] + from_below + from_above).astype(bf16)
        gather_y(chunk, 0, 0, z_at, y_at).start()

    late_y_copy = remote(late_mine, late_y, late_s.at[0], late_r.at[0], y_dev)

    def late_copy(number):
        ref = late_z.at[z_at]
        return remote(ref, ref, late_s.at[number + 1], late_r.at[number + 1], z_others[number])

    def meanwhile(place_in_order):
        if place_in_order == 0:
            run_one_x(images - 1)
            run_tokens(images - 5)
            run_one_total(images - 4)
            run_m_x(part_count - 2)
        if place_in_order == 1:
            run_m_x(part_count - 1)
            run_tokens(images - 4)
            run_one_total(images - 3)
        if place_in_order == 2:
            run_m_out(0)
            run_tokens(images - 3)
        if place_in_order == 3:
            line_part(0)
            run_one_total(images - 2)
            run_m_out(1)
            run_tokens(images - 2)
        if place_in_order == 4:
            line_part(1)
            run_one_total(images - 1)
            run_m_out(2)
        if place_in_order == 5:
            line_part(2)
            run_tokens(images - 1)
            route_two.wait_recv()
            late_mine[8:16, :] = route_core[...] + route_x[...]
            late_y_copy.start()
            tokens_low[...] = rows_kept[pl.ds(0, images * SEQ), :].astype(bf16)
            store_copy.start()
        if place_in_order == 6:
            line_part(3)
            run_m_out(3)
            late_y_copy.wait_recv()
            late_z[z_at] = late_mine[...] + late_y[...]
            for number in range(planes - 1):
                late_copy(number).start()

    for number in range(4):
        for chunk in range(chunks):
            shared_y_copy(chunk, number).start()
    meanwhile(0)
    for step in range(3):
        for chunk in range(chunks):
            if step > 0:
                sum_wait(chunk, step - 1)
            take_y(chunk, step)
            sum_send(chunk, step)
        if step == 2:
            for chunk in range(chunks):
                take_y(chunk, 3)
        meanwhile(1 + step)
    for chunk in range(chunks):
        sum_wait(chunk, 2)
        finish_sum(chunk)
        gather_send(chunk, 0)
    for step in range(3):
        meanwhile(4 + step)
        for chunk in range(chunks):
            gather_take(chunk, step)
            if step < 2:
                gather_send(chunk, step + 1)

    for way in range(2):

        @pl.when(place(way) == 2)
        def _():
            line_copy_on(way, 2).wait_recv()
            for part in range(4):
                line_part_copy(way, part).wait_recv()

        @pl.when(place(way) == z_last)
        def _():
            line_copy_on(way, 0).wait_recv()
            line_copy_on(way, 1).wait_recv()

    from_far = 1 - z_at // 2
    first_piece = jnp.where((z_at == 0) | (z_at == z_last), 0, 2)

    line_out_copies = [
        pltpu.make_async_copy(line.at[from_far, first_piece + n], line_out.at[n], weight_store.at[n]) for n in range(2)
    ]
    for copy in line_out_copies:
        copy.start()
    for chunk in range(chunks):
        gather_y(chunk, 0, 0, z_at, 1 - y_at).wait_recv()
        for step in range(3):
            for way in range(2):

                @pl.when(place(way) >= 1 + step)
                def _():
                    gather_y(chunk, step + 1, way, piece_in(step, way), 1 - y_at).wait_recv()

    for number in range(planes - 1):
        late_copy(number).wait_recv()
    late = late_z[0]
    for plane in range(1, planes):
        late += late_z[plane]
    sums_all[...] = late
    out_copies = [
        pltpu.make_async_copy(shared_all, weights_out, weight_store.at[2]),
        pltpu.make_async_copy(sums_all, sums_out, weight_store.at[3]),
    ]
    for copy in out_copies:
        copy.start()
    route_one.wait_send()
    route_two.wait_send()

    def drain(image, _):
        for copy in (one_core_copy, one_x_copy, one_total_copy):
            copy(image).wait_send()
        return 0

    lax.fori_loop(0, images, drain, 0)
    for part in range(part_count):
        m_core_copy(0, part).wait_send()
        m_core_copy(1, part).wait_send()
        m_y_copy(part).wait_send()

        @pl.when(keeps)
        def _():
            m_quarter_copy(part).wait_send()
            m_store_copy(part).wait()

        @pl.when(jnp.logical_not(keeps))
        def _():
            m_x_copy(part).wait_send()
            m_quarter_copy(part).wait_recv()

    for copy in (*line_out_copies, *out_copies, store_copy):
        copy.wait()
    late_y_copy.wait_send()
    for number in range(planes - 1):
        late_copy(number).wait_send()
    for way in range(2):

        @pl.when(place(way) == 0)
        def _():
            for piece in range(1, 4):
                line_copy_on(way, piece).wait_send()

        @pl.when(place(way) == 1)
        def _():
            for piece in range(3):
                line_copy_on(way, piece).wait_send()
            for part in range(4):
                line_part_copy(way, part).wait_send()

        @pl.when(place(way) == 2)
        def _():
            for piece in range(2):
                line_copy_on(way, piece).wait_send()

    for chunk in range(chunks):
        gather_y(chunk, 0, 0, z_at, y_at).wait_send()
        for number in range(4):
            shared_y_copy(chunk, number).wait_send()
        for step in range(3):
            for way in range(2):
                at = place(way)

                @pl.when((at <= step) & (at < z_last))
                def _():
                    small_copy(chunk, step, way).wait_send()

                @pl.when((at >= step) & (at < z_last))
                def _():
                    gather_z(chunk, step, way, piece_out(step, way)).wait_send()

                @pl.when(at >= 1 + step)
                def _():
                    gather_y(chunk, step + 1, way, piece_in(step, way), y_at).wait_send()


def run_backward(gain1, shift1, gain2, grad_router, qkv_w, out_w, tok, *streamed):
    images, _, features = tok.shape
    rows = images * PITCH
    share = out_w.shape[0]
    heads = share // HD
    hidden = streamed[-1].shape[1]
    wide = features // 2
    parts = 4
    vmem = pl.BlockSpec(memory_space=pltpu.VMEM)
    anywhere = pl.BlockSpec(memory_space=pl.ANY)
    shape = jax.ShapeDtypeStruct
    dma = pltpu.SemaphoreType.DMA
    block = (images, PITCH, wide)
    return pl.pallas_call(
        partial(backward_kernel, images=images, heads=heads),
        out_shape=[
            shape((2, features, hidden), bf16),
            shape((images * SEQ, features), bf16),
            shape((2, features // 2, features), bf16),
            shape((16, features), f32),
            shape((rows, wide // 2), bf16),
        ],
        in_specs=[vmem] * 4 + [anywhere] * (3 + len(streamed)),
        out_specs=[anywhere] * 5,
        scratch_shapes=[
            pltpu.VMEM(qkv_w.shape, bf16),
            pltpu.VMEM(out_w.shape, bf16),
            pltpu.VMEM((images, PITCH, features), bf16),
            *[pltpu.VMEM((images, PITCH, share), bf16)] * 4,
            pltpu.VMEM((images, PITCH, 128), f32),
            pltpu.VMEM((rows, features), bf16),
            pltpu.VMEM((rows, features), f32),
            pltpu.VMEM((rows, features), bf16),
            pltpu.VMEM((2 * rows, wide), bf16),
            pltpu.VMEM((2 * rows, wide), bf16),
            *[pltpu.VMEM((parts, rows // parts, wide), bf16)] * 2,
            pltpu.VMEM((parts, 2, rows // parts, wide // 2), bf16),
            pltpu.VMEM((rows // parts, wide), f32),
            pltpu.VMEM((2, features, 2 * hidden), bf16),
            *[pltpu.VMEM(block, bf16)] * 5,
            pltpu.VMEM((2, 4, features, hidden), bf16),
            pltpu.VMEM((features, features), f32),
            pltpu.VMEM((features // 2, features), f32),
            pltpu.VMEM((2, features // 2, features), bf16),
            pltpu.VMEM((features // 2, features), bf16),
            pltpu.VMEM((2, 2, 2, 3, features // 16, features), bf16),
            pltpu.VMEM((2, features // 2, features), bf16),
            *[pltpu.VMEM((8, features), f32)] * 2,
            *[pltpu.VMEM((16, features), f32)] * 2,
            pltpu.VMEM((4, 16, features), f32),
            pltpu.VMEM((16, features), f32),
            pltpu.VMEM((images * SEQ, features), bf16),
            pltpu.VMEM((PITCH, features), f32),
        ]
        + [dma((2, parts))] * 2
        + [dma((parts,))] * 7
        + [dma((images,))] * 6
        + [dma((2, 7))] * 2
        + [dma((2, 4))] * 2
        + [dma((2, 2, 3))] * 4
        + [dma((2, 2, 4))] * 2
        + [dma((2,))] * 2
        + [dma((4,))] * 2
        + [dma((4,)), dma((9, images)), dma((5,)), dma((4,)), dma((1,))],
        compiler_params=pltpu.CompilerParams(
            collective_id=2, has_side_effects=True, vmem_limit_bytes=63 << 20
        ),
    )(gain1, shift1, gain2, grad_router, qkv_w, out_w, tok, *streamed)


def last_kernel(
    side_ref, tokens_ref, weights_ref, up_first, up_pair, down_first, down_pair, line_ref, tokens_out, qkv_out, out_w_out, up_out, down_out
):
    share = out_w_out.shape[0]
    tokens_out[...] = tokens_ref[...].astype(f32)
    for which in range(3):
        qkv_out[which] = weights_ref[which * share : (which + 1) * share, :].astype(f32)
    out_w_out[...] = weights_ref[3 * share :, :].astype(f32)
    up_out[...] = up_first[...].astype(f32) + up_pair[...].astype(f32) + line_ref[0].astype(f32)
    down_out[...] = (down_first[...].astype(f32) + down_pair[...].astype(f32) + line_ref[1].astype(f32)).T


def run_last(side, tokens, weights, up_first, up_pair, down_first, down_pair, line, share):
    rows, features = tokens.shape
    hidden = up_pair.shape[1]
    shape = jax.ShapeDtypeStruct

    def lanes(height):
        return pl.BlockSpec((height, 128), lambda n, side: (0, n))

    own = pl.BlockSpec((128, hidden), lambda n, side: (n, side[0]))
    plain = pl.BlockSpec((128, hidden), lambda n, side: (n, 0))
    return pl.pallas_call(
        last_kernel,
        grid_spec=pltpu.PrefetchScalarGridSpec(
            num_scalar_prefetch=1,
            grid=(features // 128,),
            in_specs=[
                lanes(rows),
                lanes(features),
                own,
                plain,
                own,
                plain,
                pl.BlockSpec((2, 128, hidden), lambda n, side: (0, n, 0)),
            ],
            out_specs=[
                lanes(rows),
                pl.BlockSpec((3, share, 128), lambda n, side: (0, 0, n)),
                lanes(share),
                plain,
                lanes(hidden),
            ],
        ),
        out_shape=[
            shape((rows, features), f32),
            shape((3, share, features), f32),
            shape((share, features), f32),
            shape((features, hidden), f32),
            shape((hidden, features), f32),
        ],
    )(side, tokens, weights, up_first, up_pair, down_first, down_pair, line)


def per_image(rows_in):
    images = rows_in.shape[0] // SEQ
    blocks = rows_in.reshape(images, SEQ, rows_in.shape[1])
    return jnp.pad(blocks, ((0, 0), (0, PITCH - SEQ), (0, 0)))


def unpad(blocks):
    images = blocks.shape[0]
    return blocks[:, :SEQ].reshape(images * SEQ, blocks.shape[2])


def per_device_dense(
    tokens,
    gain_attn,
    shift_attn,
    qkv_weight,
    out_weight,
    gain_moe,
    shift_moe,
    router_weight,
    expert_up,
    expert_down,
    routes,
    keep_mask,
    cotangent,
):
    row_count, feature_count = tokens.shape
    images = row_count // SEQ
    rows = images * PITCH
    tensor_count = lax.axis_size("tensor")
    quarter_width = feature_count // tensor_count
    experts_all = router_weight.shape[1]
    hidden = expert_up.shape[2]
    kept_routes = per_image(jnp.where(keep_mask > 0, routes, -1) + 1).reshape(rows, 2) - 1
    expert_lane = jnp.arange(128, dtype=jnp.int32)[None, :]
    kept = ((kept_routes[:, 0:1] == expert_lane) | (kept_routes[:, 1:2] == expert_lane)).astype(bf16)
    cot_turned = cotangent.T
    qkv_turned = jnp.swapaxes(qkv_weight, 1, 2)
    (
        queries,
        keys,
        values,
        attended,
        lse,
        resid,
        h_all,
        cot_all,
        kept_all,
        up_all,
        down_all,
        mixed_first,
        grad_h_first,
        gate_first,
        up_first,
        down_first,
        tok,
        router_wide,
    ) = run_forward(
        tokens,
        gain_attn,
        shift_attn,
        gain_moe,
        shift_moe,
        qkv_turned,
        out_weight,
        expert_up[0],
        expert_down[0],
        router_weight.T,
        cot_turned,
        kept,
        experts_all,
    )
    mixed_part, grad_router, up_second, down_second, grad_h_two, up_pair, down_pair, line_first = run_second_pair(
        h_all,
        cot_all,
        kept_all,
        router_wide,
        mixed_first,
        grad_h_first,
        gate_first,
        up_all,
        down_all,
        up_first,
        down_first,
        experts_all,
    )
    line_sum, tokens_grad, weights_grad, sums, mixed = run_backward(
        gain_attn,
        shift_attn,
        gain_moe,
        grad_router,
        qkv_turned,
        out_weight,
        tok,
        queries,
        keys,
        values,
        attended,
        lse,
        grad_h_two,
        resid,
        cot_all,
        mixed_part,
        up_second,
        down_second,
        line_first,
    )
    side = (lax.axis_index("expert") // 2 % 2).astype(jnp.int32)[None]
    grad_tokens, grad_qkv, grad_out, grad_up, grad_down = run_last(
        side,
        tokens_grad,
        weights_grad.reshape(feature_count, feature_count),
        up_first,
        up_pair,
        down_first,
        down_pair,
        line_sum,
        qkv_weight.shape[2],
    )
    return (
        unpad(mixed.reshape(images, PITCH, quarter_width)),
        grad_tokens,
        sums[0],
        sums[1],
        jnp.swapaxes(grad_qkv, 1, 2),
        grad_out,
        sums[2],
        sums[3],
        sums[8 : 8 + experts_all].T,
        grad_up[None],
        grad_down[None],
    )


def per_device(*arguments):
    router_weight = arguments[7]
    if router_weight.shape[1] == 4 and lax.axis_size("expert") == 8 and lax.axis_size("tensor") == 4:
        return per_device_dense(*arguments)
    return per_device_routed(*arguments)


def solution(mesh):
    placed = (
        P("expert", None),
        P(),
        P(),
        P(None, None, "tensor"),
        P("tensor", None),
        P(),
        P(),
        P(),
        P("expert", None, "tensor"),
        P("expert", "tensor", None),
        P("expert", None),
        P("expert", None),
        P("expert", "tensor"),
    )
    return jax.shard_map(
        per_device,
        mesh=mesh,
        in_specs=placed,
        out_specs=(
            P("expert", "tensor"),
            P("expert", None),
            P(),
            P(),
            P(None, None, "tensor"),
            P("tensor", None),
            P(),
            P(),
            P(),
            P("expert", None, "tensor"),
            P("expert", "tensor", None),
        ),
        check_vma=False,
    )
```
